32 devices in a mesh: dp: 2 (over x), row: 4 (over y, core), col: 4 (over z).
Axes of the slice: x: 2, y: 2, z: 4, core: 2. Of those that a mesh axis runs over, the one named last changes fastest.
Arguments:
- tokens: bfloat16 [4096, 1600], P(('dp', 'row'), 'col'), may hold values from -6 to 6
- cotangent: bfloat16 [4096, 1600], P(('dp', 'row'), 'col'), may hold values from -6 to 6
- segments: int32 [4096], P('dp'), may hold values from 0 to 23, as said below
- w_heads: float32 [4, 2, 200, 3, 1600], P('col', 'dp', None, None, 'row'), may hold values from -0.15625 to 0.15625
- w_out: float32 [4, 2, 200, 1600], P('row', 'dp', None, 'col'), may hold values from -0.875 to 0.875
- w_up: float32 [4, 2, 200, 4, 1600], P('col', 'dp', None, None, 'row'), may hold values from -0.15625 to 0.15625
- w_down: float32 [4, 4, 2, 200, 1600], P(None, 'row', 'dp', None, 'col'), may hold values from -0.078125 to 0.078125
- norm_vectors: float32 [2, 4, 2, 200], P(None, 'col', 'dp'), as said below
- width_vectors: float32 [4, 4, 2, 200], P(None, 'col', 'dp'), as said below
- attend_bias: float32 [2, 4, 2, 200], P(None, 'row', 'dp'), may hold values from -1.25 to 1.25
- hidden_vectors: float32 [4, 4, 2, 200], P(None, 'row', 'dp'), may hold values from -1.25 to 1.25
- drift_heads: float32 [4, 2, 200, 3, 1600], P('col', 'dp', None, None, 'row'), may hold values from -128 to 128
- drift_out: float32 [4, 2, 200, 1600], P('row', 'dp', None, 'col'), may hold values from -7 to 7
- drift_up: float32 [4, 2, 200, 4, 1600], P('col', 'dp', None, None, 'row'), may hold values from -12 to 12
- drift_down: float32 [4, 4, 2, 200, 1600], P(None, 'row', 'dp', None, 'col'), may hold values from -28 to 28
- drift_norm: float32 [2, 4, 2, 200], P(None, 'col', 'dp'), may hold values from -256 to 256
- drift_width: float32 [4, 4, 2, 200], P(None, 'col', 'dp')
- drift_attend: float32 [2, 4, 2, 200], P(None, 'row', 'dp'), may hold values from -128 to 128
- drift_hidden: float32 [4, 4, 2, 200], P(None, 'row', 'dp'), may hold values from -12 to 12
- power_heads: float32 [4, 2, 200, 3, 1600], P('col', 'dp', None, None, 'row'), may hold values from 47.18592 to 188.74368
- power_out: float32 [4, 2, 200, 1600], P('row', 'dp', None, 'col'), may hold values from 0.1152 to 0.4608
- power_up: float32 [4, 2, 200, 4, 1600], P('col', 'dp', None, None, 'row'), may hold values from 0.36864 to 1.47456
- power_down: float32 [4, 4, 2, 200, 1600], P(None, 'row', 'dp', None, 'col'), may hold values from 1.72032 to 6.88128
- power_norm: float32 [2, 4, 2, 200], P(None, 'col', 'dp'), may hold values from 131.072 to 524.288
- power_width: float32 [4, 4, 2, 200], P(None, 'col', 'dp'), as said below
- power_attend: float32 [2, 4, 2, 200], P(None, 'row', 'dp'), may hold values from 47.18592 to 188.74368
- power_hidden: float32 [4, 4, 2, 200], P(None, 'row', 'dp'), may hold values from 0.36864 to 1.47456
Outputs:
- result_tokens: bfloat16 [4096, 1600], P(('dp', 'row'), 'col')
- input_gradient: float32 [4096, 1600], P(('dp', 'row'), 'col')
- heads_drift: float32 [4, 2, 200, 3, 1600], P('col', 'dp', None, None, 'row')
- heads_power: float32 [4, 2, 200, 3, 1600], P('col', 'dp', None, None, 'row')
- heads_new: float32 [4, 2, 200, 3, 1600], P('col', 'dp', None, None, 'row')
- out_drift: float32 [4, 2, 200, 1600], P('row', 'dp', None, 'col')
- out_power: float32 [4, 2, 200, 1600], P('row', 'dp', None, 'col')
- out_new: float32 [4, 2, 200, 1600], P('row', 'dp', None, 'col')
- up_drift: float32 [4, 2, 200, 4, 1600], P('col', 'dp', None, None, 'row')
- up_power: float32 [4, 2, 200, 4, 1600], P('col', 'dp', None, None, 'row')
- up_new: float32 [4, 2, 200, 4, 1600], P('col', 'dp', None, None, 'row')
- down_drift: float32 [4, 4, 2, 200, 1600], P(None, 'row', 'dp', None, 'col')
- down_power: float32 [4, 4, 2, 200, 1600], P(None, 'row', 'dp', None, 'col')
- down_new: float32 [4, 4, 2, 200, 1600], P(None, 'row', 'dp', None, 'col')
- norm_drift: float32 [2, 4, 2, 200], P(None, 'col', 'dp')
- norm_power: float32 [2, 4, 2, 200], P(None, 'col', 'dp')
- norm_new: float32 [2, 4, 2, 200], P(None, 'col', 'dp')
- width_drift: float32 [4, 4, 2, 200], P(None, 'col', 'dp')
- width_power: float32 [4, 4, 2, 200], P(None, 'col', 'dp')
- width_new: float32 [4, 4, 2, 200], P(None, 'col', 'dp')
- attend_drift: float32 [2, 4, 2, 200], P(None, 'row', 'dp')
- attend_power: float32 [2, 4, 2, 200], P(None, 'row', 'dp')
- attend_new: float32 [2, 4, 2, 200], P(None, 'row', 'dp')
- hidden_drift: float32 [4, 4, 2, 200], P(None, 'row', 'dp')
- hidden_power: float32 [4, 4, 2, 200], P(None, 'row', 'dp')
- hidden_new: float32 [4, 4, 2, 200], P(None, 'row', 'dp')
The draws below stay inside these ranges and needn't reach their ends.
Inputs may be any that keep to these rules, and one draw needn't show every extreme that they name: `segments`: never fall along the tokens; each sequence of 512 tokens holds three documents numbered for it alone, the second beginning within its first 128 tokens and the third within its last 128. `norm_vectors`: a gain about one in row 0, a shift in row 1. `width_vectors`: a gain about one in row 1, a shift and biases in the others. `power_width`: positive.
All inputs are finite; a program needn't handle non-finite values.
Results may differ from the reference program's by a relative error of at most 0.012.
Values may be sent and summed in bfloat16 or wider, within the bound.
A program may use at most 896 MiB of HBM per device.

```python
import math
import jax
import jax.numpy as jnp
from jax import lax

D = 1600
HEADS = 25
HD = 64
TOK_DEV = 128
STEP = 10
SEQ = 512
TOKENS = 4096
DB = 200
N_DP = 2
N_ROW = 4
N_COL = 4


def width_scales():
    return jnp.array([1.2, 0.6, 0.6, 1.0], jnp.float32) * TOKENS ** 0.5


def draw_segments(key, part):
    key = jax.random.fold_in(key, 11)
    count = TOKENS // SEQ
    starts = jax.random.randint(jax.random.fold_in(key, 1), (count, 1), 1, TOK_DEV)
    finish = jax.random.randint(jax.random.fold_in(key, 2), (count, 1), SEQ - TOK_DEV + 1, SEQ)
    places = jnp.arange(SEQ, dtype=jnp.int32)[None, :]
    local = (places >= starts).astype(jnp.int32) + (places >= finish).astype(jnp.int32)
    labels = local + 3 * jnp.arange(count, dtype=jnp.int32)[:, None]
    return labels.reshape(TOKENS)


def gains_and_shifts(key, count, gain_row):
    shape = (count, N_COL, N_DP, DB)
    noise = jax.random.normal(key, shape, jnp.float32)
    is_gain = (jnp.arange(count) == gain_row)[:, None, None, None]
    return jnp.where(is_gain, 1.0 + 0.25 * noise, 0.2 * noise)


def draw_norm_vectors(key, part):
    key = jax.random.fold_in(key, 22)
    return gains_and_shifts(key, 2, 0)


def draw_width_vectors(key, part):
    key = jax.random.fold_in(key, 21)
    return gains_and_shifts(key, 4, 1)


def draw_drift_width(key, part):
    key = jax.random.fold_in(key, 31)
    noise = jax.random.normal(key, (4, N_COL, N_DP, DB), jnp.float32)
    return 0.11 * width_scales()[:, None, None, None] * noise


def draw_power_width(key, part):
    key = jax.random.fold_in(key, 32)
    factor = jnp.exp(jax.random.uniform(key, (4, N_COL, N_DP, DB), jnp.float32, 0.0, math.log(4.0)))
    scales = width_scales()
    return 0.001 * (scales * scales)[:, None, None, None] * factor


def levels(stream_key, shape, cuts, least, largest):
    level, own = 1.0, jax.random.fold_in(stream_key, 6)
    for dim, blocks in cuts:
        steps = jnp.exp(jax.random.uniform(jax.random.fold_in(own, dim), (blocks,), jnp.float32, least / len(cuts), largest / len(cuts)))
        level = level * jnp.repeat(steps, shape[dim] // blocks).reshape([-1 if axis == dim else 1 for axis in range(len(shape))])
    return level


def gaussian(rng, extent, width, most, pieces=(), held_as=jnp.bfloat16):
    drawn = jax.random.normal(rng, extent, jnp.float32) * width
    if len(pieces) > 0:
        drawn = levels(rng, extent, pieces, -0.22, 0.18) * drawn
    return jnp.clip(drawn, min=-most, max=most).astype(held_as)


def setup_inputs(seed: int = 0) -> dict:
    streams_of = jax.random.split(jax.random.key(seed), 28)
    tokens = gaussian(streams_of[0], (TOKENS, D), 1.0, 6.0, ((0, 8), (1, 4)))
    cotangent = gaussian(streams_of[1], (TOKENS, D), 1.0, 6.0, ((0, 8), (1, 4)))
    segments = draw_segments(jax.random.fold_in(streams_of[27], 71), 0)
    w_heads = gaussian(streams_of[3], (N_COL, N_DP, DB, 3, D), D ** -0.5, 0.15625, ((0, 4), (1, 2), (4, 4)), jnp.float32)
    w_out = gaussian(streams_of[4], (N_ROW, N_DP, DB, D), (D * 16 // SEQ) ** -0.5, 0.875, ((0, 4), (1, 2), (3, 4)), jnp.float32)
    w_up = gaussian(streams_of[5], (N_COL, N_DP, DB, 4, D), D ** -0.5, 0.15625, ((0, 4), (1, 2), (4, 4)), jnp.float32)
    w_down = gaussian(streams_of[6], (4, N_ROW, N_DP, DB, D), (4 * D) ** -0.5, 0.078125, ((1, 4), (2, 2), (4, 4)), jnp.float32)
    norm_vectors = draw_norm_vectors(jax.random.fold_in(streams_of[27], 71), 0)
    width_vectors = draw_width_vectors(jax.random.fold_in(streams_of[27], 71), 0)
    attend_bias = gaussian(streams_of[9], (2, N_ROW, N_DP, DB), 0.2, 1.25, ((1, 4), (2, 2)), jnp.float32)
    hidden_vectors = gaussian(streams_of[10], (4, N_ROW, N_DP, DB), 0.2, 1.25, ((1, 4), (2, 2)), jnp.float32)
    drift_heads = gaussian(streams_of[11], (N_COL, N_DP, DB, 3, D), (0.0165 * (SEQ * TOKENS) ** 0.5), 128.0, ((0, 4), (1, 2), (4, 4)), jnp.float32)
    drift_out = gaussian(streams_of[12], (N_ROW, N_DP, DB, D), (0.132 * (10 * TOKENS // SEQ) ** 0.5), 7.0, ((0, 4), (1, 2), (3, 4)), jnp.float32)
    drift_up = gaussian(streams_of[13], (N_COL, N_DP, DB, 4, D), (0.033 * TOKENS ** 0.5), 12.0, ((0, 4), (1, 2), (4, 4)), jnp.float32)
    drift_down = gaussian(streams_of[14], (4, N_ROW, N_DP, DB, D), (0.0715 * TOKENS ** 0.5), 28.0, ((1, 4), (2, 2), (4, 4)), jnp.float32)
    drift_norm = gaussian(streams_of[15], (2, N_COL, N_DP, DB), (0.0275 * (SEQ * TOKENS) ** 0.5), 256.0, ((1, 4), (2, 2)), jnp.float32)
    drift_width = draw_drift_width(jax.random.fold_in(streams_of[27], 71), 0)
    drift_attend = gaussian(streams_of[17], (2, N_ROW, N_DP, DB), (0.0165 * (SEQ * TOKENS) ** 0.5), 128.0, ((1, 4), (2, 2)), jnp.float32)
    drift_hidden = gaussian(streams_of[18], (4, N_ROW, N_DP, DB), (0.033 * TOKENS ** 0.5), 12.0, ((1, 4), (2, 2)), jnp.float32)
    power_heads = jnp.clip(jnp.exp(math.log(188.74368) - 1.3862944 * jax.random.uniform(streams_of[19], (N_COL, N_DP, DB, 3, D), jnp.float32) ** levels(streams_of[19], (N_COL, N_DP, DB, 3, D), ((0, 4), (1, 2), (4, 4)), -0.2, 0.2)), 47.18592, 188.74368)
    power_out = jnp.clip(jnp.exp(math.log(0.4608) - 1.3862944 * jax.random.uniform(streams_of[20], (N_ROW, N_DP, DB, D), jnp.float32) ** levels(streams_of[20], (N_ROW, N_DP, DB, D), ((0, 4), (1, 2), (3, 4)), -0.2, 0.2)), 0.1152, 0.4608)
    power_up = jnp.clip(jnp.exp(math.log(1.47456) - 1.3862944 * jax.random.uniform(streams_of[21], (N_COL, N_DP, DB, 4, D), jnp.float32) ** levels(streams_of[21], (N_COL, N_DP, DB, 4, D), ((0, 4), (1, 2), (4, 4)), -0.2, 0.2)), 0.36864, 1.47456)
    power_down = jnp.clip(jnp.exp(math.log(6.88128) - 1.3862944 * jax.random.uniform(streams_of[22], (4, N_ROW, N_DP, DB, D), jnp.float32) ** levels(streams_of[22], (4, N_ROW, N_DP, DB, D), ((1, 4), (2, 2), (4, 4)), -0.2, 0.2)), 1.72032, 6.88128)
    power_norm = jnp.clip(jnp.exp(math.log(524.288) - 1.3862944 * jax.random.uniform(streams_of[23], (2, N_COL, N_DP, DB), jnp.float32) ** levels(streams_of[23], (2, N_COL, N_DP, DB), ((1, 4), (2, 2)), -0.2, 0.2)), 131.072, 524.288)
    power_width = draw_power_width(jax.random.fold_in(streams_of[27], 71), 0)
    power_attend = jnp.clip(jnp.exp(math.log(188.74368) - 1.3862944 * jax.random.uniform(streams_of[25], (2, N_ROW, N_DP, DB), jnp.float32) ** levels(streams_of[25], (2, N_ROW, N_DP, DB), ((1, 4), (2, 2)), -0.2, 0.2)), 47.18592, 188.74368)
    power_hidden = jnp.clip(jnp.exp(math.log(1.47456) - 1.3862944 * jax.random.uniform(streams_of[26], (4, N_ROW, N_DP, DB), jnp.float32) ** levels(streams_of[26], (4, N_ROW, N_DP, DB), ((1, 4), (2, 2)), -0.2, 0.2)), 0.36864, 1.47456)
    return dict(tokens=tokens, cotangent=cotangent, segments=segments, w_heads=w_heads, w_out=w_out, w_up=w_up, w_down=w_down, norm_vectors=norm_vectors, width_vectors=width_vectors, attend_bias=attend_bias, hidden_vectors=hidden_vectors, drift_heads=drift_heads, drift_out=drift_out, drift_up=drift_up, drift_down=drift_down, drift_norm=drift_norm, drift_width=drift_width, drift_attend=drift_attend, drift_hidden=drift_hidden, power_heads=power_heads, power_out=power_out, power_up=power_up, power_down=power_down, power_norm=power_norm, power_width=power_width, power_attend=power_attend, power_hidden=power_hidden)


NORM_EPSILON = 1e-05
BETA_FIRST = 0.9
BETA_SECOND = 0.999
ADAM_EPSILON = 1e-08
MATRIX_DECAY = 0.1
MASKED = -1e+30
HIGHEST = lax.Precision.HIGHEST

@jax.custom_vjp
def low(v):
    return lax.optimization_barrier(v.astype(jnp.bfloat16)).astype(jnp.float32)

@jax.custom_vjp
def low_back(v):
    return v

def low_keep(v):
    return (low(v), None)

def low_pass(kept, grad):
    return (grad,)

def back_keep(v):
    return (v, None)

def back_low(kept, grad):
    return (low(grad),)
low.defvjp(low_keep, low_pass)
low_back.defvjp(back_keep, back_low)

def rounded(value):
    return low(low_back(value))

def layer_norm(inputs, gain, shift):
    center = lax.optimization_barrier(jnp.mean(inputs, axis=-1, keepdims=True))
    spread = lax.optimization_barrier(jnp.mean(inputs * inputs, axis=-1, keepdims=True)) - center * center
    return (inputs - center) * lax.rsqrt(spread + NORM_EPSILON) * gain + shift

def attend(queries, key_rows, value_rows, labels):
    factor = HD ** (-0.5)
    scores = low_back(jnp.einsum('qhe,khe->hqk', queries, key_rows, precision=HIGHEST) * factor)
    places = jnp.arange(SEQ)
    allowed = (labels[:, None] == labels[None, :]) & (places[:, None] >= places[None, :])
    scores = jnp.where(allowed[None], scores, MASKED)
    highest = lax.optimization_barrier(jnp.max(scores, axis=-1, keepdims=True))
    raised = jnp.exp(scores - highest)
    weights = low(raised / lax.optimization_barrier(jnp.sum(raised, axis=-1, keepdims=True)))
    return jnp.einsum('hqk,khe->qhe', weights, value_rows, precision=HIGHEST)

def attend_packed(packed):
    return attend(packed[0], packed[1], packed[2], packed[3])

def forward(inputs, w_heads, w_out, w_up, w_down, norm_vectors, width_vectors, attend_bias, hidden_vectors, labels):
    heads_matrix = low(w_heads).reshape(D, 3 * D)
    out_matrix = low(w_out).reshape(D, D)
    up_matrix = low(w_up).reshape(D, 4 * D)
    down_matrix = low(w_down).reshape(4 * D, D)
    norm_rows = low(norm_vectors).reshape(2, D)
    width_rows = low(width_vectors).reshape(4, D)
    attend_rows = low(attend_bias).reshape(2, D)
    unit_bias = low(hidden_vectors).reshape(4 * D)
    normed = low(layer_norm(inputs, norm_rows[0], norm_rows[1]))
    heads_bias = jnp.concatenate([attend_rows[0], jnp.zeros((D,), jnp.float32), attend_rows[1]])
    projected = rounded(jnp.dot(normed, heads_matrix, precision=HIGHEST) + heads_bias)
    projected = projected.reshape(-1, SEQ, 3, HEADS, HD)
    mixed = lax.map(jax.checkpoint(attend_packed), (projected[:, :, 0], projected[:, :, 1], projected[:, :, 2], labels))
    mixed = rounded(mixed.reshape(-1, D))
    branch = low_back(jnp.dot(mixed, out_matrix, precision=HIGHEST) + width_rows[0])
    middle = inputs + branch
    normed_two = low(layer_norm(middle, width_rows[1], width_rows[2]))
    hidden = low_back(jnp.dot(normed_two, up_matrix, precision=HIGHEST) + unit_bias)
    activated = low(jax.nn.gelu(hidden, approximate=True))
    return middle + low_back(jnp.dot(activated, down_matrix, precision=HIGHEST) + width_rows[3])

def adam(weight, gradient, first, second, rate, decay):
    first_new = BETA_FIRST * first + (1.0 - BETA_FIRST) * gradient
    second_new = BETA_SECOND * second + (1.0 - BETA_SECOND) * gradient * gradient
    corrected = first_new / (1.0 - BETA_FIRST ** STEP)
    divisor = jnp.sqrt(second_new / (1.0 - BETA_SECOND ** STEP)) + ADAM_EPSILON
    return (first_new, second_new, weight - rate * (corrected / divisor + decay * weight))

def reference(tokens, cotangent, segments, w_heads, w_out, w_up, w_down, norm_vectors, width_vectors, attend_bias, hidden_vectors, drift_heads, drift_out, drift_up, drift_down, drift_norm, drift_width, drift_attend, drift_hidden, power_heads, power_out, power_up, power_down, power_norm, power_width, power_attend, power_hidden):
    labels = segments.reshape(-1, SEQ)

    def wrapped(inputs, p_heads, p_out, p_up, p_down, p_norm, p_width, p_attend, p_hidden):
        return forward(inputs, p_heads, p_out, p_up, p_down, p_norm, p_width, p_attend, p_hidden, labels)
    result, pullback = jax.vjp(wrapped, tokens.astype(jnp.float32), w_heads, w_out, w_up, w_down, norm_vectors, width_vectors, attend_bias, hidden_vectors)
    grads = pullback(cotangent.astype(jnp.float32))
    heads_up = adam(w_heads, grads[1], drift_heads, power_heads, 0.05, MATRIX_DECAY)
    out_up = adam(w_out, grads[2], drift_out, power_out, 0.2, MATRIX_DECAY)
    up_up = adam(w_up, grads[3], drift_up, power_up, 0.05, MATRIX_DECAY)
    down_up = adam(w_down, grads[4], drift_down, power_down, 0.025, MATRIX_DECAY)
    norm_up = adam(norm_vectors, grads[5], drift_norm, power_norm, 0.3, 0.0)
    width_up = adam(width_vectors, grads[6], drift_width, power_width, 0.3, 0.0)
    attend_up = adam(attend_bias, grads[7], drift_attend, power_attend, 0.3, 0.0)
    hidden_up = adam(hidden_vectors, grads[8], drift_hidden, power_hidden, 0.3, 0.0)
    return (result.astype(jnp.bfloat16), grads[0], heads_up[0], heads_up[1], heads_up[2], out_up[0], out_up[1], out_up[2], up_up[0], up_up[1], up_up[2], down_up[0], down_up[1], down_up[2], norm_up[0], norm_up[1], norm_up[2], width_up[0], width_up[1], width_up[2], attend_up[0], attend_up[1], attend_up[2], hidden_up[0], hidden_up[1], hidden_up[2])
```

```python
import jax
import jax.numpy as jnp
from jax import lax
from jax.sharding import PartitionSpec as P

HEADS = 25
HD = 64
TOK_DEV = 128
STEP = 10


NORM_EPSILON = 1e-05
BETA_FIRST = 0.9
BETA_SECOND = 0.999
ADAM_EPSILON = 1e-08
MATRIX_DECAY = 0.1
MASKED = -1e30


def normalize(inputs):
    center = jnp.mean(inputs, axis=1, keepdims=True)
    spread = jnp.mean(inputs * inputs, axis=1, keepdims=True) - center * center
    inverse = lax.rsqrt(spread + NORM_EPSILON)
    return ((inputs - center) * inverse, inverse)


def norm_pull(upstream, centered, inverse, gain):
    scaled = upstream * gain
    inner = (
        scaled
        - jnp.mean(scaled, axis=1, keepdims=True)
        - centered * jnp.mean(scaled * centered, axis=1, keepdims=True)
    )
    return inner * inverse


def times(left, right):
    return jnp.dot(left, right, preferred_element_type=jnp.float32)


def times_flipped(left, right):
    return lax.dot_general(
        left, right, (((1,), (1,)), ((), ())), preferred_element_type=jnp.float32
    )


def outer_sum(left, right):
    return lax.dot_general(
        left, right, (((0,), (0,)), ((), ())), preferred_element_type=jnp.float32
    )


def crossed(blocks, n):
    pairs = [(i * n + j, j * n + i) for i in range(n) for j in range(n)]
    return lax.ppermute(blocks, ("row", "col"), pairs)


def scatter_rows(partial):
    return lax.psum_scatter(
        partial.astype(jnp.bfloat16), "row", scatter_dimension=0, tiled=True
    ).astype(jnp.float32)


def gather_rows(local):
    return lax.all_gather(local, "row", axis=0, tiled=True)


def split_heads(rows):
    return jnp.transpose(rows.reshape(rows.shape[0], -1, HD), (1, 0, 2))


def join_heads(values):
    return jnp.transpose(values, (1, 0, 2)).reshape(values.shape[1], -1)


def scores_of(queries, keys, allowed):
    scores = jnp.einsum(
        "hqe,hke->hqk", queries, keys, preferred_element_type=jnp.float32
    ) * HD ** (-0.5)
    return jnp.where(allowed[None], scores, MASKED)


def adam(weight, gradient, first, second, rate, decay):
    first_new = BETA_FIRST * first + (1.0 - BETA_FIRST) * gradient
    second_new = BETA_SECOND * second + (1.0 - BETA_SECOND) * gradient * gradient
    corrected = first_new / (1.0 - BETA_FIRST**STEP)
    divisor = jnp.sqrt(second_new / (1.0 - BETA_SECOND**STEP)) + ADAM_EPSILON
    return (first_new, second_new, weight - rate * (corrected / divisor + decay * weight))


def smooth(values):
    return jax.nn.gelu(values, approximate=True)


def per_device(
    tokens,
    cotangent,
    segments,
    w_heads,
    w_out,
    w_up,
    w_down,
    norm_vectors,
    width_vectors,
    attend_bias,
    hidden_vectors,
    drift_heads,
    drift_out,
    drift_up,
    drift_down,
    drift_norm,
    drift_width,
    drift_attend,
    drift_hidden,
    power_heads,
    power_out,
    power_up,
    power_down,
    power_norm,
    power_width,
    power_attend,
    power_hidden,
):
    n_dp, n_row, n_col = (lax.axis_size(name) for name in ("dp", "row", "col"))
    row = lax.axis_index("row")
    low = jnp.bfloat16
    share = tokens.shape[1]
    width = share * n_col
    seq = tokens.shape[0]
    part = seq // n_row
    near = HEADS // n_row
    window = (HEADS - near * (n_row - 1)) * HD
    step = near * HD
    edge = width - (share + step * (n_row - 1)) if n_row > 1 else 0
    edge = window - share
    to_next = [(i, i + 1) for i in range(n_row - 1)]
    to_last = [(i + 1, i) for i in range(n_row - 1)]
    offset = edge - (share - step) * row

    vectors = jnp.concatenate(
        [
            norm_vectors.reshape(2, -1),
            width_vectors.reshape(4, -1),
            attend_bias.reshape(2, -1),
            hidden_vectors.reshape(4, -1),
        ]
    ).astype(low)
    vectors = lax.all_gather(vectors, ("row", "col", "dp"), axis=0, tiled=False)
    vectors = vectors.reshape(n_row, n_col, n_dp, 12, -1).astype(jnp.float32)
    by_col = jnp.transpose(vectors[0], (2, 0, 1, 3)).reshape(12, width)
    by_row = jnp.transpose(vectors[:, 0], (2, 0, 1, 3)).reshape(12, width)
    gain_one, shift_one, bias_out, gain_two, shift_two, bias_down = (by_col[i] for i in range(6))
    zeros = jnp.zeros((1, window), jnp.float32)
    attend_rows = lax.dynamic_slice_in_dim(by_row[6:8], row * step, window, axis=1)
    heads_bias = jnp.concatenate([attend_rows[0:1], zeros, attend_rows[1:2]]).reshape(-1)
    unit_bias = lax.dynamic_slice_in_dim(by_row[8:12], row * share, share, axis=1).reshape(-1)

    own = w_heads.astype(low).reshape(-1, 3, share)
    passed = lax.ppermute(own[:, :, share - edge :], "row", to_next)
    own = jnp.concatenate([passed, own, jnp.zeros_like(passed)], axis=2)
    own = lax.dynamic_slice_in_dim(own, offset, window, axis=2).reshape(-1, 3 * window)
    heads_matrix = lax.all_gather(own, ("col", "dp"), axis=0, tiled=True)
    out_matrix = lax.all_gather(w_out.astype(low).reshape(-1, share), ("col", "dp"), axis=0)
    out_matrix = jnp.transpose(out_matrix.reshape(n_col, share, share), (1, 0, 2))
    out_matrix = out_matrix.reshape(share, width)
    passed = lax.ppermute(out_matrix[share - edge :], "row", to_next)
    out_matrix = jnp.concatenate([passed, out_matrix, jnp.zeros_like(passed)])
    out_matrix = lax.dynamic_slice_in_dim(out_matrix, offset, window)
    owned = (jnp.arange(window) < step) | (row == n_row - 1)
    out_matrix = jnp.where(owned[:, None], out_matrix, jnp.zeros_like(out_matrix))
    up_matrix = lax.all_gather(
        w_up.astype(low).reshape(-1, 4 * share), ("col", "dp"), axis=0, tiled=True
    )
    down_matrix = lax.all_gather(w_down.astype(low).reshape(4, -1, share), ("col", "dp"), axis=0)
    down_matrix = down_matrix.reshape(n_col, n_dp, 4, -1, share)
    down_matrix = jnp.transpose(down_matrix, (2, 1, 3, 0, 4)).reshape(4 * share, width)

    inputs_low = lax.all_gather(crossed(tokens, n_row), "row", axis=1, tiled=True)
    upstream = lax.all_gather(crossed(cotangent, n_row), "row", axis=1, tiled=True)
    inputs = inputs_low.astype(jnp.float32)
    centered_one, inverse_one = normalize(inputs)
    normed_one = (centered_one * gain_one + shift_one).astype(low)
    projected = (times(normed_one, heads_matrix) + heads_bias).astype(low)
    queries, keys, values = (
        split_heads(projected[:, i * window : (i + 1) * window]) for i in range(3)
    )
    labels = lax.dynamic_slice_in_dim(segments, lax.axis_index("col") * seq, seq)
    places = jnp.arange(seq, dtype=jnp.int32)
    allowed = (labels[:, None] == labels[None, :]) & (places[:, None] >= places[None, :])
    scores = scores_of(queries, keys, allowed)
    highest = jnp.max(scores, axis=-1, keepdims=True)
    log_total = highest + jnp.log(jnp.sum(jnp.exp(scores - highest), axis=-1, keepdims=True))
    soft = jnp.exp(scores - log_total).astype(low)
    mixed = jnp.einsum("hqk,hke->hqe", soft, values, preferred_element_type=jnp.float32)
    mixed = join_heads(mixed.astype(low))
    branch = scatter_rows(times(mixed, out_matrix))
    mine = row * part
    middle = lax.dynamic_slice_in_dim(inputs, mine, part) + (branch + bias_out)
    centered_two, inverse_two = normalize(middle)
    normed_two = gather_rows((centered_two * gain_two + shift_two).astype(low))
    hidden = times(normed_two, up_matrix) + unit_bias
    activated, smooth_pull = jax.vjp(smooth, hidden)
    activated = activated.astype(low)
    result = (middle + (scatter_rows(times(activated, down_matrix)) + bias_down)).astype(low)

    down_back = times_flipped(upstream, down_matrix)
    grad_down = outer_sum(activated, upstream)
    hidden_back = smooth_pull(down_back)[0].astype(low)
    grad_up = outer_sum(normed_two, hidden_back)
    unit_sum = jnp.sum(hidden_back, axis=0, dtype=jnp.float32)
    normed_two_back = scatter_rows(times_flipped(hidden_back, up_matrix))
    upstream_own = lax.dynamic_slice_in_dim(upstream, mine, part).astype(jnp.float32)
    middle_back = upstream_own + norm_pull(normed_two_back, centered_two, inverse_two, gain_two)
    branch_own = middle_back.astype(low)
    branch_back = gather_rows(branch_own)
    mixed_back = times_flipped(branch_back, out_matrix).astype(low)
    grad_out = outer_sum(mixed, branch_back)
    mixed_back = split_heads(mixed_back)
    scores_again = scores_of(queries, keys, allowed)
    soft = jnp.exp(scores_again - log_total)
    soft_back = jnp.einsum("hqe,hke->hqk", mixed_back, values, preferred_element_type=jnp.float32)
    row_inner = jnp.sum(soft_back * soft, axis=-1, keepdims=True)
    score_back = (soft * (soft_back - row_inner)).astype(low)
    query_back = jnp.einsum(
        "hqk,hke->hqe", score_back, keys, preferred_element_type=jnp.float32
    ) * HD ** (-0.5)
    key_back = jnp.einsum(
        "hqk,hqe->hke", score_back, queries, preferred_element_type=jnp.float32
    ) * HD ** (-0.5)
    value_back = jnp.einsum(
        "hqk,hqe->hke", soft.astype(low), mixed_back, preferred_element_type=jnp.float32
    )
    heads_back = jnp.concatenate(
        [join_heads(each.astype(low)) for each in (query_back, key_back, value_back)], axis=1
    )
    heads_sum = jnp.sum(heads_back, axis=0, dtype=jnp.float32)
    normed_one_back = scatter_rows(times_flipped(heads_back, heads_matrix))
    grad_heads = outer_sum(normed_one, heads_back)
    centered_own = lax.dynamic_slice_in_dim(centered_one, mine, part)
    inverse_own = lax.dynamic_slice_in_dim(inverse_one, mine, part)
    input_back = middle_back + norm_pull(normed_one_back, centered_own, inverse_own, gain_one)

    def homeward(own):
        own = lax.all_to_all(own, "row", split_axis=1, concat_axis=0, tiled=True)
        return crossed(own, n_row)

    result_tokens = homeward(result)
    input_gradient = homeward(input_back.astype(low)).astype(jnp.float32)

    by_token = jnp.stack(
        [
            jnp.sum(normed_one_back * centered_own, axis=0),
            jnp.sum(normed_one_back, axis=0),
            jnp.sum(branch_own.astype(jnp.float32), axis=0),
            jnp.sum(normed_two_back * centered_two, axis=0),
            jnp.sum(normed_two_back, axis=0),
            jnp.sum(upstream_own, axis=0),
        ]
    )
    owned_rows = jnp.where(owned, heads_sum.reshape(3, window)[0::2], 0.0)
    by_unit = jnp.concatenate(
        [
            lax.dynamic_update_slice_in_dim(
                jnp.zeros((2, width), jnp.float32), owned_rows, row * step, axis=1
            ),
            lax.dynamic_update_slice_in_dim(
                jnp.zeros((4, width), jnp.float32), unit_sum.reshape(4, share), row * share, axis=1
            ),
        ]
    )
    sums = lax.psum(jnp.concatenate([by_token, by_unit]), ("dp", "row", "col"))
    pieces = share // n_dp
    inner = lax.axis_index("dp") * pieces
    col_sums = lax.dynamic_slice_in_dim(sums, lax.axis_index("col") * share + inner, pieces, axis=1)
    row_sums = lax.dynamic_slice_in_dim(sums, row * share + inner, pieces, axis=1)

    both = ("col", "dp")

    def to_owner(gradient):
        return lax.psum_scatter(gradient, both, scatter_dimension=0, tiled=True)

    got_heads = to_owner(grad_heads.astype(low)).reshape(pieces, 3, window)
    got_heads = jnp.where(owned, got_heads, jnp.zeros_like(got_heads))
    passed = lax.ppermute(got_heads[:, :, :edge], "row", to_last)
    got_heads = jnp.concatenate([got_heads, jnp.zeros_like(passed)], axis=2)
    got_heads = lax.dynamic_slice_in_dim(got_heads, edge - offset, share, axis=2)
    passed = jnp.concatenate([jnp.zeros((pieces, 3, share), low), passed, jnp.zeros_like(passed)], axis=2)
    got_heads = got_heads + lax.dynamic_slice_in_dim(passed, share - step + edge - offset, share, axis=2)
    low_out = jnp.where(owned[:, None], grad_out, 0.0).astype(low)
    passed = lax.ppermute(low_out[:edge], "row", to_last)
    low_out = jnp.concatenate([low_out, jnp.zeros_like(passed)])
    low_out = lax.dynamic_slice_in_dim(low_out, edge - offset, share)
    passed = jnp.concatenate([jnp.zeros((share, width), low), passed, jnp.zeros_like(passed)])
    low_out = low_out + lax.dynamic_slice_in_dim(passed, share - step + edge - offset, share)
    low_out = jnp.transpose(low_out.reshape(n_dp, pieces, n_col, share), (2, 0, 1, 3))
    got_out = to_owner(low_out.reshape(-1, share))
    got_up = to_owner(grad_up.astype(low))
    low_down = grad_down.astype(low).reshape(4, n_dp, pieces, n_col, share)
    low_down = jnp.transpose(low_down, (3, 1, 0, 2, 4)).reshape(-1, share)
    got_down = to_owner(low_down)

    reduced = [
        each.astype(jnp.float32).reshape(like.shape)
        for each, like in (
            (got_heads, w_heads),
            (got_out, w_out),
            (got_up, w_up),
            (got_down, w_down),
            (col_sums[0:2], norm_vectors),
            (col_sums[2:6], width_vectors),
            (row_sums[6:8], attend_bias),
            (row_sums[8:12], hidden_vectors),
        )
    ]
    heads_up = adam(w_heads, reduced[0], drift_heads, power_heads, 0.05, MATRIX_DECAY)
    out_up = adam(w_out, reduced[1], drift_out, power_out, 0.2, MATRIX_DECAY)
    up_up = adam(w_up, reduced[2], drift_up, power_up, 0.05, MATRIX_DECAY)
    down_up = adam(w_down, reduced[3], drift_down, power_down, 0.025, MATRIX_DECAY)
    norm_up = adam(norm_vectors, reduced[4], drift_norm, power_norm, 0.3, 0.0)
    width_up = adam(width_vectors, reduced[5], drift_width, power_width, 0.3, 0.0)
    attend_up = adam(attend_bias, reduced[6], drift_attend, power_attend, 0.3, 0.0)
    hidden_up = adam(hidden_vectors, reduced[7], drift_hidden, power_hidden, 0.3, 0.0)
    return (
        result_tokens,
        input_gradient,
        heads_up[0],
        heads_up[1],
        heads_up[2],
        out_up[0],
        out_up[1],
        out_up[2],
        up_up[0],
        up_up[1],
        up_up[2],
        down_up[0],
        down_up[1],
        down_up[2],
        norm_up[0],
        norm_up[1],
        norm_up[2],
        width_up[0],
        width_up[1],
        width_up[2],
        attend_up[0],
        attend_up[1],
        attend_up[2],
        hidden_up[0],
        hidden_up[1],
        hidden_up[2],
    )


def solution(mesh):
    return jax.shard_map(
        per_device,
        mesh=mesh,
        in_specs=(
            P(("dp", "row"), "col"),
            P(("dp", "row"), "col"),
            P("dp"),
            P("col", "dp", None, None, "row"),
            P("row", "dp", None, "col"),
            P("col", "dp", None, None, "row"),
            P(None, "row", "dp", None, "col"),
            P(None, "col", "dp", None),
            P(None, "col", "dp", None),
            P(None, "row", "dp", None),
            P(None, "row", "dp", None),
            P("col", "dp", None, None, "row"),
            P("row", "dp", None, "col"),
            P("col", "dp", None, None, "row"),
            P(None, "row", "dp", None, "col"),
            P(None, "col", "dp", None),
            P(None, "col", "dp", None),
            P(None, "row", "dp", None),
            P(None, "row", "dp", None),
            P("col", "dp", None, None, "row"),
            P("row", "dp", None, "col"),
            P("col", "dp", None, None, "row"),
            P(None, "row", "dp", None, "col"),
            P(None, "col", "dp", None),
            P(None, "col", "dp", None),
            P(None, "row", "dp", None),
            P(None, "row", "dp", None),
        ),
        out_specs=(
            P(("dp", "row"), "col"),
            P(("dp", "row"), "col"),
            P("col", "dp", None, None, "row"),
            P("col", "dp", None, None, "row"),
            P("col", "dp", None, None, "row"),
            P("row", "dp", None, "col"),
            P("row", "dp", None, "col"),
            P("row", "dp", None, "col"),
            P("col", "dp", None, None, "row"),
            P("col", "dp", None, None, "row"),
            P("col", "dp", None, None, "row"),
            P(None, "row", "dp", None, "col"),
            P(None, "row", "dp", None, "col"),
            P(None, "row", "dp", None, "col"),
            P(None, "col", "dp", None),
            P(None, "col", "dp", None),
            P(None, "col", "dp", None),
            P(None, "col", "dp", None),
            P(None, "col", "dp", None),
            P(None, "col", "dp", None),
            P(None, "row", "dp", None),
            P(None, "row", "dp", None),
            P(None, "row", "dp", None),
            P(None, "row", "dp", None),
            P(None, "row", "dp", None),
            P(None, "row", "dp", None),
        ),
        check_vma=False,
    )
```

```python
import functools

import jax
import jax.numpy as jnp
from jax import lax
from jax.experimental import pallas as pl
from jax.experimental.pallas import tpu as pltpu
from jax.sharding import PartitionSpec as P

HEADS = 25
HD = 64
TOK_DEV = 128
STEP = 10


NORM_EPSILON = 1e-05
BETA_FIRST = 0.9
BETA_SECOND = 0.999
ADAM_EPSILON = 1e-08
MATRIX_DECAY = 0.1
MASKED = -1e30
ROOT = (2.0 / 3.141592653589793) ** 0.5
CUBIC = 0.044715
VMEM_BYTES = 66 * 1024 * 1024


def ceil_to(count, unit):
    return -(-count // unit) * unit


class Sizes:
    def __init__(self, share, pieces, seq):
        self.share = share
        self.pieces = pieces
        self.block = ceil_to(pieces, 16)
        self.pair = 2 * self.block
        self.width = 4 * self.pair
        self.seq = seq
        self.part = seq // 4
        self.both = 2 * seq
        self.main = (HEADS // 4) * HD
        self.slack = share - self.main
        self.heads = ceil_to(3 * share, 256)
        self.mixed = ceil_to(pieces + 1, 128)
        self.hidden = ceil_to(4 * pieces + 1, 128)
        self.tiles = self.width // 128


class Place:
    def __init__(self):
        self.d, self.r, self.c = (lax.axis_index(name) for name in ("dp", "row", "col"))
        self.y, self.k = self.r // 2, self.r % 2

    def plane(self, mask):
        d = 1 - self.d if mask & 4 else self.d
        y = 1 - self.y if mask & 2 else self.y
        k = 1 - self.k if mask & 1 else self.k
        return d, 2 * y + k

    def peer(self, mask):
        d, r = self.plane(mask)
        return (d, r, self.c)

    def along(self, c):
        return (self.d, self.r, c)


def run(when, action):
    if when is None:
        action()
    else:
        pl.when(when)(action)


class Wires:
    def __init__(self, sends, arrivals):
        self.sends, self.arrivals = sends, arrivals
        self.used = 0
        self.open = []

    def make(self, source, target, index, slot, device):
        return pltpu.make_async_remote_copy(
            src_ref=source,
            dst_ref=target,
            send_sem=self.sends.at[index],
            recv_sem=self.arrivals.at[slot],
            device_id=device,
            device_id_type=pl.DeviceIdType.MESH,
        )

    def copy(self, source, target, device, slot, when=None):
        made = self.make(source, target, self.used, slot, device)
        self.used += 1
        run(when, made.start)
        item = (when, made)
        self.open.append(item)
        return item

    def arrived(self, target, slot, device, when=None):
        run(when, self.make(target, target, 0, slot, device).wait_recv)

    def close(self, some=None):
        for item in self.open if some is None else some:
            run(item[0], item[1].wait_send)
        self.open = [] if some is None else [o for o in self.open if all(o is not s for s in some)]


def greet(at, diagonal):
    barrier = pltpu.get_barrier_semaphore()

    def signal(device):
        pl.semaphore_signal(
            barrier, inc=1, device_id=device, device_id_type=pl.DeviceIdType.MESH
        )

    for mask in range(1, 8):
        signal(at.peer(mask))
    for c in range(4):
        run(at.c != c, functools.partial(signal, (at.d, at.r, c)))
        if diagonal:
            run(at.c != c, functools.partial(signal, (1 - at.d, at.r, c)))
    run(at.r != at.c, functools.partial(signal, (at.d, at.c, at.r)))
    pl.semaphore_wait(barrier, (13 if diagonal else 10) + jnp.where(at.r != at.c, 1, 0))


def rows_at(start, size):
    return pl.ds(pl.multiple_of(start, 16), size)


def lanes_at(start, size):
    return pl.ds(pl.multiple_of(start, 128), size)


def choose(shape, source):
    rows = lax.broadcasted_iota(jnp.int32, shape, 0)
    wanted = source(lax.broadcasted_iota(jnp.int32, shape, 1))
    return (rows == wanted).astype(jnp.bfloat16)


def edge_source(column):
    part, place = column // HD, column % HD
    wanted = jnp.where(place >= 16, 128 * part + place - 16, 384 + 16 * part + place)
    return jnp.where(part < 3, wanted, -1)


def spread_source(column):
    part, place = column // 128, column % 128
    return jnp.where(place < HD, HD * part + place, -1)


def picked(values, table):
    return jnp.dot(values, table, preferred_element_type=jnp.float32).astype(jnp.bfloat16)


def times(left, right):
    return jnp.dot(left, right, preferred_element_type=jnp.float32)


def times_flipped(left, right):
    return lax.dot_general(
        left, right, (((1,), (1,)), ((), ())), preferred_element_type=jnp.float32
    )


def times_outer(left, right):
    return lax.dot_general(
        left, right, (((0,), (0,)), ((), ())), preferred_element_type=jnp.float32
    )


def over_tiles(total, action, tile=256):
    @pl.loop(0, total // tile)
    def _(i):
        action(i * tile, tile)

    if total % tile:
        action(total - total % tile, total % tile)


def turned(values):
    return values.astype(jnp.float32).T


def gather_group(wires, masks, region, at, base):
    own = region(*at.plane(0))
    sent = [wires.copy(own, own, at.peer(mask), base + mask) for mask in (1, *masks)]

    def finish():
        for mask in masks:
            there = region(*at.plane(mask))
            wires.arrived(there, base + mask, at.peer(mask))
            sent.append(wires.copy(there, there, at.peer(1), base + mask + 1))
        for mask in (0, *masks):
            there = region(*at.plane(mask | 1))
            wires.arrived(there, base + (mask | 1), at.peer(1))

    return finish, sent


def scatter_group(wires, masks, partial, chunk, near, mid, far, at, base):
    sent = []
    for i, mask in enumerate((0, *masks)):
        rows = rows_at(chunk(*at.plane(mask | 1)), near.shape[1])
        sent.append(wires.copy(partial.at[rows], near.at[i], at.peer(1), base + i))

    def rows_of(mask):
        return rows_at(chunk(*at.plane(mask)), near.shape[1])

    def onward():
        for i, mask in enumerate((0, *masks)):
            wires.arrived(near.at[i], base + i, at.peer(1))
        for i, mask in enumerate(masks):
            both = partial[rows_of(mask)].astype(jnp.float32) + near[i + 1].astype(jnp.float32)
            mid[i] = both.astype(jnp.bfloat16)
            sent.append(wires.copy(mid.at[i], far.at[i], at.peer(mask), base + 4 + i))

    def total():
        for i, mask in enumerate(masks):
            wires.arrived(far.at[i], base + 4 + i, at.peer(mask))
        result = partial[rows_of(0)].astype(jnp.float32) + near[0].astype(jnp.float32)
        for i in range(len(masks)):
            result = result + far[i].astype(jnp.float32)
        return result

    return onward, total, sent


def spread_col(wires, region, at, base):
    own = region(at.c)
    for c in range(4):
        other = (at.c != c) & (at.c + c != 3 if c in (0, 3) else at.c != c)
        wires.copy(own, own, at.along(c), base + at.c, other)

    def relay():
        for here, start, end in ((2, 0, 3), (1, 3, 0)):
            block = region(start)
            wires.arrived(block, base + start, at.along(start), at.c == here)
            wires.copy(block, block, at.along(end), base + start, at.c == here)

    def finish():
        for c in range(4):
            needed = at.c != c
            if c == 0:
                needed = needed & (at.c != 2)
            if c == 3:
                needed = needed & (at.c != 1)
            wires.arrived(region(c), base + c, at.along(c), needed)

    return relay, finish


def forward_kernel(
    sz,
    x_home,
    dy_home,
    wh_own,
    wo_own,
    wu_own,
    wd_own,
    vec_own,
    row_labels,
    col_labels,
    wh,
    wo,
    wu,
    wd,
    h1_t,
    h2_t,
    dy_t,
    dy,
    u,
    gl,
    qw,
    kw,
    vw,
    a_nat,
    lse,
    x2,
    x_own,
    vec_rows,
    x_t,
    h1,
    h2,
    own_qkv,
    aw,
    vec,
    part,
    edge_out,
    edge_in,
    edge_back,
    near,
    mid,
    far,
    sends,
    arrivals,
    locals_,
):
    at = Place()
    wires = Wires(sends, arrivals)
    low = jnp.bfloat16
    pair, block = sz.pair, sz.block
    greet(at, False)

    def x_block(d, r):
        return x_t.at[rows_at(pair * r, pair)]

    def dy_block(d, r):
        return dy_t.at[rows_at(pair * r, pair), lanes_at(sz.seq * d, sz.seq)]

    across = (at.d, at.c, at.r)
    same = at.r == at.c
    stay = []

    def keep(source, target, when=None):
        made = pltpu.make_async_copy(source, target, locals_.at[len(stay)])
        run(when, made.start)
        stay.append((when, made))

    wires.copy(x_home, x_block(at.d, at.c), across, 0, jnp.logical_not(same))
    keep(x_home, x_block(at.d, at.c), same)
    vec_all = []

    def vec_block(d, c):
        return vec.at[rows_at(pair * c + block * d, block)]

    keep(vec_own, vec_block(at.d, at.c))
    for c in range(4):
        wires.copy(vec_own, vec_block(at.d, at.c), at.along(c), 2 + at.c, at.c != c)
    wires.copy(vec_own, vec_block(at.d, at.c), at.peer(4), 6 + at.c)

    def wh_block(d):
        return lambda c: wh.at[rows_at(pair * c + block * d, block)]

    def wo_block(d):
        return lambda c: wo.at[rows_at(pair * c, pair), lanes_at(sz.mixed * d, sz.mixed)]

    def wu_block(d):
        return lambda c: wu.at[rows_at(pair * c + block * d, block)]

    def wd_block(half):
        return lambda c: wd.at[rows_at(pair * c + block * half, block)]

    keep(wh_own, wh_block(at.d)(at.c))
    keep(wo_own, wo_block(at.d)(at.c))
    keep(wu_own.at[:, lanes_at(sz.hidden * at.d, sz.hidden)], wu_block(at.d)(at.c))
    keep(wd_own, wd.at[rows_at(pair * at.c, pair)])
    wires.copy(
        wu_own.at[:, lanes_at(sz.hidden * (1 - at.d), sz.hidden)],
        wu_block(at.d)(at.c),
        at.peer(4),
        10,
    )
    for when, made in stay:
        run(when, made.wait)
    wires.arrived(x_block(at.d, at.r), 0, across, jnp.logical_not(same))
    x_done, _ = gather_group(wires, (2,), x_block, at, 12)
    wh_relay, wh_done = spread_col(wires, wh_block(at.d), at, 20)
    wires.copy(wh_block(at.d)(at.c), wh_block(at.d)(at.c), at.peer(4), 24 + at.c)
    wo_relay, wo_done = spread_col(wires, wo_block(at.d), at, 28)
    wires.copy(wo_block(at.d)(at.c), wo_block(at.d)(at.c), at.peer(4), 32 + at.c)
    x_done()

    for c in range(4):
        wires.arrived(vec_block(at.d, c), 2 + c, at.along(c), at.c != c)
    wires.arrived(vec_block(1 - at.d, at.c), 6 + at.c, at.peer(4))
    for step in range(1, 4):
        there = (at.c + step) % 4
        wires.copy(
            vec_block(at.d, there), vec_block(at.d, there), at.peer(4), 6 + there
        )
    for step in range(1, 4):
        there = (at.c + step) % 4
        wires.arrived(vec_block(1 - at.d, there), 6 + there, at.peer(4))
    features = 4.0 * sz.share

    def add_up(i, carry):
        rows = rows_at(128 * i, 128)
        value = x_t[rows].astype(jnp.float32)
        return (
            carry[0] + jnp.sum(value, axis=0, keepdims=True),
            carry[1] + jnp.sum(value * value, axis=0, keepdims=True),
        )

    zero = jnp.zeros((1, sz.seq), jnp.float32)
    sums = lax.fori_loop(0, sz.tiles, add_up, (zero, zero))
    center = sums[0] / features
    inverse = lax.rsqrt(sums[1] / features - center * center + NORM_EPSILON)

    @pl.loop(0, sz.tiles)
    def _(i):
        rows, lanes = rows_at(128 * i, 128), lanes_at(128 * i, 128)
        vectors = vec[rows].astype(jnp.float32)
        value = (x_t[rows].astype(jnp.float32) - center) * inverse
        value = value * vectors[:, 0:1] + vectors[:, 1:2]
        h1_t[rows] = value.astype(low)
        h1[:, lanes] = value.T.astype(low)
        mine = x_t[rows, lanes_at(sz.part * at.r, sz.part)]
        x_own[:, lanes] = turned(mine).astype(low)
        vec_rows[:, lanes] = vectors.T[0:8]

    wh_relay()
    for c in range(4):
        needed = at.c != c
        if c == 0:
            needed = needed & (at.c != 2)
        if c == 3:
            needed = needed & (at.c != 1)
        wires.arrived(wh_block(at.d)(c), 20 + c, at.along(c), needed)
        wires.copy(wh_block(at.d)(c), wh_block(at.d)(c), at.peer(4), 24 + c, at.c != c)

    wu_first, wu_first_done = spread_col(wires, wu_block(at.d), at, 36)
    wires.arrived(wu_block(1 - at.d)(at.c), 10, at.peer(4))
    wu_second, wu_second_done = spread_col(wires, wu_block(1 - at.d), at, 40)
    for c in range(4):
        wires.arrived(wh_block(1 - at.d)(c), 24 + c, at.peer(4))

    @pl.loop(0, sz.heads // 256)
    def _(i):
        lanes = lanes_at(256 * i, 256)
        own_qkv[:, lanes] = times(h1[...], wh[:, lanes]).astype(low)

    wires.copy(dy_home, dy_block(at.d, at.c), across, 1, jnp.logical_not(same))
    made = pltpu.make_async_copy(dy_home, dy_block(at.d, at.c), locals_.at[len(stay)])
    run(same, made.start)
    run(same, made.wait)

    starts = (0, sz.main, 2 * sz.main, 3 * sz.main)
    ends = jnp.concatenate([own_qkv[:, s : s + 128] for s in starts], axis=1)
    edge_out[...] = picked(ends, choose((512, 256), edge_source))
    last = at.r == 3

    @pl.when(at.r == 0)
    def _():
        edge_in[...] = jnp.zeros_like(edge_in)

    wires.copy(edge_out, edge_in, (at.d, at.r + 1, at.c), 52, at.r < 3)
    spread = choose((256, 384), spread_source)
    extra = picked(edge_out[...], spread)
    wires.arrived(edge_in, 52, (at.d, at.r - 1, at.c), at.r > 0)
    first = picked(edge_in[...], spread)
    lane = lax.broadcasted_iota(jnp.int32, (sz.seq, 128), 1)
    for i, target in enumerate((qw, kw, vw)):
        start = starts[i]
        target[:, 0:128] = jnp.where(
            lane < sz.slack * at.r,
            first[:, 128 * i : 128 * i + 128],
            own_qkv[:, start : start + 128],
        )
        target[:, 128 : sz.main] = own_qkv[:, start + 128 : start + sz.main]
        target[:, sz.main : sz.main + 128] = extra[:, 128 * i : 128 * i + 128]

    wo_relay()
    for c in range(4):
        needed = at.c != c
        if c == 0:
            needed = needed & (at.c != 2)
        if c == 3:
            needed = needed & (at.c != 1)
        wires.arrived(wo_block(at.d)(c), 28 + c, at.along(c), needed)
        wires.copy(wo_block(at.d)(c), wo_block(at.d)(c), at.peer(4), 32 + c, at.c != c)

    wires.arrived(dy_block(at.d, at.r), 1, across, jnp.logical_not(same))
    dy_done, _ = gather_group(wires, (2, 4, 6), dy_block, at, 56)

    half = sz.seq // 2

    def heads_of(p, count):
        tile = lanes_at(128 * p, 128)
        for q in range(2):
            rows = slice(half * q, half * (q + 1))
            keys = half * (q + 1)
            order = lax.broadcasted_iota(jnp.int32, (half, keys), 0) + half * q
            allowed = (col_labels[rows, :] == row_labels[:, 0:keys]) & (
                order >= lax.broadcasted_iota(jnp.int32, (half, keys), 1)
            )
            lanes = lax.broadcasted_iota(jnp.int32, (half, 128), 1)
            side = lanes // HD
            total = jnp.zeros((half, 128), jnp.float32)
            for h in range(count):
                queries = jnp.where(side == h, qw[rows, tile].astype(jnp.float32) * HD ** (-0.5), 0.0)
                scores = times_flipped(queries.astype(low), kw[0:keys, tile])
                scores = jnp.where(allowed, scores, MASKED)
                highest = jnp.max(scores, axis=1, keepdims=True)
                raised = jnp.exp(scores - highest)
                summed = jnp.sum(raised, axis=1, keepdims=True)
                found = highest + jnp.log(summed)
                lse[rows, :] = jnp.where(lanes == 2 * p + h, found, lse[rows, :])
                soft = (raised * (1.0 / summed)).astype(low)
                total = jnp.where(side == h, times(soft, vw[0:keys, tile]), total)
            aw[rows, tile] = total.astype(low)

    lse[...] = jnp.zeros_like(lse)

    @pl.loop(0, sz.main // 128)
    def _(p):
        heads_of(p, 2)

    @pl.when(last)
    def _():
        heads_of(sz.main // 128, 1)
        edge_back[...] = aw[:, sz.main : sz.main + 128]

    wires.copy(aw.at[:, 0:128], edge_back, (at.d, at.r - 1, at.c), 53, at.r > 0)
    wd_first, wd_first_done = spread_col(wires, wd_block(0), at, 44)
    wd_second, wd_second_done = spread_col(wires, wd_block(1), at, 48)
    wu_first()
    wires.arrived(edge_back, 53, (at.d, at.r + 1, at.c), at.r < 3)

    def natural(column):
        inner = column % sz.mixed
        place = sz.pieces * (column // sz.mixed) + inner + sz.slack * at.r
        return jnp.where(inner < sz.pieces, place, -1)

    def natural_main(column):
        place = natural(column)
        return jnp.where(place < sz.main, place, -1)

    def natural_edge(column):
        return natural(column) - sz.main

    mixed = times(aw[:, 0 : sz.main], choose((sz.main, 2 * sz.mixed), natural_main))
    mixed = mixed + times(edge_back[...], choose((128, 2 * sz.mixed), natural_edge))
    ones = lax.broadcasted_iota(jnp.int32, mixed.shape, 1) % sz.mixed == sz.pieces
    a_nat[...] = jnp.where(ones, 1.0, mixed).astype(low)
    for c in range(4):
        wires.arrived(wo_block(1 - at.d)(c), 32 + c, at.peer(4))

    def project(start, tile):
        out = times_flipped(a_nat[...], wo[rows_at(start, tile)])
        part[:, lanes_at(start, tile)] = out.astype(low)

    over_tiles(sz.width, project)

    onward, total, _ = scatter_group(
        wires, (2,), part, lambda d, r: sz.part * r, near, mid, far, at, 64
    )
    onward()
    wu_second()
    middle = x_own[...].astype(jnp.float32) + total()
    x2[...] = middle
    center = jnp.sum(middle, axis=1, keepdims=True) / features
    spread_two = jnp.sum(middle * middle, axis=1, keepdims=True) / features - center * center
    normed = (middle - center) * lax.rsqrt(spread_two + NORM_EPSILON)
    own_rows = rows_at(sz.part * (4 * at.d + at.r), sz.part)
    h2[own_rows] = (normed * vec_rows[2:3] + vec_rows[3:4]).astype(low)
    h2_done, _ = gather_group(
        wires, (2, 4, 6), lambda d, r: h2.at[rows_at(sz.part * (4 * d + r), sz.part)], at, 72
    )
    dy_done()
    wd_first()

    @pl.loop(0, sz.tiles)
    def _(i):
        dy[:, lanes_at(128 * i, 128)] = turned(dy_t[rows_at(128 * i, 128)]).astype(low)

    h2_done()
    wu_first_done()
    wu_second_done()

    def expand(start, tile):
        lanes = lanes_at(start, tile)
        value = times(h2[...], wu[:, lanes])
        u[:, lanes] = value
        inner = jnp.tanh(ROOT * (value + CUBIC * value * value * value))
        value = 0.5 * value * (1.0 + inner)
        column = lax.broadcasted_iota(jnp.int32, value.shape, 1) + start
        gl[:, lanes] = jnp.where(column == 4 * sz.pieces, 1.0, value).astype(low)

    over_tiles(sz.hidden, expand)

    wd_second()

    @pl.loop(0, sz.tiles)
    def _(i):
        h2_t[rows_at(128 * i, 128)] = turned(h2[:, lanes_at(128 * i, 128)]).astype(low)

    wd_first_done()
    wd_second_done()
    wires.close()


def backward_kernel(
    sz,
    dy_all,
    dy_t_all,
    u_all,
    gl_all,
    h2_t_all,
    wd_all,
    wu_all,
    wo_all,
    wh_all,
    h1_t_all,
    qw,
    kw,
    vw,
    a_nat,
    lse,
    x2,
    x_own,
    vec_rows,
    row_labels,
    col_labels,
    zd,
    zu,
    zo,
    zh,
    result_home,
    grad_home,
    vec_sums,
    dy,
    dy_t,
    u,
    gl,
    h2_t,
    wd,
    wu,
    wo,
    wh,
    dy_own,
    du,
    gw,
    gu,
    go,
    xh,
    xo,
    near_two,
    far_two,
    near_res,
    far_res,
    near_one,
    far_one,
    mid,
    dob,
    da,
    dqw,
    dkw,
    dvw,
    dk_sum,
    dv_sum,
    dx2,
    edge_out,
    edge_in,
    fore_out,
    fore_in,
    stage,
    home,
    home_two,
    va,
    vb,
    sends,
    arrivals,
    locals_,
):
    at = Place()
    wires = Wires(sends, arrivals)
    low = jnp.bfloat16
    pair, block = sz.pair, sz.block
    features = 4.0 * sz.share
    used = [0]

    def load(source, target, when=None):
        made = pltpu.make_async_copy(source, target, locals_.at[used[0]])
        used[0] += 1
        run(when, made.start)
        return made

    own_rows = rows_at(sz.part * (4 * at.d + at.r), sz.part)
    loads = [
        load(s, t)
        for s, t in (
            (dy_t_all, dy_t),
            (gl_all, gl),
            (dy_all, dy),
            (wd_all, wd),
            (u_all, u),
            (dy_all.at[own_rows], dy_own),
            (wu_all, wu),
            (h2_t_all, h2_t),
            (wo_all, wo),
            (wh_all, wh),
        )
    ]
    greet(at, True)
    stay = []

    gd = gw.at[:, 0 : sz.hidden]
    loads[0].wait()
    loads[1].wait()
    for step in (2, 1, 3, 0):
        there = (at.c + step) % 4
        rows = rows_at(pair * there, pair)
        gw[rows, 0 : sz.hidden] = times(dy_t[rows], gl[...]).astype(low)
        if step:
            wires.copy(gd.at[rows], zd.at[at.c], at.along(there), at.c)
        else:
            stay.append(load(gd.at[rows], zd.at[at.c]))
    gd_sends, gd_stay = list(wires.open), list(stay)

    for made in loads[2:6]:
        made.wait()

    def through(start, tile):
        lanes = lanes_at(start, tile)
        upstream = times(dy[...], wd[:, lanes])
        value = u[:, lanes]
        inner = jnp.tanh(ROOT * (value + CUBIC * value * value * value))
        slope = 0.5 * (1.0 + inner) + 0.5 * value * (1.0 - inner * inner) * ROOT * (
            1.0 + 3.0 * CUBIC * value * value
        )
        du[:, lanes] = (upstream * slope).astype(low)

    over_tiles(sz.hidden, through)
    loads[6].wait()

    def back_up(start, tile):
        dy[:, lanes_at(start, tile)] = times_flipped(du[...], wu[rows_at(start, tile)]).astype(low)

    over_tiles(sz.width, back_up)

    def chunk_both(d, r):
        return sz.part * (4 * d + r)

    two_onward, two_total, two_sent = scatter_group(
        wires, (2, 4, 6), dy, chunk_both, near_two, mid, far_two, at, 16
    )
    loads[7].wait()
    for step in (2, 1, 3, 0):
        there = (at.c + step) % 4
        rows = rows_at(pair * there, pair)
        gu[rows] = times(h2_t[rows], du[...]).astype(low)
        if step == 2:
            two_onward()
        mine = gu.at[rows_at(pair * there + block * at.d, block)]
        other = gu.at[rows_at(pair * there + block * (1 - at.d), block)]
        slot = 2 * at.c + at.d
        if step:
            wires.copy(mine, zu.at[slot], at.along(there), 4 + slot)
        else:
            stay.append(load(mine, zu.at[slot]))
        wires.copy(other, zu.at[slot], (1 - at.d, at.r, there), 4 + slot)

    def norm_back(upstream, values, gain):
        center = jnp.sum(values, axis=1, keepdims=True) / features
        spread = jnp.sum(values * values, axis=1, keepdims=True) / features - center * center
        inverse = lax.rsqrt(spread + NORM_EPSILON)
        centered = (values - center) * inverse
        scaled = upstream * gain
        inner = (
            scaled
            - jnp.sum(scaled, axis=1, keepdims=True) / features
            - centered * (jnp.sum(scaled * centered, axis=1, keepdims=True) / features)
        )
        return (
            inner * inverse,
            jnp.sum(upstream * centered, axis=0, keepdims=True),
            jnp.sum(upstream, axis=0, keepdims=True),
        )

    h2_back = two_total()
    through_norm, gain_two, shift_two = norm_back(h2_back, x2[...], vec_rows[2:3])
    middle_back = dy_own[...].astype(jnp.float32) + through_norm
    dx2[...] = middle_back
    va[0, 2:3] = gain_two
    va[0, 3:4] = shift_two
    va[0, 4:8] = jnp.zeros((4, sz.width), jnp.float32)
    dob[rows_at(sz.part * at.r, sz.part)] = middle_back.astype(low)
    dob_done, dob_sent = gather_group(
        wires, (2,), lambda d, r: dob.at[rows_at(sz.part * r, sz.part)], at, 24
    )
    h1_load = load(h1_t_all, dy_t.at[:, 0 : sz.seq])

    def contract(start, tile):
        out = times_flipped(gl[...], wd[rows_at(start, tile)])
        dy[:, lanes_at(start, tile)] = out.astype(low)

    wires.close(two_sent)
    over_tiles(sz.width, contract)
    res_onward, res_total, res_sent = scatter_group(
        wires, (2, 4, 6), dy, chunk_both, near_res, mid, far_res, at, 32
    )

    dob_done()
    loads[8].wait()
    da[...] = times(dob[...], wo[...]).astype(low)
    slack, main = sz.slack, sz.main

    def from_natural(place):
        wanted = sz.mixed * (place // sz.pieces) + place % sz.pieces
        return jnp.where((place >= 0) & (place < sz.share), wanted, -1)

    fore_out[...] = picked(
        da[...], choose((2 * sz.mixed, 128), lambda j: from_natural(j + main - slack * at.r))
    )

    @pl.when(at.r == 0)
    def _():
        fore_in[...] = jnp.zeros_like(fore_in)

    wires.copy(fore_out, fore_in, (at.d, at.r + 1, at.c), 40, at.r < 3)

    @pl.loop(0, sz.tiles)
    def _(i):
        dy_t[rows_at(128 * i, 128), sz.seq : sz.both] = turned(dob[:, lanes_at(128 * i, 128)]).astype(low)

    res_onward()

    for step in range(4):
        there = (at.c + step) % 4
        rows = rows_at(pair * there, pair)
        go[rows] = times(dy_t[rows, sz.seq : sz.both], a_nat[...]).astype(low)
        wires.copy(
            go.at[rows, lanes_at(sz.mixed * (1 - at.d), sz.mixed)], xo.at[there], at.peer(4), 48 + there
        )
    wires.arrived(fore_in, 40, (at.d, at.r - 1, at.c), at.r > 0)
    window = times(da[...], choose((2 * sz.mixed, main), lambda j: from_natural(j - slack * at.r)))
    da_first = window[:, 0:128] + fore_in[...].astype(jnp.float32)
    da[:, 128:main] = window[:, 128:main].astype(low)
    da[:, 0:128] = da_first.astype(low)
    da[:, main : main + 128] = fore_out[...]

    half = sz.seq // 2

    def heads_back(p, count):
        tile = lanes_at(128 * p, 128)
        dk_sum[...] = jnp.zeros_like(dk_sum)
        dv_sum[...] = jnp.zeros_like(dv_sum)
        for q in range(2):
            rows = slice(half * q, half * (q + 1))
            keys = half * (q + 1)
            order = lax.broadcasted_iota(jnp.int32, (half, keys), 0) + half * q
            allowed = (col_labels[rows, :] == row_labels[:, 0:keys]) & (
                order >= lax.broadcasted_iota(jnp.int32, (half, keys), 1)
            )
            lanes = lax.broadcasted_iota(jnp.int32, (half, 128), 1)
            side = lanes // HD
            total = jnp.zeros((half, 128), jnp.float32)
            for h in range(count):
                queries = jnp.where(side == h, qw[rows, tile].astype(jnp.float32) * HD ** (-0.5), 0.0)
                queries = queries.astype(low)
                pulled = jnp.where(side == h, da[rows, tile].astype(jnp.float32), 0.0).astype(low)
                found = jnp.sum(jnp.where(lanes == 2 * p + h, lse[rows, :], 0.0), axis=1, keepdims=True)
                scores = times_flipped(queries, kw[0:keys, tile])
                soft = jnp.where(allowed, jnp.exp(jnp.where(allowed, scores - found, MASKED)), 0.0)
                soft_back = times_flipped(pulled, vw[0:keys, tile])
                inner = jnp.sum(soft_back * soft, axis=1, keepdims=True)
                score_back = (soft * (soft_back - inner)).astype(low)
                piece = times(score_back, kw[0:keys, tile]) * HD ** (-0.5)
                total = jnp.where(side == h, piece, total)
                dk_sum[0:keys] += times_outer(score_back, queries)
                dv_sum[0:keys] += times_outer(soft.astype(low), pulled)
            dqw[rows, tile] = total.astype(low)
        dkw[:, tile] = dk_sum[...].astype(low)
        dvw[:, tile] = dv_sum[...].astype(low)

    @pl.loop(0, main // 128)
    def _(p):
        heads_back(p, 2)

    @pl.when(at.r == 3)
    def _():
        heads_back(main // 128, 1)

    def compact(column):
        part, place = column // HD, column % HD
        return jnp.where(part < 3, 128 * part + place, -1)

    table = choose((384, 256), compact)
    backs = (dqw, dkw, dvw)
    edge_out[...] = picked(jnp.concatenate([b[:, 0:128] for b in backs], axis=1), table)
    wires.copy(edge_out, edge_in, (at.d, at.r - 1, at.c), 41, at.r > 0)

    @pl.when(at.r == 3)
    def _():
        edge_in[...] = picked(jnp.concatenate([b[:, main : main + 128] for b in backs], axis=1), table)

    for c in range(4):
        wires.arrived(xo.at[c], 48 + c, at.peer(4))
    for step in (2, 1, 3, 0):
        there = (at.c + step) % 4
        rows = rows_at(pair * there, pair)
        both = go[rows, lanes_at(sz.mixed * at.d, sz.mixed)].astype(jnp.float32) + xo[there].astype(jnp.float32)
        xo[there] = both.astype(low)
        if step:
            wires.copy(xo.at[there], zo.at[at.c], at.along(there), 52 + at.c)
        else:
            stay.append(load(xo.at[there], zo.at[at.c]))
    wires.arrived(edge_in, 41, (at.d, at.r + 1, at.c), at.r < 3)

    def unfold(column):
        tile, lane = column // 128, column % 128
        inside = jnp.where(lane < HD - 16, HD * tile + lane + 16, -1)
        tail = jnp.where(lane < 48, HD * (lane // 16) + lane % 16, -1)
        return jnp.where(tile < 3, inside, tail)

    edges = picked(edge_in[...], choose((256, 512), unfold))
    lane = lax.broadcasted_iota(jnp.int32, (sz.seq, 128), 1)
    pieces = []
    for i, back in enumerate(backs):
        first = jnp.where(lane < slack * at.r, edges[:, 128 * i : 128 * i + 128], back[:, 0:128])
        pieces += [first, back[:, 128:main]]
    pieces.append(edges[:, 384:512])
    wires.close(dob_sent)
    own_back = dob.at[:, 0 : sz.heads]
    own_back[...] = jnp.concatenate(pieces, axis=1)

    def go_home(values, base, out, home, stage):
        for r in range(4):
            stage[r] = values[:, pair * r : pair * (r + 1)].astype(low)
        mine = rows_at(sz.part * at.r, sz.part)
        sent = []
        for r in range(4):
            sent.append(
                wires.copy(stage.at[r], home.at[mine], (at.d, r, at.c), base + at.r, at.r != r)
            )

            @pl.when(at.r == r)
            def _():
                home[mine] = stage[r]

        for r in range(4):
            rows = home.at[sz.part * r : sz.part * (r + 1)]
            wires.arrived(rows, base + r, (at.d, r, at.c), at.r != r)
        sent.append(wires.copy(home, out, (at.d, at.c, at.r), base + 4, at.r != at.c))
        made = load(home, out, at.r == at.c)
        run(at.r == at.c, made.wait)
        return sent

    result = x2[...] + res_total()
    wires.close(res_sent)
    res_home = go_home(result, 56, result_home, home, stage)

    for made in loads[9:10]:
        made.wait()

    def back_in(start, tile):
        out = times_flipped(own_back[...], wh[rows_at(start, tile)])
        dy[0 : sz.seq, lanes_at(start, tile)] = out.astype(low)

    over_tiles(sz.width, back_in)
    one_onward, one_total, _ = scatter_group(
        wires, (2,), dy, lambda d, r: sz.part * r, near_one, mid, far_one, at, 64
    )
    h1_load.wait()
    wires.close(gd_sends)
    for made in gd_stay:
        made.wait()
        stay.remove(made)
    for step in range(4):
        there = (at.c + step) % 4
        rows = rows_at(pair * there, pair)
        gw[rows] = times(dy_t[rows, 0 : sz.seq], own_back[...]).astype(low)
        if step == 0:
            one_onward()
        other = gw.at[rows_at(pair * there + block * (1 - at.d), block)]
        wires.copy(other, xh.at[there], at.peer(4), 72 + there)
    for step in (2, 1, 3, 0):
        there = (at.c + step) % 4
        wires.arrived(xh.at[there], 72 + there, at.peer(4))
        mine = rows_at(pair * there + block * at.d, block)
        both = gw[mine].astype(jnp.float32) + xh[there].astype(jnp.float32)
        xh[there] = both.astype(low)
        if step:
            wires.copy(xh.at[there], zh.at[at.c], at.along(there), 76 + at.c)
        else:
            stay.append(load(xh.at[there], zh.at[at.c]))

    h1_back = one_total()
    through_norm, gain_one, shift_one = norm_back(
        h1_back, x_own[...].astype(jnp.float32), vec_rows[0:1]
    )
    va[0, 0:1] = gain_one
    va[0, 1:2] = shift_one
    for mask in range(1, 8):
        wires.copy(va.at[0], va.at[mask], at.peer(mask), 80 + mask)
    grad = dx2[...] + through_norm
    wires.close(res_home)
    go_home(grad, 92, grad_home, home_two, stage)
    for mask in range(1, 8):
        wires.arrived(va.at[mask], 80 + mask, at.peer(mask))
    vb[at.c] = functools.reduce(lambda a, b: a + b, [va[mask] for mask in range(8)])
    for c in range(4):
        wires.copy(vb.at[at.c], vb.at[at.c], at.along(c), 88 + at.c, at.c != c)
    for c in range(4):
        wires.arrived(vb.at[c], 88 + c, at.along(c), at.c != c)
    vec_sums[...] = vb[0] + vb[1] + vb[2] + vb[3]

    wires.arrived(result_home, 60, (at.d, at.c, at.r), at.r != at.c)
    wires.arrived(grad_home, 96, (at.d, at.c, at.r), at.r != at.c)
    for c in range(4):
        wires.arrived(zd.at[c], c, at.along(c), at.c != c)
        wires.arrived(zo.at[c], 52 + c, at.along(c), at.c != c)
        wires.arrived(zh.at[c], 76 + c, at.along(c), at.c != c)
        for d in range(2):
            here = jnp.logical_and(at.c == c, at.d == d)
            wires.arrived(zu.at[2 * c + d], 4 + 2 * c + d, (d, at.r, c), jnp.logical_not(here))
    for made in stay:
        made.wait()
    wires.close()


def fused(
    n_dp,
    tokens,
    cotangent,
    segments,
    w_heads,
    w_out,
    w_up,
    w_down,
    norm_vectors,
    width_vectors,
    attend_bias,
    hidden_vectors,
):
    low = jnp.bfloat16
    share, pieces = tokens.shape[1], w_out.shape[2]
    sz = Sizes(share, pieces, tokens.shape[0])
    d, r, c = (lax.axis_index(name) for name in ("dp", "row", "col"))
    block, main, slack = sz.block, sz.main, sz.slack
    quarter = jnp.asarray(0.25, low)

    def lay(rows):
        rows = rows.reshape(rows.shape[0], 2, pieces)
        return jnp.pad(rows, ((0, 0), (0, 0), (0, block - pieces))).reshape(-1, sz.pair)

    x_home = lay(tokens).T
    dy_home = lay(cotangent).T

    bias = jnp.zeros((3, n_dp, pieces), low)
    attend = attend_bias.astype(low).reshape(2, pieces) * quarter
    bias = lax.dynamic_update_slice(bias, attend[0].reshape(1, 1, pieces), (0, d, 0))
    bias = lax.dynamic_update_slice(bias, attend[1].reshape(1, 1, pieces), (2, d, 0))
    rows = jnp.concatenate([w_heads.astype(low).reshape(pieces, 3, share), bias.reshape(1, 3, share)])
    rows = jnp.concatenate([rows, rows], axis=2)
    rows = lax.dynamic_slice_in_dim(rows, share - slack * r, share, axis=2)
    wh_own = jnp.concatenate(
        [rows[:, :, :main].reshape(pieces + 1, -1), rows[:, :, main:].reshape(pieces + 1, -1)], axis=1
    )
    wh_own = jnp.pad(wh_own, ((0, block - pieces - 1), (0, sz.heads - 3 * share)))

    width = width_vectors.astype(low).reshape(4, pieces) * quarter

    def with_bias(matrix, vector, lanes):
        matrix = jnp.transpose(matrix.reshape(-1, 2, pieces), (1, 2, 0))
        column = jnp.zeros((2, pieces, 1), low)
        column = lax.dynamic_update_slice(column, vector.reshape(1, pieces, 1), (d, 0, 0))
        matrix = jnp.concatenate([matrix, column], axis=2)
        padding = ((0, 0), (0, block - pieces), (0, lanes - matrix.shape[2]))
        return jnp.pad(matrix, padding).reshape(sz.pair, lanes)

    wo_own = with_bias(w_out.astype(low).reshape(pieces, share), width[0], sz.mixed)
    wd_own = with_bias(w_down.astype(low).reshape(4 * pieces, share), width[3], sz.hidden)

    rows = jnp.transpose(w_up.astype(low).reshape(pieces, 4, 2, pieces), (0, 2, 1, 3))
    bias = jnp.zeros((1, 2, 4, pieces), low)
    hidden = hidden_vectors.astype(low).reshape(1, 1, 4, pieces) * quarter
    bias = lax.dynamic_update_slice(bias, hidden, (0, d, 0, 0))
    rows = jnp.concatenate([rows, bias]).reshape(pieces + 1, 2, 4 * pieces)
    padding = ((0, block - pieces - 1), (0, 0), (0, sz.hidden - 4 * pieces))
    wu_own = jnp.pad(rows, padding).reshape(block, 2 * sz.hidden)

    norms = jnp.concatenate(
        [norm_vectors.reshape(2, pieces), width_vectors.reshape(4, pieces)[1:3]]
    ).astype(low)
    ones = jnp.array([[0.0], [1.0], [0.0], [1.0]], low)
    vec_own = jnp.pad(jnp.concatenate([norms, ones], axis=1).T, ((0, block - pieces - 1), (0, 124)))

    labels = lax.dynamic_slice_in_dim(segments, c * sz.seq, sz.seq)
    row_labels, col_labels = labels.reshape(1, -1), labels.reshape(-1, 1)

    def made(*shape, dtype=low):
        return jax.ShapeDtypeStruct(shape, dtype)

    def held(*shape, dtype=low):
        return pltpu.VMEM(shape, dtype)

    w, seq, both, part = sz.width, sz.seq, sz.both, sz.part
    vmem, anywhere = pl.BlockSpec(memory_space=pltpu.VMEM), pl.BlockSpec(memory_space=pl.ANY)
    dma = pltpu.SemaphoreType.DMA
    f32 = jnp.float32
    wide = 3 * 128 + 128
    outs = pl.pallas_call(
        functools.partial(forward_kernel, sz),
        out_shape=(
            made(w, sz.heads),
            made(w, 2 * sz.mixed),
            made(w, sz.hidden),
            made(w, sz.hidden),
            made(w, seq),
            made(w, both),
            made(w, both),
            made(both, w),
            made(both, sz.hidden, dtype=f32),
            made(both, sz.hidden),
            made(seq, main + 128),
            made(seq, main + 128),
            made(seq, main + 128),
            made(seq, 2 * sz.mixed),
            made(seq, 128, dtype=f32),
            made(part, w, dtype=f32),
            made(part, w),
            made(8, w, dtype=f32),
        ),
        in_specs=[anywhere] * 7 + [vmem] * 2,
        out_specs=[vmem] * 18,
        scratch_shapes=[
            held(w, seq),
            held(seq, w),
            held(both, w),
            held(seq, sz.heads),
            held(seq, main + 128),
            held(w, 128),
            held(seq, w),
            held(seq, 256),
            held(seq, 256),
            held(seq, 128),
            held(2, part, w),
            held(1, part, w),
            held(1, part, w),
            dma((96,)),
            dma((96,)),
            dma((16,)),
        ],
        compiler_params=pltpu.CompilerParams(
            collective_id=0, has_side_effects=True, vmem_limit_bytes=VMEM_BYTES
        ),
        cost_estimate=pl.CostEstimate(flops=10**10, bytes_accessed=10**8, transcendentals=10**6),
    )(x_home, dy_home, wh_own, wo_own, wu_own, wd_own, vec_own, row_labels, col_labels)
    (wh, wo, wu, wd, h1_t, h2_t, dy_t, dy, u, gl, qw, kw, vw, a_nat, lse, x2, x_own, vec_rows) = outs
    outs = pl.pallas_call(
        functools.partial(backward_kernel, sz),
        out_shape=(
            made(4, sz.pair, sz.hidden),
            made(8, block, sz.hidden),
            made(4, sz.pair, sz.mixed),
            made(4, block, sz.heads),
            made(seq, sz.pair),
            made(seq, sz.pair),
            made(8, w, dtype=f32),
        ),
        in_specs=[anywhere] * 10 + [vmem] * 10,
        out_specs=[anywhere] * 6 + [vmem],
        scratch_shapes=[
            held(both, w),
            held(w, both),
            held(both, sz.hidden, dtype=f32),
            held(both, sz.hidden),
            held(w, both),
            held(w, sz.hidden),
            held(w, sz.hidden),
            held(w, 2 * sz.mixed),
            held(w, sz.heads),
            held(part, w),
            held(both, sz.hidden),
            held(w, sz.heads),
            held(w, sz.hidden),
            held(w, 2 * sz.mixed),
            held(4, block, sz.heads),
            held(4, sz.pair, sz.mixed),
            held(4, part, w),
            held(3, part, w),
            held(4, part, w),
            held(3, part, w),
            held(2, part, w),
            held(1, part, w),
            held(3, part, w),
            held(seq, w),
            held(seq, 2 * sz.mixed),
            held(seq, main + 128),
            held(seq, main + 128),
            held(seq, main + 128),
            held(seq, 128, dtype=f32),
            held(seq, 128, dtype=f32),
            held(part, w, dtype=f32),
            held(seq, 256),
            held(seq, 256),
            held(seq, 128),
            held(seq, 128),
            held(4, part, sz.pair),
            held(seq, sz.pair),
            held(seq, sz.pair),
            held(8, 8, w, dtype=f32),
            held(4, 8, w, dtype=f32),
            dma((112,)),
            dma((100,)),
            dma((24,)),
        ],
        compiler_params=pltpu.CompilerParams(
            collective_id=1, has_side_effects=True, vmem_limit_bytes=VMEM_BYTES
        ),
        cost_estimate=pl.CostEstimate(flops=2 * 10**10, bytes_accessed=10**8, transcendentals=10**6),
    )(
        dy, dy_t, u, gl, h2_t, wd, wu, wo, wh, h1_t,
        qw, kw, vw, a_nat, lse, x2, x_own, vec_rows, row_labels, col_labels,
    )
    zd, zu, zo, zh, result_home, grad_home, vec_sums = outs

    def plain(rows):
        return rows.reshape(seq, 2, block)[:, :, :pieces].reshape(seq, share)

    def total(parts):
        return jnp.sum(parts.astype(f32), axis=0)

    own = lax.dynamic_slice_in_dim(vec_sums[:4], sz.pair * c + block * d, block, axis=1)[:, :pieces]
    heads = total(zh)[: pieces + 1]
    heads = jnp.concatenate(
        [
            heads[:, : 3 * main].reshape(-1, 3, main),
            heads[:, 3 * main : 3 * share].reshape(-1, 3, slack),
        ],
        axis=2,
    )
    heads = jnp.concatenate([heads, heads], axis=2)
    heads = lax.dynamic_slice_in_dim(heads, slack * r, share, axis=2)
    attend = lax.dynamic_slice_in_dim(heads[pieces], d * pieces, pieces, axis=1)
    out = total(zo).reshape(2, block, sz.mixed)[:, :pieces]
    up = total(zu.reshape(4, 2, block, sz.hidden))
    down = total(zd).reshape(2, block, sz.hidden)[:, :pieces]
    bias_up = lax.dynamic_index_in_dim(up[:, pieces], d, 0, keepdims=False)[: 4 * pieces]
    bias_out = lax.dynamic_index_in_dim(out[:, :, pieces], d, 0, keepdims=False)
    bias_down = lax.dynamic_index_in_dim(down[:, :, 4 * pieces], d, 0, keepdims=False)
    up = up[:, :pieces, : 4 * pieces].reshape(2, pieces, 4, pieces)
    reduced = (
        heads[:pieces].reshape(w_heads.shape),
        jnp.transpose(out[:, :, :pieces], (2, 0, 1)).reshape(w_out.shape),
        jnp.transpose(up, (1, 2, 0, 3)).reshape(w_up.shape),
        jnp.transpose(down[:, :, : 4 * pieces], (2, 0, 1)).reshape(w_down.shape),
        own[0:2].reshape(norm_vectors.shape),
        jnp.stack([bias_out, own[2], own[3], bias_down]).reshape(width_vectors.shape),
        jnp.stack([attend[0], attend[2]]).reshape(attend_bias.shape),
        bias_up.reshape(hidden_vectors.shape),
    )
    return plain(result_home), plain(grad_home).astype(f32), reduced


def normalize(inputs):
    center = jnp.mean(inputs, axis=1, keepdims=True)
    spread = jnp.mean(inputs * inputs, axis=1, keepdims=True) - center * center
    inverse = lax.rsqrt(spread + NORM_EPSILON)
    return ((inputs - center) * inverse, inverse)


def norm_pull(upstream, centered, inverse, gain):
    scaled = upstream * gain
    inner = (
        scaled
        - jnp.mean(scaled, axis=1, keepdims=True)
        - centered * jnp.mean(scaled * centered, axis=1, keepdims=True)
    )
    return inner * inverse


def crossed(blocks, n):
    pairs = [(i * n + j, j * n + i) for i in range(n) for j in range(n)]
    return lax.ppermute(blocks, ("row", "col"), pairs)


def scatter_rows(partial):
    return lax.psum_scatter(
        partial.astype(jnp.bfloat16), "row", scatter_dimension=0, tiled=True
    ).astype(jnp.float32)


def gather_rows(local):
    return lax.all_gather(local, "row", axis=0, tiled=True)


def split_heads(rows):
    return jnp.transpose(rows.reshape(rows.shape[0], -1, HD), (1, 0, 2))


def join_heads(values):
    return jnp.transpose(values, (1, 0, 2)).reshape(values.shape[1], -1)


def scores_of(queries, keys, allowed):
    scores = jnp.einsum(
        "hqe,hke->hqk", queries, keys, preferred_element_type=jnp.float32
    ) * HD ** (-0.5)
    return jnp.where(allowed[None], scores, MASKED)


def gathered(
    tokens,
    cotangent,
    segments,
    w_heads,
    w_out,
    w_up,
    w_down,
    norm_vectors,
    width_vectors,
    attend_bias,
    hidden_vectors,
):
    n_dp, n_row, n_col = (lax.axis_size(name) for name in ("dp", "row", "col"))
    row = lax.axis_index("row")
    low = jnp.bfloat16
    share = tokens.shape[1]
    width = share * n_col
    seq = tokens.shape[0]
    part = seq // n_row
    near = HEADS // n_row
    window = (HEADS - near * (n_row - 1)) * HD
    step = near * HD
    edge = width - (share + step * (n_row - 1)) if n_row > 1 else 0
    edge = window - share
    to_next = [(i, i + 1) for i in range(n_row - 1)]
    to_last = [(i + 1, i) for i in range(n_row - 1)]
    offset = edge - (share - step) * row

    vectors = jnp.concatenate(
        [
            norm_vectors.reshape(2, -1),
            width_vectors.reshape(4, -1),
            attend_bias.reshape(2, -1),
            hidden_vectors.reshape(4, -1),
        ]
    ).astype(low)
    vectors = lax.all_gather(vectors, ("row", "col", "dp"), axis=0, tiled=False)
    vectors = vectors.reshape(n_row, n_col, n_dp, 12, -1).astype(jnp.float32)
    by_col = jnp.transpose(vectors[0], (2, 0, 1, 3)).reshape(12, width)
    by_row = jnp.transpose(vectors[:, 0], (2, 0, 1, 3)).reshape(12, width)
    gain_one, shift_one, bias_out, gain_two, shift_two, bias_down = (by_col[i] for i in range(6))
    zeros = jnp.zeros((1, window), jnp.float32)
    attend_rows = lax.dynamic_slice_in_dim(by_row[6:8], row * step, window, axis=1)
    heads_bias = jnp.concatenate([attend_rows[0:1], zeros, attend_rows[1:2]]).reshape(-1)
    unit_bias = lax.dynamic_slice_in_dim(by_row[8:12], row * share, share, axis=1).reshape(-1)

    own = w_heads.astype(low).reshape(-1, 3, share)
    passed = lax.ppermute(own[:, :, share - edge :], "row", to_next)
    own = jnp.concatenate([passed, own, jnp.zeros_like(passed)], axis=2)
    own = lax.dynamic_slice_in_dim(own, offset, window, axis=2).reshape(-1, 3 * window)
    heads_matrix = lax.all_gather(own, ("col", "dp"), axis=0, tiled=True)
    out_matrix = lax.all_gather(w_out.astype(low).reshape(-1, share), ("col", "dp"), axis=0)
    out_matrix = jnp.transpose(out_matrix.reshape(n_col, share, share), (1, 0, 2))
    out_matrix = out_matrix.reshape(share, width)
    passed = lax.ppermute(out_matrix[share - edge :], "row", to_next)
    out_matrix = jnp.concatenate([passed, out_matrix, jnp.zeros_like(passed)])
    out_matrix = lax.dynamic_slice_in_dim(out_matrix, offset, window)
    owned = (jnp.arange(window) < step) | (row == n_row - 1)
    out_matrix = jnp.where(owned[:, None], out_matrix, jnp.zeros_like(out_matrix))
    up_matrix = lax.all_gather(
        w_up.astype(low).reshape(-1, 4 * share), ("col", "dp"), axis=0, tiled=True
    )
    down_matrix = lax.all_gather(w_down.astype(low).reshape(4, -1, share), ("col", "dp"), axis=0)
    down_matrix = down_matrix.reshape(n_col, n_dp, 4, -1, share)
    down_matrix = jnp.transpose(down_matrix, (2, 1, 3, 0, 4)).reshape(4 * share, width)

    inputs_low = lax.all_gather(crossed(tokens, n_row), "row", axis=1, tiled=True)
    upstream = lax.all_gather(crossed(cotangent, n_row), "row", axis=1, tiled=True)
    inputs = inputs_low.astype(jnp.float32)
    centered_one, inverse_one = normalize(inputs)
    normed_one = (centered_one * gain_one + shift_one).astype(low)
    projected = (times(normed_one, heads_matrix) + heads_bias).astype(low)
    queries, keys, values = (
        split_heads(projected[:, i * window : (i + 1) * window]) for i in range(3)
    )
    labels = lax.dynamic_slice_in_dim(segments, lax.axis_index("col") * seq, seq)
    places = jnp.arange(seq, dtype=jnp.int32)
    allowed = (labels[:, None] == labels[None, :]) & (places[:, None] >= places[None, :])
    scores = scores_of(queries, keys, allowed)
    highest = jnp.max(scores, axis=-1, keepdims=True)
    log_total = highest + jnp.log(jnp.sum(jnp.exp(scores - highest), axis=-1, keepdims=True))
    soft = jnp.exp(scores - log_total).astype(low)
    mixed = jnp.einsum("hqk,hke->hqe", soft, values, preferred_element_type=jnp.float32)
    mixed = join_heads(mixed.astype(low))
    branch = scatter_rows(times(mixed, out_matrix))
    mine = row * part
    middle = lax.dynamic_slice_in_dim(inputs, mine, part) + (branch + bias_out)
    centered_two, inverse_two = normalize(middle)
    normed_two = gather_rows((centered_two * gain_two + shift_two).astype(low))
    hidden = times(normed_two, up_matrix) + unit_bias
    activated, smooth_pull = jax.vjp(smooth, hidden)
    activated = activated.astype(low)
    result = (middle + (scatter_rows(times(activated, down_matrix)) + bias_down)).astype(low)

    down_back = times_flipped(upstream, down_matrix)
    grad_down = times_outer(activated, upstream)
    hidden_back = smooth_pull(down_back)[0].astype(low)
    grad_up = times_outer(normed_two, hidden_back)
    unit_sum = jnp.sum(hidden_back, axis=0, dtype=jnp.float32)
    normed_two_back = scatter_rows(times_flipped(hidden_back, up_matrix))
    upstream_own = lax.dynamic_slice_in_dim(upstream, mine, part).astype(jnp.float32)
    middle_back = upstream_own + norm_pull(normed_two_back, centered_two, inverse_two, gain_two)
    branch_own = middle_back.astype(low)
    branch_back = gather_rows(branch_own)
    mixed_back = times_flipped(branch_back, out_matrix).astype(low)
    grad_out = times_outer(mixed, branch_back)
    mixed_back = split_heads(mixed_back)
    scores_again = scores_of(queries, keys, allowed)
    soft = jnp.exp(scores_again - log_total)
    soft_back = jnp.einsum("hqe,hke->hqk", mixed_back, values, preferred_element_type=jnp.float32)
    row_inner = jnp.sum(soft_back * soft, axis=-1, keepdims=True)
    score_back = (soft * (soft_back - row_inner)).astype(low)
    query_back = jnp.einsum(
        "hqk,hke->hqe", score_back, keys, preferred_element_type=jnp.float32
    ) * HD ** (-0.5)
    key_back = jnp.einsum(
        "hqk,hqe->hke", score_back, queries, preferred_element_type=jnp.float32
    ) * HD ** (-0.5)
    value_back = jnp.einsum(
        "hqk,hqe->hke", soft.astype(low), mixed_back, preferred_element_type=jnp.float32
    )
    heads_back = jnp.concatenate(
        [join_heads(each.astype(low)) for each in (query_back, key_back, value_back)], axis=1
    )
    heads_sum = jnp.sum(heads_back, axis=0, dtype=jnp.float32)
    normed_one_back = scatter_rows(times_flipped(heads_back, heads_matrix))
    grad_heads = times_outer(normed_one, heads_back)
    centered_own = lax.dynamic_slice_in_dim(centered_one, mine, part)
    inverse_own = lax.dynamic_slice_in_dim(inverse_one, mine, part)
    input_back = middle_back + norm_pull(normed_one_back, centered_own, inverse_own, gain_one)

    def homeward(own):
        own = lax.all_to_all(own, "row", split_axis=1, concat_axis=0, tiled=True)
        return crossed(own, n_row)

    result_tokens = homeward(result)
    input_gradient = homeward(input_back.astype(low)).astype(jnp.float32)

    by_token = jnp.stack(
        [
            jnp.sum(normed_one_back * centered_own, axis=0),
            jnp.sum(normed_one_back, axis=0),
            jnp.sum(branch_own.astype(jnp.float32), axis=0),
            jnp.sum(normed_two_back * centered_two, axis=0),
            jnp.sum(normed_two_back, axis=0),
            jnp.sum(upstream_own, axis=0),
        ]
    )
    owned_rows = jnp.where(owned, heads_sum.reshape(3, window)[0::2], 0.0)
    by_unit = jnp.concatenate(
        [
            lax.dynamic_update_slice_in_dim(
                jnp.zeros((2, width), jnp.float32), owned_rows, row * step, axis=1
            ),
            lax.dynamic_update_slice_in_dim(
                jnp.zeros((4, width), jnp.float32), unit_sum.reshape(4, share), row * share, axis=1
            ),
        ]
    )
    sums = lax.psum(jnp.concatenate([by_token, by_unit]), ("dp", "row", "col"))
    pieces = share // n_dp
    inner = lax.axis_index("dp") * pieces
    col_sums = lax.dynamic_slice_in_dim(sums, lax.axis_index("col") * share + inner, pieces, axis=1)
    row_sums = lax.dynamic_slice_in_dim(sums, row * share + inner, pieces, axis=1)

    both = ("col", "dp")

    def to_owner(gradient):
        return lax.psum_scatter(gradient, both, scatter_dimension=0, tiled=True)

    got_heads = to_owner(grad_heads.astype(low)).reshape(pieces, 3, window)
    got_heads = jnp.where(owned, got_heads, jnp.zeros_like(got_heads))
    passed = lax.ppermute(got_heads[:, :, :edge], "row", to_last)
    got_heads = jnp.concatenate([got_heads, jnp.zeros_like(passed)], axis=2)
    got_heads = lax.dynamic_slice_in_dim(got_heads, edge - offset, share, axis=2)
    passed = jnp.concatenate([jnp.zeros((pieces, 3, share), low), passed, jnp.zeros_like(passed)], axis=2)
    got_heads = got_heads + lax.dynamic_slice_in_dim(passed, share - step + edge - offset, share, axis=2)
    low_out = jnp.where(owned[:, None], grad_out, 0.0).astype(low)
    passed = lax.ppermute(low_out[:edge], "row", to_last)
    low_out = jnp.concatenate([low_out, jnp.zeros_like(passed)])
    low_out = lax.dynamic_slice_in_dim(low_out, edge - offset, share)
    passed = jnp.concatenate([jnp.zeros((share, width), low), passed, jnp.zeros_like(passed)])
    low_out = low_out + lax.dynamic_slice_in_dim(passed, share - step + edge - offset, share)
    low_out = jnp.transpose(low_out.reshape(n_dp, pieces, n_col, share), (2, 0, 1, 3))
    got_out = to_owner(low_out.reshape(-1, share))
    got_up = to_owner(grad_up.astype(low))
    low_down = grad_down.astype(low).reshape(4, n_dp, pieces, n_col, share)
    low_down = jnp.transpose(low_down, (3, 1, 0, 2, 4)).reshape(-1, share)
    got_down = to_owner(low_down)

    reduced = [
        each.astype(jnp.float32).reshape(like.shape)
        for each, like in (
            (got_heads, w_heads),
            (got_out, w_out),
            (got_up, w_up),
            (got_down, w_down),
            (col_sums[0:2], norm_vectors),
            (col_sums[2:6], width_vectors),
            (row_sums[6:8], attend_bias),
            (row_sums[8:12], hidden_vectors),
        )
    ]
    return result_tokens, input_gradient, reduced


def adam(weight, gradient, first, second, rate, decay):
    first_new = BETA_FIRST * first + (1.0 - BETA_FIRST) * gradient
    second_new = BETA_SECOND * second + (1.0 - BETA_SECOND) * gradient * gradient
    corrected = first_new / (1.0 - BETA_FIRST**STEP)
    divisor = jnp.sqrt(second_new / (1.0 - BETA_SECOND**STEP)) + ADAM_EPSILON
    return (first_new, second_new, weight - rate * (corrected / divisor + decay * weight))


def smooth(values):
    return jax.nn.gelu(values, approximate=True)


def per_device(
    tokens,
    cotangent,
    segments,
    w_heads,
    w_out,
    w_up,
    w_down,
    norm_vectors,
    width_vectors,
    attend_bias,
    hidden_vectors,
    drift_heads,
    drift_out,
    drift_up,
    drift_down,
    drift_norm,
    drift_width,
    drift_attend,
    drift_hidden,
    power_heads,
    power_out,
    power_up,
    power_down,
    power_norm,
    power_width,
    power_attend,
    power_hidden,
):
    local = (
        tokens,
        cotangent,
        segments,
        w_heads,
        w_out,
        w_up,
        w_down,
        norm_vectors,
        width_vectors,
        attend_bias,
        hidden_vectors,
    )
    sizes = tuple(lax.axis_size(name) for name in ("dp", "row", "col"))
    if sizes == (2, 4, 4):
        result_tokens, input_gradient, reduced = fused(2, *local)
    else:
        result_tokens, input_gradient, reduced = gathered(*local)
    heads_up = adam(w_heads, reduced[0], drift_heads, power_heads, 0.05, MATRIX_DECAY)
    out_up = adam(w_out, reduced[1], drift_out, power_out, 0.2, MATRIX_DECAY)
    up_up = adam(w_up, reduced[2], drift_up, power_up, 0.05, MATRIX_DECAY)
    down_up = adam(w_down, reduced[3], drift_down, power_down, 0.025, MATRIX_DECAY)
    norm_up = adam(norm_vectors, reduced[4], drift_norm, power_norm, 0.3, 0.0)
    width_up = adam(width_vectors, reduced[5], drift_width, power_width, 0.3, 0.0)
    attend_up = adam(attend_bias, reduced[6], drift_attend, power_attend, 0.3, 0.0)
    hidden_up = adam(hidden_vectors, reduced[7], drift_hidden, power_hidden, 0.3, 0.0)
    return (
        result_tokens,
        input_gradient,
        heads_up[0],
        heads_up[1],
        heads_up[2],
        out_up[0],
        out_up[1],
        out_up[2],
        up_up[0],
        up_up[1],
        up_up[2],
        down_up[0],
        down_up[1],
        down_up[2],
        norm_up[0],
        norm_up[1],
        norm_up[2],
        width_up[0],
        width_up[1],
        width_up[2],
        attend_up[0],
        attend_up[1],
        attend_up[2],
        hidden_up[0],
        hidden_up[1],
        hidden_up[2],
    )


def solution(mesh):
    return jax.shard_map(
        per_device,
        mesh=mesh,
        in_specs=(
            P(("dp", "row"), "col"),
            P(("dp", "row"), "col"),
            P("dp"),
            P("col", "dp", None, None, "row"),
            P("row", "dp", None, "col"),
            P("col", "dp", None, None, "row"),
            P(None, "row", "dp", None, "col"),
            P(None, "col", "dp", None),
            P(None, "col", "dp", None),
            P(None, "row", "dp", None),
            P(None, "row", "dp", None),
            P("col", "dp", None, None, "row"),
            P("row", "dp", None, "col"),
            P("col", "dp", None, None, "row"),
            P(None, "row", "dp", None, "col"),
            P(None, "col", "dp", None),
            P(None, "col", "dp", None),
            P(None, "row", "dp", None),
            P(None, "row", "dp", None),
            P("col", "dp", None, None, "row"),
            P("row", "dp", None, "col"),
            P("col", "dp", None, None, "row"),
            P(None, "row", "dp", None, "col"),
            P(None, "col", "dp", None),
            P(None, "col", "dp", None),
            P(None, "row", "dp", None),
            P(None, "row", "dp", None),
        ),
        out_specs=(
            P(("dp", "row"), "col"),
            P(("dp", "row"), "col"),
            P("col", "dp", None, None, "row"),
            P("col", "dp", None, None, "row"),
            P("col", "dp", None, None, "row"),
            P("row", "dp", None, "col"),
            P("row", "dp", None, "col"),
            P("row", "dp", None, "col"),
            P("col", "dp", None, None, "row"),
            P("col", "dp", None, None, "row"),
            P("col", "dp", None, None, "row"),
            P(None, "row", "dp", None, "col"),
            P(None, "row", "dp", None, "col"),
            P(None, "row", "dp", None, "col"),
            P(None, "col", "dp", None),
            P(None, "col", "dp", None),
            P(None, "col", "dp", None),
            P(None, "col", "dp", None),
            P(None, "col", "dp", None),
            P(None, "col", "dp", None),
            P(None, "row", "dp", None),
            P(None, "row", "dp", None),
            P(None, "row", "dp", None),
            P(None, "row", "dp", None),
            P(None, "row", "dp", None),
            P(None, "row", "dp", None),
        ),
        check_vma=False,
    )
```

```python
import functools

import jax
import jax.numpy as jnp
from jax import lax
from jax.experimental import pallas as pl
from jax.experimental.pallas import tpu as pltpu
from jax.sharding import PartitionSpec as P

HEADS = 25
HD = 64
TOK_DEV = 128
STEP = 10


NORM_EPSILON = 1e-05
BETA_FIRST = 0.9
BETA_SECOND = 0.999
ADAM_EPSILON = 1e-08
MATRIX_DECAY = 0.1
MASKED = -1e30
ROOT = (2.0 / 3.141592653589793) ** 0.5
CUBIC = 0.044715
VMEM_BYTES = 66 * 1024 * 1024


def ceil_to(count, unit):
    return -(-count // unit) * unit


class Sizes:
    def __init__(self, share, pieces, seq):
        self.share = share
        self.pieces = pieces
        self.block = ceil_to(pieces, 16)
        self.pair = 2 * self.block
        self.width = 4 * self.pair
        self.seq = seq
        self.part = seq // 4
        self.both = 2 * seq
        self.main = (HEADS // 4) * HD
        self.slack = share - self.main
        self.heads = ceil_to(3 * share, 256)
        self.mixed = ceil_to(pieces + 1, 128)
        self.hidden = ceil_to(4 * pieces + 1, 128)
        self.tiles = self.width // 128


class Place:
    def __init__(self):
        self.d, self.r, self.c = (lax.axis_index(name) for name in ("dp", "row", "col"))
        self.y, self.k = self.r // 2, self.r % 2

    def plane(self, mask):
        d = 1 - self.d if mask & 4 else self.d
        y = 1 - self.y if mask & 2 else self.y
        k = 1 - self.k if mask & 1 else self.k
        return d, 2 * y + k

    def peer(self, mask):
        d, r = self.plane(mask)
        return (d, r, self.c)

    def along(self, c):
        return (self.d, self.r, c)


def run(when, action):
    if when is None:
        action()
    else:
        pl.when(when)(action)


class Wires:
    def __init__(self, sends, arrivals):
        self.sends, self.arrivals = sends, arrivals
        self.used = 0
        self.open = []

    def make(self, source, target, index, slot, device):
        return pltpu.make_async_remote_copy(
            src_ref=source,
            dst_ref=target,
            send_sem=self.sends.at[index],
            recv_sem=self.arrivals.at[slot],
            device_id=device,
            device_id_type=pl.DeviceIdType.MESH,
        )

    def copy(self, source, target, device, slot, when=None):
        made = self.make(source, target, self.used, slot, device)
        self.used += 1
        run(when, made.start)
        item = (when, made)
        self.open.append(item)
        return item

    def arrived(self, target, slot, device, when=None):
        run(when, self.make(target, target, 0, slot, device).wait_recv)

    def close(self, some=None):
        for item in self.open if some is None else some:
            run(item[0], item[1].wait_send)
        self.open = [] if some is None else [o for o in self.open if all(o is not s for s in some)]


def greet(at, diagonal):
    barrier = pltpu.get_barrier_semaphore()

    def signal(device):
        pl.semaphore_signal(
            barrier, inc=1, device_id=device, device_id_type=pl.DeviceIdType.MESH
        )

    for mask in range(1, 8):
        signal(at.peer(mask))
    for c in range(4):
        run(at.c != c, functools.partial(signal, (at.d, at.r, c)))
        if diagonal:
            run(at.c != c, functools.partial(signal, (1 - at.d, at.r, c)))
    run(at.r != at.c, functools.partial(signal, (at.d, at.c, at.r)))
    pl.semaphore_wait(barrier, (13 if diagonal else 10) + jnp.where(at.r != at.c, 1, 0))


def rows_at(start, size):
    return pl.ds(pl.multiple_of(start, 16), size)


def lanes_at(start, size):
    return pl.ds(pl.multiple_of(start, 128), size)


def choose(shape, source):
    rows = lax.broadcasted_iota(jnp.int32, shape, 0)
    wanted = source(lax.broadcasted_iota(jnp.int32, shape, 1))
    return (rows == wanted).astype(jnp.bfloat16)


def edge_source(column):
    part, place = column // HD, column % HD
    wanted = jnp.where(place >= 16, 128 * part + place - 16, 384 + 16 * part + place)
    return jnp.where(part < 3, wanted, -1)


def spread_source(column):
    part, place = column // 128, column % 128
    return jnp.where(place < HD, HD * part + place, -1)


def picked(values, table):
    return jnp.dot(values, table, preferred_element_type=jnp.float32).astype(jnp.bfloat16)


def times(left, right):
    return jnp.dot(left, right, preferred_element_type=jnp.float32)


def times_flipped(left, right):
    return lax.dot_general(
        left, right, (((1,), (1,)), ((), ())), preferred_element_type=jnp.float32
    )


def times_outer(left, right):
    return lax.dot_general(
        left, right, (((0,), (0,)), ((), ())), preferred_element_type=jnp.float32
    )


def over_tiles(total, action, tile=256):
    @pl.loop(0, total // tile)
    def _(i):
        action(i * tile, tile)

    if total % tile:
        action(total - total % tile, total % tile)


def turned(values):
    return values.astype(jnp.float32).T


def gather_group(wires, masks, region, at, base):
    own = region(*at.plane(0))
    sent = [wires.copy(own, own, at.peer(mask), base + mask) for mask in (1, *masks)]

    def finish():
        for mask in masks:
            there = region(*at.plane(mask))
            wires.arrived(there, base + mask, at.peer(mask))
            sent.append(wires.copy(there, there, at.peer(1), base + mask + 1))
        for mask in (0, *masks):
            there = region(*at.plane(mask | 1))
            wires.arrived(there, base + (mask | 1), at.peer(1))

    return finish, sent


def scatter_group(wires, masks, partial, chunk, near, mid, far, at, base):
    sent = []
    for i, mask in enumerate((0, *masks)):
        rows = rows_at(chunk(*at.plane(mask | 1)), near.shape[1])
        sent.append(wires.copy(partial.at[rows], near.at[i], at.peer(1), base + i))

    def rows_of(mask):
        return rows_at(chunk(*at.plane(mask)), near.shape[1])

    def onward():
        for i, mask in enumerate((0, *masks)):
            wires.arrived(near.at[i], base + i, at.peer(1))
        for i, mask in enumerate(masks):
            both = partial[rows_of(mask)].astype(jnp.float32) + near[i + 1].astype(jnp.float32)
            mid[i] = both.astype(jnp.bfloat16)
            sent.append(wires.copy(mid.at[i], far.at[i], at.peer(mask), base + 4 + i))

    def total():
        for i, mask in enumerate(masks):
            wires.arrived(far.at[i], base + 4 + i, at.peer(mask))
        result = partial[rows_of(0)].astype(jnp.float32) + near[0].astype(jnp.float32)
        for i in range(len(masks)):
            result = result + far[i].astype(jnp.float32)
        return result

    return onward, total, sent


def spread_col(wires, region, at, base, source=None):
    own = region(at.c)
    source = own if source is None else source
    for c in range(4):
        other = (at.c != c) & (at.c + c != 3 if c in (0, 3) else at.c != c)
        wires.copy(source, own, at.along(c), base + at.c, other)

    def relay():
        for here, start, end in ((2, 0, 3), (1, 3, 0)):
            block = region(start)
            wires.arrived(block, base + start, at.along(start), at.c == here)
            wires.copy(block, block, at.along(end), base + start, at.c == here)

    def finish():
        for c in range(4):
            needed = at.c != c
            if c == 0:
                needed = needed & (at.c != 2)
            if c == 3:
                needed = needed & (at.c != 1)
            wires.arrived(region(c), base + c, at.along(c), needed)

    return relay, finish


def collect_col(wires, piece, landing, rest, at, base):
    low_end, high_end = at.c == 0, at.c == 3
    ends = low_end | high_end
    via = jnp.where(low_end, 1, 2)

    def pick(*choices):
        return jnp.where(
            low_end,
            choices[0],
            jnp.where(at.c == 1, choices[1], jnp.where(high_end, choices[3], choices[2])),
        )

    order = (pick(3, 0, 3, 0), pick(2, 2, 1, 1), pick(1, 3, 0, 2), at.c)
    target = landing.at[at.c]

    def send(step):
        there = order[step]
        block = piece(there)
        if step == 0:
            wires.copy(block, rest, at.along(via), base + 4, ends)
            wires.copy(block, target, at.along(there), base + at.c, jnp.logical_not(ends))
        elif step == 1:
            wires.copy(block, target, at.along(there), base + at.c)
        elif step == 2:
            wires.copy(block, target, at.along(there), base + at.c, ends)

    def relay(add):
        @pl.when(jnp.logical_not(ends))
        def _():
            wires.make(rest, rest, 0, base + 4, at.along(0)).wait_recv()
            add(order[2])

        wires.copy(piece(order[2]), target, at.along(order[2]), base + at.c, jnp.logical_not(ends))

    def arrived(c):
        wires.arrived(landing.at[c], base + c, at.along(c), sent_from(c))

    def sent_from(c):
        here = at.c != c
        if c in (0, 3):
            here = here & (at.c != 3 - c)
        return here

    return order, send, relay, arrived, sent_from


def forward_kernel(
    sz,
    x_home,
    dy_home,
    wh_own,
    wo_own,
    wu_own,
    wd_own,
    vec_own,
    row_labels,
    col_labels,
    wh_out,
    wo_out,
    wu_out,
    wd_out,
    h1_t_out,
    h2_t_out,
    dy_t_out,
    dy_out,
    u_out,
    gl_out,
    qw_out,
    kw_out,
    vw_out,
    a_nat_out,
    lse_out,
    x2_out,
    x_own_out,
    vec_rows_out,
    wh,
    wo,
    wu,
    wd,
    h1_t,
    h2_t,
    dy_t,
    dy,
    u,
    gl,
    qw,
    kw,
    vw,
    a_nat,
    lse,
    x2,
    x_own,
    vec_rows,
    x_t,
    h1,
    h2,
    own_qkv,
    aw,
    vec,
    part,
    edge_out,
    edge_in,
    edge_back,
    near,
    mid,
    far,
    sends,
    arrivals,
    locals_,
):
    at = Place()
    wires = Wires(sends, arrivals)
    low = jnp.bfloat16
    pair, block = sz.pair, sz.block
    greet(at, False)

    def x_block(d, r):
        return x_t.at[rows_at(pair * r, pair)]

    def dy_block(d, r):
        return dy_t.at[rows_at(pair * r, pair), lanes_at(sz.seq * d, sz.seq)]

    across = (at.d, at.c, at.r)
    same = at.r == at.c
    stay, used = [], [0]

    def keep(source, target, when=None):
        made = pltpu.make_async_copy(source, target, locals_.at[used[0]])
        used[0] += 1
        run(when, made.start)
        stay.append((when, made))

    def flush(source, target):
        made = pltpu.make_async_copy(source, target, locals_.at[used[0]])
        used[0] += 1
        made.start()
        flushed.append(made)

    flushed = []

    def vec_block(d, c):
        return vec.at[rows_at(pair * c + block * d, block)]

    def wh_block(d):
        return lambda c: wh.at[rows_at(pair * c + block * d, block)]

    def wo_block(d):
        return lambda c: wo.at[rows_at(pair * c, pair), lanes_at(sz.mixed * d, sz.mixed)]

    def wu_block(d):
        return lambda c: wu.at[rows_at(pair * c + block * d, block)]

    def wd_block(half):
        return lambda c: wd.at[rows_at(pair * c + block * half, block)]

    wires.copy(x_home, x_block(at.d, at.c), across, 0, jnp.logical_not(same))
    for c in range(4):
        wires.copy(vec_own, vec_block(at.d, at.c), at.along(c), 2 + at.c, at.c != c)
    wires.copy(vec_own, vec_block(at.d, at.c), at.peer(4), 6 + at.c)
    wh_relay, wh_done = spread_col(wires, wh_block(at.d), at, 20, wh_own)
    wires.copy(wh_own, wh_block(at.d)(at.c), at.peer(4), 24 + at.c)
    wires.copy(
        wu_own.at[:, lanes_at(sz.hidden * (1 - at.d), sz.hidden)],
        wu_block(at.d)(at.c),
        at.peer(4),
        10,
    )
    wo_relay, wo_done = spread_col(wires, wo_block(at.d), at, 28, wo_own)
    wires.copy(wo_own, wo_block(at.d)(at.c), at.peer(4), 32 + at.c)
    keep(x_home, x_block(at.d, at.c), same)
    keep(vec_own, vec_block(at.d, at.c))
    keep(wh_own, wh_block(at.d)(at.c))
    keep(wo_own, wo_block(at.d)(at.c))
    keep(wu_own.at[:, lanes_at(sz.hidden * at.d, sz.hidden)], wu_block(at.d)(at.c))
    keep(wd_own, wd.at[rows_at(pair * at.c, pair)])
    for when, made in stay:
        run(when, made.wait)
    wires.arrived(x_block(at.d, at.r), 0, across, jnp.logical_not(same))
    x_done, _ = gather_group(wires, (2,), x_block, at, 12)
    x_done()

    for c in range(4):
        wires.arrived(vec_block(at.d, c), 2 + c, at.along(c), at.c != c)
    wires.arrived(vec_block(1 - at.d, at.c), 6 + at.c, at.peer(4))
    for step in range(1, 4):
        there = (at.c + step) % 4
        wires.copy(
            vec_block(at.d, there), vec_block(at.d, there), at.peer(4), 6 + there
        )
    for step in range(1, 4):
        there = (at.c + step) % 4
        wires.arrived(vec_block(1 - at.d, there), 6 + there, at.peer(4))
    features = 4.0 * sz.share

    def add_up(i, carry):
        rows = rows_at(128 * i, 128)
        value = x_t[rows].astype(jnp.float32)
        return (
            carry[0] + jnp.sum(value, axis=0, keepdims=True),
            carry[1] + jnp.sum(value * value, axis=0, keepdims=True),
        )

    zero = jnp.zeros((1, sz.seq), jnp.float32)
    sums = lax.fori_loop(0, sz.tiles, add_up, (zero, zero))
    center = sums[0] / features
    inverse = lax.rsqrt(sums[1] / features - center * center + NORM_EPSILON)

    @pl.loop(0, sz.tiles)
    def _(i):
        rows, lanes = rows_at(128 * i, 128), lanes_at(128 * i, 128)
        vectors = vec[rows].astype(jnp.float32)
        value = (x_t[rows].astype(jnp.float32) - center) * inverse
        value = value * vectors[:, 0:1] + vectors[:, 1:2]
        h1_t[rows] = value.astype(low)
        h1[:, lanes] = value.T.astype(low)
        mine = x_t[rows, lanes_at(sz.part * at.r, sz.part)]
        x_own[:, lanes] = turned(mine).astype(low)
        vec_rows[:, lanes] = vectors.T[0:8]

    flush(h1_t, h1_t_out)
    flush(x_own, x_own_out)
    flush(vec_rows, vec_rows_out)

    wh_relay()
    for c in range(4):
        needed = at.c != c
        if c == 0:
            needed = needed & (at.c != 2)
        if c == 3:
            needed = needed & (at.c != 1)
        wires.arrived(wh_block(at.d)(c), 20 + c, at.along(c), needed)
        wires.copy(wh_block(at.d)(c), wh_block(at.d)(c), at.peer(4), 24 + c, at.c != c)

    wu_first, wu_first_done = spread_col(wires, wu_block(at.d), at, 36)
    wires.arrived(wu_block(1 - at.d)(at.c), 10, at.peer(4))
    wu_second, wu_second_done = spread_col(wires, wu_block(1 - at.d), at, 40)
    for c in range(4):
        wires.arrived(wh_block(1 - at.d)(c), 24 + c, at.peer(4))
    flush(wh, wh_out)

    @pl.loop(0, sz.heads // 256)
    def _(i):
        lanes = lanes_at(256 * i, 256)
        own_qkv[:, lanes] = times(h1[...], wh[:, lanes]).astype(low)

    wires.copy(dy_home, dy_block(at.d, at.c), across, 1, jnp.logical_not(same))
    made = pltpu.make_async_copy(dy_home, dy_block(at.d, at.c), locals_.at[31])
    run(same, made.start)
    run(same, made.wait)

    starts = (0, sz.main, 2 * sz.main, 3 * sz.main)
    ends = jnp.concatenate([own_qkv[:, s : s + 128] for s in starts], axis=1)
    edge_out[...] = picked(ends, choose((512, 256), edge_source))
    last = at.r == 3

    @pl.when(at.r == 0)
    def _():
        edge_in[...] = jnp.zeros_like(edge_in)

    wires.copy(edge_out, edge_in, (at.d, at.r + 1, at.c), 52, at.r < 3)
    spread = choose((256, 384), spread_source)
    extra = picked(edge_out[...], spread)
    wires.arrived(edge_in, 52, (at.d, at.r - 1, at.c), at.r > 0)
    first = picked(edge_in[...], spread)
    lane = lax.broadcasted_iota(jnp.int32, (sz.seq, 128), 1)
    for i, target in enumerate((qw, kw, vw)):
        start = starts[i]
        target[:, 0:128] = jnp.where(
            lane < sz.slack * at.r,
            first[:, 128 * i : 128 * i + 128],
            own_qkv[:, start : start + 128],
        )
        target[:, 128 : sz.main] = own_qkv[:, start + 128 : start + sz.main]
        target[:, sz.main : sz.main + 128] = extra[:, 128 * i : 128 * i + 128]
    flush(qw, qw_out)
    flush(kw, kw_out)
    flush(vw, vw_out)

    wo_relay()
    for c in range(4):
        needed = at.c != c
        if c == 0:
            needed = needed & (at.c != 2)
        if c == 3:
            needed = needed & (at.c != 1)
        wires.arrived(wo_block(at.d)(c), 28 + c, at.along(c), needed)
        wires.copy(wo_block(at.d)(c), wo_block(at.d)(c), at.peer(4), 32 + c, at.c != c)

    wires.arrived(dy_block(at.d, at.r), 1, across, jnp.logical_not(same))
    dy_done, _ = gather_group(wires, (2, 4, 6), dy_block, at, 56)

    half = sz.seq // 2

    def heads_of(p, count):
        tile = lanes_at(128 * p, 128)
        for q in range(2):
            rows = slice(half * q, half * (q + 1))
            keys = half * (q + 1)
            order = lax.broadcasted_iota(jnp.int32, (half, keys), 0) + half * q
            allowed = (col_labels[rows, :] == row_labels[:, 0:keys]) & (
                order >= lax.broadcasted_iota(jnp.int32, (half, keys), 1)
            )
            lanes = lax.broadcasted_iota(jnp.int32, (half, 128), 1)
            side = lanes // HD
            total = jnp.zeros((half, 128), jnp.float32)
            for h in range(count):
                queries = jnp.where(side == h, qw[rows, tile].astype(jnp.float32) * HD ** (-0.5), 0.0)
                scores = times_flipped(queries.astype(low), kw[0:keys, tile])
                scores = jnp.where(allowed, scores, MASKED)
                highest = jnp.max(scores, axis=1, keepdims=True)
                raised = jnp.exp(scores - highest)
                summed = jnp.sum(raised, axis=1, keepdims=True)
                found = highest + jnp.log(summed)
                lse[rows, :] = jnp.where(lanes == 2 * p + h, found, lse[rows, :])
                soft = (raised * (1.0 / summed)).astype(low)
                total = jnp.where(side == h, times(soft, vw[0:keys, tile]), total)
            aw[rows, tile] = total.astype(low)

    lse[...] = jnp.zeros_like(lse)

    @pl.loop(0, sz.main // 128)
    def _(p):
        heads_of(p, 2)

    @pl.when(last)
    def _():
        heads_of(sz.main // 128, 1)
        edge_back[...] = aw[:, sz.main : sz.main + 128]

    flush(lse, lse_out)

    wires.copy(aw.at[:, 0:128], edge_back, (at.d, at.r - 1, at.c), 53, at.r > 0)
    wd_first, wd_first_done = spread_col(wires, wd_block(0), at, 44)
    wd_second, wd_second_done = spread_col(wires, wd_block(1), at, 48)
    wu_first()
    wires.arrived(edge_back, 53, (at.d, at.r + 1, at.c), at.r < 3)

    def natural(column):
        inner = column % sz.mixed
        place = sz.pieces * (column // sz.mixed) + inner + sz.slack * at.r
        return jnp.where(inner < sz.pieces, place, -1)

    def natural_main(column):
        place = natural(column)
        return jnp.where(place < sz.main, place, -1)

    def natural_edge(column):
        return natural(column) - sz.main

    mixed = times(aw[:, 0 : sz.main], choose((sz.main, 2 * sz.mixed), natural_main))
    mixed = mixed + times(edge_back[...], choose((128, 2 * sz.mixed), natural_edge))
    ones = lax.broadcasted_iota(jnp.int32, mixed.shape, 1) % sz.mixed == sz.pieces
    a_nat[...] = jnp.where(ones, 1.0, mixed).astype(low)
    for c in range(4):
        wires.arrived(wo_block(1 - at.d)(c), 32 + c, at.peer(4))
    flush(wo, wo_out)
    flush(a_nat, a_nat_out)

    def project(start, tile):
        out = times_flipped(a_nat[...], wo[rows_at(start, tile)])
        part[:, lanes_at(start, tile)] = out.astype(low)

    over_tiles(sz.width, project)

    onward, total, _ = scatter_group(
        wires, (2,), part, lambda d, r: sz.part * r, near, mid, far, at, 64
    )
    onward()
    wu_second()
    middle = x_own[...].astype(jnp.float32) + total()
    x2[...] = middle
    flush(x2, x2_out)
    center = jnp.sum(middle, axis=1, keepdims=True) / features
    spread_two = jnp.sum(middle * middle, axis=1, keepdims=True) / features - center * center
    normed = (middle - center) * lax.rsqrt(spread_two + NORM_EPSILON)
    own_rows = rows_at(sz.part * (4 * at.d + at.r), sz.part)
    h2[own_rows] = (normed * vec_rows[2:3] + vec_rows[3:4]).astype(low)
    h2_done, _ = gather_group(
        wires, (2, 4, 6), lambda d, r: h2.at[rows_at(sz.part * (4 * d + r), sz.part)], at, 72
    )
    dy_done()
    flush(dy_t, dy_t_out)
    wd_first()

    @pl.loop(0, sz.tiles)
    def _(i):
        dy[:, lanes_at(128 * i, 128)] = turned(dy_t[rows_at(128 * i, 128)]).astype(low)

    flush(dy, dy_out)
    h2_done()
    wu_first_done()
    wu_second_done()
    flush(wu, wu_out)

    def expand(start, tile):
        lanes = lanes_at(start, tile)
        value = times(h2[...], wu[:, lanes])
        u[:, lanes] = value
        inner = jnp.tanh(ROOT * (value + CUBIC * value * value * value))
        value = 0.5 * value * (1.0 + inner)
        column = lax.broadcasted_iota(jnp.int32, value.shape, 1) + start
        gl[:, lanes] = jnp.where(column == 4 * sz.pieces, 1.0, value).astype(low)

    over_tiles(sz.hidden, expand)

    flush(u, u_out)
    flush(gl, gl_out)
    wd_second()

    @pl.loop(0, sz.tiles)
    def _(i):
        h2_t[rows_at(128 * i, 128)] = turned(h2[:, lanes_at(128 * i, 128)]).astype(low)

    flush(h2_t, h2_t_out)
    wd_first_done()
    wd_second_done()
    flush(wd, wd_out)
    wires.close()
    for made in flushed:
        made.wait()


def backward_kernel(
    sz,
    dy_all,
    dy_t_all,
    u_all,
    gl_all,
    h2_t_all,
    wd_all,
    wu_all,
    wo_all,
    wh_all,
    h1_t_all,
    qw_all,
    kw_all,
    vw_all,
    a_nat_all,
    lse_all,
    x2_all,
    x_own_all,
    vec_rows,
    row_labels,
    col_labels,
    out_down,
    out_up,
    out_out,
    out_heads,
    result_home,
    grad_home,
    vec_sums,
    zd,
    zu,
    zo,
    zh,
    rd,
    ru,
    ro,
    rh,
    qw,
    kw,
    vw,
    a_nat,
    lse,
    x2,
    x_own,
    xu,
    dy,
    dy_t,
    u,
    gl,
    h2_t,
    wd,
    wu,
    wo,
    wh,
    dy_own,
    du,
    gw,
    gu,
    go,
    xh,
    xo,
    near_two,
    far_two,
    near_res,
    far_res,
    near_one,
    far_one,
    mid,
    dob,
    da,
    dqw,
    dkw,
    dvw,
    dk_sum,
    dv_sum,
    dx2,
    edge_out,
    edge_in,
    fore_out,
    fore_in,
    stage,
    home,
    home_two,
    va,
    vb,
    sends,
    arrivals,
    locals_,
):
    at = Place()
    wires = Wires(sends, arrivals)
    low = jnp.bfloat16
    pair, block = sz.pair, sz.block
    features = 4.0 * sz.share
    used = [0]

    def load(source, target, when=None):
        made = pltpu.make_async_copy(source, target, locals_.at[used[0]])
        used[0] += 1
        run(when, made.start)
        return made

    own_rows = rows_at(sz.part * (4 * at.d + at.r), sz.part)
    loads = [
        load(s, t)
        for s, t in (
            (dy_t_all, dy_t),
            (gl_all, gl),
            (dy_all, dy),
            (wd_all, wd),
            (u_all, u),
            (dy_all.at[own_rows], dy_own),
            (wu_all, wu),
            (h2_t_all, h2_t),
            (wo_all, wo),
            (wh_all, wh),
            (x2_all, x2),
            (a_nat_all, a_nat),
            (qw_all, qw),
            (kw_all, kw),
            (vw_all, vw),
            (lse_all, lse),
            (x_own_all, x_own),
        )
    ]
    greet(at, False)
    stay = []

    gd = gw.at[:, 0 : sz.hidden]
    loads[0].wait()
    loads[1].wait()
    order, d_send, d_relay, d_arrived, d_from = collect_col(
        wires, lambda c: gd.at[rows_at(pair * c, pair)], zd, rd, at, 0
    )
    for step in range(4):
        rows = rows_at(pair * order[step], pair)
        gw[rows, 0 : sz.hidden] = times(dy_t[rows], gl[...]).astype(low)
        d_send(step)

    def relay_of(rest, block):
        def add(there):
            parts = (
                load(rest.at[:, 0:512], dqw.at[0:pair, 0:512]),
                load(rest.at[:, 512 : sz.hidden], dkw.at[0:pair, 0 : sz.hidden - 512]),
            )
            for made in parts:
                made.wait()
            rows = rows_at(pair * there, pair)
            for held, start, stop in ((dqw, 0, 512), (dkw, 512, sz.hidden)):
                both = block[rows, start:stop].astype(jnp.float32)
                both = both + held[0:pair, 0 : stop - start].astype(jnp.float32)
                block[rows, start:stop] = both.astype(low)

        return add

    gd_sends = list(wires.open)

    for made in loads[2:6]:
        made.wait()

    def through(start, tile):
        lanes = lanes_at(start, tile)
        upstream = times(dy[...], wd[:, lanes])
        value = u[:, lanes]
        inner = jnp.tanh(ROOT * (value + CUBIC * value * value * value))
        slope = 0.5 * (1.0 + inner) + 0.5 * value * (1.0 - inner * inner) * ROOT * (
            1.0 + 3.0 * CUBIC * value * value
        )
        du[:, lanes] = (upstream * slope).astype(low)

    over_tiles(sz.hidden, through)
    loads[6].wait()

    def back_up(start, tile):
        dy[:, lanes_at(start, tile)] = times_flipped(du[...], wu[rows_at(start, tile)]).astype(low)

    over_tiles(sz.width, back_up)

    def chunk_both(d, r):
        return sz.part * (4 * d + r)

    two_onward, two_total, two_sent = scatter_group(
        wires, (2, 4, 6), dy, chunk_both, near_two, mid, far_two, at, 16
    )
    loads[7].wait()
    order, u_send, u_relay, u_arrived, u_from = collect_col(
        wires, lambda c: gu.at[rows_at(pair * c, pair)], zu, ru, at, 5
    )
    for step in range(4):
        rows = rows_at(pair * order[step], pair)
        gu[rows] = times(h2_t[rows], du[...]).astype(low)
        u_send(step)
        if step == 1:
            two_onward()
    before = len(wires.open)
    d_relay(relay_of(rd, gd))
    gd_sends += wires.open[before:]

    def norm_back(upstream, values, gain):
        center = jnp.sum(values, axis=1, keepdims=True) / features
        spread = jnp.sum(values * values, axis=1, keepdims=True) / features - center * center
        inverse = lax.rsqrt(spread + NORM_EPSILON)
        centered = (values - center) * inverse
        scaled = upstream * gain
        inner = (
            scaled
            - jnp.sum(scaled, axis=1, keepdims=True) / features
            - centered * (jnp.sum(scaled * centered, axis=1, keepdims=True) / features)
        )
        return (
            inner * inverse,
            jnp.sum(upstream * centered, axis=0, keepdims=True),
            jnp.sum(upstream, axis=0, keepdims=True),
        )

    loads[10].wait()
    h2_back = two_total()
    through_norm, gain_two, shift_two = norm_back(h2_back, x2[...], vec_rows[2:3])
    middle_back = dy_own[...].astype(jnp.float32) + through_norm
    dx2[...] = middle_back
    va[0, 2:3] = gain_two
    va[0, 3:4] = shift_two
    va[0, 4:8] = jnp.zeros((4, sz.width), jnp.float32)
    dob[rows_at(sz.part * at.r, sz.part)] = middle_back.astype(low)
    dob_done, dob_sent = gather_group(
        wires, (2,), lambda d, r: dob.at[rows_at(sz.part * r, sz.part)], at, 24
    )
    h1_load = load(h1_t_all, dy_t.at[:, 0 : sz.seq])

    def contract(start, tile):
        out = times_flipped(gl[...], wd[rows_at(start, tile)])
        dy[:, lanes_at(start, tile)] = out.astype(low)

    wires.close(two_sent)
    over_tiles(sz.width, contract)
    res_onward, res_total, res_sent = scatter_group(
        wires, (2, 4, 6), dy, chunk_both, near_res, mid, far_res, at, 32
    )

    u_relay(relay_of(ru, gu))

    dob_done()
    loads[11].wait()
    loads[8].wait()
    da[...] = times(dob[...], wo[...]).astype(low)
    slack, main = sz.slack, sz.main

    def from_natural(place):
        wanted = sz.mixed * (place // sz.pieces) + place % sz.pieces
        return jnp.where((place >= 0) & (place < sz.share), wanted, -1)

    fore_out[...] = picked(
        da[...], choose((2 * sz.mixed, 128), lambda j: from_natural(j + main - slack * at.r))
    )

    @pl.when(at.r == 0)
    def _():
        fore_in[...] = jnp.zeros_like(fore_in)

    wires.copy(fore_out, fore_in, (at.d, at.r + 1, at.c), 40, at.r < 3)

    @pl.loop(0, sz.tiles)
    def _(i):
        dy_t[rows_at(128 * i, 128), sz.seq : sz.both] = turned(dob[:, lanes_at(128 * i, 128)]).astype(low)

    res_onward()

    for step in range(4):
        there = (at.c + step) % 4
        rows = rows_at(pair * there, pair)
        go[rows] = times(dy_t[rows, sz.seq : sz.both], a_nat[...]).astype(low)
        wires.copy(
            go.at[rows, lanes_at(sz.mixed * (1 - at.d), sz.mixed)], xo.at[there], at.peer(4), 48 + there
        )
    wires.arrived(fore_in, 40, (at.d, at.r - 1, at.c), at.r > 0)
    window = times(da[...], choose((2 * sz.mixed, main), lambda j: from_natural(j - slack * at.r)))
    da_first = window[:, 0:128] + fore_in[...].astype(jnp.float32)
    da[:, 128:main] = window[:, 128:main].astype(low)
    da[:, 0:128] = da_first.astype(low)
    da[:, main : main + 128] = fore_out[...]

    for made in loads[12:17]:
        made.wait()
    half = sz.seq // 2

    def heads_back(p, count):
        tile = lanes_at(128 * p, 128)
        dk_sum[...] = jnp.zeros_like(dk_sum)
        dv_sum[...] = jnp.zeros_like(dv_sum)
        for q in range(2):
            rows = slice(half * q, half * (q + 1))
            keys = half * (q + 1)
            order = lax.broadcasted_iota(jnp.int32, (half, keys), 0) + half * q
            allowed = (col_labels[rows, :] == row_labels[:, 0:keys]) & (
                order >= lax.broadcasted_iota(jnp.int32, (half, keys), 1)
            )
            lanes = lax.broadcasted_iota(jnp.int32, (half, 128), 1)
            side = lanes // HD
            total = jnp.zeros((half, 128), jnp.float32)
            for h in range(count):
                queries = jnp.where(side == h, qw[rows, tile].astype(jnp.float32) * HD ** (-0.5), 0.0)
                queries = queries.astype(low)
                pulled = jnp.where(side == h, da[rows, tile].astype(jnp.float32), 0.0).astype(low)
                found = jnp.sum(jnp.where(lanes == 2 * p + h, lse[rows, :], 0.0), axis=1, keepdims=True)
                scores = times_flipped(queries, kw[0:keys, tile])
                soft = jnp.where(allowed, jnp.exp(jnp.where(allowed, scores - found, MASKED)), 0.0)
                soft_back = times_flipped(pulled, vw[0:keys, tile])
                inner = jnp.sum(soft_back * soft, axis=1, keepdims=True)
                score_back = (soft * (soft_back - inner)).astype(low)
                piece = times(score_back, kw[0:keys, tile]) * HD ** (-0.5)
                total = jnp.where(side == h, piece, total)
                dk_sum[0:keys] += times_outer(score_back, queries)
                dv_sum[0:keys] += times_outer(soft.astype(low), pulled)
            dqw[rows, tile] = total.astype(low)
        dkw[:, tile] = dk_sum[...].astype(low)
        dvw[:, tile] = dv_sum[...].astype(low)

    @pl.loop(0, main // 128)
    def _(p):
        heads_back(p, 2)

    @pl.when(at.r == 3)
    def _():
        heads_back(main // 128, 1)

    def compact(column):
        part, place = column // HD, column % HD
        return jnp.where(part < 3, 128 * part + place, -1)

    table = choose((384, 256), compact)
    backs = (dqw, dkw, dvw)
    edge_out[...] = picked(jnp.concatenate([b[:, 0:128] for b in backs], axis=1), table)
    wires.copy(edge_out, edge_in, (at.d, at.r - 1, at.c), 41, at.r > 0)

    @pl.when(at.r == 3)
    def _():
        edge_in[...] = picked(jnp.concatenate([b[:, main : main + 128] for b in backs], axis=1), table)

    wires.arrived(edge_in, 41, (at.d, at.r + 1, at.c), at.r < 3)

    def unfold(column):
        tile, lane = column // 128, column % 128
        inside = jnp.where(lane < HD - 16, HD * tile + lane + 16, -1)
        tail = jnp.where(lane < 48, HD * (lane // 16) + lane % 16, -1)
        return jnp.where(tile < 3, inside, tail)

    edges = picked(edge_in[...], choose((256, 512), unfold))
    lane = lax.broadcasted_iota(jnp.int32, (sz.seq, 128), 1)
    pieces = []
    for i, back in enumerate(backs):
        first = jnp.where(lane < slack * at.r, edges[:, 128 * i : 128 * i + 128], back[:, 0:128])
        pieces += [first, back[:, 128:main]]
    pieces.append(edges[:, 384:512])
    wires.close(dob_sent)
    own_back = dob.at[:, 0 : sz.heads]
    own_back[...] = jnp.concatenate(pieces, axis=1)

    order, o_send, o_relay, o_arrived, o_from = collect_col(
        wires, lambda c: xo.at[c], zo, ro, at, 10
    )
    for step in range(4):
        there = order[step]
        wires.arrived(xo.at[there], 48 + there, at.peer(4))
        mine = go[rows_at(pair * there, pair), lanes_at(sz.mixed * at.d, sz.mixed)]
        xo[there] = (mine.astype(jnp.float32) + xo[there].astype(jnp.float32)).astype(low)
        o_send(step)

    def go_home(values, base, out, home, stage):
        for r in range(4):
            stage[r] = values[:, pair * r : pair * (r + 1)].astype(low)
        mine = rows_at(sz.part * at.r, sz.part)
        sent = []
        for r in range(4):
            sent.append(
                wires.copy(stage.at[r], home.at[mine], (at.d, r, at.c), base + at.r, at.r != r)
            )

            @pl.when(at.r == r)
            def _():
                home[mine] = stage[r]

        for r in range(4):
            rows = home.at[sz.part * r : sz.part * (r + 1)]
            wires.arrived(rows, base + r, (at.d, r, at.c), at.r != r)
        sent.append(wires.copy(home, out, (at.d, at.c, at.r), base + 4, at.r != at.c))
        made = load(home, out, at.r == at.c)
        run(at.r == at.c, made.wait)
        return sent

    def relay_out(there):
        load(ro, dqw.at[0:pair, 0 : sz.mixed]).wait()
        both = xo[there].astype(jnp.float32) + dqw[0:pair, 0 : sz.mixed].astype(jnp.float32)
        xo[there] = both.astype(low)

    result = x2[...] + res_total()
    wires.close(res_sent)
    res_home = go_home(result, 56, result_home, home, stage)

    for made in loads[9:10]:
        made.wait()

    def back_in(start, tile):
        out = times_flipped(own_back[...], wh[rows_at(start, tile)])
        dy[0 : sz.seq, lanes_at(start, tile)] = out.astype(low)

    over_tiles(sz.width, back_in)
    one_onward, one_total, _ = scatter_group(
        wires, (2,), dy, lambda d, r: sz.part * r, near_one, mid, far_one, at, 64
    )
    own = rows_at(pair * at.c, pair)

    def bring(c, landing, needed):
        made = load(landing.at[c], h2_t.at[pair * c : pair * (c + 1), 0 : sz.hidden], needed)
        run(needed, made.wait)

        @pl.when(jnp.logical_not(needed))
        def _():
            h2_t[pair * c : pair * (c + 1), 0 : sz.hidden] = jnp.zeros((pair, sz.hidden), low)

    def summed(block, lanes):
        result = block[own, lanes].astype(jnp.float32)
        for c in range(4):
            result = result + h2_t[pair * c : pair * (c + 1), lanes].astype(jnp.float32)
        return result

    half_rows = sz.pieces

    def turn_out(value, start, rows):
        flipped = value.T
        u[start : start + rows, 0:half_rows] = flipped[0:rows, 0:half_rows]
        u[start : start + rows, half_rows : 2 * half_rows] = flipped[0:rows, block : block + half_rows]

    for c in range(4):
        d_arrived(c)
        bring(c, zd, d_from(c))
    for i in range(sz.hidden // 128):
        rows = min(128, 4 * sz.pieces + 8 - 128 * i)
        turn_out(summed(gw, slice(128 * i, 128 * (i + 1))), 128 * i, rows)
    down_out = load(u.at[0 : 4 * sz.pieces + 8, 0:512], out_down)
    wires.close(gd_sends)
    h1_load.wait()
    order, h_send, h_relay, h_arrived, h_from = collect_col(
        wires, lambda c: xh.at[c], zh, rh, at, 72
    )
    for step in range(4):
        there = order[step]
        rows = rows_at(pair * there, pair)
        gw[rows] = times(dy_t[rows, 0 : sz.seq], own_back[...]).astype(low)
        if step == 0:
            one_onward()
        other = gw.at[rows_at(pair * there + block * (1 - at.d), block)]
        wires.copy(other, xh.at[there], at.peer(4), 80 + there)

    o_relay(relay_out)
    h1_back = one_total()
    through_norm, gain_one, shift_one = norm_back(
        h1_back, x_own[...].astype(jnp.float32), vec_rows[0:1]
    )
    va[0, 0:1] = gain_one
    va[0, 1:2] = shift_one
    for mask in range(1, 8):
        wires.copy(va.at[0], va.at[mask], at.peer(mask), 84 + mask)
    grad = dx2[...] + through_norm
    wires.close(res_home)
    go_home(grad, 92, grad_home, home_two, stage)
    for step in range(4):
        there = order[step]
        wires.arrived(xh.at[there], 80 + there, at.peer(4))
        mine = rows_at(pair * there + block * at.d, block)
        xh[there] = (gw[mine].astype(jnp.float32) + xh[there].astype(jnp.float32)).astype(low)
        h_send(step)

    for c in range(4):
        u_arrived(c)
        bring(c, zu, u_from(c))
    theirs = rows_at(pair * at.c + block * (1 - at.d), block)

    def part_sum(side, lanes):
        rows = rows_at(pair * at.c + block * side, block)
        result = gu[rows, lanes].astype(jnp.float32)
        for c in range(4):
            result = result + h2_t[rows_at(pair * c + block * side, block), lanes].astype(jnp.float32)
        return result

    every = slice(0, sz.hidden)
    gu[theirs] = part_sum(1 - at.d, every).astype(low)
    wires.copy(gu.at[theirs], xu, at.peer(4), 97)
    mine_sum = part_sum(at.d, every)
    down_out.wait()
    wires.arrived(xu, 97, at.peer(4))
    partner_sum = xu[...].astype(jnp.float32)
    for side in range(2):

        @pl.when(at.d == side)
        def _():
            both = (mine_sum, partner_sum) if side == 0 else (partner_sum, mine_sum)
            for j in range(4):
                rows = slice(block * j, block * (j + 1))
                for i in range(2):
                    u[rows, half_rows * i : half_rows * (i + 1)] = both[i][:, half_rows * j : half_rows * (j + 1)]

    up_out = load(u.at[0 : 4 * block, 0:512], out_up)

    for c in range(4):
        o_arrived(c)
        needed = o_from(c)
        made = load(zo.at[c], wd.at[pair * c : pair * (c + 1), 0 : sz.mixed], needed)
        run(needed, made.wait)

        @pl.when(jnp.logical_not(needed))
        def _():
            wd[pair * c : pair * (c + 1), 0 : sz.mixed] = jnp.zeros((pair, sz.mixed), low)

    value = xo[at.c].astype(jnp.float32)
    for c in range(4):
        value = value + wd[pair * c : pair * (c + 1), 0 : sz.mixed].astype(jnp.float32)
    flipped = value.T[0:block]
    flipped = jnp.concatenate(
        [flipped[:, 0:half_rows], flipped[:, block : block + half_rows]], axis=1
    )
    for i in range(4):
        held = (dk_sum, dv_sum)[i // 2].at[block * (i % 2) : block * (i % 2 + 1)]
        lanes = min(128, sz.share - 128 * i)
        held[:, 0:lanes] = flipped[:, 128 * i : 128 * i + lanes]
        stay.append(load(held, out_out.at[:, 128 * i : 128 * (i + 1)]))

    for mask in range(1, 8):
        wires.arrived(va.at[mask], 84 + mask, at.peer(mask))
    vb[at.c] = functools.reduce(lambda a, b: a + b, [va[mask] for mask in range(8)])
    for c in range(4):
        wires.copy(vb.at[at.c], vb.at[at.c], at.along(c), 98 + at.c, at.c != c)

    def relay_heads(there):
        parts = [
            load(rh.at[:, s:e], t.at[0:block, 0 : e - s])
            for t, s, e in ((dqw, 0, 512), (dkw, 512, 1024), (dvw, 1024, sz.heads))
        ]
        for made in parts:
            made.wait()
        for t, s, e in ((dqw, 0, 512), (dkw, 512, 1024), (dvw, 1024, sz.heads)):
            both = xh[there, :, s:e].astype(jnp.float32) + t[0:block, 0 : e - s].astype(jnp.float32)
            xh[there, :, s:e] = both.astype(low)

    h_relay(relay_heads)
    for c in range(4):
        wires.arrived(vb.at[c], 98 + c, at.along(c), at.c != c)
    vec_sums[...] = vb[0] + vb[1] + vb[2] + vb[3]
    wires.arrived(result_home, 60, (at.d, at.c, at.r), at.r != at.c)
    wires.arrived(grad_home, 96, (at.d, at.c, at.r), at.r != at.c)
    up_out.wait()
    rest_lanes = sz.heads - sz.hidden
    for c in range(4):
        h_arrived(c)
        needed = h_from(c)
        rows = slice(block * c, block * (c + 1))
        parts = (
            load(zh.at[c, :, 0 : sz.hidden], wd.at[rows], needed),
            load(zh.at[c, :, sz.hidden : sz.heads], wu.at[rows, 0:rest_lanes], needed),
        )
        for made in parts:
            run(needed, made.wait)

        @pl.when(jnp.logical_not(needed))
        def _():
            wd[rows] = jnp.zeros((block, sz.hidden), low)
            wu[rows, 0:rest_lanes] = jnp.zeros((block, rest_lanes), low)

    left = xh[at.c, :, 0 : sz.hidden].astype(jnp.float32)
    right = xh[at.c, :, sz.hidden : sz.heads].astype(jnp.float32)
    for c in range(4):
        rows = slice(block * c, block * (c + 1))
        left = left + wd[rows].astype(jnp.float32)
        right = right + wu[rows, 0:rest_lanes].astype(jnp.float32)
    whole = jnp.concatenate([left, right], axis=1)
    for i in range(3):
        turned_columns = jnp.concatenate(
            [
                whole[:, main * i : main * (i + 1)],
                whole[:, 3 * main + slack * i : 3 * main + slack * (i + 1)],
            ],
            axis=1,
        )
        rows = slice(block * i, block * (i + 1))
        for r in range(4):

            @pl.when(at.r == r)
            def _():
                cut = slack * r
                u[rows, 0 : sz.share - cut] = turned_columns[:, cut:]
                if cut:
                    u[rows, sz.share - cut : sz.share] = turned_columns[:, 0:cut]

    stay.append(load(u.at[0 : 3 * block, 0:512], out_heads))
    for made in stay:
        made.wait()
    wires.close()


def fused(
    n_dp,
    tokens,
    cotangent,
    segments,
    w_heads,
    w_out,
    w_up,
    w_down,
    norm_vectors,
    width_vectors,
    attend_bias,
    hidden_vectors,
):
    low = jnp.bfloat16
    share, pieces = tokens.shape[1], w_out.shape[2]
    sz = Sizes(share, pieces, tokens.shape[0])
    d, r, c = (lax.axis_index(name) for name in ("dp", "row", "col"))
    block, main, slack = sz.block, sz.main, sz.slack
    quarter = jnp.asarray(0.25, low)

    def lay(rows):
        rows = rows.reshape(rows.shape[0], 2, pieces)
        return jnp.pad(rows, ((0, 0), (0, 0), (0, block - pieces))).reshape(-1, sz.pair)

    x_home = lay(tokens).T
    dy_home = lay(cotangent).T

    bias = jnp.zeros((3, n_dp, pieces), low)
    attend = attend_bias.astype(low).reshape(2, pieces) * quarter
    bias = lax.dynamic_update_slice(bias, attend[0].reshape(1, 1, pieces), (0, d, 0))
    bias = lax.dynamic_update_slice(bias, attend[1].reshape(1, 1, pieces), (2, d, 0))
    rows = jnp.concatenate([w_heads.astype(low).reshape(pieces, 3, share), bias.reshape(1, 3, share)])
    rows = jnp.concatenate([rows, rows], axis=2)
    rows = lax.dynamic_slice_in_dim(rows, share - slack * r, share, axis=2)
    wh_own = jnp.concatenate(
        [rows[:, :, :main].reshape(pieces + 1, -1), rows[:, :, main:].reshape(pieces + 1, -1)], axis=1
    )
    wh_own = jnp.pad(wh_own, ((0, block - pieces - 1), (0, sz.heads - 3 * share)))

    width = width_vectors.astype(low).reshape(4, pieces) * quarter

    def with_bias(matrix, vector, lanes):
        matrix = jnp.transpose(matrix.reshape(-1, 2, pieces), (1, 2, 0))
        column = jnp.zeros((2, pieces, 1), low)
        column = lax.dynamic_update_slice(column, vector.reshape(1, pieces, 1), (d, 0, 0))
        matrix = jnp.concatenate([matrix, column], axis=2)
        padding = ((0, 0), (0, block - pieces), (0, lanes - matrix.shape[2]))
        return jnp.pad(matrix, padding).reshape(sz.pair, lanes)

    wo_own = with_bias(w_out.astype(low).reshape(pieces, share), width[0], sz.mixed)
    wd_own = with_bias(w_down.astype(low).reshape(4 * pieces, share), width[3], sz.hidden)

    rows = jnp.transpose(w_up.astype(low).reshape(pieces, 4, 2, pieces), (0, 2, 1, 3))
    bias = jnp.zeros((1, 2, 4, pieces), low)
    hidden = hidden_vectors.astype(low).reshape(1, 1, 4, pieces) * quarter
    bias = lax.dynamic_update_slice(bias, hidden, (0, d, 0, 0))
    rows = jnp.concatenate([rows, bias]).reshape(pieces + 1, 2, 4 * pieces)
    padding = ((0, block - pieces - 1), (0, 0), (0, sz.hidden - 4 * pieces))
    wu_own = jnp.pad(rows, padding).reshape(block, 2 * sz.hidden)

    norms = jnp.concatenate(
        [norm_vectors.reshape(2, pieces), width_vectors.reshape(4, pieces)[1:3]]
    ).astype(low)
    ones = jnp.array([[0.0], [1.0], [0.0], [1.0]], low)
    vec_own = jnp.pad(jnp.concatenate([norms, ones], axis=1).T, ((0, block - pieces - 1), (0, 124)))

    labels = lax.dynamic_slice_in_dim(segments, c * sz.seq, sz.seq)
    row_labels, col_labels = labels.reshape(1, -1), labels.reshape(-1, 1)

    def made(*shape, dtype=low):
        return jax.ShapeDtypeStruct(shape, dtype)

    def held(*shape, dtype=low):
        return pltpu.VMEM(shape, dtype)

    w, seq, both, part = sz.width, sz.seq, sz.both, sz.part
    vmem, anywhere = pl.BlockSpec(memory_space=pltpu.VMEM), pl.BlockSpec(memory_space=pl.ANY)
    dma = pltpu.SemaphoreType.DMA
    f32 = jnp.float32
    wide = 3 * 128 + 128
    outs = pl.pallas_call(
        functools.partial(forward_kernel, sz),
        out_shape=(
            made(w, sz.heads),
            made(w, 2 * sz.mixed),
            made(w, sz.hidden),
            made(w, sz.hidden),
            made(w, seq),
            made(w, both),
            made(w, both),
            made(both, w),
            made(both, sz.hidden, dtype=f32),
            made(both, sz.hidden),
            made(seq, main + 128),
            made(seq, main + 128),
            made(seq, main + 128),
            made(seq, 2 * sz.mixed),
            made(seq, 128, dtype=f32),
            made(part, w, dtype=f32),
            made(part, w),
            made(8, w, dtype=f32),
        ),
        in_specs=[anywhere] * 7 + [vmem] * 2,
        out_specs=[anywhere] * 18,
        scratch_shapes=[
            held(w, sz.heads),
            held(w, 2 * sz.mixed),
            held(w, sz.hidden),
            held(w, sz.hidden),
            held(w, seq),
            held(w, both),
            held(w, both),
            held(both, w),
            held(both, sz.hidden, dtype=f32),
            held(both, sz.hidden),
            held(seq, main + 128),
            held(seq, main + 128),
            held(seq, main + 128),
            held(seq, 2 * sz.mixed),
            held(seq, 128, dtype=f32),
            held(part, w, dtype=f32),
            held(part, w),
            held(8, w, dtype=f32),
            held(w, seq),
            held(seq, w),
            held(both, w),
            held(seq, sz.heads),
            held(seq, main + 128),
            held(w, 128),
            held(seq, w),
            held(seq, 256),
            held(seq, 256),
            held(seq, 128),
            held(2, part, w),
            held(1, part, w),
            held(1, part, w),
            dma((96,)),
            dma((96,)),
            dma((32,)),
        ],
        compiler_params=pltpu.CompilerParams(
            collective_id=0, has_side_effects=True, vmem_limit_bytes=VMEM_BYTES
        ),
        cost_estimate=pl.CostEstimate(flops=10**10, bytes_accessed=10**8, transcendentals=10**6),
    )(x_home, dy_home, wh_own, wo_own, wu_own, wd_own, vec_own, row_labels, col_labels)
    (wh, wo, wu, wd, h1_t, h2_t, dy_t, dy, u, gl, qw, kw, vw, a_nat, lse, x2, x_own, vec_rows) = outs
    outs = pl.pallas_call(
        functools.partial(backward_kernel, sz),
        out_shape=(
            made(4 * pieces + 8, 512, dtype=f32),
            made(4 * block, 512, dtype=f32),
            made(block, 512, dtype=f32),
            made(3 * block, 512, dtype=f32),
            made(seq, sz.pair),
            made(seq, sz.pair),
            made(8, w, dtype=f32),
            made(4, sz.pair, sz.hidden),
            made(4, sz.pair, sz.hidden),
            made(4, sz.pair, sz.mixed),
            made(4, block, sz.heads),
            made(sz.pair, sz.hidden),
            made(sz.pair, sz.hidden),
            made(sz.pair, sz.mixed),
            made(block, sz.heads),
        ),
        in_specs=[anywhere] * 17 + [vmem] * 3,
        out_specs=[anywhere] * 6 + [vmem] + [anywhere] * 8,
        scratch_shapes=[
            held(seq, main + 128),
            held(seq, main + 128),
            held(seq, main + 128),
            held(seq, 2 * sz.mixed),
            held(seq, 128, dtype=f32),
            held(part, w, dtype=f32),
            held(part, w),
            held(block, sz.hidden),
            held(both, w),
            held(w, both),
            held(both, sz.hidden, dtype=f32),
            held(both, sz.hidden),
            held(w, both),
            held(w, sz.hidden),
            held(w, sz.hidden),
            held(w, 2 * sz.mixed),
            held(w, sz.heads),
            held(part, w),
            held(both, sz.hidden),
            held(w, sz.heads),
            held(w, sz.hidden),
            held(w, 2 * sz.mixed),
            held(4, block, sz.heads),
            held(4, sz.pair, sz.mixed),
            held(4, part, w),
            held(3, part, w),
            held(4, part, w),
            held(3, part, w),
            held(2, part, w),
            held(1, part, w),
            held(3, part, w),
            held(seq, w),
            held(seq, 2 * sz.mixed),
            held(seq, main + 128),
            held(seq, main + 128),
            held(seq, main + 128),
            held(seq, 128, dtype=f32),
            held(seq, 128, dtype=f32),
            held(part, w, dtype=f32),
            held(seq, 256),
            held(seq, 256),
            held(seq, 128),
            held(seq, 128),
            held(4, part, sz.pair),
            held(seq, sz.pair),
            held(seq, sz.pair),
            held(8, 8, w, dtype=f32),
            held(4, 8, w, dtype=f32),
            dma((112,)),
            dma((104,)),
            dma((64,)),
        ],
        compiler_params=pltpu.CompilerParams(
            collective_id=1, has_side_effects=True, vmem_limit_bytes=VMEM_BYTES
        ),
        cost_estimate=pl.CostEstimate(flops=2 * 10**10, bytes_accessed=10**8, transcendentals=10**6),
    )(
        dy, dy_t, u, gl, h2_t, wd, wu, wo, wh, h1_t,
        qw, kw, vw, a_nat, lse, x2, x_own, vec_rows, row_labels, col_labels,
    )
    down, up, out, heads, result_home, grad_home, vec_sums = outs[:7]

    def plain(rows):
        return rows.reshape(seq, 2, block)[:, :, :pieces].reshape(seq, share)

    def half_of(rows):
        return lax.dynamic_slice_in_dim(rows, d * pieces, pieces, axis=rows.ndim - 1)

    own = lax.dynamic_slice_in_dim(vec_sums[:4], sz.pair * c + block * d, block, axis=1)[:, :pieces]
    up = up.reshape(4, block, 512)
    heads = heads.reshape(3, block, 512)
    attend = half_of(heads[:, pieces])
    reduced = (
        jnp.transpose(heads[:, :pieces, :share], (1, 0, 2)).reshape(w_heads.shape),
        out[:pieces, :share].reshape(w_out.shape),
        jnp.transpose(up[:, :pieces, :share], (1, 0, 2)).reshape(w_up.shape),
        down[: 4 * pieces, :share].reshape(w_down.shape),
        own[0:2].reshape(norm_vectors.shape),
        jnp.stack([half_of(out[pieces]), own[2], own[3], half_of(down[4 * pieces])]).reshape(
            width_vectors.shape
        ),
        jnp.stack([attend[0], attend[2]]).reshape(attend_bias.shape),
        half_of(up[:, pieces]).reshape(hidden_vectors.shape),
    )
    return plain(result_home), plain(grad_home).astype(f32), reduced


def normalize(inputs):
    center = jnp.mean(inputs, axis=1, keepdims=True)
    spread = jnp.mean(inputs * inputs, axis=1, keepdims=True) - center * center
    inverse = lax.rsqrt(spread + NORM_EPSILON)
    return ((inputs - center) * inverse, inverse)


def norm_pull(upstream, centered, inverse, gain):
    scaled = upstream * gain
    inner = (
        scaled
        - jnp.mean(scaled, axis=1, keepdims=True)
        - centered * jnp.mean(scaled * centered, axis=1, keepdims=True)
    )
    return inner * inverse


def crossed(blocks, n):
    pairs = [(i * n + j, j * n + i) for i in range(n) for j in range(n)]
    return lax.ppermute(blocks, ("row", "col"), pairs)


def scatter_rows(partial):
    return lax.psum_scatter(
        partial.astype(jnp.bfloat16), "row", scatter_dimension=0, tiled=True
    ).astype(jnp.float32)


def gather_rows(local):
    return lax.all_gather(local, "row", axis=0, tiled=True)


def split_heads(rows):
    return jnp.transpose(rows.reshape(rows.shape[0], -1, HD), (1, 0, 2))


def join_heads(values):
    return jnp.transpose(values, (1, 0, 2)).reshape(values.shape[1], -1)


def scores_of(queries, keys, allowed):
    scores = jnp.einsum(
        "hqe,hke->hqk", queries, keys, preferred_element_type=jnp.float32
    ) * HD ** (-0.5)
    return jnp.where(allowed[None], scores, MASKED)


def gathered(
    tokens,
    cotangent,
    segments,
    w_heads,
    w_out,
    w_up,
    w_down,
    norm_vectors,
    width_vectors,
    attend_bias,
    hidden_vectors,
):
    n_dp, n_row, n_col = (lax.axis_size(name) for name in ("dp", "row", "col"))
    row = lax.axis_index("row")
    low = jnp.bfloat16
    share = tokens.shape[1]
    width = share * n_col
    seq = tokens.shape[0]
    part = seq // n_row
    near = HEADS // n_row
    window = (HEADS - near * (n_row - 1)) * HD
    step = near * HD
    edge = width - (share + step * (n_row - 1)) if n_row > 1 else 0
    edge = window - share
    to_next = [(i, i + 1) for i in range(n_row - 1)]
    to_last = [(i + 1, i) for i in range(n_row - 1)]
    offset = edge - (share - step) * row

    vectors = jnp.concatenate(
        [
            norm_vectors.reshape(2, -1),
            width_vectors.reshape(4, -1),
            attend_bias.reshape(2, -1),
            hidden_vectors.reshape(4, -1),
        ]
    ).astype(low)
    vectors = lax.all_gather(vectors, ("row", "col", "dp"), axis=0, tiled=False)
    vectors = vectors.reshape(n_row, n_col, n_dp, 12, -1).astype(jnp.float32)
    by_col = jnp.transpose(vectors[0], (2, 0, 1, 3)).reshape(12, width)
    by_row = jnp.transpose(vectors[:, 0], (2, 0, 1, 3)).reshape(12, width)
    gain_one, shift_one, bias_out, gain_two, shift_two, bias_down = (by_col[i] for i in range(6))
    zeros = jnp.zeros((1, window), jnp.float32)
    attend_rows = lax.dynamic_slice_in_dim(by_row[6:8], row * step, window, axis=1)
    heads_bias = jnp.concatenate([attend_rows[0:1], zeros, attend_rows[1:2]]).reshape(-1)
    unit_bias = lax.dynamic_slice_in_dim(by_row[8:12], row * share, share, axis=1).reshape(-1)

    own = w_heads.astype(low).reshape(-1, 3, share)
    passed = lax.ppermute(own[:, :, share - edge :], "row", to_next)
    own = jnp.concatenate([passed, own, jnp.zeros_like(passed)], axis=2)
    own = lax.dynamic_slice_in_dim(own, offset, window, axis=2).reshape(-1, 3 * window)
    heads_matrix = lax.all_gather(own, ("col", "dp"), axis=0, tiled=True)
    out_matrix = lax.all_gather(w_out.astype(low).reshape(-1, share), ("col", "dp"), axis=0)
    out_matrix = jnp.transpose(out_matrix.reshape(n_col, share, share), (1, 0, 2))
    out_matrix = out_matrix.reshape(share, width)
    passed = lax.ppermute(out_matrix[share - edge :], "row", to_next)
    out_matrix = jnp.concatenate([passed, out_matrix, jnp.zeros_like(passed)])
    out_matrix = lax.dynamic_slice_in_dim(out_matrix, offset, window)
    owned = (jnp.arange(window) < step) | (row == n_row - 1)
    out_matrix = jnp.where(owned[:, None], out_matrix, jnp.zeros_like(out_matrix))
    up_matrix = lax.all_gather(
        w_up.astype(low).reshape(-1, 4 * share), ("col", "dp"), axis=0, tiled=True
    )
    down_matrix = lax.all_gather(w_down.astype(low).reshape(4, -1, share), ("col", "dp"), axis=0)
    down_matrix = down_matrix.reshape(n_col, n_dp, 4, -1, share)
    down_matrix = jnp.transpose(down_matrix, (2, 1, 3, 0, 4)).reshape(4 * share, width)

    inputs_low = lax.all_gather(crossed(tokens, n_row), "row", axis=1, tiled=True)
    upstream = lax.all_gather(crossed(cotangent, n_row), "row", axis=1, tiled=True)
    inputs = inputs_low.astype(jnp.float32)
    centered_one, inverse_one = normalize(inputs)
    normed_one = (centered_one * gain_one + shift_one).astype(low)
    projected = (times(normed_one, heads_matrix) + heads_bias).astype(low)
    queries, keys, values = (
        split_heads(projected[:, i * window : (i + 1) * window]) for i in range(3)
    )
    labels = lax.dynamic_slice_in_dim(segments, lax.axis_index("col") * seq, seq)
    places = jnp.arange(seq, dtype=jnp.int32)
    allowed = (labels[:, None] == labels[None, :]) & (places[:, None] >= places[None, :])
    scores = scores_of(queries, keys, allowed)
    highest = jnp.max(scores, axis=-1, keepdims=True)
    log_total = highest + jnp.log(jnp.sum(jnp.exp(scores - highest), axis=-1, keepdims=True))
    soft = jnp.exp(scores - log_total).astype(low)
    mixed = jnp.einsum("hqk,hke->hqe", soft, values, preferred_element_type=jnp.float32)
    mixed = join_heads(mixed.astype(low))
    branch = scatter_rows(times(mixed, out_matrix))
    mine = row * part
    middle = lax.dynamic_slice_in_dim(inputs, mine, part) + (branch + bias_out)
    centered_two, inverse_two = normalize(middle)
    normed_two = gather_rows((centered_two * gain_two + shift_two).astype(low))
    hidden = times(normed_two, up_matrix) + unit_bias
    activated, smooth_pull = jax.vjp(smooth, hidden)
    activated = activated.astype(low)
    result = (middle + (scatter_rows(times(activated, down_matrix)) + bias_down)).astype(low)

    down_back = times_flipped(upstream, down_matrix)
    grad_down = times_outer(activated, upstream)
    hidden_back = smooth_pull(down_back)[0].astype(low)
    grad_up = times_outer(normed_two, hidden_back)
    unit_sum = jnp.sum(hidden_back, axis=0, dtype=jnp.float32)
    normed_two_back = scatter_rows(times_flipped(hidden_back, up_matrix))
    upstream_own = lax.dynamic_slice_in_dim(upstream, mine, part).astype(jnp.float32)
    middle_back = upstream_own + norm_pull(normed_two_back, centered_two, inverse_two, gain_two)
    branch_own = middle_back.astype(low)
    branch_back = gather_rows(branch_own)
    mixed_back = times_flipped(branch_back, out_matrix).astype(low)
    grad_out = times_outer(mixed, branch_back)
    mixed_back = split_heads(mixed_back)
    scores_again = scores_of(queries, keys, allowed)
    soft = jnp.exp(scores_again - log_total)
    soft_back = jnp.einsum("hqe,hke->hqk", mixed_back, values, preferred_element_type=jnp.float32)
    row_inner = jnp.sum(soft_back * soft, axis=-1, keepdims=True)
    score_back = (soft * (soft_back - row_inner)).astype(low)
    query_back = jnp.einsum(
        "hqk,hke->hqe", score_back, keys, preferred_element_type=jnp.float32
    ) * HD ** (-0.5)
    key_back = jnp.einsum(
        "hqk,hqe->hke", score_back, queries, preferred_element_type=jnp.float32
    ) * HD ** (-0.5)
    value_back = jnp.einsum(
        "hqk,hqe->hke", soft.astype(low), mixed_back, preferred_element_type=jnp.float32
    )
    heads_back = jnp.concatenate(
        [join_heads(each.astype(low)) for each in (query_back, key_back, value_back)], axis=1
    )
    heads_sum = jnp.sum(heads_back, axis=0, dtype=jnp.float32)
    normed_one_back = scatter_rows(times_flipped(heads_back, heads_matrix))
    grad_heads = times_outer(normed_one, heads_back)
    centered_own = lax.dynamic_slice_in_dim(centered_one, mine, part)
    inverse_own = lax.dynamic_slice_in_dim(inverse_one, mine, part)
    input_back = middle_back + norm_pull(normed_one_back, centered_own, inverse_own, gain_one)

    def homeward(own):
        own = lax.all_to_all(own, "row", split_axis=1, concat_axis=0, tiled=True)
        return crossed(own, n_row)

    result_tokens = homeward(result)
    input_gradient = homeward(input_back.astype(low)).astype(jnp.float32)

    by_token = jnp.stack(
        [
            jnp.sum(normed_one_back * centered_own, axis=0),
            jnp.sum(normed_one_back, axis=0),
            jnp.sum(branch_own.astype(jnp.float32), axis=0),
            jnp.sum(normed_two_back * centered_two, axis=0),
            jnp.sum(normed_two_back, axis=0),
            jnp.sum(upstream_own, axis=0),
        ]
    )
    owned_rows = jnp.where(owned, heads_sum.reshape(3, window)[0::2], 0.0)
    by_unit = jnp.concatenate(
        [
            lax.dynamic_update_slice_in_dim(
                jnp.zeros((2, width), jnp.float32), owned_rows, row * step, axis=1
            ),
            lax.dynamic_update_slice_in_dim(
                jnp.zeros((4, width), jnp.float32), unit_sum.reshape(4, share), row * share, axis=1
            ),
        ]
    )
    sums = lax.psum(jnp.concatenate([by_token, by_unit]), ("dp", "row", "col"))
    pieces = share // n_dp
    inner = lax.axis_index("dp") * pieces
    col_sums = lax.dynamic_slice_in_dim(sums, lax.axis_index("col") * share + inner, pieces, axis=1)
    row_sums = lax.dynamic_slice_in_dim(sums, row * share + inner, pieces, axis=1)

    both = ("col", "dp")

    def to_owner(gradient):
        return lax.psum_scatter(gradient, both, scatter_dimension=0, tiled=True)

    got_heads = to_owner(grad_heads.astype(low)).reshape(pieces, 3, window)
    got_heads = jnp.where(owned, got_heads, jnp.zeros_like(got_heads))
    passed = lax.ppermute(got_heads[:, :, :edge], "row", to_last)
    got_heads = jnp.concatenate([got_heads, jnp.zeros_like(passed)], axis=2)
    got_heads = lax.dynamic_slice_in_dim(got_heads, edge - offset, share, axis=2)
    passed = jnp.concatenate([jnp.zeros((pieces, 3, share), low), passed, jnp.zeros_like(passed)], axis=2)
    got_heads = got_heads + lax.dynamic_slice_in_dim(passed, share - step + edge - offset, share, axis=2)
    low_out = jnp.where(owned[:, None], grad_out, 0.0).astype(low)
    passed = lax.ppermute(low_out[:edge], "row", to_last)
    low_out = jnp.concatenate([low_out, jnp.zeros_like(passed)])
    low_out = lax.dynamic_slice_in_dim(low_out, edge - offset, share)
    passed = jnp.concatenate([jnp.zeros((share, width), low), passed, jnp.zeros_like(passed)])
    low_out = low_out + lax.dynamic_slice_in_dim(passed, share - step + edge - offset, share)
    low_out = jnp.transpose(low_out.reshape(n_dp, pieces, n_col, share), (2, 0, 1, 3))
    got_out = to_owner(low_out.reshape(-1, share))
    got_up = to_owner(grad_up.astype(low))
    low_down = grad_down.astype(low).reshape(4, n_dp, pieces, n_col, share)
    low_down = jnp.transpose(low_down, (3, 1, 0, 2, 4)).reshape(-1, share)
    got_down = to_owner(low_down)

    reduced = [
        each.astype(jnp.float32).reshape(like.shape)
        for each, like in (
            (got_heads, w_heads),
            (got_out, w_out),
            (got_up, w_up),
            (got_down, w_down),
            (col_sums[0:2], norm_vectors),
            (col_sums[2:6], width_vectors),
            (row_sums[6:8], attend_bias),
            (row_sums[8:12], hidden_vectors),
        )
    ]
    return result_tokens, input_gradient, reduced


def adam(weight, gradient, first, second, rate, decay):
    first_new = BETA_FIRST * first + (1.0 - BETA_FIRST) * gradient
    second_new = BETA_SECOND * second + (1.0 - BETA_SECOND) * gradient * gradient
    corrected = first_new / (1.0 - BETA_FIRST**STEP)
    divisor = jnp.sqrt(second_new / (1.0 - BETA_SECOND**STEP)) + ADAM_EPSILON
    return (first_new, second_new, weight - rate * (corrected / divisor + decay * weight))


def smooth(values):
    return jax.nn.gelu(values, approximate=True)


def per_device(
    tokens,
    cotangent,
    segments,
    w_heads,
    w_out,
    w_up,
    w_down,
    norm_vectors,
    width_vectors,
    attend_bias,
    hidden_vectors,
    drift_heads,
    drift_out,
    drift_up,
    drift_down,
    drift_norm,
    drift_width,
    drift_attend,
    drift_hidden,
    power_heads,
    power_out,
    power_up,
    power_down,
    power_norm,
    power_width,
    power_attend,
    power_hidden,
):
    local = (
        tokens,
        cotangent,
        segments,
        w_heads,
        w_out,
        w_up,
        w_down,
        norm_vectors,
        width_vectors,
        attend_bias,
        hidden_vectors,
    )
    sizes = tuple(lax.axis_size(name) for name in ("dp", "row", "col"))
    if sizes == (2, 4, 4):
        result_tokens, input_gradient, reduced = fused(2, *local)
    else:
        result_tokens, input_gradient, reduced = gathered(*local)
    heads_up = adam(w_heads, reduced[0], drift_heads, power_heads, 0.05, MATRIX_DECAY)
    out_up = adam(w_out, reduced[1], drift_out, power_out, 0.2, MATRIX_DECAY)
    up_up = adam(w_up, reduced[2], drift_up, power_up, 0.05, MATRIX_DECAY)
    down_up = adam(w_down, reduced[3], drift_down, power_down, 0.025, MATRIX_DECAY)
    norm_up = adam(norm_vectors, reduced[4], drift_norm, power_norm, 0.3, 0.0)
    width_up = adam(width_vectors, reduced[5], drift_width, power_width, 0.3, 0.0)
    attend_up = adam(attend_bias, reduced[6], drift_attend, power_attend, 0.3, 0.0)
    hidden_up = adam(hidden_vectors, reduced[7], drift_hidden, power_hidden, 0.3, 0.0)
    return (
        result_tokens,
        input_gradient,
        heads_up[0],
        heads_up[1],
        heads_up[2],
        out_up[0],
        out_up[1],
        out_up[2],
        up_up[0],
        up_up[1],
        up_up[2],
        down_up[0],
        down_up[1],
        down_up[2],
        norm_up[0],
        norm_up[1],
        norm_up[2],
        width_up[0],
        width_up[1],
        width_up[2],
        attend_up[0],
        attend_up[1],
        attend_up[2],
        hidden_up[0],
        hidden_up[1],
        hidden_up[2],
    )


def solution(mesh):
    return jax.shard_map(
        per_device,
        mesh=mesh,
        in_specs=(
            P(("dp", "row"), "col"),
            P(("dp", "row"), "col"),
            P("dp"),
            P("col", "dp", None, None, "row"),
            P("row", "dp", None, "col"),
            P("col", "dp", None, None, "row"),
            P(None, "row", "dp", None, "col"),
            P(None, "col", "dp", None),
            P(None, "col", "dp", None),
            P(None, "row", "dp", None),
            P(None, "row", "dp", None),
            P("col", "dp", None, None, "row"),
            P("row", "dp", None, "col"),
            P("col", "dp", None, None, "row"),
            P(None, "row", "dp", None, "col"),
            P(None, "col", "dp", None),
            P(None, "col", "dp", None),
            P(None, "row", "dp", None),
            P(None, "row", "dp", None),
            P("col", "dp", None, None, "row"),
            P("row", "dp", None, "col"),
            P("col", "dp", None, None, "row"),
            P(None, "row", "dp", None, "col"),
            P(None, "col", "dp", None),
            P(None, "col", "dp", None),
            P(None, "row", "dp", None),
            P(None, "row", "dp", None),
        ),
        out_specs=(
            P(("dp", "row"), "col"),
            P(("dp", "row"), "col"),
            P("col", "dp", None, None, "row"),
            P("col", "dp", None, None, "row"),
            P("col", "dp", None, None, "row"),
            P("row", "dp", None, "col"),
            P("row", "dp", None, "col"),
            P("row", "dp", None, "col"),
            P("col", "dp", None, None, "row"),
            P("col", "dp", None, None, "row"),
            P("col", "dp", None, None, "row"),
            P(None, "row", "dp", None, "col"),
            P(None, "row", "dp", None, "col"),
            P(None, "row", "dp", None, "col"),
            P(None, "col", "dp", None),
            P(None, "col", "dp", None),
            P(None, "col", "dp", None),
            P(None, "col", "dp", None),
            P(None, "col", "dp", None),
            P(None, "col", "dp", None),
            P(None, "row", "dp", None),
            P(None, "row", "dp", None),
            P(None, "row", "dp", None),
            P(None, "row", "dp", None),
            P(None, "row", "dp", None),
            P(None, "row", "dp", None),
        ),
        check_vma=False,
    )
```

```python
import functools

import jax
import jax.numpy as jnp
from jax import lax
from jax.experimental import pallas as pl
from jax.experimental.pallas import tpu as pltpu
from jax.sharding import PartitionSpec as P

HEADS = 25
HD = 64
TOK_DEV = 128
STEP = 10


NORM_EPSILON = 1e-05
BETA_FIRST = 0.9
BETA_SECOND = 0.999
ADAM_EPSILON = 1e-08
MATRIX_DECAY = 0.1
MASKED = -1e30
ROOT = (2.0 / 3.141592653589793) ** 0.5
CUBIC = 0.044715
VMEM_BYTES = 66 * 1024 * 1024


def adam_terms(weight, gradient, first, second, rate, decay):
    first_new = BETA_FIRST * first + (1.0 - BETA_FIRST) * gradient
    second_new = BETA_SECOND * second + (1.0 - BETA_SECOND) * gradient * gradient
    corrected = first_new / (1.0 - BETA_FIRST**STEP)
    divisor = jnp.sqrt(second_new / (1.0 - BETA_SECOND**STEP)) + ADAM_EPSILON
    return (first_new, second_new, weight - rate * (corrected / divisor + decay * weight))


def smooth(values):
    return jax.nn.gelu(values, approximate=True)


def ceil_to(count, unit):
    return -(-count // unit) * unit


class Sizes:
    def __init__(self, share, pieces, seq):
        self.share = share
        self.pieces = pieces
        self.block = ceil_to(pieces, 16)
        self.pair = 2 * self.block
        self.width = 4 * self.pair
        self.seq = seq
        self.part = seq // 4
        self.both = 2 * seq
        self.main = (HEADS // 4) * HD
        self.slack = share - self.main
        self.heads = ceil_to(3 * share, 256)
        self.mixed = ceil_to(pieces + 1, 128)
        self.hidden = ceil_to(4 * pieces + 1, 128)
        self.tiles = self.width // 128


class Place:
    def __init__(self):
        self.d, self.r, self.c = (lax.axis_index(name) for name in ("dp", "row", "col"))
        self.y, self.k = self.r // 2, self.r % 2

    def plane(self, mask):
        d = 1 - self.d if mask & 4 else self.d
        y = 1 - self.y if mask & 2 else self.y
        k = 1 - self.k if mask & 1 else self.k
        return d, 2 * y + k

    def peer(self, mask):
        d, r = self.plane(mask)
        return (d, r, self.c)

    def along(self, c):
        return (self.d, self.r, c)


def run(when, action):
    if when is None:
        action()
    else:
        pl.when(when)(action)


class Wires:
    def __init__(self, sends, arrivals):
        self.sends, self.arrivals = sends, arrivals
        self.used = 0
        self.open = []

    def make(self, source, target, index, slot, device):
        return pltpu.make_async_remote_copy(
            src_ref=source,
            dst_ref=target,
            send_sem=self.sends.at[index],
            recv_sem=self.arrivals.at[slot],
            device_id=device,
            device_id_type=pl.DeviceIdType.MESH,
        )

    def copy(self, source, target, device, slot, when=None):
        made = self.make(source, target, self.used, slot, device)
        self.used += 1
        run(when, made.start)
        item = (when, made)
        self.open.append(item)
        return item

    def arrived(self, target, slot, device, when=None):
        run(when, self.make(target, target, 0, slot, device).wait_recv)

    def close(self, some=None):
        for item in self.open if some is None else some:
            run(item[0], item[1].wait_send)
        self.open = [] if some is None else [o for o in self.open if all(o is not s for s in some)]


def greet(at, diagonal):
    barrier = pltpu.get_barrier_semaphore()

    def signal(device):
        pl.semaphore_signal(
            barrier, inc=1, device_id=device, device_id_type=pl.DeviceIdType.MESH
        )

    for mask in range(1, 8):
        signal(at.peer(mask))
    for c in range(4):
        run(at.c != c, functools.partial(signal, (at.d, at.r, c)))
        if diagonal:
            run(at.c != c, functools.partial(signal, (1 - at.d, at.r, c)))
    run(at.r != at.c, functools.partial(signal, (at.d, at.c, at.r)))
    pl.semaphore_wait(barrier, (13 if diagonal else 10) + jnp.where(at.r != at.c, 1, 0))


def rows_at(start, size):
    return pl.ds(pl.multiple_of(start, 16), size)


def lanes_at(start, size):
    return pl.ds(pl.multiple_of(start, 128), size)


def choose(shape, source):
    rows = lax.broadcasted_iota(jnp.int32, shape, 0)
    wanted = source(lax.broadcasted_iota(jnp.int32, shape, 1))
    return (rows == wanted).astype(jnp.bfloat16)


def edge_source(column):
    part, place = column // HD, column % HD
    wanted = jnp.where(place >= 16, 128 * part + place - 16, 384 + 16 * part + place)
    return jnp.where(part < 3, wanted, -1)


def spread_source(column):
    part, place = column // 128, column % 128
    return jnp.where(place < HD, HD * part + place, -1)


def picked(values, table):
    return jnp.dot(values, table, preferred_element_type=jnp.float32).astype(jnp.bfloat16)


def times(left, right):
    return jnp.dot(left, right, preferred_element_type=jnp.float32)


def times_flipped(left, right):
    return lax.dot_general(
        left, right, (((1,), (1,)), ((), ())), preferred_element_type=jnp.float32
    )


def times_outer(left, right):
    return lax.dot_general(
        left, right, (((0,), (0,)), ((), ())), preferred_element_type=jnp.float32
    )


def over_tiles(total, action, tile=256):
    @pl.loop(0, total // tile)
    def _(i):
        action(i * tile, tile)

    if total % tile:
        action(total - total % tile, total % tile)


def turned(values):
    return values.astype(jnp.float32).T


def gather_group(wires, masks, region, at, base):
    own = region(*at.plane(0))
    sent = [wires.copy(own, own, at.peer(mask), base + mask) for mask in (1, *masks)]

    def finish():
        for mask in masks:
            there = region(*at.plane(mask))
            wires.arrived(there, base + mask, at.peer(mask))
            sent.append(wires.copy(there, there, at.peer(1), base + mask + 1))
        for mask in (0, *masks):
            there = region(*at.plane(mask | 1))
            wires.arrived(there, base + (mask | 1), at.peer(1))

    return finish, sent


def scatter_group(wires, masks, partial, chunk, near, mid, far, at, base):
    sent = []
    for i, mask in enumerate((0, *masks)):
        rows = rows_at(chunk(*at.plane(mask | 1)), near.shape[1])
        sent.append(wires.copy(partial.at[rows], near.at[i], at.peer(1), base + i))

    def rows_of(mask):
        return rows_at(chunk(*at.plane(mask)), near.shape[1])

    def onward():
        for i, mask in enumerate((0, *masks)):
            wires.arrived(near.at[i], base + i, at.peer(1))
        for i, mask in enumerate(masks):
            both = partial[rows_of(mask)].astype(jnp.float32) + near[i + 1].astype(jnp.float32)
            mid[i] = both.astype(jnp.bfloat16)
            sent.append(wires.copy(mid.at[i], far.at[i], at.peer(mask), base + 4 + i))

    def total():
        for i, mask in enumerate(masks):
            wires.arrived(far.at[i], base + 4 + i, at.peer(mask))
        result = partial[rows_of(0)].astype(jnp.float32) + near[0].astype(jnp.float32)
        for i in range(len(masks)):
            result = result + far[i].astype(jnp.float32)
        return result

    return onward, total, sent


def spread_col(wires, region, at, base, source=None):
    own = region(at.c)
    source = own if source is None else source
    for c in range(4):
        other = (at.c != c) & (at.c + c != 3 if c in (0, 3) else at.c != c)
        wires.copy(source, own, at.along(c), base + at.c, other)

    def relay():
        for here, start, end in ((2, 0, 3), (1, 3, 0)):
            block = region(start)
            wires.arrived(block, base + start, at.along(start), at.c == here)
            wires.copy(block, block, at.along(end), base + start, at.c == here)

    def finish():
        for c in range(4):
            needed = at.c != c
            if c == 0:
                needed = needed & (at.c != 2)
            if c == 3:
                needed = needed & (at.c != 1)
            wires.arrived(region(c), base + c, at.along(c), needed)

    return relay, finish


def collect_col(wires, piece, landing, rest, at, base):
    low_end, high_end = at.c == 0, at.c == 3
    ends = low_end | high_end
    via = jnp.where(low_end, 1, 2)

    def pick(*choices):
        return jnp.where(
            low_end,
            choices[0],
            jnp.where(at.c == 1, choices[1], jnp.where(high_end, choices[3], choices[2])),
        )

    order = (pick(3, 0, 3, 0), pick(2, 2, 1, 1), pick(1, 3, 0, 2), at.c)
    target = landing.at[at.c]

    def send(step):
        there = order[step]
        block = piece(there)
        if step == 0:
            wires.copy(block, rest, at.along(via), base + 4, ends)
            wires.copy(block, target, at.along(there), base + at.c, jnp.logical_not(ends))
        elif step == 1:
            wires.copy(block, target, at.along(there), base + at.c)
        elif step == 2:
            wires.copy(block, target, at.along(there), base + at.c, ends)

    def relay(add):
        @pl.when(jnp.logical_not(ends))
        def _():
            wires.make(rest, rest, 0, base + 4, at.along(0)).wait_recv()
            add(order[2])

        wires.copy(piece(order[2]), target, at.along(order[2]), base + at.c, jnp.logical_not(ends))

    def arrived(c):
        wires.arrived(landing.at[c], base + c, at.along(c), sent_from(c))

    def sent_from(c):
        here = at.c != c
        if c in (0, 3):
            here = here & (at.c != 3 - c)
        return here

    return order, send, relay, arrived, sent_from


def forward_kernel(
    sz,
    x_home_in,
    dy_home_in,
    w_heads,
    w_out,
    w_up,
    w_down,
    norm_vectors,
    width_vectors,
    attend_bias,
    hidden_vectors,
    segments,
    wh_out,
    wo_out,
    wu_out,
    wd_out,
    h1_t_out,
    h2_t_out,
    dy_t_out,
    dy_out,
    u_out,
    gl_out,
    qw_out,
    kw_out,
    vw_out,
    a_nat_out,
    lse_out,
    x2_out,
    x_own_out,
    vec_rows_out,
    wh,
    wo,
    wu,
    wd,
    h1_t,
    h2_t,
    dy_t,
    dy,
    u,
    gl,
    qw,
    kw,
    vw,
    a_nat,
    lse,
    x2,
    x_own,
    vec_rows,
    x_t,
    h1,
    h2,
    own_qkv,
    aw,
    vec,
    part,
    edge_out,
    edge_in,
    edge_back,
    near,
    mid,
    far,
    x_raw,
    dy_raw,
    heads_raw,
    out_raw,
    up_raw,
    down_raw,
    x_home,
    dy_home,
    wh_own,
    wo_own,
    wu_own,
    wd_own,
    vec_own,
    col_labels,
    sends,
    arrivals,
    locals_,
):
    at = Place()
    wires = Wires(sends, arrivals)
    low = jnp.bfloat16
    pair, block, pieces = sz.pair, sz.block, sz.pieces
    fetched = []
    for i, (source, target) in enumerate(
        (
            (x_home_in, x_raw),
            (w_heads, heads_raw),
            (w_up, up_raw),
            (w_out, out_raw),
            (w_down, down_raw),
            (dy_home_in, dy_raw),
        )
    ):
        fetched.append(pltpu.make_async_copy(source, target, locals_.at[40 + i]))
        fetched[i].start()
    row_labels = segments.at[:, lanes_at(sz.seq * at.c, sz.seq)]

    def halves(value, target):
        value = value.astype(jnp.float32)
        gap = jnp.zeros((block - pieces, value.shape[1]), jnp.float32)
        parts = [value[0:pieces], gap, value[pieces : 2 * pieces], gap]
        target[...] = jnp.concatenate(parts, axis=0).astype(low)

    def quarter(row):
        return row.astype(low).astype(jnp.float32) * 0.25

    def placed(row):
        both = jnp.concatenate([row, row], axis=1)
        half_of = lax.broadcasted_iota(jnp.int32, both.shape, 1) // pieces
        return jnp.where(half_of == at.d, both, 0.0)

    def with_row(value, row):
        gap = jnp.zeros((block - pieces - 1, value.shape[1]), jnp.float32)
        return jnp.concatenate([value, row, gap], axis=0)

    flat = jnp.concatenate(
        [norm_vectors[0], norm_vectors[1], width_vectors[1], width_vectors[2]], axis=0
    )
    flat = jnp.concatenate([flat, jnp.zeros((124, pieces), jnp.float32)], axis=0)
    flat = jnp.concatenate([flat, jnp.zeros((128, 256 - pieces), jnp.float32)], axis=1)
    where_row = lax.broadcasted_iota(jnp.int32, flat.shape, 0)
    where_lane = lax.broadcasted_iota(jnp.int32, flat.shape, 1)
    carrier = (where_lane == pieces) & ((where_row == 1) | (where_row == 3))
    vec_own[...] = jnp.where(carrier, 1.0, flat).T[0:block].astype(low)
    fetched[0].wait()
    halves(x_raw[...], x_home)
    greet(at, False)

    def x_block(d, r):
        return x_t.at[rows_at(pair * r, pair)]

    def dy_block(d, r):
        return dy_t.at[rows_at(pair * r, pair), lanes_at(sz.seq * d, sz.seq)]

    across = (at.d, at.c, at.r)
    same = at.r == at.c
    stay, used = [], [0]

    def keep(source, target, when=None):
        made = pltpu.make_async_copy(source, target, locals_.at[used[0]])
        used[0] += 1
        run(when, made.start)
        stay.append((when, made))

    def flush(source, target):
        made = pltpu.make_async_copy(source, target, locals_.at[used[0]])
        used[0] += 1
        made.start()
        flushed.append(made)

    flushed = []

    def vec_block(d, c):
        return vec.at[rows_at(pair * c + block * d, block)]

    def wh_block(d):
        return lambda c: wh.at[rows_at(pair * c + block * d, block)]

    def wo_block(d):
        return lambda c: wo.at[rows_at(pair * c, pair), lanes_at(sz.mixed * d, sz.mixed)]

    def wu_block(d):
        return lambda c: wu.at[rows_at(pair * c + block * d, block)]

    def wd_block(half):
        return lambda c: wd.at[rows_at(pair * c + block * half, block)]

    wires.copy(x_home, x_block(at.d, at.c), across, 0, jnp.logical_not(same))
    keep(x_home, x_block(at.d, at.c), same)
    for c in range(4):
        wires.copy(vec_own, vec_block(at.d, at.c), at.along(c), 2 + at.c, at.c != c)
    wires.copy(vec_own, vec_block(at.d, at.c), at.peer(4), 6 + at.c)
    keep(vec_own, vec_block(at.d, at.c))

    fetched[1].wait()
    for r in range(4):

        @pl.when(at.r == r)
        def _():
            cut = sz.share - sz.slack * r
            tails = []
            for i in range(3):
                value = heads_raw[i]
                row = jnp.zeros((1, sz.share), jnp.float32)
                if i != 1:
                    row = placed(quarter(attend_bias[i // 2]))
                value = with_row(value, row)
                if r:
                    value = jnp.concatenate([value[:, cut:], value[:, 0:cut]], axis=1)
                wh_own[:, sz.main * i : sz.main * (i + 1)] = value[:, 0 : sz.main].astype(low)
                tails.append(value[:, sz.main :])
            tails.append(jnp.zeros((block, sz.heads - 3 * sz.share), jnp.float32))
            wh_own[:, 3 * sz.main :] = jnp.concatenate(tails, axis=1).astype(low)

    wh_relay, wh_done = spread_col(wires, wh_block(at.d), at, 20, wh_own)
    wires.copy(wh_own, wh_block(at.d)(at.c), at.peer(4), 24 + at.c)
    keep(wh_own, wh_block(at.d)(at.c))

    fetched[2].wait()
    gap = jnp.zeros((block, sz.hidden - 4 * pieces), jnp.float32)
    values = [
        with_row(up_raw[:, j, :], placed(quarter(hidden_vectors[j]))) for j in range(4)
    ]
    for i in range(2):
        lanes = slice(pieces * i, pieces * (i + 1))
        whole = jnp.concatenate([value[:, lanes] for value in values] + [gap], axis=1)
        wu_own[:, sz.hidden * i : sz.hidden * (i + 1)] = whole.astype(low)
    wires.copy(
        wu_own.at[:, lanes_at(sz.hidden * (1 - at.d), sz.hidden)],
        wu_block(at.d)(at.c),
        at.peer(4),
        10,
    )
    keep(wu_own.at[:, lanes_at(sz.hidden * at.d, sz.hidden)], wu_block(at.d)(at.c))

    def turned_halves(value, target, lanes):
        flipped = value.T
        gap = jnp.zeros((block - pieces, flipped.shape[1]), jnp.float32)
        parts = [flipped[0:pieces], gap, flipped[pieces : 2 * pieces], gap]
        target[:, lanes] = jnp.concatenate(parts, axis=0).astype(low)

    fetched[3].wait()
    value = with_row(out_raw[...], placed(quarter(width_vectors[0])))
    value = jnp.concatenate([value, jnp.zeros((sz.mixed - block, sz.share), jnp.float32)], axis=0)
    for i in range(sz.mixed // 128):
        lanes = slice(128 * i, 128 * (i + 1))
        turned_halves(value[lanes], wo_own, lanes)
    wo_relay, wo_done = spread_col(wires, wo_block(at.d), at, 28, wo_own)
    wires.copy(wo_own, wo_block(at.d)(at.c), at.peer(4), 32 + at.c)
    keep(wo_own, wo_block(at.d)(at.c))
    wu_first, wu_first_done = spread_col(
        wires, wu_block(at.d), at, 36, wu_own.at[:, lanes_at(sz.hidden * at.d, sz.hidden)]
    )

    for when, made in stay:
        run(when, made.wait)
    wires.arrived(x_block(at.d, at.r), 0, across, jnp.logical_not(same))
    x_done, _ = gather_group(wires, (2,), x_block, at, 12)

    fetched[4].wait()
    for i in range(sz.hidden // 128):
        rows = slice(128 * i, 128 * (i + 1))
        if 128 * (i + 1) <= 4 * pieces:
            value = down_raw[rows]
        else:
            value = jnp.concatenate(
                [
                    down_raw[128 * i : 4 * pieces],
                    placed(quarter(width_vectors[3])),
                    jnp.zeros((sz.hidden - 4 * pieces - 1, sz.share), jnp.float32),
                ],
                axis=0,
            )
        turned_halves(value, wd_own, rows)
    del stay[:]
    keep(wd_own, wd.at[rows_at(pair * at.c, pair)])
    fetched[5].wait()
    halves(dy_raw[...], dy_home)
    col_labels[...] = jnp.concatenate([row_labels[...]] * 8, axis=0).astype(jnp.float32).T[:, 0:1]
    x_done()

    for c in range(4):
        wires.arrived(vec_block(at.d, c), 2 + c, at.along(c), at.c != c)
    wires.arrived(vec_block(1 - at.d, at.c), 6 + at.c, at.peer(4))
    for step in range(1, 4):
        there = (at.c + step) % 4
        wires.copy(
            vec_block(at.d, there), vec_block(at.d, there), at.peer(4), 6 + there
        )
    for step in range(1, 4):
        there = (at.c + step) % 4
        wires.arrived(vec_block(1 - at.d, there), 6 + there, at.peer(4))
    features = 4.0 * sz.share

    def add_up(i, carry):
        rows = rows_at(128 * i, 128)
        value = x_t[rows].astype(jnp.float32)
        return (
            carry[0] + jnp.sum(value, axis=0, keepdims=True),
            carry[1] + jnp.sum(value * value, axis=0, keepdims=True),
        )

    zero = jnp.zeros((1, sz.seq), jnp.float32)
    sums = lax.fori_loop(0, sz.tiles, add_up, (zero, zero))
    center = sums[0] / features
    inverse = lax.rsqrt(sums[1] / features - center * center + NORM_EPSILON)

    @pl.loop(0, sz.tiles)
    def _(i):
        rows, lanes = rows_at(128 * i, 128), lanes_at(128 * i, 128)
        vectors = vec[rows].astype(jnp.float32)
        value = (x_t[rows].astype(jnp.float32) - center) * inverse
        value = value * vectors[:, 0:1] + vectors[:, 1:2]
        h1_t[rows] = value.astype(low)
        h1[:, lanes] = value.T.astype(low)
        mine = x_t[rows, lanes_at(sz.part * at.r, sz.part)]
        x_own[:, lanes] = turned(mine).astype(low)
        vec_rows[:, lanes] = vectors.T[0:8]

    flush(h1_t, h1_t_out)
    flush(x_own, x_own_out)
    flush(vec_rows, vec_rows_out)

    wh_relay()
    for c in range(4):
        needed = at.c != c
        if c == 0:
            needed = needed & (at.c != 2)
        if c == 3:
            needed = needed & (at.c != 1)
        wires.arrived(wh_block(at.d)(c), 20 + c, at.along(c), needed)
        wires.copy(wh_block(at.d)(c), wh_block(at.d)(c), at.peer(4), 24 + c, at.c != c)

    wires.arrived(wu_block(1 - at.d)(at.c), 10, at.peer(4))
    wu_second, wu_second_done = spread_col(wires, wu_block(1 - at.d), at, 40)
    for c in range(4):
        wires.arrived(wh_block(1 - at.d)(c), 24 + c, at.peer(4))
    flush(wh, wh_out)

    @pl.loop(0, sz.heads // 256)
    def _(i):
        lanes = lanes_at(256 * i, 256)
        own_qkv[:, lanes] = times(h1[...], wh[:, lanes]).astype(low)

    wires.copy(dy_home, dy_block(at.d, at.c), across, 1, jnp.logical_not(same))
    for when, made in stay:
        run(when, made.wait)
    wd_first, wd_first_done = spread_col(wires, wd_block(0), at, 44)
    wd_second, wd_second_done = spread_col(wires, wd_block(1), at, 48)
    made = pltpu.make_async_copy(dy_home, dy_block(at.d, at.c), locals_.at[46])
    run(same, made.start)
    run(same, made.wait)

    starts = (0, sz.main, 2 * sz.main, 3 * sz.main)
    ends = jnp.concatenate([own_qkv[:, s : s + 128] for s in starts], axis=1)
    edge_out[...] = picked(ends, choose((512, 256), edge_source))
    last = at.r == 3

    @pl.when(at.r == 0)
    def _():
        edge_in[...] = jnp.zeros_like(edge_in)

    wires.copy(edge_out, edge_in, (at.d, at.r + 1, at.c), 52, at.r < 3)
    spread = choose((256, 384), spread_source)
    extra = picked(edge_out[...], spread)
    wires.arrived(edge_in, 52, (at.d, at.r - 1, at.c), at.r > 0)
    first = picked(edge_in[...], spread)
    lane = lax.broadcasted_iota(jnp.int32, (sz.seq, 128), 1)
    for i, target in enumerate((qw, kw, vw)):
        start = starts[i]
        target[:, 0:128] = jnp.where(
            lane < sz.slack * at.r,
            first[:, 128 * i : 128 * i + 128],
            own_qkv[:, start : start + 128],
        )
        target[:, 128 : sz.main] = own_qkv[:, start + 128 : start + sz.main]
        target[:, sz.main : sz.main + 128] = extra[:, 128 * i : 128 * i + 128]
    flush(qw, qw_out)
    flush(kw, kw_out)
    flush(vw, vw_out)

    wo_relay()
    for c in range(4):
        needed = at.c != c
        if c == 0:
            needed = needed & (at.c != 2)
        if c == 3:
            needed = needed & (at.c != 1)
        wires.arrived(wo_block(at.d)(c), 28 + c, at.along(c), needed)
        wires.copy(wo_block(at.d)(c), wo_block(at.d)(c), at.peer(4), 32 + c, at.c != c)

    wires.arrived(dy_block(at.d, at.r), 1, across, jnp.logical_not(same))
    dy_done, _ = gather_group(wires, (2, 4, 6), dy_block, at, 56)

    half = sz.seq // 2

    def heads_of(p, count):
        tile = lanes_at(128 * p, 128)
        for q in range(2):
            rows = slice(half * q, half * (q + 1))
            keys = half * (q + 1)
            order = lax.broadcasted_iota(jnp.int32, (half, keys), 0) + half * q
            allowed = (col_labels[rows, :] == row_labels[:, 0:keys].astype(jnp.float32)) & (
                order >= lax.broadcasted_iota(jnp.int32, (half, keys), 1)
            )
            lanes = lax.broadcasted_iota(jnp.int32, (half, 128), 1)
            side = lanes // HD
            total = jnp.zeros((half, 128), jnp.float32)
            for h in range(count):
                queries = jnp.where(side == h, qw[rows, tile].astype(jnp.float32) * HD ** (-0.5), 0.0)
                scores = times_flipped(queries.astype(low), kw[0:keys, tile])
                scores = jnp.where(allowed, scores, MASKED)
                highest = jnp.max(scores, axis=1, keepdims=True)
                raised = jnp.exp(scores - highest)
                summed = jnp.sum(raised, axis=1, keepdims=True)
                found = highest + jnp.log(summed)
                lse[rows, :] = jnp.where(lanes == 2 * p + h, found, lse[rows, :])
                soft = (raised * (1.0 / summed)).astype(low)
                total = jnp.where(side == h, times(soft, vw[0:keys, tile]), total)
            aw[rows, tile] = total.astype(low)

    lse[...] = jnp.zeros_like(lse)

    @pl.loop(0, sz.main // 128)
    def _(p):
        heads_of(p, 2)

    @pl.when(last)
    def _():
        heads_of(sz.main // 128, 1)
        edge_back[...] = aw[:, sz.main : sz.main + 128]

    flush(lse, lse_out)

    wires.copy(aw.at[:, 0:128], edge_back, (at.d, at.r - 1, at.c), 53, at.r > 0)
    wu_first()
    wires.arrived(edge_back, 53, (at.d, at.r + 1, at.c), at.r < 3)

    def natural(column):
        inner = column % sz.mixed
        place = sz.pieces * (column // sz.mixed) + inner + sz.slack * at.r
        return jnp.where(inner < sz.pieces, place, -1)

    def natural_main(column):
        place = natural(column)
        return jnp.where(place < sz.main, place, -1)

    def natural_edge(column):
        return natural(column) - sz.main

    mixed = times(aw[:, 0 : sz.main], choose((sz.main, 2 * sz.mixed), natural_main))
    mixed = mixed + times(edge_back[...], choose((128, 2 * sz.mixed), natural_edge))
    ones = lax.broadcasted_iota(jnp.int32, mixed.shape, 1) % sz.mixed == sz.pieces
    a_nat[...] = jnp.where(ones, 1.0, mixed).astype(low)
    for c in range(4):
        wires.arrived(wo_block(1 - at.d)(c), 32 + c, at.peer(4))
    flush(wo, wo_out)
    flush(a_nat, a_nat_out)

    def project(start, tile):
        out = times_flipped(a_nat[...], wo[rows_at(start, tile)])
        part[:, lanes_at(start, tile)] = out.astype(low)

    over_tiles(sz.width, project)

    onward, total, _ = scatter_group(
        wires, (2,), part, lambda d, r: sz.part * r, near, mid, far, at, 64
    )
    onward()
    middle = x_own[...].astype(jnp.float32) + total()
    x2[...] = middle
    flush(x2, x2_out)
    center = jnp.sum(middle, axis=1, keepdims=True) / features
    spread_two = jnp.sum(middle * middle, axis=1, keepdims=True) / features - center * center
    normed = (middle - center) * lax.rsqrt(spread_two + NORM_EPSILON)
    own_rows = rows_at(sz.part * (4 * at.d + at.r), sz.part)
    h2[own_rows] = (normed * vec_rows[2:3] + vec_rows[3:4]).astype(low)
    h2_done, _ = gather_group(
        wires, (2, 4, 6), lambda d, r: h2.at[rows_at(sz.part * (4 * d + r), sz.part)], at, 72
    )
    wu_second()
    dy_done()
    flush(dy_t, dy_t_out)
    wd_first()

    @pl.loop(0, sz.tiles)
    def _(i):
        dy[:, lanes_at(128 * i, 128)] = turned(dy_t[rows_at(128 * i, 128)]).astype(low)

    flush(dy, dy_out)
    h2_done()
    wu_first_done()
    wu_second_done()
    flush(wu, wu_out)

    def expand(start, tile):
        lanes = lanes_at(start, tile)
        value = times(h2[...], wu[:, lanes])
        u[:, lanes] = value
        inner = jnp.tanh(ROOT * (value + CUBIC * value * value * value))
        value = 0.5 * value * (1.0 + inner)
        column = lax.broadcasted_iota(jnp.int32, value.shape, 1) + start
        gl[:, lanes] = jnp.where(column == 4 * sz.pieces, 1.0, value).astype(low)

    over_tiles(sz.hidden, expand)

    flush(u, u_out)
    flush(gl, gl_out)
    wd_second()

    @pl.loop(0, sz.tiles)
    def _(i):
        h2_t[rows_at(128 * i, 128)] = turned(h2[:, lanes_at(128 * i, 128)]).astype(low)

    flush(h2_t, h2_t_out)
    wd_first_done()
    wd_second_done()
    flush(wd, wd_out)
    wires.close()
    for made in flushed:
        made.wait()


def backward_kernel(
    sz,
    dy_all,
    dy_t_all,
    u_all,
    gl_all,
    h2_t_all,
    wd_all,
    wu_all,
    wo_all,
    wh_all,
    h1_t_all,
    qw_all,
    kw_all,
    vw_all,
    a_nat_all,
    lse_all,
    x2_all,
    x_own_all,
    vec_rows,
    segments,
    out_down,
    out_up,
    out_out,
    out_heads,
    result_home,
    grad_home,
    vec_out,
    zd,
    zu,
    zo,
    zh,
    rd,
    ru,
    ro,
    rh,
    qw,
    kw,
    vw,
    a_nat,
    lse,
    x2,
    x_own,
    xu,
    dy,
    dy_t,
    u,
    gl,
    h2_t,
    wd,
    wu,
    wo,
    wh,
    dy_own,
    du,
    gw,
    gu,
    go,
    xh,
    xo,
    near_two,
    far_two,
    near_res,
    far_res,
    near_one,
    far_one,
    mid,
    dob,
    da,
    dqw,
    dkw,
    dvw,
    dk_sum,
    dv_sum,
    dx2,
    edge_out,
    edge_in,
    fore_out,
    fore_in,
    col_labels,
    stage,
    home,
    home_two,
    va,
    vb,
    sends,
    arrivals,
    locals_,
):
    at = Place()
    wires = Wires(sends, arrivals)
    low = jnp.bfloat16
    pair, block = sz.pair, sz.block
    features = 4.0 * sz.share
    used = [0]

    def load(source, target, when=None):
        made = pltpu.make_async_copy(source, target, locals_.at[used[0]])
        used[0] += 1
        run(when, made.start)
        return made

    own_rows = rows_at(sz.part * (4 * at.d + at.r), sz.part)
    loads = [
        load(s, t)
        for s, t in (
            (dy_t_all, dy_t),
            (gl_all, gl),
            (dy_all, dy),
            (wd_all, wd),
            (u_all, u),
            (dy_all.at[own_rows], dy_own),
            (wu_all, wu),
            (h2_t_all, h2_t),
            (wo_all, wo),
            (wh_all, wh),
            (x2_all, x2),
            (a_nat_all, a_nat),
            (qw_all, qw),
            (kw_all, kw),
            (vw_all, vw),
            (lse_all, lse),
            (x_own_all, x_own),
        )
    ]
    greet(at, False)
    stay = []

    gd = gw.at[:, 0 : sz.hidden]
    loads[0].wait()
    loads[1].wait()
    order, d_send, d_relay, d_arrived, d_from = collect_col(
        wires, lambda c: gd.at[rows_at(pair * c, pair)], zd, rd, at, 0
    )
    for step in range(4):
        rows = rows_at(pair * order[step], pair)
        gw[rows, 0 : sz.hidden] = times(dy_t[rows], gl[...]).astype(low)
        d_send(step)

    def relay_of(rest, block):
        def add(there):
            parts = (
                load(rest.at[:, 0:512], dqw.at[0:pair, 0:512]),
                load(rest.at[:, 512 : sz.hidden], dkw.at[0:pair, 0 : sz.hidden - 512]),
            )
            for made in parts:
                made.wait()
            rows = rows_at(pair * there, pair)
            for held, start, stop in ((dqw, 0, 512), (dkw, 512, sz.hidden)):
                both = block[rows, start:stop].astype(jnp.float32)
                both = both + held[0:pair, 0 : stop - start].astype(jnp.float32)
                block[rows, start:stop] = both.astype(low)

        return add

    gd_sends = list(wires.open)

    for made in loads[2:6]:
        made.wait()

    def through(start, tile):
        lanes = lanes_at(start, tile)
        upstream = times(dy[...], wd[:, lanes])
        value = u[:, lanes]
        inner = jnp.tanh(ROOT * (value + CUBIC * value * value * value))
        slope = 0.5 * (1.0 + inner) + 0.5 * value * (1.0 - inner * inner) * ROOT * (
            1.0 + 3.0 * CUBIC * value * value
        )
        du[:, lanes] = (upstream * slope).astype(low)

    over_tiles(sz.hidden, through)
    loads[6].wait()

    def back_up(start, tile):
        dy[:, lanes_at(start, tile)] = times_flipped(du[...], wu[rows_at(start, tile)]).astype(low)

    over_tiles(sz.width, back_up)

    def chunk_both(d, r):
        return sz.part * (4 * d + r)

    two_onward, two_total, two_sent = scatter_group(
        wires, (2, 4, 6), dy, chunk_both, near_two, mid, far_two, at, 16
    )
    loads[7].wait()
    order, u_send, u_relay, u_arrived, u_from = collect_col(
        wires, lambda c: gu.at[rows_at(pair * c, pair)], zu, ru, at, 5
    )
    for step in range(4):
        rows = rows_at(pair * order[step], pair)
        gu[rows] = times(h2_t[rows], du[...]).astype(low)
        u_send(step)
        if step == 1:
            two_onward()
    before = len(wires.open)
    d_relay(relay_of(rd, gd))
    gd_sends += wires.open[before:]

    def norm_back(upstream, values, gain):
        center = jnp.sum(values, axis=1, keepdims=True) / features
        spread = jnp.sum(values * values, axis=1, keepdims=True) / features - center * center
        inverse = lax.rsqrt(spread + NORM_EPSILON)
        centered = (values - center) * inverse
        scaled = upstream * gain
        inner = (
            scaled
            - jnp.sum(scaled, axis=1, keepdims=True) / features
            - centered * (jnp.sum(scaled * centered, axis=1, keepdims=True) / features)
        )
        return (
            inner * inverse,
            jnp.sum(upstream * centered, axis=0, keepdims=True),
            jnp.sum(upstream, axis=0, keepdims=True),
        )

    loads[10].wait()
    h2_back = two_total()
    through_norm, gain_two, shift_two = norm_back(h2_back, x2[...], vec_rows[2:3])
    middle_back = dy_own[...].astype(jnp.float32) + through_norm
    dx2[...] = middle_back
    va[0, 2:3] = gain_two
    va[0, 3:4] = shift_two
    va[0, 4:8] = jnp.zeros((4, sz.width), jnp.float32)
    dob[rows_at(sz.part * at.r, sz.part)] = middle_back.astype(low)
    dob_done, dob_sent = gather_group(
        wires, (2,), lambda d, r: dob.at[rows_at(sz.part * r, sz.part)], at, 24
    )
    h1_load = load(h1_t_all, dy_t.at[:, 0 : sz.seq])

    def contract(start, tile):
        out = times_flipped(gl[...], wd[rows_at(start, tile)])
        dy[:, lanes_at(start, tile)] = out.astype(low)

    wires.close(two_sent)
    over_tiles(sz.width, contract)
    res_onward, res_total, res_sent = scatter_group(
        wires, (2, 4, 6), dy, chunk_both, near_res, mid, far_res, at, 32
    )

    dob_done()
    loads[11].wait()
    loads[8].wait()
    da[...] = times(dob[...], wo[...]).astype(low)
    slack, main = sz.slack, sz.main

    def from_natural(place):
        wanted = sz.mixed * (place // sz.pieces) + place % sz.pieces
        return jnp.where((place >= 0) & (place < sz.share), wanted, -1)

    fore_out[...] = picked(
        da[...], choose((2 * sz.mixed, 128), lambda j: from_natural(j + main - slack * at.r))
    )

    @pl.when(at.r == 0)
    def _():
        fore_in[...] = jnp.zeros_like(fore_in)

    wires.copy(fore_out, fore_in, (at.d, at.r + 1, at.c), 40, at.r < 3)

    @pl.loop(0, sz.tiles)
    def _(i):
        dy_t[rows_at(128 * i, 128), sz.seq : sz.both] = turned(dob[:, lanes_at(128 * i, 128)]).astype(low)

    res_onward()

    for step in range(4):
        there = (at.c + step) % 4
        rows = rows_at(pair * there, pair)
        go[rows] = times(dy_t[rows, sz.seq : sz.both], a_nat[...]).astype(low)
        wires.copy(
            go.at[rows, lanes_at(sz.mixed * (1 - at.d), sz.mixed)], xo.at[there], at.peer(4), 48 + there
        )
    wires.arrived(fore_in, 40, (at.d, at.r - 1, at.c), at.r > 0)
    window = times(da[...], choose((2 * sz.mixed, main), lambda j: from_natural(j - slack * at.r)))
    da_first = window[:, 0:128] + fore_in[...].astype(jnp.float32)
    da[:, 128:main] = window[:, 128:main].astype(low)
    da[:, 0:128] = da_first.astype(low)
    da[:, main : main + 128] = fore_out[...]

    row_labels = segments.at[:, lanes_at(sz.seq * at.c, sz.seq)]
    col_labels[...] = jnp.concatenate([row_labels[...]] * 8, axis=0).astype(jnp.float32).T[:, 0:1]
    for made in loads[12:17]:
        made.wait()
    half = sz.seq // 2

    def heads_back(p, count):
        tile = lanes_at(128 * p, 128)
        dk_sum[...] = jnp.zeros_like(dk_sum)
        dv_sum[...] = jnp.zeros_like(dv_sum)
        for q in range(2):
            rows = slice(half * q, half * (q + 1))
            keys = half * (q + 1)
            order = lax.broadcasted_iota(jnp.int32, (half, keys), 0) + half * q
            allowed = (col_labels[rows, :] == row_labels[:, 0:keys].astype(jnp.float32)) & (
                order >= lax.broadcasted_iota(jnp.int32, (half, keys), 1)
            )
            lanes = lax.broadcasted_iota(jnp.int32, (half, 128), 1)
            side = lanes // HD
            total = jnp.zeros((half, 128), jnp.float32)
            for h in range(count):
                queries = jnp.where(side == h, qw[rows, tile].astype(jnp.float32) * HD ** (-0.5), 0.0)
                queries = queries.astype(low)
                pulled = jnp.where(side == h, da[rows, tile].astype(jnp.float32), 0.0).astype(low)
                found = jnp.sum(jnp.where(lanes == 2 * p + h, lse[rows, :], 0.0), axis=1, keepdims=True)
                scores = times_flipped(queries, kw[0:keys, tile])
                soft = jnp.where(allowed, jnp.exp(jnp.where(allowed, scores - found, MASKED)), 0.0)
                soft_back = times_flipped(pulled, vw[0:keys, tile])
                inner = jnp.sum(soft_back * soft, axis=1, keepdims=True)
                score_back = (soft * (soft_back - inner)).astype(low)
                piece = times(score_back, kw[0:keys, tile]) * HD ** (-0.5)
                total = jnp.where(side == h, piece, total)
                dk_sum[0:keys] += times_outer(score_back, queries)
                dv_sum[0:keys] += times_outer(soft.astype(low), pulled)
            dqw[rows, tile] = total.astype(low)
        dkw[:, tile] = dk_sum[...].astype(low)
        dvw[:, tile] = dv_sum[...].astype(low)

    @pl.loop(0, main // 128)
    def _(p):
        heads_back(p, 2)

    @pl.when(at.r == 3)
    def _():
        heads_back(main // 128, 1)

    def compact(column):
        part, place = column // HD, column % HD
        return jnp.where(part < 3, 128 * part + place, -1)

    table = choose((384, 256), compact)
    backs = (dqw, dkw, dvw)
    edge_out[...] = picked(jnp.concatenate([b[:, 0:128] for b in backs], axis=1), table)
    wires.copy(edge_out, edge_in, (at.d, at.r - 1, at.c), 41, at.r > 0)

    @pl.when(at.r == 3)
    def _():
        edge_in[...] = picked(jnp.concatenate([b[:, main : main + 128] for b in backs], axis=1), table)

    wires.arrived(edge_in, 41, (at.d, at.r + 1, at.c), at.r < 3)

    def unfold(column):
        tile, lane = column // 128, column % 128
        inside = jnp.where(lane < HD - 16, HD * tile + lane + 16, -1)
        tail = jnp.where(lane < 48, HD * (lane // 16) + lane % 16, -1)
        return jnp.where(tile < 3, inside, tail)

    edges = picked(edge_in[...], choose((256, 512), unfold))
    lane = lax.broadcasted_iota(jnp.int32, (sz.seq, 128), 1)
    pieces = []
    for i, back in enumerate(backs):
        first = jnp.where(lane < slack * at.r, edges[:, 128 * i : 128 * i + 128], back[:, 0:128])
        pieces += [first, back[:, 128:main]]
    pieces.append(edges[:, 384:512])
    wires.close(dob_sent)
    own_back = dob.at[:, 0 : sz.heads]
    own_back[...] = jnp.concatenate(pieces, axis=1)

    order, o_send, o_relay, o_arrived, o_from = collect_col(
        wires, lambda c: xo.at[c], zo, ro, at, 10
    )
    for step in range(4):
        there = order[step]
        wires.arrived(xo.at[there], 48 + there, at.peer(4))
        mine = go[rows_at(pair * there, pair), lanes_at(sz.mixed * at.d, sz.mixed)]
        xo[there] = (mine.astype(jnp.float32) + xo[there].astype(jnp.float32)).astype(low)
        o_send(step)

    def go_home(values, base, out, home, stage):
        for r in range(4):
            stage[r] = values[:, pair * r : pair * (r + 1)].astype(low)
        mine = rows_at(sz.part * at.r, sz.part)
        sent = []
        for r in range(4):
            sent.append(
                wires.copy(stage.at[r], home.at[mine], (at.d, r, at.c), base + at.r, at.r != r)
            )

            @pl.when(at.r == r)
            def _():
                home[mine] = stage[r]

        for r in range(4):
            rows = home.at[sz.part * r : sz.part * (r + 1)]
            wires.arrived(rows, base + r, (at.d, r, at.c), at.r != r)
        sent.append(wires.copy(home, out, (at.d, at.c, at.r), base + 4, at.r != at.c))
        made = load(home, out, at.r == at.c)
        run(at.r == at.c, made.wait)
        return sent

    def relay_out(there):
        load(ro, dqw.at[0:pair, 0 : sz.mixed]).wait()
        both = xo[there].astype(jnp.float32) + dqw[0:pair, 0 : sz.mixed].astype(jnp.float32)
        xo[there] = both.astype(low)

    result = x2[...] + res_total()
    wires.close(res_sent)
    res_home = go_home(result, 56, result_home, home, stage)

    for made in loads[9:10]:
        made.wait()

    def back_in(start, tile):
        out = times_flipped(own_back[...], wh[rows_at(start, tile)])
        dy[0 : sz.seq, lanes_at(start, tile)] = out.astype(low)

    over_tiles(sz.width, back_in)
    one_onward, one_total, _ = scatter_group(
        wires, (2,), dy, lambda d, r: sz.part * r, near_one, mid, far_one, at, 64
    )
    own = rows_at(pair * at.c, pair)

    def bring(c, landing, needed):
        made = load(landing.at[c], h2_t.at[pair * c : pair * (c + 1), 0 : sz.hidden], needed)
        run(needed, made.wait)

        @pl.when(jnp.logical_not(needed))
        def _():
            h2_t[pair * c : pair * (c + 1), 0 : sz.hidden] = jnp.zeros((pair, sz.hidden), low)

    def summed(block, lanes):
        result = block[own, lanes].astype(jnp.float32)
        for c in range(4):
            result = result + h2_t[pair * c : pair * (c + 1), lanes].astype(jnp.float32)
        return result

    half_rows = sz.pieces

    def natural_rows(value):
        flipped = value.T
        return jnp.concatenate(
            [flipped[:, 0:half_rows], flipped[:, block : block + half_rows]], axis=1
        )

    def own_half(row):
        return jnp.where(at.d == 0, row[:, 0:half_rows], row[:, half_rows : 2 * half_rows])

    for c in range(4):
        d_arrived(c)
        bring(c, zd, d_from(c))
    for i in range(sz.hidden // 128):
        rows = min(128, 4 * sz.pieces - 128 * i)
        value = natural_rows(summed(gw, slice(128 * i, 128 * (i + 1))))
        u[128 * i : 128 * i + rows, 0 : sz.share] = value[0:rows]
        if rows < 128:
            vec_out[5:6, 0:half_rows] = own_half(value[rows : rows + 1])
    down_out = load(u.at[0 : 4 * sz.pieces, 0:512], out_down)
    wires.close(gd_sends)
    h1_load.wait()
    order, h_send, h_relay, h_arrived, h_from = collect_col(
        wires, lambda c: xh.at[c], zh, rh, at, 72
    )
    for step in range(4):
        there = order[step]
        rows = rows_at(pair * there, pair)
        gw[rows] = times(dy_t[rows, 0 : sz.seq], own_back[...]).astype(low)
        if step == 0:
            one_onward()
        other = gw.at[rows_at(pair * there + block * (1 - at.d), block)]
        wires.copy(other, xh.at[there], at.peer(4), 80 + there)

    u_relay(relay_of(ru, gu))
    o_relay(relay_out)
    h1_back = one_total()
    through_norm, gain_one, shift_one = norm_back(
        h1_back, x_own[...].astype(jnp.float32), vec_rows[0:1]
    )
    va[0, 0:1] = gain_one
    va[0, 1:2] = shift_one
    for mask in range(1, 8):
        wires.copy(va.at[0], va.at[mask], at.peer(mask), 84 + mask)
    grad = dx2[...] + through_norm
    wires.close(res_home)
    go_home(grad, 92, grad_home, home_two, stage)
    for step in range(4):
        there = order[step]
        wires.arrived(xh.at[there], 80 + there, at.peer(4))
        mine = rows_at(pair * there + block * at.d, block)
        xh[there] = (gw[mine].astype(jnp.float32) + xh[there].astype(jnp.float32)).astype(low)
        h_send(step)

    for c in range(4):
        u_arrived(c)
        bring(c, zu, u_from(c))
    theirs = rows_at(pair * at.c + block * (1 - at.d), block)

    def part_sum(side, lanes):
        rows = rows_at(pair * at.c + block * side, block)
        result = gu[rows, lanes].astype(jnp.float32)
        for c in range(4):
            result = result + h2_t[rows_at(pair * c + block * side, block), lanes].astype(jnp.float32)
        return result

    every = slice(0, sz.hidden)
    gu[theirs] = part_sum(1 - at.d, every).astype(low)
    wires.copy(gu.at[theirs], xu, at.peer(4), 97)
    mine_sum = part_sum(at.d, every)
    down_out.wait()
    wires.arrived(xu, 97, at.peer(4))
    partner_sum = xu[...].astype(jnp.float32)
    for side in range(2):

        @pl.when(at.d == side)
        def _():
            both = (mine_sum, partner_sum) if side == 0 else (partner_sum, mine_sum)
            for j in range(4):
                rows = slice(block * j, block * (j + 1))
                for i in range(2):
                    u[rows, half_rows * i : half_rows * (i + 1)] = both[i][:, half_rows * j : half_rows * (j + 1)]

    bias_sum = mine_sum[half_rows : half_rows + 1]
    for j in range(4):
        vec_out[8 + j : 9 + j, 0:half_rows] = bias_sum[:, half_rows * j : half_rows * (j + 1)]
    up_out = load(u.at[0 : 4 * block, 0:512], out_up)

    for c in range(4):
        o_arrived(c)
        needed = o_from(c)
        made = load(zo.at[c], wd.at[pair * c : pair * (c + 1), 0 : sz.mixed], needed)
        run(needed, made.wait)

        @pl.when(jnp.logical_not(needed))
        def _():
            wd[pair * c : pair * (c + 1), 0 : sz.mixed] = jnp.zeros((pair, sz.mixed), low)

    value = xo[at.c].astype(jnp.float32)
    for c in range(4):
        value = value + wd[pair * c : pair * (c + 1), 0 : sz.mixed].astype(jnp.float32)
    flipped = natural_rows(value)
    vec_out[4:5, 0:half_rows] = own_half(flipped[half_rows : half_rows + 1])
    flipped = flipped[0:block]
    for i in range(4):
        held = (dk_sum, dv_sum)[i // 2].at[block * (i % 2) : block * (i % 2 + 1)]
        lanes = min(128, sz.share - 128 * i)
        held[:, 0:lanes] = flipped[:, 128 * i : 128 * i + lanes]
        stay.append(load(held, out_out.at[:, 128 * i : 128 * (i + 1)]))

    for mask in range(1, 8):
        wires.arrived(va.at[mask], 84 + mask, at.peer(mask))
    vb[at.c] = functools.reduce(lambda a, b: a + b, [va[mask] for mask in range(8)])
    for c in range(4):
        wires.copy(vb.at[at.c], vb.at[at.c], at.along(c), 98 + at.c, at.c != c)

    def relay_heads(there):
        parts = [
            load(rh.at[:, s:e], t.at[0:block, 0 : e - s])
            for t, s, e in ((dqw, 0, 512), (dkw, 512, 1024), (dvw, 1024, sz.heads))
        ]
        for made in parts:
            made.wait()
        for t, s, e in ((dqw, 0, 512), (dkw, 512, 1024), (dvw, 1024, sz.heads)):
            both = xh[there, :, s:e].astype(jnp.float32) + t[0:block, 0 : e - s].astype(jnp.float32)
            xh[there, :, s:e] = both.astype(low)

    h_relay(relay_heads)
    for c in range(4):
        wires.arrived(vb.at[c], 98 + c, at.along(c), at.c != c)
    sums = vb[0] + vb[1] + vb[2] + vb[3]
    picked_sums = jnp.zeros((4, half_rows), jnp.float32)
    for i in range(8):
        cut = sums[0:4, block * i : block * i + half_rows]
        picked_sums = jnp.where(2 * at.c + at.d == i, cut, picked_sums)
    vec_out[0:4, 0:half_rows] = picked_sums
    wires.arrived(result_home, 60, (at.d, at.c, at.r), at.r != at.c)
    wires.arrived(grad_home, 96, (at.d, at.c, at.r), at.r != at.c)
    up_out.wait()
    rest_lanes = sz.heads - sz.hidden
    for c in range(4):
        h_arrived(c)
        needed = h_from(c)
        rows = slice(block * c, block * (c + 1))
        parts = (
            load(zh.at[c, :, 0 : sz.hidden], wd.at[rows], needed),
            load(zh.at[c, :, sz.hidden : sz.heads], wu.at[rows, 0:rest_lanes], needed),
        )
        for made in parts:
            run(needed, made.wait)

        @pl.when(jnp.logical_not(needed))
        def _():
            wd[rows] = jnp.zeros((block, sz.hidden), low)
            wu[rows, 0:rest_lanes] = jnp.zeros((block, rest_lanes), low)

    left = xh[at.c, :, 0 : sz.hidden].astype(jnp.float32)
    right = xh[at.c, :, sz.hidden : sz.heads].astype(jnp.float32)
    for c in range(4):
        rows = slice(block * c, block * (c + 1))
        left = left + wd[rows].astype(jnp.float32)
        right = right + wu[rows, 0:rest_lanes].astype(jnp.float32)
    whole = jnp.concatenate([left, right], axis=1)
    for i in range(3):
        turned_columns = jnp.concatenate(
            [
                whole[:, main * i : main * (i + 1)],
                whole[:, 3 * main + slack * i : 3 * main + slack * (i + 1)],
            ],
            axis=1,
        )
        rows = slice(block * i, block * (i + 1))
        for r in range(4):

            @pl.when(at.r == r)
            def _():
                cut = slack * r
                value = turned_columns
                if cut:
                    value = jnp.concatenate([value[:, cut:], value[:, 0:cut]], axis=1)
                u[rows, 0 : sz.share] = value
                if i != 1:
                    vec_out[6 + i // 2 : 7 + i // 2, 0:half_rows] = own_half(
                        value[half_rows : half_rows + 1]
                    )

    stay.append(load(u.at[0 : 3 * block, 0:512], out_heads))
    for made in stay:
        made.wait()
    wires.close()


def update_kernel(sz, rates, grads, result_in, grad_in, weights, firsts, seconds, outs):
    down, out, up, heads, vectors = grads
    share, pieces, block = sz.share, sz.pieces, sz.block

    def move(i, place, gradient, decay):
        first_new, second_new, weight_new = adam_terms(
            weights[i][place], gradient, firsts[i][place], seconds[i][place], rates[i], decay
        )
        outs[3 * i + 2][place] = first_new
        outs[3 * i + 3][place] = second_new
        outs[3 * i + 4][place] = weight_new

    for part in range(3):
        move(0, part, heads[part, :, 0:share], MATRIX_DECAY)
    move(1, slice(None), out[:, 0:share], MATRIX_DECAY)
    for j in range(4):
        move(2, (slice(None), j), up[j, :, 0:share], MATRIX_DECAY)
    move(3, slice(None), down[:, 0:share], MATRIX_DECAY)

    @pl.when(pl.program_id(0) == 0)
    def _():
        for i, source, row in (
            (4, 0, 0), (4, 1, 1), (5, 4, 0), (5, 2, 1), (5, 3, 2), (5, 5, 3),
            (6, 6, 0), (6, 7, 1), (7, 8, 0), (7, 9, 1), (7, 10, 2), (7, 11, 3),
        ):
            move(i, row, vectors[source : source + 1, 0:pieces], 0.0)

    def plain(rows):
        flipped = rows.astype(jnp.float32).T
        return jnp.concatenate([flipped[0:pieces], flipped[block : block + pieces]], axis=0)

    @pl.when(pl.program_id(0) == 1)
    def _():
        outs[0][...] = plain(result_in[...]).astype(jnp.bfloat16)

    @pl.when(pl.program_id(0) == 2)
    def _():
        outs[1][...] = plain(grad_in[...])


def fused(
    tokens,
    cotangent,
    segments,
    weights,
    firsts,
    seconds,
):
    low = jnp.bfloat16
    seq, share = tokens.shape
    pieces = weights[1].shape[2]
    sz = Sizes(share, pieces, seq)
    block, main = sz.block, sz.main

    def views(arrays):
        heads, out, up, down, *small = arrays
        return (
            jnp.transpose(heads.reshape(pieces, 3, share), (1, 0, 2)),
            out.reshape(pieces, share),
            up.reshape(pieces, 4, share),
            down.reshape(4 * pieces, share),
            *[each.reshape(each.shape[0], 1, pieces) for each in small],
        )

    viewed = views(weights)
    labels = segments.reshape(1, -1)

    def made(*shape, dtype=low):
        return jax.ShapeDtypeStruct(shape, dtype)

    def held(*shape, dtype=low):
        return pltpu.VMEM(shape, dtype)

    w, seq, both, part = sz.width, sz.seq, sz.both, sz.part
    vmem, anywhere = pl.BlockSpec(memory_space=pltpu.VMEM), pl.BlockSpec(memory_space=pl.ANY)
    dma = pltpu.SemaphoreType.DMA
    f32 = jnp.float32
    wide = 3 * 128 + 128
    outs = pl.pallas_call(
        functools.partial(forward_kernel, sz),
        out_shape=(
            made(w, sz.heads),
            made(w, 2 * sz.mixed),
            made(w, sz.hidden),
            made(w, sz.hidden),
            made(w, seq),
            made(w, both),
            made(w, both),
            made(both, w),
            made(both, sz.hidden, dtype=f32),
            made(both, sz.hidden),
            made(seq, main + 128),
            made(seq, main + 128),
            made(seq, main + 128),
            made(seq, 2 * sz.mixed),
            made(seq, 128, dtype=f32),
            made(part, w, dtype=f32),
            made(part, w),
            made(8, w, dtype=f32),
        ),
        in_specs=[anywhere] * 6 + [vmem] * 5,
        out_specs=[anywhere] * 18,
        scratch_shapes=[
            held(w, sz.heads),
            held(w, 2 * sz.mixed),
            held(w, sz.hidden),
            held(w, sz.hidden),
            held(w, seq),
            held(w, both),
            held(w, both),
            held(both, w),
            held(both, sz.hidden, dtype=f32),
            held(both, sz.hidden),
            held(seq, main + 128),
            held(seq, main + 128),
            held(seq, main + 128),
            held(seq, 2 * sz.mixed),
            held(seq, 128, dtype=f32),
            held(part, w, dtype=f32),
            held(part, w),
            held(8, w, dtype=f32),
            held(w, seq),
            held(seq, w),
            held(both, w),
            held(seq, sz.heads),
            held(seq, main + 128),
            held(w, 128),
            held(seq, w),
            held(seq, 256),
            held(seq, 256),
            held(seq, 128),
            held(2, part, w),
            held(1, part, w),
            held(1, part, w),
            held(share, seq),
            held(share, seq),
            held(3, pieces, share, dtype=f32),
            held(pieces, share, dtype=f32),
            held(pieces, 4, share, dtype=f32),
            held(4 * pieces, share, dtype=f32),
            held(sz.pair, seq),
            held(sz.pair, seq),
            held(block, sz.heads),
            held(sz.pair, sz.mixed),
            held(block, 2 * sz.hidden),
            held(sz.pair, sz.hidden),
            held(block, 128),
            held(seq, 1, dtype=f32),
            dma((96,)),
            dma((96,)),
            dma((48,)),
        ],
        compiler_params=pltpu.CompilerParams(
            collective_id=0, has_side_effects=True, vmem_limit_bytes=VMEM_BYTES
        ),
        cost_estimate=pl.CostEstimate(flops=10**10, bytes_accessed=10**8, transcendentals=10**6),
    )(tokens.T, cotangent.T, *viewed, labels)
    (wh, wo, wu, wd, h1_t, h2_t, dy_t, dy, u, gl, qw, kw, vw, a_nat, lse, x2, x_own, vec_rows) = outs
    outs = pl.pallas_call(
        functools.partial(backward_kernel, sz),
        out_shape=(
            made(4 * pieces, 512, dtype=f32),
            made(4 * block, 512, dtype=f32),
            made(block, 512, dtype=f32),
            made(3 * block, 512, dtype=f32),
            made(seq, sz.pair),
            made(seq, sz.pair),
            made(16, 256, dtype=f32),
            made(4, sz.pair, sz.hidden),
            made(4, sz.pair, sz.hidden),
            made(4, sz.pair, sz.mixed),
            made(4, block, sz.heads),
            made(sz.pair, sz.hidden),
            made(sz.pair, sz.hidden),
            made(sz.pair, sz.mixed),
            made(block, sz.heads),
        ),
        in_specs=[anywhere] * 17 + [vmem] * 2,
        out_specs=[anywhere] * 6 + [vmem] + [anywhere] * 8,
        scratch_shapes=[
            held(seq, main + 128),
            held(seq, main + 128),
            held(seq, main + 128),
            held(seq, 2 * sz.mixed),
            held(seq, 128, dtype=f32),
            held(part, w, dtype=f32),
            held(part, w),
            held(block, sz.hidden),
            held(both, w),
            held(w, both),
            held(both, sz.hidden, dtype=f32),
            held(both, sz.hidden),
            held(w, both),
            held(w, sz.hidden),
            held(w, sz.hidden),
            held(w, 2 * sz.mixed),
            held(w, sz.heads),
            held(part, w),
            held(both, sz.hidden),
            held(w, sz.heads),
            held(w, sz.hidden),
            held(w, 2 * sz.mixed),
            held(4, block, sz.heads),
            held(4, sz.pair, sz.mixed),
            held(4, part, w),
            held(3, part, w),
            held(4, part, w),
            held(3, part, w),
            held(2, part, w),
            held(1, part, w),
            held(3, part, w),
            held(seq, w),
            held(seq, 2 * sz.mixed),
            held(seq, main + 128),
            held(seq, main + 128),
            held(seq, main + 128),
            held(seq, 128, dtype=f32),
            held(seq, 128, dtype=f32),
            held(part, w, dtype=f32),
            held(seq, 256),
            held(seq, 256),
            held(seq, 128),
            held(seq, 128),
            held(seq, 1, dtype=f32),
            held(4, part, sz.pair),
            held(seq, sz.pair),
            held(seq, sz.pair),
            held(8, 8, w, dtype=f32),
            held(4, 8, w, dtype=f32),
            dma((112,)),
            dma((104,)),
            dma((64,)),
        ],
        compiler_params=pltpu.CompilerParams(
            collective_id=1, has_side_effects=True, vmem_limit_bytes=VMEM_BYTES
        ),
        cost_estimate=pl.CostEstimate(flops=2 * 10**10, bytes_accessed=10**8, transcendentals=10**6),
    )(
        dy, dy_t, u, gl, h2_t, wd, wu, wo, wh, h1_t,
        qw, kw, vw, a_nat, lse, x2, x_own, vec_rows, labels,
    )
    down, up, out, heads, result_home, grad_home, vectors = outs[:7]
    steps = 5
    chunk = pieces // steps

    def rows_of(shape, axis, size):
        block_shape = list(shape)
        block_shape[axis] = size
        return pl.BlockSpec(tuple(block_shape), lambda i: tuple(i if a == axis else 0 for a in range(len(shape))))

    def whole(shape):
        return pl.BlockSpec(tuple(shape), lambda i: (0,) * len(shape))

    matrix_specs = (
        rows_of((3, pieces, share), 1, chunk),
        rows_of((pieces, share), 0, chunk),
        rows_of((pieces, 4, share), 0, chunk),
        rows_of((4 * pieces, share), 0, 4 * chunk),
        *[whole(each.shape) for each in viewed[4:]],
    )
    grads = (down, out, up.reshape(4, block, 512), heads.reshape(3, block, 512), vectors)
    grad_specs = (
        rows_of((4 * pieces, 512), 0, 4 * chunk),
        rows_of((block, 512), 0, chunk),
        rows_of((4, block, 512), 1, chunk),
        rows_of((3, block, 512), 1, chunk),
        whole((16, 256)),
    )
    rates = (0.05, 0.2, 0.05, 0.025, 0.3, 0.3, 0.3, 0.3)
    arguments = (*grads, result_home, grad_home, *viewed, *views(firsts), *views(seconds))
    out_shape = [made(share, seq), made(share, seq, dtype=f32)]
    out_specs = [whole((share, seq)), whole((share, seq))]
    for each, spec in zip(viewed, matrix_specs, strict=True):
        out_shape += [jax.ShapeDtypeStruct(each.shape, f32)] * 3
        out_specs += [spec] * 3

    def update(*refs):
        ins, outs = refs[:31], refs[31:]
        update_kernel(sz, rates, ins[:5], ins[5], ins[6], ins[7:15], ins[15:23], ins[23:31], outs)

    updated = pl.pallas_call(
        update,
        grid=(steps,),
        out_shape=out_shape,
        in_specs=[*grad_specs, whole((seq, sz.pair)), whole((seq, sz.pair)), *matrix_specs * 3],
        out_specs=out_specs,
        compiler_params=pltpu.CompilerParams(vmem_limit_bytes=VMEM_BYTES),
        cost_estimate=pl.CostEstimate(
            flops=20 * 10**6, bytes_accessed=30 * 10**6, transcendentals=2 * 10**6
        ),
    )(*arguments)
    results = [updated[0].T, updated[1].T]
    for i, weight in enumerate(weights):
        for each in updated[2 + 3 * i : 5 + 3 * i]:
            if i == 0:
                each = jnp.transpose(each, (1, 0, 2))
            results.append(each.reshape(weight.shape))
    return tuple(results)


def normalize(inputs):
    center = jnp.mean(inputs, axis=1, keepdims=True)
    spread = jnp.mean(inputs * inputs, axis=1, keepdims=True) - center * center
    inverse = lax.rsqrt(spread + NORM_EPSILON)
    return ((inputs - center) * inverse, inverse)


def norm_pull(upstream, centered, inverse, gain):
    scaled = upstream * gain
    inner = (
        scaled
        - jnp.mean(scaled, axis=1, keepdims=True)
        - centered * jnp.mean(scaled * centered, axis=1, keepdims=True)
    )
    return inner * inverse


def crossed(blocks, n):
    pairs = [(i * n + j, j * n + i) for i in range(n) for j in range(n)]
    return lax.ppermute(blocks, ("row", "col"), pairs)


def scatter_rows(partial):
    return lax.psum_scatter(
        partial.astype(jnp.bfloat16), "row", scatter_dimension=0, tiled=True
    ).astype(jnp.float32)


def gather_rows(local):
    return lax.all_gather(local, "row", axis=0, tiled=True)


def split_heads(rows):
    return jnp.transpose(rows.reshape(rows.shape[0], -1, HD), (1, 0, 2))


def join_heads(values):
    return jnp.transpose(values, (1, 0, 2)).reshape(values.shape[1], -1)


def scores_of(queries, keys, allowed):
    scores = jnp.einsum(
        "hqe,hke->hqk", queries, keys, preferred_element_type=jnp.float32
    ) * HD ** (-0.5)
    return jnp.where(allowed[None], scores, MASKED)


def gathered(
    tokens,
    cotangent,
    segments,
    w_heads,
    w_out,
    w_up,
    w_down,
    norm_vectors,
    width_vectors,
    attend_bias,
    hidden_vectors,
):
    n_dp, n_row, n_col = (lax.axis_size(name) for name in ("dp", "row", "col"))
    row = lax.axis_index("row")
    low = jnp.bfloat16
    share = tokens.shape[1]
    width = share * n_col
    seq = tokens.shape[0]
    part = seq // n_row
    near = HEADS // n_row
    window = (HEADS - near * (n_row - 1)) * HD
    step = near * HD
    edge = width - (share + step * (n_row - 1)) if n_row > 1 else 0
    edge = window - share
    to_next = [(i, i + 1) for i in range(n_row - 1)]
    to_last = [(i + 1, i) for i in range(n_row - 1)]
    offset = edge - (share - step) * row

    vectors = jnp.concatenate(
        [
            norm_vectors.reshape(2, -1),
            width_vectors.reshape(4, -1),
            attend_bias.reshape(2, -1),
            hidden_vectors.reshape(4, -1),
        ]
    ).astype(low)
    vectors = lax.all_gather(vectors, ("row", "col", "dp"), axis=0, tiled=False)
    vectors = vectors.reshape(n_row, n_col, n_dp, 12, -1).astype(jnp.float32)
    by_col = jnp.transpose(vectors[0], (2, 0, 1, 3)).reshape(12, width)
    by_row = jnp.transpose(vectors[:, 0], (2, 0, 1, 3)).reshape(12, width)
    gain_one, shift_one, bias_out, gain_two, shift_two, bias_down = (by_col[i] for i in range(6))
    zeros = jnp.zeros((1, window), jnp.float32)
    attend_rows = lax.dynamic_slice_in_dim(by_row[6:8], row * step, window, axis=1)
    heads_bias = jnp.concatenate([attend_rows[0:1], zeros, attend_rows[1:2]]).reshape(-1)
    unit_bias = lax.dynamic_slice_in_dim(by_row[8:12], row * share, share, axis=1).reshape(-1)

    own = w_heads.astype(low).reshape(-1, 3, share)
    passed = lax.ppermute(own[:, :, share - edge :], "row", to_next)
    own = jnp.concatenate([passed, own, jnp.zeros_like(passed)], axis=2)
    own = lax.dynamic_slice_in_dim(own, offset, window, axis=2).reshape(-1, 3 * window)
    heads_matrix = lax.all_gather(own, ("col", "dp"), axis=0, tiled=True)
    out_matrix = lax.all_gather(w_out.astype(low).reshape(-1, share), ("col", "dp"), axis=0)
    out_matrix = jnp.transpose(out_matrix.reshape(n_col, share, share), (1, 0, 2))
    out_matrix = out_matrix.reshape(share, width)
    passed = lax.ppermute(out_matrix[share - edge :], "row", to_next)
    out_matrix = jnp.concatenate([passed, out_matrix, jnp.zeros_like(passed)])
    out_matrix = lax.dynamic_slice_in_dim(out_matrix, offset, window)
    owned = (jnp.arange(window) < step) | (row == n_row - 1)
    out_matrix = jnp.where(owned[:, None], out_matrix, jnp.zeros_like(out_matrix))
    up_matrix = lax.all_gather(
        w_up.astype(low).reshape(-1, 4 * share), ("col", "dp"), axis=0, tiled=True
    )
    down_matrix = lax.all_gather(w_down.astype(low).reshape(4, -1, share), ("col", "dp"), axis=0)
    down_matrix = down_matrix.reshape(n_col, n_dp, 4, -1, share)
    down_matrix = jnp.transpose(down_matrix, (2, 1, 3, 0, 4)).reshape(4 * share, width)

    inputs_low = lax.all_gather(crossed(tokens, n_row), "row", axis=1, tiled=True)
    upstream = lax.all_gather(crossed(cotangent, n_row), "row", axis=1, tiled=True)
    inputs = inputs_low.astype(jnp.float32)
    centered_one, inverse_one = normalize(inputs)
    normed_one = (centered_one * gain_one + shift_one).astype(low)
    projected = (times(normed_one, heads_matrix) + heads_bias).astype(low)
    queries, keys, values = (
        split_heads(projected[:, i * window : (i + 1) * window]) for i in range(3)
    )
    labels = lax.dynamic_slice_in_dim(segments, lax.axis_index("col") * seq, seq)
    places = jnp.arange(seq, dtype=jnp.int32)
    allowed = (labels[:, None] == labels[None, :]) & (places[:, None] >= places[None, :])
    scores = scores_of(queries, keys, allowed)
    highest = jnp.max(scores, axis=-1, keepdims=True)
    log_total = highest + jnp.log(jnp.sum(jnp.exp(scores - highest), axis=-1, keepdims=True))
    soft = jnp.exp(scores - log_total).astype(low)
    mixed = jnp.einsum("hqk,hke->hqe", soft, values, preferred_element_type=jnp.float32)
    mixed = join_heads(mixed.astype(low))
    branch = scatter_rows(times(mixed, out_matrix))
    mine = row * part
    middle = lax.dynamic_slice_in_dim(inputs, mine, part) + (branch + bias_out)
    centered_two, inverse_two = normalize(middle)
    normed_two = gather_rows((centered_two * gain_two + shift_two).astype(low))
    hidden = times(normed_two, up_matrix) + unit_bias
    activated, smooth_pull = jax.vjp(smooth, hidden)
    activated = activated.astype(low)
    result = (middle + (scatter_rows(times(activated, down_matrix)) + bias_down)).astype(low)

    down_back = times_flipped(upstream, down_matrix)
    grad_down = times_outer(activated, upstream)
    hidden_back = smooth_pull(down_back)[0].astype(low)
    grad_up = times_outer(normed_two, hidden_back)
    unit_sum = jnp.sum(hidden_back, axis=0, dtype=jnp.float32)
    normed_two_back = scatter_rows(times_flipped(hidden_back, up_matrix))
    upstream_own = lax.dynamic_slice_in_dim(upstream, mine, part).astype(jnp.float32)
    middle_back = upstream_own + norm_pull(normed_two_back, centered_two, inverse_two, gain_two)
    branch_own = middle_back.astype(low)
    branch_back = gather_rows(branch_own)
    mixed_back = times_flipped(branch_back, out_matrix).astype(low)
    grad_out = times_outer(mixed, branch_back)
    mixed_back = split_heads(mixed_back)
    scores_again = scores_of(queries, keys, allowed)
    soft = jnp.exp(scores_again - log_total)
    soft_back = jnp.einsum("hqe,hke->hqk", mixed_back, values, preferred_element_type=jnp.float32)
    row_inner = jnp.sum(soft_back * soft, axis=-1, keepdims=True)
    score_back = (soft * (soft_back - row_inner)).astype(low)
    query_back = jnp.einsum(
        "hqk,hke->hqe", score_back, keys, preferred_element_type=jnp.float32
    ) * HD ** (-0.5)
    key_back = jnp.einsum(
        "hqk,hqe->hke", score_back, queries, preferred_element_type=jnp.float32
    ) * HD ** (-0.5)
    value_back = jnp.einsum(
        "hqk,hqe->hke", soft.astype(low), mixed_back, preferred_element_type=jnp.float32
    )
    heads_back = jnp.concatenate(
        [join_heads(each.astype(low)) for each in (query_back, key_back, value_back)], axis=1
    )
    heads_sum = jnp.sum(heads_back, axis=0, dtype=jnp.float32)
    normed_one_back = scatter_rows(times_flipped(heads_back, heads_matrix))
    grad_heads = times_outer(normed_one, heads_back)
    centered_own = lax.dynamic_slice_in_dim(centered_one, mine, part)
    inverse_own = lax.dynamic_slice_in_dim(inverse_one, mine, part)
    input_back = middle_back + norm_pull(normed_one_back, centered_own, inverse_own, gain_one)

    def homeward(own):
        own = lax.all_to_all(own, "row", split_axis=1, concat_axis=0, tiled=True)
        return crossed(own, n_row)

    result_tokens = homeward(result)
    input_gradient = homeward(input_back.astype(low)).astype(jnp.float32)

    by_token = jnp.stack(
        [
            jnp.sum(normed_one_back * centered_own, axis=0),
            jnp.sum(normed_one_back, axis=0),
            jnp.sum(branch_own.astype(jnp.float32), axis=0),
            jnp.sum(normed_two_back * centered_two, axis=0),
            jnp.sum(normed_two_back, axis=0),
            jnp.sum(upstream_own, axis=0),
        ]
    )
    owned_rows = jnp.where(owned, heads_sum.reshape(3, window)[0::2], 0.0)
    by_unit = jnp.concatenate(
        [
            lax.dynamic_update_slice_in_dim(
                jnp.zeros((2, width), jnp.float32), owned_rows, row * step, axis=1
            ),
            lax.dynamic_update_slice_in_dim(
                jnp.zeros((4, width), jnp.float32), unit_sum.reshape(4, share), row * share, axis=1
            ),
        ]
    )
    sums = lax.psum(jnp.concatenate([by_token, by_unit]), ("dp", "row", "col"))
    pieces = share // n_dp
    inner = lax.axis_index("dp") * pieces
    col_sums = lax.dynamic_slice_in_dim(sums, lax.axis_index("col") * share + inner, pieces, axis=1)
    row_sums = lax.dynamic_slice_in_dim(sums, row * share + inner, pieces, axis=1)

    both = ("col", "dp")

    def to_owner(gradient):
        return lax.psum_scatter(gradient, both, scatter_dimension=0, tiled=True)

    got_heads = to_owner(grad_heads.astype(low)).reshape(pieces, 3, window)
    got_heads = jnp.where(owned, got_heads, jnp.zeros_like(got_heads))
    passed = lax.ppermute(got_heads[:, :, :edge], "row", to_last)
    got_heads = jnp.concatenate([got_heads, jnp.zeros_like(passed)], axis=2)
    got_heads = lax.dynamic_slice_in_dim(got_heads, edge - offset, share, axis=2)
    passed = jnp.concatenate([jnp.zeros((pieces, 3, share), low), passed, jnp.zeros_like(passed)], axis=2)
    got_heads = got_heads + lax.dynamic_slice_in_dim(passed, share - step + edge - offset, share, axis=2)
    low_out = jnp.where(owned[:, None], grad_out, 0.0).astype(low)
    passed = lax.ppermute(low_out[:edge], "row", to_last)
    low_out = jnp.concatenate([low_out, jnp.zeros_like(passed)])
    low_out = lax.dynamic_slice_in_dim(low_out, edge - offset, share)
    passed = jnp.concatenate([jnp.zeros((share, width), low), passed, jnp.zeros_like(passed)])
    low_out = low_out + lax.dynamic_slice_in_dim(passed, share - step + edge - offset, share)
    low_out = jnp.transpose(low_out.reshape(n_dp, pieces, n_col, share), (2, 0, 1, 3))
    got_out = to_owner(low_out.reshape(-1, share))
    got_up = to_owner(grad_up.astype(low))
    low_down = grad_down.astype(low).reshape(4, n_dp, pieces, n_col, share)
    low_down = jnp.transpose(low_down, (3, 1, 0, 2, 4)).reshape(-1, share)
    got_down = to_owner(low_down)

    reduced = [
        each.astype(jnp.float32).reshape(like.shape)
        for each, like in (
            (got_heads, w_heads),
            (got_out, w_out),
            (got_up, w_up),
            (got_down, w_down),
            (col_sums[0:2], norm_vectors),
            (col_sums[2:6], width_vectors),
            (row_sums[6:8], attend_bias),
            (row_sums[8:12], hidden_vectors),
        )
    ]
    return result_tokens, input_gradient, reduced


def per_device(
    tokens,
    cotangent,
    segments,
    w_heads,
    w_out,
    w_up,
    w_down,
    norm_vectors,
    width_vectors,
    attend_bias,
    hidden_vectors,
    drift_heads,
    drift_out,
    drift_up,
    drift_down,
    drift_norm,
    drift_width,
    drift_attend,
    drift_hidden,
    power_heads,
    power_out,
    power_up,
    power_down,
    power_norm,
    power_width,
    power_attend,
    power_hidden,
):
    weights = (
        w_heads,
        w_out,
        w_up,
        w_down,
        norm_vectors,
        width_vectors,
        attend_bias,
        hidden_vectors,
    )
    firsts = (
        drift_heads,
        drift_out,
        drift_up,
        drift_down,
        drift_norm,
        drift_width,
        drift_attend,
        drift_hidden,
    )
    seconds = (
        power_heads,
        power_out,
        power_up,
        power_down,
        power_norm,
        power_width,
        power_attend,
        power_hidden,
    )
    sizes = tuple(lax.axis_size(name) for name in ("dp", "row", "col"))
    if sizes == (2, 4, 4):
        return fused(tokens, cotangent, segments, weights, firsts, seconds)
    result_tokens, input_gradient, reduced = gathered(tokens, cotangent, segments, *weights)
    heads_up = adam_terms(w_heads, reduced[0], drift_heads, power_heads, 0.05, MATRIX_DECAY)
    out_up = adam_terms(w_out, reduced[1], drift_out, power_out, 0.2, MATRIX_DECAY)
    up_up = adam_terms(w_up, reduced[2], drift_up, power_up, 0.05, MATRIX_DECAY)
    down_up = adam_terms(w_down, reduced[3], drift_down, power_down, 0.025, MATRIX_DECAY)
    norm_up = adam_terms(norm_vectors, reduced[4], drift_norm, power_norm, 0.3, 0.0)
    width_up = adam_terms(width_vectors, reduced[5], drift_width, power_width, 0.3, 0.0)
    attend_up = adam_terms(attend_bias, reduced[6], drift_attend, power_attend, 0.3, 0.0)
    hidden_up = adam_terms(hidden_vectors, reduced[7], drift_hidden, power_hidden, 0.3, 0.0)
    return (
        result_tokens,
        input_gradient,
        heads_up[0],
        heads_up[1],
        heads_up[2],
        out_up[0],
        out_up[1],
        out_up[2],
        up_up[0],
        up_up[1],
        up_up[2],
        down_up[0],
        down_up[1],
        down_up[2],
        norm_up[0],
        norm_up[1],
        norm_up[2],
        width_up[0],
        width_up[1],
        width_up[2],
        attend_up[0],
        attend_up[1],
        attend_up[2],
        hidden_up[0],
        hidden_up[1],
        hidden_up[2],
    )


def solution(mesh):
    return jax.shard_map(
        per_device,
        mesh=mesh,
        in_specs=(
            P(("dp", "row"), "col"),
            P(("dp", "row"), "col"),
            P("dp"),
            P("col", "dp", None, None, "row"),
            P("row", "dp", None, "col"),
            P("col", "dp", None, None, "row"),
            P(None, "row", "dp", None, "col"),
            P(None, "col", "dp", None),
            P(None, "col", "dp", None),
            P(None, "row", "dp", None),
            P(None, "row", "dp", None),
            P("col", "dp", None, None, "row"),
            P("row", "dp", None, "col"),
            P("col", "dp", None, None, "row"),
            P(None, "row", "dp", None, "col"),
            P(None, "col", "dp", None),
            P(None, "col", "dp", None),
            P(None, "row", "dp", None),
            P(None, "row", "dp", None),
            P("col", "dp", None, None, "row"),
            P("row", "dp", None, "col"),
            P("col", "dp", None, None, "row"),
            P(None, "row", "dp", None, "col"),
            P(None, "col", "dp", None),
            P(None, "col", "dp", None),
            P(None, "row", "dp", None),
            P(None, "row", "dp", None),
        ),
        out_specs=(
            P(("dp", "row"), "col"),
            P(("dp", "row"), "col"),
            P("col", "dp", None, None, "row"),
            P("col", "dp", None, None, "row"),
            P("col", "dp", None, None, "row"),
            P("row", "dp", None, "col"),
            P("row", "dp", None, "col"),
            P("row", "dp", None, "col"),
            P("col", "dp", None, None, "row"),
            P("col", "dp", None, None, "row"),
            P("col", "dp", None, None, "row"),
            P(None, "row", "dp", None, "col"),
            P(None, "row", "dp", None, "col"),
            P(None, "row", "dp", None, "col"),
            P(None, "col", "dp", None),
            P(None, "col", "dp", None),
            P(None, "col", "dp", None),
            P(None, "col", "dp", None),
            P(None, "col", "dp", None),
            P(None, "col", "dp", None),
            P(None, "row", "dp", None),
            P(None, "row", "dp", None),
            P(None, "row", "dp", None),
            P(None, "row", "dp", None),
            P(None, "row", "dp", None),
            P(None, "row", "dp", None),
        ),
        check_vma=False,
    )
```

```python
import functools

import jax
import jax.numpy as jnp
from jax import lax
from jax.experimental import pallas as pl
from jax.experimental.pallas import tpu as pltpu
from jax.sharding import PartitionSpec as P

HEADS = 25
HD = 64
TOK_DEV = 128
STEP = 10


NORM_EPSILON = 1e-05
BETA_FIRST = 0.9
BETA_SECOND = 0.999
ADAM_EPSILON = 1e-08
MATRIX_DECAY = 0.1
MASKED = -1e30
ROOT = (2.0 / 3.141592653589793) ** 0.5
CUBIC = 0.044715
VMEM_BYTES = 66 * 1024 * 1024


def adam_terms(weight, gradient, first, second, rate, decay):
    first_new = BETA_FIRST * first + (1.0 - BETA_FIRST) * gradient
    second_new = BETA_SECOND * second + (1.0 - BETA_SECOND) * gradient * gradient
    corrected = first_new / (1.0 - BETA_FIRST**STEP)
    divisor = jnp.sqrt(second_new / (1.0 - BETA_SECOND**STEP)) + ADAM_EPSILON
    return (first_new, second_new, weight - rate * (corrected / divisor + decay * weight))


def smooth(values):
    return jax.nn.gelu(values, approximate=True)


def ceil_to(count, unit):
    return -(-count // unit) * unit


class Sizes:
    def __init__(self, share, pieces, seq):
        self.share = share
        self.pieces = pieces
        self.block = ceil_to(pieces, 16)
        self.pair = 2 * self.block
        self.width = 4 * self.pair
        self.seq = seq
        self.part = seq // 4
        self.both = 2 * seq
        self.main = (HEADS // 4) * HD
        self.slack = share - self.main
        self.heads = ceil_to(3 * share, 256)
        self.mixed = ceil_to(pieces + 1, 128)
        self.hidden = ceil_to(4 * pieces + 1, 128)
        self.tiles = self.width // 128


class Place:
    def __init__(self):
        self.d, self.r, self.c = (lax.axis_index(name) for name in ("dp", "row", "col"))
        self.y, self.k = self.r // 2, self.r % 2

    def plane(self, mask):
        d = 1 - self.d if mask & 4 else self.d
        y = 1 - self.y if mask & 2 else self.y
        k = 1 - self.k if mask & 1 else self.k
        return d, 2 * y + k

    def peer(self, mask):
        d, r = self.plane(mask)
        return (d, r, self.c)

    def along(self, c):
        return (self.d, self.r, c)


def run(when, action):
    if when is None:
        action()
    else:
        pl.when(when)(action)


class Wires:
    def __init__(self, sends, arrivals):
        self.sends, self.arrivals = sends, arrivals
        self.used = 0
        self.open = []

    def make(self, source, target, index, slot, device):
        return pltpu.make_async_remote_copy(
            src_ref=source,
            dst_ref=target,
            send_sem=self.sends.at[index],
            recv_sem=self.arrivals.at[slot],
            device_id=device,
            device_id_type=pl.DeviceIdType.MESH,
        )

    def copy(self, source, target, device, slot, when=None):
        made = self.make(source, target, self.used, slot, device)
        self.used += 1
        run(when, made.start)
        item = (when, made)
        self.open.append(item)
        return item

    def arrived(self, target, slot, device, when=None):
        run(when, self.make(target, target, 0, slot, device).wait_recv)

    def close(self, some=None):
        for item in self.open if some is None else some:
            run(item[0], item[1].wait_send)
        self.open = [] if some is None else [o for o in self.open if all(o is not s for s in some)]


def greet(at, diagonal):
    barrier = pltpu.get_barrier_semaphore()

    def signal(device):
        pl.semaphore_signal(
            barrier, inc=1, device_id=device, device_id_type=pl.DeviceIdType.MESH
        )

    for mask in range(1, 8):
        signal(at.peer(mask))
    for c in range(4):
        run(at.c != c, functools.partial(signal, (at.d, at.r, c)))
        if diagonal:
            run(at.c != c, functools.partial(signal, (1 - at.d, at.r, c)))
    run(at.r != at.c, functools.partial(signal, (at.d, at.c, at.r)))
    pl.semaphore_wait(barrier, (13 if diagonal else 10) + jnp.where(at.r != at.c, 1, 0))


def rows_at(start, size):
    return pl.ds(pl.multiple_of(start, 16), size)


def lanes_at(start, size):
    return pl.ds(pl.multiple_of(start, 128), size)


def choose(shape, source):
    rows = lax.broadcasted_iota(jnp.int32, shape, 0)
    wanted = source(lax.broadcasted_iota(jnp.int32, shape, 1))
    return (rows == wanted).astype(jnp.bfloat16)


def edge_source(column):
    part, place = column // HD, column % HD
    wanted = jnp.where(place >= 16, 128 * part + place - 16, 384 + 16 * part + place)
    return jnp.where(part < 3, wanted, -1)


def spread_source(column):
    part, place = column // 128, column % 128
    return jnp.where(place < HD, HD * part + place, -1)


def picked(values, table):
    return jnp.dot(values, table, preferred_element_type=jnp.float32).astype(jnp.bfloat16)


def times(left, right):
    return jnp.dot(left, right, preferred_element_type=jnp.float32)


def times_flipped(left, right):
    return lax.dot_general(
        left, right, (((1,), (1,)), ((), ())), preferred_element_type=jnp.float32
    )


def times_outer(left, right):
    return lax.dot_general(
        left, right, (((0,), (0,)), ((), ())), preferred_element_type=jnp.float32
    )


def over_tiles(total, action, tile=256):
    @pl.loop(0, total // tile)
    def _(i):
        action(i * tile, tile)

    if total % tile:
        action(total - total % tile, total % tile)


def turned(values):
    return values.astype(jnp.float32).T


def gather_group(wires, masks, region, at, base):
    own = region(*at.plane(0))
    sent = [wires.copy(own, own, at.peer(mask), base + mask) for mask in (1, *masks)]

    def finish():
        for mask in masks:
            there = region(*at.plane(mask))
            wires.arrived(there, base + mask, at.peer(mask))
            sent.append(wires.copy(there, there, at.peer(1), base + mask + 1))
        for mask in (0, *masks):
            there = region(*at.plane(mask | 1))
            wires.arrived(there, base + (mask | 1), at.peer(1))

    return finish, sent


def cross_over(wires, keep, home, landing, region, at, base):
    rows = home.shape[0] // 2
    wires.copy(home.at[rows_at(rows * (1 - at.y), rows)], landing, at.peer(2), base)
    target = region(at.c, at.d, at.y)

    def along(source, s):
        wires.copy(source, target, at.along(s), base + 1 + at.c, s != at.c)
        keep(source, target, s == at.c)

    along(home.at[rows_at(rows * at.y, rows)], at.r)

    def onward():
        wires.arrived(landing, base, at.peer(2))
        along(landing, 2 * (1 - at.y) + at.k)

    def finish():
        for c in range(4):
            needed = (at.k == at.c % 2) & (at.c != c)
            wires.arrived(region(c, at.d, at.y), base + 1 + c, at.along(c), needed)

    return onward, finish


def share_pieces(wires, masks, region, at, base):
    holds = at.k == at.c % 2
    near = base + 4 * len(masks)

    def place(mask):
        d, r = at.plane(mask)
        return d, r // 2

    for c in range(4):
        own = region(c, *place(0))
        for i, mask in enumerate(masks):
            wires.copy(own, own, at.peer(mask), base + 4 * i + c, holds)
    for c in range(4):
        own = region(c, *place(0))
        wires.copy(own, own, at.peer(1), near + c, holds)

    def finish():
        for i, mask in enumerate(masks):
            for c in range(4):
                there = region(c, *place(mask))
                wires.arrived(there, base + 4 * i + c, at.peer(mask), holds)
                wires.copy(there, there, at.peer(1), near + 4 * (i + 1) + c, holds)
        for i, mask in enumerate((0, *masks)):
            for c in range(4):
                there = region(c, *place(mask))
                wires.arrived(there, near + 4 * i + c, at.peer(1), jnp.logical_not(holds))

    return finish


def scatter_group(wires, masks, partial, chunk, near, mid, far, at, base):
    sent = []
    for i, mask in enumerate((0, *masks)):
        rows = rows_at(chunk(*at.plane(mask | 1)), near.shape[1])
        sent.append(wires.copy(partial.at[rows], near.at[i], at.peer(1), base + i))

    def rows_of(mask):
        return rows_at(chunk(*at.plane(mask)), near.shape[1])

    def onward():
        for i, mask in enumerate((0, *masks)):
            wires.arrived(near.at[i], base + i, at.peer(1))
        for i, mask in enumerate(masks):
            both = partial[rows_of(mask)].astype(jnp.float32) + near[i + 1].astype(jnp.float32)
            mid[i] = both.astype(jnp.bfloat16)
            sent.append(wires.copy(mid.at[i], far.at[i], at.peer(mask), base + 4 + i))

    def total():
        for i, mask in enumerate(masks):
            wires.arrived(far.at[i], base + 4 + i, at.peer(mask))
        result = partial[rows_of(0)].astype(jnp.float32) + near[0].astype(jnp.float32)
        for i in range(len(masks)):
            result = result + far[i].astype(jnp.float32)
        return result

    return onward, total, sent


def spread_col(wires, region, at, base, source=None):
    own = region(at.c)
    source = own if source is None else source
    for delta in (2, -2, 1, -1):
        there = at.c + delta
        wires.copy(source, own, at.along(there), base + at.c, (there >= 0) & (there < 4))

    def relay():
        for here, start, end in ((2, 0, 3), (1, 3, 0)):
            block = region(start)
            wires.arrived(block, base + start, at.along(start), at.c == here)
            wires.copy(block, block, at.along(end), base + start, at.c == here)

    def finish():
        for c in range(4):
            needed = at.c != c
            if c == 0:
                needed = needed & (at.c != 2)
            if c == 3:
                needed = needed & (at.c != 1)
            wires.arrived(region(c), base + c, at.along(c), needed)

    return relay, finish


def collect_col(wires, piece, landing, rest, at, base):
    low_end, high_end = at.c == 0, at.c == 3
    ends = low_end | high_end
    via = jnp.where(low_end, 1, 2)

    def pick(*choices):
        return jnp.where(
            low_end,
            choices[0],
            jnp.where(at.c == 1, choices[1], jnp.where(high_end, choices[3], choices[2])),
        )

    order = (pick(3, 0, 3, 0), pick(2, 2, 1, 1), pick(1, 3, 0, 2), at.c)
    target = landing.at[at.c]

    def send(step):
        there = order[step]
        block = piece(there)
        if step == 0:
            wires.copy(block, rest, at.along(via), base + 4, ends)
            wires.copy(block, target, at.along(there), base + at.c, jnp.logical_not(ends))
        elif step == 1:
            wires.copy(block, target, at.along(there), base + at.c)
        elif step == 2:
            wires.copy(block, target, at.along(there), base + at.c, ends)

    def relay(add):
        @pl.when(jnp.logical_not(ends))
        def _():
            wires.make(rest, rest, 0, base + 4, at.along(0)).wait_recv()
            add(order[2])

        wires.copy(piece(order[2]), target, at.along(order[2]), base + at.c, jnp.logical_not(ends))

    def arrived(c):
        wires.arrived(landing.at[c], base + c, at.along(c), sent_from(c))

    def sent_from(c):
        here = at.c != c
        if c in (0, 3):
            here = here & (at.c != 3 - c)
        return here

    return order, send, relay, arrived, sent_from


def forward_kernel(
    sz,
    x_home_in,
    dy_home_in,
    w_heads,
    w_out,
    w_up,
    w_down,
    norm_vectors,
    width_vectors,
    attend_bias,
    hidden_vectors,
    segments,
    wh_out,
    wo_out,
    wu_out,
    wd_out,
    h1_t_out,
    h2_t_out,
    dy_t_out,
    dy_out,
    u_out,
    gl_out,
    qw_out,
    kw_out,
    vw_out,
    a_nat_out,
    lse_out,
    x2_out,
    x_own_out,
    vec_rows_out,
    wh,
    wo,
    wu,
    wd,
    h1_t,
    h2_t,
    dy_t,
    dy,
    u,
    gl,
    qw,
    kw,
    vw,
    a_nat,
    lse,
    x2,
    x_own,
    vec_rows,
    x_t,
    h1,
    h2,
    own_qkv,
    aw,
    vec,
    part,
    edge_out,
    edge_in,
    edge_back,
    near,
    mid,
    far,
    x_raw,
    dy_raw,
    heads_raw,
    out_raw,
    up_raw,
    down_raw,
    x_home,
    dy_home,
    wh_own,
    wo_own,
    wu_own,
    wd_own,
    vec_own,
    col_labels,
    x_half,
    dy_half,
    sends,
    arrivals,
    locals_,
):
    at = Place()
    wires = Wires(sends, arrivals)
    low = jnp.bfloat16
    pair, block, pieces = sz.pair, sz.block, sz.pieces
    fetched = []
    for i, (source, target) in enumerate(
        (
            (x_home_in, x_raw),
            (w_heads, heads_raw),
            (w_up, up_raw),
            (w_out, out_raw),
            (w_down, down_raw),
            (dy_home_in, dy_raw),
        )
    ):
        fetched.append(pltpu.make_async_copy(source, target, locals_.at[40 + i]))
        fetched[i].start()
    row_labels = segments.at[:, lanes_at(sz.seq * at.c, sz.seq)]

    def halves(value, target):
        value = value.astype(jnp.float32)
        gap = jnp.zeros((block - pieces, value.shape[1]), jnp.float32)
        parts = [value[0:pieces], gap, value[pieces : 2 * pieces], gap]
        target[...] = jnp.concatenate(parts, axis=0).astype(low)

    def quarter(row):
        return row.astype(low).astype(jnp.float32) * 0.25

    def placed(row):
        both = jnp.concatenate([row, row], axis=1)
        half_of = lax.broadcasted_iota(jnp.int32, both.shape, 1) // pieces
        return jnp.where(half_of == at.d, both, 0.0)

    def with_row(value, row):
        gap = jnp.zeros((block - pieces - 1, value.shape[1]), jnp.float32)
        return jnp.concatenate([value, row, gap], axis=0)

    flat = jnp.concatenate(
        [norm_vectors[0], norm_vectors[1], width_vectors[1], width_vectors[2]], axis=0
    )
    flat = jnp.concatenate([flat, jnp.zeros((124, pieces), jnp.float32)], axis=0)
    flat = jnp.concatenate([flat, jnp.zeros((128, 256 - pieces), jnp.float32)], axis=1)
    where_row = lax.broadcasted_iota(jnp.int32, flat.shape, 0)
    where_lane = lax.broadcasted_iota(jnp.int32, flat.shape, 1)
    carrier = (where_lane == pieces) & ((where_row == 1) | (where_row == 3))
    vec_own[...] = jnp.where(carrier, 1.0, flat).T[0:block].astype(low)
    fetched[0].wait()
    halves(x_raw[...], x_home)
    greet(at, False)

    def x_piece(c, d, y):
        return x_t.at[rows_at(pair * c + block * y, block)]

    def dy_piece(c, d, y):
        return dy_t.at[rows_at(pair * c + block * y, block), lanes_at(sz.seq * d, sz.seq)]

    stay, used = [], [0]

    def keep(source, target, when=None):
        made = pltpu.make_async_copy(source, target, locals_.at[used[0]])
        used[0] += 1
        run(when, made.start)
        stay.append((when, made))

    def flush(source, target):
        made = pltpu.make_async_copy(source, target, locals_.at[used[0]])
        used[0] += 1
        made.start()
        flushed.append(made)

    flushed = []

    def vec_block(d, c):
        return vec.at[rows_at(pair * c + block * d, block)]

    def wh_block(d):
        return lambda c: wh.at[rows_at(pair * c + block * d, block)]

    def wo_block(d):
        return lambda c: wo.at[rows_at(pair * c, pair), lanes_at(sz.mixed * d, sz.mixed)]

    def wu_block(d):
        return lambda c: wu.at[rows_at(pair * c + block * d, block)]

    def wd_block(half):
        return lambda c: wd.at[rows_at(pair * c + block * half, block)]

    x_onward, x_crossed = cross_over(wires, keep, x_home, x_half, x_piece, at, 96)
    for c in range(4):
        wires.copy(vec_own, vec_block(at.d, at.c), at.along(c), 2 + at.c, at.c != c)
    wires.copy(vec_own, vec_block(at.d, at.c), at.peer(4), 6 + at.c)
    keep(vec_own, vec_block(at.d, at.c))

    fetched[1].wait()
    for r in range(4):

        @pl.when(at.r == r)
        def _():
            cut = sz.share - sz.slack * r
            tails = []
            for i in range(3):
                value = heads_raw[i]
                row = jnp.zeros((1, sz.share), jnp.float32)
                if i != 1:
                    row = placed(quarter(attend_bias[i // 2]))
                value = with_row(value, row)
                if r:
                    value = jnp.concatenate([value[:, cut:], value[:, 0:cut]], axis=1)
                wh_own[:, sz.main * i : sz.main * (i + 1)] = value[:, 0 : sz.main].astype(low)
                tails.append(value[:, sz.main :])
            tails.append(jnp.zeros((block, sz.heads - 3 * sz.share), jnp.float32))
            wh_own[:, 3 * sz.main :] = jnp.concatenate(tails, axis=1).astype(low)

    x_onward()
    wh_relay, wh_done = spread_col(wires, wh_block(at.d), at, 20, wh_own)
    wires.copy(wh_own, wh_block(at.d)(at.c), at.peer(4), 24 + at.c)
    keep(wh_own, wh_block(at.d)(at.c))

    fetched[2].wait()
    gap = jnp.zeros((block, sz.hidden - 4 * pieces), jnp.float32)
    values = [
        with_row(up_raw[:, j, :], placed(quarter(hidden_vectors[j]))) for j in range(4)
    ]
    for i in range(2):
        lanes = slice(pieces * i, pieces * (i + 1))
        whole = jnp.concatenate([value[:, lanes] for value in values] + [gap], axis=1)
        wu_own[:, sz.hidden * i : sz.hidden * (i + 1)] = whole.astype(low)
    wires.copy(
        wu_own.at[:, lanes_at(sz.hidden * (1 - at.d), sz.hidden)],
        wu_block(at.d)(at.c),
        at.peer(4),
        10,
    )
    keep(wu_own.at[:, lanes_at(sz.hidden * at.d, sz.hidden)], wu_block(at.d)(at.c))

    def turned_halves(value, target, lanes):
        flipped = value.T
        gap = jnp.zeros((block - pieces, flipped.shape[1]), jnp.float32)
        parts = [flipped[0:pieces], gap, flipped[pieces : 2 * pieces], gap]
        target[:, lanes] = jnp.concatenate(parts, axis=0).astype(low)

    fetched[3].wait()
    value = with_row(out_raw[...], placed(quarter(width_vectors[0])))
    value = jnp.concatenate([value, jnp.zeros((sz.mixed - block, sz.share), jnp.float32)], axis=0)
    for i in range(sz.mixed // 128):
        lanes = slice(128 * i, 128 * (i + 1))
        turned_halves(value[lanes], wo_own, lanes)
    wo_relay, wo_done = spread_col(wires, wo_block(at.d), at, 28, wo_own)
    wires.copy(wo_own, wo_block(at.d)(at.c), at.peer(4), 32 + at.c)
    keep(wo_own, wo_block(at.d)(at.c))
    wu_first, wu_first_done = spread_col(
        wires, wu_block(at.d), at, 36, wu_own.at[:, lanes_at(sz.hidden * at.d, sz.hidden)]
    )

    for when, made in stay:
        run(when, made.wait)
    x_crossed()
    x_done = share_pieces(wires, (2,), x_piece, at, 104)

    fetched[4].wait()
    for i in range(sz.hidden // 128):
        rows = slice(128 * i, 128 * (i + 1))
        if 128 * (i + 1) <= 4 * pieces:
            value = down_raw[rows]
        else:
            value = jnp.concatenate(
                [
                    down_raw[128 * i : 4 * pieces],
                    placed(quarter(width_vectors[3])),
                    jnp.zeros((sz.hidden - 4 * pieces - 1, sz.share), jnp.float32),
                ],
                axis=0,
            )
        turned_halves(value, wd_own, rows)
    del stay[:]
    keep(wd_own, wd.at[rows_at(pair * at.c, pair)])
    fetched[5].wait()
    halves(dy_raw[...], dy_home)
    col_labels[...] = jnp.concatenate([row_labels[...]] * 8, axis=0).astype(jnp.float32).T[:, 0:1]
    x_done()

    for c in range(4):
        wires.arrived(vec_block(at.d, c), 2 + c, at.along(c), at.c != c)
    wires.arrived(vec_block(1 - at.d, at.c), 6 + at.c, at.peer(4))
    for step in range(1, 4):
        there = (at.c + step) % 4
        wires.copy(
            vec_block(at.d, there), vec_block(at.d, there), at.peer(4), 6 + there
        )
    for step in range(1, 4):
        there = (at.c + step) % 4
        wires.arrived(vec_block(1 - at.d, there), 6 + there, at.peer(4))
    features = 4.0 * sz.share

    def add_up(i, carry):
        rows = rows_at(128 * i, 128)
        value = x_t[rows].astype(jnp.float32)
        return (
            carry[0] + jnp.sum(value, axis=0, keepdims=True),
            carry[1] + jnp.sum(value * value, axis=0, keepdims=True),
        )

    zero = jnp.zeros((1, sz.seq), jnp.float32)
    sums = lax.fori_loop(0, sz.tiles, add_up, (zero, zero))
    center = sums[0] / features
    inverse = lax.rsqrt(sums[1] / features - center * center + NORM_EPSILON)

    @pl.loop(0, sz.tiles)
    def _(i):
        rows, lanes = rows_at(128 * i, 128), lanes_at(128 * i, 128)
        vectors = vec[rows].astype(jnp.float32)
        value = (x_t[rows].astype(jnp.float32) - center) * inverse
        value = value * vectors[:, 0:1] + vectors[:, 1:2]
        h1_t[rows] = value.astype(low)
        h1[:, lanes] = value.T.astype(low)
        mine = x_t[rows, lanes_at(sz.part * at.r, sz.part)]
        x_own[:, lanes] = turned(mine).astype(low)
        vec_rows[:, lanes] = vectors.T[0:8]

    flush(h1_t, h1_t_out)
    flush(x_own, x_own_out)
    flush(vec_rows, vec_rows_out)

    wh_relay()
    for c in range(4):
        needed = at.c != c
        if c == 0:
            needed = needed & (at.c != 2)
        if c == 3:
            needed = needed & (at.c != 1)
        wires.arrived(wh_block(at.d)(c), 20 + c, at.along(c), needed)
        wires.copy(wh_block(at.d)(c), wh_block(at.d)(c), at.peer(4), 24 + c, at.c != c)

    wires.arrived(wu_block(1 - at.d)(at.c), 10, at.peer(4))
    wu_second, wu_second_done = spread_col(wires, wu_block(1 - at.d), at, 40)
    for c in range(4):
        wires.arrived(wh_block(1 - at.d)(c), 24 + c, at.peer(4))
    flush(wh, wh_out)

    @pl.loop(0, sz.heads // 256)
    def _(i):
        lanes = lanes_at(256 * i, 256)
        own_qkv[:, lanes] = times(h1[...], wh[:, lanes]).astype(low)

    for when, made in stay:
        run(when, made.wait)
    del stay[:]
    dy_onward, dy_crossed = cross_over(wires, keep, dy_home, dy_half, dy_piece, at, 116)
    wd_first, wd_first_done = spread_col(wires, wd_block(0), at, 44)
    wd_second, wd_second_done = spread_col(wires, wd_block(1), at, 48)

    starts = (0, sz.main, 2 * sz.main, 3 * sz.main)
    ends = jnp.concatenate([own_qkv[:, s : s + 128] for s in starts], axis=1)
    edge_out[...] = picked(ends, choose((512, 256), edge_source))
    last = at.r == 3

    @pl.when(at.r == 0)
    def _():
        edge_in[...] = jnp.zeros_like(edge_in)

    wires.copy(edge_out, edge_in, (at.d, at.r + 1, at.c), 52, at.r < 3)
    spread = choose((256, 384), spread_source)
    extra = picked(edge_out[...], spread)
    wires.arrived(edge_in, 52, (at.d, at.r - 1, at.c), at.r > 0)
    first = picked(edge_in[...], spread)
    lane = lax.broadcasted_iota(jnp.int32, (sz.seq, 128), 1)
    for i, target in enumerate((qw, kw, vw)):
        start = starts[i]
        target[:, 0:128] = jnp.where(
            lane < sz.slack * at.r,
            first[:, 128 * i : 128 * i + 128],
            own_qkv[:, start : start + 128],
        )
        target[:, 128 : sz.main] = own_qkv[:, start + 128 : start + sz.main]
        target[:, sz.main : sz.main + 128] = extra[:, 128 * i : 128 * i + 128]
    flush(qw, qw_out)
    flush(kw, kw_out)
    flush(vw, vw_out)

    dy_onward()
    wo_relay()
    for c in range(4):
        needed = at.c != c
        if c == 0:
            needed = needed & (at.c != 2)
        if c == 3:
            needed = needed & (at.c != 1)
        wires.arrived(wo_block(at.d)(c), 28 + c, at.along(c), needed)
        wires.copy(wo_block(at.d)(c), wo_block(at.d)(c), at.peer(4), 32 + c, at.c != c)

    half = sz.seq // 2

    def heads_of(p, count):
        tile = lanes_at(128 * p, 128)
        for q in range(2):
            rows = slice(half * q, half * (q + 1))
            keys = half * (q + 1)
            order = lax.broadcasted_iota(jnp.int32, (half, keys), 0) + half * q
            allowed = (col_labels[rows, :] == row_labels[:, 0:keys].astype(jnp.float32)) & (
                order >= lax.broadcasted_iota(jnp.int32, (half, keys), 1)
            )
            lanes = lax.broadcasted_iota(jnp.int32, (half, 128), 1)
            side = lanes // HD
            total = jnp.zeros((half, 128), jnp.float32)
            for h in range(count):
                queries = jnp.where(side == h, qw[rows, tile].astype(jnp.float32) * HD ** (-0.5), 0.0)
                scores = times_flipped(queries.astype(low), kw[0:keys, tile])
                scores = jnp.where(allowed, scores, MASKED)
                highest = jnp.max(scores, axis=1, keepdims=True)
                raised = jnp.exp(scores - highest)
                summed = jnp.sum(raised, axis=1, keepdims=True)
                found = highest + jnp.log(summed)
                lse[rows, :] = jnp.where(lanes == 2 * p + h, found, lse[rows, :])
                soft = (raised * (1.0 / summed)).astype(low)
                total = jnp.where(side == h, times(soft, vw[0:keys, tile]), total)
            aw[rows, tile] = total.astype(low)

    lse[...] = jnp.zeros_like(lse)

    @pl.loop(0, sz.main // 128)
    def _(p):
        heads_of(p, 2)

    @pl.when(last)
    def _():
        heads_of(sz.main // 128, 1)
        edge_back[...] = aw[:, sz.main : sz.main + 128]

    flush(lse, lse_out)

    wires.copy(aw.at[:, 0:128], edge_back, (at.d, at.r - 1, at.c), 53, at.r > 0)
    for when, made in stay:
        run(when, made.wait)
    dy_crossed()
    dy_done = share_pieces(wires, (2, 4, 6), dy_piece, at, 124)
    wu_first()
    wires.arrived(edge_back, 53, (at.d, at.r + 1, at.c), at.r < 3)

    def natural(column):
        inner = column % sz.mixed
        place = sz.pieces * (column // sz.mixed) + inner + sz.slack * at.r
        return jnp.where(inner < sz.pieces, place, -1)

    def natural_main(column):
        place = natural(column)
        return jnp.where(place < sz.main, place, -1)

    def natural_edge(column):
        return natural(column) - sz.main

    mixed = times(aw[:, 0 : sz.main], choose((sz.main, 2 * sz.mixed), natural_main))
    mixed = mixed + times(edge_back[...], choose((128, 2 * sz.mixed), natural_edge))
    ones = lax.broadcasted_iota(jnp.int32, mixed.shape, 1) % sz.mixed == sz.pieces
    a_nat[...] = jnp.where(ones, 1.0, mixed).astype(low)
    for c in range(4):
        wires.arrived(wo_block(1 - at.d)(c), 32 + c, at.peer(4))
    flush(wo, wo_out)
    flush(a_nat, a_nat_out)

    def project(start, tile):
        out = times_flipped(a_nat[...], wo[rows_at(start, tile)])
        part[:, lanes_at(start, tile)] = out.astype(low)

    over_tiles(sz.width, project)

    onward, total, _ = scatter_group(
        wires, (2,), part, lambda d, r: sz.part * r, near, mid, far, at, 64
    )
    onward()
    middle = x_own[...].astype(jnp.float32) + total()
    x2[...] = middle
    flush(x2, x2_out)
    center = jnp.sum(middle, axis=1, keepdims=True) / features
    spread_two = jnp.sum(middle * middle, axis=1, keepdims=True) / features - center * center
    normed = (middle - center) * lax.rsqrt(spread_two + NORM_EPSILON)
    own_rows = rows_at(sz.part * (4 * at.d + at.r), sz.part)
    h2[own_rows] = (normed * vec_rows[2:3] + vec_rows[3:4]).astype(low)
    h2_done, _ = gather_group(
        wires, (2, 4, 6), lambda d, r: h2.at[rows_at(sz.part * (4 * d + r), sz.part)], at, 72
    )
    wu_second()
    dy_done()
    flush(dy_t, dy_t_out)
    wd_first()

    @pl.loop(0, sz.tiles)
    def _(i):
        dy[:, lanes_at(128 * i, 128)] = turned(dy_t[rows_at(128 * i, 128)]).astype(low)

    flush(dy, dy_out)
    h2_done()
    wu_first_done()
    wu_second_done()
    flush(wu, wu_out)

    def expand(start, tile):
        lanes = lanes_at(start, tile)
        value = times(h2[...], wu[:, lanes])
        u[:, lanes] = value
        inner = jnp.tanh(ROOT * (value + CUBIC * value * value * value))
        value = 0.5 * value * (1.0 + inner)
        column = lax.broadcasted_iota(jnp.int32, value.shape, 1) + start
        gl[:, lanes] = jnp.where(column == 4 * sz.pieces, 1.0, value).astype(low)

    over_tiles(sz.hidden, expand)

    flush(u, u_out)
    flush(gl, gl_out)
    wd_second()

    @pl.loop(0, sz.tiles)
    def _(i):
        h2_t[rows_at(128 * i, 128)] = turned(h2[:, lanes_at(128 * i, 128)]).astype(low)

    flush(h2_t, h2_t_out)
    wd_first_done()
    wd_second_done()
    flush(wd, wd_out)
    wires.close()
    for made in flushed:
        made.wait()


def backward_kernel(
    sz,
    dy_all,
    dy_t_all,
    u_all,
    gl_all,
    h2_t_all,
    wd_all,
    wu_all,
    wo_all,
    wh_all,
    h1_t_all,
    qw_all,
    kw_all,
    vw_all,
    a_nat_all,
    lse_all,
    x2_all,
    x_own_all,
    vec_rows,
    segments,
    out_down,
    out_up,
    out_out,
    out_heads,
    result_home,
    grad_home,
    vec_out,
    zd,
    zu,
    zo,
    zh,
    rd,
    ru,
    ro,
    rh,
    res_all,
    res_two,
    grad_all,
    grad_two,
    qw,
    kw,
    vw,
    a_nat,
    lse,
    x2,
    x_own,
    xu,
    dy,
    dy_t,
    u,
    gl,
    h2_t,
    wd,
    wu,
    wo,
    wh,
    dy_own,
    du,
    gw,
    gu,
    go,
    xh,
    xo,
    near_two,
    far_two,
    near_res,
    far_res,
    near_one,
    far_one,
    mid,
    dob,
    da,
    dqw,
    dkw,
    dvw,
    dk_sum,
    dv_sum,
    dx2,
    edge_out,
    edge_in,
    fore_out,
    fore_in,
    col_labels,
    res_stage,
    grad_stage,
    va,
    vb,
    sends,
    arrivals,
    locals_,
):
    at = Place()
    wires = Wires(sends, arrivals)
    low = jnp.bfloat16
    pair, block = sz.pair, sz.block
    features = 4.0 * sz.share
    used = [0]

    def load(source, target, when=None):
        made = pltpu.make_async_copy(source, target, locals_.at[used[0]])
        used[0] += 1
        run(when, made.start)
        return made

    own_rows = rows_at(sz.part * (4 * at.d + at.r), sz.part)
    loads = [
        load(s, t)
        for s, t in (
            (dy_t_all, dy_t),
            (gl_all, gl),
            (dy_all, dy),
            (wd_all, wd),
            (u_all, u),
            (dy_all.at[own_rows], dy_own),
            (wu_all, wu),
            (h2_t_all, h2_t),
            (wo_all, wo),
            (wh_all, wh),
            (x2_all, x2),
            (a_nat_all, a_nat),
            (qw_all, qw),
            (kw_all, kw),
            (vw_all, vw),
            (lse_all, lse),
            (x_own_all, x_own),
        )
    ]
    greet(at, False)
    stay = []

    gd = gw.at[:, 0 : sz.hidden]
    loads[0].wait()
    loads[1].wait()
    order, d_send, d_relay, d_arrived, d_from = collect_col(
        wires, lambda c: gd.at[rows_at(pair * c, pair)], zd, rd, at, 0
    )
    for step in range(4):
        rows = rows_at(pair * order[step], pair)
        gw[rows, 0 : sz.hidden] = times(dy_t[rows], gl[...]).astype(low)
        d_send(step)

    def relay_of(rest, block):
        def add(there):
            parts = (
                load(rest.at[:, 0:512], dqw.at[0:pair, 0:512]),
                load(rest.at[:, 512 : sz.hidden], dkw.at[0:pair, 0 : sz.hidden - 512]),
            )
            for made in parts:
                made.wait()
            rows = rows_at(pair * there, pair)
            for held, start, stop in ((dqw, 0, 512), (dkw, 512, sz.hidden)):
                both = block[rows, start:stop].astype(jnp.float32)
                both = both + held[0:pair, 0 : stop - start].astype(jnp.float32)
                block[rows, start:stop] = both.astype(low)

        return add

    gd_sends = list(wires.open)

    for made in loads[2:6]:
        made.wait()

    def through(start, tile):
        lanes = lanes_at(start, tile)
        upstream = times(dy[...], wd[:, lanes])
        value = u[:, lanes]
        inner = jnp.tanh(ROOT * (value + CUBIC * value * value * value))
        slope = 0.5 * (1.0 + inner) + 0.5 * value * (1.0 - inner * inner) * ROOT * (
            1.0 + 3.0 * CUBIC * value * value
        )
        du[:, lanes] = (upstream * slope).astype(low)

    over_tiles(sz.hidden, through)
    loads[6].wait()

    def back_up(start, tile):
        dy[:, lanes_at(start, tile)] = times_flipped(du[...], wu[rows_at(start, tile)]).astype(low)

    over_tiles(sz.width, back_up)

    def chunk_both(d, r):
        return sz.part * (4 * d + r)

    two_onward, two_total, two_sent = scatter_group(
        wires, (2, 4, 6), dy, chunk_both, near_two, mid, far_two, at, 16
    )
    loads[7].wait()
    order, u_send, u_relay, u_arrived, u_from = collect_col(
        wires, lambda c: gu.at[rows_at(pair * c, pair)], zu, ru, at, 5
    )
    for step in range(4):
        rows = rows_at(pair * order[step], pair)
        gu[rows] = times(h2_t[rows], du[...]).astype(low)
        u_send(step)
        if step == 1:
            two_onward()
    own = rows_at(pair * at.c, pair)
    own_slot = h2_t.at[own, 0 : sz.hidden]
    gd_own = load(gd.at[own], own_slot)
    before = len(wires.open)
    d_relay(relay_of(rd, gd))
    gd_sends += wires.open[before:]

    def norm_back(upstream, values, gain):
        center = jnp.sum(values, axis=1, keepdims=True) / features
        spread = jnp.sum(values * values, axis=1, keepdims=True) / features - center * center
        inverse = lax.rsqrt(spread + NORM_EPSILON)
        centered = (values - center) * inverse
        scaled = upstream * gain
        inner = (
            scaled
            - jnp.sum(scaled, axis=1, keepdims=True) / features
            - centered * (jnp.sum(scaled * centered, axis=1, keepdims=True) / features)
        )
        return (
            inner * inverse,
            jnp.sum(upstream * centered, axis=0, keepdims=True),
            jnp.sum(upstream, axis=0, keepdims=True),
        )

    loads[10].wait()
    h2_back = two_total()
    through_norm, gain_two, shift_two = norm_back(h2_back, x2[...], vec_rows[2:3])
    middle_back = dy_own[...].astype(jnp.float32) + through_norm
    dx2[...] = middle_back
    va[0, 2:3] = gain_two
    va[0, 3:4] = shift_two
    va[0, 4:8] = jnp.zeros((4, sz.width), jnp.float32)
    dob[rows_at(sz.part * at.r, sz.part)] = middle_back.astype(low)
    dob_done, dob_sent = gather_group(
        wires, (2,), lambda d, r: dob.at[rows_at(sz.part * r, sz.part)], at, 24
    )
    h1_load = load(h1_t_all, dy_t.at[:, 0 : sz.seq])

    def contract(start, tile):
        out = times_flipped(gl[...], wd[rows_at(start, tile)])
        dy[:, lanes_at(start, tile)] = out.astype(low)

    wires.close(two_sent)
    over_tiles(sz.width, contract)
    res_onward, res_total, res_sent = scatter_group(
        wires, (2, 4, 6), dy, chunk_both, near_res, mid, far_res, at, 32
    )

    dob_done()
    loads[11].wait()
    loads[8].wait()
    da[...] = times(dob[...], wo[...]).astype(low)
    slack, main = sz.slack, sz.main

    def from_natural(place):
        wanted = sz.mixed * (place // sz.pieces) + place % sz.pieces
        return jnp.where((place >= 0) & (place < sz.share), wanted, -1)

    fore_out[...] = picked(
        da[...], choose((2 * sz.mixed, 128), lambda j: from_natural(j + main - slack * at.r))
    )

    @pl.when(at.r == 0)
    def _():
        fore_in[...] = jnp.zeros_like(fore_in)

    wires.copy(fore_out, fore_in, (at.d, at.r + 1, at.c), 40, at.r < 3)

    @pl.loop(0, sz.tiles)
    def _(i):
        dy_t[rows_at(128 * i, 128), sz.seq : sz.both] = turned(dob[:, lanes_at(128 * i, 128)]).astype(low)

    res_onward()

    for step in range(4):
        there = (at.c + step) % 4
        rows = rows_at(pair * there, pair)
        go[rows] = times(dy_t[rows, sz.seq : sz.both], a_nat[...]).astype(low)
        wires.copy(
            go.at[rows, lanes_at(sz.mixed * (1 - at.d), sz.mixed)], xo.at[there], at.peer(4), 48 + there
        )
    wires.arrived(fore_in, 40, (at.d, at.r - 1, at.c), at.r > 0)
    window = times(da[...], choose((2 * sz.mixed, main), lambda j: from_natural(j - slack * at.r)))
    da_first = window[:, 0:128] + fore_in[...].astype(jnp.float32)
    da[:, 128:main] = window[:, 128:main].astype(low)
    da[:, 0:128] = da_first.astype(low)
    da[:, main : main + 128] = fore_out[...]

    row_labels = segments.at[:, lanes_at(sz.seq * at.c, sz.seq)]
    col_labels[...] = jnp.concatenate([row_labels[...]] * 8, axis=0).astype(jnp.float32).T[:, 0:1]
    for made in loads[12:17]:
        made.wait()
    half = sz.seq // 2

    def heads_back(p, count):
        tile = lanes_at(128 * p, 128)
        dk_sum[...] = jnp.zeros_like(dk_sum)
        dv_sum[...] = jnp.zeros_like(dv_sum)
        for q in range(2):
            rows = slice(half * q, half * (q + 1))
            keys = half * (q + 1)
            order = lax.broadcasted_iota(jnp.int32, (half, keys), 0) + half * q
            allowed = (col_labels[rows, :] == row_labels[:, 0:keys].astype(jnp.float32)) & (
                order >= lax.broadcasted_iota(jnp.int32, (half, keys), 1)
            )
            lanes = lax.broadcasted_iota(jnp.int32, (half, 128), 1)
            side = lanes // HD
            total = jnp.zeros((half, 128), jnp.float32)
            for h in range(count):
                queries = jnp.where(side == h, qw[rows, tile].astype(jnp.float32) * HD ** (-0.5), 0.0)
                queries = queries.astype(low)
                pulled = jnp.where(side == h, da[rows, tile].astype(jnp.float32), 0.0).astype(low)
                found = jnp.sum(jnp.where(lanes == 2 * p + h, lse[rows, :], 0.0), axis=1, keepdims=True)
                scores = times_flipped(queries, kw[0:keys, tile])
                soft = jnp.where(allowed, jnp.exp(jnp.where(allowed, scores - found, MASKED)), 0.0)
                soft_back = times_flipped(pulled, vw[0:keys, tile])
                inner = jnp.sum(soft_back * soft, axis=1, keepdims=True)
                score_back = (soft * (soft_back - inner)).astype(low)
                piece = times(score_back, kw[0:keys, tile]) * HD ** (-0.5)
                total = jnp.where(side == h, piece, total)
                dk_sum[0:keys] += times_outer(score_back, queries)
                dv_sum[0:keys] += times_outer(soft.astype(low), pulled)
            dqw[rows, tile] = total.astype(low)
        dkw[:, tile] = dk_sum[...].astype(low)
        dvw[:, tile] = dv_sum[...].astype(low)

    @pl.loop(0, main // 128)
    def _(p):
        heads_back(p, 2)

    @pl.when(at.r == 3)
    def _():
        heads_back(main // 128, 1)

    def compact(column):
        part, place = column // HD, column % HD
        return jnp.where(part < 3, 128 * part + place, -1)

    table = choose((384, 256), compact)
    backs = (dqw, dkw, dvw)
    edge_out[...] = picked(jnp.concatenate([b[:, 0:128] for b in backs], axis=1), table)
    wires.copy(edge_out, edge_in, (at.d, at.r - 1, at.c), 41, at.r > 0)

    @pl.when(at.r == 3)
    def _():
        edge_in[...] = picked(jnp.concatenate([b[:, main : main + 128] for b in backs], axis=1), table)

    def go_home(values, stage, every, halves, out, base):
        flipped = values.T
        for c in range(4):
            for y in range(2):
                rows = slice(pair * c + block * y, pair * c + block * (y + 1))
                stage[c, y] = flipped[rows].astype(low)
        holds = at.k == at.c % 2
        lanes = lanes_at(sz.part * at.r, sz.part)
        held = []
        for y in range(2):
            there = 2 * y + at.c % 2
            wires.copy(
                stage.at[:, y], every.at[:, :, lanes], (at.d, there, at.c), base + at.r, there != at.r
            )
            held.append((there == at.r, load(stage.at[:, y], every.at[:, :, lanes], there == at.r)))

        def along():
            for r in range(4):
                block_r = every.at[:, :, sz.part * r : sz.part * (r + 1)]
                wires.arrived(block_r, base + r, (at.d, r, at.c), holds & (at.r != r))
            for when, made in held:
                run(when, made.wait)
            del held[:]
            for c in range(4):
                wires.copy(
                    every.at[c], halves.at[at.c // 2], at.along(c), base + 4 + at.c // 2, holds & (at.c != c)
                )
                when = holds & (at.c == c)
                held.append((when, load(every.at[c], halves.at[at.c // 2], when)))

        def across():
            for when, made in held:
                run(when, made.wait)
            for t in range(2):
                there = 2 * t + at.k
                wires.arrived(halves.at[t], base + 4 + t, at.along(there), there != at.c)
            mine = out.at[rows_at(block * at.y, block)]
            wires.copy(halves.at[1 - at.y], mine, at.peer(2), base + 6)
            stay.append(load(halves.at[at.y], mine))

        def finish():
            wires.arrived(out.at[rows_at(block * (1 - at.y), block)], base + 6, at.peer(2))

        return along, across, finish

    res_along, res_across, res_finish = go_home(
        x2[...] + res_total(), res_stage, res_all, res_two, result_home, 56
    )
    wires.close(res_sent)

    wires.arrived(edge_in, 41, (at.d, at.r + 1, at.c), at.r < 3)

    def unfold(column):
        tile, lane = column // 128, column % 128
        inside = jnp.where(lane < HD - 16, HD * tile + lane + 16, -1)
        tail = jnp.where(lane < 48, HD * (lane // 16) + lane % 16, -1)
        return jnp.where(tile < 3, inside, tail)

    edges = picked(edge_in[...], choose((256, 512), unfold))
    lane = lax.broadcasted_iota(jnp.int32, (sz.seq, 128), 1)
    pieces = []
    for i, back in enumerate(backs):
        first = jnp.where(lane < slack * at.r, edges[:, 128 * i : 128 * i + 128], back[:, 0:128])
        pieces += [first, back[:, 128:main]]
    pieces.append(edges[:, 384:512])
    wires.close(dob_sent)
    own_back = dob.at[:, 0 : sz.heads]
    own_back[...] = jnp.concatenate(pieces, axis=1)

    wires.close(gd_sends)
    gd_own.wait()
    h1_load.wait()
    h_order, h_send, h_relay, h_arrived, h_from = collect_col(
        wires, lambda c: xh.at[c], zh, rh, at, 72
    )
    for step in range(4):
        there = h_order[step]
        rows = rows_at(pair * there, pair)
        gw[rows] = times(dy_t[rows, 0 : sz.seq], own_back[...]).astype(low)
        other = gw.at[rows_at(pair * there + block * (1 - at.d), block)]
        wires.copy(other, xh.at[there], at.peer(4), 80 + there)

    def o_heads(step):
        there = h_order[step]
        wires.arrived(xh.at[there], 80 + there, at.peer(4))
        mine = rows_at(pair * there + block * at.d, block)
        xh[there] = (gw[mine].astype(jnp.float32) + xh[there].astype(jnp.float32)).astype(low)
        h_send(step)

    for made in loads[9:10]:
        made.wait()

    def back_in(start, tile):
        out = times_flipped(own_back[...], wh[rows_at(start, tile)])
        dy[0 : sz.seq, lanes_at(start, tile)] = out.astype(low)

    over_tiles(sz.width, back_in)
    one_onward, one_total, _ = scatter_group(
        wires, (2,), dy, lambda d, r: sz.part * r, near_one, mid, far_one, at, 64
    )
    order, o_send, o_relay, o_arrived, o_from = collect_col(
        wires, lambda c: xo.at[c], zo, ro, at, 10
    )
    for step in range(4):
        there = order[step]
        wires.arrived(xo.at[there], 48 + there, at.peer(4))
        mine = go[rows_at(pair * there, pair), lanes_at(sz.mixed * at.d, sz.mixed)]
        xo[there] = (mine.astype(jnp.float32) + xo[there].astype(jnp.float32)).astype(low)
        o_send(step)

    def relay_out(there):
        load(ro, dqw.at[0:pair, 0 : sz.mixed]).wait()
        both = xo[there].astype(jnp.float32) + dqw[0:pair, 0 : sz.mixed].astype(jnp.float32)
        xo[there] = both.astype(low)

    res_along()
    one_onward()
    o_heads(0)
    h1_back = one_total()
    through_norm, gain_one, shift_one = norm_back(
        h1_back, x_own[...].astype(jnp.float32), vec_rows[0:1]
    )
    va[0, 0:1] = gain_one
    va[0, 1:2] = shift_one
    for mask in range(1, 8):
        wires.copy(va.at[0], va.at[mask], at.peer(mask), 84 + mask)
    grad_along, grad_across, grad_finish = go_home(
        dx2[...] + through_norm, grad_stage, grad_all, grad_two, grad_home, 104
    )
    o_heads(1)
    u_relay(relay_of(ru, gu))
    o_heads(2)
    grad_along()
    res_across()
    o_relay(relay_out)
    o_heads(3)
    grad_across()


    def bring(c, landing, needed):
        made = load(landing.at[c], h2_t.at[pair * c : pair * (c + 1), 0 : sz.hidden], needed)
        run(needed, made.wait)

        @pl.when(jnp.logical_not(needed) & (at.c != c))
        def _():
            h2_t[pair * c : pair * (c + 1), 0 : sz.hidden] = jnp.zeros((pair, sz.hidden), low)

    def summed(lanes):
        result = jnp.zeros((pair, lanes.stop - lanes.start), jnp.float32)
        for c in range(4):
            result = result + h2_t[pair * c : pair * (c + 1), lanes].astype(jnp.float32)
        return result

    half_rows = sz.pieces

    def natural_rows(value):
        flipped = value.T
        return jnp.concatenate(
            [flipped[:, 0:half_rows], flipped[:, block : block + half_rows]], axis=1
        )

    def own_half(row):
        return jnp.where(at.d == 0, row[:, 0:half_rows], row[:, half_rows : 2 * half_rows])

    for c in range(4):
        d_arrived(c)
        bring(c, zd, d_from(c))
    for i in range(sz.hidden // 128):
        rows = min(128, 4 * sz.pieces - 128 * i)
        value = natural_rows(summed(slice(128 * i, 128 * (i + 1))))
        u[128 * i : 128 * i + rows, 0 : sz.share] = value[0:rows]
        if rows < 128:
            vec_out[5:6, 0:half_rows] = own_half(value[rows : rows + 1])
    down_out = load(u.at[0 : 4 * sz.pieces, 0:512], out_down)
    def relay_heads(there):
        parts = [
            load(rh.at[:, s:e], t.at[0:block, 0 : e - s])
            for t, s, e in ((dqw, 0, 512), (dkw, 512, 1024), (dvw, 1024, sz.heads))
        ]
        for made in parts:
            made.wait()
        for t, s, e in ((dqw, 0, 512), (dkw, 512, 1024), (dvw, 1024, sz.heads)):
            both = xh[there, :, s:e].astype(jnp.float32) + t[0:block, 0 : e - s].astype(jnp.float32)
            xh[there, :, s:e] = both.astype(low)

    h_relay(relay_heads)
    gu_own = load(gu.at[own], own_slot)
    for c in range(4):
        u_arrived(c)
        bring(c, zu, u_from(c))
    gu_own.wait()
    theirs = rows_at(pair * at.c + block * (1 - at.d), block)

    def part_sum(side, lanes):
        result = jnp.zeros((block, sz.hidden), jnp.float32)
        for c in range(4):
            result = result + h2_t[rows_at(pair * c + block * side, block), lanes].astype(jnp.float32)
        return result

    every = slice(0, sz.hidden)
    gu[theirs] = part_sum(1 - at.d, every).astype(low)
    wires.copy(gu.at[theirs], xu, at.peer(4), 97)
    mine_sum = part_sum(at.d, every)
    down_out.wait()
    wires.arrived(xu, 97, at.peer(4))
    partner_sum = xu[...].astype(jnp.float32)
    for side in range(2):

        @pl.when(at.d == side)
        def _():
            both = (mine_sum, partner_sum) if side == 0 else (partner_sum, mine_sum)
            for j in range(4):
                rows = slice(block * j, block * (j + 1))
                for i in range(2):
                    u[rows, half_rows * i : half_rows * (i + 1)] = both[i][:, half_rows * j : half_rows * (j + 1)]

    bias_sum = mine_sum[half_rows : half_rows + 1]
    for j in range(4):
        vec_out[8 + j : 9 + j, 0:half_rows] = bias_sum[:, half_rows * j : half_rows * (j + 1)]
    up_out = load(u.at[0 : 4 * block, 0:512], out_up)

    for c in range(4):
        o_arrived(c)
        needed = o_from(c)
        made = load(zo.at[c], wd.at[pair * c : pair * (c + 1), 0 : sz.mixed], needed)
        run(needed, made.wait)

        @pl.when(jnp.logical_not(needed))
        def _():
            wd[pair * c : pair * (c + 1), 0 : sz.mixed] = jnp.zeros((pair, sz.mixed), low)

    value = xo[at.c].astype(jnp.float32)
    for c in range(4):
        value = value + wd[pair * c : pair * (c + 1), 0 : sz.mixed].astype(jnp.float32)
    flipped = natural_rows(value)
    vec_out[4:5, 0:half_rows] = own_half(flipped[half_rows : half_rows + 1])
    flipped = flipped[0:block]
    for i in range(4):
        held = (dk_sum, dv_sum)[i // 2].at[block * (i % 2) : block * (i % 2 + 1)]
        lanes = min(128, sz.share - 128 * i)
        held[:, 0:lanes] = flipped[:, 128 * i : 128 * i + lanes]
        stay.append(load(held, out_out.at[:, 128 * i : 128 * (i + 1)]))

    for mask in range(1, 8):
        wires.arrived(va.at[mask], 84 + mask, at.peer(mask))
    vb[at.c] = functools.reduce(lambda a, b: a + b, [va[mask] for mask in range(8)])
    for c in range(4):
        wires.copy(vb.at[at.c], vb.at[at.c], at.along(c), 98 + at.c, at.c != c)

    for c in range(4):
        wires.arrived(vb.at[c], 98 + c, at.along(c), at.c != c)
    sums = vb[0] + vb[1] + vb[2] + vb[3]
    picked_sums = jnp.zeros((4, half_rows), jnp.float32)
    for i in range(8):
        cut = sums[0:4, block * i : block * i + half_rows]
        picked_sums = jnp.where(2 * at.c + at.d == i, cut, picked_sums)
    vec_out[0:4, 0:half_rows] = picked_sums
    res_finish()
    grad_finish()
    up_out.wait()
    rest_lanes = sz.heads - sz.hidden
    for c in range(4):
        h_arrived(c)
        needed = h_from(c)
        rows = slice(block * c, block * (c + 1))
        parts = (
            load(zh.at[c, :, 0 : sz.hidden], wd.at[rows], needed),
            load(zh.at[c, :, sz.hidden : sz.heads], wu.at[rows, 0:rest_lanes], needed),
        )
        for made in parts:
            run(needed, made.wait)

        @pl.when(jnp.logical_not(needed))
        def _():
            wd[rows] = jnp.zeros((block, sz.hidden), low)
            wu[rows, 0:rest_lanes] = jnp.zeros((block, rest_lanes), low)

    left = xh[at.c, :, 0 : sz.hidden].astype(jnp.float32)
    right = xh[at.c, :, sz.hidden : sz.heads].astype(jnp.float32)
    for c in range(4):
        rows = slice(block * c, block * (c + 1))
        left = left + wd[rows].astype(jnp.float32)
        right = right + wu[rows, 0:rest_lanes].astype(jnp.float32)
    whole = jnp.concatenate([left, right], axis=1)
    for i in range(3):
        turned_columns = jnp.concatenate(
            [
                whole[:, main * i : main * (i + 1)],
                whole[:, 3 * main + slack * i : 3 * main + slack * (i + 1)],
            ],
            axis=1,
        )
        rows = slice(block * i, block * (i + 1))
        for r in range(4):

            @pl.when(at.r == r)
            def _():
                cut = slack * r
                value = turned_columns
                if cut:
                    value = jnp.concatenate([value[:, cut:], value[:, 0:cut]], axis=1)
                u[rows, 0 : sz.share] = value
                if i != 1:
                    vec_out[6 + i // 2 : 7 + i // 2, 0:half_rows] = own_half(
                        value[half_rows : half_rows + 1]
                    )

    stay.append(load(u.at[0 : 3 * block, 0:512], out_heads))
    for made in stay:
        made.wait()
    wires.close()


def update_kernel(sz, rates, grads, result_in, grad_in, weights, firsts, seconds, outs):
    down, out, up, heads, vectors = grads
    share, pieces, block = sz.share, sz.pieces, sz.block

    def move(i, place, gradient, decay):
        first_new, second_new, weight_new = adam_terms(
            weights[i][place], gradient, firsts[i][place], seconds[i][place], rates[i], decay
        )
        outs[3 * i + 2][place] = first_new
        outs[3 * i + 3][place] = second_new
        outs[3 * i + 4][place] = weight_new

    for part in range(3):
        move(0, part, heads[part, :, 0:share], MATRIX_DECAY)
    move(1, slice(None), out[:, 0:share], MATRIX_DECAY)
    move(2, slice(None), jnp.stack([up[j, :, 0:share] for j in range(4)], axis=1), MATRIX_DECAY)
    move(3, slice(None), down[:, 0:share], MATRIX_DECAY)

    @pl.when(pl.program_id(0) == 0)
    def _():
        for i, source, row in (
            (4, 0, 0), (4, 1, 1), (5, 4, 0), (5, 2, 1), (5, 3, 2), (5, 5, 3),
            (6, 6, 0), (6, 7, 1), (7, 8, 0), (7, 9, 1), (7, 10, 2), (7, 11, 3),
        ):
            move(i, row, vectors[source : source + 1, 0:pieces], 0.0)

    def plain(rows):
        rows = rows.astype(jnp.float32)
        return jnp.concatenate([rows[0:pieces], rows[block : block + pieces]], axis=0)

    @pl.when(pl.program_id(0) == 1)
    def _():
        outs[0][...] = plain(result_in[...]).astype(jnp.bfloat16)

    @pl.when(pl.program_id(0) == 2)
    def _():
        outs[1][...] = plain(grad_in[...])


def fused(
    tokens,
    cotangent,
    segments,
    weights,
    firsts,
    seconds,
):
    low = jnp.bfloat16
    seq, share = tokens.shape
    pieces = weights[1].shape[2]
    sz = Sizes(share, pieces, seq)
    block, main = sz.block, sz.main

    def views(arrays):
        heads, out, up, down, *small = arrays
        return (
            jnp.transpose(heads.reshape(pieces, 3, share), (1, 0, 2)),
            out.reshape(pieces, share),
            up.reshape(pieces, 4, share),
            down.reshape(4 * pieces, share),
            *[each.reshape(each.shape[0], 1, pieces) for each in small],
        )

    viewed = views(weights)
    labels = segments.reshape(1, -1)

    def made(*shape, dtype=low):
        return jax.ShapeDtypeStruct(shape, dtype)

    def held(*shape, dtype=low):
        return pltpu.VMEM(shape, dtype)

    w, seq, both, part = sz.width, sz.seq, sz.both, sz.part
    vmem, anywhere = pl.BlockSpec(memory_space=pltpu.VMEM), pl.BlockSpec(memory_space=pl.ANY)
    dma = pltpu.SemaphoreType.DMA
    f32 = jnp.float32
    wide = 3 * 128 + 128
    outs = pl.pallas_call(
        functools.partial(forward_kernel, sz),
        out_shape=(
            made(w, sz.heads),
            made(w, 2 * sz.mixed),
            made(w, sz.hidden),
            made(w, sz.hidden),
            made(w, seq),
            made(w, both),
            made(w, both),
            made(both, w),
            made(both, sz.hidden, dtype=f32),
            made(both, sz.hidden),
            made(seq, main + 128),
            made(seq, main + 128),
            made(seq, main + 128),
            made(seq, 2 * sz.mixed),
            made(seq, 128, dtype=f32),
            made(part, w, dtype=f32),
            made(part, w),
            made(8, w, dtype=f32),
        ),
        in_specs=[anywhere] * 6 + [vmem] * 5,
        out_specs=[anywhere] * 18,
        scratch_shapes=[
            held(w, sz.heads),
            held(w, 2 * sz.mixed),
            held(w, sz.hidden),
            held(w, sz.hidden),
            held(w, seq),
            held(w, both),
            held(w, both),
            held(both, w),
            held(both, sz.hidden, dtype=f32),
            held(both, sz.hidden),
            held(seq, main + 128),
            held(seq, main + 128),
            held(seq, main + 128),
            held(seq, 2 * sz.mixed),
            held(seq, 128, dtype=f32),
            held(part, w, dtype=f32),
            held(part, w),
            held(8, w, dtype=f32),
            held(w, seq),
            held(seq, w),
            held(both, w),
            held(seq, sz.heads),
            held(seq, main + 128),
            held(w, 128),
            held(seq, w),
            held(seq, 256),
            held(seq, 256),
            held(seq, 128),
            held(2, part, w),
            held(1, part, w),
            held(1, part, w),
            held(share, seq),
            held(share, seq),
            held(3, pieces, share, dtype=f32),
            held(pieces, share, dtype=f32),
            held(pieces, 4, share, dtype=f32),
            held(4 * pieces, share, dtype=f32),
            held(sz.pair, seq),
            held(sz.pair, seq),
            held(block, sz.heads),
            held(sz.pair, sz.mixed),
            held(block, 2 * sz.hidden),
            held(sz.pair, sz.hidden),
            held(block, 128),
            held(seq, 1, dtype=f32),
            held(block, seq),
            held(block, seq),
            dma((160,)),
            dma((160,)),
            dma((48,)),
        ],
        compiler_params=pltpu.CompilerParams(
            collective_id=0, has_side_effects=True, vmem_limit_bytes=VMEM_BYTES
        ),
        cost_estimate=pl.CostEstimate(flops=10**10, bytes_accessed=10**8, transcendentals=10**6),
    )(tokens.T, cotangent.T, *viewed, labels)
    (wh, wo, wu, wd, h1_t, h2_t, dy_t, dy, u, gl, qw, kw, vw, a_nat, lse, x2, x_own, vec_rows) = outs
    outs = pl.pallas_call(
        functools.partial(backward_kernel, sz),
        out_shape=(
            made(4 * pieces, 512, dtype=f32),
            made(4 * block, 512, dtype=f32),
            made(block, 512, dtype=f32),
            made(3 * block, 512, dtype=f32),
            made(sz.pair, seq),
            made(sz.pair, seq),
            made(16, 256, dtype=f32),
            made(4, sz.pair, sz.hidden),
            made(4, sz.pair, sz.hidden),
            made(4, sz.pair, sz.mixed),
            made(4, block, sz.heads),
            made(sz.pair, sz.hidden),
            made(sz.pair, sz.hidden),
            made(sz.pair, sz.mixed),
            made(block, sz.heads),
            made(4, block, seq),
            made(2, block, seq),
            made(4, block, seq),
            made(2, block, seq),
        ),
        in_specs=[anywhere] * 17 + [vmem] * 2,
        out_specs=[anywhere] * 6 + [vmem] + [anywhere] * 12,
        scratch_shapes=[
            held(seq, main + 128),
            held(seq, main + 128),
            held(seq, main + 128),
            held(seq, 2 * sz.mixed),
            held(seq, 128, dtype=f32),
            held(part, w, dtype=f32),
            held(part, w),
            held(block, sz.hidden),
            held(both, w),
            held(w, both),
            held(both, sz.hidden, dtype=f32),
            held(both, sz.hidden),
            held(w, both),
            held(w, sz.hidden),
            held(w, sz.hidden),
            held(w, 2 * sz.mixed),
            held(w, sz.heads),
            held(part, w),
            held(both, sz.hidden),
            held(w, sz.heads),
            held(w, sz.hidden),
            held(w, 2 * sz.mixed),
            held(4, block, sz.heads),
            held(4, sz.pair, sz.mixed),
            held(4, part, w),
            held(3, part, w),
            held(4, part, w),
            held(3, part, w),
            held(2, part, w),
            held(1, part, w),
            held(3, part, w),
            held(seq, w),
            held(seq, 2 * sz.mixed),
            held(seq, main + 128),
            held(seq, main + 128),
            held(seq, main + 128),
            held(seq, 128, dtype=f32),
            held(seq, 128, dtype=f32),
            held(part, w, dtype=f32),
            held(seq, 256),
            held(seq, 256),
            held(seq, 128),
            held(seq, 128),
            held(seq, 1, dtype=f32),
            held(4, 2, block, part),
            held(4, 2, block, part),
            held(8, 8, w, dtype=f32),
            held(4, 8, w, dtype=f32),
            dma((128,)),
            dma((120,)),
            dma((80,)),
        ],
        compiler_params=pltpu.CompilerParams(
            collective_id=1, has_side_effects=True, vmem_limit_bytes=VMEM_BYTES
        ),
        cost_estimate=pl.CostEstimate(flops=2 * 10**10, bytes_accessed=10**8, transcendentals=10**6),
    )(
        dy, dy_t, u, gl, h2_t, wd, wu, wo, wh, h1_t,
        qw, kw, vw, a_nat, lse, x2, x_own, vec_rows, labels,
    )
    down, up, out, heads, result_home, grad_home, vectors = outs[:7]
    steps = 5
    chunk = pieces // steps

    def rows_of(shape, axis, size):
        block_shape = list(shape)
        block_shape[axis] = size
        return pl.BlockSpec(tuple(block_shape), lambda i: tuple(i if a == axis else 0 for a in range(len(shape))))

    def whole(shape):
        return pl.BlockSpec(tuple(shape), lambda i: (0,) * len(shape))

    matrix_specs = (
        rows_of((3, pieces, share), 1, chunk),
        rows_of((pieces, share), 0, chunk),
        rows_of((pieces, 4, share), 0, chunk),
        rows_of((4 * pieces, share), 0, 4 * chunk),
        *[whole(each.shape) for each in viewed[4:]],
    )
    grads = (down, out, up.reshape(4, block, 512), heads.reshape(3, block, 512), vectors)
    grad_specs = (
        rows_of((4 * pieces, 512), 0, 4 * chunk),
        rows_of((block, 512), 0, chunk),
        rows_of((4, block, 512), 1, chunk),
        rows_of((3, block, 512), 1, chunk),
        whole((16, 256)),
    )
    rates = (0.05, 0.2, 0.05, 0.025, 0.3, 0.3, 0.3, 0.3)
    arguments = (*grads, result_home, grad_home, *viewed, *views(firsts), *views(seconds))
    out_shape = [made(share, seq), made(share, seq, dtype=f32)]
    out_specs = [whole((share, seq)), whole((share, seq))]
    for each, spec in zip(viewed, matrix_specs, strict=True):
        out_shape += [jax.ShapeDtypeStruct(each.shape, f32)] * 3
        out_specs += [spec] * 3

    def update(*refs):
        ins, outs = refs[:31], refs[31:]
        update_kernel(sz, rates, ins[:5], ins[5], ins[6], ins[7:15], ins[15:23], ins[23:31], outs)

    updated = pl.pallas_call(
        update,
        grid=(steps,),
        out_shape=out_shape,
        in_specs=[*grad_specs, whole((sz.pair, seq)), whole((sz.pair, seq)), *matrix_specs * 3],
        out_specs=out_specs,
        compiler_params=pltpu.CompilerParams(vmem_limit_bytes=VMEM_BYTES),
        cost_estimate=pl.CostEstimate(
            flops=20 * 10**6, bytes_accessed=30 * 10**6, transcendentals=2 * 10**6
        ),
    )(*arguments)
    results = [updated[0].T, updated[1].T]
    for i, weight in enumerate(weights):
        for each in updated[2 + 3 * i : 5 + 3 * i]:
            if i == 0:
                each = jnp.transpose(each, (1, 0, 2))
            results.append(each.reshape(weight.shape))
    return tuple(results)


def normalize(inputs):
    center = jnp.mean(inputs, axis=1, keepdims=True)
    spread = jnp.mean(inputs * inputs, axis=1, keepdims=True) - center * center
    inverse = lax.rsqrt(spread + NORM_EPSILON)
    return ((inputs - center) * inverse, inverse)


def norm_pull(upstream, centered, inverse, gain):
    scaled = upstream * gain
    inner = (
        scaled
        - jnp.mean(scaled, axis=1, keepdims=True)
        - centered * jnp.mean(scaled * centered, axis=1, keepdims=True)
    )
    return inner * inverse


def crossed(blocks, n):
    pairs = [(i * n + j, j * n + i) for i in range(n) for j in range(n)]
    return lax.ppermute(blocks, ("row", "col"), pairs)


def scatter_rows(partial):
    return lax.psum_scatter(
        partial.astype(jnp.bfloat16), "row", scatter_dimension=0, tiled=True
    ).astype(jnp.float32)


def gather_rows(local):
    return lax.all_gather(local, "row", axis=0, tiled=True)


def split_heads(rows):
    return jnp.transpose(rows.reshape(rows.shape[0], -1, HD), (1, 0, 2))


def join_heads(values):
    return jnp.transpose(values, (1, 0, 2)).reshape(values.shape[1], -1)


def scores_of(queries, keys, allowed):
    scores = jnp.einsum(
        "hqe,hke->hqk", queries, keys, preferred_element_type=jnp.float32
    ) * HD ** (-0.5)
    return jnp.where(allowed[None], scores, MASKED)


def gathered(
    tokens,
    cotangent,
    segments,
    w_heads,
    w_out,
    w_up,
    w_down,
    norm_vectors,
    width_vectors,
    attend_bias,
    hidden_vectors,
):
    n_dp, n_row, n_col = (lax.axis_size(name) for name in ("dp", "row", "col"))
    row = lax.axis_index("row")
    low = jnp.bfloat16
    share = tokens.shape[1]
    width = share * n_col
    seq = tokens.shape[0]
    part = seq // n_row
    near = HEADS // n_row
    window = (HEADS - near * (n_row - 1)) * HD
    step = near * HD
    edge = width - (share + step * (n_row - 1)) if n_row > 1 else 0
    edge = window - share
    to_next = [(i, i + 1) for i in range(n_row - 1)]
    to_last = [(i + 1, i) for i in range(n_row - 1)]
    offset = edge - (share - step) * row

    vectors = jnp.concatenate(
        [
            norm_vectors.reshape(2, -1),
            width_vectors.reshape(4, -1),
            attend_bias.reshape(2, -1),
            hidden_vectors.reshape(4, -1),
        ]
    ).astype(low)
    vectors = lax.all_gather(vectors, ("row", "col", "dp"), axis=0, tiled=False)
    vectors = vectors.reshape(n_row, n_col, n_dp, 12, -1).astype(jnp.float32)
    by_col = jnp.transpose(vectors[0], (2, 0, 1, 3)).reshape(12, width)
    by_row = jnp.transpose(vectors[:, 0], (2, 0, 1, 3)).reshape(12, width)
    gain_one, shift_one, bias_out, gain_two, shift_two, bias_down = (by_col[i] for i in range(6))
    zeros = jnp.zeros((1, window), jnp.float32)
    attend_rows = lax.dynamic_slice_in_dim(by_row[6:8], row * step, window, axis=1)
    heads_bias = jnp.concatenate([attend_rows[0:1], zeros, attend_rows[1:2]]).reshape(-1)
    unit_bias = lax.dynamic_slice_in_dim(by_row[8:12], row * share, share, axis=1).reshape(-1)

    own = w_heads.astype(low).reshape(-1, 3, share)
    passed = lax.ppermute(own[:, :, share - edge :], "row", to_next)
    own = jnp.concatenate([passed, own, jnp.zeros_like(passed)], axis=2)
    own = lax.dynamic_slice_in_dim(own, offset, window, axis=2).reshape(-1, 3 * window)
    heads_matrix = lax.all_gather(own, ("col", "dp"), axis=0, tiled=True)
    out_matrix = lax.all_gather(w_out.astype(low).reshape(-1, share), ("col", "dp"), axis=0)
    out_matrix = jnp.transpose(out_matrix.reshape(n_col, share, share), (1, 0, 2))
    out_matrix = out_matrix.reshape(share, width)
    passed = lax.ppermute(out_matrix[share - edge :], "row", to_next)
    out_matrix = jnp.concatenate([passed, out_matrix, jnp.zeros_like(passed)])
    out_matrix = lax.dynamic_slice_in_dim(out_matrix, offset, window)
    owned = (jnp.arange(window) < step) | (row == n_row - 1)
    out_matrix = jnp.where(owned[:, None], out_matrix, jnp.zeros_like(out_matrix))
    up_matrix = lax.all_gather(
        w_up.astype(low).reshape(-1, 4 * share), ("col", "dp"), axis=0, tiled=True
    )
    down_matrix = lax.all_gather(w_down.astype(low).reshape(4, -1, share), ("col", "dp"), axis=0)
    down_matrix = down_matrix.reshape(n_col, n_dp, 4, -1, share)
    down_matrix = jnp.transpose(down_matrix, (2, 1, 3, 0, 4)).reshape(4 * share, width)

    inputs_low = lax.all_gather(crossed(tokens, n_row), "row", axis=1, tiled=True)
    upstream = lax.all_gather(crossed(cotangent, n_row), "row", axis=1, tiled=True)
    inputs = inputs_low.astype(jnp.float32)
    centered_one, inverse_one = normalize(inputs)
    normed_one = (centered_one * gain_one + shift_one).astype(low)
    projected = (times(normed_one, heads_matrix) + heads_bias).astype(low)
    queries, keys, values = (
        split_heads(projected[:, i * window : (i + 1) * window]) for i in range(3)
    )
    labels = lax.dynamic_slice_in_dim(segments, lax.axis_index("col") * seq, seq)
    places = jnp.arange(seq, dtype=jnp.int32)
    allowed = (labels[:, None] == labels[None, :]) & (places[:, None] >= places[None, :])
    scores = scores_of(queries, keys, allowed)
    highest = jnp.max(scores, axis=-1, keepdims=True)
    log_total = highest + jnp.log(jnp.sum(jnp.exp(scores - highest), axis=-1, keepdims=True))
    soft = jnp.exp(scores - log_total).astype(low)
    mixed = jnp.einsum("hqk,hke->hqe", soft, values, preferred_element_type=jnp.float32)
    mixed = join_heads(mixed.astype(low))
    branch = scatter_rows(times(mixed, out_matrix))
    mine = row * part
    middle = lax.dynamic_slice_in_dim(inputs, mine, part) + (branch + bias_out)
    centered_two, inverse_two = normalize(middle)
    normed_two = gather_rows((centered_two * gain_two + shift_two).astype(low))
    hidden = times(normed_two, up_matrix) + unit_bias
    activated, smooth_pull = jax.vjp(smooth, hidden)
    activated = activated.astype(low)
    result = (middle + (scatter_rows(times(activated, down_matrix)) + bias_down)).astype(low)

    down_back = times_flipped(upstream, down_matrix)
    grad_down = times_outer(activated, upstream)
    hidden_back = smooth_pull(down_back)[0].astype(low)
    grad_up = times_outer(normed_two, hidden_back)
    unit_sum = jnp.sum(hidden_back, axis=0, dtype=jnp.float32)
    normed_two_back = scatter_rows(times_flipped(hidden_back, up_matrix))
    upstream_own = lax.dynamic_slice_in_dim(upstream, mine, part).astype(jnp.float32)
    middle_back = upstream_own + norm_pull(normed_two_back, centered_two, inverse_two, gain_two)
    branch_own = middle_back.astype(low)
    branch_back = gather_rows(branch_own)
    mixed_back = times_flipped(branch_back, out_matrix).astype(low)
    grad_out = times_outer(mixed, branch_back)
    mixed_back = split_heads(mixed_back)
    scores_again = scores_of(queries, keys, allowed)
    soft = jnp.exp(scores_again - log_total)
    soft_back = jnp.einsum("hqe,hke->hqk", mixed_back, values, preferred_element_type=jnp.float32)
    row_inner = jnp.sum(soft_back * soft, axis=-1, keepdims=True)
    score_back = (soft * (soft_back - row_inner)).astype(low)
    query_back = jnp.einsum(
        "hqk,hke->hqe", score_back, keys, preferred_element_type=jnp.float32
    ) * HD ** (-0.5)
    key_back = jnp.einsum(
        "hqk,hqe->hke", score_back, queries, preferred_element_type=jnp.float32
    ) * HD ** (-0.5)
    value_back = jnp.einsum(
        "hqk,hqe->hke", soft.astype(low), mixed_back, preferred_element_type=jnp.float32
    )
    heads_back = jnp.concatenate(
        [join_heads(each.astype(low)) for each in (query_back, key_back, value_back)], axis=1
    )
    heads_sum = jnp.sum(heads_back, axis=0, dtype=jnp.float32)
    normed_one_back = scatter_rows(times_flipped(heads_back, heads_matrix))
    grad_heads = times_outer(normed_one, heads_back)
    centered_own = lax.dynamic_slice_in_dim(centered_one, mine, part)
    inverse_own = lax.dynamic_slice_in_dim(inverse_one, mine, part)
    input_back = middle_back + norm_pull(normed_one_back, centered_own, inverse_own, gain_one)

    def homeward(own):
        own = lax.all_to_all(own, "row", split_axis=1, concat_axis=0, tiled=True)
        return crossed(own, n_row)

    result_tokens = homeward(result)
    input_gradient = homeward(input_back.astype(low)).astype(jnp.float32)

    by_token = jnp.stack(
        [
            jnp.sum(normed_one_back * centered_own, axis=0),
            jnp.sum(normed_one_back, axis=0),
            jnp.sum(branch_own.astype(jnp.float32), axis=0),
            jnp.sum(normed_two_back * centered_two, axis=0),
            jnp.sum(normed_two_back, axis=0),
            jnp.sum(upstream_own, axis=0),
        ]
    )
    owned_rows = jnp.where(owned, heads_sum.reshape(3, window)[0::2], 0.0)
    by_unit = jnp.concatenate(
        [
            lax.dynamic_update_slice_in_dim(
                jnp.zeros((2, width), jnp.float32), owned_rows, row * step, axis=1
            ),
            lax.dynamic_update_slice_in_dim(
                jnp.zeros((4, width), jnp.float32), unit_sum.reshape(4, share), row * share, axis=1
            ),
        ]
    )
    sums = lax.psum(jnp.concatenate([by_token, by_unit]), ("dp", "row", "col"))
    pieces = share // n_dp
    inner = lax.axis_index("dp") * pieces
    col_sums = lax.dynamic_slice_in_dim(sums, lax.axis_index("col") * share + inner, pieces, axis=1)
    row_sums = lax.dynamic_slice_in_dim(sums, row * share + inner, pieces, axis=1)

    both = ("col", "dp")

    def to_owner(gradient):
        return lax.psum_scatter(gradient, both, scatter_dimension=0, tiled=True)

    got_heads = to_owner(grad_heads.astype(low)).reshape(pieces, 3, window)
    got_heads = jnp.where(owned, got_heads, jnp.zeros_like(got_heads))
    passed = lax.ppermute(got_heads[:, :, :edge], "row", to_last)
    got_heads = jnp.concatenate([got_heads, jnp.zeros_like(passed)], axis=2)
    got_heads = lax.dynamic_slice_in_dim(got_heads, edge - offset, share, axis=2)
    passed = jnp.concatenate([jnp.zeros((pieces, 3, share), low), passed, jnp.zeros_like(passed)], axis=2)
    got_heads = got_heads + lax.dynamic_slice_in_dim(passed, share - step + edge - offset, share, axis=2)
    low_out = jnp.where(owned[:, None], grad_out, 0.0).astype(low)
    passed = lax.ppermute(low_out[:edge], "row", to_last)
    low_out = jnp.concatenate([low_out, jnp.zeros_like(passed)])
    low_out = lax.dynamic_slice_in_dim(low_out, edge - offset, share)
    passed = jnp.concatenate([jnp.zeros((share, width), low), passed, jnp.zeros_like(passed)])
    low_out = low_out + lax.dynamic_slice_in_dim(passed, share - step + edge - offset, share)
    low_out = jnp.transpose(low_out.reshape(n_dp, pieces, n_col, share), (2, 0, 1, 3))
    got_out = to_owner(low_out.reshape(-1, share))
    got_up = to_owner(grad_up.astype(low))
    low_down = grad_down.astype(low).reshape(4, n_dp, pieces, n_col, share)
    low_down = jnp.transpose(low_down, (3, 1, 0, 2, 4)).reshape(-1, share)
    got_down = to_owner(low_down)

    reduced = [
        each.astype(jnp.float32).reshape(like.shape)
        for each, like in (
            (got_heads, w_heads),
            (got_out, w_out),
            (got_up, w_up),
            (got_down, w_down),
            (col_sums[0:2], norm_vectors),
            (col_sums[2:6], width_vectors),
            (row_sums[6:8], attend_bias),
            (row_sums[8:12], hidden_vectors),
        )
    ]
    return result_tokens, input_gradient, reduced


def per_device(
    tokens,
    cotangent,
    segments,
    w_heads,
    w_out,
    w_up,
    w_down,
    norm_vectors,
    width_vectors,
    attend_bias,
    hidden_vectors,
    drift_heads,
    drift_out,
    drift_up,
    drift_down,
    drift_norm,
    drift_width,
    drift_attend,
    drift_hidden,
    power_heads,
    power_out,
    power_up,
    power_down,
    power_norm,
    power_width,
    power_attend,
    power_hidden,
):
    weights = (
        w_heads,
        w_out,
        w_up,
        w_down,
        norm_vectors,
        width_vectors,
        attend_bias,
        hidden_vectors,
    )
    firsts = (
        drift_heads,
        drift_out,
        drift_up,
        drift_down,
        drift_norm,
        drift_width,
        drift_attend,
        drift_hidden,
    )
    seconds = (
        power_heads,
        power_out,
        power_up,
        power_down,
        power_norm,
        power_width,
        power_attend,
        power_hidden,
    )
    sizes = tuple(lax.axis_size(name) for name in ("dp", "row", "col"))
    if sizes == (2, 4, 4):
        return fused(tokens, cotangent, segments, weights, firsts, seconds)
    result_tokens, input_gradient, reduced = gathered(tokens, cotangent, segments, *weights)
    heads_up = adam_terms(w_heads, reduced[0], drift_heads, power_heads, 0.05, MATRIX_DECAY)
    out_up = adam_terms(w_out, reduced[1], drift_out, power_out, 0.2, MATRIX_DECAY)
    up_up = adam_terms(w_up, reduced[2], drift_up, power_up, 0.05, MATRIX_DECAY)
    down_up = adam_terms(w_down, reduced[3], drift_down, power_down, 0.025, MATRIX_DECAY)
    norm_up = adam_terms(norm_vectors, reduced[4], drift_norm, power_norm, 0.3, 0.0)
    width_up = adam_terms(width_vectors, reduced[5], drift_width, power_width, 0.3, 0.0)
    attend_up = adam_terms(attend_bias, reduced[6], drift_attend, power_attend, 0.3, 0.0)
    hidden_up = adam_terms(hidden_vectors, reduced[7], drift_hidden, power_hidden, 0.3, 0.0)
    return (
        result_tokens,
        input_gradient,
        heads_up[0],
        heads_up[1],
        heads_up[2],
        out_up[0],
        out_up[1],
        out_up[2],
        up_up[0],
        up_up[1],
        up_up[2],
        down_up[0],
        down_up[1],
        down_up[2],
        norm_up[0],
        norm_up[1],
        norm_up[2],
        width_up[0],
        width_up[1],
        width_up[2],
        attend_up[0],
        attend_up[1],
        attend_up[2],
        hidden_up[0],
        hidden_up[1],
        hidden_up[2],
    )


def solution(mesh):
    return jax.shard_map(
        per_device,
        mesh=mesh,
        in_specs=(
            P(("dp", "row"), "col"),
            P(("dp", "row"), "col"),
            P("dp"),
            P("col", "dp", None, None, "row"),
            P("row", "dp", None, "col"),
            P("col", "dp", None, None, "row"),
            P(None, "row", "dp", None, "col"),
            P(None, "col", "dp", None),
            P(None, "col", "dp", None),
            P(None, "row", "dp", None),
            P(None, "row", "dp", None),
            P("col", "dp", None, None, "row"),
            P("row", "dp", None, "col"),
            P("col", "dp", None, None, "row"),
            P(None, "row", "dp", None, "col"),
            P(None, "col", "dp", None),
            P(None, "col", "dp", None),
            P(None, "row", "dp", None),
            P(None, "row", "dp", None),
            P("col", "dp", None, None, "row"),
            P("row", "dp", None, "col"),
            P("col", "dp", None, None, "row"),
            P(None, "row", "dp", None, "col"),
            P(None, "col", "dp", None),
            P(None, "col", "dp", None),
            P(None, "row", "dp", None),
            P(None, "row", "dp", None),
        ),
        out_specs=(
            P(("dp", "row"), "col"),
            P(("dp", "row"), "col"),
            P("col", "dp", None, None, "row"),
            P("col", "dp", None, None, "row"),
            P("col", "dp", None, None, "row"),
            P("row", "dp", None, "col"),
            P("row", "dp", None, "col"),
            P("row", "dp", None, "col"),
            P("col", "dp", None, None, "row"),
            P("col", "dp", None, None, "row"),
            P("col", "dp", None, None, "row"),
            P(None, "row", "dp", None, "col"),
            P(None, "row", "dp", None, "col"),
            P(None, "row", "dp", None, "col"),
            P(None, "col", "dp", None),
            P(None, "col", "dp", None),
            P(None, "col", "dp", None),
            P(None, "col", "dp", None),
            P(None, "col", "dp", None),
            P(None, "col", "dp", None),
            P(None, "row", "dp", None),
            P(None, "row", "dp", None),
            P(None, "row", "dp", None),
            P(None, "row", "dp", None),
            P(None, "row", "dp", None),
            P(None, "row", "dp", None),
        ),
        check_vma=False,
    )
```

```python
import functools

import jax
import jax.numpy as jnp
from jax import lax
from jax.experimental import pallas as pl
from jax.experimental.pallas import tpu as pltpu
from jax.sharding import PartitionSpec as P

HEADS = 25
HD = 64
TOK_DEV = 128
STEP = 10


NORM_EPSILON = 1e-05
BETA_FIRST = 0.9
BETA_SECOND = 0.999
ADAM_EPSILON = 1e-08
MATRIX_DECAY = 0.1
MASKED = -1e30
ROOT = (2.0 / 3.141592653589793) ** 0.5
CUBIC = 0.044715
VMEM_BYTES = 66 * 1024 * 1024


def adam_terms(weight, gradient, first, second, rate, decay):
    first_new = BETA_FIRST * first + (1.0 - BETA_FIRST) * gradient
    second_new = BETA_SECOND * second + (1.0 - BETA_SECOND) * gradient * gradient
    corrected = first_new * (1.0 / (1.0 - BETA_FIRST**STEP))
    divisor = jnp.sqrt(second_new * (1.0 / (1.0 - BETA_SECOND**STEP))) + ADAM_EPSILON
    return (first_new, second_new, weight - rate * (corrected / divisor + decay * weight))


def smooth(values):
    return jax.nn.gelu(values, approximate=True)


def ceil_to(count, unit):
    return -(-count // unit) * unit


class Sizes:
    def __init__(self, share, pieces, seq):
        self.share = share
        self.pieces = pieces
        self.block = ceil_to(pieces, 16)
        self.pair = 2 * self.block
        self.width = 4 * self.pair
        self.seq = seq
        self.part = seq // 4
        self.both = 2 * seq
        self.main = (HEADS // 4) * HD
        self.slack = share - self.main
        self.heads = ceil_to(3 * share, 256)
        self.mixed = ceil_to(pieces + 1, 128)
        self.hidden = ceil_to(4 * pieces + 1, 128)
        self.tiles = self.width // 128


class Place:
    def __init__(self):
        self.d, self.r, self.c = (lax.axis_index(name) for name in ("dp", "row", "col"))
        self.y, self.k = self.r // 2, self.r % 2

    def plane(self, mask):
        d = 1 - self.d if mask & 4 else self.d
        y = 1 - self.y if mask & 2 else self.y
        k = 1 - self.k if mask & 1 else self.k
        return d, 2 * y + k

    def peer(self, mask):
        d, r = self.plane(mask)
        return (d, r, self.c)

    def along(self, c):
        return (self.d, self.r, c)


def run(when, action):
    if when is None:
        action()
    else:
        pl.when(when)(action)


class Wires:
    def __init__(self, sends, arrivals):
        self.sends, self.arrivals = sends, arrivals
        self.used = 0
        self.open = []

    def make(self, source, target, index, slot, device):
        return pltpu.make_async_remote_copy(
            src_ref=source,
            dst_ref=target,
            send_sem=self.sends.at[index],
            recv_sem=self.arrivals.at[slot],
            device_id=device,
            device_id_type=pl.DeviceIdType.MESH,
        )

    def copy(self, source, target, device, slot, when=None):
        made = self.make(source, target, self.used, slot, device)
        self.used += 1
        run(when, made.start)
        item = (when, made)
        self.open.append(item)
        return item

    def arrived(self, target, slot, device, when=None):
        run(when, self.make(target, target, 0, slot, device).wait_recv)

    def close(self, some=None):
        for item in self.open if some is None else some:
            run(item[0], item[1].wait_send)
        self.open = [] if some is None else [o for o in self.open if all(o is not s for s in some)]


def greet(at, diagonal):
    barrier = pltpu.get_barrier_semaphore()

    def signal(device):
        pl.semaphore_signal(
            barrier, inc=1, device_id=device, device_id_type=pl.DeviceIdType.MESH
        )

    for mask in range(1, 8):
        signal(at.peer(mask))
    for c in range(4):
        run(at.c != c, functools.partial(signal, (at.d, at.r, c)))
        if diagonal:
            run(at.c != c, functools.partial(signal, (1 - at.d, at.r, c)))
    run(at.r != at.c, functools.partial(signal, (at.d, at.c, at.r)))
    pl.semaphore_wait(barrier, (13 if diagonal else 10) + jnp.where(at.r != at.c, 1, 0))


def rows_at(start, size):
    return pl.ds(pl.multiple_of(start, 16), size)


def lanes_at(start, size):
    return pl.ds(pl.multiple_of(start, 128), size)


def choose(shape, source):
    rows = lax.broadcasted_iota(jnp.int32, shape, 0)
    wanted = source(lax.broadcasted_iota(jnp.int32, shape, 1))
    return (rows == wanted).astype(jnp.bfloat16)


def edge_source(column):
    part, place = column // HD, column % HD
    wanted = jnp.where(place >= 16, 128 * part + place - 16, 384 + 16 * part + place)
    return jnp.where(part < 3, wanted, -1)


def spread_source(column):
    part, place = column // 128, column % 128
    return jnp.where(place < HD, HD * part + place, -1)


def picked(values, table):
    return jnp.dot(values, table, preferred_element_type=jnp.float32).astype(jnp.bfloat16)


def times(left, right):
    return jnp.dot(left, right, preferred_element_type=jnp.float32)


def times_flipped(left, right):
    return lax.dot_general(
        left, right, (((1,), (1,)), ((), ())), preferred_element_type=jnp.float32
    )


def times_outer(left, right):
    return lax.dot_general(
        left, right, (((0,), (0,)), ((), ())), preferred_element_type=jnp.float32
    )


def over_tiles(total, action, tile=256):
    @pl.loop(0, total // tile)
    def _(i):
        action(i * tile, tile)

    if total % tile:
        action(total - total % tile, total % tile)


def turned(values):
    return values.astype(jnp.float32).T


def gather_group(wires, masks, region, at, base):
    own = region(*at.plane(0))
    sent = [wires.copy(own, own, at.peer(mask), base + mask) for mask in (1, *masks)]

    def finish():
        for mask in masks:
            there = region(*at.plane(mask))
            wires.arrived(there, base + mask, at.peer(mask))
            sent.append(wires.copy(there, there, at.peer(1), base + mask + 1))
        for mask in (0, *masks):
            there = region(*at.plane(mask | 1))
            wires.arrived(there, base + (mask | 1), at.peer(1))

    return finish, sent


def cross_over(wires, home, landing, region, at, base):
    rows = home.shape[0] // 2
    wires.copy(home.at[rows_at(rows * (1 - at.y), rows)], landing, at.peer(2), base)
    target = region(at.c, at.d, at.y)

    def along(source, s):
        wires.copy(source, target, at.along(s), base + 1 + at.c, s != at.c)

        @pl.when(s == at.c)
        def _():
            target[...] = source[...]

    along(home.at[rows_at(rows * at.y, rows)], at.r)

    def onward():
        wires.arrived(landing, base, at.peer(2))
        along(landing, 2 * (1 - at.y) + at.k)

    def finish():
        for c in range(4):
            needed = (at.k == at.c % 2) & (at.c != c)
            wires.arrived(region(c, at.d, at.y), base + 1 + c, at.along(c), needed)

    return onward, finish


def share_pieces(wires, masks, region, at, base):
    holds = at.k == at.c % 2
    near = base + 4 * len(masks)

    def place(mask):
        d, r = at.plane(mask)
        return d, r // 2

    for c in range(4):
        own = region(c, *place(0))
        for i, mask in enumerate(masks):
            wires.copy(own, own, at.peer(mask), base + 4 * i + c, holds)
    for c in range(4):
        own = region(c, *place(0))
        wires.copy(own, own, at.peer(1), near + c, holds)

    def finish():
        for i, mask in enumerate(masks):
            for c in range(4):
                there = region(c, *place(mask))
                wires.arrived(there, base + 4 * i + c, at.peer(mask), holds)
                wires.copy(there, there, at.peer(1), near + 4 * (i + 1) + c, holds)
        for i, mask in enumerate((0, *masks)):
            for c in range(4):
                there = region(c, *place(mask))
                wires.arrived(there, near + 4 * i + c, at.peer(1), jnp.logical_not(holds))

    return finish


def scatter_group(wires, masks, partial, chunk, near, mid, far, at, base):
    sent = []
    for i, mask in enumerate((0, *masks)):
        rows = rows_at(chunk(*at.plane(mask | 1)), near.shape[1])
        sent.append(wires.copy(partial.at[rows], near.at[i], at.peer(1), base + i))

    def rows_of(mask):
        return rows_at(chunk(*at.plane(mask)), near.shape[1])

    def onward():
        for i, mask in enumerate((0, *masks)):
            wires.arrived(near.at[i], base + i, at.peer(1))
        for i, mask in enumerate(masks):
            both = partial[rows_of(mask)].astype(jnp.float32) + near[i + 1].astype(jnp.float32)
            mid[i] = both.astype(jnp.bfloat16)
            sent.append(wires.copy(mid.at[i], far.at[i], at.peer(mask), base + 4 + i))

    def total():
        for i, mask in enumerate(masks):
            wires.arrived(far.at[i], base + 4 + i, at.peer(mask))
        result = partial[rows_of(0)].astype(jnp.float32) + near[0].astype(jnp.float32)
        for i in range(len(masks)):
            result = result + far[i].astype(jnp.float32)
        return result

    return onward, total, sent


def spread_col(wires, region, at, base, source=None):
    own = region(at.c)
    source = own if source is None else source
    for delta in (2, -2, 1, -1):
        there = at.c + delta
        wires.copy(source, own, at.along(there), base + at.c, (there >= 0) & (there < 4))

    def relay():
        for here, start, end in ((2, 0, 3), (1, 3, 0)):
            block = region(start)
            wires.arrived(block, base + start, at.along(start), at.c == here)
            wires.copy(block, block, at.along(end), base + start, at.c == here)

    def finish():
        for c in range(4):
            needed = at.c != c
            if c == 0:
                needed = needed & (at.c != 2)
            if c == 3:
                needed = needed & (at.c != 1)
            wires.arrived(region(c), base + c, at.along(c), needed)

    return relay, finish


def collect_col(wires, piece, landing, rest, at, base):
    low_end, high_end = at.c == 0, at.c == 3
    ends = low_end | high_end
    via = jnp.where(low_end, 1, 2)

    def pick(*choices):
        return jnp.where(
            low_end,
            choices[0],
            jnp.where(at.c == 1, choices[1], jnp.where(high_end, choices[3], choices[2])),
        )

    order = (pick(3, 0, 3, 0), pick(2, 2, 1, 1), pick(1, 3, 0, 2), at.c)
    target = landing.at[at.c]

    def send(step):
        there = order[step]
        block = piece(there)
        if step == 0:
            wires.copy(block, rest, at.along(via), base + 4, ends)
            wires.copy(block, target, at.along(there), base + at.c, jnp.logical_not(ends))
        elif step == 1:
            wires.copy(block, target, at.along(there), base + at.c)
        elif step == 2:
            wires.copy(block, target, at.along(there), base + at.c, ends)

    def relay(add):
        @pl.when(jnp.logical_not(ends))
        def _():
            wires.make(rest, rest, 0, base + 4, at.along(0)).wait_recv()
            add(order[2])

        wires.copy(piece(order[2]), target, at.along(order[2]), base + at.c, jnp.logical_not(ends))

    def arrived(c):
        wires.arrived(landing.at[c], base + c, at.along(c), sent_from(c))

    def sent_from(c):
        here = at.c != c
        if c in (0, 3):
            here = here & (at.c != 3 - c)
        return here

    return order, send, relay, arrived, sent_from


def forward_kernel(
    sz,
    x_home_in,
    dy_home_in,
    w_heads,
    w_out,
    w_up,
    w_down,
    norm_vectors,
    width_vectors,
    attend_bias,
    hidden_vectors,
    segments,
    wh_out,
    wo_out,
    wu_out,
    wd_out,
    h1_t_out,
    h2_t_out,
    dy_t_out,
    dy_out,
    u_out,
    gl_out,
    qw_out,
    kw_out,
    vw_out,
    a_nat_out,
    lse_out,
    x2_out,
    x_own_out,
    vec_rows_out,
    wh,
    wo,
    wu,
    wd,
    h1_t,
    h2_t,
    dy_t,
    dy,
    u,
    gl,
    qw,
    kw,
    vw,
    a_nat,
    lse,
    x2,
    x_own,
    vec_rows,
    x_t,
    h1,
    h2,
    own_qkv,
    aw,
    vec,
    part,
    edge_out,
    edge_in,
    edge_back,
    near,
    mid,
    far,
    x_raw,
    dy_raw,
    heads_raw,
    out_raw,
    up_raw,
    down_raw,
    x_home,
    dy_home,
    wu_own,
    col_labels,
    x_half,
    dy_half,
    sends,
    arrivals,
    locals_,
):
    at = Place()
    wires = Wires(sends, arrivals)
    low = jnp.bfloat16
    pair, block, pieces = sz.pair, sz.block, sz.pieces
    fetched = []
    for i, (source, target) in enumerate(
        (
            (x_home_in, x_raw),
            (w_heads, heads_raw),
            (w_up, up_raw),
            (w_out, out_raw),
            (w_down, down_raw),
            (dy_home_in, dy_raw),
        )
    ):
        fetched.append(pltpu.make_async_copy(source, target, locals_.at[40 + i]))
        fetched[i].start()
    row_labels = segments.at[:, lanes_at(sz.seq * at.c, sz.seq)]

    def halves(value, target):
        value = value.astype(jnp.float32)
        gap = jnp.zeros((block - pieces, value.shape[1]), jnp.float32)
        parts = [value[0:pieces], gap, value[pieces : 2 * pieces], gap]
        target[...] = jnp.concatenate(parts, axis=0).astype(low)

    def quarter(row):
        return row.astype(low).astype(jnp.float32) * 0.25

    def placed(row):
        both = jnp.concatenate([row, row], axis=1)
        half_of = lax.broadcasted_iota(jnp.int32, both.shape, 1) // pieces
        return jnp.where(half_of == at.d, both, 0.0)

    def with_row(value, row):
        gap = jnp.zeros((block - pieces - 1, value.shape[1]), jnp.float32)
        return jnp.concatenate([value, row, gap], axis=0)

    flat = jnp.concatenate(
        [norm_vectors[0], norm_vectors[1], width_vectors[1], width_vectors[2]], axis=0
    )
    flat = jnp.concatenate([flat, jnp.zeros((124, pieces), jnp.float32)], axis=0)
    flat = jnp.concatenate([flat, jnp.zeros((128, 256 - pieces), jnp.float32)], axis=1)
    where_row = lax.broadcasted_iota(jnp.int32, flat.shape, 0)
    where_lane = lax.broadcasted_iota(jnp.int32, flat.shape, 1)
    carrier = (where_lane == pieces) & ((where_row == 1) | (where_row == 3))
    own_rows = rows_at(pair * at.c + block * at.d, block)
    vec[own_rows] = jnp.where(carrier, 1.0, flat).T[0:block].astype(low)
    fetched[0].wait()
    halves(x_raw[...], x_home)
    greet(at, False)

    def x_piece(c, d, y):
        return x_t.at[rows_at(pair * c + block * y, block)]

    def dy_piece(c, d, y):
        return dy_t.at[rows_at(pair * c + block * y, block), lanes_at(sz.seq * d, sz.seq)]

    used = [0]

    def flush(source, target):
        made = pltpu.make_async_copy(source, target, locals_.at[used[0]])
        used[0] += 1
        made.start()
        flushed.append(made)

    flushed = []

    def vec_block(d, c):
        return vec.at[rows_at(pair * c + block * d, block)]

    def wh_block(d):
        return lambda c: wh.at[rows_at(pair * c + block * d, block)]

    def wo_block(d):
        return lambda c: wo.at[rows_at(pair * c, pair), lanes_at(sz.mixed * d, sz.mixed)]

    def wu_block(d):
        return lambda c: wu.at[rows_at(pair * c + block * d, block)]

    def wd_block(half):
        return lambda c: wd.at[rows_at(pair * c + block * half, block)]

    x_onward, x_crossed = cross_over(wires, x_home, x_half, x_piece, at, 96)
    for c in range(4):
        wires.copy(vec_block(at.d, at.c), vec_block(at.d, at.c), at.along(c), 2 + at.c, at.c != c)
    wires.copy(vec_block(at.d, at.c), vec_block(at.d, at.c), at.peer(4), 6 + at.c)

    fetched[1].wait()
    for r in range(4):

        @pl.when(at.r == r)
        def _():
            cut = sz.share - sz.slack * r
            tails = []
            for i in range(3):
                value = heads_raw[i]
                row = jnp.zeros((1, sz.share), jnp.float32)
                if i != 1:
                    row = placed(quarter(attend_bias[i // 2]))
                value = with_row(value, row)
                if r:
                    value = jnp.concatenate([value[:, cut:], value[:, 0:cut]], axis=1)
                wh[own_rows, sz.main * i : sz.main * (i + 1)] = value[:, 0 : sz.main].astype(low)
                tails.append(value[:, sz.main :])
            tails.append(jnp.zeros((block, sz.heads - 3 * sz.share), jnp.float32))
            wh[own_rows, 3 * sz.main : sz.heads] = jnp.concatenate(tails, axis=1).astype(low)

    x_onward()
    wh_relay, wh_done = spread_col(wires, wh_block(at.d), at, 20)
    wires.copy(wh_block(at.d)(at.c), wh_block(at.d)(at.c), at.peer(4), 24 + at.c)

    fetched[2].wait()
    gap = jnp.zeros((block, sz.hidden - 4 * pieces), jnp.float32)
    values = [
        with_row(up_raw[:, j, :], placed(quarter(hidden_vectors[j]))) for j in range(4)
    ]
    for i in range(2):
        lanes = slice(pieces * i, pieces * (i + 1))
        whole = jnp.concatenate([value[:, lanes] for value in values] + [gap], axis=1)

        @pl.when(at.d == i)
        def _():
            wu[own_rows] = whole.astype(low)

        @pl.when(at.d != i)
        def _():
            wu_own[...] = whole.astype(low)

    wires.copy(wu_own, wu_block(at.d)(at.c), at.peer(4), 10)

    def turned_halves(value, target, lanes):
        flipped = value.T
        gap = jnp.zeros((block - pieces, flipped.shape[1]), jnp.float32)
        parts = [flipped[0:pieces], gap, flipped[pieces : 2 * pieces], gap]
        target[rows_at(pair * at.c, pair), lanes] = jnp.concatenate(parts, axis=0).astype(low)

    fetched[3].wait()
    value = with_row(out_raw[...], placed(quarter(width_vectors[0])))
    value = jnp.concatenate([value, jnp.zeros((sz.mixed - block, sz.share), jnp.float32)], axis=0)
    for i in range(sz.mixed // 128):
        lanes = slice(128 * i, 128 * (i + 1))
        turned_halves(value[lanes], wo, lanes_at(sz.mixed * at.d + 128 * i, 128))
    wo_relay, wo_done = spread_col(wires, wo_block(at.d), at, 28)
    wires.copy(wo_block(at.d)(at.c), wo_block(at.d)(at.c), at.peer(4), 32 + at.c)

    x_crossed()
    x_done = share_pieces(wires, (2,), x_piece, at, 104)

    fetched[4].wait()
    for i in range(sz.hidden // 128):
        rows = slice(128 * i, 128 * (i + 1))
        if 128 * (i + 1) <= 4 * pieces:
            value = down_raw[rows]
        else:
            value = jnp.concatenate(
                [
                    down_raw[128 * i : 4 * pieces],
                    placed(quarter(width_vectors[3])),
                    jnp.zeros((sz.hidden - 4 * pieces - 1, sz.share), jnp.float32),
                ],
                axis=0,
            )
        turned_halves(value, wd, rows)
    fetched[5].wait()
    halves(dy_raw[...], dy_home)
    col_labels[...] = jnp.concatenate([row_labels[...]] * 8, axis=0).astype(jnp.float32).T[:, 0:1]
    x_done()
    wu_first, wu_first_done = spread_col(wires, wu_block(at.d), at, 36)

    for c in range(4):
        wires.arrived(vec_block(at.d, c), 2 + c, at.along(c), at.c != c)
    wires.arrived(vec_block(1 - at.d, at.c), 6 + at.c, at.peer(4))
    for step in range(1, 4):
        there = (at.c + step) % 4
        wires.copy(
            vec_block(at.d, there), vec_block(at.d, there), at.peer(4), 6 + there
        )
    for step in range(1, 4):
        there = (at.c + step) % 4
        wires.arrived(vec_block(1 - at.d, there), 6 + there, at.peer(4))
    features = 4.0 * sz.share

    def add_up(i, carry):
        rows = rows_at(128 * i, 128)
        value = x_t[rows].astype(jnp.float32)
        return (
            carry[0] + jnp.sum(value, axis=0, keepdims=True),
            carry[1] + jnp.sum(value * value, axis=0, keepdims=True),
        )

    zero = jnp.zeros((1, sz.seq), jnp.float32)
    sums = lax.fori_loop(0, sz.tiles, add_up, (zero, zero))
    center = sums[0] / features
    inverse = lax.rsqrt(sums[1] / features - center * center + NORM_EPSILON)

    @pl.loop(0, sz.tiles)
    def _(i):
        rows, lanes = rows_at(128 * i, 128), lanes_at(128 * i, 128)
        vectors = vec[rows].astype(jnp.float32)
        value = (x_t[rows].astype(jnp.float32) - center) * inverse
        value = value * vectors[:, 0:1] + vectors[:, 1:2]
        h1_t[rows] = value.astype(low)
        h1[:, lanes] = value.T.astype(low)
        mine = x_t[rows, lanes_at(sz.part * at.r, sz.part)]
        x_own[:, lanes] = turned(mine).astype(low)
        vec_rows[:, lanes] = vectors.T[0:8]

    flush(h1_t, h1_t_out)
    flush(x_own, x_own_out)
    flush(vec_rows, vec_rows_out)

    wh_relay()
    for c in range(4):
        needed = at.c != c
        if c == 0:
            needed = needed & (at.c != 2)
        if c == 3:
            needed = needed & (at.c != 1)
        wires.arrived(wh_block(at.d)(c), 20 + c, at.along(c), needed)
        wires.copy(wh_block(at.d)(c), wh_block(at.d)(c), at.peer(4), 24 + c, at.c != c)

    wires.arrived(wu_block(1 - at.d)(at.c), 10, at.peer(4))
    wu_second, wu_second_done = spread_col(wires, wu_block(1 - at.d), at, 40)
    for c in range(4):
        wires.arrived(wh_block(1 - at.d)(c), 24 + c, at.peer(4))
    flush(wh, wh_out)

    @pl.loop(0, sz.heads // 256)
    def _(i):
        lanes = lanes_at(256 * i, 256)
        own_qkv[:, lanes] = times(h1[...], wh[:, lanes]).astype(low)

    dy_onward, dy_crossed = cross_over(wires, dy_home, dy_half, dy_piece, at, 116)

    starts = (0, sz.main, 2 * sz.main, 3 * sz.main)
    ends = jnp.concatenate([own_qkv[:, s : s + 128] for s in starts], axis=1)
    edge_out[...] = picked(ends, choose((512, 256), edge_source))
    last = at.r == 3

    @pl.when(at.r == 0)
    def _():
        edge_in[...] = jnp.zeros_like(edge_in)

    wires.copy(edge_out, edge_in, (at.d, at.r + 1, at.c), 52, at.r < 3)
    spread = choose((256, 384), spread_source)
    extra = picked(edge_out[...], spread)
    wires.arrived(edge_in, 52, (at.d, at.r - 1, at.c), at.r > 0)
    first = picked(edge_in[...], spread)
    lane = lax.broadcasted_iota(jnp.int32, (sz.seq, 128), 1)
    for i, target in enumerate((qw, kw, vw)):
        start = starts[i]
        target[:, 0:128] = jnp.where(
            lane < sz.slack * at.r,
            first[:, 128 * i : 128 * i + 128],
            own_qkv[:, start : start + 128],
        )
        target[:, 128 : sz.main] = own_qkv[:, start + 128 : start + sz.main]
        target[:, sz.main : sz.main + 128] = extra[:, 128 * i : 128 * i + 128]
    flush(qw, qw_out)
    flush(kw, kw_out)
    flush(vw, vw_out)

    dy_onward()
    wo_relay()
    for c in range(4):
        needed = at.c != c
        if c == 0:
            needed = needed & (at.c != 2)
        if c == 3:
            needed = needed & (at.c != 1)
        wires.arrived(wo_block(at.d)(c), 28 + c, at.along(c), needed)
        wires.copy(wo_block(at.d)(c), wo_block(at.d)(c), at.peer(4), 32 + c, at.c != c)

    half = sz.seq // 2

    def heads_of(p, count):
        tile = lanes_at(128 * p, 128)
        for q in range(2):
            rows = slice(half * q, half * (q + 1))
            keys = half * (q + 1)
            order = lax.broadcasted_iota(jnp.int32, (half, keys), 0) + half * q
            allowed = (col_labels[rows, :] == row_labels[:, 0:keys].astype(jnp.float32)) & (
                order >= lax.broadcasted_iota(jnp.int32, (half, keys), 1)
            )
            lanes = lax.broadcasted_iota(jnp.int32, (half, 128), 1)
            side = lanes // HD
            total = jnp.zeros((half, 128), jnp.float32)
            for h in range(count):
                queries = jnp.where(side == h, qw[rows, tile].astype(jnp.float32) * HD ** (-0.5), 0.0)
                scores = times_flipped(queries.astype(low), kw[0:keys, tile])
                scores = jnp.where(allowed, scores, MASKED)
                highest = jnp.max(scores, axis=1, keepdims=True)
                raised = jnp.exp(scores - highest)
                summed = jnp.sum(raised, axis=1, keepdims=True)
                found = highest + jnp.log(summed)
                lse[rows, :] = jnp.where(lanes == 2 * p + h, found, lse[rows, :])
                soft = (raised * (1.0 / summed)).astype(low)
                total = jnp.where(side == h, times(soft, vw[0:keys, tile]), total)
            aw[rows, tile] = total.astype(low)

    lse[...] = jnp.zeros_like(lse)

    @pl.loop(0, sz.main // 128)
    def _(p):
        heads_of(p, 2)

    @pl.when(last)
    def _():
        heads_of(sz.main // 128, 1)
        edge_back[...] = aw[:, sz.main : sz.main + 128]

    flush(lse, lse_out)

    wires.copy(aw.at[:, 0:128], edge_back, (at.d, at.r - 1, at.c), 53, at.r > 0)
    wd_first, wd_first_done = spread_col(wires, wd_block(0), at, 44)
    wd_second, wd_second_done = spread_col(wires, wd_block(1), at, 48)
    wu_first()
    wires.arrived(edge_back, 53, (at.d, at.r + 1, at.c), at.r < 3)

    def natural(column):
        inner = column % sz.mixed
        place = sz.pieces * (column // sz.mixed) + inner + sz.slack * at.r
        return jnp.where(inner < sz.pieces, place, -1)

    def natural_main(column):
        place = natural(column)
        return jnp.where(place < sz.main, place, -1)

    def natural_edge(column):
        return natural(column) - sz.main

    mixed = times(aw[:, 0 : sz.main], choose((sz.main, 2 * sz.mixed), natural_main))
    mixed = mixed + times(edge_back[...], choose((128, 2 * sz.mixed), natural_edge))
    ones = lax.broadcasted_iota(jnp.int32, mixed.shape, 1) % sz.mixed == sz.pieces
    a_nat[...] = jnp.where(ones, 1.0, mixed).astype(low)
    for c in range(4):
        wires.arrived(wo_block(1 - at.d)(c), 32 + c, at.peer(4))
    flush(wo, wo_out)
    flush(a_nat, a_nat_out)

    def project(start, tile):
        out = times_flipped(a_nat[...], wo[rows_at(start, tile)])
        part[:, lanes_at(start, tile)] = out.astype(low)

    over_tiles(sz.width, project)

    onward, total, _ = scatter_group(
        wires, (2,), part, lambda d, r: sz.part * r, near, mid, far, at, 64
    )
    onward()
    middle = x_own[...].astype(jnp.float32) + total()
    x2[...] = middle
    flush(x2, x2_out)
    center = jnp.sum(middle, axis=1, keepdims=True) / features
    spread_two = jnp.sum(middle * middle, axis=1, keepdims=True) / features - center * center
    normed = (middle - center) * lax.rsqrt(spread_two + NORM_EPSILON)
    own_rows = rows_at(sz.part * (4 * at.d + at.r), sz.part)
    h2[own_rows] = (normed * vec_rows[2:3] + vec_rows[3:4]).astype(low)
    h2_done, _ = gather_group(
        wires, (2, 4, 6), lambda d, r: h2.at[rows_at(sz.part * (4 * d + r), sz.part)], at, 72
    )
    wu_second()
    h2_done()
    wu_first_done()
    wu_second_done()
    flush(wu, wu_out)

    def expand(start, tile):
        lanes = lanes_at(start, tile)
        value = times(h2[...], wu[:, lanes])
        u[:, lanes] = value
        inner = jnp.tanh(ROOT * (value + CUBIC * value * value * value))
        value = 0.5 * value * (1.0 + inner)
        column = lax.broadcasted_iota(jnp.int32, value.shape, 1) + start
        gl[:, lanes] = jnp.where(column == 4 * sz.pieces, 1.0, value).astype(low)

    over_tiles(sz.hidden, expand)

    dy_crossed()
    dy_done = share_pieces(wires, (2, 4, 6), dy_piece, at, 124)
    flush(u, u_out)
    flush(gl, gl_out)
    wd_first()

    @pl.loop(0, sz.tiles)
    def _(i):
        h2_t[rows_at(128 * i, 128)] = turned(h2[:, lanes_at(128 * i, 128)]).astype(low)

    flush(h2_t, h2_t_out)
    wd_second()
    dy_done()
    flush(dy_t, dy_t_out)

    @pl.loop(0, sz.tiles)
    def _(i):
        dy[:, lanes_at(128 * i, 128)] = turned(dy_t[rows_at(128 * i, 128)]).astype(low)

    flush(dy, dy_out)
    wd_first_done()
    wd_second_done()
    flush(wd, wd_out)
    wires.close()
    for made in flushed:
        made.wait()


def backward_kernel(
    sz,
    dy_all,
    dy_t_all,
    u_all,
    gl_all,
    h2_t_all,
    wd_all,
    wu_all,
    wo_all,
    wh_all,
    h1_t_all,
    qw_all,
    kw_all,
    vw_all,
    a_nat_all,
    lse_all,
    x2_all,
    x_own_all,
    vec_rows,
    segments,
    out_down,
    out_up,
    out_out,
    out_heads,
    result_home,
    grad_home,
    vec_out,
    zd,
    zu,
    zo,
    zh,
    res_all,
    res_two,
    grad_all,
    grad_two,
    rd,
    ru,
    ro,
    rh,
    qw,
    kw,
    vw,
    a_nat,
    lse,
    x2,
    x_own,
    xu,
    dy,
    dy_t,
    u,
    gl,
    h2_t,
    wd,
    wu,
    wo,
    wh,
    dy_own,
    du,
    gw,
    gu,
    go,
    xh,
    xo,
    near_two,
    far_two,
    near_res,
    far_res,
    near_one,
    far_one,
    mid,
    dob,
    da,
    dk_sum,
    dv_sum,
    dx2,
    edge_out,
    edge_in,
    fore_out,
    fore_in,
    col_labels,
    res_stage,
    grad_stage,
    va,
    vb,
    sends,
    arrivals,
    locals_,
):
    at = Place()
    wires = Wires(sends, arrivals)
    low = jnp.bfloat16
    pair, block = sz.pair, sz.block
    features = 4.0 * sz.share
    used = [0]

    def load(source, target, when=None):
        made = pltpu.make_async_copy(source, target, locals_.at[used[0]])
        used[0] += 1
        run(when, made.start)
        return made

    own_rows = rows_at(sz.part * (4 * at.d + at.r), sz.part)
    loads = [
        load(s, t)
        for s, t in (
            (dy_t_all, dy_t),
            (gl_all, gl),
            (dy_all, dy),
            (wd_all, wd),
            (u_all, u),
            (dy_all.at[own_rows], dy_own),
            (wu_all, wu),
            (h2_t_all, h2_t),
            (wo_all, wo),
            (wh_all, wh),
            (x2_all, x2),
            (a_nat_all, a_nat),
            (qw_all, qw),
            (kw_all, kw),
            (vw_all, vw),
            (lse_all, lse),
            (x_own_all, x_own),
        )
    ]
    greet(at, False)
    stay = []

    gd = gw.at[:, 0 : sz.hidden]
    loads[0].wait()
    loads[1].wait()
    order, d_send, d_relay, d_arrived, d_from = collect_col(
        wires, lambda c: gd.at[rows_at(pair * c, pair)], zd, rd, at, 0
    )
    for step in range(4):
        rows = rows_at(pair * order[step], pair)
        gw[rows, 0 : sz.hidden] = times(dy_t[rows], gl[...]).astype(low)
        d_send(step)

    def relay_of(rest, block):
        def add(there):
            rows = rows_at(pair * there, pair)
            block[rows] = (block[rows].astype(jnp.float32) + rest[...].astype(jnp.float32)).astype(low)

        return add

    gd_sends = list(wires.open)

    for made in loads[2:6]:
        made.wait()

    def through(start, tile):
        lanes = lanes_at(start, tile)
        upstream = times(dy[...], wd[:, lanes])
        value = u[:, lanes]
        inner = jnp.tanh(ROOT * (value + CUBIC * value * value * value))
        slope = 0.5 * (1.0 + inner) + 0.5 * value * (1.0 - inner * inner) * ROOT * (
            1.0 + 3.0 * CUBIC * value * value
        )
        du[:, lanes] = (upstream * slope).astype(low)

    over_tiles(sz.hidden, through)
    loads[6].wait()

    def back_up(start, tile):
        dy[:, lanes_at(start, tile)] = times_flipped(du[...], wu[rows_at(start, tile)]).astype(low)

    over_tiles(sz.width, back_up)

    def chunk_both(d, r):
        return sz.part * (4 * d + r)

    two_onward, two_total, two_sent = scatter_group(
        wires, (2, 4, 6), dy, chunk_both, near_two, mid, far_two, at, 16
    )
    loads[7].wait()
    order, u_send, u_relay, u_arrived, u_from = collect_col(
        wires, lambda c: gu.at[rows_at(pair * c, pair)], zu, ru, at, 5
    )
    for step in range(4):
        rows = rows_at(pair * order[step], pair)
        gu[rows] = times(h2_t[rows], du[...]).astype(low)
        u_send(step)
        if step == 1:
            two_onward()
    own = rows_at(pair * at.c, pair)
    own_slot = h2_t.at[own, 0 : sz.hidden]
    gd_own = load(gd.at[own], own_slot)
    before = len(wires.open)
    d_relay(relay_of(rd, gd))
    gd_sends += wires.open[before:]

    def norm_back(upstream, values, gain):
        center = jnp.sum(values, axis=1, keepdims=True) / features
        spread = jnp.sum(values * values, axis=1, keepdims=True) / features - center * center
        inverse = lax.rsqrt(spread + NORM_EPSILON)
        centered = (values - center) * inverse
        scaled = upstream * gain
        inner = (
            scaled
            - jnp.sum(scaled, axis=1, keepdims=True) / features
            - centered * (jnp.sum(scaled * centered, axis=1, keepdims=True) / features)
        )
        return (
            inner * inverse,
            jnp.sum(upstream * centered, axis=0, keepdims=True),
            jnp.sum(upstream, axis=0, keepdims=True),
        )

    loads[10].wait()
    h2_back = two_total()
    through_norm, gain_two, shift_two = norm_back(h2_back, x2[...], vec_rows[2:3])
    middle_back = dy_own[...].astype(jnp.float32) + through_norm
    dx2[...] = middle_back
    va[0, 2:3] = gain_two
    va[0, 3:4] = shift_two
    va[0, 4:8] = jnp.zeros((4, sz.width), jnp.float32)
    dob[rows_at(sz.part * at.r, sz.part)] = middle_back.astype(low)
    dob_done, dob_sent = gather_group(
        wires, (2,), lambda d, r: dob.at[rows_at(sz.part * r, sz.part)], at, 24
    )
    h1_load = load(h1_t_all, dy_t.at[:, 0 : sz.seq])

    def contract(start, tile):
        out = times_flipped(gl[...], wd[rows_at(start, tile)])
        dy[:, lanes_at(start, tile)] = out.astype(low)

    wires.close(two_sent)
    over_tiles(sz.width, contract)
    res_onward, res_total, res_sent = scatter_group(
        wires, (2, 4, 6), dy, chunk_both, near_res, mid, far_res, at, 32
    )

    dob_done()
    loads[11].wait()
    loads[8].wait()
    da[...] = times(dob[...], wo[...]).astype(low)
    slack, main = sz.slack, sz.main

    def from_natural(place):
        wanted = sz.mixed * (place // sz.pieces) + place % sz.pieces
        return jnp.where((place >= 0) & (place < sz.share), wanted, -1)

    fore_out[...] = picked(
        da[...], choose((2 * sz.mixed, 128), lambda j: from_natural(j + main - slack * at.r))
    )

    @pl.when(at.r == 0)
    def _():
        fore_in[...] = jnp.zeros_like(fore_in)

    wires.copy(fore_out, fore_in, (at.d, at.r + 1, at.c), 40, at.r < 3)

    @pl.loop(0, sz.tiles)
    def _(i):
        dy_t[rows_at(128 * i, 128), sz.seq : sz.both] = turned(dob[:, lanes_at(128 * i, 128)]).astype(low)

    res_onward()

    for step in range(4):
        there = (at.c + step) % 4
        rows = rows_at(pair * there, pair)
        go[rows] = times(dy_t[rows, sz.seq : sz.both], a_nat[...]).astype(low)
        wires.copy(
            go.at[rows, lanes_at(sz.mixed * (1 - at.d), sz.mixed)], xo.at[there], at.peer(4), 48 + there
        )
    wires.arrived(fore_in, 40, (at.d, at.r - 1, at.c), at.r > 0)
    window = times(da[...], choose((2 * sz.mixed, main), lambda j: from_natural(j - slack * at.r)))
    da_first = window[:, 0:128] + fore_in[...].astype(jnp.float32)
    da[:, 128:main] = window[:, 128:main].astype(low)
    da[:, 0:128] = da_first.astype(low)
    da[:, main : main + 128] = fore_out[...]

    row_labels = segments.at[:, lanes_at(sz.seq * at.c, sz.seq)]
    col_labels[...] = jnp.concatenate([row_labels[...]] * 8, axis=0).astype(jnp.float32).T[:, 0:1]
    for made in loads[12:17]:
        made.wait()
    half = sz.seq // 2
    dqw, dkw = (du.at[sz.seq * i : sz.seq * (i + 1), 0 : main + 128] for i in range(2))
    dvw = gl.at[0 : sz.seq, 0 : main + 128]

    def heads_back(p, count):
        tile = lanes_at(128 * p, 128)
        dk_sum[...] = jnp.zeros_like(dk_sum)
        dv_sum[...] = jnp.zeros_like(dv_sum)
        for q in range(2):
            rows = slice(half * q, half * (q + 1))
            keys = half * (q + 1)
            order = lax.broadcasted_iota(jnp.int32, (half, keys), 0) + half * q
            allowed = (col_labels[rows, :] == row_labels[:, 0:keys].astype(jnp.float32)) & (
                order >= lax.broadcasted_iota(jnp.int32, (half, keys), 1)
            )
            lanes = lax.broadcasted_iota(jnp.int32, (half, 128), 1)
            side = lanes // HD
            total = jnp.zeros((half, 128), jnp.float32)
            for h in range(count):
                queries = jnp.where(side == h, qw[rows, tile].astype(jnp.float32) * HD ** (-0.5), 0.0)
                queries = queries.astype(low)
                pulled = jnp.where(side == h, da[rows, tile].astype(jnp.float32), 0.0).astype(low)
                found = jnp.sum(jnp.where(lanes == 2 * p + h, lse[rows, :], 0.0), axis=1, keepdims=True)
                scores = times_flipped(queries, kw[0:keys, tile])
                soft = jnp.where(allowed, jnp.exp(jnp.where(allowed, scores - found, MASKED)), 0.0)
                soft_back = times_flipped(pulled, vw[0:keys, tile])
                inner = jnp.sum(soft_back * soft, axis=1, keepdims=True)
                score_back = (soft * (soft_back - inner)).astype(low)
                piece = times(score_back, kw[0:keys, tile]) * HD ** (-0.5)
                total = jnp.where(side == h, piece, total)
                dk_sum[0:keys] += times_outer(score_back, queries)
                dv_sum[0:keys] += times_outer(soft.astype(low), pulled)
            dqw[rows, tile] = total.astype(low)
        dkw[:, tile] = dk_sum[...].astype(low)
        dvw[:, tile] = dv_sum[...].astype(low)

    @pl.loop(0, main // 128)
    def _(p):
        heads_back(p, 2)

    @pl.when(at.r == 3)
    def _():
        heads_back(main // 128, 1)

    def compact(column):
        part, place = column // HD, column % HD
        return jnp.where(part < 3, 128 * part + place, -1)

    table = choose((384, 256), compact)
    backs = (dqw, dkw, dvw)
    edge_out[...] = picked(jnp.concatenate([b[:, 0:128] for b in backs], axis=1), table)
    wires.copy(edge_out, edge_in, (at.d, at.r - 1, at.c), 41, at.r > 0)

    @pl.when(at.r == 3)
    def _():
        edge_in[...] = picked(jnp.concatenate([b[:, main : main + 128] for b in backs], axis=1), table)

    def go_home(values, stage, every, halves, out, base):
        flipped = values.T
        for c in range(4):
            for y in range(2):
                rows = slice(pair * c + block * y, pair * c + block * (y + 1))
                stage[c, y] = flipped[rows].astype(low)
        holds = at.k == at.c % 2
        lanes = lanes_at(sz.part * at.r, sz.part)
        held = []
        for y in range(2):
            there = 2 * y + at.c % 2
            wires.copy(
                stage.at[:, y], every.at[:, :, lanes], (at.d, there, at.c), base + at.r, there != at.r
            )
            held.append((there == at.r, load(stage.at[:, y], every.at[:, :, lanes], there == at.r)))

        def along():
            for r in range(4):
                block_r = every.at[:, :, sz.part * r : sz.part * (r + 1)]
                wires.arrived(block_r, base + r, (at.d, r, at.c), holds & (at.r != r))
            for when, made in held:
                run(when, made.wait)
            del held[:]
            for c in range(4):
                wires.copy(
                    every.at[c], halves.at[at.c // 2], at.along(c), base + 4 + at.c // 2, holds & (at.c != c)
                )
                when = holds & (at.c == c)
                held.append((when, load(every.at[c], halves.at[at.c // 2], when)))

        def across():
            for when, made in held:
                run(when, made.wait)
            for t in range(2):
                there = 2 * t + at.k
                wires.arrived(halves.at[t], base + 4 + t, at.along(there), there != at.c)
            mine = out.at[rows_at(block * at.y, block)]
            wires.copy(halves.at[1 - at.y], mine, at.peer(2), base + 6)
            stay.append(load(halves.at[at.y], mine))

        def finish():
            wires.arrived(out.at[rows_at(block * (1 - at.y), block)], base + 6, at.peer(2))

        return along, across, finish

    res_along, res_across, res_finish = go_home(
        x2[...] + res_total(), res_stage, res_all, res_two, result_home, 56
    )
    wires.close(res_sent)

    wires.arrived(edge_in, 41, (at.d, at.r + 1, at.c), at.r < 3)

    def unfold(column):
        tile, lane = column // 128, column % 128
        inside = jnp.where(lane < HD - 16, HD * tile + lane + 16, -1)
        tail = jnp.where(lane < 48, HD * (lane // 16) + lane % 16, -1)
        return jnp.where(tile < 3, inside, tail)

    edges = picked(edge_in[...], choose((256, 512), unfold))
    lane = lax.broadcasted_iota(jnp.int32, (sz.seq, 128), 1)
    pieces = []
    for i, back in enumerate(backs):
        first = jnp.where(lane < slack * at.r, edges[:, 128 * i : 128 * i + 128], back[:, 0:128])
        pieces += [first, back[:, 128:main]]
    pieces.append(edges[:, 384:512])
    wires.close(dob_sent)
    own_back = dob.at[:, 0 : sz.heads]
    own_back[...] = jnp.concatenate(pieces, axis=1)

    wires.close(gd_sends)
    gd_own.wait()
    h1_load.wait()
    h_order, h_send, h_relay, h_arrived, h_from = collect_col(
        wires, lambda c: xh.at[c], zh, rh, at, 72
    )
    for step in range(4):
        there = h_order[step]
        rows = rows_at(pair * there, pair)
        gw[rows] = times(dy_t[rows, 0 : sz.seq], own_back[...]).astype(low)
        other = gw.at[rows_at(pair * there + block * (1 - at.d), block)]
        wires.copy(other, xh.at[there], at.peer(4), 80 + there)

    def o_heads(step):
        there = h_order[step]
        wires.arrived(xh.at[there], 80 + there, at.peer(4))
        mine = rows_at(pair * there + block * at.d, block)
        xh[there] = (gw[mine].astype(jnp.float32) + xh[there].astype(jnp.float32)).astype(low)
        h_send(step)

    for made in loads[9:10]:
        made.wait()

    def back_in(start, tile):
        out = times_flipped(own_back[...], wh[rows_at(start, tile)])
        dy[0 : sz.seq, lanes_at(start, tile)] = out.astype(low)

    over_tiles(sz.width, back_in)
    one_onward, one_total, _ = scatter_group(
        wires, (2,), dy, lambda d, r: sz.part * r, near_one, mid, far_one, at, 64
    )
    order, o_send, o_relay, o_arrived, o_from = collect_col(
        wires, lambda c: xo.at[c], zo, ro, at, 10
    )
    for step in range(4):
        there = order[step]
        wires.arrived(xo.at[there], 48 + there, at.peer(4))
        mine = go[rows_at(pair * there, pair), lanes_at(sz.mixed * at.d, sz.mixed)]
        xo[there] = (mine.astype(jnp.float32) + xo[there].astype(jnp.float32)).astype(low)
        o_send(step)

    def relay_out(there):
        both = xo[there].astype(jnp.float32) + ro[...].astype(jnp.float32)
        xo[there] = both.astype(low)

    res_along()
    one_onward()
    o_heads(0)
    h1_back = one_total()
    through_norm, gain_one, shift_one = norm_back(
        h1_back, x_own[...].astype(jnp.float32), vec_rows[0:1]
    )
    va[0, 0:1] = gain_one
    va[0, 1:2] = shift_one
    for mask in range(1, 8):
        wires.copy(va.at[0], va.at[mask], at.peer(mask), 84 + mask)
    grad_along, grad_across, grad_finish = go_home(
        dx2[...] + through_norm, grad_stage, grad_all, grad_two, grad_home, 104
    )
    o_heads(1)
    u_relay(relay_of(ru, gu))
    o_heads(2)
    grad_along()
    res_across()
    o_relay(relay_out)
    o_heads(3)
    grad_across()

    brought = []

    def bring(c, landing, needed):
        made = load(landing.at[c], h2_t.at[pair * c : pair * (c + 1), 0 : sz.hidden], needed)
        brought.append((needed, made))

        @pl.when(jnp.logical_not(needed) & (at.c != c))
        def _():
            h2_t[pair * c : pair * (c + 1), 0 : sz.hidden] = jnp.zeros((pair, sz.hidden), low)

    def summed(lanes):
        result = jnp.zeros((pair, lanes.stop - lanes.start), jnp.float32)
        for c in range(4):
            result = result + h2_t[pair * c : pair * (c + 1), lanes].astype(jnp.float32)
        return result

    half_rows = sz.pieces

    def natural_rows(value):
        flipped = value.T
        return jnp.concatenate(
            [flipped[:, 0:half_rows], flipped[:, block : block + half_rows]], axis=1
        )

    def own_half(row):
        return jnp.where(at.d == 0, row[:, 0:half_rows], row[:, half_rows : 2 * half_rows])

    def all_brought():
        for needed, made in brought:
            run(needed, made.wait)
        del brought[:]

    for c in range(4):
        d_arrived(c)
        bring(c, zd, d_from(c))
    all_brought()
    for i in range(sz.hidden // 128):
        rows = min(128, 4 * sz.pieces - 128 * i)
        value = natural_rows(summed(slice(128 * i, 128 * (i + 1))))
        u[128 * i : 128 * i + rows, 0 : sz.share] = value[0:rows]
        if rows < 128:
            vec_out[5:6, 0:half_rows] = own_half(value[rows : rows + 1])
    down_out = load(u.at[0 : 4 * sz.pieces, 0:512], out_down)
    def relay_heads(there):
        xh[there] = (xh[there].astype(jnp.float32) + rh[...].astype(jnp.float32)).astype(low)

    h_relay(relay_heads)
    gu_own = load(gu.at[own], own_slot)
    for c in range(4):
        u_arrived(c)
        bring(c, zu, u_from(c))
    all_brought()
    gu_own.wait()
    theirs = rows_at(pair * at.c + block * (1 - at.d), block)

    def part_sum(side, lanes):
        result = jnp.zeros((block, sz.hidden), jnp.float32)
        for c in range(4):
            result = result + h2_t[rows_at(pair * c + block * side, block), lanes].astype(jnp.float32)
        return result

    every = slice(0, sz.hidden)
    gu[theirs] = part_sum(1 - at.d, every).astype(low)
    wires.copy(gu.at[theirs], xu, at.peer(4), 97)
    mine_sum = part_sum(at.d, every)
    down_out.wait()
    wires.arrived(xu, 97, at.peer(4))
    partner_sum = xu[...].astype(jnp.float32)
    for side in range(2):

        @pl.when(at.d == side)
        def _():
            both = (mine_sum, partner_sum) if side == 0 else (partner_sum, mine_sum)
            for j in range(4):
                rows = slice(block * j, block * (j + 1))
                for i in range(2):
                    u[rows, half_rows * i : half_rows * (i + 1)] = both[i][:, half_rows * j : half_rows * (j + 1)]

    bias_sum = mine_sum[half_rows : half_rows + 1]
    for j in range(4):
        vec_out[8 + j : 9 + j, 0:half_rows] = bias_sum[:, half_rows * j : half_rows * (j + 1)]
    up_out = load(u.at[0 : 4 * block, 0:512], out_up)

    for c in range(4):
        o_arrived(c)
        needed = o_from(c)
        made = load(zo.at[c], wd.at[pair * c : pair * (c + 1), 0 : sz.mixed], needed)
        brought.append((needed, made))

        @pl.when(jnp.logical_not(needed))
        def _():
            wd[pair * c : pair * (c + 1), 0 : sz.mixed] = jnp.zeros((pair, sz.mixed), low)

    all_brought()
    value = xo[at.c].astype(jnp.float32)
    for c in range(4):
        value = value + wd[pair * c : pair * (c + 1), 0 : sz.mixed].astype(jnp.float32)
    flipped = natural_rows(value)
    vec_out[4:5, 0:half_rows] = own_half(flipped[half_rows : half_rows + 1])
    flipped = flipped[0:block]
    for i in range(4):
        held = (dk_sum, dv_sum)[i // 2].at[block * (i % 2) : block * (i % 2 + 1)]
        lanes = min(128, sz.share - 128 * i)
        held[:, 0:lanes] = flipped[:, 128 * i : 128 * i + lanes]
        stay.append(load(held, out_out.at[:, 128 * i : 128 * (i + 1)]))

    for mask in range(1, 8):
        wires.arrived(va.at[mask], 84 + mask, at.peer(mask))
    vb[at.c] = functools.reduce(lambda a, b: a + b, [va[mask] for mask in range(8)])
    for c in range(4):
        wires.copy(vb.at[at.c], vb.at[at.c], at.along(c), 98 + at.c, at.c != c)

    for c in range(4):
        wires.arrived(vb.at[c], 98 + c, at.along(c), at.c != c)
    sums = vb[0] + vb[1] + vb[2] + vb[3]
    picked_sums = jnp.zeros((4, half_rows), jnp.float32)
    for i in range(8):
        cut = sums[0:4, block * i : block * i + half_rows]
        picked_sums = jnp.where(2 * at.c + at.d == i, cut, picked_sums)
    vec_out[0:4, 0:half_rows] = picked_sums
    res_finish()
    grad_finish()
    up_out.wait()
    rest_lanes = sz.heads - sz.hidden
    for c in range(4):
        h_arrived(c)
        needed = h_from(c)
        rows = slice(block * c, block * (c + 1))
        parts = (
            load(zh.at[c, :, 0 : sz.hidden], wd.at[rows], needed),
            load(zh.at[c, :, sz.hidden : sz.heads], wu.at[rows, 0:rest_lanes], needed),
        )
        brought += [(needed, made) for made in parts]

        @pl.when(jnp.logical_not(needed))
        def _():
            wd[rows] = jnp.zeros((block, sz.hidden), low)
            wu[rows, 0:rest_lanes] = jnp.zeros((block, rest_lanes), low)

    all_brought()
    left = xh[at.c, :, 0 : sz.hidden].astype(jnp.float32)
    right = xh[at.c, :, sz.hidden : sz.heads].astype(jnp.float32)
    for c in range(4):
        rows = slice(block * c, block * (c + 1))
        left = left + wd[rows].astype(jnp.float32)
        right = right + wu[rows, 0:rest_lanes].astype(jnp.float32)
    whole = jnp.concatenate([left, right], axis=1)
    for i in range(3):
        turned_columns = jnp.concatenate(
            [
                whole[:, main * i : main * (i + 1)],
                whole[:, 3 * main + slack * i : 3 * main + slack * (i + 1)],
            ],
            axis=1,
        )
        rows = slice(block * i, block * (i + 1))
        for r in range(4):

            @pl.when(at.r == r)
            def _():
                cut = slack * r
                value = turned_columns
                if cut:
                    value = jnp.concatenate([value[:, cut:], value[:, 0:cut]], axis=1)
                u[rows, 0 : sz.share] = value
                if i != 1:
                    vec_out[6 + i // 2 : 7 + i // 2, 0:half_rows] = own_half(
                        value[half_rows : half_rows + 1]
                    )

    stay.append(load(u.at[0 : 3 * block, 0:512], out_heads))
    for made in stay:
        made.wait()
    wires.close()


def update_kernel(sz, rates, grads, result_in, grad_in, weights, firsts, seconds, outs):
    down, out, up, heads, vectors = grads
    share, pieces, block = sz.share, sz.pieces, sz.block

    def move(i, place, gradient, decay):
        first_new, second_new, weight_new = adam_terms(
            weights[i][place], gradient, firsts[i][place], seconds[i][place], rates[i], decay
        )
        outs[3 * i + 2][place] = first_new
        outs[3 * i + 3][place] = second_new
        outs[3 * i + 4][place] = weight_new

    for part in range(3):
        move(0, part, heads[part, :, 0:share], MATRIX_DECAY)
    move(1, slice(None), out[:, 0:share], MATRIX_DECAY)
    move(2, slice(None), jnp.stack([up[j, :, 0:share] for j in range(4)], axis=1), MATRIX_DECAY)
    move(3, slice(None), down[:, 0:share], MATRIX_DECAY)

    @pl.when(pl.program_id(0) == 0)
    def _():
        for i, source, row in (
            (4, 0, 0), (4, 1, 1), (5, 4, 0), (5, 2, 1), (5, 3, 2), (5, 5, 3),
            (6, 6, 0), (6, 7, 1), (7, 8, 0), (7, 9, 1), (7, 10, 2), (7, 11, 3),
        ):
            move(i, row, vectors[source : source + 1, 0:pieces], 0.0)

    def plain(rows):
        rows = rows.astype(jnp.float32)
        return jnp.concatenate([rows[0:pieces], rows[block : block + pieces]], axis=0)

    @pl.when(pl.program_id(0) == 1)
    def _():
        outs[0][...] = plain(result_in[...]).astype(jnp.bfloat16)

    @pl.when(pl.program_id(0) == 2)
    def _():
        outs[1][...] = plain(grad_in[...])


def fused(
    tokens,
    cotangent,
    segments,
    weights,
    firsts,
    seconds,
):
    low = jnp.bfloat16
    seq, share = tokens.shape
    pieces = weights[1].shape[2]
    sz = Sizes(share, pieces, seq)
    block, main = sz.block, sz.main

    def views(arrays):
        heads, out, up, down, *small = arrays
        return (
            jnp.transpose(heads.reshape(pieces, 3, share), (1, 0, 2)),
            out.reshape(pieces, share),
            up.reshape(pieces, 4, share),
            down.reshape(4 * pieces, share),
            *[each.reshape(each.shape[0], 1, pieces) for each in small],
        )

    viewed = views(weights)
    labels = segments.reshape(1, -1)

    def made(*shape, dtype=low):
        return jax.ShapeDtypeStruct(shape, dtype)

    def held(*shape, dtype=low):
        return pltpu.VMEM(shape, dtype)

    w, seq, both, part = sz.width, sz.seq, sz.both, sz.part
    vmem, anywhere = pl.BlockSpec(memory_space=pltpu.VMEM), pl.BlockSpec(memory_space=pl.ANY)
    dma = pltpu.SemaphoreType.DMA
    f32 = jnp.float32
    wide = 3 * 128 + 128
    outs = pl.pallas_call(
        functools.partial(forward_kernel, sz),
        out_shape=(
            made(w, sz.heads),
            made(w, 2 * sz.mixed),
            made(w, sz.hidden),
            made(w, sz.hidden),
            made(w, seq),
            made(w, both),
            made(w, both),
            made(both, w),
            made(both, sz.hidden, dtype=f32),
            made(both, sz.hidden),
            made(seq, main + 128),
            made(seq, main + 128),
            made(seq, main + 128),
            made(seq, 2 * sz.mixed),
            made(seq, 128, dtype=f32),
            made(part, w, dtype=f32),
            made(part, w),
            made(8, w, dtype=f32),
        ),
        in_specs=[anywhere] * 6 + [vmem] * 5,
        out_specs=[anywhere] * 18,
        scratch_shapes=[
            held(w, sz.heads),
            held(w, 2 * sz.mixed),
            held(w, sz.hidden),
            held(w, sz.hidden),
            held(w, seq),
            held(w, both),
            held(w, both),
            held(both, w),
            held(both, sz.hidden, dtype=f32),
            held(both, sz.hidden),
            held(seq, main + 128),
            held(seq, main + 128),
            held(seq, main + 128),
            held(seq, 2 * sz.mixed),
            held(seq, 128, dtype=f32),
            held(part, w, dtype=f32),
            held(part, w),
            held(8, w, dtype=f32),
            held(w, seq),
            held(seq, w),
            held(both, w),
            held(seq, sz.heads),
            held(seq, main + 128),
            held(w, 128),
            held(seq, w),
            held(seq, 256),
            held(seq, 256),
            held(seq, 128),
            held(2, part, w),
            held(1, part, w),
            held(1, part, w),
            held(share, seq),
            held(share, seq),
            held(3, pieces, share, dtype=f32),
            held(pieces, share, dtype=f32),
            held(pieces, 4, share, dtype=f32),
            held(4 * pieces, share, dtype=f32),
            held(sz.pair, seq),
            held(sz.pair, seq),
            held(block, sz.hidden),
            held(seq, 1, dtype=f32),
            held(block, seq),
            held(block, seq),
            dma((160,)),
            dma((160,)),
            dma((48,)),
        ],
        compiler_params=pltpu.CompilerParams(
            collective_id=0, has_side_effects=True, vmem_limit_bytes=VMEM_BYTES
        ),
        cost_estimate=pl.CostEstimate(flops=10**10, bytes_accessed=10**8, transcendentals=10**6),
    )(tokens.T, cotangent.T, *viewed, labels)
    (wh, wo, wu, wd, h1_t, h2_t, dy_t, dy, u, gl, qw, kw, vw, a_nat, lse, x2, x_own, vec_rows) = outs
    outs = pl.pallas_call(
        functools.partial(backward_kernel, sz),
        out_shape=(
            made(4 * pieces, 512, dtype=f32),
            made(4 * block, 512, dtype=f32),
            made(block, 512, dtype=f32),
            made(3 * block, 512, dtype=f32),
            made(sz.pair, seq),
            made(sz.pair, seq),
            made(16, 256, dtype=f32),
            made(4, sz.pair, sz.hidden),
            made(4, sz.pair, sz.hidden),
            made(4, sz.pair, sz.mixed),
            made(4, block, sz.heads),
            made(4, block, seq),
            made(2, block, seq),
            made(4, block, seq),
            made(2, block, seq),
        ),
        in_specs=[anywhere] * 17 + [vmem] * 2,
        out_specs=[anywhere] * 6 + [vmem] + [anywhere] * 8,
        scratch_shapes=[
            held(sz.pair, sz.hidden),
            held(sz.pair, sz.hidden),
            held(sz.pair, sz.mixed),
            held(block, sz.heads),
            held(seq, main + 128),
            held(seq, main + 128),
            held(seq, main + 128),
            held(seq, 2 * sz.mixed),
            held(seq, 128, dtype=f32),
            held(part, w, dtype=f32),
            held(part, w),
            held(block, sz.hidden),
            held(both, w),
            held(w, both),
            held(both, sz.hidden, dtype=f32),
            held(both, sz.hidden),
            held(w, both),
            held(w, sz.hidden),
            held(w, sz.hidden),
            held(w, 2 * sz.mixed),
            held(w, sz.heads),
            held(part, w),
            held(both, sz.hidden),
            held(w, sz.heads),
            held(w, sz.hidden),
            held(w, 2 * sz.mixed),
            held(4, block, sz.heads),
            held(4, sz.pair, sz.mixed),
            held(4, part, w),
            held(3, part, w),
            held(4, part, w),
            held(3, part, w),
            held(2, part, w),
            held(1, part, w),
            held(3, part, w),
            held(seq, w),
            held(seq, 2 * sz.mixed),
            held(seq, 128, dtype=f32),
            held(seq, 128, dtype=f32),
            held(part, w, dtype=f32),
            held(seq, 256),
            held(seq, 256),
            held(seq, 128),
            held(seq, 128),
            held(seq, 1, dtype=f32),
            held(4, 2, block, part),
            held(4, 2, block, part),
            held(8, 8, w, dtype=f32),
            held(4, 8, w, dtype=f32),
            dma((128,)),
            dma((120,)),
            dma((80,)),
        ],
        compiler_params=pltpu.CompilerParams(
            collective_id=1, has_side_effects=True, vmem_limit_bytes=VMEM_BYTES
        ),
        cost_estimate=pl.CostEstimate(flops=2 * 10**10, bytes_accessed=10**8, transcendentals=10**6),
    )(
        dy, dy_t, u, gl, h2_t, wd, wu, wo, wh, h1_t,
        qw, kw, vw, a_nat, lse, x2, x_own, vec_rows, labels,
    )
    down, up, out, heads, result_home, grad_home, vectors = outs[:7]
    steps = 5
    chunk = pieces // steps

    def rows_of(shape, axis, size):
        block_shape = list(shape)
        block_shape[axis] = size
        return pl.BlockSpec(tuple(block_shape), lambda i: tuple(i if a == axis else 0 for a in range(len(shape))))

    def whole(shape):
        return pl.BlockSpec(tuple(shape), lambda i: (0,) * len(shape))

    matrix_specs = (
        rows_of((3, pieces, share), 1, chunk),
        rows_of((pieces, share), 0, chunk),
        rows_of((pieces, 4, share), 0, chunk),
        rows_of((4 * pieces, share), 0, 4 * chunk),
        *[whole(each.shape) for each in viewed[4:]],
    )
    grads = (down, out, up.reshape(4, block, 512), heads.reshape(3, block, 512), vectors)
    grad_specs = (
        rows_of((4 * pieces, 512), 0, 4 * chunk),
        rows_of((block, 512), 0, chunk),
        rows_of((4, block, 512), 1, chunk),
        rows_of((3, block, 512), 1, chunk),
        whole((16, 256)),
    )
    rates = (0.05, 0.2, 0.05, 0.025, 0.3, 0.3, 0.3, 0.3)
    arguments = (*grads, result_home, grad_home, *viewed, *views(firsts), *views(seconds))
    out_shape = [made(share, seq), made(share, seq, dtype=f32)]
    out_specs = [whole((share, seq)), whole((share, seq))]
    for each, spec in zip(viewed, matrix_specs, strict=True):
        out_shape += [jax.ShapeDtypeStruct(each.shape, f32)] * 3
        out_specs += [spec] * 3

    def update(*refs):
        ins, outs = refs[:31], refs[31:]
        update_kernel(sz, rates, ins[:5], ins[5], ins[6], ins[7:15], ins[15:23], ins[23:31], outs)

    updated = pl.pallas_call(
        update,
        grid=(steps,),
        out_shape=out_shape,
        in_specs=[*grad_specs, whole((sz.pair, seq)), whole((sz.pair, seq)), *matrix_specs * 3],
        out_specs=out_specs,
        compiler_params=pltpu.CompilerParams(vmem_limit_bytes=VMEM_BYTES),
        cost_estimate=pl.CostEstimate(
            flops=20 * 10**6, bytes_accessed=30 * 10**6, transcendentals=2 * 10**6
        ),
    )(*arguments)
    results = [updated[0].T, updated[1].T]
    for i, weight in enumerate(weights):
        for each in updated[2 + 3 * i : 5 + 3 * i]:
            if i == 0:
                each = jnp.transpose(each, (1, 0, 2))
            results.append(each.reshape(weight.shape))
    return tuple(results)


def normalize(inputs):
    center = jnp.mean(inputs, axis=1, keepdims=True)
    spread = jnp.mean(inputs * inputs, axis=1, keepdims=True) - center * center
    inverse = lax.rsqrt(spread + NORM_EPSILON)
    return ((inputs - center) * inverse, inverse)


def norm_pull(upstream, centered, inverse, gain):
    scaled = upstream * gain
    inner = (
        scaled
        - jnp.mean(scaled, axis=1, keepdims=True)
        - centered * jnp.mean(scaled * centered, axis=1, keepdims=True)
    )
    return inner * inverse


def crossed(blocks, n):
    pairs = [(i * n + j, j * n + i) for i in range(n) for j in range(n)]
    return lax.ppermute(blocks, ("row", "col"), pairs)


def scatter_rows(partial):
    return lax.psum_scatter(
        partial.astype(jnp.bfloat16), "row", scatter_dimension=0, tiled=True
    ).astype(jnp.float32)


def gather_rows(local):
    return lax.all_gather(local, "row", axis=0, tiled=True)


def split_heads(rows):
    return jnp.transpose(rows.reshape(rows.shape[0], -1, HD), (1, 0, 2))


def join_heads(values):
    return jnp.transpose(values, (1, 0, 2)).reshape(values.shape[1], -1)


def scores_of(queries, keys, allowed):
    scores = jnp.einsum(
        "hqe,hke->hqk", queries, keys, preferred_element_type=jnp.float32
    ) * HD ** (-0.5)
    return jnp.where(allowed[None], scores, MASKED)


def gathered(
    tokens,
    cotangent,
    segments,
    w_heads,
    w_out,
    w_up,
    w_down,
    norm_vectors,
    width_vectors,
    attend_bias,
    hidden_vectors,
):
    n_dp, n_row, n_col = (lax.axis_size(name) for name in ("dp", "row", "col"))
    row = lax.axis_index("row")
    low = jnp.bfloat16
    share = tokens.shape[1]
    width = share * n_col
    seq = tokens.shape[0]
    part = seq // n_row
    near = HEADS // n_row
    window = (HEADS - near * (n_row - 1)) * HD
    step = near * HD
    edge = width - (share + step * (n_row - 1)) if n_row > 1 else 0
    edge = window - share
    to_next = [(i, i + 1) for i in range(n_row - 1)]
    to_last = [(i + 1, i) for i in range(n_row - 1)]
    offset = edge - (share - step) * row

    vectors = jnp.concatenate(
        [
            norm_vectors.reshape(2, -1),
            width_vectors.reshape(4, -1),
            attend_bias.reshape(2, -1),
            hidden_vectors.reshape(4, -1),
        ]
    ).astype(low)
    vectors = lax.all_gather(vectors, ("row", "col", "dp"), axis=0, tiled=False)
    vectors = vectors.reshape(n_row, n_col, n_dp, 12, -1).astype(jnp.float32)
    by_col = jnp.transpose(vectors[0], (2, 0, 1, 3)).reshape(12, width)
    by_row = jnp.transpose(vectors[:, 0], (2, 0, 1, 3)).reshape(12, width)
    gain_one, shift_one, bias_out, gain_two, shift_two, bias_down = (by_col[i] for i in range(6))
    zeros = jnp.zeros((1, window), jnp.float32)
    attend_rows = lax.dynamic_slice_in_dim(by_row[6:8], row * step, window, axis=1)
    heads_bias = jnp.concatenate([attend_rows[0:1], zeros, attend_rows[1:2]]).reshape(-1)
    unit_bias = lax.dynamic_slice_in_dim(by_row[8:12], row * share, share, axis=1).reshape(-1)

    own = w_heads.astype(low).reshape(-1, 3, share)
    passed = lax.ppermute(own[:, :, share - edge :], "row", to_next)
    own = jnp.concatenate([passed, own, jnp.zeros_like(passed)], axis=2)
    own = lax.dynamic_slice_in_dim(own, offset, window, axis=2).reshape(-1, 3 * window)
    heads_matrix = lax.all_gather(own, ("col", "dp"), axis=0, tiled=True)
    out_matrix = lax.all_gather(w_out.astype(low).reshape(-1, share), ("col", "dp"), axis=0)
    out_matrix = jnp.transpose(out_matrix.reshape(n_col, share, share), (1, 0, 2))
    out_matrix = out_matrix.reshape(share, width)
    passed = lax.ppermute(out_matrix[share - edge :], "row", to_next)
    out_matrix = jnp.concatenate([passed, out_matrix, jnp.zeros_like(passed)])
    out_matrix = lax.dynamic_slice_in_dim(out_matrix, offset, window)
    owned = (jnp.arange(window) < step) | (row == n_row - 1)
    out_matrix = jnp.where(owned[:, None], out_matrix, jnp.zeros_like(out_matrix))
    up_matrix = lax.all_gather(
        w_up.astype(low).reshape(-1, 4 * share), ("col", "dp"), axis=0, tiled=True
    )
    down_matrix = lax.all_gather(w_down.astype(low).reshape(4, -1, share), ("col", "dp"), axis=0)
    down_matrix = down_matrix.reshape(n_col, n_dp, 4, -1, share)
    down_matrix = jnp.transpose(down_matrix, (2, 1, 3, 0, 4)).reshape(4 * share, width)

    inputs_low = lax.all_gather(crossed(tokens, n_row), "row", axis=1, tiled=True)
    upstream = lax.all_gather(crossed(cotangent, n_row), "row", axis=1, tiled=True)
    inputs = inputs_low.astype(jnp.float32)
    centered_one, inverse_one = normalize(inputs)
    normed_one = (centered_one * gain_one + shift_one).astype(low)
    projected = (times(normed_one, heads_matrix) + heads_bias).astype(low)
    queries, keys, values = (
        split_heads(projected[:, i * window : (i + 1) * window]) for i in range(3)
    )
    labels = lax.dynamic_slice_in_dim(segments, lax.axis_index("col") * seq, seq)
    places = jnp.arange(seq, dtype=jnp.int32)
    allowed = (labels[:, None] == labels[None, :]) & (places[:, None] >= places[None, :])
    scores = scores_of(queries, keys, allowed)
    highest = jnp.max(scores, axis=-1, keepdims=True)
    log_total = highest + jnp.log(jnp.sum(jnp.exp(scores - highest), axis=-1, keepdims=True))
    soft = jnp.exp(scores - log_total).astype(low)
    mixed = jnp.einsum("hqk,hke->hqe", soft, values, preferred_element_type=jnp.float32)
    mixed = join_heads(mixed.astype(low))
    branch = scatter_rows(times(mixed, out_matrix))
    mine = row * part
    middle = lax.dynamic_slice_in_dim(inputs, mine, part) + (branch + bias_out)
    centered_two, inverse_two = normalize(middle)
    normed_two = gather_rows((centered_two * gain_two + shift_two).astype(low))
    hidden = times(normed_two, up_matrix) + unit_bias
    activated, smooth_pull = jax.vjp(smooth, hidden)
    activated = activated.astype(low)
    result = (middle + (scatter_rows(times(activated, down_matrix)) + bias_down)).astype(low)

    down_back = times_flipped(upstream, down_matrix)
    grad_down = times_outer(activated, upstream)
    hidden_back = smooth_pull(down_back)[0].astype(low)
    grad_up = times_outer(normed_two, hidden_back)
    unit_sum = jnp.sum(hidden_back, axis=0, dtype=jnp.float32)
    normed_two_back = scatter_rows(times_flipped(hidden_back, up_matrix))
    upstream_own = lax.dynamic_slice_in_dim(upstream, mine, part).astype(jnp.float32)
    middle_back = upstream_own + norm_pull(normed_two_back, centered_two, inverse_two, gain_two)
    branch_own = middle_back.astype(low)
    branch_back = gather_rows(branch_own)
    mixed_back = times_flipped(branch_back, out_matrix).astype(low)
    grad_out = times_outer(mixed, branch_back)
    mixed_back = split_heads(mixed_back)
    scores_again = scores_of(queries, keys, allowed)
    soft = jnp.exp(scores_again - log_total)
    soft_back = jnp.einsum("hqe,hke->hqk", mixed_back, values, preferred_element_type=jnp.float32)
    row_inner = jnp.sum(soft_back * soft, axis=-1, keepdims=True)
    score_back = (soft * (soft_back - row_inner)).astype(low)
    query_back = jnp.einsum(
        "hqk,hke->hqe", score_back, keys, preferred_element_type=jnp.float32
    ) * HD ** (-0.5)
    key_back = jnp.einsum(
        "hqk,hqe->hke", score_back, queries, preferred_element_type=jnp.float32
    ) * HD ** (-0.5)
    value_back = jnp.einsum(
        "hqk,hqe->hke", soft.astype(low), mixed_back, preferred_element_type=jnp.float32
    )
    heads_back = jnp.concatenate(
        [join_heads(each.astype(low)) for each in (query_back, key_back, value_back)], axis=1
    )
    heads_sum = jnp.sum(heads_back, axis=0, dtype=jnp.float32)
    normed_one_back = scatter_rows(times_flipped(heads_back, heads_matrix))
    grad_heads = times_outer(normed_one, heads_back)
    centered_own = lax.dynamic_slice_in_dim(centered_one, mine, part)
    inverse_own = lax.dynamic_slice_in_dim(inverse_one, mine, part)
    input_back = middle_back + norm_pull(normed_one_back, centered_own, inverse_own, gain_one)

    def homeward(own):
        own = lax.all_to_all(own, "row", split_axis=1, concat_axis=0, tiled=True)
        return crossed(own, n_row)

    result_tokens = homeward(result)
    input_gradient = homeward(input_back.astype(low)).astype(jnp.float32)

    by_token = jnp.stack(
        [
            jnp.sum(normed_one_back * centered_own, axis=0),
            jnp.sum(normed_one_back, axis=0),
            jnp.sum(branch_own.astype(jnp.float32), axis=0),
            jnp.sum(normed_two_back * centered_two, axis=0),
            jnp.sum(normed_two_back, axis=0),
            jnp.sum(upstream_own, axis=0),
        ]
    )
    owned_rows = jnp.where(owned, heads_sum.reshape(3, window)[0::2], 0.0)
    by_unit = jnp.concatenate(
        [
            lax.dynamic_update_slice_in_dim(
                jnp.zeros((2, width), jnp.float32), owned_rows, row * step, axis=1
            ),
            lax.dynamic_update_slice_in_dim(
                jnp.zeros((4, width), jnp.float32), unit_sum.reshape(4, share), row * share, axis=1
            ),
        ]
    )
    sums = lax.psum(jnp.concatenate([by_token, by_unit]), ("dp", "row", "col"))
    pieces = share // n_dp
    inner = lax.axis_index("dp") * pieces
    col_sums = lax.dynamic_slice_in_dim(sums, lax.axis_index("col") * share + inner, pieces, axis=1)
    row_sums = lax.dynamic_slice_in_dim(sums, row * share + inner, pieces, axis=1)

    both = ("col", "dp")

    def to_owner(gradient):
        return lax.psum_scatter(gradient, both, scatter_dimension=0, tiled=True)

    got_heads = to_owner(grad_heads.astype(low)).reshape(pieces, 3, window)
    got_heads = jnp.where(owned, got_heads, jnp.zeros_like(got_heads))
    passed = lax.ppermute(got_heads[:, :, :edge], "row", to_last)
    got_heads = jnp.concatenate([got_heads, jnp.zeros_like(passed)], axis=2)
    got_heads = lax.dynamic_slice_in_dim(got_heads, edge - offset, share, axis=2)
    passed = jnp.concatenate([jnp.zeros((pieces, 3, share), low), passed, jnp.zeros_like(passed)], axis=2)
    got_heads = got_heads + lax.dynamic_slice_in_dim(passed, share - step + edge - offset, share, axis=2)
    low_out = jnp.where(owned[:, None], grad_out, 0.0).astype(low)
    passed = lax.ppermute(low_out[:edge], "row", to_last)
    low_out = jnp.concatenate([low_out, jnp.zeros_like(passed)])
    low_out = lax.dynamic_slice_in_dim(low_out, edge - offset, share)
    passed = jnp.concatenate([jnp.zeros((share, width), low), passed, jnp.zeros_like(passed)])
    low_out = low_out + lax.dynamic_slice_in_dim(passed, share - step + edge - offset, share)
    low_out = jnp.transpose(low_out.reshape(n_dp, pieces, n_col, share), (2, 0, 1, 3))
    got_out = to_owner(low_out.reshape(-1, share))
    got_up = to_owner(grad_up.astype(low))
    low_down = grad_down.astype(low).reshape(4, n_dp, pieces, n_col, share)
    low_down = jnp.transpose(low_down, (3, 1, 0, 2, 4)).reshape(-1, share)
    got_down = to_owner(low_down)

    reduced = [
        each.astype(jnp.float32).reshape(like.shape)
        for each, like in (
            (got_heads, w_heads),
            (got_out, w_out),
            (got_up, w_up),
            (got_down, w_down),
            (col_sums[0:2], norm_vectors),
            (col_sums[2:6], width_vectors),
            (row_sums[6:8], attend_bias),
            (row_sums[8:12], hidden_vectors),
        )
    ]
    return result_tokens, input_gradient, reduced


def per_device(
    tokens,
    cotangent,
    segments,
    w_heads,
    w_out,
    w_up,
    w_down,
    norm_vectors,
    width_vectors,
    attend_bias,
    hidden_vectors,
    drift_heads,
    drift_out,
    drift_up,
    drift_down,
    drift_norm,
    drift_width,
    drift_attend,
    drift_hidden,
    power_heads,
    power_out,
    power_up,
    power_down,
    power_norm,
    power_width,
    power_attend,
    power_hidden,
):
    weights = (
        w_heads,
        w_out,
        w_up,
        w_down,
        norm_vectors,
        width_vectors,
        attend_bias,
        hidden_vectors,
    )
    firsts = (
        drift_heads,
        drift_out,
        drift_up,
        drift_down,
        drift_norm,
        drift_width,
        drift_attend,
        drift_hidden,
    )
    seconds = (
        power_heads,
        power_out,
        power_up,
        power_down,
        power_norm,
        power_width,
        power_attend,
        power_hidden,
    )
    sizes = tuple(lax.axis_size(name) for name in ("dp", "row", "col"))
    if sizes == (2, 4, 4):
        return fused(tokens, cotangent, segments, weights, firsts, seconds)
    result_tokens, input_gradient, reduced = gathered(tokens, cotangent, segments, *weights)
    heads_up = adam_terms(w_heads, reduced[0], drift_heads, power_heads, 0.05, MATRIX_DECAY)
    out_up = adam_terms(w_out, reduced[1], drift_out, power_out, 0.2, MATRIX_DECAY)
    up_up = adam_terms(w_up, reduced[2], drift_up, power_up, 0.05, MATRIX_DECAY)
    down_up = adam_terms(w_down, reduced[3], drift_down, power_down, 0.025, MATRIX_DECAY)
    norm_up = adam_terms(norm_vectors, reduced[4], drift_norm, power_norm, 0.3, 0.0)
    width_up = adam_terms(width_vectors, reduced[5], drift_width, power_width, 0.3, 0.0)
    attend_up = adam_terms(attend_bias, reduced[6], drift_attend, power_attend, 0.3, 0.0)
    hidden_up = adam_terms(hidden_vectors, reduced[7], drift_hidden, power_hidden, 0.3, 0.0)
    return (
        result_tokens,
        input_gradient,
        heads_up[0],
        heads_up[1],
        heads_up[2],
        out_up[0],
        out_up[1],
        out_up[2],
        up_up[0],
        up_up[1],
        up_up[2],
        down_up[0],
        down_up[1],
        down_up[2],
        norm_up[0],
        norm_up[1],
        norm_up[2],
        width_up[0],
        width_up[1],
        width_up[2],
        attend_up[0],
        attend_up[1],
        attend_up[2],
        hidden_up[0],
        hidden_up[1],
        hidden_up[2],
    )


def solution(mesh):
    return jax.shard_map(
        per_device,
        mesh=mesh,
        in_specs=(
            P(("dp", "row"), "col"),
            P(("dp", "row"), "col"),
            P("dp"),
            P("col", "dp", None, None, "row"),
            P("row", "dp", None, "col"),
            P("col", "dp", None, None, "row"),
            P(None, "row", "dp", None, "col"),
            P(None, "col", "dp", None),
            P(None, "col", "dp", None),
            P(None, "row", "dp", None),
            P(None, "row", "dp", None),
            P("col", "dp", None, None, "row"),
            P("row", "dp", None, "col"),
            P("col", "dp", None, None, "row"),
            P(None, "row", "dp", None, "col"),
            P(None, "col", "dp", None),
            P(None, "col", "dp", None),
            P(None, "row", "dp", None),
            P(None, "row", "dp", None),
            P("col", "dp", None, None, "row"),
            P("row", "dp", None, "col"),
            P("col", "dp", None, None, "row"),
            P(None, "row", "dp", None, "col"),
            P(None, "col", "dp", None),
            P(None, "col", "dp", None),
            P(None, "row", "dp", None),
            P(None, "row", "dp", None),
        ),
        out_specs=(
            P(("dp", "row"), "col"),
            P(("dp", "row"), "col"),
            P("col", "dp", None, None, "row"),
            P("col", "dp", None, None, "row"),
            P("col", "dp", None, None, "row"),
            P("row", "dp", None, "col"),
            P("row", "dp", None, "col"),
            P("row", "dp", None, "col"),
            P("col", "dp", None, None, "row"),
            P("col", "dp", None, None, "row"),
            P("col", "dp", None, None, "row"),
            P(None, "row", "dp", None, "col"),
            P(None, "row", "dp", None, "col"),
            P(None, "row", "dp", None, "col"),
            P(None, "col", "dp", None),
            P(None, "col", "dp", None),
            P(None, "col", "dp", None),
            P(None, "col", "dp", None),
            P(None, "col", "dp", None),
            P(None, "col", "dp", None),
            P(None, "row", "dp", None),
            P(None, "row", "dp", None),
            P(None, "row", "dp", None),
            P(None, "row", "dp", None),
            P(None, "row", "dp", None),
            P(None, "row", "dp", None),
        ),
        check_vma=False,
    )
```

```python
import functools

import jax
import jax.numpy as jnp
from jax import lax
from jax.experimental import pallas as pl
from jax.experimental.pallas import tpu as pltpu
from jax.sharding import PartitionSpec as P

HEADS = 25
HD = 64
TOK_DEV = 128
STEP = 10


NORM_EPSILON = 1e-05
BETA_FIRST = 0.9
BETA_SECOND = 0.999
ADAM_EPSILON = 1e-08
MATRIX_DECAY = 0.1
MASKED = -1e30
ROOT = (2.0 / 3.141592653589793) ** 0.5
CUBIC = 0.044715
VMEM_BYTES = 66 * 1024 * 1024


def adam(weight, gradient, first, second, rate, decay):
    first_new = BETA_FIRST * first + (1.0 - BETA_FIRST) * gradient
    second_new = BETA_SECOND * second + (1.0 - BETA_SECOND) * gradient * gradient
    corrected = first_new / (1.0 - BETA_FIRST**STEP)
    divisor = jnp.sqrt(second_new / (1.0 - BETA_SECOND**STEP)) + ADAM_EPSILON
    return (first_new, second_new, weight - rate * (corrected / divisor + decay * weight))


def smooth(values):
    return jax.nn.gelu(values, approximate=True)


def ceil_to(count, unit):
    return -(-count // unit) * unit


class Sizes:
    def __init__(self, share, pieces, seq):
        self.share = share
        self.pieces = pieces
        self.block = ceil_to(pieces, 16)
        self.pair = 2 * self.block
        self.width = 4 * self.pair
        self.seq = seq
        self.part = seq // 4
        self.both = 2 * seq
        self.main = (HEADS // 4) * HD
        self.slack = share - self.main
        self.heads = ceil_to(3 * share, 256)
        self.mixed = ceil_to(pieces + 1, 128)
        self.hidden = ceil_to(4 * pieces + 1, 128)
        self.tiles = self.width // 128


class Place:
    def __init__(self):
        self.d, self.r, self.c = (lax.axis_index(name) for name in ("dp", "row", "col"))
        self.y, self.k = self.r // 2, self.r % 2

    def plane(self, mask):
        d = 1 - self.d if mask & 4 else self.d
        y = 1 - self.y if mask & 2 else self.y
        k = 1 - self.k if mask & 1 else self.k
        return d, 2 * y + k

    def peer(self, mask):
        d, r = self.plane(mask)
        return (d, r, self.c)

    def along(self, c):
        return (self.d, self.r, c)


def run(when, action):
    if when is None:
        action()
    else:
        pl.when(when)(action)


class Wires:
    def __init__(self, sends, arrivals):
        self.sends, self.arrivals = sends, arrivals
        self.used = 0
        self.open = []

    def make(self, source, target, index, slot, device):
        return pltpu.make_async_remote_copy(
            src_ref=source,
            dst_ref=target,
            send_sem=self.sends.at[index],
            recv_sem=self.arrivals.at[slot],
            device_id=device,
            device_id_type=pl.DeviceIdType.MESH,
        )

    def copy(self, source, target, device, slot, when=None):
        made = self.make(source, target, self.used, slot, device)
        self.used += 1
        run(when, made.start)
        item = (when, made)
        self.open.append(item)
        return item

    def arrived(self, target, slot, device, when=None):
        run(when, self.make(target, target, 0, slot, device).wait_recv)

    def close(self, some=None):
        for item in self.open if some is None else some:
            run(item[0], item[1].wait_send)
        self.open = [] if some is None else [o for o in self.open if all(o is not s for s in some)]


def greet(at, diagonal):
    barrier = pltpu.get_barrier_semaphore()

    def signal(device):
        pl.semaphore_signal(
            barrier, inc=1, device_id=device, device_id_type=pl.DeviceIdType.MESH
        )

    for mask in range(1, 8):
        signal(at.peer(mask))
    for c in range(4):
        run(at.c != c, functools.partial(signal, (at.d, at.r, c)))
        if diagonal:
            run(at.c != c, functools.partial(signal, (1 - at.d, at.r, c)))
    run(at.r != at.c, functools.partial(signal, (at.d, at.c, at.r)))
    pl.semaphore_wait(barrier, (13 if diagonal else 10) + jnp.where(at.r != at.c, 1, 0))


def rows_at(start, size):
    return pl.ds(pl.multiple_of(start, 16), size)


def lanes_at(start, size):
    return pl.ds(pl.multiple_of(start, 128), size)


def choose(shape, source):
    rows = lax.broadcasted_iota(jnp.int32, shape, 0)
    wanted = source(lax.broadcasted_iota(jnp.int32, shape, 1))
    return (rows == wanted).astype(jnp.bfloat16)


def edge_source(column):
    part, place = column // HD, column % HD
    wanted = jnp.where(place >= 16, 128 * part + place - 16, 384 + 16 * part + place)
    return jnp.where(part < 3, wanted, -1)


def spread_source(column):
    part, place = column // 128, column % 128
    return jnp.where(place < HD, HD * part + place, -1)


def picked(values, table):
    return jnp.dot(values, table, preferred_element_type=jnp.float32).astype(jnp.bfloat16)


def times(left, right):
    return jnp.dot(left, right, preferred_element_type=jnp.float32)


def times_flipped(left, right):
    return lax.dot_general(
        left, right, (((1,), (1,)), ((), ())), preferred_element_type=jnp.float32
    )


def times_outer(left, right):
    return lax.dot_general(
        left, right, (((0,), (0,)), ((), ())), preferred_element_type=jnp.float32
    )


def over_tiles(total, action, tile=256):
    @pl.loop(0, total // tile)
    def _(i):
        action(i * tile, tile)

    if total % tile:
        action(total - total % tile, total % tile)


def turned(values):
    return values.astype(jnp.float32).T


def gather_group(wires, masks, region, at, base):
    own = region(*at.plane(0))
    sent = [wires.copy(own, own, at.peer(mask), base + mask) for mask in (1, *masks)]

    def finish():
        for mask in masks:
            there = region(*at.plane(mask))
            wires.arrived(there, base + mask, at.peer(mask))
            sent.append(wires.copy(there, there, at.peer(1), base + mask + 1))
        for mask in (0, *masks):
            there = region(*at.plane(mask | 1))
            wires.arrived(there, base + (mask | 1), at.peer(1))

    return finish, sent


def cross_over(wires, home, landing, region, at, base):
    rows = home.shape[0] // 2
    wires.copy(home.at[rows_at(rows * (1 - at.y), rows)], landing, at.peer(2), base)
    target = region(at.c, at.d, at.y)

    def along(source, s):
        wires.copy(source, target, at.along(s), base + 1 + at.c, s != at.c)

        @pl.when(s == at.c)
        def _():
            target[...] = source[...]

    along(home.at[rows_at(rows * at.y, rows)], at.r)

    def onward():
        wires.arrived(landing, base, at.peer(2))
        along(landing, 2 * (1 - at.y) + at.k)

    def finish():
        for c in range(4):
            needed = (at.k == at.c % 2) & (at.c != c)
            wires.arrived(region(c, at.d, at.y), base + 1 + c, at.along(c), needed)

    return onward, finish


def share_pieces(wires, masks, region, at, base):
    holds = at.k == at.c % 2
    near = base + 4 * len(masks)

    def place(mask):
        d, r = at.plane(mask)
        return d, r // 2

    for c in range(4):
        own = region(c, *place(0))
        for i, mask in enumerate(masks):
            wires.copy(own, own, at.peer(mask), base + 4 * i + c, holds)
    for c in range(4):
        own = region(c, *place(0))
        wires.copy(own, own, at.peer(1), near + c, holds)

    def finish():
        for i, mask in enumerate(masks):
            for c in range(4):
                there = region(c, *place(mask))
                wires.arrived(there, base + 4 * i + c, at.peer(mask), holds)
                wires.copy(there, there, at.peer(1), near + 4 * (i + 1) + c, holds)
        for i, mask in enumerate((0, *masks)):
            for c in range(4):
                there = region(c, *place(mask))
                wires.arrived(there, near + 4 * i + c, at.peer(1), jnp.logical_not(holds))

    return finish


def scatter_group(wires, masks, partial, chunk, near, mid, far, at, base):
    sent = []
    for i, mask in enumerate((0, *masks)):
        rows = rows_at(chunk(*at.plane(mask | 1)), near.shape[1])
        sent.append(wires.copy(partial.at[rows], near.at[i], at.peer(1), base + i))

    def rows_of(mask):
        return rows_at(chunk(*at.plane(mask)), near.shape[1])

    def onward():
        for i, mask in enumerate((0, *masks)):
            wires.arrived(near.at[i], base + i, at.peer(1))
        for i, mask in enumerate(masks):
            both = partial[rows_of(mask)].astype(jnp.float32) + near[i + 1].astype(jnp.float32)
            mid[i] = both.astype(jnp.bfloat16)
            sent.append(wires.copy(mid.at[i], far.at[i], at.peer(mask), base + 4 + i))

    def total():
        for i, mask in enumerate(masks):
            wires.arrived(far.at[i], base + 4 + i, at.peer(mask))
        result = partial[rows_of(0)].astype(jnp.float32) + near[0].astype(jnp.float32)
        for i in range(len(masks)):
            result = result + far[i].astype(jnp.float32)
        return result

    return onward, total, sent


def spread_col(wires, region, at, base, wait=False):
    own = region(at.c)

    def send(distance):
        for delta in (distance, -distance):
            there = at.c + delta
            wires.copy(own, own, at.along(there), base + at.c, (there >= 0) & (there < 4))

    if not wait:
        send(2)
        send(1)

    def relay():
        for here, start, end in ((2, 0, 3), (1, 3, 0)):
            block = region(start)
            wires.arrived(block, base + start, at.along(start), at.c == here)
            wires.copy(block, block, at.along(end), base + start, at.c == here)

    def finish():
        for c in range(4):
            needed = at.c != c
            if c == 0:
                needed = needed & (at.c != 2)
            if c == 3:
                needed = needed & (at.c != 1)
            wires.arrived(region(c), base + c, at.along(c), needed)

    return (send, relay, finish) if wait else (relay, finish)


def collect_col(wires, piece, landing, rest, at, base, direct=None):
    low_end, high_end = at.c == 0, at.c == 3
    ends = low_end | high_end
    via = jnp.where(low_end, 1, 2)

    def pick(*choices):
        return jnp.where(
            low_end,
            choices[0],
            jnp.where(at.c == 1, choices[1], jnp.where(high_end, choices[3], choices[2])),
        )

    order = (pick(3, 0, 3, 0), pick(2, 2, 1, 1), pick(1, 3, 0, 2), at.c)
    target = landing.at[at.c]

    def send(step):
        there = order[step]
        block = (direct or piece)(there)
        if step == 0:
            wires.copy(block, rest, at.along(via), base + 4, ends)
            wires.copy(block, target, at.along(there), base + at.c, jnp.logical_not(ends))
        elif step == 1:
            wires.copy(block, target, at.along(there), base + at.c)
        elif step == 2:
            wires.copy(block, target, at.along(there), base + at.c, ends)

    def relay(add):
        @pl.when(jnp.logical_not(ends))
        def _():
            wires.make(rest, rest, 0, base + 4, at.along(0)).wait_recv()
            add(order[2])

        wires.copy(piece(order[2]), target, at.along(order[2]), base + at.c, jnp.logical_not(ends))

    def arrived(c):
        wires.arrived(landing.at[c], base + c, at.along(c), sent_from(c))

    def sent_from(c):
        here = at.c != c
        if c in (0, 3):
            here = here & (at.c != 3 - c)
        return here

    return order, send, relay, arrived, sent_from


def forward_kernel(
    sz,
    x_home_in,
    dy_home_in,
    w_heads,
    w_out,
    w_up,
    w_down,
    norm_vectors,
    width_vectors,
    attend_bias,
    hidden_vectors,
    segments,
    wh_out,
    wo_out,
    wu_out,
    wd_out,
    h1_t_out,
    h2_t_out,
    gd_out,
    dy_out,
    u_out,
    gl_out,
    qw_out,
    kw_out,
    vw_out,
    a_nat_out,
    lse_out,
    x2_out,
    x_own_out,
    vec_rows_out,
    wh,
    wo,
    wu,
    wd,
    h1_t,
    h2_t,
    gd,
    dy_t,
    dy,
    u,
    gl,
    qw,
    kw,
    vw,
    a_nat,
    lse,
    x2,
    x_own,
    vec_rows,
    x_t,
    h1,
    h2,
    own_qkv,
    aw,
    vec,
    part,
    edge_out,
    edge_in,
    edge_back,
    near,
    mid,
    far,
    x_raw,
    dy_raw,
    heads_raw,
    out_raw,
    up_raw,
    down_raw,
    x_home,
    dy_home,
    wu_own,
    col_labels,
    x_half,
    dy_half,
    sends,
    arrivals,
    locals_,
):
    at = Place()
    wires = Wires(sends, arrivals)
    low = jnp.bfloat16
    pair, block, pieces = sz.pair, sz.block, sz.pieces
    fetched = []
    for i, (source, target) in enumerate(
        (
            (x_home_in, x_raw),
            (w_heads, heads_raw),
            (w_up, up_raw),
            (w_out, out_raw),
            (w_down, down_raw),
            (dy_home_in, dy_raw),
        )
    ):
        fetched.append(pltpu.make_async_copy(source, target, locals_.at[40 + i]))
        fetched[i].start()
    row_labels = segments.at[:, lanes_at(sz.seq * at.c, sz.seq)]

    def halves(value, target):
        value = value.astype(jnp.float32)
        gap = jnp.zeros((block - pieces, value.shape[1]), jnp.float32)
        parts = [value[0:pieces], gap, value[pieces : 2 * pieces], gap]
        target[...] = jnp.concatenate(parts, axis=0).astype(low)

    def quarter(row):
        return row.astype(low).astype(jnp.float32) * 0.25

    def placed(row):
        both = jnp.concatenate([row, row], axis=1)
        half_of = lax.broadcasted_iota(jnp.int32, both.shape, 1) // pieces
        return jnp.where(half_of == at.d, both, 0.0)

    def with_row(value, row):
        gap = jnp.zeros((block - pieces - 1, value.shape[1]), jnp.float32)
        return jnp.concatenate([value, row, gap], axis=0)

    flat = jnp.concatenate(
        [norm_vectors[0], norm_vectors[1], width_vectors[1], width_vectors[2]], axis=0
    )
    flat = jnp.concatenate([flat, jnp.zeros((124, pieces), jnp.float32)], axis=0)
    flat = jnp.concatenate([flat, jnp.zeros((128, 256 - pieces), jnp.float32)], axis=1)
    where_row = lax.broadcasted_iota(jnp.int32, flat.shape, 0)
    where_lane = lax.broadcasted_iota(jnp.int32, flat.shape, 1)
    carrier = (where_lane == pieces) & ((where_row == 1) | (where_row == 3))
    own_rows = rows_at(pair * at.c + block * at.d, block)
    vec[own_rows] = jnp.where(carrier, 1.0, flat).T[0:block].astype(low)
    fetched[0].wait()
    halves(x_raw[...], x_home)
    greet(at, False)

    def x_piece(c, d, y):
        return x_t.at[rows_at(pair * c + block * y, block)]

    def dy_piece(c, d, y):
        return dy_t.at[rows_at(pair * c + block * y, block), lanes_at(sz.seq * d, sz.seq)]

    used = [0]

    def flush(source, target):
        made = pltpu.make_async_copy(source, target, locals_.at[used[0]])
        used[0] += 1
        made.start()
        flushed.append(made)

    flushed = []

    def vec_block(d, c):
        return vec.at[rows_at(pair * c + block * d, block)]

    def wh_block(d):
        return lambda c: wh.at[rows_at(pair * c + block * d, block)]

    def wo_block(d):
        return lambda c: wo.at[rows_at(pair * c, pair), lanes_at(sz.mixed * d, sz.mixed)]

    def wu_block(d):
        return lambda c: wu.at[rows_at(pair * c + block * d, block)]

    def wd_block(half):
        return lambda c: wd.at[rows_at(pair * c + block * half, block)]

    x_onward, x_crossed = cross_over(wires, x_home, x_half, x_piece, at, 96)
    for c in range(4):
        wires.copy(vec_block(at.d, at.c), vec_block(at.d, at.c), at.along(c), 2 + at.c, at.c != c)
    wires.copy(vec_block(at.d, at.c), vec_block(at.d, at.c), at.peer(4), 6 + at.c)

    fetched[1].wait()
    for r in range(4):

        @pl.when(at.r == r)
        def _():
            cut = sz.share - sz.slack * r
            tails = []
            for i in range(3):
                value = heads_raw[i]
                row = jnp.zeros((1, sz.share), jnp.float32)
                if i != 1:
                    row = placed(quarter(attend_bias[i // 2]))
                value = with_row(value, row)
                if r:
                    value = jnp.concatenate([value[:, cut:], value[:, 0:cut]], axis=1)
                wh[own_rows, sz.main * i : sz.main * (i + 1)] = value[:, 0 : sz.main].astype(low)
                tails.append(value[:, sz.main :])
            tails.append(jnp.zeros((block, sz.heads - 3 * sz.share), jnp.float32))
            wh[own_rows, 3 * sz.main : sz.heads] = jnp.concatenate(tails, axis=1).astype(low)

    x_onward()
    wh_relay, wh_done = spread_col(wires, wh_block(at.d), at, 20)
    wires.copy(wh_block(at.d)(at.c), wh_block(at.d)(at.c), at.peer(4), 24 + at.c)

    fetched[2].wait()
    gap = jnp.zeros((block, sz.hidden - 4 * pieces), jnp.float32)
    values = [
        with_row(up_raw[:, j, :], placed(quarter(hidden_vectors[j]))) for j in range(4)
    ]
    for i in range(2):
        lanes = slice(pieces * i, pieces * (i + 1))
        whole = jnp.concatenate([value[:, lanes] for value in values] + [gap], axis=1)

        @pl.when(at.d == i)
        def _():
            wu[own_rows] = whole.astype(low)

        @pl.when(at.d != i)
        def _():
            wu_own[...] = whole.astype(low)

    wires.copy(wu_own, wu_block(at.d)(at.c), at.peer(4), 10)

    def turned_halves(value, target, lanes):
        flipped = value.T
        gap = jnp.zeros((block - pieces, flipped.shape[1]), jnp.float32)
        parts = [flipped[0:pieces], gap, flipped[pieces : 2 * pieces], gap]
        target[rows_at(pair * at.c, pair), lanes] = jnp.concatenate(parts, axis=0).astype(low)

    fetched[3].wait()
    value = with_row(out_raw[...], placed(quarter(width_vectors[0])))
    value = jnp.concatenate([value, jnp.zeros((sz.mixed - block, sz.share), jnp.float32)], axis=0)
    for i in range(sz.mixed // 128):
        lanes = slice(128 * i, 128 * (i + 1))
        turned_halves(value[lanes], wo, lanes_at(sz.mixed * at.d + 128 * i, 128))
    wo_relay, wo_done = spread_col(wires, wo_block(at.d), at, 28)
    wires.copy(wo_block(at.d)(at.c), wo_block(at.d)(at.c), at.peer(4), 32 + at.c)

    x_crossed()
    x_done = share_pieces(wires, (2,), x_piece, at, 104)

    fetched[4].wait()
    for i in range(sz.hidden // 128):
        rows = slice(128 * i, 128 * (i + 1))
        if 128 * (i + 1) <= 4 * pieces:
            value = down_raw[rows]
        else:
            value = jnp.concatenate(
                [
                    down_raw[128 * i : 4 * pieces],
                    placed(quarter(width_vectors[3])),
                    jnp.zeros((sz.hidden - 4 * pieces - 1, sz.share), jnp.float32),
                ],
                axis=0,
            )
        turned_halves(value, wd, rows)
    fetched[5].wait()
    halves(dy_raw[...], dy_home)
    col_labels[...] = jnp.concatenate([row_labels[...]] * 8, axis=0).astype(jnp.float32).T[:, 0:1]
    x_done()
    wu_first, wu_first_done = spread_col(wires, wu_block(at.d), at, 36)

    for c in range(4):
        wires.arrived(vec_block(at.d, c), 2 + c, at.along(c), at.c != c)
    wires.arrived(vec_block(1 - at.d, at.c), 6 + at.c, at.peer(4))
    for step in range(1, 4):
        there = (at.c + step) % 4
        wires.copy(
            vec_block(at.d, there), vec_block(at.d, there), at.peer(4), 6 + there
        )
    for step in range(1, 4):
        there = (at.c + step) % 4
        wires.arrived(vec_block(1 - at.d, there), 6 + there, at.peer(4))
    features = 4.0 * sz.share

    def add_up(i, carry):
        rows = rows_at(128 * i, 128)
        value = x_t[rows].astype(jnp.float32)
        return (
            carry[0] + jnp.sum(value, axis=0, keepdims=True),
            carry[1] + jnp.sum(value * value, axis=0, keepdims=True),
        )

    zero = jnp.zeros((1, sz.seq), jnp.float32)
    sums = lax.fori_loop(0, sz.tiles, add_up, (zero, zero))
    center = sums[0] / features
    inverse = lax.rsqrt(sums[1] / features - center * center + NORM_EPSILON)

    @pl.loop(0, sz.tiles)
    def _(i):
        rows, lanes = rows_at(128 * i, 128), lanes_at(128 * i, 128)
        vectors = vec[rows].astype(jnp.float32)
        value = (x_t[rows].astype(jnp.float32) - center) * inverse
        value = value * vectors[:, 0:1] + vectors[:, 1:2]
        h1_t[rows] = value.astype(low)
        h1[:, lanes] = value.T.astype(low)
        mine = x_t[rows, lanes_at(sz.part * at.r, sz.part)]
        x_own[:, lanes] = turned(mine).astype(low)
        vec_rows[:, lanes] = vectors.T[0:8]

    flush(h1_t, h1_t_out)
    flush(x_own, x_own_out)
    flush(vec_rows, vec_rows_out)

    wh_relay()
    for c in range(4):
        needed = at.c != c
        if c == 0:
            needed = needed & (at.c != 2)
        if c == 3:
            needed = needed & (at.c != 1)
        wires.arrived(wh_block(at.d)(c), 20 + c, at.along(c), needed)
        wires.copy(wh_block(at.d)(c), wh_block(at.d)(c), at.peer(4), 24 + c, at.c != c)

    wires.arrived(wu_block(1 - at.d)(at.c), 10, at.peer(4))
    wu_second, wu_second_done = spread_col(wires, wu_block(1 - at.d), at, 40)
    for c in range(4):
        wires.arrived(wh_block(1 - at.d)(c), 24 + c, at.peer(4))
    flush(wh, wh_out)

    @pl.loop(0, sz.heads // 256)
    def _(i):
        lanes = lanes_at(256 * i, 256)
        own_qkv[:, lanes] = times(h1[...], wh[:, lanes]).astype(low)

    dy_onward, dy_crossed = cross_over(wires, dy_home, dy_half, dy_piece, at, 116)

    starts = (0, sz.main, 2 * sz.main, 3 * sz.main)
    ends = jnp.concatenate([own_qkv[:, s : s + 128] for s in starts], axis=1)
    edge_out[...] = picked(ends, choose((512, 256), edge_source))
    last = at.r == 3

    @pl.when(at.r == 0)
    def _():
        edge_in[...] = jnp.zeros_like(edge_in)

    wires.copy(edge_out, edge_in, (at.d, at.r + 1, at.c), 52, at.r < 3)
    spread = choose((256, 384), spread_source)
    extra = picked(edge_out[...], spread)
    wires.arrived(edge_in, 52, (at.d, at.r - 1, at.c), at.r > 0)
    first = picked(edge_in[...], spread)
    lane = lax.broadcasted_iota(jnp.int32, (sz.seq, 128), 1)
    for i, target in enumerate((qw, kw, vw)):
        start = starts[i]
        target[:, 0:128] = jnp.where(
            lane < sz.slack * at.r,
            first[:, 128 * i : 128 * i + 128],
            own_qkv[:, start : start + 128],
        )
        target[:, 128 : sz.main] = own_qkv[:, start + 128 : start + sz.main]
        target[:, sz.main : sz.main + 128] = extra[:, 128 * i : 128 * i + 128]
    flush(qw, qw_out)
    flush(kw, kw_out)
    flush(vw, vw_out)

    dy_onward()
    wo_relay()
    for c in range(4):
        needed = at.c != c
        if c == 0:
            needed = needed & (at.c != 2)
        if c == 3:
            needed = needed & (at.c != 1)
        wires.arrived(wo_block(at.d)(c), 28 + c, at.along(c), needed)
        wires.copy(wo_block(at.d)(c), wo_block(at.d)(c), at.peer(4), 32 + c, at.c != c)

    half = sz.seq // 2

    def heads_of(p, count):
        tile = lanes_at(128 * p, 128)
        for q in range(2):
            rows = slice(half * q, half * (q + 1))
            keys = half * (q + 1)
            order = lax.broadcasted_iota(jnp.int32, (half, keys), 0) + half * q
            allowed = (col_labels[rows, :] == row_labels[:, 0:keys].astype(jnp.float32)) & (
                order >= lax.broadcasted_iota(jnp.int32, (half, keys), 1)
            )
            lanes = lax.broadcasted_iota(jnp.int32, (half, 128), 1)
            side = lanes // HD
            total = jnp.zeros((half, 128), jnp.float32)
            for h in range(count):
                queries = jnp.where(side == h, qw[rows, tile].astype(jnp.float32) * HD ** (-0.5), 0.0)
                scores = times_flipped(queries.astype(low), kw[0:keys, tile])
                scores = jnp.where(allowed, scores, MASKED)
                highest = jnp.max(scores, axis=1, keepdims=True)
                raised = jnp.exp(scores - highest)
                summed = jnp.sum(raised, axis=1, keepdims=True)
                found = highest + jnp.log(summed)
                lse[rows, :] = jnp.where(lanes == 2 * p + h, found, lse[rows, :])
                soft = (raised * (1.0 / summed)).astype(low)
                total = jnp.where(side == h, times(soft, vw[0:keys, tile]), total)
            aw[rows, tile] = total.astype(low)

    lse[...] = jnp.zeros_like(lse)

    @pl.loop(0, sz.main // 128)
    def _(p):
        heads_of(p, 2)

    @pl.when(last)
    def _():
        heads_of(sz.main // 128, 1)
        edge_back[...] = aw[:, sz.main : sz.main + 128]

    flush(lse, lse_out)

    wires.copy(aw.at[:, 0:128], edge_back, (at.d, at.r - 1, at.c), 53, at.r > 0)
    wd_first_send, wd_first, wd_first_done = spread_col(wires, wd_block(0), at, 44, True)
    wd_second_send, wd_second, wd_second_done = spread_col(wires, wd_block(1), at, 48, True)
    for distance in (2, 1):
        wd_first_send(distance)
        wd_second_send(distance)
    wu_first()
    wires.arrived(edge_back, 53, (at.d, at.r + 1, at.c), at.r < 3)

    def natural(column):
        inner = column % sz.mixed
        place = sz.pieces * (column // sz.mixed) + inner + sz.slack * at.r
        return jnp.where(inner < sz.pieces, place, -1)

    def natural_main(column):
        place = natural(column)
        return jnp.where(place < sz.main, place, -1)

    def natural_edge(column):
        return natural(column) - sz.main

    mixed = times(aw[:, 0 : sz.main], choose((sz.main, 2 * sz.mixed), natural_main))
    mixed = mixed + times(edge_back[...], choose((128, 2 * sz.mixed), natural_edge))
    ones = lax.broadcasted_iota(jnp.int32, mixed.shape, 1) % sz.mixed == sz.pieces
    a_nat[...] = jnp.where(ones, 1.0, mixed).astype(low)
    for c in range(4):
        wires.arrived(wo_block(1 - at.d)(c), 32 + c, at.peer(4))
    flush(wo, wo_out)
    flush(a_nat, a_nat_out)

    def project(start, tile):
        out = times_flipped(a_nat[...], wo[rows_at(start, tile)])
        part[:, lanes_at(start, tile)] = out.astype(low)

    over_tiles(sz.width, project)

    onward, total, _ = scatter_group(
        wires, (2,), part, lambda d, r: sz.part * r, near, mid, far, at, 64
    )
    onward()
    middle = x_own[...].astype(jnp.float32) + total()
    x2[...] = middle
    flush(x2, x2_out)
    center = jnp.sum(middle, axis=1, keepdims=True) / features
    spread_two = jnp.sum(middle * middle, axis=1, keepdims=True) / features - center * center
    normed = (middle - center) * lax.rsqrt(spread_two + NORM_EPSILON)
    own_rows = rows_at(sz.part * (4 * at.d + at.r), sz.part)
    h2[own_rows] = (normed * vec_rows[2:3] + vec_rows[3:4]).astype(low)
    h2_done, _ = gather_group(
        wires, (2, 4, 6), lambda d, r: h2.at[rows_at(sz.part * (4 * d + r), sz.part)], at, 72
    )
    wu_second()
    h2_done()
    wu_first_done()
    wu_second_done()
    flush(wu, wu_out)

    def expand(start, tile):
        lanes = lanes_at(start, tile)
        value = times(h2[...], wu[:, lanes])
        u[:, lanes] = value
        inner = jnp.tanh(ROOT * (value + CUBIC * value * value * value))
        value = 0.5 * value * (1.0 + inner)
        column = lax.broadcasted_iota(jnp.int32, value.shape, 1) + start
        gl[:, lanes] = jnp.where(column == 4 * sz.pieces, 1.0, value).astype(low)

    over_tiles(sz.hidden, expand)

    dy_crossed()
    dy_done = share_pieces(wires, (2, 4, 6), dy_piece, at, 124)
    flush(u, u_out)
    flush(gl, gl_out)
    wd_first()

    @pl.loop(0, sz.tiles)
    def _(i):
        h2_t[rows_at(128 * i, 128)] = turned(h2[:, lanes_at(128 * i, 128)]).astype(low)

    flush(h2_t, h2_t_out)
    wd_second()
    dy_done()

    @pl.loop(0, sz.tiles)
    def _(i):
        dy[:, lanes_at(128 * i, 128)] = turned(dy_t[rows_at(128 * i, 128)]).astype(low)

    flush(dy, dy_out)

    @pl.loop(0, 4)
    def _(i):
        rows = rows_at(pair * i, pair)
        gd[rows] = times(dy_t[rows], gl[...]).astype(low)

    flush(gd, gd_out)
    wd_first_done()
    wd_second_done()
    flush(wd, wd_out)
    wires.close()
    for made in flushed:
        made.wait()


def backward_kernel(
    sz,
    dy_all,
    gd_all,
    u_all,
    gl_all,
    h2_t_all,
    wd_all,
    wu_all,
    wo_all,
    wh_all,
    h1_t_all,
    qw_all,
    kw_all,
    vw_all,
    a_nat_all,
    lse_all,
    x2_all,
    x_own_all,
    vec_rows,
    segments,
    out_down,
    out_up,
    out_out,
    out_heads,
    result_home,
    grad_home,
    vec_out,
    zd,
    zu,
    zo,
    zh,
    res_all,
    res_two,
    grad_all,
    grad_two,
    rd,
    ru,
    ro,
    rh,
    qw,
    kw,
    vw,
    a_nat,
    lse,
    x2,
    x_own,
    xu,
    dy,
    dy_t,
    u,
    gl,
    h2_t,
    wd,
    wu,
    wo,
    wh,
    dy_own,
    du,
    gw,
    gu,
    go,
    xh,
    xo,
    near_two,
    far_two,
    near_res,
    far_res,
    near_one,
    far_one,
    mid,
    dob,
    da,
    dk_sum,
    dv_sum,
    dx2,
    edge_out,
    edge_in,
    fore_out,
    fore_in,
    col_labels,
    res_stage,
    grad_stage,
    va,
    vb,
    sends,
    arrivals,
    locals_,
):
    at = Place()
    wires = Wires(sends, arrivals)
    low = jnp.bfloat16
    pair, block = sz.pair, sz.block
    features = 4.0 * sz.share
    used = [0]

    def load(source, target, when=None):
        made = pltpu.make_async_copy(source, target, locals_.at[used[0]])
        used[0] += 1
        run(when, made.start)
        return made

    own_rows = rows_at(sz.part * (4 * at.d + at.r), sz.part)
    gd = gw.at[:, 0 : sz.hidden]
    loads = [
        load(s, t)
        for s, t in (
            (dy_all, dy),
            (wd_all, wd),
            (u_all, u),
            (dy_all.at[own_rows], dy_own),
            (wu_all, wu),
            (h2_t_all, h2_t),
            (gl_all, gl),
            (gd_all, gd),
            (wo_all, wo),
            (wh_all, wh),
            (x2_all, x2),
            (a_nat_all, a_nat),
            (qw_all, qw),
            (kw_all, kw),
            (vw_all, vw),
            (lse_all, lse),
            (x_own_all, x_own),
            (h1_t_all, dy_t.at[:, 0 : sz.seq]),
        )
    ]
    greet(at, False)
    stay = []

    order, d_send, d_relay, d_arrived, d_from = collect_col(
        wires,
        lambda c: gd.at[rows_at(pair * c, pair)],
        zd,
        rd,
        at,
        0,
        lambda c: gd_all.at[rows_at(pair * c, pair)],
    )
    for step in range(4):
        d_send(step)

    def relay_of(rest, block):
        def add(there):
            rows = rows_at(pair * there, pair)
            block[rows] = (block[rows].astype(jnp.float32) + rest[...].astype(jnp.float32)).astype(low)

        return add

    for made in loads[0:3]:
        made.wait()

    def through(start, tile):
        lanes = lanes_at(start, tile)
        upstream = times(dy[...], wd[:, lanes])
        value = u[:, lanes]
        inner = jnp.tanh(ROOT * (value + CUBIC * value * value * value))
        slope = 0.5 * (1.0 + inner) + 0.5 * value * (1.0 - inner * inner) * ROOT * (
            1.0 + 3.0 * CUBIC * value * value
        )
        du[:, lanes] = (upstream * slope).astype(low)

    over_tiles(sz.hidden, through)
    loads[4].wait()

    def back_up(start, tile):
        dy[:, lanes_at(start, tile)] = times_flipped(du[...], wu[rows_at(start, tile)]).astype(low)

    over_tiles(sz.width, back_up)

    def chunk_both(d, r):
        return sz.part * (4 * d + r)

    two_onward, two_total, two_sent = scatter_group(
        wires, (2, 4, 6), dy, chunk_both, near_two, mid, far_two, at, 16
    )
    loads[5].wait()
    order, u_send, u_relay, u_arrived, u_from = collect_col(
        wires, lambda c: gu.at[rows_at(pair * c, pair)], zu, ru, at, 5
    )
    for step in range(4):
        rows = rows_at(pair * order[step], pair)
        gu[rows] = times(h2_t[rows], du[...]).astype(low)
        u_send(step)
        if step == 1:
            two_onward()
    own = rows_at(pair * at.c, pair)
    own_slot = h2_t.at[own, 0 : sz.hidden]
    gd_own = load(gd_all.at[own], own_slot)
    loads[7].wait()
    before = len(wires.open)
    d_relay(relay_of(rd, gd))
    gd_sends = wires.open[before:]

    def norm_back(upstream, values, gain):
        center = jnp.sum(values, axis=1, keepdims=True) / features
        spread = jnp.sum(values * values, axis=1, keepdims=True) / features - center * center
        inverse = lax.rsqrt(spread + NORM_EPSILON)
        centered = (values - center) * inverse
        scaled = upstream * gain
        inner = (
            scaled
            - jnp.sum(scaled, axis=1, keepdims=True) / features
            - centered * (jnp.sum(scaled * centered, axis=1, keepdims=True) / features)
        )
        return (
            inner * inverse,
            jnp.sum(upstream * centered, axis=0, keepdims=True),
            jnp.sum(upstream, axis=0, keepdims=True),
        )

    loads[10].wait()
    loads[3].wait()
    h2_back = two_total()
    through_norm, gain_two, shift_two = norm_back(h2_back, x2[...], vec_rows[2:3])
    middle_back = dy_own[...].astype(jnp.float32) + through_norm
    dx2[...] = middle_back
    va[0, 2:3] = gain_two
    va[0, 3:4] = shift_two
    va[0, 4:8] = jnp.zeros((4, sz.width), jnp.float32)
    dob[rows_at(sz.part * at.r, sz.part)] = middle_back.astype(low)
    dob_done, dob_sent = gather_group(
        wires, (2,), lambda d, r: dob.at[rows_at(sz.part * r, sz.part)], at, 24
    )

    def contract(start, tile):
        out = times_flipped(gl[...], wd[rows_at(start, tile)])
        dy[:, lanes_at(start, tile)] = out.astype(low)

    wires.close(two_sent)
    loads[6].wait()
    over_tiles(sz.width, contract)
    res_onward, res_total, res_sent = scatter_group(
        wires, (2, 4, 6), dy, chunk_both, near_res, mid, far_res, at, 32
    )

    dob_done()
    loads[11].wait()
    loads[8].wait()
    da[...] = times(dob[...], wo[...]).astype(low)
    slack, main = sz.slack, sz.main

    def from_natural(place):
        wanted = sz.mixed * (place // sz.pieces) + place % sz.pieces
        return jnp.where((place >= 0) & (place < sz.share), wanted, -1)

    fore_out[...] = picked(
        da[...], choose((2 * sz.mixed, 128), lambda j: from_natural(j + main - slack * at.r))
    )

    @pl.when(at.r == 0)
    def _():
        fore_in[...] = jnp.zeros_like(fore_in)

    wires.copy(fore_out, fore_in, (at.d, at.r + 1, at.c), 40, at.r < 3)

    @pl.loop(0, sz.tiles)
    def _(i):
        dy_t[rows_at(128 * i, 128), sz.seq : sz.both] = turned(dob[:, lanes_at(128 * i, 128)]).astype(low)

    res_onward()

    for step in range(4):
        there = (at.c + step) % 4
        rows = rows_at(pair * there, pair)
        go[rows] = times(dy_t[rows, sz.seq : sz.both], a_nat[...]).astype(low)
        wires.copy(
            go.at[rows, lanes_at(sz.mixed * (1 - at.d), sz.mixed)], xo.at[there], at.peer(4), 48 + there
        )
    wires.arrived(fore_in, 40, (at.d, at.r - 1, at.c), at.r > 0)
    window = times(da[...], choose((2 * sz.mixed, main), lambda j: from_natural(j - slack * at.r)))
    da_first = window[:, 0:128] + fore_in[...].astype(jnp.float32)
    da[:, 128:main] = window[:, 128:main].astype(low)
    da[:, 0:128] = da_first.astype(low)
    da[:, main : main + 128] = fore_out[...]

    row_labels = segments.at[:, lanes_at(sz.seq * at.c, sz.seq)]
    col_labels[...] = jnp.concatenate([row_labels[...]] * 8, axis=0).astype(jnp.float32).T[:, 0:1]
    for made in loads[12:17]:
        made.wait()
    half = sz.seq // 2
    dqw, dkw = (du.at[sz.seq * i : sz.seq * (i + 1), 0 : main + 128] for i in range(2))
    dvw = gl.at[0 : sz.seq, 0 : main + 128]

    def heads_back(p, count):
        tile = lanes_at(128 * p, 128)
        dk_sum[...] = jnp.zeros_like(dk_sum)
        dv_sum[...] = jnp.zeros_like(dv_sum)
        for q in range(2):
            rows = slice(half * q, half * (q + 1))
            keys = half * (q + 1)
            order = lax.broadcasted_iota(jnp.int32, (half, keys), 0) + half * q
            allowed = (col_labels[rows, :] == row_labels[:, 0:keys].astype(jnp.float32)) & (
                order >= lax.broadcasted_iota(jnp.int32, (half, keys), 1)
            )
            lanes = lax.broadcasted_iota(jnp.int32, (half, 128), 1)
            side = lanes // HD
            total = jnp.zeros((half, 128), jnp.float32)
            for h in range(count):
                queries = jnp.where(side == h, qw[rows, tile].astype(jnp.float32) * HD ** (-0.5), 0.0)
                queries = queries.astype(low)
                pulled = jnp.where(side == h, da[rows, tile].astype(jnp.float32), 0.0).astype(low)
                found = jnp.sum(jnp.where(lanes == 2 * p + h, lse[rows, :], 0.0), axis=1, keepdims=True)
                scores = times_flipped(queries, kw[0:keys, tile])
                soft = jnp.where(allowed, jnp.exp(jnp.where(allowed, scores - found, MASKED)), 0.0)
                soft_back = times_flipped(pulled, vw[0:keys, tile])
                inner = jnp.sum(soft_back * soft, axis=1, keepdims=True)
                score_back = (soft * (soft_back - inner)).astype(low)
                piece = times(score_back, kw[0:keys, tile]) * HD ** (-0.5)
                total = jnp.where(side == h, piece, total)
                dk_sum[0:keys] += times_outer(score_back, queries)
                dv_sum[0:keys] += times_outer(soft.astype(low), pulled)
            dqw[rows, tile] = total.astype(low)
        dkw[:, tile] = dk_sum[...].astype(low)
        dvw[:, tile] = dv_sum[...].astype(low)

    @pl.loop(0, main // 128)
    def _(p):
        heads_back(p, 2)

    @pl.when(at.r == 3)
    def _():
        heads_back(main // 128, 1)

    def compact(column):
        part, place = column // HD, column % HD
        return jnp.where(part < 3, 128 * part + place, -1)

    table = choose((384, 256), compact)
    backs = (dqw, dkw, dvw)
    edge_out[...] = picked(jnp.concatenate([b[:, 0:128] for b in backs], axis=1), table)
    wires.copy(edge_out, edge_in, (at.d, at.r - 1, at.c), 41, at.r > 0)

    @pl.when(at.r == 3)
    def _():
        edge_in[...] = picked(jnp.concatenate([b[:, main : main + 128] for b in backs], axis=1), table)

    def go_home(values, stage, every, halves, out, base):
        flipped = values.T
        for c in range(4):
            for y in range(2):
                rows = slice(pair * c + block * y, pair * c + block * (y + 1))
                stage[c, y] = flipped[rows].astype(low)
        holds = at.k == at.c % 2
        lanes = lanes_at(sz.part * at.r, sz.part)
        held = []
        for y in range(2):
            there = 2 * y + at.c % 2
            wires.copy(
                stage.at[:, y], every.at[:, :, lanes], (at.d, there, at.c), base + at.r, there != at.r
            )
            held.append((there == at.r, load(stage.at[:, y], every.at[:, :, lanes], there == at.r)))

        def along():
            for r in range(4):
                block_r = every.at[:, :, sz.part * r : sz.part * (r + 1)]
                wires.arrived(block_r, base + r, (at.d, r, at.c), holds & (at.r != r))
            for when, made in held:
                run(when, made.wait)
            del held[:]
            for c in range(4):
                wires.copy(
                    every.at[c], halves.at[at.c // 2], at.along(c), base + 4 + at.c // 2, holds & (at.c != c)
                )
                when = holds & (at.c == c)
                held.append((when, load(every.at[c], halves.at[at.c // 2], when)))

        def across():
            for when, made in held:
                run(when, made.wait)
            for t in range(2):
                there = 2 * t + at.k
                wires.arrived(halves.at[t], base + 4 + t, at.along(there), there != at.c)
            mine = out.at[rows_at(block * at.y, block)]
            wires.copy(halves.at[1 - at.y], mine, at.peer(2), base + 6)
            stay.append(load(halves.at[at.y], mine))

        def finish():
            wires.arrived(out.at[rows_at(block * (1 - at.y), block)], base + 6, at.peer(2))

        return along, across, finish

    res_along, res_across, res_finish = go_home(
        x2[...] + res_total(), res_stage, res_all, res_two, result_home, 56
    )
    wires.close(res_sent)

    wires.arrived(edge_in, 41, (at.d, at.r + 1, at.c), at.r < 3)

    def unfold(column):
        tile, lane = column // 128, column % 128
        inside = jnp.where(lane < HD - 16, HD * tile + lane + 16, -1)
        tail = jnp.where(lane < 48, HD * (lane // 16) + lane % 16, -1)
        return jnp.where(tile < 3, inside, tail)

    edges = picked(edge_in[...], choose((256, 512), unfold))
    lane = lax.broadcasted_iota(jnp.int32, (sz.seq, 128), 1)
    pieces = []
    for i, back in enumerate(backs):
        first = jnp.where(lane < slack * at.r, edges[:, 128 * i : 128 * i + 128], back[:, 0:128])
        pieces += [first, back[:, 128:main]]
    pieces.append(edges[:, 384:512])
    wires.close(dob_sent)
    own_back = dob.at[:, 0 : sz.heads]
    own_back[...] = jnp.concatenate(pieces, axis=1)

    wires.close(gd_sends)
    gd_own.wait()
    loads[17].wait()
    h_order, h_send, h_relay, h_arrived, h_from = collect_col(
        wires, lambda c: xh.at[c], zh, rh, at, 72
    )
    for step in range(4):
        there = h_order[step]
        rows = rows_at(pair * there, pair)
        gw[rows] = times(dy_t[rows, 0 : sz.seq], own_back[...]).astype(low)
        other = gw.at[rows_at(pair * there + block * (1 - at.d), block)]
        wires.copy(other, xh.at[there], at.peer(4), 80 + there)

    def o_heads(step):
        there = h_order[step]
        wires.arrived(xh.at[there], 80 + there, at.peer(4))
        mine = rows_at(pair * there + block * at.d, block)
        xh[there] = (gw[mine].astype(jnp.float32) + xh[there].astype(jnp.float32)).astype(low)
        h_send(step)

    for made in loads[9:10]:
        made.wait()

    def back_in(start, tile):
        out = times_flipped(own_back[...], wh[rows_at(start, tile)])
        dy[0 : sz.seq, lanes_at(start, tile)] = out.astype(low)

    over_tiles(sz.width, back_in)
    one_onward, one_total, _ = scatter_group(
        wires, (2,), dy, lambda d, r: sz.part * r, near_one, mid, far_one, at, 64
    )
    order, o_send, o_relay, o_arrived, o_from = collect_col(
        wires, lambda c: xo.at[c], zo, ro, at, 10
    )
    for step in range(4):
        there = order[step]
        wires.arrived(xo.at[there], 48 + there, at.peer(4))
        mine = go[rows_at(pair * there, pair), lanes_at(sz.mixed * at.d, sz.mixed)]
        xo[there] = (mine.astype(jnp.float32) + xo[there].astype(jnp.float32)).astype(low)
        o_send(step)

    def relay_out(there):
        both = xo[there].astype(jnp.float32) + ro[...].astype(jnp.float32)
        xo[there] = both.astype(low)

    res_along()
    one_onward()
    o_heads(0)
    h1_back = one_total()
    through_norm, gain_one, shift_one = norm_back(
        h1_back, x_own[...].astype(jnp.float32), vec_rows[0:1]
    )
    va[0, 0:1] = gain_one
    va[0, 1:2] = shift_one
    for mask in range(1, 8):
        wires.copy(va.at[0], va.at[mask], at.peer(mask), 84 + mask)
    grad_along, grad_across, grad_finish = go_home(
        dx2[...] + through_norm, grad_stage, grad_all, grad_two, grad_home, 104
    )
    o_heads(1)
    u_relay(relay_of(ru, gu))
    o_heads(2)
    grad_along()
    res_across()
    o_relay(relay_out)
    o_heads(3)
    grad_across()

    brought = []

    def bring(c, landing, needed):
        made = load(landing.at[c], h2_t.at[pair * c : pair * (c + 1), 0 : sz.hidden], needed)
        brought.append((needed, made))

        @pl.when(jnp.logical_not(needed) & (at.c != c))
        def _():
            h2_t[pair * c : pair * (c + 1), 0 : sz.hidden] = jnp.zeros((pair, sz.hidden), low)

    def summed(lanes):
        result = jnp.zeros((pair, lanes.stop - lanes.start), jnp.float32)
        for c in range(4):
            result = result + h2_t[pair * c : pair * (c + 1), lanes].astype(jnp.float32)
        return result

    half_rows = sz.pieces

    def natural_rows(value):
        flipped = value.T
        return jnp.concatenate(
            [flipped[:, 0:half_rows], flipped[:, block : block + half_rows]], axis=1
        )

    def own_half(row):
        return jnp.where(at.d == 0, row[:, 0:half_rows], row[:, half_rows : 2 * half_rows])

    def all_brought():
        for needed, made in brought:
            run(needed, made.wait)
        del brought[:]

    for c in range(4):
        d_arrived(c)
        bring(c, zd, d_from(c))
    all_brought()
    for i in range(sz.hidden // 128):
        rows = min(128, 4 * sz.pieces - 128 * i)
        value = natural_rows(summed(slice(128 * i, 128 * (i + 1))))
        u[128 * i : 128 * i + rows, 0 : sz.share] = value[0:rows]
        if rows < 128:
            vec_out[5:6, 0:half_rows] = own_half(value[rows : rows + 1])
    down_out = load(u.at[0 : 4 * sz.pieces, 0:512], out_down)
    def relay_heads(there):
        xh[there] = (xh[there].astype(jnp.float32) + rh[...].astype(jnp.float32)).astype(low)

    h_relay(relay_heads)
    gu_own = load(gu.at[own], own_slot)
    for c in range(4):
        u_arrived(c)
        bring(c, zu, u_from(c))
    all_brought()
    gu_own.wait()
    theirs = rows_at(pair * at.c + block * (1 - at.d), block)

    def part_sum(side, lanes):
        result = jnp.zeros((block, sz.hidden), jnp.float32)
        for c in range(4):
            result = result + h2_t[rows_at(pair * c + block * side, block), lanes].astype(jnp.float32)
        return result

    every = slice(0, sz.hidden)
    gu[theirs] = part_sum(1 - at.d, every).astype(low)
    wires.copy(gu.at[theirs], xu, at.peer(4), 97)
    mine_sum = part_sum(at.d, every)
    down_out.wait()
    wires.arrived(xu, 97, at.peer(4))
    partner_sum = xu[...].astype(jnp.float32)
    for side in range(2):

        @pl.when(at.d == side)
        def _():
            both = (mine_sum, partner_sum) if side == 0 else (partner_sum, mine_sum)
            for j in range(4):
                rows = slice(block * j, block * (j + 1))
                for i in range(2):
                    u[rows, half_rows * i : half_rows * (i + 1)] = both[i][:, half_rows * j : half_rows * (j + 1)]

    bias_sum = mine_sum[half_rows : half_rows + 1]
    for j in range(4):
        vec_out[8 + j : 9 + j, 0:half_rows] = bias_sum[:, half_rows * j : half_rows * (j + 1)]
    up_out = load(u.at[0 : 4 * block, 0:512], out_up)

    for c in range(4):
        o_arrived(c)
        needed = o_from(c)
        made = load(zo.at[c], wd.at[pair * c : pair * (c + 1), 0 : sz.mixed], needed)
        brought.append((needed, made))

        @pl.when(jnp.logical_not(needed))
        def _():
            wd[pair * c : pair * (c + 1), 0 : sz.mixed] = jnp.zeros((pair, sz.mixed), low)

    all_brought()
    value = xo[at.c].astype(jnp.float32)
    for c in range(4):
        value = value + wd[pair * c : pair * (c + 1), 0 : sz.mixed].astype(jnp.float32)
    flipped = natural_rows(value)
    vec_out[4:5, 0:half_rows] = own_half(flipped[half_rows : half_rows + 1])
    flipped = flipped[0:block]
    for i in range(4):
        held = (dk_sum, dv_sum)[i // 2].at[block * (i % 2) : block * (i % 2 + 1)]
        lanes = min(128, sz.share - 128 * i)
        held[:, 0:lanes] = flipped[:, 128 * i : 128 * i + lanes]
        stay.append(load(held, out_out.at[:, 128 * i : 128 * (i + 1)]))

    for mask in range(1, 8):
        wires.arrived(va.at[mask], 84 + mask, at.peer(mask))
    vb[at.c] = functools.reduce(lambda a, b: a + b, [va[mask] for mask in range(8)])
    for c in range(4):
        wires.copy(vb.at[at.c], vb.at[at.c], at.along(c), 98 + at.c, at.c != c)

    for c in range(4):
        wires.arrived(vb.at[c], 98 + c, at.along(c), at.c != c)
    sums = vb[0] + vb[1] + vb[2] + vb[3]
    picked_sums = jnp.zeros((4, half_rows), jnp.float32)
    for i in range(8):
        cut = sums[0:4, block * i : block * i + half_rows]
        picked_sums = jnp.where(2 * at.c + at.d == i, cut, picked_sums)
    vec_out[0:4, 0:half_rows] = picked_sums
    res_finish()
    grad_finish()
    up_out.wait()
    rest_lanes = sz.heads - sz.hidden
    for c in range(4):
        h_arrived(c)
        needed = h_from(c)
        rows = slice(block * c, block * (c + 1))
        parts = (
            load(zh.at[c, :, 0 : sz.hidden], wd.at[rows], needed),
            load(zh.at[c, :, sz.hidden : sz.heads], wu.at[rows, 0:rest_lanes], needed),
        )
        brought += [(needed, made) for made in parts]

        @pl.when(jnp.logical_not(needed))
        def _():
            wd[rows] = jnp.zeros((block, sz.hidden), low)
            wu[rows, 0:rest_lanes] = jnp.zeros((block, rest_lanes), low)

    all_brought()
    left = xh[at.c, :, 0 : sz.hidden].astype(jnp.float32)
    right = xh[at.c, :, sz.hidden : sz.heads].astype(jnp.float32)
    for c in range(4):
        rows = slice(block * c, block * (c + 1))
        left = left + wd[rows].astype(jnp.float32)
        right = right + wu[rows, 0:rest_lanes].astype(jnp.float32)
    whole = jnp.concatenate([left, right], axis=1)
    for i in range(3):
        turned_columns = jnp.concatenate(
            [
                whole[:, main * i : main * (i + 1)],
                whole[:, 3 * main + slack * i : 3 * main + slack * (i + 1)],
            ],
            axis=1,
        )
        rows = slice(block * i, block * (i + 1))
        for r in range(4):

            @pl.when(at.r == r)
            def _():
                cut = slack * r
                value = turned_columns
                if cut:
                    value = jnp.concatenate([value[:, cut:], value[:, 0:cut]], axis=1)
                u[rows, 0 : sz.share] = value
                if i != 1:
                    vec_out[6 + i // 2 : 7 + i // 2, 0:half_rows] = own_half(
                        value[half_rows : half_rows + 1]
                    )

    stay.append(load(u.at[0 : 3 * block, 0:512], out_heads))
    for made in stay:
        made.wait()
    wires.close()


def update_kernel(sz, rates, grads, result_in, grad_in, weights, firsts, seconds, outs):
    down, out, up, heads, vectors = grads
    share, pieces, block = sz.share, sz.pieces, sz.block

    def move(i, place, gradient, decay):
        weight = weights[i][place]
        first_new = BETA_FIRST * firsts[i][place] + (1.0 - BETA_FIRST) * gradient
        second_new = BETA_SECOND * seconds[i][place] + (1.0 - BETA_SECOND) * (gradient * gradient)
        divisor = jnp.sqrt(second_new * (1.0 / (1.0 - BETA_SECOND**STEP))) + ADAM_EPSILON
        change = first_new * (rates[i] / (1.0 - BETA_FIRST**STEP)) / divisor
        weight_new = weight * (1.0 - rates[i] * decay) - change
        outs[3 * i + 2][place] = first_new
        outs[3 * i + 3][place] = second_new
        outs[3 * i + 4][place] = weight_new

    for part in range(3):
        move(0, part, heads[part, :, 0:share], MATRIX_DECAY)
    move(1, slice(None), out[:, 0:share], MATRIX_DECAY)
    move(2, slice(None), jnp.stack([up[j, :, 0:share] for j in range(4)], axis=1), MATRIX_DECAY)
    move(3, slice(None), down[:, 0:share], MATRIX_DECAY)

    @pl.when(pl.program_id(0) == 0)
    def _():
        for i, source, row in (
            (4, 0, 0), (4, 1, 1), (5, 4, 0), (5, 2, 1), (5, 3, 2), (5, 5, 3),
            (6, 6, 0), (6, 7, 1), (7, 8, 0), (7, 9, 1), (7, 10, 2), (7, 11, 3),
        ):
            move(i, row, vectors[source : source + 1, 0:pieces], 0.0)

    def plain(rows):
        rows = rows.astype(jnp.float32)
        return jnp.concatenate([rows[0:pieces], rows[block : block + pieces]], axis=0)

    @pl.when(pl.program_id(0) == 1)
    def _():
        outs[0][...] = plain(result_in[...]).astype(jnp.bfloat16)

    @pl.when(pl.program_id(0) == 2)
    def _():
        outs[1][...] = plain(grad_in[...])


def fused(
    tokens,
    cotangent,
    segments,
    weights,
    firsts,
    seconds,
):
    low = jnp.bfloat16
    seq, share = tokens.shape
    pieces = weights[1].shape[2]
    sz = Sizes(share, pieces, seq)
    block, main = sz.block, sz.main

    def views(arrays):
        heads, out, up, down, *small = arrays
        return (
            jnp.transpose(heads.reshape(pieces, 3, share), (1, 0, 2)),
            out.reshape(pieces, share),
            up.reshape(pieces, 4, share),
            down.reshape(4 * pieces, share),
            *[each.reshape(each.shape[0], 1, pieces) for each in small],
        )

    viewed = views(weights)
    labels = segments.reshape(1, -1)

    def made(*shape, dtype=low):
        return jax.ShapeDtypeStruct(shape, dtype)

    def held(*shape, dtype=low):
        return pltpu.VMEM(shape, dtype)

    w, seq, both, part = sz.width, sz.seq, sz.both, sz.part
    vmem, anywhere = pl.BlockSpec(memory_space=pltpu.VMEM), pl.BlockSpec(memory_space=pl.ANY)
    dma = pltpu.SemaphoreType.DMA
    f32 = jnp.float32
    wide = 3 * 128 + 128
    outs = pl.pallas_call(
        functools.partial(forward_kernel, sz),
        out_shape=(
            made(w, sz.heads),
            made(w, 2 * sz.mixed),
            made(w, sz.hidden),
            made(w, sz.hidden),
            made(w, seq),
            made(w, both),
            made(w, sz.hidden),
            made(both, w),
            made(both, sz.hidden, dtype=f32),
            made(both, sz.hidden),
            made(seq, main + 128),
            made(seq, main + 128),
            made(seq, main + 128),
            made(seq, 2 * sz.mixed),
            made(seq, 128, dtype=f32),
            made(part, w, dtype=f32),
            made(part, w),
            made(8, w, dtype=f32),
        ),
        in_specs=[anywhere] * 6 + [vmem] * 5,
        out_specs=[anywhere] * 18,
        scratch_shapes=[
            held(w, sz.heads),
            held(w, 2 * sz.mixed),
            held(w, sz.hidden),
            held(w, sz.hidden),
            held(w, seq),
            held(w, both),
            held(w, sz.hidden),
            held(w, both),
            held(both, w),
            held(both, sz.hidden, dtype=f32),
            held(both, sz.hidden),
            held(seq, main + 128),
            held(seq, main + 128),
            held(seq, main + 128),
            held(seq, 2 * sz.mixed),
            held(seq, 128, dtype=f32),
            held(part, w, dtype=f32),
            held(part, w),
            held(8, w, dtype=f32),
            held(w, seq),
            held(seq, w),
            held(both, w),
            held(seq, sz.heads),
            held(seq, main + 128),
            held(w, 128),
            held(seq, w),
            held(seq, 256),
            held(seq, 256),
            held(seq, 128),
            held(2, part, w),
            held(1, part, w),
            held(1, part, w),
            held(share, seq),
            held(share, seq),
            held(3, pieces, share, dtype=f32),
            held(pieces, share, dtype=f32),
            held(pieces, 4, share, dtype=f32),
            held(4 * pieces, share, dtype=f32),
            held(sz.pair, seq),
            held(sz.pair, seq),
            held(block, sz.hidden),
            held(seq, 1, dtype=f32),
            held(block, seq),
            held(block, seq),
            dma((160,)),
            dma((160,)),
            dma((48,)),
        ],
        compiler_params=pltpu.CompilerParams(
            collective_id=0, has_side_effects=True, vmem_limit_bytes=VMEM_BYTES
        ),
        cost_estimate=pl.CostEstimate(flops=10**10, bytes_accessed=10**8, transcendentals=10**6),
    )(tokens.T, cotangent.T, *viewed, labels)
    (wh, wo, wu, wd, h1_t, h2_t, gd, dy, u, gl, qw, kw, vw, a_nat, lse, x2, x_own, vec_rows) = outs
    outs = pl.pallas_call(
        functools.partial(backward_kernel, sz),
        out_shape=(
            made(4 * pieces, 512, dtype=f32),
            made(4 * block, 512, dtype=f32),
            made(block, 512, dtype=f32),
            made(3 * block, 512, dtype=f32),
            made(sz.pair, seq),
            made(sz.pair, seq),
            made(16, 256, dtype=f32),
            made(4, sz.pair, sz.hidden),
            made(4, sz.pair, sz.hidden),
            made(4, sz.pair, sz.mixed),
            made(4, block, sz.heads),
            made(4, block, seq),
            made(2, block, seq),
            made(4, block, seq),
            made(2, block, seq),
        ),
        in_specs=[anywhere] * 17 + [vmem] * 2,
        out_specs=[anywhere] * 6 + [vmem] + [anywhere] * 8,
        scratch_shapes=[
            held(sz.pair, sz.hidden),
            held(sz.pair, sz.hidden),
            held(sz.pair, sz.mixed),
            held(block, sz.heads),
            held(seq, main + 128),
            held(seq, main + 128),
            held(seq, main + 128),
            held(seq, 2 * sz.mixed),
            held(seq, 128, dtype=f32),
            held(part, w, dtype=f32),
            held(part, w),
            held(block, sz.hidden),
            held(both, w),
            held(w, both),
            held(both, sz.hidden, dtype=f32),
            held(both, sz.hidden),
            held(w, both),
            held(w, sz.hidden),
            held(w, sz.hidden),
            held(w, 2 * sz.mixed),
            held(w, sz.heads),
            held(part, w),
            held(both, sz.hidden),
            held(w, sz.heads),
            held(w, sz.hidden),
            held(w, 2 * sz.mixed),
            held(4, block, sz.heads),
            held(4, sz.pair, sz.mixed),
            held(4, part, w),
            held(3, part, w),
            held(4, part, w),
            held(3, part, w),
            held(2, part, w),
            held(1, part, w),
            held(3, part, w),
            held(seq, w),
            held(seq, 2 * sz.mixed),
            held(seq, 128, dtype=f32),
            held(seq, 128, dtype=f32),
            held(part, w, dtype=f32),
            held(seq, 256),
            held(seq, 256),
            held(seq, 128),
            held(seq, 128),
            held(seq, 1, dtype=f32),
            held(4, 2, block, part),
            held(4, 2, block, part),
            held(8, 8, w, dtype=f32),
            held(4, 8, w, dtype=f32),
            dma((128,)),
            dma((120,)),
            dma((80,)),
        ],
        compiler_params=pltpu.CompilerParams(
            collective_id=1, has_side_effects=True, vmem_limit_bytes=VMEM_BYTES
        ),
        cost_estimate=pl.CostEstimate(flops=2 * 10**10, bytes_accessed=10**8, transcendentals=10**6),
    )(
        dy, gd, u, gl, h2_t, wd, wu, wo, wh, h1_t,
        qw, kw, vw, a_nat, lse, x2, x_own, vec_rows, labels,
    )
    down, up, out, heads, result_home, grad_home, vectors = outs[:7]
    steps = 5
    chunk = pieces // steps

    def rows_of(shape, axis, size):
        block_shape = list(shape)
        block_shape[axis] = size
        return pl.BlockSpec(tuple(block_shape), lambda i: tuple(i if a == axis else 0 for a in range(len(shape))))

    def whole(shape):
        return pl.BlockSpec(tuple(shape), lambda i: (0,) * len(shape))

    matrix_specs = (
        rows_of((3, pieces, share), 1, chunk),
        rows_of((pieces, share), 0, chunk),
        rows_of((pieces, 4, share), 0, chunk),
        rows_of((4 * pieces, share), 0, 4 * chunk),
        *[whole(each.shape) for each in viewed[4:]],
    )
    grads = (down, out, up.reshape(4, block, 512), heads.reshape(3, block, 512), vectors)
    grad_specs = (
        rows_of((4 * pieces, 512), 0, 4 * chunk),
        rows_of((block, 512), 0, chunk),
        rows_of((4, block, 512), 1, chunk),
        rows_of((3, block, 512), 1, chunk),
        whole((16, 256)),
    )
    rates = (0.05, 0.2, 0.05, 0.025, 0.3, 0.3, 0.3, 0.3)
    arguments = (*grads, result_home, grad_home, *viewed, *views(firsts), *views(seconds))
    out_shape = [made(share, seq), made(share, seq, dtype=f32)]
    out_specs = [whole((share, seq)), whole((share, seq))]
    for each, spec in zip(viewed, matrix_specs, strict=True):
        out_shape += [jax.ShapeDtypeStruct(each.shape, f32)] * 3
        out_specs += [spec] * 3

    def update(*refs):
        ins, outs = refs[:31], refs[31:]
        update_kernel(sz, rates, ins[:5], ins[5], ins[6], ins[7:15], ins[15:23], ins[23:31], outs)

    updated = pl.pallas_call(
        update,
        grid=(steps,),
        out_shape=out_shape,
        in_specs=[*grad_specs, whole((sz.pair, seq)), whole((sz.pair, seq)), *matrix_specs * 3],
        out_specs=out_specs,
        compiler_params=pltpu.CompilerParams(vmem_limit_bytes=VMEM_BYTES),
        cost_estimate=pl.CostEstimate(
            flops=20 * 10**6, bytes_accessed=30 * 10**6, transcendentals=2 * 10**6
        ),
    )(*arguments)
    results = [updated[0].T, updated[1].T]
    for i, weight in enumerate(weights):
        for each in updated[2 + 3 * i : 5 + 3 * i]:
            if i == 0:
                each = jnp.transpose(each, (1, 0, 2))
            results.append(each.reshape(weight.shape))
    return tuple(results)


def normalize(inputs):
    center = jnp.mean(inputs, axis=1, keepdims=True)
    spread = jnp.mean(inputs * inputs, axis=1, keepdims=True) - center * center
    inverse = lax.rsqrt(spread + NORM_EPSILON)
    return ((inputs - center) * inverse, inverse)


def norm_pull(upstream, centered, inverse, gain):
    scaled = upstream * gain
    inner = (
        scaled
        - jnp.mean(scaled, axis=1, keepdims=True)
        - centered * jnp.mean(scaled * centered, axis=1, keepdims=True)
    )
    return inner * inverse


def crossed(blocks, n):
    pairs = [(i * n + j, j * n + i) for i in range(n) for j in range(n)]
    return lax.ppermute(blocks, ("row", "col"), pairs)


def scatter_rows(partial):
    return lax.psum_scatter(
        partial.astype(jnp.bfloat16), "row", scatter_dimension=0, tiled=True
    ).astype(jnp.float32)


def gather_rows(local):
    return lax.all_gather(local, "row", axis=0, tiled=True)


def split_heads(rows):
    return jnp.transpose(rows.reshape(rows.shape[0], -1, HD), (1, 0, 2))


def join_heads(values):
    return jnp.transpose(values, (1, 0, 2)).reshape(values.shape[1], -1)


def scores_of(queries, keys, allowed):
    scores = jnp.einsum(
        "hqe,hke->hqk", queries, keys, preferred_element_type=jnp.float32
    ) * HD ** (-0.5)
    return jnp.where(allowed[None], scores, MASKED)


def gathered(
    tokens,
    cotangent,
    segments,
    w_heads,
    w_out,
    w_up,
    w_down,
    norm_vectors,
    width_vectors,
    attend_bias,
    hidden_vectors,
):
    n_dp, n_row, n_col = (lax.axis_size(name) for name in ("dp", "row", "col"))
    row = lax.axis_index("row")
    low = jnp.bfloat16
    share = tokens.shape[1]
    width = share * n_col
    seq = tokens.shape[0]
    part = seq // n_row
    near = HEADS // n_row
    window = (HEADS - near * (n_row - 1)) * HD
    step = near * HD
    edge = width - (share + step * (n_row - 1)) if n_row > 1 else 0
    edge = window - share
    to_next = [(i, i + 1) for i in range(n_row - 1)]
    to_last = [(i + 1, i) for i in range(n_row - 1)]
    offset = edge - (share - step) * row

    vectors = jnp.concatenate(
        [
            norm_vectors.reshape(2, -1),
            width_vectors.reshape(4, -1),
            attend_bias.reshape(2, -1),
            hidden_vectors.reshape(4, -1),
        ]
    ).astype(low)
    vectors = lax.all_gather(vectors, ("row", "col", "dp"), axis=0, tiled=False)
    vectors = vectors.reshape(n_row, n_col, n_dp, 12, -1).astype(jnp.float32)
    by_col = jnp.transpose(vectors[0], (2, 0, 1, 3)).reshape(12, width)
    by_row = jnp.transpose(vectors[:, 0], (2, 0, 1, 3)).reshape(12, width)
    gain_one, shift_one, bias_out, gain_two, shift_two, bias_down = (by_col[i] for i in range(6))
    zeros = jnp.zeros((1, window), jnp.float32)
    attend_rows = lax.dynamic_slice_in_dim(by_row[6:8], row * step, window, axis=1)
    heads_bias = jnp.concatenate([attend_rows[0:1], zeros, attend_rows[1:2]]).reshape(-1)
    unit_bias = lax.dynamic_slice_in_dim(by_row[8:12], row * share, share, axis=1).reshape(-1)

    own = w_heads.astype(low).reshape(-1, 3, share)
    passed = lax.ppermute(own[:, :, share - edge :], "row", to_next)
    own = jnp.concatenate([passed, own, jnp.zeros_like(passed)], axis=2)
    own = lax.dynamic_slice_in_dim(own, offset, window, axis=2).reshape(-1, 3 * window)
    heads_matrix = lax.all_gather(own, ("col", "dp"), axis=0, tiled=True)
    out_matrix = lax.all_gather(w_out.astype(low).reshape(-1, share), ("col", "dp"), axis=0)
    out_matrix = jnp.transpose(out_matrix.reshape(n_col, share, share), (1, 0, 2))
    out_matrix = out_matrix.reshape(share, width)
    passed = lax.ppermute(out_matrix[share - edge :], "row", to_next)
    out_matrix = jnp.concatenate([passed, out_matrix, jnp.zeros_like(passed)])
    out_matrix = lax.dynamic_slice_in_dim(out_matrix, offset, window)
    owned = (jnp.arange(window) < step) | (row == n_row - 1)
    out_matrix = jnp.where(owned[:, None], out_matrix, jnp.zeros_like(out_matrix))
    up_matrix = lax.all_gather(
        w_up.astype(low).reshape(-1, 4 * share), ("col", "dp"), axis=0, tiled=True
    )
    down_matrix = lax.all_gather(w_down.astype(low).reshape(4, -1, share), ("col", "dp"), axis=0)
    down_matrix = down_matrix.reshape(n_col, n_dp, 4, -1, share)
    down_matrix = jnp.transpose(down_matrix, (2, 1, 3, 0, 4)).reshape(4 * share, width)

    inputs_low = lax.all_gather(crossed(tokens, n_row), "row", axis=1, tiled=True)
    upstream = lax.all_gather(crossed(cotangent, n_row), "row", axis=1, tiled=True)
    inputs = inputs_low.astype(jnp.float32)
    centered_one, inverse_one = normalize(inputs)
    normed_one = (centered_one * gain_one + shift_one).astype(low)
    projected = (times(normed_one, heads_matrix) + heads_bias).astype(low)
    queries, keys, values = (
        split_heads(projected[:, i * window : (i + 1) * window]) for i in range(3)
    )
    labels = lax.dynamic_slice_in_dim(segments, lax.axis_index("col") * seq, seq)
    places = jnp.arange(seq, dtype=jnp.int32)
    allowed = (labels[:, None] == labels[None, :]) & (places[:, None] >= places[None, :])
    scores = scores_of(queries, keys, allowed)
    highest = jnp.max(scores, axis=-1, keepdims=True)
    log_total = highest + jnp.log(jnp.sum(jnp.exp(scores - highest), axis=-1, keepdims=True))
    soft = jnp.exp(scores - log_total).astype(low)
    mixed = jnp.einsum("hqk,hke->hqe", soft, values, preferred_element_type=jnp.float32)
    mixed = join_heads(mixed.astype(low))
    branch = scatter_rows(times(mixed, out_matrix))
    mine = row * part
    middle = lax.dynamic_slice_in_dim(inputs, mine, part) + (branch + bias_out)
    centered_two, inverse_two = normalize(middle)
    normed_two = gather_rows((centered_two * gain_two + shift_two).astype(low))
    hidden = times(normed_two, up_matrix) + unit_bias
    activated, smooth_pull = jax.vjp(smooth, hidden)
    activated = activated.astype(low)
    result = (middle + (scatter_rows(times(activated, down_matrix)) + bias_down)).astype(low)

    down_back = times_flipped(upstream, down_matrix)
    grad_down = times_outer(activated, upstream)
    hidden_back = smooth_pull(down_back)[0].astype(low)
    grad_up = times_outer(normed_two, hidden_back)
    unit_sum = jnp.sum(hidden_back, axis=0, dtype=jnp.float32)
    normed_two_back = scatter_rows(times_flipped(hidden_back, up_matrix))
    upstream_own = lax.dynamic_slice_in_dim(upstream, mine, part).astype(jnp.float32)
    middle_back = upstream_own + norm_pull(normed_two_back, centered_two, inverse_two, gain_two)
    branch_own = middle_back.astype(low)
    branch_back = gather_rows(branch_own)
    mixed_back = times_flipped(branch_back, out_matrix).astype(low)
    grad_out = times_outer(mixed, branch_back)
    mixed_back = split_heads(mixed_back)
    scores_again = scores_of(queries, keys, allowed)
    soft = jnp.exp(scores_again - log_total)
    soft_back = jnp.einsum("hqe,hke->hqk", mixed_back, values, preferred_element_type=jnp.float32)
    row_inner = jnp.sum(soft_back * soft, axis=-1, keepdims=True)
    score_back = (soft * (soft_back - row_inner)).astype(low)
    query_back = jnp.einsum(
        "hqk,hke->hqe", score_back, keys, preferred_element_type=jnp.float32
    ) * HD ** (-0.5)
    key_back = jnp.einsum(
        "hqk,hqe->hke", score_back, queries, preferred_element_type=jnp.float32
    ) * HD ** (-0.5)
    value_back = jnp.einsum(
        "hqk,hqe->hke", soft.astype(low), mixed_back, preferred_element_type=jnp.float32
    )
    heads_back = jnp.concatenate(
        [join_heads(each.astype(low)) for each in (query_back, key_back, value_back)], axis=1
    )
    heads_sum = jnp.sum(heads_back, axis=0, dtype=jnp.float32)
    normed_one_back = scatter_rows(times_flipped(heads_back, heads_matrix))
    grad_heads = times_outer(normed_one, heads_back)
    centered_own = lax.dynamic_slice_in_dim(centered_one, mine, part)
    inverse_own = lax.dynamic_slice_in_dim(inverse_one, mine, part)
    input_back = middle_back + norm_pull(normed_one_back, centered_own, inverse_own, gain_one)

    def homeward(own):
        own = lax.all_to_all(own, "row", split_axis=1, concat_axis=0, tiled=True)
        return crossed(own, n_row)

    result_tokens = homeward(result)
    input_gradient = homeward(input_back.astype(low)).astype(jnp.float32)

    by_token = jnp.stack(
        [
            jnp.sum(normed_one_back * centered_own, axis=0),
            jnp.sum(normed_one_back, axis=0),
            jnp.sum(branch_own.astype(jnp.float32), axis=0),
            jnp.sum(normed_two_back * centered_two, axis=0),
            jnp.sum(normed_two_back, axis=0),
            jnp.sum(upstream_own, axis=0),
        ]
    )
    owned_rows = jnp.where(owned, heads_sum.reshape(3, window)[0::2], 0.0)
    by_unit = jnp.concatenate(
        [
            lax.dynamic_update_slice_in_dim(
                jnp.zeros((2, width), jnp.float32), owned_rows, row * step, axis=1
            ),
            lax.dynamic_update_slice_in_dim(
                jnp.zeros((4, width), jnp.float32), unit_sum.reshape(4, share), row * share, axis=1
            ),
        ]
    )
    sums = lax.psum(jnp.concatenate([by_token, by_unit]), ("dp", "row", "col"))
    pieces = share // n_dp
    inner = lax.axis_index("dp") * pieces
    col_sums = lax.dynamic_slice_in_dim(sums, lax.axis_index("col") * share + inner, pieces, axis=1)
    row_sums = lax.dynamic_slice_in_dim(sums, row * share + inner, pieces, axis=1)

    both = ("col", "dp")

    def to_owner(gradient):
        return lax.psum_scatter(gradient, both, scatter_dimension=0, tiled=True)

    got_heads = to_owner(grad_heads.astype(low)).reshape(pieces, 3, window)
    got_heads = jnp.where(owned, got_heads, jnp.zeros_like(got_heads))
    passed = lax.ppermute(got_heads[:, :, :edge], "row", to_last)
    got_heads = jnp.concatenate([got_heads, jnp.zeros_like(passed)], axis=2)
    got_heads = lax.dynamic_slice_in_dim(got_heads, edge - offset, share, axis=2)
    passed = jnp.concatenate([jnp.zeros((pieces, 3, share), low), passed, jnp.zeros_like(passed)], axis=2)
    got_heads = got_heads + lax.dynamic_slice_in_dim(passed, share - step + edge - offset, share, axis=2)
    low_out = jnp.where(owned[:, None], grad_out, 0.0).astype(low)
    passed = lax.ppermute(low_out[:edge], "row", to_last)
    low_out = jnp.concatenate([low_out, jnp.zeros_like(passed)])
    low_out = lax.dynamic_slice_in_dim(low_out, edge - offset, share)
    passed = jnp.concatenate([jnp.zeros((share, width), low), passed, jnp.zeros_like(passed)])
    low_out = low_out + lax.dynamic_slice_in_dim(passed, share - step + edge - offset, share)
    low_out = jnp.transpose(low_out.reshape(n_dp, pieces, n_col, share), (2, 0, 1, 3))
    got_out = to_owner(low_out.reshape(-1, share))
    got_up = to_owner(grad_up.astype(low))
    low_down = grad_down.astype(low).reshape(4, n_dp, pieces, n_col, share)
    low_down = jnp.transpose(low_down, (3, 1, 0, 2, 4)).reshape(-1, share)
    got_down = to_owner(low_down)

    reduced = [
        each.astype(jnp.float32).reshape(like.shape)
        for each, like in (
            (got_heads, w_heads),
            (got_out, w_out),
            (got_up, w_up),
            (got_down, w_down),
            (col_sums[0:2], norm_vectors),
            (col_sums[2:6], width_vectors),
            (row_sums[6:8], attend_bias),
            (row_sums[8:12], hidden_vectors),
        )
    ]
    return result_tokens, input_gradient, reduced


def per_device(
    tokens,
    cotangent,
    segments,
    w_heads,
    w_out,
    w_up,
    w_down,
    norm_vectors,
    width_vectors,
    attend_bias,
    hidden_vectors,
    drift_heads,
    drift_out,
    drift_up,
    drift_down,
    drift_norm,
    drift_width,
    drift_attend,
    drift_hidden,
    power_heads,
    power_out,
    power_up,
    power_down,
    power_norm,
    power_width,
    power_attend,
    power_hidden,
):
    weights = (
        w_heads,
        w_out,
        w_up,
        w_down,
        norm_vectors,
        width_vectors,
        attend_bias,
        hidden_vectors,
    )
    firsts = (
        drift_heads,
        drift_out,
        drift_up,
        drift_down,
        drift_norm,
        drift_width,
        drift_attend,
        drift_hidden,
    )
    seconds = (
        power_heads,
        power_out,
        power_up,
        power_down,
        power_norm,
        power_width,
        power_attend,
        power_hidden,
    )
    sizes = tuple(lax.axis_size(name) for name in ("dp", "row", "col"))
    if sizes == (2, 4, 4):
        return fused(tokens, cotangent, segments, weights, firsts, seconds)
    result_tokens, input_gradient, reduced = gathered(tokens, cotangent, segments, *weights)
    heads_up = adam(w_heads, reduced[0], drift_heads, power_heads, 0.05, MATRIX_DECAY)
    out_up = adam(w_out, reduced[1], drift_out, power_out, 0.2, MATRIX_DECAY)
    up_up = adam(w_up, reduced[2], drift_up, power_up, 0.05, MATRIX_DECAY)
    down_up = adam(w_down, reduced[3], drift_down, power_down, 0.025, MATRIX_DECAY)
    norm_up = adam(norm_vectors, reduced[4], drift_norm, power_norm, 0.3, 0.0)
    width_up = adam(width_vectors, reduced[5], drift_width, power_width, 0.3, 0.0)
    attend_up = adam(attend_bias, reduced[6], drift_attend, power_attend, 0.3, 0.0)
    hidden_up = adam(hidden_vectors, reduced[7], drift_hidden, power_hidden, 0.3, 0.0)
    return (
        result_tokens,
        input_gradient,
        heads_up[0],
        heads_up[1],
        heads_up[2],
        out_up[0],
        out_up[1],
        out_up[2],
        up_up[0],
        up_up[1],
        up_up[2],
        down_up[0],
        down_up[1],
        down_up[2],
        norm_up[0],
        norm_up[1],
        norm_up[2],
        width_up[0],
        width_up[1],
        width_up[2],
        attend_up[0],
        attend_up[1],
        attend_up[2],
        hidden_up[0],
        hidden_up[1],
        hidden_up[2],
    )


def solution(mesh):
    return jax.shard_map(
        per_device,
        mesh=mesh,
        in_specs=(
            P(("dp", "row"), "col"),
            P(("dp", "row"), "col"),
            P("dp"),
            P("col", "dp", None, None, "row"),
            P("row", "dp", None, "col"),
            P("col", "dp", None, None, "row"),
            P(None, "row", "dp", None, "col"),
            P(None, "col", "dp", None),
            P(None, "col", "dp", None),
            P(None, "row", "dp", None),
            P(None, "row", "dp", None),
            P("col", "dp", None, None, "row"),
            P("row", "dp", None, "col"),
            P("col", "dp", None, None, "row"),
            P(None, "row", "dp", None, "col"),
            P(None, "col", "dp", None),
            P(None, "col", "dp", None),
            P(None, "row", "dp", None),
            P(None, "row", "dp", None),
            P("col", "dp", None, None, "row"),
            P("row", "dp", None, "col"),
            P("col", "dp", None, None, "row"),
            P(None, "row", "dp", None, "col"),
            P(None, "col", "dp", None),
            P(None, "col", "dp", None),
            P(None, "row", "dp", None),
            P(None, "row", "dp", None),
        ),
        out_specs=(
            P(("dp", "row"), "col"),
            P(("dp", "row"), "col"),
            P("col", "dp", None, None, "row"),
            P("col", "dp", None, None, "row"),
            P("col", "dp", None, None, "row"),
            P("row", "dp", None, "col"),
            P("row", "dp", None, "col"),
            P("row", "dp", None, "col"),
            P("col", "dp", None, None, "row"),
            P("col", "dp", None, None, "row"),
            P("col", "dp", None, None, "row"),
            P(None, "row", "dp", None, "col"),
            P(None, "row", "dp", None, "col"),
            P(None, "row", "dp", None, "col"),
            P(None, "col", "dp", None),
            P(None, "col", "dp", None),
            P(None, "col", "dp", None),
            P(None, "col", "dp", None),
            P(None, "col", "dp", None),
            P(None, "col", "dp", None),
            P(None, "row", "dp", None),
            P(None, "row", "dp", None),
            P(None, "row", "dp", None),
            P(None, "row", "dp", None),
            P(None, "row", "dp", None),
            P(None, "row", "dp", None),
        ),
        check_vma=False,
    )
```

```python
import functools

import jax
import jax.numpy as jnp
from jax import lax
from jax.experimental import pallas as pl
from jax.experimental.pallas import tpu as pltpu
from jax.sharding import PartitionSpec as P

HEADS = 25
HD = 64
TOK_DEV = 128
STEP = 10


NORM_EPSILON = 1e-05
BETA_FIRST = 0.9
BETA_SECOND = 0.999
ADAM_EPSILON = 1e-08
MATRIX_DECAY = 0.1
MASKED = -1e30
ROOT = (2.0 / 3.141592653589793) ** 0.5
CUBIC = 0.044715
VMEM_BYTES = 66 * 1024 * 1024


def adam(weight, gradient, first, second, rate, decay):
    first_new = BETA_FIRST * first + (1.0 - BETA_FIRST) * gradient
    second_new = BETA_SECOND * second + (1.0 - BETA_SECOND) * gradient * gradient
    corrected = first_new / (1.0 - BETA_FIRST**STEP)
    divisor = jnp.sqrt(second_new / (1.0 - BETA_SECOND**STEP)) + ADAM_EPSILON
    return (first_new, second_new, weight - rate * (corrected / divisor + decay * weight))


def smooth(values):
    return jax.nn.gelu(values, approximate=True)


def ceil_to(count, unit):
    return -(-count // unit) * unit


class Sizes:
    def __init__(self, share, pieces, seq):
        self.share = share
        self.pieces = pieces
        self.block = ceil_to(pieces, 16)
        self.pair = 2 * self.block
        self.width = 4 * self.pair
        self.seq = seq
        self.part = seq // 4
        self.both = 2 * seq
        self.main = (HEADS // 4) * HD
        self.slack = share - self.main
        self.heads = ceil_to(3 * share, 256)
        self.mixed = ceil_to(pieces + 1, 128)
        self.hidden = ceil_to(4 * pieces + 1, 128)
        self.tiles = self.width // 128


class Place:
    def __init__(self):
        self.d, self.r, self.c = (lax.axis_index(name) for name in ("dp", "row", "col"))
        self.y, self.k = self.r // 2, self.r % 2

    def plane(self, mask):
        d = 1 - self.d if mask & 4 else self.d
        y = 1 - self.y if mask & 2 else self.y
        k = 1 - self.k if mask & 1 else self.k
        return d, 2 * y + k

    def peer(self, mask):
        d, r = self.plane(mask)
        return (d, r, self.c)

    def along(self, c):
        return (self.d, self.r, c)


def run(when, action):
    if when is None:
        action()
    else:
        pl.when(when)(action)


class Wires:
    def __init__(self, sends, arrivals):
        self.sends, self.arrivals = sends, arrivals
        self.used = 0
        self.open = []

    def make(self, source, target, index, slot, device):
        return pltpu.make_async_remote_copy(
            src_ref=source,
            dst_ref=target,
            send_sem=self.sends.at[index],
            recv_sem=self.arrivals.at[slot],
            device_id=device,
            device_id_type=pl.DeviceIdType.MESH,
        )

    def copy(self, source, target, device, slot, when=None):
        made = self.make(source, target, self.used, slot, device)
        self.used += 1
        run(when, made.start)
        item = (when, made)
        self.open.append(item)
        return item

    def arrived(self, target, slot, device, when=None):
        run(when, self.make(target, target, 0, slot, device).wait_recv)

    def close(self, some=None):
        for item in self.open if some is None else some:
            run(item[0], item[1].wait_send)
        self.open = [] if some is None else [o for o in self.open if all(o is not s for s in some)]


def greet(at, diagonal):
    barrier = pltpu.get_barrier_semaphore()

    def signal(device):
        pl.semaphore_signal(
            barrier, inc=1, device_id=device, device_id_type=pl.DeviceIdType.MESH
        )

    for mask in range(1, 8):
        signal(at.peer(mask))
    for c in range(4):
        run(at.c != c, functools.partial(signal, (at.d, at.r, c)))
        if diagonal:
            run(at.c != c, functools.partial(signal, (1 - at.d, at.r, c)))
    run(at.r != at.c, functools.partial(signal, (at.d, at.c, at.r)))
    pl.semaphore_wait(barrier, (13 if diagonal else 10) + jnp.where(at.r != at.c, 1, 0))


def rows_at(start, size):
    return pl.ds(pl.multiple_of(start, 16), size)


def lanes_at(start, size):
    return pl.ds(pl.multiple_of(start, 128), size)


def choose(shape, source):
    rows = lax.broadcasted_iota(jnp.int32, shape, 0)
    wanted = source(lax.broadcasted_iota(jnp.int32, shape, 1))
    return (rows == wanted).astype(jnp.bfloat16)


def edge_source(column):
    part, place = column // HD, column % HD
    wanted = jnp.where(place >= 16, 128 * part + place - 16, 384 + 16 * part + place)
    return jnp.where(part < 3, wanted, -1)


def spread_source(column):
    part, place = column // 128, column % 128
    return jnp.where(place < HD, HD * part + place, -1)


def picked(values, table):
    return jnp.dot(values, table, preferred_element_type=jnp.float32).astype(jnp.bfloat16)


def times(left, right):
    return jnp.dot(left, right, preferred_element_type=jnp.float32)


def times_flipped(left, right):
    return lax.dot_general(
        left, right, (((1,), (1,)), ((), ())), preferred_element_type=jnp.float32
    )


def times_outer(left, right):
    return lax.dot_general(
        left, right, (((0,), (0,)), ((), ())), preferred_element_type=jnp.float32
    )


def over_tiles(total, action, tile=256):
    @pl.loop(0, total // tile)
    def _(i):
        action(i * tile, tile)

    if total % tile:
        action(total - total % tile, total % tile)


def turned(values):
    return values.astype(jnp.float32).T


def gather_group(wires, masks, region, at, base):
    own = region(*at.plane(0))
    sent = [wires.copy(own, own, at.peer(mask), base + mask) for mask in (1, *masks)]

    def finish():
        for mask in masks:
            there = region(*at.plane(mask))
            wires.arrived(there, base + mask, at.peer(mask))
            sent.append(wires.copy(there, there, at.peer(1), base + mask + 1))
        for mask in (0, *masks):
            there = region(*at.plane(mask | 1))
            wires.arrived(there, base + (mask | 1), at.peer(1))

    return finish, sent


def cross_over(wires, home, landing, region, at, base):
    rows = home.shape[0] // 2
    wires.copy(home.at[rows_at(rows * (1 - at.y), rows)], landing, at.peer(2), base)
    target = region(at.c, at.d, at.y)

    def along(source, s):
        wires.copy(source, target, at.along(s), base + 1 + at.c, s != at.c)

        @pl.when(s == at.c)
        def _():
            target[...] = source[...]

    along(home.at[rows_at(rows * at.y, rows)], at.r)

    def onward():
        wires.arrived(landing, base, at.peer(2))
        along(landing, 2 * (1 - at.y) + at.k)

    def finish():
        for c in range(4):
            needed = (at.k == at.c % 2) & (at.c != c)
            wires.arrived(region(c, at.d, at.y), base + 1 + c, at.along(c), needed)

    return onward, finish


def share_pieces(wires, masks, region, at, base):
    holds = at.k == at.c % 2
    near = base + 4 * len(masks)

    def place(mask):
        d, r = at.plane(mask)
        return d, r // 2

    for c in range(4):
        own = region(c, *place(0))
        for i, mask in enumerate(masks):
            wires.copy(own, own, at.peer(mask), base + 4 * i + c, holds)
    for c in range(4):
        own = region(c, *place(0))
        wires.copy(own, own, at.peer(1), near + c, holds)

    def finish():
        for i, mask in enumerate(masks):
            for c in range(4):
                there = region(c, *place(mask))
                wires.arrived(there, base + 4 * i + c, at.peer(mask), holds)
                wires.copy(there, there, at.peer(1), near + 4 * (i + 1) + c, holds)
        for i, mask in enumerate((0, *masks)):
            for c in range(4):
                there = region(c, *place(mask))
                wires.arrived(there, near + 4 * i + c, at.peer(1), jnp.logical_not(holds))

    return finish


def scatter_group(wires, masks, partial, chunk, near, mid, far, at, base):
    sent = []
    for i, mask in enumerate((0, *masks)):
        rows = rows_at(chunk(*at.plane(mask | 1)), near.shape[1])
        sent.append(wires.copy(partial.at[rows], near.at[i], at.peer(1), base + i))

    def rows_of(mask):
        return rows_at(chunk(*at.plane(mask)), near.shape[1])

    def onward():
        for i, mask in enumerate((0, *masks)):
            wires.arrived(near.at[i], base + i, at.peer(1))
        for i, mask in enumerate(masks):
            both = partial[rows_of(mask)].astype(jnp.float32) + near[i + 1].astype(jnp.float32)
            mid[i] = both.astype(jnp.bfloat16)
            sent.append(wires.copy(mid.at[i], far.at[i], at.peer(mask), base + 4 + i))

    def total():
        for i, mask in enumerate(masks):
            wires.arrived(far.at[i], base + 4 + i, at.peer(mask))
        result = partial[rows_of(0)].astype(jnp.float32) + near[0].astype(jnp.float32)
        for i in range(len(masks)):
            result = result + far[i].astype(jnp.float32)
        return result

    return onward, total, sent


def spread_col(wires, region, at, base, wait=False):
    own = region(at.c)

    def send(distance):
        for delta in (distance, -distance):
            there = at.c + delta
            wires.copy(own, own, at.along(there), base + at.c, (there >= 0) & (there < 4))

    if not wait:
        send(2)
        send(1)

    def relay():
        for here, start, end in ((2, 0, 3), (1, 3, 0)):
            block = region(start)
            wires.arrived(block, base + start, at.along(start), at.c == here)
            wires.copy(block, block, at.along(end), base + start, at.c == here)

    def finish():
        for c in range(4):
            needed = at.c != c
            if c == 0:
                needed = needed & (at.c != 2)
            if c == 3:
                needed = needed & (at.c != 1)
            wires.arrived(region(c), base + c, at.along(c), needed)

    return (send, relay, finish) if wait else (relay, finish)


def collect_col(wires, piece, landing, rest, at, base, direct=None):
    low_end, high_end = at.c == 0, at.c == 3
    ends = low_end | high_end
    via = jnp.where(low_end, 1, 2)

    def pick(*choices):
        return jnp.where(
            low_end,
            choices[0],
            jnp.where(at.c == 1, choices[1], jnp.where(high_end, choices[3], choices[2])),
        )

    order = (pick(3, 0, 3, 0), pick(2, 2, 1, 1), pick(1, 3, 0, 2), at.c)
    target = landing.at[at.c]

    def send(step):
        there = order[step]
        block = (direct or piece)(there)
        if step == 0:
            wires.copy(block, rest, at.along(via), base + 4, ends)
            wires.copy(block, target, at.along(there), base + at.c, jnp.logical_not(ends))
        elif step == 1:
            wires.copy(block, target, at.along(there), base + at.c)
        elif step == 2:
            wires.copy(block, target, at.along(there), base + at.c, ends)

    def relay(add):
        @pl.when(jnp.logical_not(ends))
        def _():
            wires.make(rest, rest, 0, base + 4, at.along(0)).wait_recv()
            add(order[2])

        wires.copy(piece(order[2]), target, at.along(order[2]), base + at.c, jnp.logical_not(ends))

    def arrived(c):
        wires.arrived(landing.at[c], base + c, at.along(c), sent_from(c))

    def sent_from(c):
        here = at.c != c
        if c in (0, 3):
            here = here & (at.c != 3 - c)
        return here

    return order, send, relay, arrived, sent_from


def forward_kernel(
    sz,
    x_home_in,
    dy_home_in,
    w_heads,
    w_out,
    w_up,
    w_down,
    norm_vectors,
    width_vectors,
    attend_bias,
    hidden_vectors,
    segments,
    wh_out,
    wo_out,
    wu_out,
    wd_out,
    h1_t_out,
    h2_t_out,
    gd_out,
    dy_out,
    u_out,
    gl_out,
    qw_out,
    kw_out,
    vw_out,
    a_nat_out,
    lse_out,
    x2_out,
    x_own_out,
    vec_rows_out,
    wh,
    wo,
    wu,
    wd,
    h1_t,
    h2_t,
    gd,
    dy_t,
    dy,
    u,
    gl,
    qw,
    kw,
    vw,
    a_nat,
    lse,
    x2,
    x_own,
    vec_rows,
    x_t,
    h1,
    h2,
    own_qkv,
    aw,
    vec,
    part,
    edge_out,
    edge_in,
    edge_back,
    near,
    mid,
    far,
    x_raw,
    dy_raw,
    heads_raw,
    out_raw,
    up_raw,
    down_raw,
    x_home,
    dy_home,
    wu_own,
    col_labels,
    x_half,
    dy_half,
    sends,
    arrivals,
    locals_,
):
    at = Place()
    wires = Wires(sends, arrivals)
    low = jnp.bfloat16
    pair, block, pieces = sz.pair, sz.block, sz.pieces
    fetched = []
    for i, (source, target) in enumerate(
        (
            (x_home_in, x_raw),
            (w_heads, heads_raw),
            (w_up, up_raw),
            (w_out, out_raw),
            (w_down, down_raw),
            (dy_home_in, dy_raw),
        )
    ):
        fetched.append(pltpu.make_async_copy(source, target, locals_.at[40 + i]))
        fetched[i].start()
    row_labels = segments.at[:, lanes_at(sz.seq * at.c, sz.seq)]

    def halves(value, target):
        value = value.astype(jnp.float32)
        gap = jnp.zeros((block - pieces, value.shape[1]), jnp.float32)
        parts = [value[0:pieces], gap, value[pieces : 2 * pieces], gap]
        target[...] = jnp.concatenate(parts, axis=0).astype(low)

    def quarter(row):
        return row.astype(low).astype(jnp.float32) * 0.25

    def placed(row):
        both = jnp.concatenate([row, row], axis=1)
        half_of = lax.broadcasted_iota(jnp.int32, both.shape, 1) // pieces
        return jnp.where(half_of == at.d, both, 0.0)

    def with_row(value, row):
        gap = jnp.zeros((block - pieces - 1, value.shape[1]), jnp.float32)
        return jnp.concatenate([value, row, gap], axis=0)

    flat = jnp.concatenate(
        [norm_vectors[0], norm_vectors[1], width_vectors[1], width_vectors[2]], axis=0
    )
    flat = jnp.concatenate([flat, jnp.zeros((124, pieces), jnp.float32)], axis=0)
    flat = jnp.concatenate([flat, jnp.zeros((128, 256 - pieces), jnp.float32)], axis=1)
    where_row = lax.broadcasted_iota(jnp.int32, flat.shape, 0)
    where_lane = lax.broadcasted_iota(jnp.int32, flat.shape, 1)
    carrier = (where_lane == pieces) & ((where_row == 1) | (where_row == 3))
    own_rows = rows_at(pair * at.c + block * at.d, block)
    vec[own_rows] = jnp.where(carrier, 1.0, flat).T[0:block].astype(low)
    fetched[0].wait()
    halves(x_raw[...], x_home)
    greet(at, False)

    def x_piece(c, d, y):
        return x_t.at[rows_at(pair * c + block * y, block)]

    def dy_piece(c, d, y):
        return dy_t.at[rows_at(pair * c + block * y, block), lanes_at(sz.seq * d, sz.seq)]

    used = [0]

    def flush(source, target):
        made = pltpu.make_async_copy(source, target, locals_.at[used[0]])
        used[0] += 1
        made.start()
        flushed.append(made)

    flushed = []

    def vec_block(d, c):
        return vec.at[rows_at(pair * c + block * d, block)]

    def wh_block(d):
        return lambda c: wh.at[rows_at(pair * c + block * d, block)]

    def wo_block(d):
        return lambda c: wo.at[rows_at(pair * c, pair), lanes_at(sz.mixed * d, sz.mixed)]

    def wu_block(d):
        return lambda c: wu.at[rows_at(pair * c + block * d, block)]

    def wd_block(half):
        return lambda c: wd.at[rows_at(pair * c + block * half, block)]

    x_onward, x_crossed = cross_over(wires, x_home, x_half, x_piece, at, 96)
    for c in range(4):
        wires.copy(vec_block(at.d, at.c), vec_block(at.d, at.c), at.along(c), 2 + at.c, at.c != c)
    wires.copy(vec_block(at.d, at.c), vec_block(at.d, at.c), at.peer(4), 6 + at.c)

    fetched[1].wait()
    for r in range(4):

        @pl.when(at.r == r)
        def _():
            cut = sz.share - sz.slack * r
            tails = []
            for i in range(3):
                value = heads_raw[i]
                row = jnp.zeros((1, sz.share), jnp.float32)
                if i != 1:
                    row = placed(quarter(attend_bias[i // 2]))
                value = with_row(value, row)
                if r:
                    value = jnp.concatenate([value[:, cut:], value[:, 0:cut]], axis=1)
                wh[own_rows, sz.main * i : sz.main * (i + 1)] = value[:, 0 : sz.main].astype(low)
                tails.append(value[:, sz.main :])
            tails.append(jnp.zeros((block, sz.heads - 3 * sz.share), jnp.float32))
            wh[own_rows, 3 * sz.main : sz.heads] = jnp.concatenate(tails, axis=1).astype(low)

    x_onward()
    wh_relay, wh_done = spread_col(wires, wh_block(at.d), at, 20)
    wires.copy(wh_block(at.d)(at.c), wh_block(at.d)(at.c), at.peer(4), 24 + at.c)

    fetched[2].wait()
    gap = jnp.zeros((block, sz.hidden - 4 * pieces), jnp.float32)
    values = [
        with_row(up_raw[:, j, :], placed(quarter(hidden_vectors[j]))) for j in range(4)
    ]
    for i in range(2):
        lanes = slice(pieces * i, pieces * (i + 1))
        whole = jnp.concatenate([value[:, lanes] for value in values] + [gap], axis=1)

        @pl.when(at.d == i)
        def _():
            wu[own_rows] = whole.astype(low)

        @pl.when(at.d != i)
        def _():
            wu_own[...] = whole.astype(low)

    wires.copy(wu_own, wu_block(at.d)(at.c), at.peer(4), 10)

    def turned_halves(value, target, lanes):
        flipped = value.T
        gap = jnp.zeros((block - pieces, flipped.shape[1]), jnp.float32)
        parts = [flipped[0:pieces], gap, flipped[pieces : 2 * pieces], gap]
        target[rows_at(pair * at.c, pair), lanes] = jnp.concatenate(parts, axis=0).astype(low)

    fetched[3].wait()
    value = with_row(out_raw[...], placed(quarter(width_vectors[0])))
    value = jnp.concatenate([value, jnp.zeros((sz.mixed - block, sz.share), jnp.float32)], axis=0)
    for i in range(sz.mixed // 128):
        lanes = slice(128 * i, 128 * (i + 1))
        turned_halves(value[lanes], wo, lanes_at(sz.mixed * at.d + 128 * i, 128))
    wo_relay, wo_done = spread_col(wires, wo_block(at.d), at, 28)
    wires.copy(wo_block(at.d)(at.c), wo_block(at.d)(at.c), at.peer(4), 32 + at.c)

    fetched[5].wait()
    halves(dy_raw[...], dy_home)
    dy_onward, dy_crossed = cross_over(wires, dy_home, dy_half, dy_piece, at, 116)

    x_crossed()
    x_done = share_pieces(wires, (2,), x_piece, at, 104)

    fetched[4].wait()
    for i in range(sz.hidden // 128):
        rows = slice(128 * i, 128 * (i + 1))
        if 128 * (i + 1) <= 4 * pieces:
            value = down_raw[rows]
        else:
            value = jnp.concatenate(
                [
                    down_raw[128 * i : 4 * pieces],
                    placed(quarter(width_vectors[3])),
                    jnp.zeros((sz.hidden - 4 * pieces - 1, sz.share), jnp.float32),
                ],
                axis=0,
            )
        turned_halves(value, wd, rows)
    col_labels[...] = jnp.concatenate([row_labels[...]] * 8, axis=0).astype(jnp.float32).T[:, 0:1]
    x_done()
    dy_onward()
    wires.arrived(wu_block(1 - at.d)(at.c), 10, at.peer(4))
    wu_first_send, wu_first, wu_first_done = spread_col(wires, wu_block(at.d), at, 36, True)
    wu_second_send, wu_second, wu_second_done = spread_col(wires, wu_block(1 - at.d), at, 40, True)
    for distance in (2, 1):
        wu_first_send(distance)
        wu_second_send(distance)

    for c in range(4):
        wires.arrived(vec_block(at.d, c), 2 + c, at.along(c), at.c != c)
    wires.arrived(vec_block(1 - at.d, at.c), 6 + at.c, at.peer(4))
    for step in range(1, 4):
        there = (at.c + step) % 4
        wires.copy(
            vec_block(at.d, there), vec_block(at.d, there), at.peer(4), 6 + there
        )
    for step in range(1, 4):
        there = (at.c + step) % 4
        wires.arrived(vec_block(1 - at.d, there), 6 + there, at.peer(4))
    features = 4.0 * sz.share

    def add_up(i, carry):
        rows = rows_at(128 * i, 128)
        value = x_t[rows].astype(jnp.float32)
        return (
            carry[0] + jnp.sum(value, axis=0, keepdims=True),
            carry[1] + jnp.sum(value * value, axis=0, keepdims=True),
        )

    zero = jnp.zeros((1, sz.seq), jnp.float32)
    sums = lax.fori_loop(0, sz.tiles, add_up, (zero, zero))
    center = sums[0] / features
    inverse = lax.rsqrt(sums[1] / features - center * center + NORM_EPSILON)

    @pl.loop(0, sz.tiles)
    def _(i):
        rows, lanes = rows_at(128 * i, 128), lanes_at(128 * i, 128)
        vectors = vec[rows].astype(jnp.float32)
        value = (x_t[rows].astype(jnp.float32) - center) * inverse
        value = value * vectors[:, 0:1] + vectors[:, 1:2]
        h1_t[rows] = value.astype(low)
        h1[:, lanes] = value.T.astype(low)
        mine = x_t[rows, lanes_at(sz.part * at.r, sz.part)]
        x_own[:, lanes] = turned(mine).astype(low)
        vec_rows[:, lanes] = vectors.T[0:8]

    flush(h1_t, h1_t_out)
    flush(x_own, x_own_out)
    flush(vec_rows, vec_rows_out)

    wh_relay()
    for c in range(4):
        needed = at.c != c
        if c == 0:
            needed = needed & (at.c != 2)
        if c == 3:
            needed = needed & (at.c != 1)
        wires.arrived(wh_block(at.d)(c), 20 + c, at.along(c), needed)
        wires.copy(wh_block(at.d)(c), wh_block(at.d)(c), at.peer(4), 24 + c, at.c != c)

    for c in range(4):
        wires.arrived(wh_block(1 - at.d)(c), 24 + c, at.peer(4))
    flush(wh, wh_out)

    @pl.loop(0, sz.heads // 256)
    def _(i):
        lanes = lanes_at(256 * i, 256)
        own_qkv[:, lanes] = times(h1[...], wh[:, lanes]).astype(low)

    starts = (0, sz.main, 2 * sz.main, 3 * sz.main)
    ends = jnp.concatenate([own_qkv[:, s : s + 128] for s in starts], axis=1)
    edge_out[...] = picked(ends, choose((512, 256), edge_source))
    last = at.r == 3

    @pl.when(at.r == 0)
    def _():
        edge_in[...] = jnp.zeros_like(edge_in)

    wires.copy(edge_out, edge_in, (at.d, at.r + 1, at.c), 52, at.r < 3)
    spread = choose((256, 384), spread_source)
    extra = picked(edge_out[...], spread)
    wires.arrived(edge_in, 52, (at.d, at.r - 1, at.c), at.r > 0)
    first = picked(edge_in[...], spread)
    lane = lax.broadcasted_iota(jnp.int32, (sz.seq, 128), 1)
    for i, target in enumerate((qw, kw, vw)):
        start = starts[i]
        target[:, 0:128] = jnp.where(
            lane < sz.slack * at.r,
            first[:, 128 * i : 128 * i + 128],
            own_qkv[:, start : start + 128],
        )
        target[:, 128 : sz.main] = own_qkv[:, start + 128 : start + sz.main]
        target[:, sz.main : sz.main + 128] = extra[:, 128 * i : 128 * i + 128]
    flush(qw, qw_out)
    flush(kw, kw_out)
    flush(vw, vw_out)

    wo_relay()
    for c in range(4):
        needed = at.c != c
        if c == 0:
            needed = needed & (at.c != 2)
        if c == 3:
            needed = needed & (at.c != 1)
        wires.arrived(wo_block(at.d)(c), 28 + c, at.along(c), needed)
        wires.copy(wo_block(at.d)(c), wo_block(at.d)(c), at.peer(4), 32 + c, at.c != c)

    dy_crossed()
    dy_done = share_pieces(wires, (2, 4, 6), dy_piece, at, 124)

    half = sz.seq // 2

    def heads_of(p, count):
        tile = lanes_at(128 * p, 128)
        for q in range(2):
            rows = slice(half * q, half * (q + 1))
            keys = half * (q + 1)
            order = lax.broadcasted_iota(jnp.int32, (half, keys), 0) + half * q
            allowed = (col_labels[rows, :] == row_labels[:, 0:keys].astype(jnp.float32)) & (
                order >= lax.broadcasted_iota(jnp.int32, (half, keys), 1)
            )
            lanes = lax.broadcasted_iota(jnp.int32, (half, 128), 1)
            side = lanes // HD
            total = jnp.zeros((half, 128), jnp.float32)
            for h in range(count):
                queries = jnp.where(side == h, qw[rows, tile].astype(jnp.float32) * HD ** (-0.5), 0.0)
                scores = times_flipped(queries.astype(low), kw[0:keys, tile])
                scores = jnp.where(allowed, scores, MASKED)
                highest = jnp.max(scores, axis=1, keepdims=True)
                raised = jnp.exp(scores - highest)
                summed = jnp.sum(raised, axis=1, keepdims=True)
                found = highest + jnp.log(summed)
                lse[rows, :] = jnp.where(lanes == 2 * p + h, found, lse[rows, :])
                soft = (raised * (1.0 / summed)).astype(low)
                total = jnp.where(side == h, times(soft, vw[0:keys, tile]), total)
            aw[rows, tile] = total.astype(low)

    lse[...] = jnp.zeros_like(lse)

    @pl.loop(0, sz.main // 128)
    def _(p):
        heads_of(p, 2)

    @pl.when(last)
    def _():
        heads_of(sz.main // 128, 1)
        edge_back[...] = aw[:, sz.main : sz.main + 128]

    flush(lse, lse_out)

    wires.copy(aw.at[:, 0:128], edge_back, (at.d, at.r - 1, at.c), 53, at.r > 0)
    wd_first_send, wd_first, wd_first_done = spread_col(wires, wd_block(0), at, 44, True)
    wd_second_send, wd_second, wd_second_done = spread_col(wires, wd_block(1), at, 48, True)
    for distance in (2, 1):
        wd_first_send(distance)
        wd_second_send(distance)
    wires.arrived(edge_back, 53, (at.d, at.r + 1, at.c), at.r < 3)

    def natural(column):
        inner = column % sz.mixed
        place = sz.pieces * (column // sz.mixed) + inner + sz.slack * at.r
        return jnp.where(inner < sz.pieces, place, -1)

    def natural_main(column):
        place = natural(column)
        return jnp.where(place < sz.main, place, -1)

    def natural_edge(column):
        return natural(column) - sz.main

    mixed = times(aw[:, 0 : sz.main], choose((sz.main, 2 * sz.mixed), natural_main))
    mixed = mixed + times(edge_back[...], choose((128, 2 * sz.mixed), natural_edge))
    ones = lax.broadcasted_iota(jnp.int32, mixed.shape, 1) % sz.mixed == sz.pieces
    a_nat[...] = jnp.where(ones, 1.0, mixed).astype(low)
    for c in range(4):
        wires.arrived(wo_block(1 - at.d)(c), 32 + c, at.peer(4))
    flush(wo, wo_out)
    flush(a_nat, a_nat_out)

    def project(start, tile):
        out = times_flipped(a_nat[...], wo[rows_at(start, tile)])
        part[:, lanes_at(start, tile)] = out.astype(low)

    over_tiles(sz.width, project)

    onward, total, _ = scatter_group(
        wires, (2,), part, lambda d, r: sz.part * r, near, mid, far, at, 64
    )
    onward()
    wu_first()
    wu_second()
    dy_done()
    middle = x_own[...].astype(jnp.float32) + total()
    x2[...] = middle
    flush(x2, x2_out)
    center = jnp.sum(middle, axis=1, keepdims=True) / features
    spread_two = jnp.sum(middle * middle, axis=1, keepdims=True) / features - center * center
    normed = (middle - center) * lax.rsqrt(spread_two + NORM_EPSILON)
    own_rows = rows_at(sz.part * (4 * at.d + at.r), sz.part)
    h2[own_rows] = (normed * vec_rows[2:3] + vec_rows[3:4]).astype(low)
    h2_done, _ = gather_group(
        wires, (2, 4, 6), lambda d, r: h2.at[rows_at(sz.part * (4 * d + r), sz.part)], at, 72
    )
    @pl.loop(0, sz.tiles)
    def _(i):
        dy[:, lanes_at(128 * i, 128)] = turned(dy_t[rows_at(128 * i, 128)]).astype(low)

    flush(dy, dy_out)
    h2_done()
    wu_first_done()
    wu_second_done()
    flush(wu, wu_out)

    def expand(start, tile):
        lanes = lanes_at(start, tile)
        value = times(h2[...], wu[:, lanes])
        u[:, lanes] = value
        inner = jnp.tanh(ROOT * (value + CUBIC * value * value * value))
        value = 0.5 * value * (1.0 + inner)
        column = lax.broadcasted_iota(jnp.int32, value.shape, 1) + start
        gl[:, lanes] = jnp.where(column == 4 * sz.pieces, 1.0, value).astype(low)

    over_tiles(sz.hidden, expand)

    flush(u, u_out)
    flush(gl, gl_out)
    wd_first()

    @pl.loop(0, sz.tiles)
    def _(i):
        h2_t[rows_at(128 * i, 128)] = turned(h2[:, lanes_at(128 * i, 128)]).astype(low)

    flush(h2_t, h2_t_out)
    wd_second()

    @pl.loop(0, 4)
    def _(i):
        rows = rows_at(pair * i, pair)
        gd[rows] = times(dy_t[rows], gl[...]).astype(low)

    flush(gd, gd_out)
    wd_first_done()
    wd_second_done()
    flush(wd, wd_out)
    wires.close()
    for made in flushed:
        made.wait()


def backward_kernel(
    sz,
    dy_all,
    gd_all,
    u_all,
    gl_all,
    h2_t_all,
    wd_all,
    wu_all,
    wo_all,
    wh_all,
    h1_t_all,
    qw_all,
    kw_all,
    vw_all,
    a_nat_all,
    lse_all,
    x2_all,
    x_own_all,
    vec_rows,
    segments,
    out_down,
    out_up,
    out_out,
    out_heads,
    result_home,
    grad_home,
    vec_out,
    zd,
    zu,
    zo,
    zh,
    res_all,
    res_two,
    grad_all,
    grad_two,
    rd,
    ru,
    ro,
    rh,
    qw,
    kw,
    vw,
    a_nat,
    lse,
    x2,
    x_own,
    xu,
    dy,
    dy_t,
    u,
    gl,
    h2_t,
    wd,
    wu,
    wo,
    wh,
    dy_own,
    du,
    gw,
    gu,
    go,
    xh,
    xo,
    near_two,
    far_two,
    near_res,
    far_res,
    near_one,
    far_one,
    mid,
    dob,
    da,
    dk_sum,
    dv_sum,
    dx2,
    edge_out,
    edge_in,
    fore_out,
    fore_in,
    col_labels,
    res_stage,
    grad_stage,
    va,
    vb,
    sends,
    arrivals,
    locals_,
):
    at = Place()
    wires = Wires(sends, arrivals)
    low = jnp.bfloat16
    pair, block = sz.pair, sz.block
    features = 4.0 * sz.share
    used = [0]

    def load(source, target, when=None):
        made = pltpu.make_async_copy(source, target, locals_.at[used[0]])
        used[0] += 1
        run(when, made.start)
        return made

    own_rows = rows_at(sz.part * (4 * at.d + at.r), sz.part)
    gd = gw.at[:, 0 : sz.hidden]
    loads = [
        load(s, t)
        for s, t in (
            (dy_all, dy),
            (wd_all, wd),
            (u_all, u),
            (dy_all.at[own_rows], dy_own),
            (wu_all, wu),
            (h2_t_all, h2_t),
            (gl_all, gl),
            (gd_all, gd),
            (wo_all, wo),
            (wh_all, wh),
            (x2_all, x2),
            (a_nat_all, a_nat),
            (qw_all, qw),
            (kw_all, kw),
            (vw_all, vw),
            (lse_all, lse),
            (x_own_all, x_own),
            (h1_t_all, dy_t.at[:, 0 : sz.seq]),
        )
    ]
    greet(at, False)
    stay = []

    order, d_send, d_relay, d_arrived, d_from = collect_col(
        wires,
        lambda c: gd.at[rows_at(pair * c, pair)],
        zd,
        rd,
        at,
        0,
        lambda c: gd_all.at[rows_at(pair * c, pair)],
    )
    for step in range(4):
        d_send(step)

    def relay_of(rest, block):
        def add(there):
            rows = rows_at(pair * there, pair)
            block[rows] = (block[rows].astype(jnp.float32) + rest[...].astype(jnp.float32)).astype(low)

        return add

    for made in loads[0:3]:
        made.wait()

    def through(start, tile):
        lanes = lanes_at(start, tile)
        upstream = times(dy[...], wd[:, lanes])
        value = u[:, lanes]
        inner = jnp.tanh(ROOT * (value + CUBIC * value * value * value))
        slope = 0.5 * (1.0 + inner) + 0.5 * value * (1.0 - inner * inner) * ROOT * (
            1.0 + 3.0 * CUBIC * value * value
        )
        du[:, lanes] = (upstream * slope).astype(low)

    over_tiles(sz.hidden, through)
    loads[4].wait()

    def back_up(start, tile):
        dy[:, lanes_at(start, tile)] = times_flipped(du[...], wu[rows_at(start, tile)]).astype(low)

    over_tiles(sz.width, back_up)

    def chunk_both(d, r):
        return sz.part * (4 * d + r)

    two_onward, two_total, two_sent = scatter_group(
        wires, (2, 4, 6), dy, chunk_both, near_two, mid, far_two, at, 16
    )
    loads[5].wait()
    order, u_send, u_relay, u_arrived, u_from = collect_col(
        wires, lambda c: gu.at[rows_at(pair * c, pair)], zu, ru, at, 5
    )
    for step in range(4):
        rows = rows_at(pair * order[step], pair)
        gu[rows] = times(h2_t[rows], du[...]).astype(low)
        u_send(step)
        if step == 1:
            two_onward()
    own = rows_at(pair * at.c, pair)
    own_slot = h2_t.at[own, 0 : sz.hidden]
    gd_own = load(gd_all.at[own], own_slot)
    loads[7].wait()
    before = len(wires.open)
    d_relay(relay_of(rd, gd))
    gd_sends = wires.open[before:]

    def norm_back(upstream, values, gain):
        center = jnp.sum(values, axis=1, keepdims=True) / features
        spread = jnp.sum(values * values, axis=1, keepdims=True) / features - center * center
        inverse = lax.rsqrt(spread + NORM_EPSILON)
        centered = (values - center) * inverse
        scaled = upstream * gain
        inner = (
            scaled
            - jnp.sum(scaled, axis=1, keepdims=True) / features
            - centered * (jnp.sum(scaled * centered, axis=1, keepdims=True) / features)
        )
        return (
            inner * inverse,
            jnp.sum(upstream * centered, axis=0, keepdims=True),
            jnp.sum(upstream, axis=0, keepdims=True),
        )

    loads[10].wait()
    loads[3].wait()
    h2_back = two_total()
    through_norm, gain_two, shift_two = norm_back(h2_back, x2[...], vec_rows[2:3])
    middle_back = dy_own[...].astype(jnp.float32) + through_norm
    dx2[...] = middle_back
    va[0, 2:3] = gain_two
    va[0, 3:4] = shift_two
    va[0, 4:8] = jnp.zeros((4, sz.width), jnp.float32)
    dob[rows_at(sz.part * at.r, sz.part)] = middle_back.astype(low)
    dob_done, dob_sent = gather_group(
        wires, (2,), lambda d, r: dob.at[rows_at(sz.part * r, sz.part)], at, 24
    )

    def contract(start, tile):
        out = times_flipped(gl[...], wd[rows_at(start, tile)])
        dy[:, lanes_at(start, tile)] = out.astype(low)

    wires.close(two_sent)
    loads[6].wait()
    over_tiles(sz.width, contract)
    res_onward, res_total, res_sent = scatter_group(
        wires, (2, 4, 6), dy, chunk_both, near_res, mid, far_res, at, 32
    )

    dob_done()
    loads[11].wait()
    loads[8].wait()
    da[...] = times(dob[...], wo[...]).astype(low)
    slack, main = sz.slack, sz.main

    def from_natural(place):
        wanted = sz.mixed * (place // sz.pieces) + place % sz.pieces
        return jnp.where((place >= 0) & (place < sz.share), wanted, -1)

    fore_out[...] = picked(
        da[...], choose((2 * sz.mixed, 128), lambda j: from_natural(j + main - slack * at.r))
    )

    @pl.when(at.r == 0)
    def _():
        fore_in[...] = jnp.zeros_like(fore_in)

    wires.copy(fore_out, fore_in, (at.d, at.r + 1, at.c), 40, at.r < 3)

    @pl.loop(0, sz.tiles)
    def _(i):
        dy_t[rows_at(128 * i, 128), sz.seq : sz.both] = turned(dob[:, lanes_at(128 * i, 128)]).astype(low)

    res_onward()

    for step in range(4):
        there = (at.c + step) % 4
        rows = rows_at(pair * there, pair)
        go[rows] = times(dy_t[rows, sz.seq : sz.both], a_nat[...]).astype(low)
        wires.copy(
            go.at[rows, lanes_at(sz.mixed * (1 - at.d), sz.mixed)], xo.at[there], at.peer(4), 48 + there
        )
    wires.arrived(fore_in, 40, (at.d, at.r - 1, at.c), at.r > 0)
    window = times(da[...], choose((2 * sz.mixed, main), lambda j: from_natural(j - slack * at.r)))
    da_first = window[:, 0:128] + fore_in[...].astype(jnp.float32)
    da[:, 128:main] = window[:, 128:main].astype(low)
    da[:, 0:128] = da_first.astype(low)
    da[:, main : main + 128] = fore_out[...]

    row_labels = segments.at[:, lanes_at(sz.seq * at.c, sz.seq)]
    col_labels[...] = jnp.concatenate([row_labels[...]] * 8, axis=0).astype(jnp.float32).T[:, 0:1]
    for made in loads[12:17]:
        made.wait()
    half = sz.seq // 2
    dqw, dkw = (du.at[sz.seq * i : sz.seq * (i + 1), 0 : main + 128] for i in range(2))
    dvw = gl.at[0 : sz.seq, 0 : main + 128]

    def heads_back(p, count):
        tile = lanes_at(128 * p, 128)
        dk_sum[...] = jnp.zeros_like(dk_sum)
        dv_sum[...] = jnp.zeros_like(dv_sum)
        for q in range(2):
            rows = slice(half * q, half * (q + 1))
            keys = half * (q + 1)
            order = lax.broadcasted_iota(jnp.int32, (half, keys), 0) + half * q
            allowed = (col_labels[rows, :] == row_labels[:, 0:keys].astype(jnp.float32)) & (
                order >= lax.broadcasted_iota(jnp.int32, (half, keys), 1)
            )
            lanes = lax.broadcasted_iota(jnp.int32, (half, 128), 1)
            side = lanes // HD
            total = jnp.zeros((half, 128), jnp.float32)
            for h in range(count):
                queries = jnp.where(side == h, qw[rows, tile].astype(jnp.float32) * HD ** (-0.5), 0.0)
                queries = queries.astype(low)
                pulled = jnp.where(side == h, da[rows, tile].astype(jnp.float32), 0.0).astype(low)
                found = jnp.sum(jnp.where(lanes == 2 * p + h, lse[rows, :], 0.0), axis=1, keepdims=True)
                scores = times_flipped(queries, kw[0:keys, tile])
                soft = jnp.where(allowed, jnp.exp(jnp.where(allowed, scores - found, MASKED)), 0.0)
                soft_back = times_flipped(pulled, vw[0:keys, tile])
                inner = jnp.sum(soft_back * soft, axis=1, keepdims=True)
                score_back = (soft * (soft_back - inner)).astype(low)
                piece = times(score_back, kw[0:keys, tile]) * HD ** (-0.5)
                total = jnp.where(side == h, piece, total)
                dk_sum[0:keys] += times_outer(score_back, queries)
                dv_sum[0:keys] += times_outer(soft.astype(low), pulled)
            dqw[rows, tile] = total.astype(low)
        dkw[:, tile] = dk_sum[...].astype(low)
        dvw[:, tile] = dv_sum[...].astype(low)

    @pl.loop(0, main // 128)
    def _(p):
        heads_back(p, 2)

    @pl.when(at.r == 3)
    def _():
        heads_back(main // 128, 1)

    def compact(column):
        part, place = column // HD, column % HD
        return jnp.where(part < 3, 128 * part + place, -1)

    table = choose((384, 256), compact)
    backs = (dqw, dkw, dvw)
    edge_out[...] = picked(jnp.concatenate([b[:, 0:128] for b in backs], axis=1), table)
    wires.copy(edge_out, edge_in, (at.d, at.r - 1, at.c), 41, at.r > 0)

    @pl.when(at.r == 3)
    def _():
        edge_in[...] = picked(jnp.concatenate([b[:, main : main + 128] for b in backs], axis=1), table)

    u_relay(relay_of(ru, gu))

    def go_home(values, stage, every, halves, out, base):
        flipped = values.T
        for c in range(4):
            for y in range(2):
                rows = slice(pair * c + block * y, pair * c + block * (y + 1))
                stage[c, y] = flipped[rows].astype(low)
        holds = at.k == at.c % 2
        lanes = lanes_at(sz.part * at.r, sz.part)
        held = []
        for y in range(2):
            there = 2 * y + at.c % 2
            wires.copy(
                stage.at[:, y], every.at[:, :, lanes], (at.d, there, at.c), base + at.r, there != at.r
            )
            held.append((there == at.r, load(stage.at[:, y], every.at[:, :, lanes], there == at.r)))

        def along():
            for r in range(4):
                block_r = every.at[:, :, sz.part * r : sz.part * (r + 1)]
                wires.arrived(block_r, base + r, (at.d, r, at.c), holds & (at.r != r))
            for when, made in held:
                run(when, made.wait)
            del held[:]
            for c in range(4):
                wires.copy(
                    every.at[c], halves.at[at.c // 2], at.along(c), base + 4 + at.c // 2, holds & (at.c != c)
                )
                when = holds & (at.c == c)
                held.append((when, load(every.at[c], halves.at[at.c // 2], when)))

        def across():
            for when, made in held:
                run(when, made.wait)
            for t in range(2):
                there = 2 * t + at.k
                wires.arrived(halves.at[t], base + 4 + t, at.along(there), there != at.c)
            mine = out.at[rows_at(block * at.y, block)]
            wires.copy(halves.at[1 - at.y], mine, at.peer(2), base + 6)
            stay.append(load(halves.at[at.y], mine))

        def finish():
            wires.arrived(out.at[rows_at(block * (1 - at.y), block)], base + 6, at.peer(2))

        return along, across, finish

    res_along, res_across, res_finish = go_home(
        x2[...] + res_total(), res_stage, res_all, res_two, result_home, 56
    )
    wires.close(res_sent)

    wires.arrived(edge_in, 41, (at.d, at.r + 1, at.c), at.r < 3)

    def unfold(column):
        tile, lane = column // 128, column % 128
        inside = jnp.where(lane < HD - 16, HD * tile + lane + 16, -1)
        tail = jnp.where(lane < 48, HD * (lane // 16) + lane % 16, -1)
        return jnp.where(tile < 3, inside, tail)

    edges = picked(edge_in[...], choose((256, 512), unfold))
    lane = lax.broadcasted_iota(jnp.int32, (sz.seq, 128), 1)
    pieces = []
    for i, back in enumerate(backs):
        first = jnp.where(lane < slack * at.r, edges[:, 128 * i : 128 * i + 128], back[:, 0:128])
        pieces += [first, back[:, 128:main]]
    pieces.append(edges[:, 384:512])
    wires.close(dob_sent)
    own_back = dob.at[:, 0 : sz.heads]
    own_back[...] = jnp.concatenate(pieces, axis=1)

    wires.close(gd_sends)
    gd_own.wait()
    loads[17].wait()
    h_order, h_send, h_relay, h_arrived, h_from = collect_col(
        wires, lambda c: xh.at[c], zh, rh, at, 72
    )
    for step in range(4):
        there = h_order[step]
        rows = rows_at(pair * there, pair)
        gw[rows] = times(dy_t[rows, 0 : sz.seq], own_back[...]).astype(low)
        other = gw.at[rows_at(pair * there + block * (1 - at.d), block)]
        wires.copy(other, xh.at[there], at.peer(4), 80 + there)

    def o_heads(step):
        there = h_order[step]
        wires.arrived(xh.at[there], 80 + there, at.peer(4))
        mine = rows_at(pair * there + block * at.d, block)
        xh[there] = (gw[mine].astype(jnp.float32) + xh[there].astype(jnp.float32)).astype(low)
        h_send(step)

    for made in loads[9:10]:
        made.wait()

    def back_in(start, tile):
        out = times_flipped(own_back[...], wh[rows_at(start, tile)])
        dy[0 : sz.seq, lanes_at(start, tile)] = out.astype(low)

    over_tiles(sz.width, back_in)
    one_onward, one_total, _ = scatter_group(
        wires, (2,), dy, lambda d, r: sz.part * r, near_one, mid, far_one, at, 64
    )
    order, o_send, o_relay, o_arrived, o_from = collect_col(
        wires, lambda c: xo.at[c], zo, ro, at, 10
    )
    for step in range(4):
        there = order[step]
        wires.arrived(xo.at[there], 48 + there, at.peer(4))
        mine = go[rows_at(pair * there, pair), lanes_at(sz.mixed * at.d, sz.mixed)]
        xo[there] = (mine.astype(jnp.float32) + xo[there].astype(jnp.float32)).astype(low)
        o_send(step)

    def relay_out(there):
        both = xo[there].astype(jnp.float32) + ro[...].astype(jnp.float32)
        xo[there] = both.astype(low)

    brought = []

    def bring(c, landing, needed):
        made = load(landing.at[c], h2_t.at[pair * c : pair * (c + 1), 0 : sz.hidden], needed)
        brought.append((needed, made))

        @pl.when(jnp.logical_not(needed) & (at.c != c))
        def _():
            h2_t[pair * c : pair * (c + 1), 0 : sz.hidden] = jnp.zeros((pair, sz.hidden), low)

    def summed(lanes):
        result = jnp.zeros((pair, lanes.stop - lanes.start), jnp.float32)
        for c in range(4):
            result = result + h2_t[pair * c : pair * (c + 1), lanes].astype(jnp.float32)
        return result

    half_rows = sz.pieces

    def natural_rows(value):
        flipped = value.T
        return jnp.concatenate(
            [flipped[:, 0:half_rows], flipped[:, block : block + half_rows]], axis=1
        )

    def own_half(row):
        return jnp.where(at.d == 0, row[:, 0:half_rows], row[:, half_rows : 2 * half_rows])

    def all_brought():
        for needed, made in brought:
            run(needed, made.wait)
        del brought[:]

    def relay_heads(there):
        xh[there] = (xh[there].astype(jnp.float32) + rh[...].astype(jnp.float32)).astype(low)

    res_along()
    one_onward()
    o_heads(0)
    h1_back = one_total()
    through_norm, gain_one, shift_one = norm_back(
        h1_back, x_own[...].astype(jnp.float32), vec_rows[0:1]
    )
    va[0, 0:1] = gain_one
    va[0, 1:2] = shift_one
    for mask in range(1, 8):
        wires.copy(va.at[0], va.at[mask], at.peer(mask), 84 + mask)
    grad_along, grad_across, grad_finish = go_home(
        dx2[...] + through_norm, grad_stage, grad_all, grad_two, grad_home, 104
    )
    for c in range(4):
        d_arrived(c)
        bring(c, zd, d_from(c))
    all_brought()
    for i in range(sz.hidden // 128):
        rows = min(128, 4 * sz.pieces - 128 * i)
        value = natural_rows(summed(slice(128 * i, 128 * (i + 1))))
        u[128 * i : 128 * i + rows, 0 : sz.share] = value[0:rows]
        if rows < 128:
            vec_out[5:6, 0:half_rows] = own_half(value[rows : rows + 1])
    down_out = load(u.at[0 : 4 * sz.pieces, 0:512], out_down)
    o_heads(1)
    grad_along()
    o_heads(2)
    h_relay(relay_heads)
    gu_own = load(gu.at[own], own_slot)
    for c in range(4):
        u_arrived(c)
        bring(c, zu, u_from(c))
    all_brought()
    gu_own.wait()
    theirs = rows_at(pair * at.c + block * (1 - at.d), block)

    def part_sum(side, lanes):
        result = jnp.zeros((block, sz.hidden), jnp.float32)
        for c in range(4):
            result = result + h2_t[rows_at(pair * c + block * side, block), lanes].astype(jnp.float32)
        return result

    every = slice(0, sz.hidden)
    gu[theirs] = part_sum(1 - at.d, every).astype(low)
    wires.copy(gu.at[theirs], xu, at.peer(4), 97)
    o_relay(relay_out)
    o_heads(3)
    res_across()
    mine_sum = part_sum(at.d, every)
    down_out.wait()
    wires.arrived(xu, 97, at.peer(4))
    partner_sum = xu[...].astype(jnp.float32)
    for side in range(2):

        @pl.when(at.d == side)
        def _():
            both = (mine_sum, partner_sum) if side == 0 else (partner_sum, mine_sum)
            for j in range(4):
                rows = slice(block * j, block * (j + 1))
                for i in range(2):
                    u[rows, half_rows * i : half_rows * (i + 1)] = both[i][:, half_rows * j : half_rows * (j + 1)]

    bias_sum = mine_sum[half_rows : half_rows + 1]
    for j in range(4):
        vec_out[8 + j : 9 + j, 0:half_rows] = bias_sum[:, half_rows * j : half_rows * (j + 1)]
    up_out = load(u.at[0 : 4 * block, 0:512], out_up)

    for c in range(4):
        o_arrived(c)
        needed = o_from(c)
        made = load(zo.at[c], wd.at[pair * c : pair * (c + 1), 0 : sz.mixed], needed)
        brought.append((needed, made))

        @pl.when(jnp.logical_not(needed))
        def _():
            wd[pair * c : pair * (c + 1), 0 : sz.mixed] = jnp.zeros((pair, sz.mixed), low)

    all_brought()
    value = xo[at.c].astype(jnp.float32)
    for c in range(4):
        value = value + wd[pair * c : pair * (c + 1), 0 : sz.mixed].astype(jnp.float32)
    flipped = natural_rows(value)
    vec_out[4:5, 0:half_rows] = own_half(flipped[half_rows : half_rows + 1])
    flipped = flipped[0:block]
    for i in range(4):
        held = (dk_sum, dv_sum)[i // 2].at[block * (i % 2) : block * (i % 2 + 1)]
        lanes = min(128, sz.share - 128 * i)
        held[:, 0:lanes] = flipped[:, 128 * i : 128 * i + lanes]
        stay.append(load(held, out_out.at[:, 128 * i : 128 * (i + 1)]))

    grad_across()

    for mask in range(1, 8):
        wires.arrived(va.at[mask], 84 + mask, at.peer(mask))
    vb[at.c] = functools.reduce(lambda a, b: a + b, [va[mask] for mask in range(8)])
    for c in range(4):
        wires.copy(vb.at[at.c], vb.at[at.c], at.along(c), 98 + at.c, at.c != c)

    for c in range(4):
        wires.arrived(vb.at[c], 98 + c, at.along(c), at.c != c)
    sums = vb[0] + vb[1] + vb[2] + vb[3]
    picked_sums = jnp.zeros((4, half_rows), jnp.float32)
    for i in range(8):
        cut = sums[0:4, block * i : block * i + half_rows]
        picked_sums = jnp.where(2 * at.c + at.d == i, cut, picked_sums)
    vec_out[0:4, 0:half_rows] = picked_sums
    res_finish()
    grad_finish()
    up_out.wait()
    rest_lanes = sz.heads - sz.hidden
    for c in range(4):
        h_arrived(c)
        needed = h_from(c)
        rows = slice(block * c, block * (c + 1))
        parts = (
            load(zh.at[c, :, 0 : sz.hidden], wd.at[rows], needed),
            load(zh.at[c, :, sz.hidden : sz.heads], wu.at[rows, 0:rest_lanes], needed),
        )
        brought += [(needed, made) for made in parts]

        @pl.when(jnp.logical_not(needed))
        def _():
            wd[rows] = jnp.zeros((block, sz.hidden), low)
            wu[rows, 0:rest_lanes] = jnp.zeros((block, rest_lanes), low)

    all_brought()
    left = xh[at.c, :, 0 : sz.hidden].astype(jnp.float32)
    right = xh[at.c, :, sz.hidden : sz.heads].astype(jnp.float32)
    for c in range(4):
        rows = slice(block * c, block * (c + 1))
        left = left + wd[rows].astype(jnp.float32)
        right = right + wu[rows, 0:rest_lanes].astype(jnp.float32)
    whole = jnp.concatenate([left, right], axis=1)
    for i in range(3):
        turned_columns = jnp.concatenate(
            [
                whole[:, main * i : main * (i + 1)],
                whole[:, 3 * main + slack * i : 3 * main + slack * (i + 1)],
            ],
            axis=1,
        )
        rows = slice(block * i, block * (i + 1))
        for r in range(4):

            @pl.when(at.r == r)
            def _():
                cut = slack * r
                value = turned_columns
                if cut:
                    value = jnp.concatenate([value[:, cut:], value[:, 0:cut]], axis=1)
                u[rows, 0 : sz.share] = value
                if i != 1:
                    vec_out[6 + i // 2 : 7 + i // 2, 0:half_rows] = own_half(
                        value[half_rows : half_rows + 1]
                    )

    stay.append(load(u.at[0 : 3 * block, 0:512], out_heads))
    for made in stay:
        made.wait()
    wires.close()


def update_kernel(sz, rates, grads, result_in, grad_in, weights, firsts, seconds, outs):
    down, out, up, heads, vectors = grads
    share, pieces, block = sz.share, sz.pieces, sz.block

    def move(i, place, gradient, decay):
        weight = weights[i][place]
        first_new = BETA_FIRST * firsts[i][place] + (1.0 - BETA_FIRST) * gradient
        second_new = BETA_SECOND * seconds[i][place] + (1.0 - BETA_SECOND) * (gradient * gradient)
        divisor = jnp.sqrt(second_new * (1.0 / (1.0 - BETA_SECOND**STEP))) + ADAM_EPSILON
        change = first_new * (rates[i] / (1.0 - BETA_FIRST**STEP)) / divisor
        weight_new = weight * (1.0 - rates[i] * decay) - change
        outs[3 * i + 2][place] = first_new
        outs[3 * i + 3][place] = second_new
        outs[3 * i + 4][place] = weight_new

    for part in range(3):
        move(0, part, heads[part, :, 0:share], MATRIX_DECAY)
    move(1, slice(None), out[:, 0:share], MATRIX_DECAY)
    move(2, slice(None), jnp.stack([up[j, :, 0:share] for j in range(4)], axis=1), MATRIX_DECAY)
    move(3, slice(None), down[:, 0:share], MATRIX_DECAY)

    @pl.when(pl.program_id(0) == 0)
    def _():
        for i, source, row in (
            (4, 0, 0), (4, 1, 1), (5, 4, 0), (5, 2, 1), (5, 3, 2), (5, 5, 3),
            (6, 6, 0), (6, 7, 1), (7, 8, 0), (7, 9, 1), (7, 10, 2), (7, 11, 3),
        ):
            move(i, row, vectors[source : source + 1, 0:pieces], 0.0)

    def plain(rows):
        rows = rows.astype(jnp.float32)
        return jnp.concatenate([rows[0:pieces], rows[block : block + pieces]], axis=0)

    @pl.when(pl.program_id(0) == 1)
    def _():
        outs[0][...] = plain(result_in[...]).astype(jnp.bfloat16)

    @pl.when(pl.program_id(0) == 2)
    def _():
        outs[1][...] = plain(grad_in[...])


def fused(
    tokens,
    cotangent,
    segments,
    weights,
    firsts,
    seconds,
):
    low = jnp.bfloat16
    seq, share = tokens.shape
    pieces = weights[1].shape[2]
    sz = Sizes(share, pieces, seq)
    block, main = sz.block, sz.main

    def views(arrays):
        heads, out, up, down, *small = arrays
        return (
            jnp.transpose(heads.reshape(pieces, 3, share), (1, 0, 2)),
            out.reshape(pieces, share),
            up.reshape(pieces, 4, share),
            down.reshape(4 * pieces, share),
            *[each.reshape(each.shape[0], 1, pieces) for each in small],
        )

    viewed = views(weights)
    labels = segments.reshape(1, -1)

    def made(*shape, dtype=low):
        return jax.ShapeDtypeStruct(shape, dtype)

    def held(*shape, dtype=low):
        return pltpu.VMEM(shape, dtype)

    w, seq, both, part = sz.width, sz.seq, sz.both, sz.part
    vmem, anywhere = pl.BlockSpec(memory_space=pltpu.VMEM), pl.BlockSpec(memory_space=pl.ANY)
    dma = pltpu.SemaphoreType.DMA
    f32 = jnp.float32
    wide = 3 * 128 + 128
    outs = pl.pallas_call(
        functools.partial(forward_kernel, sz),
        out_shape=(
            made(w, sz.heads),
            made(w, 2 * sz.mixed),
            made(w, sz.hidden),
            made(w, sz.hidden),
            made(w, seq),
            made(w, both),
            made(w, sz.hidden),
            made(both, w),
            made(both, sz.hidden, dtype=f32),
            made(both, sz.hidden),
            made(seq, main + 128),
            made(seq, main + 128),
            made(seq, main + 128),
            made(seq, 2 * sz.mixed),
            made(seq, 128, dtype=f32),
            made(part, w, dtype=f32),
            made(part, w),
            made(8, w, dtype=f32),
        ),
        in_specs=[anywhere] * 6 + [vmem] * 5,
        out_specs=[anywhere] * 18,
        scratch_shapes=[
            held(w, sz.heads),
            held(w, 2 * sz.mixed),
            held(w, sz.hidden),
            held(w, sz.hidden),
            held(w, seq),
            held(w, both),
            held(w, sz.hidden),
            held(w, both),
            held(both, w),
            held(both, sz.hidden, dtype=f32),
            held(both, sz.hidden),
            held(seq, main + 128),
            held(seq, main + 128),
            held(seq, main + 128),
            held(seq, 2 * sz.mixed),
            held(seq, 128, dtype=f32),
            held(part, w, dtype=f32),
            held(part, w),
            held(8, w, dtype=f32),
            held(w, seq),
            held(seq, w),
            held(both, w),
            held(seq, sz.heads),
            held(seq, main + 128),
            held(w, 128),
            held(seq, w),
            held(seq, 256),
            held(seq, 256),
            held(seq, 128),
            held(2, part, w),
            held(1, part, w),
            held(1, part, w),
            held(share, seq),
            held(share, seq),
            held(3, pieces, share, dtype=f32),
            held(pieces, share, dtype=f32),
            held(pieces, 4, share, dtype=f32),
            held(4 * pieces, share, dtype=f32),
            held(sz.pair, seq),
            held(sz.pair, seq),
            held(block, sz.hidden),
            held(seq, 1, dtype=f32),
            held(block, seq),
            held(block, seq),
            dma((160,)),
            dma((160,)),
            dma((48,)),
        ],
        compiler_params=pltpu.CompilerParams(
            collective_id=0, has_side_effects=True, vmem_limit_bytes=VMEM_BYTES
        ),
        cost_estimate=pl.CostEstimate(flops=10**10, bytes_accessed=10**8, transcendentals=10**6),
    )(tokens.T, cotangent.T, *viewed, labels)
    (wh, wo, wu, wd, h1_t, h2_t, gd, dy, u, gl, qw, kw, vw, a_nat, lse, x2, x_own, vec_rows) = outs
    outs = pl.pallas_call(
        functools.partial(backward_kernel, sz),
        out_shape=(
            made(4 * pieces, 512, dtype=f32),
            made(4 * block, 512, dtype=f32),
            made(block, 512, dtype=f32),
            made(3 * block, 512, dtype=f32),
            made(sz.pair, seq),
            made(sz.pair, seq),
            made(16, 256, dtype=f32),
            made(4, sz.pair, sz.hidden),
            made(4, sz.pair, sz.hidden),
            made(4, sz.pair, sz.mixed),
            made(4, block, sz.heads),
            made(4, block, seq),
            made(2, block, seq),
            made(4, block, seq),
            made(2, block, seq),
        ),
        in_specs=[anywhere] * 17 + [vmem] * 2,
        out_specs=[anywhere] * 6 + [vmem] + [anywhere] * 8,
        scratch_shapes=[
            held(sz.pair, sz.hidden),
            held(sz.pair, sz.hidden),
            held(sz.pair, sz.mixed),
            held(block, sz.heads),
            held(seq, main + 128),
            held(seq, main + 128),
            held(seq, main + 128),
            held(seq, 2 * sz.mixed),
            held(seq, 128, dtype=f32),
            held(part, w, dtype=f32),
            held(part, w),
            held(block, sz.hidden),
            held(both, w),
            held(w, both),
            held(both, sz.hidden, dtype=f32),
            held(both, sz.hidden),
            held(w, both),
            held(w, sz.hidden),
            held(w, sz.hidden),
            held(w, 2 * sz.mixed),
            held(w, sz.heads),
            held(part, w),
            held(both, sz.hidden),
            held(w, sz.heads),
            held(w, sz.hidden),
            held(w, 2 * sz.mixed),
            held(4, block, sz.heads),
            held(4, sz.pair, sz.mixed),
            held(4, part, w),
            held(3, part, w),
            held(4, part, w),
            held(3, part, w),
            held(2, part, w),
            held(1, part, w),
            held(3, part, w),
            held(seq, w),
            held(seq, 2 * sz.mixed),
            held(seq, 128, dtype=f32),
            held(seq, 128, dtype=f32),
            held(part, w, dtype=f32),
            held(seq, 256),
            held(seq, 256),
            held(seq, 128),
            held(seq, 128),
            held(seq, 1, dtype=f32),
            held(4, 2, block, part),
            held(4, 2, block, part),
            held(8, 8, w, dtype=f32),
            held(4, 8, w, dtype=f32),
            dma((128,)),
            dma((120,)),
            dma((80,)),
        ],
        compiler_params=pltpu.CompilerParams(
            collective_id=1, has_side_effects=True, vmem_limit_bytes=VMEM_BYTES
        ),
        cost_estimate=pl.CostEstimate(flops=2 * 10**10, bytes_accessed=10**8, transcendentals=10**6),
    )(
        dy, gd, u, gl, h2_t, wd, wu, wo, wh, h1_t,
        qw, kw, vw, a_nat, lse, x2, x_own, vec_rows, labels,
    )
    down, up, out, heads, result_home, grad_home, vectors = outs[:7]
    steps = 5
    chunk = pieces // steps

    def rows_of(shape, axis, size):
        block_shape = list(shape)
        block_shape[axis] = size
        return pl.BlockSpec(tuple(block_shape), lambda i: tuple(i if a == axis else 0 for a in range(len(shape))))

    def whole(shape):
        return pl.BlockSpec(tuple(shape), lambda i: (0,) * len(shape))

    matrix_specs = (
        rows_of((3, pieces, share), 1, chunk),
        rows_of((pieces, share), 0, chunk),
        rows_of((pieces, 4, share), 0, chunk),
        rows_of((4 * pieces, share), 0, 4 * chunk),
        *[whole(each.shape) for each in viewed[4:]],
    )
    grads = (down, out, up.reshape(4, block, 512), heads.reshape(3, block, 512), vectors)
    grad_specs = (
        rows_of((4 * pieces, 512), 0, 4 * chunk),
        rows_of((block, 512), 0, chunk),
        rows_of((4, block, 512), 1, chunk),
        rows_of((3, block, 512), 1, chunk),
        whole((16, 256)),
    )
    rates = (0.05, 0.2, 0.05, 0.025, 0.3, 0.3, 0.3, 0.3)
    arguments = (*grads, result_home, grad_home, *viewed, *views(firsts), *views(seconds))
    out_shape = [made(share, seq), made(share, seq, dtype=f32)]
    out_specs = [whole((share, seq)), whole((share, seq))]
    for each, spec in zip(viewed, matrix_specs, strict=True):
        out_shape += [jax.ShapeDtypeStruct(each.shape, f32)] * 3
        out_specs += [spec] * 3

    def update(*refs):
        ins, outs = refs[:31], refs[31:]
        update_kernel(sz, rates, ins[:5], ins[5], ins[6], ins[7:15], ins[15:23], ins[23:31], outs)

    updated = pl.pallas_call(
        update,
        grid=(steps,),
        out_shape=out_shape,
        in_specs=[*grad_specs, whole((sz.pair, seq)), whole((sz.pair, seq)), *matrix_specs * 3],
        out_specs=out_specs,
        compiler_params=pltpu.CompilerParams(vmem_limit_bytes=VMEM_BYTES),
        cost_estimate=pl.CostEstimate(
            flops=20 * 10**6, bytes_accessed=30 * 10**6, transcendentals=2 * 10**6
        ),
    )(*arguments)
    results = [updated[0].T, updated[1].T]
    for i, weight in enumerate(weights):
        for each in updated[2 + 3 * i : 5 + 3 * i]:
            if i == 0:
                each = jnp.transpose(each, (1, 0, 2))
            results.append(each.reshape(weight.shape))
    return tuple(results)


def normalize(inputs):
    center = jnp.mean(inputs, axis=1, keepdims=True)
    spread = jnp.mean(inputs * inputs, axis=1, keepdims=True) - center * center
    inverse = lax.rsqrt(spread + NORM_EPSILON)
    return ((inputs - center) * inverse, inverse)


def norm_pull(upstream, centered, inverse, gain):
    scaled = upstream * gain
    inner = (
        scaled
        - jnp.mean(scaled, axis=1, keepdims=True)
        - centered * jnp.mean(scaled * centered, axis=1, keepdims=True)
    )
    return inner * inverse


def crossed(blocks, n):
    pairs = [(i * n + j, j * n + i) for i in range(n) for j in range(n)]
    return lax.ppermute(blocks, ("row", "col"), pairs)


def scatter_rows(partial):
    return lax.psum_scatter(
        partial.astype(jnp.bfloat16), "row", scatter_dimension=0, tiled=True
    ).astype(jnp.float32)


def gather_rows(local):
    return lax.all_gather(local, "row", axis=0, tiled=True)


def split_heads(rows):
    return jnp.transpose(rows.reshape(rows.shape[0], -1, HD), (1, 0, 2))


def join_heads(values):
    return jnp.transpose(values, (1, 0, 2)).reshape(values.shape[1], -1)


def scores_of(queries, keys, allowed):
    scores = jnp.einsum(
        "hqe,hke->hqk", queries, keys, preferred_element_type=jnp.float32
    ) * HD ** (-0.5)
    return jnp.where(allowed[None], scores, MASKED)


def gathered(
    tokens,
    cotangent,
    segments,
    w_heads,
    w_out,
    w_up,
    w_down,
    norm_vectors,
    width_vectors,
    attend_bias,
    hidden_vectors,
):
    n_dp, n_row, n_col = (lax.axis_size(name) for name in ("dp", "row", "col"))
    row = lax.axis_index("row")
    low = jnp.bfloat16
    share = tokens.shape[1]
    width = share * n_col
    seq = tokens.shape[0]
    part = seq // n_row
    near = HEADS // n_row
    window = (HEADS - near * (n_row - 1)) * HD
    step = near * HD
    edge = width - (share + step * (n_row - 1)) if n_row > 1 else 0
    edge = window - share
    to_next = [(i, i + 1) for i in range(n_row - 1)]
    to_last = [(i + 1, i) for i in range(n_row - 1)]
    offset = edge - (share - step) * row

    vectors = jnp.concatenate(
        [
            norm_vectors.reshape(2, -1),
            width_vectors.reshape(4, -1),
            attend_bias.reshape(2, -1),
            hidden_vectors.reshape(4, -1),
        ]
    ).astype(low)
    vectors = lax.all_gather(vectors, ("row", "col", "dp"), axis=0, tiled=False)
    vectors = vectors.reshape(n_row, n_col, n_dp, 12, -1).astype(jnp.float32)
    by_col = jnp.transpose(vectors[0], (2, 0, 1, 3)).reshape(12, width)
    by_row = jnp.transpose(vectors[:, 0], (2, 0, 1, 3)).reshape(12, width)
    gain_one, shift_one, bias_out, gain_two, shift_two, bias_down = (by_col[i] for i in range(6))
    zeros = jnp.zeros((1, window), jnp.float32)
    attend_rows = lax.dynamic_slice_in_dim(by_row[6:8], row * step, window, axis=1)
    heads_bias = jnp.concatenate([attend_rows[0:1], zeros, attend_rows[1:2]]).reshape(-1)
    unit_bias = lax.dynamic_slice_in_dim(by_row[8:12], row * share, share, axis=1).reshape(-1)

    own = w_heads.astype(low).reshape(-1, 3, share)
    passed = lax.ppermute(own[:, :, share - edge :], "row", to_next)
    own = jnp.concatenate([passed, own, jnp.zeros_like(passed)], axis=2)
    own = lax.dynamic_slice_in_dim(own, offset, window, axis=2).reshape(-1, 3 * window)
    heads_matrix = lax.all_gather(own, ("col", "dp"), axis=0, tiled=True)
    out_matrix = lax.all_gather(w_out.astype(low).reshape(-1, share), ("col", "dp"), axis=0)
    out_matrix = jnp.transpose(out_matrix.reshape(n_col, share, share), (1, 0, 2))
    out_matrix = out_matrix.reshape(share, width)
    passed = lax.ppermute(out_matrix[share - edge :], "row", to_next)
    out_matrix = jnp.concatenate([passed, out_matrix, jnp.zeros_like(passed)])
    out_matrix = lax.dynamic_slice_in_dim(out_matrix, offset, window)
    owned = (jnp.arange(window) < step) | (row == n_row - 1)
    out_matrix = jnp.where(owned[:, None], out_matrix, jnp.zeros_like(out_matrix))
    up_matrix = lax.all_gather(
        w_up.astype(low).reshape(-1, 4 * share), ("col", "dp"), axis=0, tiled=True
    )
    down_matrix = lax.all_gather(w_down.astype(low).reshape(4, -1, share), ("col", "dp"), axis=0)
    down_matrix = down_matrix.reshape(n_col, n_dp, 4, -1, share)
    down_matrix = jnp.transpose(down_matrix, (2, 1, 3, 0, 4)).reshape(4 * share, width)

    inputs_low = lax.all_gather(crossed(tokens, n_row), "row", axis=1, tiled=True)
    upstream = lax.all_gather(crossed(cotangent, n_row), "row", axis=1, tiled=True)
    inputs = inputs_low.astype(jnp.float32)
    centered_one, inverse_one = normalize(inputs)
    normed_one = (centered_one * gain_one + shift_one).astype(low)
    projected = (times(normed_one, heads_matrix) + heads_bias).astype(low)
    queries, keys, values = (
        split_heads(projected[:, i * window : (i + 1) * window]) for i in range(3)
    )
    labels = lax.dynamic_slice_in_dim(segments, lax.axis_index("col") * seq, seq)
    places = jnp.arange(seq, dtype=jnp.int32)
    allowed = (labels[:, None] == labels[None, :]) & (places[:, None] >= places[None, :])
    scores = scores_of(queries, keys, allowed)
    highest = jnp.max(scores, axis=-1, keepdims=True)
    log_total = highest + jnp.log(jnp.sum(jnp.exp(scores - highest), axis=-1, keepdims=True))
    soft = jnp.exp(scores - log_total).astype(low)
    mixed = jnp.einsum("hqk,hke->hqe", soft, values, preferred_element_type=jnp.float32)
    mixed = join_heads(mixed.astype(low))
    branch = scatter_rows(times(mixed, out_matrix))
    mine = row * part
    middle = lax.dynamic_slice_in_dim(inputs, mine, part) + (branch + bias_out)
    centered_two, inverse_two = normalize(middle)
    normed_two = gather_rows((centered_two * gain_two + shift_two).astype(low))
    hidden = times(normed_two, up_matrix) + unit_bias
    activated, smooth_pull = jax.vjp(smooth, hidden)
    activated = activated.astype(low)
    result = (middle + (scatter_rows(times(activated, down_matrix)) + bias_down)).astype(low)

    down_back = times_flipped(upstream, down_matrix)
    grad_down = times_outer(activated, upstream)
    hidden_back = smooth_pull(down_back)[0].astype(low)
    grad_up = times_outer(normed_two, hidden_back)
    unit_sum = jnp.sum(hidden_back, axis=0, dtype=jnp.float32)
    normed_two_back = scatter_rows(times_flipped(hidden_back, up_matrix))
    upstream_own = lax.dynamic_slice_in_dim(upstream, mine, part).astype(jnp.float32)
    middle_back = upstream_own + norm_pull(normed_two_back, centered_two, inverse_two, gain_two)
    branch_own = middle_back.astype(low)
    branch_back = gather_rows(branch_own)
    mixed_back = times_flipped(branch_back, out_matrix).astype(low)
    grad_out = times_outer(mixed, branch_back)
    mixed_back = split_heads(mixed_back)
    scores_again = scores_of(queries, keys, allowed)
    soft = jnp.exp(scores_again - log_total)
    soft_back = jnp.einsum("hqe,hke->hqk", mixed_back, values, preferred_element_type=jnp.float32)
    row_inner = jnp.sum(soft_back * soft, axis=-1, keepdims=True)
    score_back = (soft * (soft_back - row_inner)).astype(low)
    query_back = jnp.einsum(
        "hqk,hke->hqe", score_back, keys, preferred_element_type=jnp.float32
    ) * HD ** (-0.5)
    key_back = jnp.einsum(
        "hqk,hqe->hke", score_back, queries, preferred_element_type=jnp.float32
    ) * HD ** (-0.5)
    value_back = jnp.einsum(
        "hqk,hqe->hke", soft.astype(low), mixed_back, preferred_element_type=jnp.float32
    )
    heads_back = jnp.concatenate(
        [join_heads(each.astype(low)) for each in (query_back, key_back, value_back)], axis=1
    )
    heads_sum = jnp.sum(heads_back, axis=0, dtype=jnp.float32)
    normed_one_back = scatter_rows(times_flipped(heads_back, heads_matrix))
    grad_heads = times_outer(normed_one, heads_back)
    centered_own = lax.dynamic_slice_in_dim(centered_one, mine, part)
    inverse_own = lax.dynamic_slice_in_dim(inverse_one, mine, part)
    input_back = middle_back + norm_pull(normed_one_back, centered_own, inverse_own, gain_one)

    def homeward(own):
        own = lax.all_to_all(own, "row", split_axis=1, concat_axis=0, tiled=True)
        return crossed(own, n_row)

    result_tokens = homeward(result)
    input_gradient = homeward(input_back.astype(low)).astype(jnp.float32)

    by_token = jnp.stack(
        [
            jnp.sum(normed_one_back * centered_own, axis=0),
            jnp.sum(normed_one_back, axis=0),
            jnp.sum(branch_own.astype(jnp.float32), axis=0),
            jnp.sum(normed_two_back * centered_two, axis=0),
            jnp.sum(normed_two_back, axis=0),
            jnp.sum(upstream_own, axis=0),
        ]
    )
    owned_rows = jnp.where(owned, heads_sum.reshape(3, window)[0::2], 0.0)
    by_unit = jnp.concatenate(
        [
            lax.dynamic_update_slice_in_dim(
                jnp.zeros((2, width), jnp.float32), owned_rows, row * step, axis=1
            ),
            lax.dynamic_update_slice_in_dim(
                jnp.zeros((4, width), jnp.float32), unit_sum.reshape(4, share), row * share, axis=1
            ),
        ]
    )
    sums = lax.psum(jnp.concatenate([by_token, by_unit]), ("dp", "row", "col"))
    pieces = share // n_dp
    inner = lax.axis_index("dp") * pieces
    col_sums = lax.dynamic_slice_in_dim(sums, lax.axis_index("col") * share + inner, pieces, axis=1)
    row_sums = lax.dynamic_slice_in_dim(sums, row * share + inner, pieces, axis=1)

    both = ("col", "dp")

    def to_owner(gradient):
        return lax.psum_scatter(gradient, both, scatter_dimension=0, tiled=True)

    got_heads = to_owner(grad_heads.astype(low)).reshape(pieces, 3, window)
    got_heads = jnp.where(owned, got_heads, jnp.zeros_like(got_heads))
    passed = lax.ppermute(got_heads[:, :, :edge], "row", to_last)
    got_heads = jnp.concatenate([got_heads, jnp.zeros_like(passed)], axis=2)
    got_heads = lax.dynamic_slice_in_dim(got_heads, edge - offset, share, axis=2)
    passed = jnp.concatenate([jnp.zeros((pieces, 3, share), low), passed, jnp.zeros_like(passed)], axis=2)
    got_heads = got_heads + lax.dynamic_slice_in_dim(passed, share - step + edge - offset, share, axis=2)
    low_out = jnp.where(owned[:, None], grad_out, 0.0).astype(low)
    passed = lax.ppermute(low_out[:edge], "row", to_last)
    low_out = jnp.concatenate([low_out, jnp.zeros_like(passed)])
    low_out = lax.dynamic_slice_in_dim(low_out, edge - offset, share)
    passed = jnp.concatenate([jnp.zeros((share, width), low), passed, jnp.zeros_like(passed)])
    low_out = low_out + lax.dynamic_slice_in_dim(passed, share - step + edge - offset, share)
    low_out = jnp.transpose(low_out.reshape(n_dp, pieces, n_col, share), (2, 0, 1, 3))
    got_out = to_owner(low_out.reshape(-1, share))
    got_up = to_owner(grad_up.astype(low))
    low_down = grad_down.astype(low).reshape(4, n_dp, pieces, n_col, share)
    low_down = jnp.transpose(low_down, (3, 1, 0, 2, 4)).reshape(-1, share)
    got_down = to_owner(low_down)

    reduced = [
        each.astype(jnp.float32).reshape(like.shape)
        for each, like in (
            (got_heads, w_heads),
            (got_out, w_out),
            (got_up, w_up),
            (got_down, w_down),
            (col_sums[0:2], norm_vectors),
            (col_sums[2:6], width_vectors),
            (row_sums[6:8], attend_bias),
            (row_sums[8:12], hidden_vectors),
        )
    ]
    return result_tokens, input_gradient, reduced


def per_device(
    tokens,
    cotangent,
    segments,
    w_heads,
    w_out,
    w_up,
    w_down,
    norm_vectors,
    width_vectors,
    attend_bias,
    hidden_vectors,
    drift_heads,
    drift_out,
    drift_up,
    drift_down,
    drift_norm,
    drift_width,
    drift_attend,
    drift_hidden,
    power_heads,
    power_out,
    power_up,
    power_down,
    power_norm,
    power_width,
    power_attend,
    power_hidden,
):
    weights = (
        w_heads,
        w_out,
        w_up,
        w_down,
        norm_vectors,
        width_vectors,
        attend_bias,
        hidden_vectors,
    )
    firsts = (
        drift_heads,
        drift_out,
        drift_up,
        drift_down,
        drift_norm,
        drift_width,
        drift_attend,
        drift_hidden,
    )
    seconds = (
        power_heads,
        power_out,
        power_up,
        power_down,
        power_norm,
        power_width,
        power_attend,
        power_hidden,
    )
    sizes = tuple(lax.axis_size(name) for name in ("dp", "row", "col"))
    if sizes == (2, 4, 4):
        return fused(tokens, cotangent, segments, weights, firsts, seconds)
    result_tokens, input_gradient, reduced = gathered(tokens, cotangent, segments, *weights)
    heads_up = adam(w_heads, reduced[0], drift_heads, power_heads, 0.05, MATRIX_DECAY)
    out_up = adam(w_out, reduced[1], drift_out, power_out, 0.2, MATRIX_DECAY)
    up_up = adam(w_up, reduced[2], drift_up, power_up, 0.05, MATRIX_DECAY)
    down_up = adam(w_down, reduced[3], drift_down, power_down, 0.025, MATRIX_DECAY)
    norm_up = adam(norm_vectors, reduced[4], drift_norm, power_norm, 0.3, 0.0)
    width_up = adam(width_vectors, reduced[5], drift_width, power_width, 0.3, 0.0)
    attend_up = adam(attend_bias, reduced[6], drift_attend, power_attend, 0.3, 0.0)
    hidden_up = adam(hidden_vectors, reduced[7], drift_hidden, power_hidden, 0.3, 0.0)
    return (
        result_tokens,
        input_gradient,
        heads_up[0],
        heads_up[1],
        heads_up[2],
        out_up[0],
        out_up[1],
        out_up[2],
        up_up[0],
        up_up[1],
        up_up[2],
        down_up[0],
        down_up[1],
        down_up[2],
        norm_up[0],
        norm_up[1],
        norm_up[2],
        width_up[0],
        width_up[1],
        width_up[2],
        attend_up[0],
        attend_up[1],
        attend_up[2],
        hidden_up[0],
        hidden_up[1],
        hidden_up[2],
    )


def solution(mesh):
    return jax.shard_map(
        per_device,
        mesh=mesh,
        in_specs=(
            P(("dp", "row"), "col"),
            P(("dp", "row"), "col"),
            P("dp"),
            P("col", "dp", None, None, "row"),
            P("row", "dp", None, "col"),
            P("col", "dp", None, None, "row"),
            P(None, "row", "dp", None, "col"),
            P(None, "col", "dp", None),
            P(None, "col", "dp", None),
            P(None, "row", "dp", None),
            P(None, "row", "dp", None),
            P("col", "dp", None, None, "row"),
            P("row", "dp", None, "col"),
            P("col", "dp", None, None, "row"),
            P(None, "row", "dp", None, "col"),
            P(None, "col", "dp", None),
            P(None, "col", "dp", None),
            P(None, "row", "dp", None),
            P(None, "row", "dp", None),
            P("col", "dp", None, None, "row"),
            P("row", "dp", None, "col"),
            P("col", "dp", None, None, "row"),
            P(None, "row", "dp", None, "col"),
            P(None, "col", "dp", None),
            P(None, "col", "dp", None),
            P(None, "row", "dp", None),
            P(None, "row", "dp", None),
        ),
        out_specs=(
            P(("dp", "row"), "col"),
            P(("dp", "row"), "col"),
            P("col", "dp", None, None, "row"),
            P("col", "dp", None, None, "row"),
            P("col", "dp", None, None, "row"),
            P("row", "dp", None, "col"),
            P("row", "dp", None, "col"),
            P("row", "dp", None, "col"),
            P("col", "dp", None, None, "row"),
            P("col", "dp", None, None, "row"),
            P("col", "dp", None, None, "row"),
            P(None, "row", "dp", None, "col"),
            P(None, "row", "dp", None, "col"),
            P(None, "row", "dp", None, "col"),
            P(None, "col", "dp", None),
            P(None, "col", "dp", None),
            P(None, "col", "dp", None),
            P(None, "col", "dp", None),
            P(None, "col", "dp", None),
            P(None, "col", "dp", None),
            P(None, "row", "dp", None),
            P(None, "row", "dp", None),
            P(None, "row", "dp", None),
            P(None, "row", "dp", None),
            P(None, "row", "dp", None),
            P(None, "row", "dp", None),
        ),
        check_vma=False,
    )
```

```python
import functools

import jax
import jax.numpy as jnp
from jax import lax
from jax.experimental import pallas as pl
from jax.experimental.pallas import tpu as pltpu
from jax.sharding import PartitionSpec as P

HEADS = 25
HD = 64
TOK_DEV = 128
STEP = 10


NORM_EPSILON = 1e-05
BETA_FIRST = 0.9
BETA_SECOND = 0.999
ADAM_EPSILON = 1e-08
MATRIX_DECAY = 0.1
MASKED = -1e30
ROOT = (2.0 / 3.141592653589793) ** 0.5
CUBIC = 0.044715
VMEM_BYTES = 66 * 1024 * 1024


def adam(weight, gradient, first, second, rate, decay):
    first_new = BETA_FIRST * first + (1.0 - BETA_FIRST) * gradient
    second_new = BETA_SECOND * second + (1.0 - BETA_SECOND) * gradient * gradient
    corrected = first_new / (1.0 - BETA_FIRST**STEP)
    divisor = jnp.sqrt(second_new / (1.0 - BETA_SECOND**STEP)) + ADAM_EPSILON
    return (first_new, second_new, weight - rate * (corrected / divisor + decay * weight))


def smooth(values):
    return jax.nn.gelu(values, approximate=True)


def ceil_to(count, unit):
    return -(-count // unit) * unit


class Sizes:
    def __init__(self, share, pieces, seq):
        self.share = share
        self.pieces = pieces
        self.block = ceil_to(pieces, 16)
        self.pair = 2 * self.block
        self.width = 4 * self.pair
        self.seq = seq
        self.part = seq // 4
        self.both = 2 * seq
        self.main = (HEADS // 4) * HD
        self.slack = share - self.main
        self.heads = ceil_to(3 * share, 256)
        self.mixed = ceil_to(pieces + 1, 128)
        self.hidden = ceil_to(4 * pieces + 1, 128)
        self.tiles = self.width // 128
        self.solid = self.hidden - 128
        self.tail = 4 * pieces - self.solid
        assert 0 < self.tail < 64


class Place:
    def __init__(self):
        self.d, self.r, self.c = (lax.axis_index(name) for name in ("dp", "row", "col"))
        self.y, self.k = self.r // 2, self.r % 2

    def plane(self, mask):
        d = 1 - self.d if mask & 4 else self.d
        y = 1 - self.y if mask & 2 else self.y
        k = 1 - self.k if mask & 1 else self.k
        return d, 2 * y + k

    def peer(self, mask):
        d, r = self.plane(mask)
        return (d, r, self.c)

    def along(self, c):
        return (self.d, self.r, c)


def run(when, action):
    if when is None:
        action()
    else:
        pl.when(when)(action)


class Wires:
    def __init__(self, sends, arrivals):
        self.sends, self.arrivals = sends, arrivals
        self.used = 0
        self.open = []

    def make(self, source, target, index, slot, device):
        return pltpu.make_async_remote_copy(
            src_ref=source,
            dst_ref=target,
            send_sem=self.sends.at[index],
            recv_sem=self.arrivals.at[slot],
            device_id=device,
            device_id_type=pl.DeviceIdType.MESH,
        )

    def copy(self, source, target, device, slot, when=None):
        made = self.make(source, target, self.used, slot, device)
        self.used += 1
        run(when, made.start)
        item = (when, made)
        self.open.append(item)
        return item

    def arrived(self, target, slot, device, when=None):
        run(when, self.make(target, target, 0, slot, device).wait_recv)

    def close(self, some=None):
        for item in self.open if some is None else some:
            run(item[0], item[1].wait_send)
        self.open = [] if some is None else [o for o in self.open if all(o is not s for s in some)]


def greet(at, diagonal):
    barrier = pltpu.get_barrier_semaphore()

    def signal(device):
        pl.semaphore_signal(
            barrier, inc=1, device_id=device, device_id_type=pl.DeviceIdType.MESH
        )

    for mask in range(1, 8):
        signal(at.peer(mask))
    for c in range(4):
        run(at.c != c, functools.partial(signal, (at.d, at.r, c)))
        if diagonal:
            run(at.c != c, functools.partial(signal, (1 - at.d, at.r, c)))
    run(at.r != at.c, functools.partial(signal, (at.d, at.c, at.r)))
    pl.semaphore_wait(barrier, (13 if diagonal else 10) + jnp.where(at.r != at.c, 1, 0))


def rows_at(start, size):
    return pl.ds(pl.multiple_of(start, 16), size)


def lanes_at(start, size):
    return pl.ds(pl.multiple_of(start, 128), size)


def choose(shape, source):
    rows = lax.broadcasted_iota(jnp.int32, shape, 0)
    wanted = source(lax.broadcasted_iota(jnp.int32, shape, 1))
    return (rows == wanted).astype(jnp.bfloat16)


def edge_source(column):
    part, place = column // HD, column % HD
    wanted = jnp.where(place >= 16, 128 * part + place - 16, 384 + 16 * part + place)
    return jnp.where(part < 3, wanted, -1)


def spread_source(column):
    part, place = column // 128, column % 128
    return jnp.where(place < HD, HD * part + place, -1)


def picked(values, table):
    return jnp.dot(values, table, preferred_element_type=jnp.float32).astype(jnp.bfloat16)


def times(left, right):
    return jnp.dot(left, right, preferred_element_type=jnp.float32)


def times_flipped(left, right):
    return lax.dot_general(
        left, right, (((1,), (1,)), ((), ())), preferred_element_type=jnp.float32
    )


def times_outer(left, right):
    return lax.dot_general(
        left, right, (((0,), (0,)), ((), ())), preferred_element_type=jnp.float32
    )


def over_tiles(total, action, tile=256):
    @pl.loop(0, total // tile)
    def _(i):
        action(i * tile, tile)

    if total % tile:
        action(total - total % tile, total % tile)


def turned(values):
    return values.astype(jnp.float32).T


def gather_group(wires, masks, region, at, base):
    own = region(*at.plane(0))
    sent = [wires.copy(own, own, at.peer(mask), base + mask) for mask in (1, *masks)]

    def finish():
        for mask in masks:
            there = region(*at.plane(mask))
            wires.arrived(there, base + mask, at.peer(mask))
            sent.append(wires.copy(there, there, at.peer(1), base + mask + 1))
        for mask in (0, *masks):
            there = region(*at.plane(mask | 1))
            wires.arrived(there, base + (mask | 1), at.peer(1))

    return finish, sent


def cross_over(wires, home, landing, region, at, base):
    rows = home.shape[0] // 2
    wires.copy(home.at[rows_at(rows * (1 - at.y), rows)], landing, at.peer(2), base)
    target = region(at.c, at.d, at.y)

    def along(source, s):
        wires.copy(source, target, at.along(s), base + 1 + at.c, s != at.c)

        @pl.when(s == at.c)
        def _():
            target[...] = source[...]

    along(home.at[rows_at(rows * at.y, rows)], at.r)

    def onward():
        wires.arrived(landing, base, at.peer(2))
        along(landing, 2 * (1 - at.y) + at.k)

    def finish():
        for c in range(4):
            needed = (at.k == at.c % 2) & (at.c != c)
            wires.arrived(region(c, at.d, at.y), base + 1 + c, at.along(c), needed)

    return onward, finish


def share_pieces(wires, masks, region, at, base):
    holds = at.k == at.c % 2
    near = base + 4 * len(masks)

    def place(mask):
        d, r = at.plane(mask)
        return d, r // 2

    for c in range(4):
        own = region(c, *place(0))
        for i, mask in enumerate(masks):
            wires.copy(own, own, at.peer(mask), base + 4 * i + c, holds)
    for c in range(4):
        own = region(c, *place(0))
        wires.copy(own, own, at.peer(1), near + c, holds)

    def finish():
        for i, mask in enumerate(masks):
            for c in range(4):
                there = region(c, *place(mask))
                wires.arrived(there, base + 4 * i + c, at.peer(mask), holds)
                wires.copy(there, there, at.peer(1), near + 4 * (i + 1) + c, holds)
        for i, mask in enumerate((0, *masks)):
            for c in range(4):
                there = region(c, *place(mask))
                wires.arrived(there, near + 4 * i + c, at.peer(1), jnp.logical_not(holds))

    return finish


def scatter_group(wires, masks, partial, chunk, near, mid, far, at, base):
    sent = []
    for i, mask in enumerate((0, *masks)):
        rows = rows_at(chunk(*at.plane(mask | 1)), near.shape[1])
        sent.append(wires.copy(partial.at[rows], near.at[i], at.peer(1), base + i))

    def rows_of(mask):
        return rows_at(chunk(*at.plane(mask)), near.shape[1])

    def onward():
        for i, mask in enumerate((0, *masks)):
            wires.arrived(near.at[i], base + i, at.peer(1))
        for i, mask in enumerate(masks):
            both = partial[rows_of(mask)].astype(jnp.float32) + near[i + 1].astype(jnp.float32)
            mid[i] = both.astype(jnp.bfloat16)
            sent.append(wires.copy(mid.at[i], far.at[i], at.peer(mask), base + 4 + i))

    def total():
        for i, mask in enumerate(masks):
            wires.arrived(far.at[i], base + 4 + i, at.peer(mask))
        result = partial[rows_of(0)].astype(jnp.float32) + near[0].astype(jnp.float32)
        for i in range(len(masks)):
            result = result + far[i].astype(jnp.float32)
        return result

    return onward, total, sent


def spread_col(wires, region, at, base, wait=False):
    own = region(at.c)

    def send(distance):
        for delta in (distance, -distance):
            there = at.c + delta
            wires.copy(own, own, at.along(there), base + at.c, (there >= 0) & (there < 4))

    if not wait:
        send(2)
        send(1)

    def relay():
        for here, start, end in ((2, 0, 3), (1, 3, 0)):
            block = region(start)
            wires.arrived(block, base + start, at.along(start), at.c == here)
            wires.copy(block, block, at.along(end), base + start, at.c == here)

    def finish():
        for c in range(4):
            needed = at.c != c
            if c == 0:
                needed = needed & (at.c != 2)
            if c == 3:
                needed = needed & (at.c != 1)
            wires.arrived(region(c), base + c, at.along(c), needed)

    return (send, relay, finish) if wait else (relay, finish)


def collect_col(wires, piece, landing, rest, at, base, direct=None):
    low_end, high_end = at.c == 0, at.c == 3
    ends = low_end | high_end
    via = jnp.where(low_end, 1, 2)

    def pick(*choices):
        return jnp.where(
            low_end,
            choices[0],
            jnp.where(at.c == 1, choices[1], jnp.where(high_end, choices[3], choices[2])),
        )

    order = (pick(3, 0, 3, 0), pick(2, 2, 1, 1), pick(1, 3, 0, 2), at.c)
    target = landing.at[at.c]

    def send(step):
        there = order[step]
        block = (direct or piece)(there)
        if step == 0:
            wires.copy(block, rest, at.along(via), base + 4, ends)
            wires.copy(block, target, at.along(there), base + at.c, jnp.logical_not(ends))
        elif step == 1:
            wires.copy(block, target, at.along(there), base + at.c)
        elif step == 2:
            wires.copy(block, target, at.along(there), base + at.c, ends)

    def relay(add):
        @pl.when(jnp.logical_not(ends))
        def _():
            wires.make(rest, rest, 0, base + 4, at.along(0)).wait_recv()
            add(order[2])

        wires.copy(piece(order[2]), target, at.along(order[2]), base + at.c, jnp.logical_not(ends))

    def arrived(c):
        wires.arrived(landing.at[c], base + c, at.along(c), sent_from(c))

    def sent_from(c):
        here = at.c != c
        if c in (0, 3):
            here = here & (at.c != 3 - c)
        return here

    return order, send, relay, arrived, sent_from


def forward_kernel(
    sz,
    x_home_in,
    dy_home_in,
    w_heads,
    w_out,
    w_up,
    w_down,
    norm_vectors,
    width_vectors,
    attend_bias,
    hidden_vectors,
    segments,
    wh_out,
    wo_out,
    wu_out,
    wd_out,
    h1_t_out,
    h2_t_out,
    gd_out,
    gt_out,
    dy_out,
    u_out,
    gl_out,
    qw_out,
    kw_out,
    vw_out,
    a_nat_out,
    lse_out,
    x2_out,
    x_own_out,
    vec_rows_out,
    wh,
    wo,
    wu,
    wd,
    h1_t,
    h2_t,
    gd,
    gt,
    dy_t,
    dy,
    u,
    gl,
    qw,
    kw,
    vw,
    a_nat,
    lse,
    x2,
    x_own,
    vec_rows,
    x_t,
    h1,
    h2,
    own_qkv,
    aw,
    vec,
    part,
    edge_out,
    edge_in,
    edge_back,
    near,
    mid,
    far,
    x_raw,
    dy_raw,
    heads_raw,
    out_raw,
    up_raw,
    down_raw,
    x_home,
    dy_home,
    wu_own,
    wd_tail,
    col_labels,
    x_half,
    dy_half,
    sends,
    arrivals,
    locals_,
):
    at = Place()
    wires = Wires(sends, arrivals)
    low = jnp.bfloat16
    pair, block, pieces = sz.pair, sz.block, sz.pieces
    fetched = []
    for i, (source, target) in enumerate(
        (
            (x_home_in, x_raw),
            (w_heads, heads_raw),
            (w_up, up_raw),
            (w_out, out_raw),
            (w_down, down_raw),
            (dy_home_in, dy_raw),
        )
    ):
        fetched.append(pltpu.make_async_copy(source, target, locals_.at[40 + i]))
        fetched[i].start()
    row_labels = segments.at[:, lanes_at(sz.seq * at.c, sz.seq)]

    def halves(value, target):
        value = value.astype(jnp.float32)
        gap = jnp.zeros((block - pieces, value.shape[1]), jnp.float32)
        parts = [value[0:pieces], gap, value[pieces : 2 * pieces], gap]
        target[...] = jnp.concatenate(parts, axis=0).astype(low)

    def quarter(row):
        return row.astype(low).astype(jnp.float32) * 0.25

    def placed(row):
        both = jnp.concatenate([row, row], axis=1)
        half_of = lax.broadcasted_iota(jnp.int32, both.shape, 1) // pieces
        return jnp.where(half_of == at.d, both, 0.0)

    def with_row(value, row):
        gap = jnp.zeros((block - pieces - 1, value.shape[1]), jnp.float32)
        return jnp.concatenate([value, row, gap], axis=0)

    flat = jnp.concatenate(
        [norm_vectors[0], norm_vectors[1], width_vectors[1], width_vectors[2]], axis=0
    )
    flat = jnp.concatenate([flat, jnp.zeros((124, pieces), jnp.float32)], axis=0)
    flat = jnp.concatenate([flat, jnp.zeros((128, 256 - pieces), jnp.float32)], axis=1)
    where_row = lax.broadcasted_iota(jnp.int32, flat.shape, 0)
    where_lane = lax.broadcasted_iota(jnp.int32, flat.shape, 1)
    carrier = (where_lane == pieces) & ((where_row == 1) | (where_row == 3))
    own_rows = rows_at(pair * at.c + block * at.d, block)
    vec[own_rows] = jnp.where(carrier, 1.0, flat).T[0:block].astype(low)
    fetched[0].wait()
    halves(x_raw[...], x_home)
    greet(at, False)

    def x_piece(c, d, y):
        return x_t.at[rows_at(pair * c + block * y, block)]

    def dy_piece(c, d, y):
        return dy_t.at[rows_at(pair * c + block * y, block), lanes_at(sz.seq * d, sz.seq)]

    used = [0]

    def flush(source, target):
        made = pltpu.make_async_copy(source, target, locals_.at[used[0]])
        used[0] += 1
        made.start()
        flushed.append(made)

    flushed = []

    def vec_block(d, c):
        return vec.at[rows_at(pair * c + block * d, block)]

    def wh_block(d):
        return lambda c: wh.at[rows_at(pair * c + block * d, block)]

    def wo_block(d):
        return lambda c: wo.at[rows_at(pair * c, pair), lanes_at(sz.mixed * d, sz.mixed)]

    def wu_block(d):
        return lambda c: wu.at[rows_at(pair * c + block * d, block)]

    def wd_block(half):
        return lambda c: wd.at[rows_at(pair * c + block * half, block)]

    x_onward, x_crossed = cross_over(wires, x_home, x_half, x_piece, at, 96)
    for c in range(4):
        wires.copy(vec_block(at.d, at.c), vec_block(at.d, at.c), at.along(c), 2 + at.c, at.c != c)
    wires.copy(vec_block(at.d, at.c), vec_block(at.d, at.c), at.peer(4), 6 + at.c)

    fetched[1].wait()
    for r in range(4):

        @pl.when(at.r == r)
        def _():
            cut = sz.share - sz.slack * r
            tails = []
            for i in range(3):
                value = heads_raw[i]
                row = jnp.zeros((1, sz.share), jnp.float32)
                if i != 1:
                    row = placed(quarter(attend_bias[i // 2]))
                value = with_row(value, row)
                if r:
                    value = jnp.concatenate([value[:, cut:], value[:, 0:cut]], axis=1)
                wh[own_rows, sz.main * i : sz.main * (i + 1)] = value[:, 0 : sz.main].astype(low)
                tails.append(value[:, sz.main :])
            tails.append(jnp.zeros((block, sz.heads - 3 * sz.share), jnp.float32))
            wh[own_rows, 3 * sz.main : sz.heads] = jnp.concatenate(tails, axis=1).astype(low)

    x_onward()
    wh_relay, wh_done = spread_col(wires, wh_block(at.d), at, 20)
    wires.copy(wh_block(at.d)(at.c), wh_block(at.d)(at.c), at.peer(4), 24 + at.c)

    fetched[2].wait()
    gap = jnp.zeros((block, sz.hidden - 4 * pieces), jnp.float32)
    values = [
        with_row(up_raw[:, j, :], placed(quarter(hidden_vectors[j]))) for j in range(4)
    ]
    for i in range(2):
        lanes = slice(pieces * i, pieces * (i + 1))
        whole = jnp.concatenate([value[:, lanes] for value in values] + [gap], axis=1)

        @pl.when(at.d == i)
        def _():
            wu[own_rows] = whole.astype(low)

        @pl.when(at.d != i)
        def _():
            wu_own[...] = whole.astype(low)

    wires.copy(wu_own, wu_block(at.d)(at.c), at.peer(4), 10)

    def turned_halves(value, target, rows, lanes):
        flipped = value.T
        gap = jnp.zeros((block - pieces, flipped.shape[1]), jnp.float32)
        parts = [flipped[0:pieces], gap, flipped[pieces : 2 * pieces], gap]
        target[rows, lanes] = jnp.concatenate(parts, axis=0).astype(low)

    fetched[3].wait()
    value = with_row(out_raw[...], placed(quarter(width_vectors[0])))
    value = jnp.concatenate([value, jnp.zeros((sz.mixed - block, sz.share), jnp.float32)], axis=0)
    for i in range(sz.mixed // 128):
        lanes = slice(128 * i, 128 * (i + 1))
        turned_halves(
            value[lanes], wo, rows_at(pair * at.c, pair), lanes_at(sz.mixed * at.d + 128 * i, 128)
        )
    wo_relay, wo_done = spread_col(wires, wo_block(at.d), at, 28)
    wires.copy(wo_block(at.d)(at.c), wo_block(at.d)(at.c), at.peer(4), 32 + at.c)

    fetched[5].wait()
    halves(dy_raw[...], dy_home)
    dy_onward, dy_crossed = cross_over(wires, dy_home, dy_half, dy_piece, at, 116)

    x_crossed()
    x_done = share_pieces(wires, (2,), x_piece, at, 104)

    fetched[4].wait()
    for i in range(sz.solid // 128):
        rows = slice(128 * i, 128 * (i + 1))
        turned_halves(down_raw[rows], wd, rows_at(pair * at.c, pair), rows)
    value = [
        jnp.zeros((64, sz.share), jnp.float32),
        down_raw[sz.solid : 4 * pieces],
        placed(quarter(width_vectors[3])),
        jnp.zeros((63 - sz.tail, sz.share), jnp.float32),
    ]
    turned_halves(jnp.concatenate(value, axis=0), wd_tail, slice(0, pair), slice(0, 128))

    def add_tail(d):
        rows = rows_at(pair * at.c + block * d, block)
        both = wu[rows, sz.solid : sz.hidden].astype(jnp.float32)
        both = both + wd_tail[rows_at(block * d, block)].astype(jnp.float32)
        wu[rows, sz.solid : sz.hidden] = both.astype(low)

    add_tail(at.d)
    col_labels[...] = jnp.concatenate([row_labels[...]] * 8, axis=0).astype(jnp.float32).T[:, 0:1]
    x_done()
    dy_onward()
    wires.arrived(wu_block(1 - at.d)(at.c), 10, at.peer(4))
    add_tail(1 - at.d)
    wu_first_send, wu_first, wu_first_done = spread_col(wires, wu_block(at.d), at, 36, True)
    wu_second_send, wu_second, wu_second_done = spread_col(wires, wu_block(1 - at.d), at, 40, True)
    for distance in (2, 1):
        wu_first_send(distance)
        wu_second_send(distance)

    for c in range(4):
        wires.arrived(vec_block(at.d, c), 2 + c, at.along(c), at.c != c)
    wires.arrived(vec_block(1 - at.d, at.c), 6 + at.c, at.peer(4))
    for step in range(1, 4):
        there = (at.c + step) % 4
        wires.copy(
            vec_block(at.d, there), vec_block(at.d, there), at.peer(4), 6 + there
        )
    for step in range(1, 4):
        there = (at.c + step) % 4
        wires.arrived(vec_block(1 - at.d, there), 6 + there, at.peer(4))
    features = 4.0 * sz.share

    def add_up(i, carry):
        rows = rows_at(128 * i, 128)
        value = x_t[rows].astype(jnp.float32)
        return (
            carry[0] + jnp.sum(value, axis=0, keepdims=True),
            carry[1] + jnp.sum(value * value, axis=0, keepdims=True),
        )

    zero = jnp.zeros((1, sz.seq), jnp.float32)
    sums = lax.fori_loop(0, sz.tiles, add_up, (zero, zero))
    center = sums[0] / features
    inverse = lax.rsqrt(sums[1] / features - center * center + NORM_EPSILON)

    @pl.loop(0, sz.tiles)
    def _(i):
        rows, lanes = rows_at(128 * i, 128), lanes_at(128 * i, 128)
        vectors = vec[rows].astype(jnp.float32)
        value = (x_t[rows].astype(jnp.float32) - center) * inverse
        value = value * vectors[:, 0:1] + vectors[:, 1:2]
        h1_t[rows] = value.astype(low)
        h1[:, lanes] = value.T.astype(low)
        mine = x_t[rows, lanes_at(sz.part * at.r, sz.part)]
        x_own[:, lanes] = turned(mine).astype(low)
        vec_rows[:, lanes] = vectors.T[0:8]

    flush(h1_t, h1_t_out)
    flush(x_own, x_own_out)
    flush(vec_rows, vec_rows_out)

    wh_relay()
    for c in range(4):
        needed = at.c != c
        if c == 0:
            needed = needed & (at.c != 2)
        if c == 3:
            needed = needed & (at.c != 1)
        wires.arrived(wh_block(at.d)(c), 20 + c, at.along(c), needed)
        wires.copy(wh_block(at.d)(c), wh_block(at.d)(c), at.peer(4), 24 + c, at.c != c)

    for c in range(4):
        wires.arrived(wh_block(1 - at.d)(c), 24 + c, at.peer(4))
    flush(wh, wh_out)

    @pl.loop(0, sz.heads // 256)
    def _(i):
        lanes = lanes_at(256 * i, 256)
        own_qkv[:, lanes] = times(h1[...], wh[:, lanes]).astype(low)

    starts = (0, sz.main, 2 * sz.main, 3 * sz.main)
    ends = jnp.concatenate([own_qkv[:, s : s + 128] for s in starts], axis=1)
    edge_out[...] = picked(ends, choose((512, 256), edge_source))
    last = at.r == 3

    @pl.when(at.r == 0)
    def _():
        edge_in[...] = jnp.zeros_like(edge_in)

    wires.copy(edge_out, edge_in, (at.d, at.r + 1, at.c), 52, at.r < 3)
    spread = choose((256, 384), spread_source)
    extra = picked(edge_out[...], spread)
    wires.arrived(edge_in, 52, (at.d, at.r - 1, at.c), at.r > 0)
    first = picked(edge_in[...], spread)
    lane = lax.broadcasted_iota(jnp.int32, (sz.seq, 128), 1)
    for i, target in enumerate((qw, kw, vw)):
        start = starts[i]
        target[:, 0:128] = jnp.where(
            lane < sz.slack * at.r,
            first[:, 128 * i : 128 * i + 128],
            own_qkv[:, start : start + 128],
        )
        target[:, 128 : sz.main] = own_qkv[:, start + 128 : start + sz.main]
        target[:, sz.main : sz.main + 128] = extra[:, 128 * i : 128 * i + 128]
    flush(qw, qw_out)
    flush(kw, kw_out)
    flush(vw, vw_out)

    wo_relay()
    for c in range(4):
        needed = at.c != c
        if c == 0:
            needed = needed & (at.c != 2)
        if c == 3:
            needed = needed & (at.c != 1)
        wires.arrived(wo_block(at.d)(c), 28 + c, at.along(c), needed)
        wires.copy(wo_block(at.d)(c), wo_block(at.d)(c), at.peer(4), 32 + c, at.c != c)

    dy_crossed()
    dy_done = share_pieces(wires, (2, 4, 6), dy_piece, at, 124)

    half = sz.seq // 2

    def heads_of(p, count):
        tile = lanes_at(128 * p, 128)
        for q in range(2):
            rows = slice(half * q, half * (q + 1))
            keys = half * (q + 1)
            order = lax.broadcasted_iota(jnp.int32, (half, keys), 0) + half * q
            allowed = (col_labels[rows, :] == row_labels[:, 0:keys].astype(jnp.float32)) & (
                order >= lax.broadcasted_iota(jnp.int32, (half, keys), 1)
            )
            lanes = lax.broadcasted_iota(jnp.int32, (half, 128), 1)
            side = lanes // HD
            total = jnp.zeros((half, 128), jnp.float32)
            for h in range(count):
                queries = jnp.where(side == h, qw[rows, tile].astype(jnp.float32) * HD ** (-0.5), 0.0)
                scores = times_flipped(queries.astype(low), kw[0:keys, tile])
                scores = jnp.where(allowed, scores, MASKED)
                highest = jnp.max(scores, axis=1, keepdims=True)
                raised = jnp.exp(scores - highest)
                summed = jnp.sum(raised, axis=1, keepdims=True)
                found = highest + jnp.log(summed)
                lse[rows, :] = jnp.where(lanes == 2 * p + h, found, lse[rows, :])
                soft = (raised * (1.0 / summed)).astype(low)
                total = jnp.where(side == h, times(soft, vw[0:keys, tile]), total)
            aw[rows, tile] = total.astype(low)

    lse[...] = jnp.zeros_like(lse)

    @pl.loop(0, sz.main // 128)
    def _(p):
        heads_of(p, 2)

    @pl.when(last)
    def _():
        heads_of(sz.main // 128, 1)
        edge_back[...] = aw[:, sz.main : sz.main + 128]

    flush(lse, lse_out)

    wires.copy(aw.at[:, 0:128], edge_back, (at.d, at.r - 1, at.c), 53, at.r > 0)
    wd_first_send, wd_first, wd_first_done = spread_col(wires, wd_block(0), at, 44, True)
    wd_second_send, wd_second, wd_second_done = spread_col(wires, wd_block(1), at, 48, True)
    for distance in (2, 1):
        wd_first_send(distance)
        wd_second_send(distance)
    wires.arrived(edge_back, 53, (at.d, at.r + 1, at.c), at.r < 3)

    def natural(column):
        inner = column % sz.mixed
        place = sz.pieces * (column // sz.mixed) + inner + sz.slack * at.r
        return jnp.where(inner < sz.pieces, place, -1)

    def natural_main(column):
        place = natural(column)
        return jnp.where(place < sz.main, place, -1)

    def natural_edge(column):
        return natural(column) - sz.main

    mixed = times(aw[:, 0 : sz.main], choose((sz.main, 2 * sz.mixed), natural_main))
    mixed = mixed + times(edge_back[...], choose((128, 2 * sz.mixed), natural_edge))
    ones = lax.broadcasted_iota(jnp.int32, mixed.shape, 1) % sz.mixed == sz.pieces
    a_nat[...] = jnp.where(ones, 1.0, mixed).astype(low)
    for c in range(4):
        wires.arrived(wo_block(1 - at.d)(c), 32 + c, at.peer(4))
    flush(wo, wo_out)
    flush(a_nat, a_nat_out)

    def project(start, tile):
        out = times_flipped(a_nat[...], wo[rows_at(start, tile)])
        part[:, lanes_at(start, tile)] = out.astype(low)

    over_tiles(sz.width, project)

    onward, total, _ = scatter_group(
        wires, (2,), part, lambda d, r: sz.part * r, near, mid, far, at, 64
    )
    onward()
    wu_first()
    wu_second()
    dy_done()
    middle = x_own[...].astype(jnp.float32) + total()
    x2[...] = middle
    flush(x2, x2_out)
    center = jnp.sum(middle, axis=1, keepdims=True) / features
    spread_two = jnp.sum(middle * middle, axis=1, keepdims=True) / features - center * center
    normed = (middle - center) * lax.rsqrt(spread_two + NORM_EPSILON)
    own_rows = rows_at(sz.part * (4 * at.d + at.r), sz.part)
    h2[own_rows] = (normed * vec_rows[2:3] + vec_rows[3:4]).astype(low)
    h2_done, _ = gather_group(
        wires, (2, 4, 6), lambda d, r: h2.at[rows_at(sz.part * (4 * d + r), sz.part)], at, 72
    )
    @pl.loop(0, sz.tiles)
    def _(i):
        dy[:, lanes_at(128 * i, 128)] = turned(dy_t[rows_at(128 * i, 128)]).astype(low)

    flush(dy, dy_out)
    h2_done()
    wu_first_done()
    wu_second_done()
    flush(wu, wu_out)

    def expand(start, tile):
        lanes = lanes_at(start, tile)
        value = times(h2[...], wu[:, lanes])
        u[:, lanes] = value
        inner = jnp.tanh(ROOT * (value + CUBIC * value * value * value))
        value = 0.5 * value * (1.0 + inner)
        if isinstance(start, int):
            column = lax.broadcasted_iota(jnp.int32, value.shape, 1)
            inside = (column >= 64) & (column < 64 + sz.tail)
            value = jnp.where(inside, pltpu.roll(value, 64, 1), 0.0)
            value = jnp.where(column == 64 + sz.tail, 1.0, value)
        gl[:, lanes] = value.astype(low)

    over_tiles(sz.hidden, expand)

    flush(u, u_out)
    flush(gl, gl_out)
    wd_first()

    @pl.loop(0, sz.tiles)
    def _(i):
        h2_t[rows_at(128 * i, 128)] = turned(h2[:, lanes_at(128 * i, 128)]).astype(low)

    flush(h2_t, h2_t_out)
    wd_second()

    @pl.loop(0, 4)
    def _(i):
        rows = rows_at(pair * i, pair)
        gd[rows] = times(dy_t[rows], gl[:, 0 : sz.solid]).astype(low)
        gt[rows] = times(dy_t[rows], gl[:, sz.solid : sz.hidden]).astype(low)

    flush(gd, gd_out)
    flush(gt, gt_out)
    wd_first_done()
    wd_second_done()
    flush(wd, wd_out)
    wires.close()
    for made in flushed:
        made.wait()


def backward_kernel(
    sz,
    dy_all,
    gd_all,
    gt_all,
    u_all,
    gl_all,
    h2_t_all,
    wd_all,
    wu_all,
    wo_all,
    wh_all,
    h1_t_all,
    qw_all,
    kw_all,
    vw_all,
    a_nat_all,
    lse_all,
    x2_all,
    x_own_all,
    vec_rows,
    segments,
    out_down,
    out_up,
    out_out,
    out_heads,
    result_home,
    grad_home,
    vec_out,
    zd,
    zu,
    zo,
    zh,
    res_all,
    res_two,
    grad_all,
    grad_two,
    rd,
    ru,
    ro,
    rh,
    qw,
    kw,
    vw,
    a_nat,
    lse,
    x2,
    x_own,
    xu,
    dy,
    dy_t,
    u,
    gl,
    h2_t,
    wd,
    wu,
    wo,
    wh,
    gt,
    dy_own,
    du,
    gw,
    gu,
    go,
    xh,
    xo,
    near_two,
    far_two,
    near_res,
    far_res,
    near_one,
    far_one,
    mid,
    dob,
    da,
    dk_sum,
    dv_sum,
    dx2,
    edge_out,
    edge_in,
    fore_out,
    fore_in,
    col_labels,
    res_stage,
    grad_stage,
    va,
    vb,
    sends,
    arrivals,
    locals_,
):
    at = Place()
    wires = Wires(sends, arrivals)
    low = jnp.bfloat16
    pair, block = sz.pair, sz.block
    features = 4.0 * sz.share
    used = [0]

    def load(source, target, when=None):
        made = pltpu.make_async_copy(source, target, locals_.at[used[0]])
        used[0] += 1
        run(when, made.start)
        return made

    own_rows = rows_at(sz.part * (4 * at.d + at.r), sz.part)
    gd = gw.at[:, 0 : sz.solid]
    loads = [
        load(s, t)
        for s, t in (
            (dy_all, dy),
            (wd_all, wd),
            (u_all, u),
            (dy_all.at[own_rows], dy_own),
            (wu_all, wu),
            (h2_t_all, h2_t),
            (gl_all, gl),
            (gd_all, gd),
            (wo_all, wo),
            (wh_all, wh),
            (x2_all, x2),
            (a_nat_all, a_nat),
            (qw_all, qw),
            (kw_all, kw),
            (vw_all, vw),
            (lse_all, lse),
            (x_own_all, x_own),
            (h1_t_all, dy_t.at[:, 0 : sz.seq]),
            (gt_all, gt),
        )
    ]
    greet(at, False)
    stay = []

    order, d_send, d_relay, d_arrived, d_from = collect_col(
        wires,
        lambda c: gd.at[rows_at(pair * c, pair)],
        zd,
        rd,
        at,
        0,
        lambda c: gd_all.at[rows_at(pair * c, pair)],
    )
    for step in range(4):
        d_send(step)

    def relay_of(rest, block):
        def add(there):
            rows = rows_at(pair * there, pair)
            block[rows] = (block[rows].astype(jnp.float32) + rest[...].astype(jnp.float32)).astype(low)

        return add

    for made in (*loads[0:3], loads[4]):
        made.wait()

    def through(start, tile):
        lanes = lanes_at(start, tile)
        last = isinstance(start, int)
        if last:
            upstream = pltpu.roll(times(dy[...], wu[:, lanes]), 64, 1)
        else:
            upstream = times(dy[...], wd[:, lanes])
        value = u[:, lanes]
        inner = jnp.tanh(ROOT * (value + CUBIC * value * value * value))
        slope = 0.5 * (1.0 + inner) + 0.5 * value * (1.0 - inner * inner) * ROOT * (
            1.0 + 3.0 * CUBIC * value * value
        )
        upstream = upstream * slope
        if last:
            column = lax.broadcasted_iota(jnp.int32, upstream.shape, 1)
            upstream = jnp.where(column < sz.tail, upstream, 0.0)
        du[:, lanes] = upstream.astype(low)

    over_tiles(sz.hidden, through)
    def back_up(start, tile):
        dy[:, lanes_at(start, tile)] = times_flipped(du[...], wu[rows_at(start, tile)]).astype(low)

    over_tiles(sz.width, back_up)

    def chunk_both(d, r):
        return sz.part * (4 * d + r)

    two_onward, two_total, two_sent = scatter_group(
        wires, (2, 4, 6), dy, chunk_both, near_two, mid, far_two, at, 16
    )
    loads[5].wait()
    loads[18].wait()
    order, u_send, u_relay, u_arrived, u_from = collect_col(
        wires, lambda c: gu.at[rows_at(pair * c, pair)], zu, ru, at, 5
    )
    for step in range(4):
        rows = rows_at(pair * order[step], pair)
        value = times(h2_t[rows], du[...])
        gu[rows, 0 : sz.solid] = value[:, 0 : sz.solid].astype(low)
        both = value[:, sz.solid : sz.hidden] + gt[rows].astype(jnp.float32)
        gu[rows, sz.solid : sz.hidden] = both.astype(low)
        u_send(step)
        if step == 1:
            two_onward()
    own = rows_at(pair * at.c, pair)
    gd_own = load(gd_all.at[own], h2_t.at[own, 0 : sz.solid])
    loads[7].wait()
    before = len(wires.open)
    d_relay(relay_of(rd, gd))
    gd_sends = wires.open[before:]

    def norm_back(upstream, values, gain):
        center = jnp.sum(values, axis=1, keepdims=True) / features
        spread = jnp.sum(values * values, axis=1, keepdims=True) / features - center * center
        inverse = lax.rsqrt(spread + NORM_EPSILON)
        centered = (values - center) * inverse
        scaled = upstream * gain
        inner = (
            scaled
            - jnp.sum(scaled, axis=1, keepdims=True) / features
            - centered * (jnp.sum(scaled * centered, axis=1, keepdims=True) / features)
        )
        return (
            inner * inverse,
            jnp.sum(upstream * centered, axis=0, keepdims=True),
            jnp.sum(upstream, axis=0, keepdims=True),
        )

    loads[10].wait()
    loads[3].wait()
    h2_back = two_total()
    through_norm, gain_two, shift_two = norm_back(h2_back, x2[...], vec_rows[2:3])
    middle_back = dy_own[...].astype(jnp.float32) + through_norm
    dx2[...] = middle_back
    va[0, 2:3] = gain_two
    va[0, 3:4] = shift_two
    va[0, 4:8] = jnp.zeros((4, sz.width), jnp.float32)
    dob[rows_at(sz.part * at.r, sz.part)] = middle_back.astype(low)
    dob_done, dob_sent = gather_group(
        wires, (2,), lambda d, r: dob.at[rows_at(sz.part * r, sz.part)], at, 24
    )

    def contract(start, tile):
        rows = rows_at(start, tile)
        out = times_flipped(gl[:, 0 : sz.solid], wd[rows])
        out = out + times_flipped(gl[:, sz.solid : sz.hidden], wu[rows, sz.solid : sz.hidden])
        dy[:, lanes_at(start, tile)] = out.astype(low)

    wires.close(two_sent)
    loads[6].wait()
    over_tiles(sz.width, contract)
    res_onward, res_total, res_sent = scatter_group(
        wires, (2, 4, 6), dy, chunk_both, near_res, mid, far_res, at, 32
    )

    dob_done()
    loads[11].wait()
    loads[8].wait()
    da[...] = times(dob[...], wo[...]).astype(low)
    slack, main = sz.slack, sz.main

    def from_natural(place):
        wanted = sz.mixed * (place // sz.pieces) + place % sz.pieces
        return jnp.where((place >= 0) & (place < sz.share), wanted, -1)

    fore_out[...] = picked(
        da[...], choose((2 * sz.mixed, 128), lambda j: from_natural(j + main - slack * at.r))
    )

    @pl.when(at.r == 0)
    def _():
        fore_in[...] = jnp.zeros_like(fore_in)

    wires.copy(fore_out, fore_in, (at.d, at.r + 1, at.c), 40, at.r < 3)

    @pl.loop(0, sz.tiles)
    def _(i):
        dy_t[rows_at(128 * i, 128), sz.seq : sz.both] = turned(dob[:, lanes_at(128 * i, 128)]).astype(low)

    res_onward()

    for step in range(4):
        there = (at.c + step) % 4
        rows = rows_at(pair * there, pair)
        go[rows] = times(dy_t[rows, sz.seq : sz.both], a_nat[...]).astype(low)
        wires.copy(
            go.at[rows, lanes_at(sz.mixed * (1 - at.d), sz.mixed)], xo.at[there], at.peer(4), 48 + there
        )
    wires.arrived(fore_in, 40, (at.d, at.r - 1, at.c), at.r > 0)
    window = times(da[...], choose((2 * sz.mixed, main), lambda j: from_natural(j - slack * at.r)))
    da_first = window[:, 0:128] + fore_in[...].astype(jnp.float32)
    da[:, 128:main] = window[:, 128:main].astype(low)
    da[:, 0:128] = da_first.astype(low)
    da[:, main : main + 128] = fore_out[...]

    row_labels = segments.at[:, lanes_at(sz.seq * at.c, sz.seq)]
    col_labels[...] = jnp.concatenate([row_labels[...]] * 8, axis=0).astype(jnp.float32).T[:, 0:1]
    for made in loads[12:17]:
        made.wait()
    half = sz.seq // 2
    dqw, dkw = (du.at[sz.seq * i : sz.seq * (i + 1), 0 : main + 128] for i in range(2))
    dvw = gl.at[0 : sz.seq, 0 : main + 128]

    def heads_back(p, count):
        tile = lanes_at(128 * p, 128)
        dk_sum[...] = jnp.zeros_like(dk_sum)
        dv_sum[...] = jnp.zeros_like(dv_sum)
        for q in range(2):
            rows = slice(half * q, half * (q + 1))
            keys = half * (q + 1)
            order = lax.broadcasted_iota(jnp.int32, (half, keys), 0) + half * q
            allowed = (col_labels[rows, :] == row_labels[:, 0:keys].astype(jnp.float32)) & (
                order >= lax.broadcasted_iota(jnp.int32, (half, keys), 1)
            )
            lanes = lax.broadcasted_iota(jnp.int32, (half, 128), 1)
            side = lanes // HD
            total = jnp.zeros((half, 128), jnp.float32)
            for h in range(count):
                queries = jnp.where(side == h, qw[rows, tile].astype(jnp.float32) * HD ** (-0.5), 0.0)
                queries = queries.astype(low)
                pulled = jnp.where(side == h, da[rows, tile].astype(jnp.float32), 0.0).astype(low)
                found = jnp.sum(jnp.where(lanes == 2 * p + h, lse[rows, :], 0.0), axis=1, keepdims=True)
                scores = times_flipped(queries, kw[0:keys, tile])
                soft = jnp.where(allowed, jnp.exp(jnp.where(allowed, scores - found, MASKED)), 0.0)
                soft_back = times_flipped(pulled, vw[0:keys, tile])
                inner = jnp.sum(soft_back * soft, axis=1, keepdims=True)
                score_back = (soft * (soft_back - inner)).astype(low)
                piece = times(score_back, kw[0:keys, tile]) * HD ** (-0.5)
                total = jnp.where(side == h, piece, total)
                dk_sum[0:keys] += times_outer(score_back, queries)
                dv_sum[0:keys] += times_outer(soft.astype(low), pulled)
            dqw[rows, tile] = total.astype(low)
        dkw[:, tile] = dk_sum[...].astype(low)
        dvw[:, tile] = dv_sum[...].astype(low)

    @pl.loop(0, main // 128)
    def _(p):
        heads_back(p, 2)

    @pl.when(at.r == 3)
    def _():
        heads_back(main // 128, 1)

    def compact(column):
        part, place = column // HD, column % HD
        return jnp.where(part < 3, 128 * part + place, -1)

    table = choose((384, 256), compact)
    backs = (dqw, dkw, dvw)
    edge_out[...] = picked(jnp.concatenate([b[:, 0:128] for b in backs], axis=1), table)
    wires.copy(edge_out, edge_in, (at.d, at.r - 1, at.c), 41, at.r > 0)

    @pl.when(at.r == 3)
    def _():
        edge_in[...] = picked(jnp.concatenate([b[:, main : main + 128] for b in backs], axis=1), table)

    u_relay(relay_of(ru, gu))

    def go_home(values, stage, every, halves, out, base):
        flipped = values.T
        for c in range(4):
            for y in range(2):
                rows = slice(pair * c + block * y, pair * c + block * (y + 1))
                stage[c, y] = flipped[rows].astype(low)
        holds = at.k == at.c % 2
        lanes = lanes_at(sz.part * at.r, sz.part)
        held = []
        for y in range(2):
            there = 2 * y + at.c % 2
            wires.copy(
                stage.at[:, y], every.at[:, :, lanes], (at.d, there, at.c), base + at.r, there != at.r
            )
            held.append((there == at.r, load(stage.at[:, y], every.at[:, :, lanes], there == at.r)))

        def along():
            for r in range(4):
                block_r = every.at[:, :, sz.part * r : sz.part * (r + 1)]
                wires.arrived(block_r, base + r, (at.d, r, at.c), holds & (at.r != r))
            for when, made in held:
                run(when, made.wait)
            del held[:]
            for c in range(4):
                wires.copy(
                    every.at[c], halves.at[at.c // 2], at.along(c), base + 4 + at.c // 2, holds & (at.c != c)
                )
                when = holds & (at.c == c)
                held.append((when, load(every.at[c], halves.at[at.c // 2], when)))

        def across():
            for when, made in held:
                run(when, made.wait)
            for t in range(2):
                there = 2 * t + at.k
                wires.arrived(halves.at[t], base + 4 + t, at.along(there), there != at.c)
            mine = out.at[rows_at(block * at.y, block)]
            wires.copy(halves.at[1 - at.y], mine, at.peer(2), base + 6)
            stay.append(load(halves.at[at.y], mine))

        def finish():
            wires.arrived(out.at[rows_at(block * (1 - at.y), block)], base + 6, at.peer(2))

        return along, across, finish

    res_along, res_across, res_finish = go_home(
        x2[...] + res_total(), res_stage, res_all, res_two, result_home, 56
    )
    wires.close(res_sent)

    wires.arrived(edge_in, 41, (at.d, at.r + 1, at.c), at.r < 3)

    def unfold(column):
        tile, lane = column // 128, column % 128
        inside = jnp.where(lane < HD - 16, HD * tile + lane + 16, -1)
        tail = jnp.where(lane < 48, HD * (lane // 16) + lane % 16, -1)
        return jnp.where(tile < 3, inside, tail)

    edges = picked(edge_in[...], choose((256, 512), unfold))
    lane = lax.broadcasted_iota(jnp.int32, (sz.seq, 128), 1)
    pieces = []
    for i, back in enumerate(backs):
        first = jnp.where(lane < slack * at.r, edges[:, 128 * i : 128 * i + 128], back[:, 0:128])
        pieces += [first, back[:, 128:main]]
    pieces.append(edges[:, 384:512])
    wires.close(dob_sent)
    own_back = dob.at[:, 0 : sz.heads]
    own_back[...] = jnp.concatenate(pieces, axis=1)

    wires.close(gd_sends)
    gd_own.wait()
    loads[17].wait()
    h_order, h_send, h_relay, h_arrived, h_from = collect_col(
        wires, lambda c: xh.at[c], zh, rh, at, 72
    )
    for step in range(4):
        there = h_order[step]
        rows = rows_at(pair * there, pair)
        gw[rows] = times(dy_t[rows, 0 : sz.seq], own_back[...]).astype(low)
        other = gw.at[rows_at(pair * there + block * (1 - at.d), block)]
        wires.copy(other, xh.at[there], at.peer(4), 80 + there)

    def o_heads(step):
        there = h_order[step]
        wires.arrived(xh.at[there], 80 + there, at.peer(4))
        mine = rows_at(pair * there + block * at.d, block)
        xh[there] = (gw[mine].astype(jnp.float32) + xh[there].astype(jnp.float32)).astype(low)
        h_send(step)

    for made in loads[9:10]:
        made.wait()

    def back_in(start, tile):
        out = times_flipped(own_back[...], wh[rows_at(start, tile)])
        dy[0 : sz.seq, lanes_at(start, tile)] = out.astype(low)

    over_tiles(sz.width, back_in)
    one_onward, one_total, _ = scatter_group(
        wires, (2,), dy, lambda d, r: sz.part * r, near_one, mid, far_one, at, 64
    )
    order, o_send, o_relay, o_arrived, o_from = collect_col(
        wires, lambda c: xo.at[c], zo, ro, at, 10
    )
    for step in range(4):
        there = order[step]
        wires.arrived(xo.at[there], 48 + there, at.peer(4))
        mine = go[rows_at(pair * there, pair), lanes_at(sz.mixed * at.d, sz.mixed)]
        xo[there] = (mine.astype(jnp.float32) + xo[there].astype(jnp.float32)).astype(low)
        o_send(step)

    def relay_out(there):
        both = xo[there].astype(jnp.float32) + ro[...].astype(jnp.float32)
        xo[there] = both.astype(low)

    brought = []

    def bring(c, landing, needed, lanes):
        made = load(landing.at[c], h2_t.at[pair * c : pair * (c + 1), 0:lanes], needed)
        brought.append((needed, made))

        @pl.when(jnp.logical_not(needed) & (at.c != c))
        def _():
            h2_t[pair * c : pair * (c + 1), 0:lanes] = jnp.zeros((pair, lanes), low)

    def summed(lanes):
        result = jnp.zeros((pair, lanes.stop - lanes.start), jnp.float32)
        for c in range(4):
            result = result + h2_t[pair * c : pair * (c + 1), lanes].astype(jnp.float32)
        return result

    half_rows = sz.pieces

    def natural_rows(value):
        flipped = value.T
        return jnp.concatenate(
            [flipped[:, 0:half_rows], flipped[:, block : block + half_rows]], axis=1
        )

    def own_half(row):
        return jnp.where(at.d == 0, row[:, 0:half_rows], row[:, half_rows : 2 * half_rows])

    def all_brought():
        for needed, made in brought:
            run(needed, made.wait)
        del brought[:]

    def relay_heads(there):
        xh[there] = (xh[there].astype(jnp.float32) + rh[...].astype(jnp.float32)).astype(low)

    res_along()
    one_onward()
    o_heads(0)
    h1_back = one_total()
    through_norm, gain_one, shift_one = norm_back(
        h1_back, x_own[...].astype(jnp.float32), vec_rows[0:1]
    )
    va[0, 0:1] = gain_one
    va[0, 1:2] = shift_one
    for mask in range(1, 8):
        wires.copy(va.at[0], va.at[mask], at.peer(mask), 84 + mask)
    grad_along, grad_across, grad_finish = go_home(
        dx2[...] + through_norm, grad_stage, grad_all, grad_two, grad_home, 104
    )
    for c in range(4):
        d_arrived(c)
        bring(c, zd, d_from(c), sz.solid)
    all_brought()
    for i in range(sz.solid // 128):
        rows = slice(128 * i, 128 * (i + 1))
        u[rows, 0 : sz.share] = natural_rows(summed(rows))
    down_out = load(u.at[0 : sz.solid, 0:512], out_down.at[0 : sz.solid])
    o_heads(1)
    grad_along()
    o_heads(2)
    h_relay(relay_heads)
    gu_own = load(gu.at[own], h2_t.at[own, 0 : sz.hidden])
    for c in range(4):
        u_arrived(c)
        bring(c, zu, u_from(c), sz.hidden)
    all_brought()
    gu_own.wait()
    value = natural_rows(summed(slice(sz.solid, sz.hidden)))
    end = 4 * sz.pieces
    u[sz.solid : end, 0 : sz.share] = value[64 : 64 + sz.tail]
    vec_out[5:6, 0:half_rows] = own_half(value[64 + sz.tail : 65 + sz.tail])
    tail_out = load(u.at[sz.solid : end, 0:512], out_down.at[sz.solid : end])
    theirs = rows_at(pair * at.c + block * (1 - at.d), block)

    def part_sum(side, lanes):
        result = jnp.zeros((block, sz.hidden), jnp.float32)
        for c in range(4):
            result = result + h2_t[rows_at(pair * c + block * side, block), lanes].astype(jnp.float32)
        return result

    every = slice(0, sz.hidden)
    gu[theirs] = part_sum(1 - at.d, every).astype(low)
    wires.copy(gu.at[theirs], xu, at.peer(4), 97)
    o_relay(relay_out)
    o_heads(3)
    res_across()
    mine_sum = part_sum(at.d, every)
    down_out.wait()
    tail_out.wait()
    wires.arrived(xu, 97, at.peer(4))
    partner_sum = xu[...].astype(jnp.float32)
    for side in range(2):

        @pl.when(at.d == side)
        def _():
            both = (mine_sum, partner_sum) if side == 0 else (partner_sum, mine_sum)
            for j in range(4):
                rows = slice(block * j, block * (j + 1))
                for i in range(2):
                    u[rows, half_rows * i : half_rows * (i + 1)] = both[i][:, half_rows * j : half_rows * (j + 1)]

    bias_sum = mine_sum[half_rows : half_rows + 1]
    for j in range(4):
        vec_out[8 + j : 9 + j, 0:half_rows] = bias_sum[:, half_rows * j : half_rows * (j + 1)]
    up_out = load(u.at[0 : 4 * block, 0:512], out_up)

    for c in range(4):
        o_arrived(c)
        needed = o_from(c)
        made = load(zo.at[c], wd.at[pair * c : pair * (c + 1), 0 : sz.mixed], needed)
        brought.append((needed, made))

        @pl.when(jnp.logical_not(needed))
        def _():
            wd[pair * c : pair * (c + 1), 0 : sz.mixed] = jnp.zeros((pair, sz.mixed), low)

    all_brought()
    value = xo[at.c].astype(jnp.float32)
    for c in range(4):
        value = value + wd[pair * c : pair * (c + 1), 0 : sz.mixed].astype(jnp.float32)
    flipped = natural_rows(value)
    vec_out[4:5, 0:half_rows] = own_half(flipped[half_rows : half_rows + 1])
    flipped = flipped[0:block]
    for i in range(4):
        held = (dk_sum, dv_sum)[i // 2].at[block * (i % 2) : block * (i % 2 + 1)]
        lanes = min(128, sz.share - 128 * i)
        held[:, 0:lanes] = flipped[:, 128 * i : 128 * i + lanes]
        stay.append(load(held, out_out.at[:, 128 * i : 128 * (i + 1)]))

    grad_across()

    for mask in range(1, 8):
        wires.arrived(va.at[mask], 84 + mask, at.peer(mask))
    vb[at.c] = functools.reduce(lambda a, b: a + b, [va[mask] for mask in range(8)])
    for c in range(4):
        wires.copy(vb.at[at.c], vb.at[at.c], at.along(c), 98 + at.c, at.c != c)

    for c in range(4):
        wires.arrived(vb.at[c], 98 + c, at.along(c), at.c != c)
    sums = vb[0] + vb[1] + vb[2] + vb[3]
    picked_sums = jnp.zeros((4, half_rows), jnp.float32)
    for i in range(8):
        cut = sums[0:4, block * i : block * i + half_rows]
        picked_sums = jnp.where(2 * at.c + at.d == i, cut, picked_sums)
    vec_out[0:4, 0:half_rows] = picked_sums
    res_finish()
    grad_finish()
    up_out.wait()
    rest_lanes = sz.heads - sz.solid
    for c in range(4):
        h_arrived(c)
        needed = h_from(c)
        rows = slice(block * c, block * (c + 1))
        parts = (
            load(zh.at[c, :, 0 : sz.solid], wd.at[rows], needed),
            load(zh.at[c, :, sz.solid : sz.heads], wu.at[rows, 0:rest_lanes], needed),
        )
        brought += [(needed, made) for made in parts]

        @pl.when(jnp.logical_not(needed))
        def _():
            wd[rows] = jnp.zeros((block, sz.solid), low)
            wu[rows, 0:rest_lanes] = jnp.zeros((block, rest_lanes), low)

    all_brought()
    left = xh[at.c, :, 0 : sz.solid].astype(jnp.float32)
    right = xh[at.c, :, sz.solid : sz.heads].astype(jnp.float32)
    for c in range(4):
        rows = slice(block * c, block * (c + 1))
        left = left + wd[rows].astype(jnp.float32)
        right = right + wu[rows, 0:rest_lanes].astype(jnp.float32)
    whole = jnp.concatenate([left, right], axis=1)
    for i in range(3):
        turned_columns = jnp.concatenate(
            [
                whole[:, main * i : main * (i + 1)],
                whole[:, 3 * main + slack * i : 3 * main + slack * (i + 1)],
            ],
            axis=1,
        )
        rows = slice(block * i, block * (i + 1))
        for r in range(4):

            @pl.when(at.r == r)
            def _():
                cut = slack * r
                value = turned_columns
                if cut:
                    value = jnp.concatenate([value[:, cut:], value[:, 0:cut]], axis=1)
                u[rows, 0 : sz.share] = value
                if i != 1:
                    vec_out[6 + i // 2 : 7 + i // 2, 0:half_rows] = own_half(
                        value[half_rows : half_rows + 1]
                    )

    stay.append(load(u.at[0 : 3 * block, 0:512], out_heads))
    for made in stay:
        made.wait()
    wires.close()


def update_kernel(sz, rates, grads, result_in, grad_in, weights, firsts, seconds, outs):
    down, out, up, heads, vectors = grads
    share, pieces, block = sz.share, sz.pieces, sz.block

    def move(i, place, gradient, decay):
        weight = weights[i][place]
        first_new = BETA_FIRST * firsts[i][place] + (1.0 - BETA_FIRST) * gradient
        second_new = BETA_SECOND * seconds[i][place] + (1.0 - BETA_SECOND) * (gradient * gradient)
        divisor = jnp.sqrt(second_new * (1.0 / (1.0 - BETA_SECOND**STEP))) + ADAM_EPSILON
        change = first_new * (rates[i] / (1.0 - BETA_FIRST**STEP)) / divisor
        weight_new = weight * (1.0 - rates[i] * decay) - change
        outs[3 * i + 2][place] = first_new
        outs[3 * i + 3][place] = second_new
        outs[3 * i + 4][place] = weight_new

    for part in range(3):
        move(0, part, heads[part, :, 0:share], MATRIX_DECAY)
    move(1, slice(None), out[:, 0:share], MATRIX_DECAY)
    move(2, slice(None), jnp.stack([up[j, :, 0:share] for j in range(4)], axis=1), MATRIX_DECAY)
    move(3, slice(None), down[:, 0:share], MATRIX_DECAY)

    @pl.when(pl.program_id(0) == 0)
    def _():
        for i, source, row in (
            (4, 0, 0), (4, 1, 1), (5, 4, 0), (5, 2, 1), (5, 3, 2), (5, 5, 3),
            (6, 6, 0), (6, 7, 1), (7, 8, 0), (7, 9, 1), (7, 10, 2), (7, 11, 3),
        ):
            move(i, row, vectors[source : source + 1, 0:pieces], 0.0)

    def plain(rows):
        rows = rows.astype(jnp.float32)
        return jnp.concatenate([rows[0:pieces], rows[block : block + pieces]], axis=0)

    @pl.when(pl.program_id(0) == 1)
    def _():
        outs[0][...] = plain(result_in[...]).astype(jnp.bfloat16)

    @pl.when(pl.program_id(0) == 2)
    def _():
        outs[1][...] = plain(grad_in[...])


def fused(
    tokens,
    cotangent,
    segments,
    weights,
    firsts,
    seconds,
):
    low = jnp.bfloat16
    seq, share = tokens.shape
    pieces = weights[1].shape[2]
    sz = Sizes(share, pieces, seq)
    block, main = sz.block, sz.main

    def views(arrays):
        heads, out, up, down, *small = arrays
        return (
            jnp.transpose(heads.reshape(pieces, 3, share), (1, 0, 2)),
            out.reshape(pieces, share),
            up.reshape(pieces, 4, share),
            down.reshape(4 * pieces, share),
            *[each.reshape(each.shape[0], 1, pieces) for each in small],
        )

    viewed = views(weights)
    labels = segments.reshape(1, -1)

    def made(*shape, dtype=low):
        return jax.ShapeDtypeStruct(shape, dtype)

    def held(*shape, dtype=low):
        return pltpu.VMEM(shape, dtype)

    w, seq, both, part = sz.width, sz.seq, sz.both, sz.part
    vmem, anywhere = pl.BlockSpec(memory_space=pltpu.VMEM), pl.BlockSpec(memory_space=pl.ANY)
    dma = pltpu.SemaphoreType.DMA
    f32 = jnp.float32
    wide = 3 * 128 + 128
    outs = pl.pallas_call(
        functools.partial(forward_kernel, sz),
        out_shape=(
            made(w, sz.heads),
            made(w, 2 * sz.mixed),
            made(w, sz.hidden),
            made(w, sz.solid),
            made(w, seq),
            made(w, both),
            made(w, sz.solid),
            made(w, 128),
            made(both, w),
            made(both, sz.hidden, dtype=f32),
            made(both, sz.hidden),
            made(seq, main + 128),
            made(seq, main + 128),
            made(seq, main + 128),
            made(seq, 2 * sz.mixed),
            made(seq, 128, dtype=f32),
            made(part, w, dtype=f32),
            made(part, w),
            made(8, w, dtype=f32),
        ),
        in_specs=[anywhere] * 6 + [vmem] * 5,
        out_specs=[anywhere] * 19,
        scratch_shapes=[
            held(w, sz.heads),
            held(w, 2 * sz.mixed),
            held(w, sz.hidden),
            held(w, sz.solid),
            held(w, seq),
            held(w, both),
            held(w, sz.solid),
            held(w, 128),
            held(w, both),
            held(both, w),
            held(both, sz.hidden, dtype=f32),
            held(both, sz.hidden),
            held(seq, main + 128),
            held(seq, main + 128),
            held(seq, main + 128),
            held(seq, 2 * sz.mixed),
            held(seq, 128, dtype=f32),
            held(part, w, dtype=f32),
            held(part, w),
            held(8, w, dtype=f32),
            held(w, seq),
            held(seq, w),
            held(both, w),
            held(seq, sz.heads),
            held(seq, main + 128),
            held(w, 128),
            held(seq, w),
            held(seq, 256),
            held(seq, 256),
            held(seq, 128),
            held(2, part, w),
            held(1, part, w),
            held(1, part, w),
            held(share, seq),
            held(share, seq),
            held(3, pieces, share, dtype=f32),
            held(pieces, share, dtype=f32),
            held(pieces, 4, share, dtype=f32),
            held(4 * pieces, share, dtype=f32),
            held(sz.pair, seq),
            held(sz.pair, seq),
            held(block, sz.hidden),
            held(sz.pair, 128),
            held(seq, 1, dtype=f32),
            held(block, seq),
            held(block, seq),
            dma((160,)),
            dma((160,)),
            dma((48,)),
        ],
        compiler_params=pltpu.CompilerParams(
            collective_id=0, has_side_effects=True, vmem_limit_bytes=VMEM_BYTES
        ),
        cost_estimate=pl.CostEstimate(flops=10**10, bytes_accessed=10**8, transcendentals=10**6),
    )(tokens.T, cotangent.T, *viewed, labels)
    (wh, wo, wu, wd, h1_t, h2_t, gd, gt, dy, u, gl, qw, kw, vw, a_nat, lse, x2, x_own, vec_rows) = outs
    outs = pl.pallas_call(
        functools.partial(backward_kernel, sz),
        out_shape=(
            made(4 * pieces, 512, dtype=f32),
            made(4 * block, 512, dtype=f32),
            made(block, 512, dtype=f32),
            made(3 * block, 512, dtype=f32),
            made(sz.pair, seq),
            made(sz.pair, seq),
            made(16, 256, dtype=f32),
            made(4, sz.pair, sz.solid),
            made(4, sz.pair, sz.hidden),
            made(4, sz.pair, sz.mixed),
            made(4, block, sz.heads),
            made(4, block, seq),
            made(2, block, seq),
            made(4, block, seq),
            made(2, block, seq),
        ),
        in_specs=[anywhere] * 18 + [vmem] * 2,
        out_specs=[anywhere] * 6 + [vmem] + [anywhere] * 8,
        scratch_shapes=[
            held(sz.pair, sz.solid),
            held(sz.pair, sz.hidden),
            held(sz.pair, sz.mixed),
            held(block, sz.heads),
            held(seq, main + 128),
            held(seq, main + 128),
            held(seq, main + 128),
            held(seq, 2 * sz.mixed),
            held(seq, 128, dtype=f32),
            held(part, w, dtype=f32),
            held(part, w),
            held(block, sz.hidden),
            held(both, w),
            held(w, both),
            held(both, sz.hidden, dtype=f32),
            held(both, sz.hidden),
            held(w, both),
            held(w, sz.solid),
            held(w, sz.hidden),
            held(w, 2 * sz.mixed),
            held(w, sz.heads),
            held(w, 128),
            held(part, w),
            held(both, sz.hidden),
            held(w, sz.heads),
            held(w, sz.hidden),
            held(w, 2 * sz.mixed),
            held(4, block, sz.heads),
            held(4, sz.pair, sz.mixed),
            held(4, part, w),
            held(3, part, w),
            held(4, part, w),
            held(3, part, w),
            held(2, part, w),
            held(1, part, w),
            held(3, part, w),
            held(seq, w),
            held(seq, 2 * sz.mixed),
            held(seq, 128, dtype=f32),
            held(seq, 128, dtype=f32),
            held(part, w, dtype=f32),
            held(seq, 256),
            held(seq, 256),
            held(seq, 128),
            held(seq, 128),
            held(seq, 1, dtype=f32),
            held(4, 2, block, part),
            held(4, 2, block, part),
            held(8, 8, w, dtype=f32),
            held(4, 8, w, dtype=f32),
            dma((128,)),
            dma((120,)),
            dma((80,)),
        ],
        compiler_params=pltpu.CompilerParams(
            collective_id=1, has_side_effects=True, vmem_limit_bytes=VMEM_BYTES
        ),
        cost_estimate=pl.CostEstimate(flops=2 * 10**10, bytes_accessed=10**8, transcendentals=10**6),
    )(
        dy, gd, gt, u, gl, h2_t, wd, wu, wo, wh, h1_t,
        qw, kw, vw, a_nat, lse, x2, x_own, vec_rows, labels,
    )
    down, up, out, heads, result_home, grad_home, vectors = outs[:7]
    steps = 5
    chunk = pieces // steps

    def rows_of(shape, axis, size):
        block_shape = list(shape)
        block_shape[axis] = size
        return pl.BlockSpec(tuple(block_shape), lambda i: tuple(i if a == axis else 0 for a in range(len(shape))))

    def whole(shape):
        return pl.BlockSpec(tuple(shape), lambda i: (0,) * len(shape))

    matrix_specs = (
        rows_of((3, pieces, share), 1, chunk),
        rows_of((pieces, share), 0, chunk),
        rows_of((pieces, 4, share), 0, chunk),
        rows_of((4 * pieces, share), 0, 4 * chunk),
        *[whole(each.shape) for each in viewed[4:]],
    )
    grads = (down, out, up.reshape(4, block, 512), heads.reshape(3, block, 512), vectors)
    grad_specs = (
        rows_of((4 * pieces, 512), 0, 4 * chunk),
        rows_of((block, 512), 0, chunk),
        rows_of((4, block, 512), 1, chunk),
        rows_of((3, block, 512), 1, chunk),
        whole((16, 256)),
    )
    rates = (0.05, 0.2, 0.05, 0.025, 0.3, 0.3, 0.3, 0.3)
    arguments = (*grads, result_home, grad_home, *viewed, *views(firsts), *views(seconds))
    out_shape = [made(share, seq), made(share, seq, dtype=f32)]
    out_specs = [whole((share, seq)), whole((share, seq))]
    for each, spec in zip(viewed, matrix_specs, strict=True):
        out_shape += [jax.ShapeDtypeStruct(each.shape, f32)] * 3
        out_specs += [spec] * 3

    def update(*refs):
        ins, outs = refs[:31], refs[31:]
        update_kernel(sz, rates, ins[:5], ins[5], ins[6], ins[7:15], ins[15:23], ins[23:31], outs)

    updated = pl.pallas_call(
        update,
        grid=(steps,),
        out_shape=out_shape,
        in_specs=[*grad_specs, whole((sz.pair, seq)), whole((sz.pair, seq)), *matrix_specs * 3],
        out_specs=out_specs,
        compiler_params=pltpu.CompilerParams(vmem_limit_bytes=VMEM_BYTES),
        cost_estimate=pl.CostEstimate(
            flops=20 * 10**6, bytes_accessed=30 * 10**6, transcendentals=2 * 10**6
        ),
    )(*arguments)
    results = [updated[0].T, updated[1].T]
    for i, weight in enumerate(weights):
        for each in updated[2 + 3 * i : 5 + 3 * i]:
            if i == 0:
                each = jnp.transpose(each, (1, 0, 2))
            results.append(each.reshape(weight.shape))
    return tuple(results)


def normalize(inputs):
    center = jnp.mean(inputs, axis=1, keepdims=True)
    spread = jnp.mean(inputs * inputs, axis=1, keepdims=True) - center * center
    inverse = lax.rsqrt(spread + NORM_EPSILON)
    return ((inputs - center) * inverse, inverse)


def norm_pull(upstream, centered, inverse, gain):
    scaled = upstream * gain
    inner = (
        scaled
        - jnp.mean(scaled, axis=1, keepdims=True)
        - centered * jnp.mean(scaled * centered, axis=1, keepdims=True)
    )
    return inner * inverse


def crossed(blocks, n):
    pairs = [(i * n + j, j * n + i) for i in range(n) for j in range(n)]
    return lax.ppermute(blocks, ("row", "col"), pairs)


def scatter_rows(partial):
    return lax.psum_scatter(
        partial.astype(jnp.bfloat16), "row", scatter_dimension=0, tiled=True
    ).astype(jnp.float32)


def gather_rows(local):
    return lax.all_gather(local, "row", axis=0, tiled=True)


def split_heads(rows):
    return jnp.transpose(rows.reshape(rows.shape[0], -1, HD), (1, 0, 2))


def join_heads(values):
    return jnp.transpose(values, (1, 0, 2)).reshape(values.shape[1], -1)


def scores_of(queries, keys, allowed):
    scores = jnp.einsum(
        "hqe,hke->hqk", queries, keys, preferred_element_type=jnp.float32
    ) * HD ** (-0.5)
    return jnp.where(allowed[None], scores, MASKED)


def gathered(
    tokens,
    cotangent,
    segments,
    w_heads,
    w_out,
    w_up,
    w_down,
    norm_vectors,
    width_vectors,
    attend_bias,
    hidden_vectors,
):
    n_dp, n_row, n_col = (lax.axis_size(name) for name in ("dp", "row", "col"))
    row = lax.axis_index("row")
    low = jnp.bfloat16
    share = tokens.shape[1]
    width = share * n_col
    seq = tokens.shape[0]
    part = seq // n_row
    near = HEADS // n_row
    window = (HEADS - near * (n_row - 1)) * HD
    step = near * HD
    edge = width - (share + step * (n_row - 1)) if n_row > 1 else 0
    edge = window - share
    to_next = [(i, i + 1) for i in range(n_row - 1)]
    to_last = [(i + 1, i) for i in range(n_row - 1)]
    offset = edge - (share - step) * row

    vectors = jnp.concatenate(
        [
            norm_vectors.reshape(2, -1),
            width_vectors.reshape(4, -1),
            attend_bias.reshape(2, -1),
            hidden_vectors.reshape(4, -1),
        ]
    ).astype(low)
    vectors = lax.all_gather(vectors, ("row", "col", "dp"), axis=0, tiled=False)
    vectors = vectors.reshape(n_row, n_col, n_dp, 12, -1).astype(jnp.float32)
    by_col = jnp.transpose(vectors[0], (2, 0, 1, 3)).reshape(12, width)
    by_row = jnp.transpose(vectors[:, 0], (2, 0, 1, 3)).reshape(12, width)
    gain_one, shift_one, bias_out, gain_two, shift_two, bias_down = (by_col[i] for i in range(6))
    zeros = jnp.zeros((1, window), jnp.float32)
    attend_rows = lax.dynamic_slice_in_dim(by_row[6:8], row * step, window, axis=1)
    heads_bias = jnp.concatenate([attend_rows[0:1], zeros, attend_rows[1:2]]).reshape(-1)
    unit_bias = lax.dynamic_slice_in_dim(by_row[8:12], row * share, share, axis=1).reshape(-1)

    own = w_heads.astype(low).reshape(-1, 3, share)
    passed = lax.ppermute(own[:, :, share - edge :], "row", to_next)
    own = jnp.concatenate([passed, own, jnp.zeros_like(passed)], axis=2)
    own = lax.dynamic_slice_in_dim(own, offset, window, axis=2).reshape(-1, 3 * window)
    heads_matrix = lax.all_gather(own, ("col", "dp"), axis=0, tiled=True)
    out_matrix = lax.all_gather(w_out.astype(low).reshape(-1, share), ("col", "dp"), axis=0)
    out_matrix = jnp.transpose(out_matrix.reshape(n_col, share, share), (1, 0, 2))
    out_matrix = out_matrix.reshape(share, width)
    passed = lax.ppermute(out_matrix[share - edge :], "row", to_next)
    out_matrix = jnp.concatenate([passed, out_matrix, jnp.zeros_like(passed)])
    out_matrix = lax.dynamic_slice_in_dim(out_matrix, offset, window)
    owned = (jnp.arange(window) < step) | (row == n_row - 1)
    out_matrix = jnp.where(owned[:, None], out_matrix, jnp.zeros_like(out_matrix))
    up_matrix = lax.all_gather(
        w_up.astype(low).reshape(-1, 4 * share), ("col", "dp"), axis=0, tiled=True
    )
    down_matrix = lax.all_gather(w_down.astype(low).reshape(4, -1, share), ("col", "dp"), axis=0)
    down_matrix = down_matrix.reshape(n_col, n_dp, 4, -1, share)
    down_matrix = jnp.transpose(down_matrix, (2, 1, 3, 0, 4)).reshape(4 * share, width)

    inputs_low = lax.all_gather(crossed(tokens, n_row), "row", axis=1, tiled=True)
    upstream = lax.all_gather(crossed(cotangent, n_row), "row", axis=1, tiled=True)
    inputs = inputs_low.astype(jnp.float32)
    centered_one, inverse_one = normalize(inputs)
    normed_one = (centered_one * gain_one + shift_one).astype(low)
    projected = (times(normed_one, heads_matrix) + heads_bias).astype(low)
    queries, keys, values = (
        split_heads(projected[:, i * window : (i + 1) * window]) for i in range(3)
    )
    labels = lax.dynamic_slice_in_dim(segments, lax.axis_index("col") * seq, seq)
    places = jnp.arange(seq, dtype=jnp.int32)
    allowed = (labels[:, None] == labels[None, :]) & (places[:, None] >= places[None, :])
    scores = scores_of(queries, keys, allowed)
    highest = jnp.max(scores, axis=-1, keepdims=True)
    log_total = highest + jnp.log(jnp.sum(jnp.exp(scores - highest), axis=-1, keepdims=True))
    soft = jnp.exp(scores - log_total).astype(low)
    mixed = jnp.einsum("hqk,hke->hqe", soft, values, preferred_element_type=jnp.float32)
    mixed = join_heads(mixed.astype(low))
    branch = scatter_rows(times(mixed, out_matrix))
    mine = row * part
    middle = lax.dynamic_slice_in_dim(inputs, mine, part) + (branch + bias_out)
    centered_two, inverse_two = normalize(middle)
    normed_two = gather_rows((centered_two * gain_two + shift_two).astype(low))
    hidden = times(normed_two, up_matrix) + unit_bias
    activated, smooth_pull = jax.vjp(smooth, hidden)
    activated = activated.astype(low)
    result = (middle + (scatter_rows(times(activated, down_matrix)) + bias_down)).astype(low)

    down_back = times_flipped(upstream, down_matrix)
    grad_down = times_outer(activated, upstream)
    hidden_back = smooth_pull(down_back)[0].astype(low)
    grad_up = times_outer(normed_two, hidden_back)
    unit_sum = jnp.sum(hidden_back, axis=0, dtype=jnp.float32)
    normed_two_back = scatter_rows(times_flipped(hidden_back, up_matrix))
    upstream_own = lax.dynamic_slice_in_dim(upstream, mine, part).astype(jnp.float32)
    middle_back = upstream_own + norm_pull(normed_two_back, centered_two, inverse_two, gain_two)
    branch_own = middle_back.astype(low)
    branch_back = gather_rows(branch_own)
    mixed_back = times_flipped(branch_back, out_matrix).astype(low)
    grad_out = times_outer(mixed, branch_back)
    mixed_back = split_heads(mixed_back)
    scores_again = scores_of(queries, keys, allowed)
    soft = jnp.exp(scores_again - log_total)
    soft_back = jnp.einsum("hqe,hke->hqk", mixed_back, values, preferred_element_type=jnp.float32)
    row_inner = jnp.sum(soft_back * soft, axis=-1, keepdims=True)
    score_back = (soft * (soft_back - row_inner)).astype(low)
    query_back = jnp.einsum(
        "hqk,hke->hqe", score_back, keys, preferred_element_type=jnp.float32
    ) * HD ** (-0.5)
    key_back = jnp.einsum(
        "hqk,hqe->hke", score_back, queries, preferred_element_type=jnp.float32
    ) * HD ** (-0.5)
    value_back = jnp.einsum(
        "hqk,hqe->hke", soft.astype(low), mixed_back, preferred_element_type=jnp.float32
    )
    heads_back = jnp.concatenate(
        [join_heads(each.astype(low)) for each in (query_back, key_back, value_back)], axis=1
    )
    heads_sum = jnp.sum(heads_back, axis=0, dtype=jnp.float32)
    normed_one_back = scatter_rows(times_flipped(heads_back, heads_matrix))
    grad_heads = times_outer(normed_one, heads_back)
    centered_own = lax.dynamic_slice_in_dim(centered_one, mine, part)
    inverse_own = lax.dynamic_slice_in_dim(inverse_one, mine, part)
    input_back = middle_back + norm_pull(normed_one_back, centered_own, inverse_own, gain_one)

    def homeward(own):
        own = lax.all_to_all(own, "row", split_axis=1, concat_axis=0, tiled=True)
        return crossed(own, n_row)

    result_tokens = homeward(result)
    input_gradient = homeward(input_back.astype(low)).astype(jnp.float32)

    by_token = jnp.stack(
        [
            jnp.sum(normed_one_back * centered_own, axis=0),
            jnp.sum(normed_one_back, axis=0),
            jnp.sum(branch_own.astype(jnp.float32), axis=0),
            jnp.sum(normed_two_back * centered_two, axis=0),
            jnp.sum(normed_two_back, axis=0),
            jnp.sum(upstream_own, axis=0),
        ]
    )
    owned_rows = jnp.where(owned, heads_sum.reshape(3, window)[0::2], 0.0)
    by_unit = jnp.concatenate(
        [
            lax.dynamic_update_slice_in_dim(
                jnp.zeros((2, width), jnp.float32), owned_rows, row * step, axis=1
            ),
            lax.dynamic_update_slice_in_dim(
                jnp.zeros((4, width), jnp.float32), unit_sum.reshape(4, share), row * share, axis=1
            ),
        ]
    )
    sums = lax.psum(jnp.concatenate([by_token, by_unit]), ("dp", "row", "col"))
    pieces = share // n_dp
    inner = lax.axis_index("dp") * pieces
    col_sums = lax.dynamic_slice_in_dim(sums, lax.axis_index("col") * share + inner, pieces, axis=1)
    row_sums = lax.dynamic_slice_in_dim(sums, row * share + inner, pieces, axis=1)

    both = ("col", "dp")

    def to_owner(gradient):
        return lax.psum_scatter(gradient, both, scatter_dimension=0, tiled=True)

    got_heads = to_owner(grad_heads.astype(low)).reshape(pieces, 3, window)
    got_heads = jnp.where(owned, got_heads, jnp.zeros_like(got_heads))
    passed = lax.ppermute(got_heads[:, :, :edge], "row", to_last)
    got_heads = jnp.concatenate([got_heads, jnp.zeros_like(passed)], axis=2)
    got_heads = lax.dynamic_slice_in_dim(got_heads, edge - offset, share, axis=2)
    passed = jnp.concatenate([jnp.zeros((pieces, 3, share), low), passed, jnp.zeros_like(passed)], axis=2)
    got_heads = got_heads + lax.dynamic_slice_in_dim(passed, share - step + edge - offset, share, axis=2)
    low_out = jnp.where(owned[:, None], grad_out, 0.0).astype(low)
    passed = lax.ppermute(low_out[:edge], "row", to_last)
    low_out = jnp.concatenate([low_out, jnp.zeros_like(passed)])
    low_out = lax.dynamic_slice_in_dim(low_out, edge - offset, share)
    passed = jnp.concatenate([jnp.zeros((share, width), low), passed, jnp.zeros_like(passed)])
    low_out = low_out + lax.dynamic_slice_in_dim(passed, share - step + edge - offset, share)
    low_out = jnp.transpose(low_out.reshape(n_dp, pieces, n_col, share), (2, 0, 1, 3))
    got_out = to_owner(low_out.reshape(-1, share))
    got_up = to_owner(grad_up.astype(low))
    low_down = grad_down.astype(low).reshape(4, n_dp, pieces, n_col, share)
    low_down = jnp.transpose(low_down, (3, 1, 0, 2, 4)).reshape(-1, share)
    got_down = to_owner(low_down)

    reduced = [
        each.astype(jnp.float32).reshape(like.shape)
        for each, like in (
            (got_heads, w_heads),
            (got_out, w_out),
            (got_up, w_up),
            (got_down, w_down),
            (col_sums[0:2], norm_vectors),
            (col_sums[2:6], width_vectors),
            (row_sums[6:8], attend_bias),
            (row_sums[8:12], hidden_vectors),
        )
    ]
    return result_tokens, input_gradient, reduced


def per_device(
    tokens,
    cotangent,
    segments,
    w_heads,
    w_out,
    w_up,
    w_down,
    norm_vectors,
    width_vectors,
    attend_bias,
    hidden_vectors,
    drift_heads,
    drift_out,
    drift_up,
    drift_down,
    drift_norm,
    drift_width,
    drift_attend,
    drift_hidden,
    power_heads,
    power_out,
    power_up,
    power_down,
    power_norm,
    power_width,
    power_attend,
    power_hidden,
):
    weights = (
        w_heads,
        w_out,
        w_up,
        w_down,
        norm_vectors,
        width_vectors,
        attend_bias,
        hidden_vectors,
    )
    firsts = (
        drift_heads,
        drift_out,
        drift_up,
        drift_down,
        drift_norm,
        drift_width,
        drift_attend,
        drift_hidden,
    )
    seconds = (
        power_heads,
        power_out,
        power_up,
        power_down,
        power_norm,
        power_width,
        power_attend,
        power_hidden,
    )
    sizes = tuple(lax.axis_size(name) for name in ("dp", "row", "col"))
    if sizes == (2, 4, 4):
        return fused(tokens, cotangent, segments, weights, firsts, seconds)
    result_tokens, input_gradient, reduced = gathered(tokens, cotangent, segments, *weights)
    heads_up = adam(w_heads, reduced[0], drift_heads, power_heads, 0.05, MATRIX_DECAY)
    out_up = adam(w_out, reduced[1], drift_out, power_out, 0.2, MATRIX_DECAY)
    up_up = adam(w_up, reduced[2], drift_up, power_up, 0.05, MATRIX_DECAY)
    down_up = adam(w_down, reduced[3], drift_down, power_down, 0.025, MATRIX_DECAY)
    norm_up = adam(norm_vectors, reduced[4], drift_norm, power_norm, 0.3, 0.0)
    width_up = adam(width_vectors, reduced[5], drift_width, power_width, 0.3, 0.0)
    attend_up = adam(attend_bias, reduced[6], drift_attend, power_attend, 0.3, 0.0)
    hidden_up = adam(hidden_vectors, reduced[7], drift_hidden, power_hidden, 0.3, 0.0)
    return (
        result_tokens,
        input_gradient,
        heads_up[0],
        heads_up[1],
        heads_up[2],
        out_up[0],
        out_up[1],
        out_up[2],
        up_up[0],
        up_up[1],
        up_up[2],
        down_up[0],
        down_up[1],
        down_up[2],
        norm_up[0],
        norm_up[1],
        norm_up[2],
        width_up[0],
        width_up[1],
        width_up[2],
        attend_up[0],
        attend_up[1],
        attend_up[2],
        hidden_up[0],
        hidden_up[1],
        hidden_up[2],
    )


def solution(mesh):
    return jax.shard_map(
        per_device,
        mesh=mesh,
        in_specs=(
            P(("dp", "row"), "col"),
            P(("dp", "row"), "col"),
            P("dp"),
            P("col", "dp", None, None, "row"),
            P("row", "dp", None, "col"),
            P("col", "dp", None, None, "row"),
            P(None, "row", "dp", None, "col"),
            P(None, "col", "dp", None),
            P(None, "col", "dp", None),
            P(None, "row", "dp", None),
            P(None, "row", "dp", None),
            P("col", "dp", None, None, "row"),
            P("row", "dp", None, "col"),
            P("col", "dp", None, None, "row"),
            P(None, "row", "dp", None, "col"),
            P(None, "col", "dp", None),
            P(None, "col", "dp", None),
            P(None, "row", "dp", None),
            P(None, "row", "dp", None),
            P("col", "dp", None, None, "row"),
            P("row", "dp", None, "col"),
            P("col", "dp", None, None, "row"),
            P(None, "row", "dp", None, "col"),
            P(None, "col", "dp", None),
            P(None, "col", "dp", None),
            P(None, "row", "dp", None),
            P(None, "row", "dp", None),
        ),
        out_specs=(
            P(("dp", "row"), "col"),
            P(("dp", "row"), "col"),
            P("col", "dp", None, None, "row"),
            P("col", "dp", None, None, "row"),
            P("col", "dp", None, None, "row"),
            P("row", "dp", None, "col"),
            P("row", "dp", None, "col"),
            P("row", "dp", None, "col"),
            P("col", "dp", None, None, "row"),
            P("col", "dp", None, None, "row"),
            P("col", "dp", None, None, "row"),
            P(None, "row", "dp", None, "col"),
            P(None, "row", "dp", None, "col"),
            P(None, "row", "dp", None, "col"),
            P(None, "col", "dp", None),
            P(None, "col", "dp", None),
            P(None, "col", "dp", None),
            P(None, "col", "dp", None),
            P(None, "col", "dp", None),
            P(None, "col", "dp", None),
            P(None, "row", "dp", None),
            P(None, "row", "dp", None),
            P(None, "row", "dp", None),
            P(None, "row", "dp", None),
            P(None, "row", "dp", None),
            P(None, "row", "dp", None),
        ),
        check_vma=False,
    )
```

```python
import functools

import jax
import jax.numpy as jnp
from jax import lax
from jax.experimental import pallas as pl
from jax.experimental.pallas import tpu as pltpu
from jax.sharding import PartitionSpec as P

HEADS = 25
HD = 64
TOK_DEV = 128
STEP = 10


NORM_EPSILON = 1e-05
BETA_FIRST = 0.9
BETA_SECOND = 0.999
ADAM_EPSILON = 1e-08
MATRIX_DECAY = 0.1
MASKED = -1e30
ROOT = (2.0 / 3.141592653589793) ** 0.5
CUBIC = 0.044715
VMEM_BYTES = 66 * 1024 * 1024


def adam(weight, gradient, first, second, rate, decay):
    first_new = BETA_FIRST * first + (1.0 - BETA_FIRST) * gradient
    second_new = BETA_SECOND * second + (1.0 - BETA_SECOND) * gradient * gradient
    corrected = first_new / (1.0 - BETA_FIRST**STEP)
    divisor = jnp.sqrt(second_new / (1.0 - BETA_SECOND**STEP)) + ADAM_EPSILON
    return (first_new, second_new, weight - rate * (corrected / divisor + decay * weight))


def smooth(values):
    return jax.nn.gelu(values, approximate=True)


def ceil_to(count, unit):
    return -(-count // unit) * unit


class Sizes:
    def __init__(self, share, pieces, seq):
        self.share = share
        self.pieces = pieces
        self.block = ceil_to(pieces, 16)
        self.pair = 2 * self.block
        self.width = 4 * self.pair
        self.seq = seq
        self.part = seq // 4
        self.both = 2 * seq
        self.main = (HEADS // 4) * HD
        self.slack = share - self.main
        self.heads = ceil_to(3 * share, 256)
        self.mixed = ceil_to(pieces + 1, 128)
        self.hidden = ceil_to(4 * pieces + 1, 128)
        self.tiles = self.width // 128
        self.solid = self.hidden - 128
        self.tail = 4 * pieces - self.solid
        assert 0 < self.tail < 64


class Place:
    def __init__(self):
        self.d, self.r, self.c = (lax.axis_index(name) for name in ("dp", "row", "col"))
        self.y, self.k = self.r // 2, self.r % 2

    def plane(self, mask):
        d = 1 - self.d if mask & 4 else self.d
        y = 1 - self.y if mask & 2 else self.y
        k = 1 - self.k if mask & 1 else self.k
        return d, 2 * y + k

    def peer(self, mask):
        d, r = self.plane(mask)
        return (d, r, self.c)

    def along(self, c):
        return (self.d, self.r, c)


def run(when, action):
    if when is None:
        action()
    else:
        pl.when(when)(action)


class Wires:
    def __init__(self, sends, arrivals):
        self.sends, self.arrivals = sends, arrivals
        self.used = 0
        self.open = []

    def make(self, source, target, index, slot, device):
        return pltpu.make_async_remote_copy(
            src_ref=source,
            dst_ref=target,
            send_sem=self.sends.at[index],
            recv_sem=self.arrivals.at[slot],
            device_id=device,
            device_id_type=pl.DeviceIdType.MESH,
        )

    def copy(self, source, target, device, slot, when=None):
        made = self.make(source, target, self.used, slot, device)
        self.used += 1
        run(when, made.start)
        item = (when, made)
        self.open.append(item)
        return item

    def arrived(self, target, slot, device, when=None):
        run(when, self.make(target, target, 0, slot, device).wait_recv)

    def close(self, some=None):
        for item in self.open if some is None else some:
            run(item[0], item[1].wait_send)
        self.open = [] if some is None else [o for o in self.open if all(o is not s for s in some)]


def greet(at, diagonal):
    barrier = pltpu.get_barrier_semaphore()

    def signal(device):
        pl.semaphore_signal(
            barrier, inc=1, device_id=device, device_id_type=pl.DeviceIdType.MESH
        )

    for mask in range(1, 8):
        signal(at.peer(mask))
    for c in range(4):
        run(at.c != c, functools.partial(signal, (at.d, at.r, c)))
        if diagonal:
            run(at.c != c, functools.partial(signal, (1 - at.d, at.r, c)))
    run(at.r != at.c, functools.partial(signal, (at.d, at.c, at.r)))
    pl.semaphore_wait(barrier, (13 if diagonal else 10) + jnp.where(at.r != at.c, 1, 0))


def rows_at(start, size):
    return pl.ds(pl.multiple_of(start, 16), size)


def lanes_at(start, size):
    return pl.ds(pl.multiple_of(start, 128), size)


def choose(shape, source):
    rows = lax.broadcasted_iota(jnp.int32, shape, 0)
    wanted = source(lax.broadcasted_iota(jnp.int32, shape, 1))
    return (rows == wanted).astype(jnp.bfloat16)


def edge_source(column):
    part, place = column // HD, column % HD
    wanted = jnp.where(place >= 16, 128 * part + place - 16, 384 + 16 * part + place)
    return jnp.where(part < 3, wanted, -1)


def spread_source(column):
    part, place = column // 128, column % 128
    return jnp.where(place < HD, HD * part + place, -1)


def picked(values, table):
    return jnp.dot(values, table, preferred_element_type=jnp.float32).astype(jnp.bfloat16)


def times(left, right):
    return jnp.dot(left, right, preferred_element_type=jnp.float32)


def times_flipped(left, right):
    return lax.dot_general(
        left, right, (((1,), (1,)), ((), ())), preferred_element_type=jnp.float32
    )


def times_outer(left, right):
    return lax.dot_general(
        left, right, (((0,), (0,)), ((), ())), preferred_element_type=jnp.float32
    )


def over_tiles(total, action, tile=256):
    @pl.loop(0, total // tile)
    def _(i):
        action(i * tile, tile)

    if total % tile:
        action(total - total % tile, total % tile)


def turned(values):
    return values.astype(jnp.float32).T


def gather_group(wires, masks, region, at, base):
    own = region(*at.plane(0))
    sent = [wires.copy(own, own, at.peer(mask), base + mask) for mask in (1, *masks)]

    def finish():
        for mask in masks:
            there = region(*at.plane(mask))
            wires.arrived(there, base + mask, at.peer(mask))
            sent.append(wires.copy(there, there, at.peer(1), base + mask + 1))
        for mask in (0, *masks):
            there = region(*at.plane(mask | 1))
            wires.arrived(there, base + (mask | 1), at.peer(1))

    return finish, sent


def cross_over(wires, home, landing, region, at, base):
    rows = home.shape[0] // 2
    wires.copy(home.at[rows_at(rows * (1 - at.y), rows)], landing, at.peer(2), base)
    target = region(at.c, at.d, at.y)

    def along(source, s):
        wires.copy(source, target, at.along(s), base + 1 + at.c, s != at.c)

        @pl.when(s == at.c)
        def _():
            target[...] = source[...]

    along(home.at[rows_at(rows * at.y, rows)], at.r)

    def onward():
        wires.arrived(landing, base, at.peer(2))
        along(landing, 2 * (1 - at.y) + at.k)

    def finish():
        for c in range(4):
            needed = (at.k == at.c % 2) & (at.c != c)
            wires.arrived(region(c, at.d, at.y), base + 1 + c, at.along(c), needed)

    return onward, finish


def share_pieces(wires, masks, region, at, base):
    holds = at.k == at.c % 2
    near = base + 4 * len(masks)

    def place(mask):
        d, r = at.plane(mask)
        return d, r // 2

    for c in range(4):
        own = region(c, *place(0))
        for i, mask in enumerate(masks):
            wires.copy(own, own, at.peer(mask), base + 4 * i + c, holds)
    for c in range(4):
        own = region(c, *place(0))
        wires.copy(own, own, at.peer(1), near + c, holds)

    def finish():
        for i, mask in enumerate(masks):
            for c in range(4):
                there = region(c, *place(mask))
                wires.arrived(there, base + 4 * i + c, at.peer(mask), holds)
                wires.copy(there, there, at.peer(1), near + 4 * (i + 1) + c, holds)
        for i, mask in enumerate((0, *masks)):
            for c in range(4):
                there = region(c, *place(mask))
                wires.arrived(there, near + 4 * i + c, at.peer(1), jnp.logical_not(holds))

    return finish


def scatter_group(wires, masks, partial, chunk, near, mid, far, at, base):
    sent = []
    for i, mask in enumerate((0, *masks)):
        rows = rows_at(chunk(*at.plane(mask | 1)), near.shape[1])
        sent.append(wires.copy(partial.at[rows], near.at[i], at.peer(1), base + i))

    def rows_of(mask):
        return rows_at(chunk(*at.plane(mask)), near.shape[1])

    def onward():
        for i, mask in enumerate((0, *masks)):
            wires.arrived(near.at[i], base + i, at.peer(1))
        for i, mask in enumerate(masks):
            both = partial[rows_of(mask)].astype(jnp.float32) + near[i + 1].astype(jnp.float32)
            mid[i] = both.astype(jnp.bfloat16)
            sent.append(wires.copy(mid.at[i], far.at[i], at.peer(mask), base + 4 + i))

    def total():
        for i, mask in enumerate(masks):
            wires.arrived(far.at[i], base + 4 + i, at.peer(mask))
        result = partial[rows_of(0)].astype(jnp.float32) + near[0].astype(jnp.float32)
        for i in range(len(masks)):
            result = result + far[i].astype(jnp.float32)
        return result

    return onward, total, sent


def spread_col(wires, region, at, base, wait=False):
    own = region(at.c)

    def send(distance):
        for delta in (distance, -distance):
            there = at.c + delta
            wires.copy(own, own, at.along(there), base + at.c, (there >= 0) & (there < 4))

    if not wait:
        send(2)
        send(1)

    def relay():
        for here, start, end in ((2, 0, 3), (1, 3, 0)):
            block = region(start)
            wires.arrived(block, base + start, at.along(start), at.c == here)
            wires.copy(block, block, at.along(end), base + start, at.c == here)

    def finish():
        for c in range(4):
            needed = at.c != c
            if c == 0:
                needed = needed & (at.c != 2)
            if c == 3:
                needed = needed & (at.c != 1)
            wires.arrived(region(c), base + c, at.along(c), needed)

    return (send, relay, finish) if wait else (relay, finish)


def collect_col(wires, piece, landing, rest, at, base, direct=None):
    low_end, high_end = at.c == 0, at.c == 3
    ends = low_end | high_end
    via = jnp.where(low_end, 1, 2)

    def pick(*choices):
        return jnp.where(
            low_end,
            choices[0],
            jnp.where(at.c == 1, choices[1], jnp.where(high_end, choices[3], choices[2])),
        )

    order = (pick(3, 0, 3, 0), pick(2, 2, 1, 1), pick(1, 3, 0, 2), at.c)
    target = landing.at[at.c]

    def send(step):
        there = order[step]
        block = (direct or piece)(there)
        if step == 0:
            wires.copy(block, rest, at.along(via), base + 4, ends)
            wires.copy(block, target, at.along(there), base + at.c, jnp.logical_not(ends))
        elif step == 1:
            wires.copy(block, target, at.along(there), base + at.c)
        elif step == 2:
            wires.copy(block, target, at.along(there), base + at.c, ends)

    def relay(add):
        @pl.when(jnp.logical_not(ends))
        def _():
            wires.make(rest, rest, 0, base + 4, at.along(0)).wait_recv()
            add(order[2])

        wires.copy(piece(order[2]), target, at.along(order[2]), base + at.c, jnp.logical_not(ends))

    def arrived(c):
        wires.arrived(landing.at[c], base + c, at.along(c), sent_from(c))

    def sent_from(c):
        here = at.c != c
        if c in (0, 3):
            here = here & (at.c != 3 - c)
        return here

    return order, send, relay, arrived, sent_from


def forward_kernel(
    sz,
    x_home_in,
    dy_home_in,
    w_heads,
    w_out,
    w_up,
    w_down,
    norm_vectors,
    width_vectors,
    attend_bias,
    hidden_vectors,
    segments,
    wh_out,
    wo_out,
    wu_out,
    wd_out,
    h1_t_out,
    h2_t_out,
    gd_out,
    gt_out,
    dy_out,
    u_out,
    gl_out,
    qw_out,
    kw_out,
    vw_out,
    a_nat_out,
    lse_out,
    x2_out,
    x_own_out,
    vec_rows_out,
    wh,
    wo,
    wu,
    wd,
    h1_t,
    h2_t,
    gd,
    gt,
    dy_t,
    dy,
    u,
    gl,
    qw,
    kw,
    vw,
    a_nat,
    lse,
    x2,
    x_own,
    vec_rows,
    x_t,
    h1,
    h2,
    own_qkv,
    aw,
    vec,
    part,
    edge_out,
    edge_in,
    edge_back,
    near,
    mid,
    far,
    x_raw,
    dy_raw,
    heads_raw,
    out_raw,
    up_raw,
    down_raw,
    x_home,
    dy_home,
    wu_own,
    wd_tail,
    col_labels,
    x_half,
    dy_half,
    sends,
    arrivals,
    locals_,
):
    at = Place()
    wires = Wires(sends, arrivals)
    low = jnp.bfloat16
    pair, block, pieces = sz.pair, sz.block, sz.pieces
    fetched = []
    for i, (source, target) in enumerate(
        (
            (x_home_in, x_raw),
            (w_heads, heads_raw),
            (w_up, up_raw),
            (w_out, out_raw),
            (w_down, down_raw),
            (dy_home_in, dy_raw),
        )
    ):
        fetched.append(pltpu.make_async_copy(source, target, locals_.at[40 + i]))
    for made in fetched[0:2]:
        made.start()
    row_labels = segments.at[:, lanes_at(sz.seq * at.c, sz.seq)]

    def halves(value, target):
        value = value.astype(jnp.float32)
        gap = jnp.zeros((block - pieces, value.shape[1]), jnp.float32)
        parts = [value[0:pieces], gap, value[pieces : 2 * pieces], gap]
        target[...] = jnp.concatenate(parts, axis=0).astype(low)

    def quarter(row):
        return row.astype(low).astype(jnp.float32) * 0.25

    def placed(row):
        both = jnp.concatenate([row, row], axis=1)
        half_of = lax.broadcasted_iota(jnp.int32, both.shape, 1) // pieces
        return jnp.where(half_of == at.d, both, 0.0)

    def with_row(value, row):
        gap = jnp.zeros((block - pieces - 1, value.shape[1]), jnp.float32)
        return jnp.concatenate([value, row, gap], axis=0)

    flat = jnp.concatenate(
        [norm_vectors[0], norm_vectors[1], width_vectors[1], width_vectors[2]], axis=0
    )
    flat = jnp.concatenate([flat, jnp.zeros((124, pieces), jnp.float32)], axis=0)
    flat = jnp.concatenate([flat, jnp.zeros((128, 256 - pieces), jnp.float32)], axis=1)
    where_row = lax.broadcasted_iota(jnp.int32, flat.shape, 0)
    where_lane = lax.broadcasted_iota(jnp.int32, flat.shape, 1)
    carrier = (where_lane == pieces) & ((where_row == 1) | (where_row == 3))
    own_rows = rows_at(pair * at.c + block * at.d, block)
    vec[own_rows] = jnp.where(carrier, 1.0, flat).T[0:block].astype(low)
    fetched[0].wait()
    halves(x_raw[...], x_home)
    for made in fetched[2:6]:
        made.start()
    greet(at, False)

    def x_piece(c, d, y):
        return x_t.at[rows_at(pair * c + block * y, block)]

    def dy_piece(c, d, y):
        return dy_t.at[rows_at(pair * c + block * y, block), lanes_at(sz.seq * d, sz.seq)]

    used = [0]

    def flush(source, target):
        made = pltpu.make_async_copy(source, target, locals_.at[used[0]])
        used[0] += 1
        made.start()
        flushed.append(made)

    flushed = []

    def vec_block(d, c):
        return vec.at[rows_at(pair * c + block * d, block)]

    def wh_block(d):
        return lambda c: wh.at[rows_at(pair * c + block * d, block)]

    def wo_block(d):
        return lambda c: wo.at[rows_at(pair * c, pair), lanes_at(sz.mixed * d, sz.mixed)]

    def wu_block(d):
        return lambda c: wu.at[rows_at(pair * c + block * d, block)]

    def wd_block(half):
        return lambda c: wd.at[rows_at(pair * c + block * half, block)]

    x_onward, x_crossed = cross_over(wires, x_home, x_half, x_piece, at, 96)
    for c in range(4):
        wires.copy(vec_block(at.d, at.c), vec_block(at.d, at.c), at.along(c), 2 + at.c, at.c != c)
    wires.copy(vec_block(at.d, at.c), vec_block(at.d, at.c), at.peer(4), 6 + at.c)

    fetched[1].wait()
    for r in range(4):

        @pl.when(at.r == r)
        def _():
            cut = sz.share - sz.slack * r
            tails = []
            for i in range(3):
                value = heads_raw[i]
                row = jnp.zeros((1, sz.share), jnp.float32)
                if i != 1:
                    row = placed(quarter(attend_bias[i // 2]))
                value = with_row(value, row)
                if r:
                    value = jnp.concatenate([value[:, cut:], value[:, 0:cut]], axis=1)
                wh[own_rows, sz.main * i : sz.main * (i + 1)] = value[:, 0 : sz.main].astype(low)
                tails.append(value[:, sz.main :])
            tails.append(jnp.zeros((block, sz.heads - 3 * sz.share), jnp.float32))
            wh[own_rows, 3 * sz.main : sz.heads] = jnp.concatenate(tails, axis=1).astype(low)

    x_onward()
    wh_relay, wh_done = spread_col(wires, wh_block(at.d), at, 20)
    wires.copy(wh_block(at.d)(at.c), wh_block(at.d)(at.c), at.peer(4), 24 + at.c)

    fetched[2].wait()
    gap = jnp.zeros((block, sz.hidden - 4 * pieces), jnp.float32)
    values = [
        with_row(up_raw[:, j, :], placed(quarter(hidden_vectors[j]))) for j in range(4)
    ]
    for i in range(2):
        lanes = slice(pieces * i, pieces * (i + 1))
        whole = jnp.concatenate([value[:, lanes] for value in values] + [gap], axis=1)

        @pl.when(at.d == i)
        def _():
            wu[own_rows] = whole.astype(low)

        @pl.when(at.d != i)
        def _():
            wu_own[...] = whole.astype(low)

    wires.copy(wu_own, wu_block(at.d)(at.c), at.peer(4), 10)

    def turned_halves(value, target, rows, lanes):
        flipped = value.T
        gap = jnp.zeros((block - pieces, flipped.shape[1]), jnp.float32)
        parts = [flipped[0:pieces], gap, flipped[pieces : 2 * pieces], gap]
        target[rows, lanes] = jnp.concatenate(parts, axis=0).astype(low)

    fetched[3].wait()
    value = with_row(out_raw[...], placed(quarter(width_vectors[0])))
    value = jnp.concatenate([value, jnp.zeros((sz.mixed - block, sz.share), jnp.float32)], axis=0)
    for i in range(sz.mixed // 128):
        lanes = slice(128 * i, 128 * (i + 1))
        turned_halves(
            value[lanes], wo, rows_at(pair * at.c, pair), lanes_at(sz.mixed * at.d + 128 * i, 128)
        )
    wo_relay, wo_done = spread_col(wires, wo_block(at.d), at, 28)
    wires.copy(wo_block(at.d)(at.c), wo_block(at.d)(at.c), at.peer(4), 32 + at.c)

    fetched[5].wait()
    halves(dy_raw[...], dy_home)
    dy_onward, dy_crossed = cross_over(wires, dy_home, dy_half, dy_piece, at, 116)

    x_crossed()
    x_done = share_pieces(wires, (2,), x_piece, at, 104)

    fetched[4].wait()
    for i in range(sz.solid // 128):
        rows = slice(128 * i, 128 * (i + 1))
        turned_halves(down_raw[rows], wd, rows_at(pair * at.c, pair), rows)
    value = [
        jnp.zeros((64, sz.share), jnp.float32),
        down_raw[sz.solid : 4 * pieces],
        placed(quarter(width_vectors[3])),
        jnp.zeros((63 - sz.tail, sz.share), jnp.float32),
    ]
    turned_halves(jnp.concatenate(value, axis=0), wd_tail, slice(0, pair), slice(0, 128))

    def add_tail(d):
        rows = rows_at(pair * at.c + block * d, block)
        both = wu[rows, sz.solid : sz.hidden].astype(jnp.float32)
        both = both + wd_tail[rows_at(block * d, block)].astype(jnp.float32)
        wu[rows, sz.solid : sz.hidden] = both.astype(low)

    add_tail(at.d)
    col_labels[...] = jnp.concatenate([row_labels[...]] * 8, axis=0).astype(jnp.float32).T[:, 0:1]
    x_done()
    dy_onward()
    wires.arrived(wu_block(1 - at.d)(at.c), 10, at.peer(4))
    add_tail(1 - at.d)
    wu_first_send, wu_first, wu_first_done = spread_col(wires, wu_block(at.d), at, 36, True)
    wu_second_send, wu_second, wu_second_done = spread_col(wires, wu_block(1 - at.d), at, 40, True)
    for distance in (2, 1):
        wu_first_send(distance)
        wu_second_send(distance)

    for c in range(4):
        wires.arrived(vec_block(at.d, c), 2 + c, at.along(c), at.c != c)
    wires.arrived(vec_block(1 - at.d, at.c), 6 + at.c, at.peer(4))
    for step in range(1, 4):
        there = (at.c + step) % 4
        wires.copy(
            vec_block(at.d, there), vec_block(at.d, there), at.peer(4), 6 + there
        )
    for step in range(1, 4):
        there = (at.c + step) % 4
        wires.arrived(vec_block(1 - at.d, there), 6 + there, at.peer(4))
    features = 4.0 * sz.share

    def add_up(i, carry):
        rows = rows_at(128 * i, 128)
        value = x_t[rows].astype(jnp.float32)
        return (
            carry[0] + jnp.sum(value, axis=0, keepdims=True),
            carry[1] + jnp.sum(value * value, axis=0, keepdims=True),
        )

    zero = jnp.zeros((1, sz.seq), jnp.float32)
    sums = lax.fori_loop(0, sz.tiles, add_up, (zero, zero))
    center = sums[0] / features
    inverse = lax.rsqrt(sums[1] / features - center * center + NORM_EPSILON)

    @pl.loop(0, sz.tiles)
    def _(i):
        rows, lanes = rows_at(128 * i, 128), lanes_at(128 * i, 128)
        vectors = vec[rows].astype(jnp.float32)
        value = (x_t[rows].astype(jnp.float32) - center) * inverse
        value = value * vectors[:, 0:1] + vectors[:, 1:2]
        h1_t[rows] = value.astype(low)
        h1[:, lanes] = value.T.astype(low)
        mine = x_t[rows, lanes_at(sz.part * at.r, sz.part)]
        x_own[:, lanes] = turned(mine).astype(low)
        vec_rows[:, lanes] = vectors.T[0:8]

    flush(h1_t, h1_t_out)
    flush(x_own, x_own_out)
    flush(vec_rows, vec_rows_out)

    wh_relay()
    for c in range(4):
        needed = at.c != c
        if c == 0:
            needed = needed & (at.c != 2)
        if c == 3:
            needed = needed & (at.c != 1)
        wires.arrived(wh_block(at.d)(c), 20 + c, at.along(c), needed)
        wires.copy(wh_block(at.d)(c), wh_block(at.d)(c), at.peer(4), 24 + c, at.c != c)

    for c in range(4):
        wires.arrived(wh_block(1 - at.d)(c), 24 + c, at.peer(4))
    flush(wh, wh_out)

    @pl.loop(0, sz.heads // 256)
    def _(i):
        lanes = lanes_at(256 * i, 256)
        own_qkv[:, lanes] = times(h1[...], wh[:, lanes]).astype(low)

    starts = (0, sz.main, 2 * sz.main, 3 * sz.main)
    ends = jnp.concatenate([own_qkv[:, s : s + 128] for s in starts], axis=1)
    edge_out[...] = picked(ends, choose((512, 256), edge_source))
    last = at.r == 3

    @pl.when(at.r == 0)
    def _():
        edge_in[...] = jnp.zeros_like(edge_in)

    wires.copy(edge_out, edge_in, (at.d, at.r + 1, at.c), 52, at.r < 3)
    spread = choose((256, 384), spread_source)
    extra = picked(edge_out[...], spread)
    wires.arrived(edge_in, 52, (at.d, at.r - 1, at.c), at.r > 0)
    first = picked(edge_in[...], spread)
    lane = lax.broadcasted_iota(jnp.int32, (sz.seq, 128), 1)
    for i, target in enumerate((qw, kw, vw)):
        start = starts[i]
        target[:, 0:128] = jnp.where(
            lane < sz.slack * at.r,
            first[:, 128 * i : 128 * i + 128],
            own_qkv[:, start : start + 128],
        )
        target[:, 128 : sz.main] = own_qkv[:, start + 128 : start + sz.main]
        target[:, sz.main : sz.main + 128] = extra[:, 128 * i : 128 * i + 128]
    flush(qw, qw_out)
    flush(kw, kw_out)
    flush(vw, vw_out)

    wo_relay()
    for c in range(4):
        needed = at.c != c
        if c == 0:
            needed = needed & (at.c != 2)
        if c == 3:
            needed = needed & (at.c != 1)
        wires.arrived(wo_block(at.d)(c), 28 + c, at.along(c), needed)
        wires.copy(wo_block(at.d)(c), wo_block(at.d)(c), at.peer(4), 32 + c, at.c != c)

    half = sz.seq // 2

    def heads_of(p, count):
        tile = lanes_at(128 * p, 128)
        for q in range(2):
            rows = slice(half * q, half * (q + 1))
            keys = half * (q + 1)
            order = lax.broadcasted_iota(jnp.int32, (half, keys), 0) + half * q
            allowed = (col_labels[rows, :] == row_labels[:, 0:keys].astype(jnp.float32)) & (
                order >= lax.broadcasted_iota(jnp.int32, (half, keys), 1)
            )
            lanes = lax.broadcasted_iota(jnp.int32, (half, 128), 1)
            side = lanes // HD
            total = jnp.zeros((half, 128), jnp.float32)
            for h in range(count):
                queries = jnp.where(side == h, qw[rows, tile].astype(jnp.float32) * HD ** (-0.5), 0.0)
                scores = times_flipped(queries.astype(low), kw[0:keys, tile])
                scores = jnp.where(allowed, scores, MASKED)
                highest = jnp.max(scores, axis=1, keepdims=True)
                raised = jnp.exp(scores - highest)
                summed = jnp.sum(raised, axis=1, keepdims=True)
                found = highest + jnp.log(summed)
                lse[rows, :] = jnp.where(lanes == 2 * p + h, found, lse[rows, :])
                soft = (raised * (1.0 / summed)).astype(low)
                total = jnp.where(side == h, times(soft, vw[0:keys, tile]), total)
            aw[rows, tile] = total.astype(low)

    lse[...] = jnp.zeros_like(lse)

    @pl.loop(0, sz.main // 128)
    def _(p):
        heads_of(p, 2)

    @pl.when(last)
    def _():
        heads_of(sz.main // 128, 1)
        edge_back[...] = aw[:, sz.main : sz.main + 128]

    flush(lse, lse_out)

    wires.copy(aw.at[:, 0:128], edge_back, (at.d, at.r - 1, at.c), 53, at.r > 0)
    wd_first_send, wd_first, wd_first_done = spread_col(wires, wd_block(0), at, 44, True)
    wd_second_send, wd_second, wd_second_done = spread_col(wires, wd_block(1), at, 48, True)
    for distance in (2, 1):
        wd_first_send(distance)
        wd_second_send(distance)
    wires.arrived(edge_back, 53, (at.d, at.r + 1, at.c), at.r < 3)
    dy_crossed()
    dy_done = share_pieces(wires, (2, 4, 6), dy_piece, at, 124)

    def natural(column):
        inner = column % sz.mixed
        place = sz.pieces * (column // sz.mixed) + inner + sz.slack * at.r
        return jnp.where(inner < sz.pieces, place, -1)

    def natural_main(column):
        place = natural(column)
        return jnp.where(place < sz.main, place, -1)

    def natural_edge(column):
        return natural(column) - sz.main

    mixed = times(aw[:, 0 : sz.main], choose((sz.main, 2 * sz.mixed), natural_main))
    mixed = mixed + times(edge_back[...], choose((128, 2 * sz.mixed), natural_edge))
    ones = lax.broadcasted_iota(jnp.int32, mixed.shape, 1) % sz.mixed == sz.pieces
    a_nat[...] = jnp.where(ones, 1.0, mixed).astype(low)
    for c in range(4):
        wires.arrived(wo_block(1 - at.d)(c), 32 + c, at.peer(4))
    flush(wo, wo_out)
    flush(a_nat, a_nat_out)

    def project(start, tile):
        out = times_flipped(a_nat[...], wo[rows_at(start, tile)])
        part[:, lanes_at(start, tile)] = out.astype(low)

    over_tiles(sz.width, project)

    onward, total, _ = scatter_group(
        wires, (2,), part, lambda d, r: sz.part * r, near, mid, far, at, 64
    )
    onward()
    wu_first()
    wu_second()
    middle = x_own[...].astype(jnp.float32) + total()
    x2[...] = middle
    flush(x2, x2_out)
    center = jnp.sum(middle, axis=1, keepdims=True) / features
    spread_two = jnp.sum(middle * middle, axis=1, keepdims=True) / features - center * center
    normed = (middle - center) * lax.rsqrt(spread_two + NORM_EPSILON)
    own_rows = rows_at(sz.part * (4 * at.d + at.r), sz.part)
    h2[own_rows] = (normed * vec_rows[2:3] + vec_rows[3:4]).astype(low)
    h2_done, _ = gather_group(
        wires, (2, 4, 6), lambda d, r: h2.at[rows_at(sz.part * (4 * d + r), sz.part)], at, 72
    )
    dy_done()

    @pl.loop(0, sz.tiles)
    def _(i):
        dy[:, lanes_at(128 * i, 128)] = turned(dy_t[rows_at(128 * i, 128)]).astype(low)

    flush(dy, dy_out)
    h2_done()
    wu_first_done()
    wu_second_done()
    flush(wu, wu_out)

    def expand(start, tile):
        lanes = lanes_at(start, tile)
        value = times(h2[...], wu[:, lanes])
        u[:, lanes] = value
        inner = jnp.tanh(ROOT * (value + CUBIC * value * value * value))
        value = 0.5 * value * (1.0 + inner)
        if isinstance(start, int):
            column = lax.broadcasted_iota(jnp.int32, value.shape, 1)
            inside = (column >= 64) & (column < 64 + sz.tail)
            value = jnp.where(inside, pltpu.roll(value, 64, 1), 0.0)
            value = jnp.where(column == 64 + sz.tail, 1.0, value)
        gl[:, lanes] = value.astype(low)

    over_tiles(sz.hidden, expand)

    flush(u, u_out)
    flush(gl, gl_out)
    wd_first()

    @pl.loop(0, sz.tiles)
    def _(i):
        h2_t[rows_at(128 * i, 128)] = turned(h2[:, lanes_at(128 * i, 128)]).astype(low)

    flush(h2_t, h2_t_out)
    wd_second()

    @pl.loop(0, 4)
    def _(i):
        rows = rows_at(pair * i, pair)
        gd[rows] = times(dy_t[rows], gl[:, 0 : sz.solid]).astype(low)
        gt[rows] = times(dy_t[rows], gl[:, sz.solid : sz.hidden]).astype(low)

    flush(gd, gd_out)
    flush(gt, gt_out)
    wd_first_done()
    wd_second_done()
    flush(wd, wd_out)
    wires.close()
    for made in flushed:
        made.wait()


def backward_kernel(
    sz,
    dy_all,
    gd_all,
    gt_all,
    u_all,
    gl_all,
    h2_t_all,
    wd_all,
    wu_all,
    wo_all,
    wh_all,
    h1_t_all,
    qw_all,
    kw_all,
    vw_all,
    a_nat_all,
    lse_all,
    x2_all,
    x_own_all,
    vec_rows,
    segments,
    out_down,
    out_up,
    out_out,
    out_heads,
    result_home,
    grad_home,
    vec_out,
    zd,
    zu,
    zo,
    zh,
    res_all,
    res_two,
    grad_all,
    grad_two,
    rd,
    ru,
    ro,
    rh,
    qw,
    kw,
    vw,
    a_nat,
    lse,
    x2,
    x_own,
    xu,
    dy,
    dy_t,
    u,
    gl,
    h2_t,
    wd,
    wu,
    wo,
    wh,
    gt,
    dy_own,
    du,
    gw,
    gu,
    go,
    xh,
    xo,
    near_two,
    far_two,
    near_res,
    far_res,
    near_one,
    far_one,
    mid,
    dob,
    da,
    dk_sum,
    dv_sum,
    dx2,
    edge_out,
    edge_in,
    fore_out,
    fore_in,
    col_labels,
    res_stage,
    grad_stage,
    va,
    vb,
    sends,
    arrivals,
    locals_,
):
    at = Place()
    wires = Wires(sends, arrivals)
    low = jnp.bfloat16
    pair, block = sz.pair, sz.block
    features = 4.0 * sz.share
    used = [0]

    def load(source, target, when=None):
        made = pltpu.make_async_copy(source, target, locals_.at[used[0]])
        used[0] += 1
        run(when, made.start)
        return made

    own_rows = rows_at(sz.part * (4 * at.d + at.r), sz.part)
    gd = gw.at[:, 0 : sz.solid]
    wanted = (
        (dy_all, dy),
        (wd_all, wd),
        (u_all, u),
        (dy_all.at[own_rows], dy_own),
        (wu_all, wu),
        (h2_t_all, h2_t),
        (gl_all, gl),
        (gd_all, gd),
        (wo_all, wo),
        (wh_all, wh),
        (x2_all, x2),
        (a_nat_all, a_nat),
        (qw_all, qw),
        (kw_all, kw),
        (vw_all, vw),
        (lse_all, lse),
        (x_own_all, x_own),
        (h1_t_all, dy_t.at[:, 0 : sz.seq]),
        (gt_all, gt),
    )
    loads = {}

    def begin(*which):
        for i in which:
            loads[i] = load(*wanted[i])

    begin(0, 1, 2)
    greet(at, False)
    stay = []

    order, d_send, d_relay, d_arrived, d_from = collect_col(
        wires,
        lambda c: gd.at[rows_at(pair * c, pair)],
        zd,
        rd,
        at,
        0,
        lambda c: gd_all.at[rows_at(pair * c, pair)],
    )
    for step in range(4):
        d_send(step)

    def relay_of(rest, block):
        def add(there):
            rows = rows_at(pair * there, pair)
            block[rows] = (block[rows].astype(jnp.float32) + rest[...].astype(jnp.float32)).astype(low)

        return add

    for i in range(3):
        loads[i].wait()
    begin(4, 5, 18)

    def through(start, tile):
        lanes = lanes_at(start, tile)
        last = isinstance(start, int)
        if last:
            loads[4].wait()
            upstream = pltpu.roll(times(dy[...], wu[:, lanes]), 64, 1)
        else:
            upstream = times(dy[...], wd[:, lanes])
        value = u[:, lanes]
        inner = jnp.tanh(ROOT * (value + CUBIC * value * value * value))
        slope = 0.5 * (1.0 + inner) + 0.5 * value * (1.0 - inner * inner) * ROOT * (
            1.0 + 3.0 * CUBIC * value * value
        )
        upstream = upstream * slope
        if last:
            column = lax.broadcasted_iota(jnp.int32, upstream.shape, 1)
            upstream = jnp.where(column < sz.tail, upstream, 0.0)
        du[:, lanes] = upstream.astype(low)

    over_tiles(sz.hidden, through)
    def back_up(start, tile):
        dy[:, lanes_at(start, tile)] = times_flipped(du[...], wu[rows_at(start, tile)]).astype(low)

    over_tiles(sz.width, back_up)
    begin(3, 10, 7, 6, 8, 11, 12, 13, 14, 15, 16, 9, 17)

    def chunk_both(d, r):
        return sz.part * (4 * d + r)

    two_onward, two_total, two_sent = scatter_group(
        wires, (2, 4, 6), dy, chunk_both, near_two, mid, far_two, at, 16
    )
    loads[5].wait()
    loads[18].wait()
    order, u_send, u_relay, u_arrived, u_from = collect_col(
        wires, lambda c: gu.at[rows_at(pair * c, pair)], zu, ru, at, 5
    )
    for step in range(4):
        rows = rows_at(pair * order[step], pair)
        value = times(h2_t[rows], du[...])
        gu[rows, 0 : sz.solid] = value[:, 0 : sz.solid].astype(low)
        both = value[:, sz.solid : sz.hidden] + gt[rows].astype(jnp.float32)
        gu[rows, sz.solid : sz.hidden] = both.astype(low)
        u_send(step)
        if step == 1:
            two_onward()
    own = rows_at(pair * at.c, pair)
    gd_own = load(gd_all.at[own], h2_t.at[own, 0 : sz.solid])
    loads[7].wait()
    before = len(wires.open)
    d_relay(relay_of(rd, gd))
    gd_sends = wires.open[before:]

    def norm_back(upstream, values, gain):
        center = jnp.sum(values, axis=1, keepdims=True) / features
        spread = jnp.sum(values * values, axis=1, keepdims=True) / features - center * center
        inverse = lax.rsqrt(spread + NORM_EPSILON)
        centered = (values - center) * inverse
        scaled = upstream * gain
        inner = (
            scaled
            - jnp.sum(scaled, axis=1, keepdims=True) / features
            - centered * (jnp.sum(scaled * centered, axis=1, keepdims=True) / features)
        )
        return (
            inner * inverse,
            jnp.sum(upstream * centered, axis=0, keepdims=True),
            jnp.sum(upstream, axis=0, keepdims=True),
        )

    loads[10].wait()
    loads[3].wait()
    h2_back = two_total()
    through_norm, gain_two, shift_two = norm_back(h2_back, x2[...], vec_rows[2:3])
    middle_back = dy_own[...].astype(jnp.float32) + through_norm
    dx2[...] = middle_back
    va[0, 2:3] = gain_two
    va[0, 3:4] = shift_two
    va[0, 4:8] = jnp.zeros((4, sz.width), jnp.float32)
    dob[rows_at(sz.part * at.r, sz.part)] = middle_back.astype(low)
    dob_done, dob_sent = gather_group(
        wires, (2,), lambda d, r: dob.at[rows_at(sz.part * r, sz.part)], at, 24
    )

    def contract(start, tile):
        rows = rows_at(start, tile)
        out = times_flipped(gl[:, 0 : sz.solid], wd[rows])
        out = out + times_flipped(gl[:, sz.solid : sz.hidden], wu[rows, sz.solid : sz.hidden])
        dy[:, lanes_at(start, tile)] = out.astype(low)

    wires.close(two_sent)
    loads[6].wait()
    over_tiles(sz.width, contract)
    res_onward, res_total, res_sent = scatter_group(
        wires, (2, 4, 6), dy, chunk_both, near_res, mid, far_res, at, 32
    )

    dob_done()
    loads[11].wait()
    loads[8].wait()
    da[...] = times(dob[...], wo[...]).astype(low)
    slack, main = sz.slack, sz.main

    def from_natural(place):
        wanted = sz.mixed * (place // sz.pieces) + place % sz.pieces
        return jnp.where((place >= 0) & (place < sz.share), wanted, -1)

    fore_out[...] = picked(
        da[...], choose((2 * sz.mixed, 128), lambda j: from_natural(j + main - slack * at.r))
    )

    @pl.when(at.r == 0)
    def _():
        fore_in[...] = jnp.zeros_like(fore_in)

    wires.copy(fore_out, fore_in, (at.d, at.r + 1, at.c), 40, at.r < 3)

    @pl.loop(0, sz.tiles)
    def _(i):
        dy_t[rows_at(128 * i, 128), sz.seq : sz.both] = turned(dob[:, lanes_at(128 * i, 128)]).astype(low)

    res_onward()

    for step in range(4):
        there = (at.c + step) % 4
        rows = rows_at(pair * there, pair)
        go[rows] = times(dy_t[rows, sz.seq : sz.both], a_nat[...]).astype(low)
        wires.copy(
            go.at[rows, lanes_at(sz.mixed * (1 - at.d), sz.mixed)], xo.at[there], at.peer(4), 48 + there
        )
    wires.arrived(fore_in, 40, (at.d, at.r - 1, at.c), at.r > 0)
    window = times(da[...], choose((2 * sz.mixed, main), lambda j: from_natural(j - slack * at.r)))
    da_first = window[:, 0:128] + fore_in[...].astype(jnp.float32)
    da[:, 128:main] = window[:, 128:main].astype(low)
    da[:, 0:128] = da_first.astype(low)
    da[:, main : main + 128] = fore_out[...]

    row_labels = segments.at[:, lanes_at(sz.seq * at.c, sz.seq)]
    col_labels[...] = jnp.concatenate([row_labels[...]] * 8, axis=0).astype(jnp.float32).T[:, 0:1]
    for i in range(12, 17):
        loads[i].wait()
    half = sz.seq // 2
    dqw, dkw = (du.at[sz.seq * i : sz.seq * (i + 1), 0 : main + 128] for i in range(2))
    dvw = gl.at[0 : sz.seq, 0 : main + 128]

    def heads_back(p, count):
        tile = lanes_at(128 * p, 128)
        dk_sum[...] = jnp.zeros_like(dk_sum)
        dv_sum[...] = jnp.zeros_like(dv_sum)
        for q in range(2):
            rows = slice(half * q, half * (q + 1))
            keys = half * (q + 1)
            order = lax.broadcasted_iota(jnp.int32, (half, keys), 0) + half * q
            allowed = (col_labels[rows, :] == row_labels[:, 0:keys].astype(jnp.float32)) & (
                order >= lax.broadcasted_iota(jnp.int32, (half, keys), 1)
            )
            lanes = lax.broadcasted_iota(jnp.int32, (half, 128), 1)
            side = lanes // HD
            total = jnp.zeros((half, 128), jnp.float32)
            for h in range(count):
                queries = jnp.where(side == h, qw[rows, tile].astype(jnp.float32) * HD ** (-0.5), 0.0)
                queries = queries.astype(low)
                pulled = jnp.where(side == h, da[rows, tile].astype(jnp.float32), 0.0).astype(low)
                found = jnp.sum(jnp.where(lanes == 2 * p + h, lse[rows, :], 0.0), axis=1, keepdims=True)
                scores = times_flipped(queries, kw[0:keys, tile])
                soft = jnp.where(allowed, jnp.exp(jnp.where(allowed, scores - found, MASKED)), 0.0)
                soft_back = times_flipped(pulled, vw[0:keys, tile])
                inner = jnp.sum(soft_back * soft, axis=1, keepdims=True)
                score_back = (soft * (soft_back - inner)).astype(low)
                piece = times(score_back, kw[0:keys, tile]) * HD ** (-0.5)
                total = jnp.where(side == h, piece, total)
                dk_sum[0:keys] += times_outer(score_back, queries)
                dv_sum[0:keys] += times_outer(soft.astype(low), pulled)
            dqw[rows, tile] = total.astype(low)
        dkw[:, tile] = dk_sum[...].astype(low)
        dvw[:, tile] = dv_sum[...].astype(low)

    @pl.loop(0, main // 128)
    def _(p):
        heads_back(p, 2)

    @pl.when(at.r == 3)
    def _():
        heads_back(main // 128, 1)

    def compact(column):
        part, place = column // HD, column % HD
        return jnp.where(part < 3, 128 * part + place, -1)

    table = choose((384, 256), compact)
    backs = (dqw, dkw, dvw)
    edge_out[...] = picked(jnp.concatenate([b[:, 0:128] for b in backs], axis=1), table)
    wires.copy(edge_out, edge_in, (at.d, at.r - 1, at.c), 41, at.r > 0)

    @pl.when(at.r == 3)
    def _():
        edge_in[...] = picked(jnp.concatenate([b[:, main : main + 128] for b in backs], axis=1), table)

    u_relay(relay_of(ru, gu))

    def go_home(values, stage, every, halves, out, base):
        flipped = values.T
        for c in range(4):
            for y in range(2):
                rows = slice(pair * c + block * y, pair * c + block * (y + 1))
                stage[c, y] = flipped[rows].astype(low)
        holds = at.k == at.c % 2
        lanes = lanes_at(sz.part * at.r, sz.part)
        held = []
        for y in range(2):
            there = 2 * y + at.c % 2
            wires.copy(
                stage.at[:, y], every.at[:, :, lanes], (at.d, there, at.c), base + at.r, there != at.r
            )
            held.append((there == at.r, load(stage.at[:, y], every.at[:, :, lanes], there == at.r)))

        def along():
            for r in range(4):
                block_r = every.at[:, :, sz.part * r : sz.part * (r + 1)]
                wires.arrived(block_r, base + r, (at.d, r, at.c), holds & (at.r != r))
            for when, made in held:
                run(when, made.wait)
            del held[:]
            for c in range(4):
                wires.copy(
                    every.at[c], halves.at[at.c // 2], at.along(c), base + 4 + at.c // 2, holds & (at.c != c)
                )
                when = holds & (at.c == c)
                held.append((when, load(every.at[c], halves.at[at.c // 2], when)))

        def across():
            for when, made in held:
                run(when, made.wait)
            for t in range(2):
                there = 2 * t + at.k
                wires.arrived(halves.at[t], base + 4 + t, at.along(there), there != at.c)
            mine = out.at[rows_at(block * at.y, block)]
            wires.copy(halves.at[1 - at.y], mine, at.peer(2), base + 6)
            stay.append(load(halves.at[at.y], mine))

        def finish():
            wires.arrived(out.at[rows_at(block * (1 - at.y), block)], base + 6, at.peer(2))

        return along, across, finish

    res_along, res_across, res_finish = go_home(
        x2[...] + res_total(), res_stage, res_all, res_two, result_home, 56
    )
    wires.close(res_sent)

    wires.arrived(edge_in, 41, (at.d, at.r + 1, at.c), at.r < 3)

    def unfold(column):
        tile, lane = column // 128, column % 128
        inside = jnp.where(lane < HD - 16, HD * tile + lane + 16, -1)
        tail = jnp.where(lane < 48, HD * (lane // 16) + lane % 16, -1)
        return jnp.where(tile < 3, inside, tail)

    edges = picked(edge_in[...], choose((256, 512), unfold))
    lane = lax.broadcasted_iota(jnp.int32, (sz.seq, 128), 1)
    pieces = []
    for i, back in enumerate(backs):
        first = jnp.where(lane < slack * at.r, edges[:, 128 * i : 128 * i + 128], back[:, 0:128])
        pieces += [first, back[:, 128:main]]
    pieces.append(edges[:, 384:512])
    wires.close(dob_sent)
    own_back = dob.at[:, 0 : sz.heads]
    own_back[...] = jnp.concatenate(pieces, axis=1)

    wires.close(gd_sends)
    gd_own.wait()
    loads[17].wait()
    h_order, h_send, h_relay, h_arrived, h_from = collect_col(
        wires, lambda c: xh.at[c], zh, rh, at, 72
    )
    for step in range(4):
        there = h_order[step]
        rows = rows_at(pair * there, pair)
        gw[rows] = times(dy_t[rows, 0 : sz.seq], own_back[...]).astype(low)
        other = gw.at[rows_at(pair * there + block * (1 - at.d), block)]
        wires.copy(other, xh.at[there], at.peer(4), 80 + there)

    def o_heads(step):
        there = h_order[step]
        wires.arrived(xh.at[there], 80 + there, at.peer(4))
        mine = rows_at(pair * there + block * at.d, block)
        xh[there] = (gw[mine].astype(jnp.float32) + xh[there].astype(jnp.float32)).astype(low)
        h_send(step)

    loads[9].wait()

    def back_in(start, tile):
        out = times_flipped(own_back[...], wh[rows_at(start, tile)])
        dy[0 : sz.seq, lanes_at(start, tile)] = out.astype(low)

    over_tiles(sz.width, back_in)
    one_onward, one_total, _ = scatter_group(
        wires, (2,), dy, lambda d, r: sz.part * r, near_one, mid, far_one, at, 64
    )
    order, o_send, o_relay, o_arrived, o_from = collect_col(
        wires, lambda c: xo.at[c], zo, ro, at, 10
    )
    for step in range(4):
        there = order[step]
        wires.arrived(xo.at[there], 48 + there, at.peer(4))
        mine = go[rows_at(pair * there, pair), lanes_at(sz.mixed * at.d, sz.mixed)]
        xo[there] = (mine.astype(jnp.float32) + xo[there].astype(jnp.float32)).astype(low)
        o_send(step)

    def relay_out(there):
        both = xo[there].astype(jnp.float32) + ro[...].astype(jnp.float32)
        xo[there] = both.astype(low)

    brought = []

    def bring(c, landing, needed, lanes):
        made = load(landing.at[c], h2_t.at[pair * c : pair * (c + 1), 0:lanes], needed)
        brought.append((needed, made))

        @pl.when(jnp.logical_not(needed) & (at.c != c))
        def _():
            h2_t[pair * c : pair * (c + 1), 0:lanes] = jnp.zeros((pair, lanes), low)

    def summed(lanes):
        result = jnp.zeros((pair, lanes.stop - lanes.start), jnp.float32)
        for c in range(4):
            result = result + h2_t[pair * c : pair * (c + 1), lanes].astype(jnp.float32)
        return result

    half_rows = sz.pieces

    def natural_rows(value):
        flipped = value.T
        return jnp.concatenate(
            [flipped[:, 0:half_rows], flipped[:, block : block + half_rows]], axis=1
        )

    def own_half(row):
        return jnp.where(at.d == 0, row[:, 0:half_rows], row[:, half_rows : 2 * half_rows])

    def all_brought():
        for needed, made in brought:
            run(needed, made.wait)
        del brought[:]

    def relay_heads(there):
        xh[there] = (xh[there].astype(jnp.float32) + rh[...].astype(jnp.float32)).astype(low)

    res_along()
    one_onward()
    o_heads(0)
    h1_back = one_total()
    through_norm, gain_one, shift_one = norm_back(
        h1_back, x_own[...].astype(jnp.float32), vec_rows[0:1]
    )
    va[0, 0:1] = gain_one
    va[0, 1:2] = shift_one
    for mask in range(1, 8):
        wires.copy(va.at[0], va.at[mask], at.peer(mask), 84 + mask)
    grad_along, grad_across, grad_finish = go_home(
        dx2[...] + through_norm, grad_stage, grad_all, grad_two, grad_home, 104
    )
    for c in range(4):
        d_arrived(c)
        bring(c, zd, d_from(c), sz.solid)
    all_brought()
    for i in range(sz.solid // 128):
        rows = slice(128 * i, 128 * (i + 1))
        u[rows, 0 : sz.share] = natural_rows(summed(rows))
    down_out = load(u.at[0 : sz.solid, 0:512], out_down.at[0 : sz.solid])
    o_heads(1)
    grad_along()
    o_heads(2)
    h_relay(relay_heads)
    gu_own = load(gu.at[own], h2_t.at[own, 0 : sz.hidden])
    for c in range(4):
        u_arrived(c)
        bring(c, zu, u_from(c), sz.hidden)
    all_brought()
    gu_own.wait()
    value = natural_rows(summed(slice(sz.solid, sz.hidden)))
    end = 4 * sz.pieces
    u[sz.solid : end, 0 : sz.share] = value[64 : 64 + sz.tail]
    vec_out[5:6, 0:half_rows] = own_half(value[64 + sz.tail : 65 + sz.tail])
    tail_out = load(u.at[sz.solid : end, 0:512], out_down.at[sz.solid : end])
    theirs = rows_at(pair * at.c + block * (1 - at.d), block)

    def part_sum(side, lanes):
        result = jnp.zeros((block, sz.hidden), jnp.float32)
        for c in range(4):
            result = result + h2_t[rows_at(pair * c + block * side, block), lanes].astype(jnp.float32)
        return result

    every = slice(0, sz.hidden)
    gu[theirs] = part_sum(1 - at.d, every).astype(low)
    wires.copy(gu.at[theirs], xu, at.peer(4), 97)
    o_relay(relay_out)
    o_heads(3)
    res_across()
    mine_sum = part_sum(at.d, every)
    down_out.wait()
    tail_out.wait()
    wires.arrived(xu, 97, at.peer(4))
    partner_sum = xu[...].astype(jnp.float32)
    for side in range(2):

        @pl.when(at.d == side)
        def _():
            both = (mine_sum, partner_sum) if side == 0 else (partner_sum, mine_sum)
            for j in range(4):
                rows = slice(block * j, block * (j + 1))
                for i in range(2):
                    u[rows, half_rows * i : half_rows * (i + 1)] = both[i][:, half_rows * j : half_rows * (j + 1)]

    bias_sum = mine_sum[half_rows : half_rows + 1]
    for j in range(4):
        vec_out[8 + j : 9 + j, 0:half_rows] = bias_sum[:, half_rows * j : half_rows * (j + 1)]
    up_out = load(u.at[0 : 4 * block, 0:512], out_up)

    for c in range(4):
        o_arrived(c)
        needed = o_from(c)
        made = load(zo.at[c], wd.at[pair * c : pair * (c + 1), 0 : sz.mixed], needed)
        brought.append((needed, made))

        @pl.when(jnp.logical_not(needed))
        def _():
            wd[pair * c : pair * (c + 1), 0 : sz.mixed] = jnp.zeros((pair, sz.mixed), low)

    all_brought()
    value = xo[at.c].astype(jnp.float32)
    for c in range(4):
        value = value + wd[pair * c : pair * (c + 1), 0 : sz.mixed].astype(jnp.float32)
    flipped = natural_rows(value)
    vec_out[4:5, 0:half_rows] = own_half(flipped[half_rows : half_rows + 1])
    flipped = flipped[0:block]
    for i in range(4):
        held = (dk_sum, dv_sum)[i // 2].at[block * (i % 2) : block * (i % 2 + 1)]
        lanes = min(128, sz.share - 128 * i)
        held[:, 0:lanes] = flipped[:, 128 * i : 128 * i + lanes]
        stay.append(load(held, out_out.at[:, 128 * i : 128 * (i + 1)]))

    grad_across()

    for mask in range(1, 8):
        wires.arrived(va.at[mask], 84 + mask, at.peer(mask))
    vb[at.c] = functools.reduce(lambda a, b: a + b, [va[mask] for mask in range(8)])
    for c in range(4):
        wires.copy(vb.at[at.c], vb.at[at.c], at.along(c), 98 + at.c, at.c != c)

    for c in range(4):
        wires.arrived(vb.at[c], 98 + c, at.along(c), at.c != c)
    sums = vb[0] + vb[1] + vb[2] + vb[3]
    picked_sums = jnp.zeros((4, half_rows), jnp.float32)
    for i in range(8):
        cut = sums[0:4, block * i : block * i + half_rows]
        picked_sums = jnp.where(2 * at.c + at.d == i, cut, picked_sums)
    vec_out[0:4, 0:half_rows] = picked_sums
    res_finish()
    grad_finish()
    up_out.wait()
    rest_lanes = sz.heads - sz.solid
    for c in range(4):
        h_arrived(c)
        needed = h_from(c)
        rows = slice(block * c, block * (c + 1))
        parts = (
            load(zh.at[c, :, 0 : sz.solid], wd.at[rows], needed),
            load(zh.at[c, :, sz.solid : sz.heads], wu.at[rows, 0:rest_lanes], needed),
        )
        brought += [(needed, made) for made in parts]

        @pl.when(jnp.logical_not(needed))
        def _():
            wd[rows] = jnp.zeros((block, sz.solid), low)
            wu[rows, 0:rest_lanes] = jnp.zeros((block, rest_lanes), low)

    all_brought()
    left = xh[at.c, :, 0 : sz.solid].astype(jnp.float32)
    right = xh[at.c, :, sz.solid : sz.heads].astype(jnp.float32)
    for c in range(4):
        rows = slice(block * c, block * (c + 1))
        left = left + wd[rows].astype(jnp.float32)
        right = right + wu[rows, 0:rest_lanes].astype(jnp.float32)
    whole = jnp.concatenate([left, right], axis=1)
    for i in range(3):
        turned_columns = jnp.concatenate(
            [
                whole[:, main * i : main * (i + 1)],
                whole[:, 3 * main + slack * i : 3 * main + slack * (i + 1)],
            ],
            axis=1,
        )
        rows = slice(block * i, block * (i + 1))
        for r in range(4):

            @pl.when(at.r == r)
            def _():
                cut = slack * r
                value = turned_columns
                if cut:
                    value = jnp.concatenate([value[:, cut:], value[:, 0:cut]], axis=1)
                u[rows, 0 : sz.share] = value
                if i != 1:
                    vec_out[6 + i // 2 : 7 + i // 2, 0:half_rows] = own_half(
                        value[half_rows : half_rows + 1]
                    )

    stay.append(load(u.at[0 : 3 * block, 0:512], out_heads))
    for made in stay:
        made.wait()
    wires.close()


def update_kernel(sz, rates, grads, result_in, grad_in, weights, firsts, seconds, outs):
    down, out, up, heads, vectors = grads
    share, pieces, block = sz.share, sz.pieces, sz.block

    def move(i, place, gradient, decay):
        weight = weights[i][place]
        first_new = BETA_FIRST * firsts[i][place] + (1.0 - BETA_FIRST) * gradient
        second_new = BETA_SECOND * seconds[i][place] + (1.0 - BETA_SECOND) * (gradient * gradient)
        divisor = jnp.sqrt(second_new * (1.0 / (1.0 - BETA_SECOND**STEP))) + ADAM_EPSILON
        change = first_new * (rates[i] / (1.0 - BETA_FIRST**STEP)) / divisor
        weight_new = weight * (1.0 - rates[i] * decay) - change
        outs[3 * i + 2][place] = first_new
        outs[3 * i + 3][place] = second_new
        outs[3 * i + 4][place] = weight_new

    for part in range(3):
        move(0, part, heads[part, :, 0:share], MATRIX_DECAY)
    move(1, slice(None), out[:, 0:share], MATRIX_DECAY)
    move(2, slice(None), jnp.stack([up[j, :, 0:share] for j in range(4)], axis=1), MATRIX_DECAY)
    move(3, slice(None), down[:, 0:share], MATRIX_DECAY)

    @pl.when(pl.program_id(0) == 0)
    def _():
        for i, source, row in (
            (4, 0, 0), (4, 1, 1), (5, 4, 0), (5, 2, 1), (5, 3, 2), (5, 5, 3),
            (6, 6, 0), (6, 7, 1), (7, 8, 0), (7, 9, 1), (7, 10, 2), (7, 11, 3),
        ):
            move(i, row, vectors[source : source + 1, 0:pieces], 0.0)

    def plain(rows):
        rows = rows.astype(jnp.float32)
        return jnp.concatenate([rows[0:pieces], rows[block : block + pieces]], axis=0)

    @pl.when(pl.program_id(0) == 1)
    def _():
        outs[0][...] = plain(result_in[...]).astype(jnp.bfloat16)

    @pl.when(pl.program_id(0) == 2)
    def _():
        outs[1][...] = plain(grad_in[...])


def fused(
    tokens,
    cotangent,
    segments,
    weights,
    firsts,
    seconds,
):
    low = jnp.bfloat16
    seq, share = tokens.shape
    pieces = weights[1].shape[2]
    sz = Sizes(share, pieces, seq)
    block, main = sz.block, sz.main

    def views(arrays):
        heads, out, up, down, *small = arrays
        return (
            jnp.transpose(heads.reshape(pieces, 3, share), (1, 0, 2)),
            out.reshape(pieces, share),
            up.reshape(pieces, 4, share),
            down.reshape(4 * pieces, share),
            *[each.reshape(each.shape[0], 1, pieces) for each in small],
        )

    viewed = views(weights)
    labels = segments.reshape(1, -1)

    def made(*shape, dtype=low):
        return jax.ShapeDtypeStruct(shape, dtype)

    def held(*shape, dtype=low):
        return pltpu.VMEM(shape, dtype)

    w, seq, both, part = sz.width, sz.seq, sz.both, sz.part
    vmem, anywhere = pl.BlockSpec(memory_space=pltpu.VMEM), pl.BlockSpec(memory_space=pl.ANY)
    dma = pltpu.SemaphoreType.DMA
    f32 = jnp.float32
    wide = 3 * 128 + 128
    outs = pl.pallas_call(
        functools.partial(forward_kernel, sz),
        out_shape=(
            made(w, sz.heads),
            made(w, 2 * sz.mixed),
            made(w, sz.hidden),
            made(w, sz.solid),
            made(w, seq),
            made(w, both),
            made(w, sz.solid),
            made(w, 128),
            made(both, w),
            made(both, sz.hidden, dtype=f32),
            made(both, sz.hidden),
            made(seq, main + 128),
            made(seq, main + 128),
            made(seq, main + 128),
            made(seq, 2 * sz.mixed),
            made(seq, 128, dtype=f32),
            made(part, w, dtype=f32),
            made(part, w),
            made(8, w, dtype=f32),
        ),
        in_specs=[anywhere] * 6 + [vmem] * 5,
        out_specs=[anywhere] * 19,
        scratch_shapes=[
            held(w, sz.heads),
            held(w, 2 * sz.mixed),
            held(w, sz.hidden),
            held(w, sz.solid),
            held(w, seq),
            held(w, both),
            held(w, sz.solid),
            held(w, 128),
            held(w, both),
            held(both, w),
            held(both, sz.hidden, dtype=f32),
            held(both, sz.hidden),
            held(seq, main + 128),
            held(seq, main + 128),
            held(seq, main + 128),
            held(seq, 2 * sz.mixed),
            held(seq, 128, dtype=f32),
            held(part, w, dtype=f32),
            held(part, w),
            held(8, w, dtype=f32),
            held(w, seq),
            held(seq, w),
            held(both, w),
            held(seq, sz.heads),
            held(seq, main + 128),
            held(w, 128),
            held(seq, w),
            held(seq, 256),
            held(seq, 256),
            held(seq, 128),
            held(2, part, w),
            held(1, part, w),
            held(1, part, w),
            held(share, seq),
            held(share, seq),
            held(3, pieces, share, dtype=f32),
            held(pieces, share, dtype=f32),
            held(pieces, 4, share, dtype=f32),
            held(4 * pieces, share, dtype=f32),
            held(sz.pair, seq),
            held(sz.pair, seq),
            held(block, sz.hidden),
            held(sz.pair, 128),
            held(seq, 1, dtype=f32),
            held(block, seq),
            held(block, seq),
            dma((160,)),
            dma((160,)),
            dma((48,)),
        ],
        compiler_params=pltpu.CompilerParams(
            collective_id=0, has_side_effects=True, vmem_limit_bytes=VMEM_BYTES
        ),
        cost_estimate=pl.CostEstimate(flops=10**10, bytes_accessed=10**8, transcendentals=10**6),
    )(tokens.T, cotangent.T, *viewed, labels)
    (wh, wo, wu, wd, h1_t, h2_t, gd, gt, dy, u, gl, qw, kw, vw, a_nat, lse, x2, x_own, vec_rows) = outs
    outs = pl.pallas_call(
        functools.partial(backward_kernel, sz),
        out_shape=(
            made(4 * pieces, 512, dtype=f32),
            made(4 * block, 512, dtype=f32),
            made(block, 512, dtype=f32),
            made(3 * block, 512, dtype=f32),
            made(sz.pair, seq),
            made(sz.pair, seq),
            made(16, 256, dtype=f32),
            made(4, sz.pair, sz.solid),
            made(4, sz.pair, sz.hidden),
            made(4, sz.pair, sz.mixed),
            made(4, block, sz.heads),
            made(4, block, seq),
            made(2, block, seq),
            made(4, block, seq),
            made(2, block, seq),
        ),
        in_specs=[anywhere] * 18 + [vmem] * 2,
        out_specs=[anywhere] * 6 + [vmem] + [anywhere] * 8,
        scratch_shapes=[
            held(sz.pair, sz.solid),
            held(sz.pair, sz.hidden),
            held(sz.pair, sz.mixed),
            held(block, sz.heads),
            held(seq, main + 128),
            held(seq, main + 128),
            held(seq, main + 128),
            held(seq, 2 * sz.mixed),
            held(seq, 128, dtype=f32),
            held(part, w, dtype=f32),
            held(part, w),
            held(block, sz.hidden),
            held(both, w),
            held(w, both),
            held(both, sz.hidden, dtype=f32),
            held(both, sz.hidden),
            held(w, both),
            held(w, sz.solid),
            held(w, sz.hidden),
            held(w, 2 * sz.mixed),
            held(w, sz.heads),
            held(w, 128),
            held(part, w),
            held(both, sz.hidden),
            held(w, sz.heads),
            held(w, sz.hidden),
            held(w, 2 * sz.mixed),
            held(4, block, sz.heads),
            held(4, sz.pair, sz.mixed),
            held(4, part, w),
            held(3, part, w),
            held(4, part, w),
            held(3, part, w),
            held(2, part, w),
            held(1, part, w),
            held(3, part, w),
            held(seq, w),
            held(seq, 2 * sz.mixed),
            held(seq, 128, dtype=f32),
            held(seq, 128, dtype=f32),
            held(part, w, dtype=f32),
            held(seq, 256),
            held(seq, 256),
            held(seq, 128),
            held(seq, 128),
            held(seq, 1, dtype=f32),
            held(4, 2, block, part),
            held(4, 2, block, part),
            held(8, 8, w, dtype=f32),
            held(4, 8, w, dtype=f32),
            dma((128,)),
            dma((120,)),
            dma((80,)),
        ],
        compiler_params=pltpu.CompilerParams(
            collective_id=1, has_side_effects=True, vmem_limit_bytes=VMEM_BYTES
        ),
        cost_estimate=pl.CostEstimate(flops=2 * 10**10, bytes_accessed=10**8, transcendentals=10**6),
    )(
        dy, gd, gt, u, gl, h2_t, wd, wu, wo, wh, h1_t,
        qw, kw, vw, a_nat, lse, x2, x_own, vec_rows, labels,
    )
    down, up, out, heads, result_home, grad_home, vectors = outs[:7]
    steps = 5
    chunk = pieces // steps

    def rows_of(shape, axis, size):
        block_shape = list(shape)
        block_shape[axis] = size
        return pl.BlockSpec(tuple(block_shape), lambda i: tuple(i if a == axis else 0 for a in range(len(shape))))

    def whole(shape):
        return pl.BlockSpec(tuple(shape), lambda i: (0,) * len(shape))

    matrix_specs = (
        rows_of((3, pieces, share), 1, chunk),
        rows_of((pieces, share), 0, chunk),
        rows_of((pieces, 4, share), 0, chunk),
        rows_of((4 * pieces, share), 0, 4 * chunk),
        *[whole(each.shape) for each in viewed[4:]],
    )
    grads = (down, out, up.reshape(4, block, 512), heads.reshape(3, block, 512), vectors)
    grad_specs = (
        rows_of((4 * pieces, 512), 0, 4 * chunk),
        rows_of((block, 512), 0, chunk),
        rows_of((4, block, 512), 1, chunk),
        rows_of((3, block, 512), 1, chunk),
        whole((16, 256)),
    )
    rates = (0.05, 0.2, 0.05, 0.025, 0.3, 0.3, 0.3, 0.3)
    arguments = (*grads, result_home, grad_home, *viewed, *views(firsts), *views(seconds))
    out_shape = [made(share, seq), made(share, seq, dtype=f32)]
    out_specs = [whole((share, seq)), whole((share, seq))]
    for each, spec in zip(viewed, matrix_specs, strict=True):
        out_shape += [jax.ShapeDtypeStruct(each.shape, f32)] * 3
        out_specs += [spec] * 3

    def update(*refs):
        ins, outs = refs[:31], refs[31:]
        update_kernel(sz, rates, ins[:5], ins[5], ins[6], ins[7:15], ins[15:23], ins[23:31], outs)

    updated = pl.pallas_call(
        update,
        grid=(steps,),
        out_shape=out_shape,
        in_specs=[*grad_specs, whole((sz.pair, seq)), whole((sz.pair, seq)), *matrix_specs * 3],
        out_specs=out_specs,
        compiler_params=pltpu.CompilerParams(vmem_limit_bytes=VMEM_BYTES),
        cost_estimate=pl.CostEstimate(
            flops=20 * 10**6, bytes_accessed=30 * 10**6, transcendentals=2 * 10**6
        ),
    )(*arguments)
    results = [updated[0].T, updated[1].T]
    for i, weight in enumerate(weights):
        for each in updated[2 + 3 * i : 5 + 3 * i]:
            if i == 0:
                each = jnp.transpose(each, (1, 0, 2))
            results.append(each.reshape(weight.shape))
    return tuple(results)


def normalize(inputs):
    center = jnp.mean(inputs, axis=1, keepdims=True)
    spread = jnp.mean(inputs * inputs, axis=1, keepdims=True) - center * center
    inverse = lax.rsqrt(spread + NORM_EPSILON)
    return ((inputs - center) * inverse, inverse)


def norm_pull(upstream, centered, inverse, gain):
    scaled = upstream * gain
    inner = (
        scaled
        - jnp.mean(scaled, axis=1, keepdims=True)
        - centered * jnp.mean(scaled * centered, axis=1, keepdims=True)
    )
    return inner * inverse


def crossed(blocks, n):
    pairs = [(i * n + j, j * n + i) for i in range(n) for j in range(n)]
    return lax.ppermute(blocks, ("row", "col"), pairs)


def scatter_rows(partial):
    return lax.psum_scatter(
        partial.astype(jnp.bfloat16), "row", scatter_dimension=0, tiled=True
    ).astype(jnp.float32)


def gather_rows(local):
    return lax.all_gather(local, "row", axis=0, tiled=True)


def split_heads(rows):
    return jnp.transpose(rows.reshape(rows.shape[0], -1, HD), (1, 0, 2))


def join_heads(values):
    return jnp.transpose(values, (1, 0, 2)).reshape(values.shape[1], -1)


def scores_of(queries, keys, allowed):
    scores = jnp.einsum(
        "hqe,hke->hqk", queries, keys, preferred_element_type=jnp.float32
    ) * HD ** (-0.5)
    return jnp.where(allowed[None], scores, MASKED)


def gathered(
    tokens,
    cotangent,
    segments,
    w_heads,
    w_out,
    w_up,
    w_down,
    norm_vectors,
    width_vectors,
    attend_bias,
    hidden_vectors,
):
    n_dp, n_row, n_col = (lax.axis_size(name) for name in ("dp", "row", "col"))
    row = lax.axis_index("row")
    low = jnp.bfloat16
    share = tokens.shape[1]
    width = share * n_col
    seq = tokens.shape[0]
    part = seq // n_row
    near = HEADS // n_row
    window = (HEADS - near * (n_row - 1)) * HD
    step = near * HD
    edge = width - (share + step * (n_row - 1)) if n_row > 1 else 0
    edge = window - share
    to_next = [(i, i + 1) for i in range(n_row - 1)]
    to_last = [(i + 1, i) for i in range(n_row - 1)]
    offset = edge - (share - step) * row

    vectors = jnp.concatenate(
        [
            norm_vectors.reshape(2, -1),
            width_vectors.reshape(4, -1),
            attend_bias.reshape(2, -1),
            hidden_vectors.reshape(4, -1),
        ]
    ).astype(low)
    vectors = lax.all_gather(vectors, ("row", "col", "dp"), axis=0, tiled=False)
    vectors = vectors.reshape(n_row, n_col, n_dp, 12, -1).astype(jnp.float32)
    by_col = jnp.transpose(vectors[0], (2, 0, 1, 3)).reshape(12, width)
    by_row = jnp.transpose(vectors[:, 0], (2, 0, 1, 3)).reshape(12, width)
    gain_one, shift_one, bias_out, gain_two, shift_two, bias_down = (by_col[i] for i in range(6))
    zeros = jnp.zeros((1, window), jnp.float32)
    attend_rows = lax.dynamic_slice_in_dim(by_row[6:8], row * step, window, axis=1)
    heads_bias = jnp.concatenate([attend_rows[0:1], zeros, attend_rows[1:2]]).reshape(-1)
    unit_bias = lax.dynamic_slice_in_dim(by_row[8:12], row * share, share, axis=1).reshape(-1)

    own = w_heads.astype(low).reshape(-1, 3, share)
    passed = lax.ppermute(own[:, :, share - edge :], "row", to_next)
    own = jnp.concatenate([passed, own, jnp.zeros_like(passed)], axis=2)
    own = lax.dynamic_slice_in_dim(own, offset, window, axis=2).reshape(-1, 3 * window)
    heads_matrix = lax.all_gather(own, ("col", "dp"), axis=0, tiled=True)
    out_matrix = lax.all_gather(w_out.astype(low).reshape(-1, share), ("col", "dp"), axis=0)
    out_matrix = jnp.transpose(out_matrix.reshape(n_col, share, share), (1, 0, 2))
    out_matrix = out_matrix.reshape(share, width)
    passed = lax.ppermute(out_matrix[share - edge :], "row", to_next)
    out_matrix = jnp.concatenate([passed, out_matrix, jnp.zeros_like(passed)])
    out_matrix = lax.dynamic_slice_in_dim(out_matrix, offset, window)
    owned = (jnp.arange(window) < step) | (row == n_row - 1)
    out_matrix = jnp.where(owned[:, None], out_matrix, jnp.zeros_like(out_matrix))
    up_matrix = lax.all_gather(
        w_up.astype(low).reshape(-1, 4 * share), ("col", "dp"), axis=0, tiled=True
    )
    down_matrix = lax.all_gather(w_down.astype(low).reshape(4, -1, share), ("col", "dp"), axis=0)
    down_matrix = down_matrix.reshape(n_col, n_dp, 4, -1, share)
    down_matrix = jnp.transpose(down_matrix, (2, 1, 3, 0, 4)).reshape(4 * share, width)

    inputs_low = lax.all_gather(crossed(tokens, n_row), "row", axis=1, tiled=True)
    upstream = lax.all_gather(crossed(cotangent, n_row), "row", axis=1, tiled=True)
    inputs = inputs_low.astype(jnp.float32)
    centered_one, inverse_one = normalize(inputs)
    normed_one = (centered_one * gain_one + shift_one).astype(low)
    projected = (times(normed_one, heads_matrix) + heads_bias).astype(low)
    queries, keys, values = (
        split_heads(projected[:, i * window : (i + 1) * window]) for i in range(3)
    )
    labels = lax.dynamic_slice_in_dim(segments, lax.axis_index("col") * seq, seq)
    places = jnp.arange(seq, dtype=jnp.int32)
    allowed = (labels[:, None] == labels[None, :]) & (places[:, None] >= places[None, :])
    scores = scores_of(queries, keys, allowed)
    highest = jnp.max(scores, axis=-1, keepdims=True)
    log_total = highest + jnp.log(jnp.sum(jnp.exp(scores - highest), axis=-1, keepdims=True))
    soft = jnp.exp(scores - log_total).astype(low)
    mixed = jnp.einsum("hqk,hke->hqe", soft, values, preferred_element_type=jnp.float32)
    mixed = join_heads(mixed.astype(low))
    branch = scatter_rows(times(mixed, out_matrix))
    mine = row * part
    middle = lax.dynamic_slice_in_dim(inputs, mine, part) + (branch + bias_out)
    centered_two, inverse_two = normalize(middle)
    normed_two = gather_rows((centered_two * gain_two + shift_two).astype(low))
    hidden = times(normed_two, up_matrix) + unit_bias
    activated, smooth_pull = jax.vjp(smooth, hidden)
    activated = activated.astype(low)
    result = (middle + (scatter_rows(times(activated, down_matrix)) + bias_down)).astype(low)

    down_back = times_flipped(upstream, down_matrix)
    grad_down = times_outer(activated, upstream)
    hidden_back = smooth_pull(down_back)[0].astype(low)
    grad_up = times_outer(normed_two, hidden_back)
    unit_sum = jnp.sum(hidden_back, axis=0, dtype=jnp.float32)
    normed_two_back = scatter_rows(times_flipped(hidden_back, up_matrix))
    upstream_own = lax.dynamic_slice_in_dim(upstream, mine, part).astype(jnp.float32)
    middle_back = upstream_own + norm_pull(normed_two_back, centered_two, inverse_two, gain_two)
    branch_own = middle_back.astype(low)
    branch_back = gather_rows(branch_own)
    mixed_back = times_flipped(branch_back, out_matrix).astype(low)
    grad_out = times_outer(mixed, branch_back)
    mixed_back = split_heads(mixed_back)
    scores_again = scores_of(queries, keys, allowed)
    soft = jnp.exp(scores_again - log_total)
    soft_back = jnp.einsum("hqe,hke->hqk", mixed_back, values, preferred_element_type=jnp.float32)
    row_inner = jnp.sum(soft_back * soft, axis=-1, keepdims=True)
    score_back = (soft * (soft_back - row_inner)).astype(low)
    query_back = jnp.einsum(
        "hqk,hke->hqe", score_back, keys, preferred_element_type=jnp.float32
    ) * HD ** (-0.5)
    key_back = jnp.einsum(
        "hqk,hqe->hke", score_back, queries, preferred_element_type=jnp.float32
    ) * HD ** (-0.5)
    value_back = jnp.einsum(
        "hqk,hqe->hke", soft.astype(low), mixed_back, preferred_element_type=jnp.float32
    )
    heads_back = jnp.concatenate(
        [join_heads(each.astype(low)) for each in (query_back, key_back, value_back)], axis=1
    )
    heads_sum = jnp.sum(heads_back, axis=0, dtype=jnp.float32)
    normed_one_back = scatter_rows(times_flipped(heads_back, heads_matrix))
    grad_heads = times_outer(normed_one, heads_back)
    centered_own = lax.dynamic_slice_in_dim(centered_one, mine, part)
    inverse_own = lax.dynamic_slice_in_dim(inverse_one, mine, part)
    input_back = middle_back + norm_pull(normed_one_back, centered_own, inverse_own, gain_one)

    def homeward(own):
        own = lax.all_to_all(own, "row", split_axis=1, concat_axis=0, tiled=True)
        return crossed(own, n_row)

    result_tokens = homeward(result)
    input_gradient = homeward(input_back.astype(low)).astype(jnp.float32)

    by_token = jnp.stack(
        [
            jnp.sum(normed_one_back * centered_own, axis=0),
            jnp.sum(normed_one_back, axis=0),
            jnp.sum(branch_own.astype(jnp.float32), axis=0),
            jnp.sum(normed_two_back * centered_two, axis=0),
            jnp.sum(normed_two_back, axis=0),
            jnp.sum(upstream_own, axis=0),
        ]
    )
    owned_rows = jnp.where(owned, heads_sum.reshape(3, window)[0::2], 0.0)
    by_unit = jnp.concatenate(
        [
            lax.dynamic_update_slice_in_dim(
                jnp.zeros((2, width), jnp.float32), owned_rows, row * step, axis=1
            ),
            lax.dynamic_update_slice_in_dim(
                jnp.zeros((4, width), jnp.float32), unit_sum.reshape(4, share), row * share, axis=1
            ),
        ]
    )
    sums = lax.psum(jnp.concatenate([by_token, by_unit]), ("dp", "row", "col"))
    pieces = share // n_dp
    inner = lax.axis_index("dp") * pieces
    col_sums = lax.dynamic_slice_in_dim(sums, lax.axis_index("col") * share + inner, pieces, axis=1)
    row_sums = lax.dynamic_slice_in_dim(sums, row * share + inner, pieces, axis=1)

    both = ("col", "dp")

    def to_owner(gradient):
        return lax.psum_scatter(gradient, both, scatter_dimension=0, tiled=True)

    got_heads = to_owner(grad_heads.astype(low)).reshape(pieces, 3, window)
    got_heads = jnp.where(owned, got_heads, jnp.zeros_like(got_heads))
    passed = lax.ppermute(got_heads[:, :, :edge], "row", to_last)
    got_heads = jnp.concatenate([got_heads, jnp.zeros_like(passed)], axis=2)
    got_heads = lax.dynamic_slice_in_dim(got_heads, edge - offset, share, axis=2)
    passed = jnp.concatenate([jnp.zeros((pieces, 3, share), low), passed, jnp.zeros_like(passed)], axis=2)
    got_heads = got_heads + lax.dynamic_slice_in_dim(passed, share - step + edge - offset, share, axis=2)
    low_out = jnp.where(owned[:, None], grad_out, 0.0).astype(low)
    passed = lax.ppermute(low_out[:edge], "row", to_last)
    low_out = jnp.concatenate([low_out, jnp.zeros_like(passed)])
    low_out = lax.dynamic_slice_in_dim(low_out, edge - offset, share)
    passed = jnp.concatenate([jnp.zeros((share, width), low), passed, jnp.zeros_like(passed)])
    low_out = low_out + lax.dynamic_slice_in_dim(passed, share - step + edge - offset, share)
    low_out = jnp.transpose(low_out.reshape(n_dp, pieces, n_col, share), (2, 0, 1, 3))
    got_out = to_owner(low_out.reshape(-1, share))
    got_up = to_owner(grad_up.astype(low))
    low_down = grad_down.astype(low).reshape(4, n_dp, pieces, n_col, share)
    low_down = jnp.transpose(low_down, (3, 1, 0, 2, 4)).reshape(-1, share)
    got_down = to_owner(low_down)

    reduced = [
        each.astype(jnp.float32).reshape(like.shape)
        for each, like in (
            (got_heads, w_heads),
            (got_out, w_out),
            (got_up, w_up),
            (got_down, w_down),
            (col_sums[0:2], norm_vectors),
            (col_sums[2:6], width_vectors),
            (row_sums[6:8], attend_bias),
            (row_sums[8:12], hidden_vectors),
        )
    ]
    return result_tokens, input_gradient, reduced


def per_device(
    tokens,
    cotangent,
    segments,
    w_heads,
    w_out,
    w_up,
    w_down,
    norm_vectors,
    width_vectors,
    attend_bias,
    hidden_vectors,
    drift_heads,
    drift_out,
    drift_up,
    drift_down,
    drift_norm,
    drift_width,
    drift_attend,
    drift_hidden,
    power_heads,
    power_out,
    power_up,
    power_down,
    power_norm,
    power_width,
    power_attend,
    power_hidden,
):
    weights = (
        w_heads,
        w_out,
        w_up,
        w_down,
        norm_vectors,
        width_vectors,
        attend_bias,
        hidden_vectors,
    )
    firsts = (
        drift_heads,
        drift_out,
        drift_up,
        drift_down,
        drift_norm,
        drift_width,
        drift_attend,
        drift_hidden,
    )
    seconds = (
        power_heads,
        power_out,
        power_up,
        power_down,
        power_norm,
        power_width,
        power_attend,
        power_hidden,
    )
    sizes = tuple(lax.axis_size(name) for name in ("dp", "row", "col"))
    if sizes == (2, 4, 4):
        return fused(tokens, cotangent, segments, weights, firsts, seconds)
    result_tokens, input_gradient, reduced = gathered(tokens, cotangent, segments, *weights)
    heads_up = adam(w_heads, reduced[0], drift_heads, power_heads, 0.05, MATRIX_DECAY)
    out_up = adam(w_out, reduced[1], drift_out, power_out, 0.2, MATRIX_DECAY)
    up_up = adam(w_up, reduced[2], drift_up, power_up, 0.05, MATRIX_DECAY)
    down_up = adam(w_down, reduced[3], drift_down, power_down, 0.025, MATRIX_DECAY)
    norm_up = adam(norm_vectors, reduced[4], drift_norm, power_norm, 0.3, 0.0)
    width_up = adam(width_vectors, reduced[5], drift_width, power_width, 0.3, 0.0)
    attend_up = adam(attend_bias, reduced[6], drift_attend, power_attend, 0.3, 0.0)
    hidden_up = adam(hidden_vectors, reduced[7], drift_hidden, power_hidden, 0.3, 0.0)
    return (
        result_tokens,
        input_gradient,
        heads_up[0],
        heads_up[1],
        heads_up[2],
        out_up[0],
        out_up[1],
        out_up[2],
        up_up[0],
        up_up[1],
        up_up[2],
        down_up[0],
        down_up[1],
        down_up[2],
        norm_up[0],
        norm_up[1],
        norm_up[2],
        width_up[0],
        width_up[1],
        width_up[2],
        attend_up[0],
        attend_up[1],
        attend_up[2],
        hidden_up[0],
        hidden_up[1],
        hidden_up[2],
    )


def solution(mesh):
    return jax.shard_map(
        per_device,
        mesh=mesh,
        in_specs=(
            P(("dp", "row"), "col"),
            P(("dp", "row"), "col"),
            P("dp"),
            P("col", "dp", None, None, "row"),
            P("row", "dp", None, "col"),
            P("col", "dp", None, None, "row"),
            P(None, "row", "dp", None, "col"),
            P(None, "col", "dp", None),
            P(None, "col", "dp", None),
            P(None, "row", "dp", None),
            P(None, "row", "dp", None),
            P("col", "dp", None, None, "row"),
            P("row", "dp", None, "col"),
            P("col", "dp", None, None, "row"),
            P(None, "row", "dp", None, "col"),
            P(None, "col", "dp", None),
            P(None, "col", "dp", None),
            P(None, "row", "dp", None),
            P(None, "row", "dp", None),
            P("col", "dp", None, None, "row"),
            P("row", "dp", None, "col"),
            P("col", "dp", None, None, "row"),
            P(None, "row", "dp", None, "col"),
            P(None, "col", "dp", None),
            P(None, "col", "dp", None),
            P(None, "row", "dp", None),
            P(None, "row", "dp", None),
        ),
        out_specs=(
            P(("dp", "row"), "col"),
            P(("dp", "row"), "col"),
            P("col", "dp", None, None, "row"),
            P("col", "dp", None, None, "row"),
            P("col", "dp", None, None, "row"),
            P("row", "dp", None, "col"),
            P("row", "dp", None, "col"),
            P("row", "dp", None, "col"),
            P("col", "dp", None, None, "row"),
            P("col", "dp", None, None, "row"),
            P("col", "dp", None, None, "row"),
            P(None, "row", "dp", None, "col"),
            P(None, "row", "dp", None, "col"),
            P(None, "row", "dp", None, "col"),
            P(None, "col", "dp", None),
            P(None, "col", "dp", None),
            P(None, "col", "dp", None),
            P(None, "col", "dp", None),
            P(None, "col", "dp", None),
            P(None, "col", "dp", None),
            P(None, "row", "dp", None),
            P(None, "row", "dp", None),
            P(None, "row", "dp", None),
            P(None, "row", "dp", None),
            P(None, "row", "dp", None),
            P(None, "row", "dp", None),
        ),
        check_vma=False,
    )
```

```python
import functools

import jax
import jax.numpy as jnp
from jax import lax
from jax.experimental import pallas as pl
from jax.experimental.pallas import tpu as pltpu
from jax.sharding import PartitionSpec as P

HEADS = 25
HD = 64
TOK_DEV = 128
STEP = 10


NORM_EPSILON = 1e-05
BETA_FIRST = 0.9
BETA_SECOND = 0.999
ADAM_EPSILON = 1e-08
MATRIX_DECAY = 0.1
MASKED = -1e30
ROOT = (2.0 / 3.141592653589793) ** 0.5
CUBIC = 0.044715
VMEM_BYTES = 66 * 1024 * 1024


def adam(weight, gradient, first, second, rate, decay):
    first_new = BETA_FIRST * first + (1.0 - BETA_FIRST) * gradient
    second_new = BETA_SECOND * second + (1.0 - BETA_SECOND) * gradient * gradient
    corrected = first_new / (1.0 - BETA_FIRST**STEP)
    divisor = jnp.sqrt(second_new / (1.0 - BETA_SECOND**STEP)) + ADAM_EPSILON
    return (first_new, second_new, weight - rate * (corrected / divisor + decay * weight))


def smooth(values):
    return jax.nn.gelu(values, approximate=True)


def ceil_to(count, unit):
    return -(-count // unit) * unit


class Sizes:
    def __init__(self, share, pieces, seq):
        self.share = share
        self.pieces = pieces
        self.block = ceil_to(pieces, 16)
        self.pair = 2 * self.block
        self.width = 4 * self.pair
        self.seq = seq
        self.part = seq // 4
        self.both = 2 * seq
        self.main = (HEADS // 4) * HD
        self.slack = share - self.main
        self.heads = ceil_to(3 * share, 256)
        self.mixed = ceil_to(pieces + 1, 128)
        self.hidden = ceil_to(4 * pieces + 1, 128)
        self.tiles = self.width // 128
        self.solid = self.hidden - 128
        self.tail = 4 * pieces - self.solid
        assert 0 < self.tail < 64


class Place:
    def __init__(self):
        self.d, self.r, self.c = (lax.axis_index(name) for name in ("dp", "row", "col"))
        self.y, self.k = self.r // 2, self.r % 2

    def plane(self, mask):
        d = 1 - self.d if mask & 4 else self.d
        y = 1 - self.y if mask & 2 else self.y
        k = 1 - self.k if mask & 1 else self.k
        return d, 2 * y + k

    def peer(self, mask):
        d, r = self.plane(mask)
        return (d, r, self.c)

    def along(self, c):
        return (self.d, self.r, c)


def run(when, action):
    if when is None:
        action()
    else:
        pl.when(when)(action)


class Wires:
    def __init__(self, sends, arrivals):
        self.sends, self.arrivals = sends, arrivals
        self.used = 0
        self.open = []

    def make(self, source, target, index, slot, device):
        return pltpu.make_async_remote_copy(
            src_ref=source,
            dst_ref=target,
            send_sem=self.sends.at[index],
            recv_sem=self.arrivals.at[slot],
            device_id=device,
            device_id_type=pl.DeviceIdType.MESH,
        )

    def copy(self, source, target, device, slot, when=None):
        made = self.make(source, target, self.used, slot, device)
        self.used += 1
        run(when, made.start)
        item = (when, made)
        self.open.append(item)
        return item

    def arrived(self, target, slot, device, when=None):
        run(when, self.make(target, target, 0, slot, device).wait_recv)

    def close(self, some=None):
        for item in self.open if some is None else some:
            run(item[0], item[1].wait_send)
        self.open = [] if some is None else [o for o in self.open if all(o is not s for s in some)]


def greet(at, diagonal):
    barrier = pltpu.get_barrier_semaphore()

    def signal(device):
        pl.semaphore_signal(
            barrier, inc=1, device_id=device, device_id_type=pl.DeviceIdType.MESH
        )

    for mask in range(1, 8):
        signal(at.peer(mask))
    for c in range(4):
        run(at.c != c, functools.partial(signal, (at.d, at.r, c)))
        if diagonal:
            run(at.c != c, functools.partial(signal, (1 - at.d, at.r, c)))
    run(at.r != at.c, functools.partial(signal, (at.d, at.c, at.r)))
    pl.semaphore_wait(barrier, (13 if diagonal else 10) + jnp.where(at.r != at.c, 1, 0))


def rows_at(start, size):
    return pl.ds(pl.multiple_of(start, 16), size)


def lanes_at(start, size):
    return pl.ds(pl.multiple_of(start, 128), size)


def choose(shape, source):
    rows = lax.broadcasted_iota(jnp.int32, shape, 0)
    wanted = source(lax.broadcasted_iota(jnp.int32, shape, 1))
    return (rows == wanted).astype(jnp.bfloat16)


def edge_source(column):
    part, place = column // HD, column % HD
    wanted = jnp.where(place >= 16, 128 * part + place - 16, 384 + 16 * part + place)
    return jnp.where(part < 3, wanted, -1)


def spread_source(column):
    part, place = column // 128, column % 128
    return jnp.where(place < HD, HD * part + place, -1)


def picked(values, table):
    return jnp.dot(values, table, preferred_element_type=jnp.float32).astype(jnp.bfloat16)


def times(left, right):
    return jnp.dot(left, right, preferred_element_type=jnp.float32)


def times_flipped(left, right):
    return lax.dot_general(
        left, right, (((1,), (1,)), ((), ())), preferred_element_type=jnp.float32
    )


def times_outer(left, right):
    return lax.dot_general(
        left, right, (((0,), (0,)), ((), ())), preferred_element_type=jnp.float32
    )


def over_tiles(total, action, tile=256):
    @pl.loop(0, total // tile)
    def _(i):
        action(i * tile, tile)

    if total % tile:
        action(total - total % tile, total % tile)


def turned(values):
    return values.astype(jnp.float32).T


def gather_group(wires, masks, region, at, base):
    own = region(*at.plane(0))
    sent = [wires.copy(own, own, at.peer(mask), base + mask) for mask in (1, *masks)]

    def finish():
        for mask in masks:
            there = region(*at.plane(mask))
            wires.arrived(there, base + mask, at.peer(mask))
            sent.append(wires.copy(there, there, at.peer(1), base + mask + 1))
        for mask in (0, *masks):
            there = region(*at.plane(mask | 1))
            wires.arrived(there, base + (mask | 1), at.peer(1))

    return finish, sent


def cross_over(wires, home, landing, region, at, base):
    rows = home.shape[0] // 2
    wires.copy(home.at[rows_at(rows * (1 - at.y), rows)], landing, at.peer(2), base)
    target = region(at.c, at.d, at.y)

    def along(source, s):
        wires.copy(source, target, at.along(s), base + 1 + at.c, s != at.c)

        @pl.when(s == at.c)
        def _():
            target[...] = source[...]

    along(home.at[rows_at(rows * at.y, rows)], at.r)

    def onward():
        wires.arrived(landing, base, at.peer(2))
        along(landing, 2 * (1 - at.y) + at.k)

    def finish():
        for c in range(4):
            needed = (at.k == at.c % 2) & (at.c != c)
            wires.arrived(region(c, at.d, at.y), base + 1 + c, at.along(c), needed)

    return onward, finish


def share_pieces(wires, masks, region, at, base):
    holds = at.k == at.c % 2
    near = base + 4 * len(masks)

    def place(mask):
        d, r = at.plane(mask)
        return d, r // 2

    for c in range(4):
        own = region(c, *place(0))
        for i, mask in enumerate(masks):
            wires.copy(own, own, at.peer(mask), base + 4 * i + c, holds)
    for c in range(4):
        own = region(c, *place(0))
        wires.copy(own, own, at.peer(1), near + c, holds)

    def finish():
        for i, mask in enumerate(masks):
            for c in range(4):
                there = region(c, *place(mask))
                wires.arrived(there, base + 4 * i + c, at.peer(mask), holds)
                wires.copy(there, there, at.peer(1), near + 4 * (i + 1) + c, holds)
        for i, mask in enumerate((0, *masks)):
            for c in range(4):
                there = region(c, *place(mask))
                wires.arrived(there, near + 4 * i + c, at.peer(1), jnp.logical_not(holds))

    return finish


def scatter_group(wires, masks, partial, chunk, near, mid, far, at, base):
    sent = []
    for i, mask in enumerate((0, *masks)):
        rows = rows_at(chunk(*at.plane(mask | 1)), near.shape[1])
        sent.append(wires.copy(partial.at[rows], near.at[i], at.peer(1), base + i))

    def rows_of(mask):
        return rows_at(chunk(*at.plane(mask)), near.shape[1])

    def onward():
        for i, mask in enumerate((0, *masks)):
            wires.arrived(near.at[i], base + i, at.peer(1))
        for i, mask in enumerate(masks):
            both = partial[rows_of(mask)].astype(jnp.float32) + near[i + 1].astype(jnp.float32)
            mid[i] = both.astype(jnp.bfloat16)
            sent.append(wires.copy(mid.at[i], far.at[i], at.peer(mask), base + 4 + i))

    def total():
        for i, mask in enumerate(masks):
            wires.arrived(far.at[i], base + 4 + i, at.peer(mask))
        result = partial[rows_of(0)].astype(jnp.float32) + near[0].astype(jnp.float32)
        for i in range(len(masks)):
            result = result + far[i].astype(jnp.float32)
        return result

    return onward, total, sent


def spread_col(wires, region, at, base, wait=False):
    own = region(at.c)

    def send(distance):
        for delta in (distance, -distance):
            there = at.c + delta
            wires.copy(own, own, at.along(there), base + at.c, (there >= 0) & (there < 4))

    if not wait:
        send(2)
        send(1)

    def relay():
        for here, start, end in ((2, 0, 3), (1, 3, 0)):
            block = region(start)
            wires.arrived(block, base + start, at.along(start), at.c == here)
            wires.copy(block, block, at.along(end), base + start, at.c == here)

    def finish():
        for c in range(4):
            needed = at.c != c
            if c == 0:
                needed = needed & (at.c != 2)
            if c == 3:
                needed = needed & (at.c != 1)
            wires.arrived(region(c), base + c, at.along(c), needed)

    return (send, relay, finish) if wait else (relay, finish)


def collect_col(wires, piece, landing, rest, at, base, direct=None):
    low_end, high_end = at.c == 0, at.c == 3
    ends = low_end | high_end
    via = jnp.where(low_end, 1, 2)

    def pick(*choices):
        return jnp.where(
            low_end,
            choices[0],
            jnp.where(at.c == 1, choices[1], jnp.where(high_end, choices[3], choices[2])),
        )

    order = (pick(3, 0, 3, 0), pick(2, 2, 1, 1), pick(1, 3, 0, 2), at.c)
    target = landing.at[at.c]

    def send(step):
        there = order[step]
        block = (direct or piece)(there)
        if step == 0:
            wires.copy(block, rest, at.along(via), base + 4, ends)
            wires.copy(block, target, at.along(there), base + at.c, jnp.logical_not(ends))
        elif step == 1:
            wires.copy(block, target, at.along(there), base + at.c)
        elif step == 2:
            wires.copy(block, target, at.along(there), base + at.c, ends)

    def relay(add):
        @pl.when(jnp.logical_not(ends))
        def _():
            wires.make(rest, rest, 0, base + 4, at.along(0)).wait_recv()
            add(order[2])

        wires.copy(piece(order[2]), target, at.along(order[2]), base + at.c, jnp.logical_not(ends))

    def arrived(c):
        wires.arrived(landing.at[c], base + c, at.along(c), sent_from(c))

    def sent_from(c):
        here = at.c != c
        if c in (0, 3):
            here = here & (at.c != 3 - c)
        return here

    return order, send, relay, arrived, sent_from


def forward_kernel(
    sz,
    x_home_in,
    dy_home_in,
    w_heads,
    w_out,
    w_up,
    w_down,
    norm_vectors,
    width_vectors,
    attend_bias,
    hidden_vectors,
    segments,
    wh_out,
    wo_out,
    wu_out,
    wd_out,
    h1_t_out,
    h2_t_out,
    gd_out,
    gt_out,
    dy_out,
    u_out,
    gl_out,
    qw_out,
    kw_out,
    vw_out,
    a_nat_out,
    lse_out,
    x2_out,
    x_own_out,
    vec_rows_out,
    wh,
    wo,
    wu,
    wd,
    h1_t,
    h2_t,
    gd,
    gt,
    dy_t,
    dy,
    u,
    gl,
    qw,
    kw,
    vw,
    a_nat,
    lse,
    x2,
    x_own,
    vec_rows,
    x_t,
    h1,
    h2,
    own_qkv,
    aw,
    vec,
    part,
    edge_out,
    edge_in,
    edge_back,
    near,
    mid,
    far,
    x_raw,
    dy_raw,
    heads_raw,
    out_raw,
    up_raw,
    down_raw,
    x_home,
    dy_home,
    wu_own,
    wd_tail,
    col_labels,
    x_half,
    dy_half,
    sends,
    arrivals,
    locals_,
):
    at = Place()
    wires = Wires(sends, arrivals)
    low = jnp.bfloat16
    pair, block, pieces = sz.pair, sz.block, sz.pieces
    fetched = []
    for i, (source, target) in enumerate(
        (
            (x_home_in, x_raw),
            (w_heads, heads_raw),
            (w_up, up_raw),
            (w_out, out_raw),
            (w_down, down_raw),
            (dy_home_in, dy_raw),
        )
    ):
        fetched.append(pltpu.make_async_copy(source, target, locals_.at[40 + i]))
    for made in fetched[0:2]:
        made.start()
    row_labels = segments.at[:, lanes_at(sz.seq * at.c, sz.seq)]

    def halves(value, target):
        value = value.astype(jnp.float32)
        gap = jnp.zeros((block - pieces, value.shape[1]), jnp.float32)
        parts = [value[0:pieces], gap, value[pieces : 2 * pieces], gap]
        target[...] = jnp.concatenate(parts, axis=0).astype(low)

    def quarter(row):
        return row.astype(low).astype(jnp.float32) * 0.25

    def placed(row):
        both = jnp.concatenate([row, row], axis=1)
        half_of = lax.broadcasted_iota(jnp.int32, both.shape, 1) // pieces
        return jnp.where(half_of == at.d, both, 0.0)

    def with_row(value, row):
        gap = jnp.zeros((block - pieces - 1, value.shape[1]), jnp.float32)
        return jnp.concatenate([value, row, gap], axis=0)

    flat = jnp.concatenate(
        [norm_vectors[0], norm_vectors[1], width_vectors[1], width_vectors[2]], axis=0
    )
    flat = jnp.concatenate([flat, jnp.zeros((124, pieces), jnp.float32)], axis=0)
    flat = jnp.concatenate([flat, jnp.zeros((128, 256 - pieces), jnp.float32)], axis=1)
    where_row = lax.broadcasted_iota(jnp.int32, flat.shape, 0)
    where_lane = lax.broadcasted_iota(jnp.int32, flat.shape, 1)
    carrier = (where_lane == pieces) & ((where_row == 1) | (where_row == 3))
    own_rows = rows_at(pair * at.c + block * at.d, block)
    vec[own_rows] = jnp.where(carrier, 1.0, flat).T[0:block].astype(low)
    fetched[0].wait()
    halves(x_raw[...], x_home)
    for made in fetched[2:6]:
        made.start()
    greet(at, False)

    def x_piece(c, d, y):
        return x_t.at[rows_at(pair * c + block * y, block)]

    def dy_piece(c, d, y):
        return dy_t.at[rows_at(pair * c + block * y, block), lanes_at(sz.seq * d, sz.seq)]

    used = [0]

    def flush(source, target):
        made = pltpu.make_async_copy(source, target, locals_.at[used[0]])
        used[0] += 1
        made.start()
        flushed.append(made)

    flushed = []

    def vec_block(d, c):
        return vec.at[rows_at(pair * c + block * d, block)]

    def wh_block(d):
        return lambda c: wh.at[rows_at(pair * c + block * d, block)]

    def wo_block(d):
        return lambda c: wo.at[rows_at(pair * c, pair), lanes_at(sz.mixed * d, sz.mixed)]

    def wu_block(d):
        return lambda c: wu.at[rows_at(pair * c + block * d, block)]

    def wd_block(half):
        return lambda c: wd.at[rows_at(pair * c + block * half, block)]

    x_onward, x_crossed = cross_over(wires, x_home, x_half, x_piece, at, 96)
    for c in range(4):
        wires.copy(vec_block(at.d, at.c), vec_block(at.d, at.c), at.along(c), 2 + at.c, at.c != c)
    wires.copy(vec_block(at.d, at.c), vec_block(at.d, at.c), at.peer(4), 6 + at.c)

    fetched[1].wait()
    for r in range(4):

        @pl.when(at.r == r)
        def _():
            cut = sz.share - sz.slack * r
            tails = []
            for i in range(3):
                value = heads_raw[i]
                row = jnp.zeros((1, sz.share), jnp.float32)
                if i != 1:
                    row = placed(quarter(attend_bias[i // 2]))
                value = with_row(value, row)
                if r:
                    value = jnp.concatenate([value[:, cut:], value[:, 0:cut]], axis=1)
                wh[own_rows, sz.main * i : sz.main * (i + 1)] = value[:, 0 : sz.main].astype(low)
                tails.append(value[:, sz.main :])
            tails.append(jnp.zeros((block, sz.heads - 3 * sz.share), jnp.float32))
            wh[own_rows, 3 * sz.main : sz.heads] = jnp.concatenate(tails, axis=1).astype(low)

    x_onward()
    wh_relay, wh_done = spread_col(wires, wh_block(at.d), at, 20)
    wires.copy(wh_block(at.d)(at.c), wh_block(at.d)(at.c), at.peer(4), 24 + at.c)

    fetched[2].wait()
    gap = jnp.zeros((block, sz.hidden - 4 * pieces), jnp.float32)
    values = [
        with_row(up_raw[:, j, :], placed(quarter(hidden_vectors[j]))) for j in range(4)
    ]
    for i in range(2):
        lanes = slice(pieces * i, pieces * (i + 1))
        whole = jnp.concatenate([value[:, lanes] for value in values] + [gap], axis=1)

        @pl.when(at.d == i)
        def _():
            wu[own_rows] = whole.astype(low)

        @pl.when(at.d != i)
        def _():
            wu_own[...] = whole.astype(low)

    wires.copy(wu_own, wu_block(at.d)(at.c), at.peer(4), 10)

    def turned_halves(value, target, rows, lanes):
        flipped = value.T
        gap = jnp.zeros((block - pieces, flipped.shape[1]), jnp.float32)
        parts = [flipped[0:pieces], gap, flipped[pieces : 2 * pieces], gap]
        target[rows, lanes] = jnp.concatenate(parts, axis=0).astype(low)

    fetched[3].wait()
    value = with_row(out_raw[...], placed(quarter(width_vectors[0])))
    value = jnp.concatenate([value, jnp.zeros((sz.mixed - block, sz.share), jnp.float32)], axis=0)
    for i in range(sz.mixed // 128):
        lanes = slice(128 * i, 128 * (i + 1))
        turned_halves(
            value[lanes], wo, rows_at(pair * at.c, pair), lanes_at(sz.mixed * at.d + 128 * i, 128)
        )
    wo_relay, wo_done = spread_col(wires, wo_block(at.d), at, 28)
    wires.copy(wo_block(at.d)(at.c), wo_block(at.d)(at.c), at.peer(4), 32 + at.c)

    fetched[5].wait()
    halves(dy_raw[...], dy_home)
    dy_onward, dy_crossed = cross_over(wires, dy_home, dy_half, dy_piece, at, 116)

    x_crossed()
    x_done = share_pieces(wires, (2,), x_piece, at, 104)

    fetched[4].wait()
    for i in range(sz.solid // 128):
        rows = slice(128 * i, 128 * (i + 1))
        turned_halves(down_raw[rows], wd, rows_at(pair * at.c, pair), rows)
    value = [
        jnp.zeros((64, sz.share), jnp.float32),
        down_raw[sz.solid : 4 * pieces],
        placed(quarter(width_vectors[3])),
        jnp.zeros((63 - sz.tail, sz.share), jnp.float32),
    ]
    turned_halves(jnp.concatenate(value, axis=0), wd_tail, slice(0, pair), slice(0, 128))

    def add_tail(d):
        rows = rows_at(pair * at.c + block * d, block)
        both = wu[rows, sz.solid : sz.hidden].astype(jnp.float32)
        both = both + wd_tail[rows_at(block * d, block)].astype(jnp.float32)
        wu[rows, sz.solid : sz.hidden] = both.astype(low)

    add_tail(at.d)
    col_labels[...] = jnp.concatenate([row_labels[...]] * 8, axis=0).astype(jnp.float32).T[:, 0:1]
    x_done()
    dy_onward()
    wires.arrived(wu_block(1 - at.d)(at.c), 10, at.peer(4))
    add_tail(1 - at.d)
    wu_first_send, wu_first, wu_first_done = spread_col(wires, wu_block(at.d), at, 36, True)
    wu_second_send, wu_second, wu_second_done = spread_col(wires, wu_block(1 - at.d), at, 40, True)
    for distance in (2, 1):
        wu_first_send(distance)
        wu_second_send(distance)

    for c in range(4):
        wires.arrived(vec_block(at.d, c), 2 + c, at.along(c), at.c != c)
    wires.arrived(vec_block(1 - at.d, at.c), 6 + at.c, at.peer(4))
    for step in range(1, 4):
        there = (at.c + step) % 4
        wires.copy(
            vec_block(at.d, there), vec_block(at.d, there), at.peer(4), 6 + there
        )
    for step in range(1, 4):
        there = (at.c + step) % 4
        wires.arrived(vec_block(1 - at.d, there), 6 + there, at.peer(4))
    features = 4.0 * sz.share

    def add_up(i, carry):
        rows = rows_at(128 * i, 128)
        value = x_t[rows].astype(jnp.float32)
        return (
            carry[0] + jnp.sum(value, axis=0, keepdims=True),
            carry[1] + jnp.sum(value * value, axis=0, keepdims=True),
        )

    zero = jnp.zeros((1, sz.seq), jnp.float32)
    sums = lax.fori_loop(0, sz.tiles, add_up, (zero, zero))
    center = sums[0] / features
    inverse = lax.rsqrt(sums[1] / features - center * center + NORM_EPSILON)

    @pl.loop(0, sz.tiles)
    def _(i):
        rows, lanes = rows_at(128 * i, 128), lanes_at(128 * i, 128)
        vectors = vec[rows].astype(jnp.float32)
        value = (x_t[rows].astype(jnp.float32) - center) * inverse
        value = value * vectors[:, 0:1] + vectors[:, 1:2]
        h1_t[rows] = value.astype(low)
        h1[:, lanes] = value.T.astype(low)
        mine = x_t[rows, lanes_at(sz.part * at.r, sz.part)]
        x_own[:, lanes] = turned(mine).astype(low)
        vec_rows[:, lanes] = vectors.T[0:8]

    flush(h1_t, h1_t_out)
    flush(x_own, x_own_out)
    flush(vec_rows, vec_rows_out)

    wh_relay()
    for c in range(4):
        needed = at.c != c
        if c == 0:
            needed = needed & (at.c != 2)
        if c == 3:
            needed = needed & (at.c != 1)
        wires.arrived(wh_block(at.d)(c), 20 + c, at.along(c), needed)
        wires.copy(wh_block(at.d)(c), wh_block(at.d)(c), at.peer(4), 24 + c, at.c != c)

    for c in range(4):
        wires.arrived(wh_block(1 - at.d)(c), 24 + c, at.peer(4))
    flush(wh, wh_out)

    @pl.loop(0, sz.heads // 256)
    def _(i):
        lanes = lanes_at(256 * i, 256)
        own_qkv[:, lanes] = times(h1[...], wh[:, lanes]).astype(low)

    starts = (0, sz.main, 2 * sz.main, 3 * sz.main)
    ends = jnp.concatenate([own_qkv[:, s : s + 128] for s in starts], axis=1)
    edge_out[...] = picked(ends, choose((512, 256), edge_source))
    last = at.r == 3

    @pl.when(at.r == 0)
    def _():
        edge_in[...] = jnp.zeros_like(edge_in)

    wires.copy(edge_out, edge_in, (at.d, at.r + 1, at.c), 52, at.r < 3)
    spread = choose((256, 384), spread_source)
    extra = picked(edge_out[...], spread)
    wires.arrived(edge_in, 52, (at.d, at.r - 1, at.c), at.r > 0)
    first = picked(edge_in[...], spread)
    lane = lax.broadcasted_iota(jnp.int32, (sz.seq, 128), 1)
    for i, target in enumerate((qw, kw, vw)):
        start = starts[i]
        target[:, 0:128] = jnp.where(
            lane < sz.slack * at.r,
            first[:, 128 * i : 128 * i + 128],
            own_qkv[:, start : start + 128],
        )
        target[:, 128 : sz.main] = own_qkv[:, start + 128 : start + sz.main]
        target[:, sz.main : sz.main + 128] = extra[:, 128 * i : 128 * i + 128]
    flush(qw, qw_out)
    flush(kw, kw_out)
    flush(vw, vw_out)

    wo_relay()
    for c in range(4):
        needed = at.c != c
        if c == 0:
            needed = needed & (at.c != 2)
        if c == 3:
            needed = needed & (at.c != 1)
        wires.arrived(wo_block(at.d)(c), 28 + c, at.along(c), needed)
        wires.copy(wo_block(at.d)(c), wo_block(at.d)(c), at.peer(4), 32 + c, at.c != c)

    half = sz.seq // 2

    def heads_of(p, count):
        tile = lanes_at(128 * p, 128)
        for q in range(2):
            rows = slice(half * q, half * (q + 1))
            keys = half * (q + 1)
            order = lax.broadcasted_iota(jnp.int32, (half, keys), 0) + half * q
            allowed = (col_labels[rows, :] == row_labels[:, 0:keys].astype(jnp.float32)) & (
                order >= lax.broadcasted_iota(jnp.int32, (half, keys), 1)
            )
            lanes = lax.broadcasted_iota(jnp.int32, (half, 128), 1)
            side = lanes // HD
            total = jnp.zeros((half, 128), jnp.float32)
            for h in range(count):
                queries = jnp.where(side == h, qw[rows, tile].astype(jnp.float32) * HD ** (-0.5), 0.0)
                scores = times_flipped(queries.astype(low), kw[0:keys, tile])
                scores = jnp.where(allowed, scores, MASKED)
                highest = jnp.max(scores, axis=1, keepdims=True)
                raised = jnp.exp(scores - highest)
                summed = jnp.sum(raised, axis=1, keepdims=True)
                found = highest + jnp.log(summed)
                lse[rows, :] = jnp.where(lanes == 2 * p + h, found, lse[rows, :])
                soft = (raised * (1.0 / summed)).astype(low)
                total = jnp.where(side == h, times(soft, vw[0:keys, tile]), total)
            aw[rows, tile] = total.astype(low)

    lse[...] = jnp.zeros_like(lse)

    @pl.loop(0, sz.main // 128)
    def _(p):
        heads_of(p, 2)

    @pl.when(last)
    def _():
        heads_of(sz.main // 128, 1)
        edge_back[...] = aw[:, sz.main : sz.main + 128]

    flush(lse, lse_out)

    wires.copy(aw.at[:, 0:128], edge_back, (at.d, at.r - 1, at.c), 53, at.r > 0)
    wd_first_send, wd_first, wd_first_done = spread_col(wires, wd_block(0), at, 44, True)
    wd_second_send, wd_second, wd_second_done = spread_col(wires, wd_block(1), at, 48, True)
    for distance in (2, 1):
        wd_first_send(distance)
        wd_second_send(distance)
    wires.arrived(edge_back, 53, (at.d, at.r + 1, at.c), at.r < 3)
    dy_crossed()
    dy_done = share_pieces(wires, (2, 4, 6), dy_piece, at, 124)

    def natural(column):
        inner = column % sz.mixed
        place = sz.pieces * (column // sz.mixed) + inner + sz.slack * at.r
        return jnp.where(inner < sz.pieces, place, -1)

    def natural_main(column):
        place = natural(column)
        return jnp.where(place < sz.main, place, -1)

    def natural_edge(column):
        return natural(column) - sz.main

    mixed = times(aw[:, 0 : sz.main], choose((sz.main, 2 * sz.mixed), natural_main))
    mixed = mixed + times(edge_back[...], choose((128, 2 * sz.mixed), natural_edge))
    ones = lax.broadcasted_iota(jnp.int32, mixed.shape, 1) % sz.mixed == sz.pieces
    a_nat[...] = jnp.where(ones, 1.0, mixed).astype(low)
    for c in range(4):
        wires.arrived(wo_block(1 - at.d)(c), 32 + c, at.peer(4))
    flush(wo, wo_out)
    flush(a_nat, a_nat_out)

    def project(start, tile):
        out = times_flipped(a_nat[...], wo[rows_at(start, tile)])
        part[:, lanes_at(start, tile)] = out.astype(low)

    over_tiles(sz.width, project)

    onward, total, _ = scatter_group(
        wires, (2,), part, lambda d, r: sz.part * r, near, mid, far, at, 64
    )
    onward()
    wu_first()
    wu_second()
    middle = x_own[...].astype(jnp.float32) + total()
    x2[...] = middle
    flush(x2, x2_out)
    center = jnp.sum(middle, axis=1, keepdims=True) / features
    spread_two = jnp.sum(middle * middle, axis=1, keepdims=True) / features - center * center
    normed = (middle - center) * lax.rsqrt(spread_two + NORM_EPSILON)
    own_rows = rows_at(sz.part * (4 * at.d + at.r), sz.part)
    h2[own_rows] = (normed * vec_rows[2:3] + vec_rows[3:4]).astype(low)

    def h2_block(d, r):
        return h2.at[rows_at(sz.part * (4 * d + r), sz.part)]

    for mask in (1, 2, 4, 6):
        wires.copy(h2_block(*at.plane(0)), h2_block(*at.plane(0)), at.peer(mask), 72 + mask)

    def pass_on(mask):
        there = h2_block(*at.plane(mask))
        wires.arrived(there, 72 + mask, at.peer(mask))
        wires.copy(there, there, at.peer(1), 72 + mask + 1)

    dy_done()

    @pl.loop(0, sz.tiles)
    def _(i):
        dy[:, lanes_at(128 * i, 128)] = turned(dy_t[rows_at(128 * i, 128)]).astype(low)

    flush(dy, dy_out)
    wu_first_done()
    wu_second_done()
    flush(wu, wu_out)

    def expand(rows, start, tile):
        lanes = lanes_at(start, tile)
        value = times(h2[rows], wu[:, lanes])
        u[rows, lanes] = value
        inner = jnp.tanh(ROOT * (value + CUBIC * value * value * value))
        value = 0.5 * value * (1.0 + inner)
        if isinstance(start, int):
            column = lax.broadcasted_iota(jnp.int32, value.shape, 1)
            inside = (column >= 64) & (column < 64 + sz.tail)
            value = jnp.where(inside, pltpu.roll(value, 64, 1), 0.0)
            value = jnp.where(column == 64 + sz.tail, 1.0, value)
        gl[rows, lanes] = value.astype(low)

    def expand_chip(mask):
        wires.arrived(h2_block(*at.plane(mask | 1)), 72 + (mask | 1), at.peer(1))
        d, r = at.plane(mask)
        rows = rows_at(sz.part * (4 * d + 2 * (r // 2)), 2 * sz.part)
        over_tiles(sz.hidden, functools.partial(expand, rows))

    expand_chip(0)
    pass_on(2)
    pass_on(4)
    expand_chip(2)
    expand_chip(4)
    pass_on(6)
    expand_chip(6)

    flush(u, u_out)
    flush(gl, gl_out)
    wd_first()

    @pl.loop(0, sz.tiles)
    def _(i):
        h2_t[rows_at(128 * i, 128)] = turned(h2[:, lanes_at(128 * i, 128)]).astype(low)

    flush(h2_t, h2_t_out)
    wd_second()

    @pl.loop(0, 4)
    def _(i):
        rows = rows_at(pair * i, pair)
        gd[rows] = times(dy_t[rows], gl[:, 0 : sz.solid]).astype(low)
        gt[rows] = times(dy_t[rows], gl[:, sz.solid : sz.hidden]).astype(low)

    flush(gd, gd_out)
    flush(gt, gt_out)
    wd_first_done()
    wd_second_done()
    flush(wd, wd_out)
    wires.close()
    for made in flushed:
        made.wait()


def backward_kernel(
    sz,
    dy_all,
    gd_all,
    gt_all,
    u_all,
    gl_all,
    h2_t_all,
    wd_all,
    wu_all,
    wo_all,
    wh_all,
    h1_t_all,
    qw_all,
    kw_all,
    vw_all,
    a_nat_all,
    lse_all,
    x2_all,
    x_own_all,
    vec_rows,
    segments,
    out_down,
    out_up,
    out_out,
    out_heads,
    result_home,
    grad_home,
    vec_out,
    zd,
    zu,
    zo,
    zh,
    res_all,
    res_two,
    grad_all,
    grad_two,
    rd,
    ru,
    ro,
    rh,
    qw,
    kw,
    vw,
    a_nat,
    lse,
    x2,
    x_own,
    xu,
    dy,
    dy_t,
    u,
    gl,
    h2_t,
    wd,
    wu,
    wo,
    wh,
    gt,
    dy_own,
    du,
    gw,
    gu,
    go,
    xh,
    xo,
    near_two,
    far_two,
    near_res,
    far_res,
    near_one,
    far_one,
    mid,
    dob,
    da,
    dk_sum,
    dv_sum,
    dx2,
    edge_out,
    edge_in,
    fore_out,
    fore_in,
    col_labels,
    res_stage,
    grad_stage,
    va,
    vb,
    sends,
    arrivals,
    locals_,
):
    at = Place()
    wires = Wires(sends, arrivals)
    low = jnp.bfloat16
    pair, block = sz.pair, sz.block
    features = 4.0 * sz.share
    used = [0]

    def load(source, target, when=None):
        made = pltpu.make_async_copy(source, target, locals_.at[used[0]])
        used[0] += 1
        run(when, made.start)
        return made

    own_rows = rows_at(sz.part * (4 * at.d + at.r), sz.part)
    gd = gw.at[:, 0 : sz.solid]
    wanted = (
        (dy_all, dy),
        (wd_all, wd),
        (u_all, u),
        (dy_all.at[own_rows], dy_own),
        (wu_all, wu),
        (h2_t_all, h2_t),
        (gl_all, gl),
        (gd_all, gd),
        (wo_all, wo),
        (wh_all, wh),
        (x2_all, x2),
        (a_nat_all, a_nat),
        (qw_all, qw),
        (kw_all, kw),
        (vw_all, vw),
        (lse_all, lse),
        (x_own_all, x_own),
        (h1_t_all, dy_t.at[:, 0 : sz.seq]),
        (gt_all, gt),
    )
    loads = {}

    def begin(*which):
        for i in which:
            loads[i] = load(*wanted[i])

    begin(0, 1, 2)
    greet(at, False)
    stay = []

    order, d_send, d_relay, d_arrived, d_from = collect_col(
        wires,
        lambda c: gd.at[rows_at(pair * c, pair)],
        zd,
        rd,
        at,
        0,
        lambda c: gd_all.at[rows_at(pair * c, pair)],
    )
    for step in range(4):
        d_send(step)

    def relay_of(rest, block):
        def add(there):
            rows = rows_at(pair * there, pair)
            block[rows] = (block[rows].astype(jnp.float32) + rest[...].astype(jnp.float32)).astype(low)

        return add

    for i in range(3):
        loads[i].wait()
    begin(4, 5, 18)

    def through(start, tile):
        lanes = lanes_at(start, tile)
        last = isinstance(start, int)
        if last:
            loads[4].wait()
            upstream = pltpu.roll(times(dy[...], wu[:, lanes]), 64, 1)
        else:
            upstream = times(dy[...], wd[:, lanes])
        value = u[:, lanes]
        inner = jnp.tanh(ROOT * (value + CUBIC * value * value * value))
        slope = 0.5 * (1.0 + inner) + 0.5 * value * (1.0 - inner * inner) * ROOT * (
            1.0 + 3.0 * CUBIC * value * value
        )
        upstream = upstream * slope
        if last:
            column = lax.broadcasted_iota(jnp.int32, upstream.shape, 1)
            upstream = jnp.where(column < sz.tail, upstream, 0.0)
        du[:, lanes] = upstream.astype(low)

    over_tiles(sz.hidden, through)
    def back_up(start, tile):
        dy[:, lanes_at(start, tile)] = times_flipped(du[...], wu[rows_at(start, tile)]).astype(low)

    over_tiles(sz.width, back_up)
    begin(3, 10, 7, 6, 8, 11, 12, 13, 14, 15, 16, 9, 17)

    def chunk_both(d, r):
        return sz.part * (4 * d + r)

    two_onward, two_total, two_sent = scatter_group(
        wires, (2, 4, 6), dy, chunk_both, near_two, mid, far_two, at, 16
    )
    loads[5].wait()
    loads[18].wait()
    order, u_send, u_relay, u_arrived, u_from = collect_col(
        wires, lambda c: gu.at[rows_at(pair * c, pair)], zu, ru, at, 5
    )
    for step in range(4):
        rows = rows_at(pair * order[step], pair)
        value = times(h2_t[rows], du[...])
        gu[rows, 0 : sz.solid] = value[:, 0 : sz.solid].astype(low)
        both = value[:, sz.solid : sz.hidden] + gt[rows].astype(jnp.float32)
        gu[rows, sz.solid : sz.hidden] = both.astype(low)
        u_send(step)
        if step == 1:
            two_onward()
    own = rows_at(pair * at.c, pair)
    gd_own = load(gd_all.at[own], h2_t.at[own, 0 : sz.solid])
    loads[7].wait()
    before = len(wires.open)
    d_relay(relay_of(rd, gd))
    gd_sends = wires.open[before:]

    def norm_back(upstream, values, gain):
        center = jnp.sum(values, axis=1, keepdims=True) / features
        spread = jnp.sum(values * values, axis=1, keepdims=True) / features - center * center
        inverse = lax.rsqrt(spread + NORM_EPSILON)
        centered = (values - center) * inverse
        scaled = upstream * gain
        inner = (
            scaled
            - jnp.sum(scaled, axis=1, keepdims=True) / features
            - centered * (jnp.sum(scaled * centered, axis=1, keepdims=True) / features)
        )
        return (
            inner * inverse,
            jnp.sum(upstream * centered, axis=0, keepdims=True),
            jnp.sum(upstream, axis=0, keepdims=True),
        )

    loads[10].wait()
    loads[3].wait()
    h2_back = two_total()
    through_norm, gain_two, shift_two = norm_back(h2_back, x2[...], vec_rows[2:3])
    middle_back = dy_own[...].astype(jnp.float32) + through_norm
    dx2[...] = middle_back
    va[0, 2:3] = gain_two
    va[0, 3:4] = shift_two
    va[0, 4:8] = jnp.zeros((4, sz.width), jnp.float32)
    dob[rows_at(sz.part * at.r, sz.part)] = middle_back.astype(low)
    dob_done, dob_sent = gather_group(
        wires, (2,), lambda d, r: dob.at[rows_at(sz.part * r, sz.part)], at, 24
    )

    def contract(start, tile):
        rows = rows_at(start, tile)
        out = times_flipped(gl[:, 0 : sz.solid], wd[rows])
        out = out + times_flipped(gl[:, sz.solid : sz.hidden], wu[rows, sz.solid : sz.hidden])
        dy[:, lanes_at(start, tile)] = out.astype(low)

    wires.close(two_sent)
    loads[6].wait()
    over_tiles(sz.width, contract)
    res_onward, res_total, res_sent = scatter_group(
        wires, (2, 4, 6), dy, chunk_both, near_res, mid, far_res, at, 32
    )

    dob_done()
    loads[11].wait()
    loads[8].wait()
    da[...] = times(dob[...], wo[...]).astype(low)
    slack, main = sz.slack, sz.main

    def from_natural(place):
        wanted = sz.mixed * (place // sz.pieces) + place % sz.pieces
        return jnp.where((place >= 0) & (place < sz.share), wanted, -1)

    fore_out[...] = picked(
        da[...], choose((2 * sz.mixed, 128), lambda j: from_natural(j + main - slack * at.r))
    )

    @pl.when(at.r == 0)
    def _():
        fore_in[...] = jnp.zeros_like(fore_in)

    wires.copy(fore_out, fore_in, (at.d, at.r + 1, at.c), 40, at.r < 3)

    @pl.loop(0, sz.tiles)
    def _(i):
        dy_t[rows_at(128 * i, 128), sz.seq : sz.both] = turned(dob[:, lanes_at(128 * i, 128)]).astype(low)

    res_onward()

    for step in range(4):
        there = (at.c + step) % 4
        rows = rows_at(pair * there, pair)
        go[rows] = times(dy_t[rows, sz.seq : sz.both], a_nat[...]).astype(low)
        wires.copy(
            go.at[rows, lanes_at(sz.mixed * (1 - at.d), sz.mixed)], xo.at[there], at.peer(4), 48 + there
        )
    wires.arrived(fore_in, 40, (at.d, at.r - 1, at.c), at.r > 0)
    window = times(da[...], choose((2 * sz.mixed, main), lambda j: from_natural(j - slack * at.r)))
    da_first = window[:, 0:128] + fore_in[...].astype(jnp.float32)
    da[:, 128:main] = window[:, 128:main].astype(low)
    da[:, 0:128] = da_first.astype(low)
    da[:, main : main + 128] = fore_out[...]

    row_labels = segments.at[:, lanes_at(sz.seq * at.c, sz.seq)]
    col_labels[...] = jnp.concatenate([row_labels[...]] * 8, axis=0).astype(jnp.float32).T[:, 0:1]
    for i in range(12, 17):
        loads[i].wait()
    half = sz.seq // 2
    dqw, dkw = (du.at[sz.seq * i : sz.seq * (i + 1), 0 : main + 128] for i in range(2))
    dvw = gl.at[0 : sz.seq, 0 : main + 128]

    def heads_back(p, count):
        tile = lanes_at(128 * p, 128)
        dk_sum[...] = jnp.zeros_like(dk_sum)
        dv_sum[...] = jnp.zeros_like(dv_sum)
        for q in range(2):
            rows = slice(half * q, half * (q + 1))
            keys = half * (q + 1)
            order = lax.broadcasted_iota(jnp.int32, (half, keys), 0) + half * q
            allowed = (col_labels[rows, :] == row_labels[:, 0:keys].astype(jnp.float32)) & (
                order >= lax.broadcasted_iota(jnp.int32, (half, keys), 1)
            )
            lanes = lax.broadcasted_iota(jnp.int32, (half, 128), 1)
            side = lanes // HD
            total = jnp.zeros((half, 128), jnp.float32)
            for h in range(count):
                queries = jnp.where(side == h, qw[rows, tile].astype(jnp.float32) * HD ** (-0.5), 0.0)
                queries = queries.astype(low)
                pulled = jnp.where(side == h, da[rows, tile].astype(jnp.float32), 0.0).astype(low)
                found = jnp.sum(jnp.where(lanes == 2 * p + h, lse[rows, :], 0.0), axis=1, keepdims=True)
                scores = times_flipped(queries, kw[0:keys, tile])
                soft = jnp.where(allowed, jnp.exp(jnp.where(allowed, scores - found, MASKED)), 0.0)
                soft_back = times_flipped(pulled, vw[0:keys, tile])
                inner = jnp.sum(soft_back * soft, axis=1, keepdims=True)
                score_back = (soft * (soft_back - inner)).astype(low)
                piece = times(score_back, kw[0:keys, tile]) * HD ** (-0.5)
                total = jnp.where(side == h, piece, total)
                dk_sum[0:keys] += times_outer(score_back, queries)
                dv_sum[0:keys] += times_outer(soft.astype(low), pulled)
            dqw[rows, tile] = total.astype(low)
        dkw[:, tile] = dk_sum[...].astype(low)
        dvw[:, tile] = dv_sum[...].astype(low)

    @pl.loop(0, main // 128)
    def _(p):
        heads_back(p, 2)

    @pl.when(at.r == 3)
    def _():
        heads_back(main // 128, 1)

    def compact(column):
        part, place = column // HD, column % HD
        return jnp.where(part < 3, 128 * part + place, -1)

    table = choose((384, 256), compact)
    backs = (dqw, dkw, dvw)
    edge_out[...] = picked(jnp.concatenate([b[:, 0:128] for b in backs], axis=1), table)
    wires.copy(edge_out, edge_in, (at.d, at.r - 1, at.c), 41, at.r > 0)

    @pl.when(at.r == 3)
    def _():
        edge_in[...] = picked(jnp.concatenate([b[:, main : main + 128] for b in backs], axis=1), table)

    u_relay(relay_of(ru, gu))

    def go_home(values, stage, every, halves, out, base):
        flipped = values.T
        for c in range(4):
            for y in range(2):
                rows = slice(pair * c + block * y, pair * c + block * (y + 1))
                stage[c, y] = flipped[rows].astype(low)
        holds = at.k == at.c % 2
        lanes = lanes_at(sz.part * at.r, sz.part)
        held = []
        for y in range(2):
            there = 2 * y + at.c % 2
            wires.copy(
                stage.at[:, y], every.at[:, :, lanes], (at.d, there, at.c), base + at.r, there != at.r
            )
            held.append((there == at.r, load(stage.at[:, y], every.at[:, :, lanes], there == at.r)))

        def along():
            for r in range(4):
                block_r = every.at[:, :, sz.part * r : sz.part * (r + 1)]
                wires.arrived(block_r, base + r, (at.d, r, at.c), holds & (at.r != r))
            for when, made in held:
                run(when, made.wait)
            del held[:]
            for c in range(4):
                wires.copy(
                    every.at[c], halves.at[at.c // 2], at.along(c), base + 4 + at.c // 2, holds & (at.c != c)
                )
                when = holds & (at.c == c)
                held.append((when, load(every.at[c], halves.at[at.c // 2], when)))

        def across():
            for when, made in held:
                run(when, made.wait)
            for t in range(2):
                there = 2 * t + at.k
                wires.arrived(halves.at[t], base + 4 + t, at.along(there), there != at.c)
            mine = out.at[rows_at(block * at.y, block)]
            wires.copy(halves.at[1 - at.y], mine, at.peer(2), base + 6)
            stay.append(load(halves.at[at.y], mine))

        def finish():
            wires.arrived(out.at[rows_at(block * (1 - at.y), block)], base + 6, at.peer(2))

        return along, across, finish

    res_along, res_across, res_finish = go_home(
        x2[...] + res_total(), res_stage, res_all, res_two, result_home, 56
    )
    wires.close(res_sent)

    wires.arrived(edge_in, 41, (at.d, at.r + 1, at.c), at.r < 3)

    def unfold(column):
        tile, lane = column // 128, column % 128
        inside = jnp.where(lane < HD - 16, HD * tile + lane + 16, -1)
        tail = jnp.where(lane < 48, HD * (lane // 16) + lane % 16, -1)
        return jnp.where(tile < 3, inside, tail)

    edges = picked(edge_in[...], choose((256, 512), unfold))
    lane = lax.broadcasted_iota(jnp.int32, (sz.seq, 128), 1)
    pieces = []
    for i, back in enumerate(backs):
        first = jnp.where(lane < slack * at.r, edges[:, 128 * i : 128 * i + 128], back[:, 0:128])
        pieces += [first, back[:, 128:main]]
    pieces.append(edges[:, 384:512])
    wires.close(dob_sent)
    own_back = dob.at[:, 0 : sz.heads]
    own_back[...] = jnp.concatenate(pieces, axis=1)

    wires.close(gd_sends)
    gd_own.wait()
    loads[17].wait()
    h_order, h_send, h_relay, h_arrived, h_from = collect_col(
        wires, lambda c: xh.at[c], zh, rh, at, 72
    )
    for step in range(4):
        there = h_order[step]
        rows = rows_at(pair * there, pair)
        gw[rows] = times(dy_t[rows, 0 : sz.seq], own_back[...]).astype(low)
        other = gw.at[rows_at(pair * there + block * (1 - at.d), block)]
        wires.copy(other, xh.at[there], at.peer(4), 80 + there)

    def o_heads(step):
        there = h_order[step]
        wires.arrived(xh.at[there], 80 + there, at.peer(4))
        mine = rows_at(pair * there + block * at.d, block)
        xh[there] = (gw[mine].astype(jnp.float32) + xh[there].astype(jnp.float32)).astype(low)
        h_send(step)

    loads[9].wait()

    def back_in(start, tile):
        out = times_flipped(own_back[...], wh[rows_at(start, tile)])
        dy[0 : sz.seq, lanes_at(start, tile)] = out.astype(low)

    over_tiles(sz.width, back_in)
    one_onward, one_total, _ = scatter_group(
        wires, (2,), dy, lambda d, r: sz.part * r, near_one, mid, far_one, at, 64
    )
    order, o_send, o_relay, o_arrived, o_from = collect_col(
        wires, lambda c: xo.at[c], zo, ro, at, 10
    )
    for step in range(4):
        there = order[step]
        wires.arrived(xo.at[there], 48 + there, at.peer(4))
        mine = go[rows_at(pair * there, pair), lanes_at(sz.mixed * at.d, sz.mixed)]
        xo[there] = (mine.astype(jnp.float32) + xo[there].astype(jnp.float32)).astype(low)
        o_send(step)

    def relay_out(there):
        both = xo[there].astype(jnp.float32) + ro[...].astype(jnp.float32)
        xo[there] = both.astype(low)

    brought = []

    def bring(c, landing, needed, lanes):
        made = load(landing.at[c], h2_t.at[pair * c : pair * (c + 1), 0:lanes], needed)
        brought.append((needed, made))

        @pl.when(jnp.logical_not(needed) & (at.c != c))
        def _():
            h2_t[pair * c : pair * (c + 1), 0:lanes] = jnp.zeros((pair, lanes), low)

    def summed(lanes):
        result = jnp.zeros((pair, lanes.stop - lanes.start), jnp.float32)
        for c in range(4):
            result = result + h2_t[pair * c : pair * (c + 1), lanes].astype(jnp.float32)
        return result

    half_rows = sz.pieces

    def natural_rows(value):
        flipped = value.T
        return jnp.concatenate(
            [flipped[:, 0:half_rows], flipped[:, block : block + half_rows]], axis=1
        )

    def own_half(row):
        return jnp.where(at.d == 0, row[:, 0:half_rows], row[:, half_rows : 2 * half_rows])

    def all_brought():
        for needed, made in brought:
            run(needed, made.wait)
        del brought[:]

    def relay_heads(there):
        xh[there] = (xh[there].astype(jnp.float32) + rh[...].astype(jnp.float32)).astype(low)

    res_along()
    one_onward()
    o_heads(0)
    h1_back = one_total()
    through_norm, gain_one, shift_one = norm_back(
        h1_back, x_own[...].astype(jnp.float32), vec_rows[0:1]
    )
    va[0, 0:1] = gain_one
    va[0, 1:2] = shift_one
    for mask in range(1, 8):
        wires.copy(va.at[0], va.at[mask], at.peer(mask), 84 + mask)
    grad_along, grad_across, grad_finish = go_home(
        dx2[...] + through_norm, grad_stage, grad_all, grad_two, grad_home, 104
    )
    for c in range(4):
        d_arrived(c)
        bring(c, zd, d_from(c), sz.solid)
    all_brought()
    for i in range(sz.solid // 128):
        rows = slice(128 * i, 128 * (i + 1))
        u[rows, 0 : sz.share] = natural_rows(summed(rows))
    down_out = load(u.at[0 : sz.solid, 0:512], out_down.at[0 : sz.solid])
    o_heads(1)
    grad_along()
    o_heads(2)
    h_relay(relay_heads)
    gu_own = load(gu.at[own], h2_t.at[own, 0 : sz.hidden])
    for c in range(4):
        u_arrived(c)
        bring(c, zu, u_from(c), sz.hidden)
    all_brought()
    gu_own.wait()
    value = natural_rows(summed(slice(sz.solid, sz.hidden)))
    end = 4 * sz.pieces
    u[sz.solid : end, 0 : sz.share] = value[64 : 64 + sz.tail]
    vec_out[5:6, 0:half_rows] = own_half(value[64 + sz.tail : 65 + sz.tail])
    tail_out = load(u.at[sz.solid : end, 0:512], out_down.at[sz.solid : end])
    theirs = rows_at(pair * at.c + block * (1 - at.d), block)

    def part_sum(side, lanes):
        result = jnp.zeros((block, sz.hidden), jnp.float32)
        for c in range(4):
            result = result + h2_t[rows_at(pair * c + block * side, block), lanes].astype(jnp.float32)
        return result

    every = slice(0, sz.hidden)
    gu[theirs] = part_sum(1 - at.d, every).astype(low)
    wires.copy(gu.at[theirs], xu, at.peer(4), 97)
    o_relay(relay_out)
    o_heads(3)
    res_across()
    mine_sum = part_sum(at.d, every)
    down_out.wait()
    tail_out.wait()
    wires.arrived(xu, 97, at.peer(4))
    partner_sum = xu[...].astype(jnp.float32)
    for side in range(2):

        @pl.when(at.d == side)
        def _():
            both = (mine_sum, partner_sum) if side == 0 else (partner_sum, mine_sum)
            for j in range(4):
                rows = slice(block * j, block * (j + 1))
                for i in range(2):
                    u[rows, half_rows * i : half_rows * (i + 1)] = both[i][:, half_rows * j : half_rows * (j + 1)]

    bias_sum = mine_sum[half_rows : half_rows + 1]
    for j in range(4):
        vec_out[8 + j : 9 + j, 0:half_rows] = bias_sum[:, half_rows * j : half_rows * (j + 1)]
    up_out = load(u.at[0 : 4 * block, 0:512], out_up)

    for c in range(4):
        o_arrived(c)
        needed = o_from(c)
        made = load(zo.at[c], wd.at[pair * c : pair * (c + 1), 0 : sz.mixed], needed)
        brought.append((needed, made))

        @pl.when(jnp.logical_not(needed))
        def _():
            wd[pair * c : pair * (c + 1), 0 : sz.mixed] = jnp.zeros((pair, sz.mixed), low)

    all_brought()
    value = xo[at.c].astype(jnp.float32)
    for c in range(4):
        value = value + wd[pair * c : pair * (c + 1), 0 : sz.mixed].astype(jnp.float32)
    flipped = natural_rows(value)
    vec_out[4:5, 0:half_rows] = own_half(flipped[half_rows : half_rows + 1])
    flipped = flipped[0:block]
    for i in range(4):
        held = (dk_sum, dv_sum)[i // 2].at[block * (i % 2) : block * (i % 2 + 1)]
        lanes = min(128, sz.share - 128 * i)
        held[:, 0:lanes] = flipped[:, 128 * i : 128 * i + lanes]
        stay.append(load(held, out_out.at[:, 128 * i : 128 * (i + 1)]))

    grad_across()

    for mask in range(1, 8):
        wires.arrived(va.at[mask], 84 + mask, at.peer(mask))
    vb[at.c] = functools.reduce(lambda a, b: a + b, [va[mask] for mask in range(8)])
    for c in range(4):
        wires.copy(vb.at[at.c], vb.at[at.c], at.along(c), 98 + at.c, at.c != c)

    for c in range(4):
        wires.arrived(vb.at[c], 98 + c, at.along(c), at.c != c)
    sums = vb[0] + vb[1] + vb[2] + vb[3]
    picked_sums = jnp.zeros((4, half_rows), jnp.float32)
    for i in range(8):
        cut = sums[0:4, block * i : block * i + half_rows]
        picked_sums = jnp.where(2 * at.c + at.d == i, cut, picked_sums)
    vec_out[0:4, 0:half_rows] = picked_sums
    res_finish()
    grad_finish()
    up_out.wait()
    rest_lanes = sz.heads - sz.solid
    for c in range(4):
        h_arrived(c)
        needed = h_from(c)
        rows = slice(block * c, block * (c + 1))
        parts = (
            load(zh.at[c, :, 0 : sz.solid], wd.at[rows], needed),
            load(zh.at[c, :, sz.solid : sz.heads], wu.at[rows, 0:rest_lanes], needed),
        )
        brought += [(needed, made) for made in parts]

        @pl.when(jnp.logical_not(needed))
        def _():
            wd[rows] = jnp.zeros((block, sz.solid), low)
            wu[rows, 0:rest_lanes] = jnp.zeros((block, rest_lanes), low)

    all_brought()
    left = xh[at.c, :, 0 : sz.solid].astype(jnp.float32)
    right = xh[at.c, :, sz.solid : sz.heads].astype(jnp.float32)
    for c in range(4):
        rows = slice(block * c, block * (c + 1))
        left = left + wd[rows].astype(jnp.float32)
        right = right + wu[rows, 0:rest_lanes].astype(jnp.float32)
    whole = jnp.concatenate([left, right], axis=1)
    for i in range(3):
        turned_columns = jnp.concatenate(
            [
                whole[:, main * i : main * (i + 1)],
                whole[:, 3 * main + slack * i : 3 * main + slack * (i + 1)],
            ],
            axis=1,
        )
        rows = slice(block * i, block * (i + 1))
        for r in range(4):

            @pl.when(at.r == r)
            def _():
                cut = slack * r
                value = turned_columns
                if cut:
                    value = jnp.concatenate([value[:, cut:], value[:, 0:cut]], axis=1)
                u[rows, 0 : sz.share] = value
                if i != 1:
                    vec_out[6 + i // 2 : 7 + i // 2, 0:half_rows] = own_half(
                        value[half_rows : half_rows + 1]
                    )

    stay.append(load(u.at[0 : 3 * block, 0:512], out_heads))
    for made in stay:
        made.wait()
    wires.close()


def update_kernel(sz, rates, grads, result_in, grad_in, weights, firsts, seconds, outs):
    down, out, up, heads, vectors = grads
    share, pieces, block = sz.share, sz.pieces, sz.block

    def move(i, place, gradient, decay):
        weight = weights[i][place]
        first_new = BETA_FIRST * firsts[i][place] + (1.0 - BETA_FIRST) * gradient
        second_new = BETA_SECOND * seconds[i][place] + (1.0 - BETA_SECOND) * (gradient * gradient)
        divisor = jnp.sqrt(second_new * (1.0 / (1.0 - BETA_SECOND**STEP))) + ADAM_EPSILON
        change = first_new * (rates[i] / (1.0 - BETA_FIRST**STEP)) / divisor
        weight_new = weight * (1.0 - rates[i] * decay) - change
        outs[3 * i + 2][place] = first_new
        outs[3 * i + 3][place] = second_new
        outs[3 * i + 4][place] = weight_new

    for part in range(3):
        move(0, part, heads[part, :, 0:share], MATRIX_DECAY)
    move(1, slice(None), out[:, 0:share], MATRIX_DECAY)
    move(2, slice(None), jnp.stack([up[j, :, 0:share] for j in range(4)], axis=1), MATRIX_DECAY)
    move(3, slice(None), down[:, 0:share], MATRIX_DECAY)

    @pl.when(pl.program_id(0) == 0)
    def _():
        for i, source, row in (
            (4, 0, 0), (4, 1, 1), (5, 4, 0), (5, 2, 1), (5, 3, 2), (5, 5, 3),
            (6, 6, 0), (6, 7, 1), (7, 8, 0), (7, 9, 1), (7, 10, 2), (7, 11, 3),
        ):
            move(i, row, vectors[source : source + 1, 0:pieces], 0.0)

    def plain(rows):
        rows = rows.astype(jnp.float32)
        return jnp.concatenate([rows[0:pieces], rows[block : block + pieces]], axis=0)

    @pl.when(pl.program_id(0) == 1)
    def _():
        outs[0][...] = plain(result_in[...]).astype(jnp.bfloat16)

    @pl.when(pl.program_id(0) == 2)
    def _():
        outs[1][...] = plain(grad_in[...])


def fused(
    tokens,
    cotangent,
    segments,
    weights,
    firsts,
    seconds,
):
    low = jnp.bfloat16
    seq, share = tokens.shape
    pieces = weights[1].shape[2]
    sz = Sizes(share, pieces, seq)
    block, main = sz.block, sz.main

    def views(arrays):
        heads, out, up, down, *small = arrays
        return (
            jnp.transpose(heads.reshape(pieces, 3, share), (1, 0, 2)),
            out.reshape(pieces, share),
            up.reshape(pieces, 4, share),
            down.reshape(4 * pieces, share),
            *[each.reshape(each.shape[0], 1, pieces) for each in small],
        )

    viewed = views(weights)
    labels = segments.reshape(1, -1)

    def made(*shape, dtype=low):
        return jax.ShapeDtypeStruct(shape, dtype)

    def held(*shape, dtype=low):
        return pltpu.VMEM(shape, dtype)

    w, seq, both, part = sz.width, sz.seq, sz.both, sz.part
    vmem, anywhere = pl.BlockSpec(memory_space=pltpu.VMEM), pl.BlockSpec(memory_space=pl.ANY)
    dma = pltpu.SemaphoreType.DMA
    f32 = jnp.float32
    wide = 3 * 128 + 128
    outs = pl.pallas_call(
        functools.partial(forward_kernel, sz),
        out_shape=(
            made(w, sz.heads),
            made(w, 2 * sz.mixed),
            made(w, sz.hidden),
            made(w, sz.solid),
            made(w, seq),
            made(w, both),
            made(w, sz.solid),
            made(w, 128),
            made(both, w),
            made(both, sz.hidden, dtype=f32),
            made(both, sz.hidden),
            made(seq, main + 128),
            made(seq, main + 128),
            made(seq, main + 128),
            made(seq, 2 * sz.mixed),
            made(seq, 128, dtype=f32),
            made(part, w, dtype=f32),
            made(part, w),
            made(8, w, dtype=f32),
        ),
        in_specs=[anywhere] * 6 + [vmem] * 5,
        out_specs=[anywhere] * 19,
        scratch_shapes=[
            held(w, sz.heads),
            held(w, 2 * sz.mixed),
            held(w, sz.hidden),
            held(w, sz.solid),
            held(w, seq),
            held(w, both),
            held(w, sz.solid),
            held(w, 128),
            held(w, both),
            held(both, w),
            held(both, sz.hidden, dtype=f32),
            held(both, sz.hidden),
            held(seq, main + 128),
            held(seq, main + 128),
            held(seq, main + 128),
            held(seq, 2 * sz.mixed),
            held(seq, 128, dtype=f32),
            held(part, w, dtype=f32),
            held(part, w),
            held(8, w, dtype=f32),
            held(w, seq),
            held(seq, w),
            held(both, w),
            held(seq, sz.heads),
            held(seq, main + 128),
            held(w, 128),
            held(seq, w),
            held(seq, 256),
            held(seq, 256),
            held(seq, 128),
            held(2, part, w),
            held(1, part, w),
            held(1, part, w),
            held(share, seq),
            held(share, seq),
            held(3, pieces, share, dtype=f32),
            held(pieces, share, dtype=f32),
            held(pieces, 4, share, dtype=f32),
            held(4 * pieces, share, dtype=f32),
            held(sz.pair, seq),
            held(sz.pair, seq),
            held(block, sz.hidden),
            held(sz.pair, 128),
            held(seq, 1, dtype=f32),
            held(block, seq),
            held(block, seq),
            dma((160,)),
            dma((160,)),
            dma((48,)),
        ],
        compiler_params=pltpu.CompilerParams(
            collective_id=0, has_side_effects=True, vmem_limit_bytes=VMEM_BYTES
        ),
        cost_estimate=pl.CostEstimate(flops=10**10, bytes_accessed=10**8, transcendentals=10**6),
    )(tokens.T, cotangent.T, *viewed, labels)
    (wh, wo, wu, wd, h1_t, h2_t, gd, gt, dy, u, gl, qw, kw, vw, a_nat, lse, x2, x_own, vec_rows) = outs
    outs = pl.pallas_call(
        functools.partial(backward_kernel, sz),
        out_shape=(
            made(4 * pieces, 512, dtype=f32),
            made(4 * block, 512, dtype=f32),
            made(block, 512, dtype=f32),
            made(3 * block, 512, dtype=f32),
            made(sz.pair, seq),
            made(sz.pair, seq),
            made(16, 256, dtype=f32),
            made(4, sz.pair, sz.solid),
            made(4, sz.pair, sz.hidden),
            made(4, sz.pair, sz.mixed),
            made(4, block, sz.heads),
            made(4, block, seq),
            made(2, block, seq),
            made(4, block, seq),
            made(2, block, seq),
        ),
        in_specs=[anywhere] * 18 + [vmem] * 2,
        out_specs=[anywhere] * 6 + [vmem] + [anywhere] * 8,
        scratch_shapes=[
            held(sz.pair, sz.solid),
            held(sz.pair, sz.hidden),
            held(sz.pair, sz.mixed),
            held(block, sz.heads),
            held(seq, main + 128),
            held(seq, main + 128),
            held(seq, main + 128),
            held(seq, 2 * sz.mixed),
            held(seq, 128, dtype=f32),
            held(part, w, dtype=f32),
            held(part, w),
            held(block, sz.hidden),
            held(both, w),
            held(w, both),
            held(both, sz.hidden, dtype=f32),
            held(both, sz.hidden),
            held(w, both),
            held(w, sz.solid),
            held(w, sz.hidden),
            held(w, 2 * sz.mixed),
            held(w, sz.heads),
            held(w, 128),
            held(part, w),
            held(both, sz.hidden),
            held(w, sz.heads),
            held(w, sz.hidden),
            held(w, 2 * sz.mixed),
            held(4, block, sz.heads),
            held(4, sz.pair, sz.mixed),
            held(4, part, w),
            held(3, part, w),
            held(4, part, w),
            held(3, part, w),
            held(2, part, w),
            held(1, part, w),
            held(3, part, w),
            held(seq, w),
            held(seq, 2 * sz.mixed),
            held(seq, 128, dtype=f32),
            held(seq, 128, dtype=f32),
            held(part, w, dtype=f32),
            held(seq, 256),
            held(seq, 256),
            held(seq, 128),
            held(seq, 128),
            held(seq, 1, dtype=f32),
            held(4, 2, block, part),
            held(4, 2, block, part),
            held(8, 8, w, dtype=f32),
            held(4, 8, w, dtype=f32),
            dma((128,)),
            dma((120,)),
            dma((80,)),
        ],
        compiler_params=pltpu.CompilerParams(
            collective_id=1, has_side_effects=True, vmem_limit_bytes=VMEM_BYTES
        ),
        cost_estimate=pl.CostEstimate(flops=2 * 10**10, bytes_accessed=10**8, transcendentals=10**6),
    )(
        dy, gd, gt, u, gl, h2_t, wd, wu, wo, wh, h1_t,
        qw, kw, vw, a_nat, lse, x2, x_own, vec_rows, labels,
    )
    down, up, out, heads, result_home, grad_home, vectors = outs[:7]
    steps = 5
    chunk = pieces // steps

    def rows_of(shape, axis, size):
        block_shape = list(shape)
        block_shape[axis] = size
        return pl.BlockSpec(tuple(block_shape), lambda i: tuple(i if a == axis else 0 for a in range(len(shape))))

    def whole(shape):
        return pl.BlockSpec(tuple(shape), lambda i: (0,) * len(shape))

    matrix_specs = (
        rows_of((3, pieces, share), 1, chunk),
        rows_of((pieces, share), 0, chunk),
        rows_of((pieces, 4, share), 0, chunk),
        rows_of((4 * pieces, share), 0, 4 * chunk),
        *[whole(each.shape) for each in viewed[4:]],
    )
    grads = (down, out, up.reshape(4, block, 512), heads.reshape(3, block, 512), vectors)
    grad_specs = (
        rows_of((4 * pieces, 512), 0, 4 * chunk),
        rows_of((block, 512), 0, chunk),
        rows_of((4, block, 512), 1, chunk),
        rows_of((3, block, 512), 1, chunk),
        whole((16, 256)),
    )
    rates = (0.05, 0.2, 0.05, 0.025, 0.3, 0.3, 0.3, 0.3)
    arguments = (*grads, result_home, grad_home, *viewed, *views(firsts), *views(seconds))
    out_shape = [made(share, seq), made(share, seq, dtype=f32)]
    out_specs = [whole((share, seq)), whole((share, seq))]
    for each, spec in zip(viewed, matrix_specs, strict=True):
        out_shape += [jax.ShapeDtypeStruct(each.shape, f32)] * 3
        out_specs += [spec] * 3

    def update(*refs):
        ins, outs = refs[:31], refs[31:]
        update_kernel(sz, rates, ins[:5], ins[5], ins[6], ins[7:15], ins[15:23], ins[23:31], outs)

    updated = pl.pallas_call(
        update,
        grid=(steps,),
        out_shape=out_shape,
        in_specs=[*grad_specs, whole((sz.pair, seq)), whole((sz.pair, seq)), *matrix_specs * 3],
        out_specs=out_specs,
        compiler_params=pltpu.CompilerParams(vmem_limit_bytes=VMEM_BYTES),
        cost_estimate=pl.CostEstimate(
            flops=20 * 10**6, bytes_accessed=30 * 10**6, transcendentals=2 * 10**6
        ),
    )(*arguments)
    results = [updated[0].T, updated[1].T]
    for i, weight in enumerate(weights):
        for each in updated[2 + 3 * i : 5 + 3 * i]:
            if i == 0:
                each = jnp.transpose(each, (1, 0, 2))
            results.append(each.reshape(weight.shape))
    return tuple(results)


def normalize(inputs):
    center = jnp.mean(inputs, axis=1, keepdims=True)
    spread = jnp.mean(inputs * inputs, axis=1, keepdims=True) - center * center
    inverse = lax.rsqrt(spread + NORM_EPSILON)
    return ((inputs - center) * inverse, inverse)


def norm_pull(upstream, centered, inverse, gain):
    scaled = upstream * gain
    inner = (
        scaled
        - jnp.mean(scaled, axis=1, keepdims=True)
        - centered * jnp.mean(scaled * centered, axis=1, keepdims=True)
    )
    return inner * inverse


def crossed(blocks, n):
    pairs = [(i * n + j, j * n + i) for i in range(n) for j in range(n)]
    return lax.ppermute(blocks, ("row", "col"), pairs)


def scatter_rows(partial):
    return lax.psum_scatter(
        partial.astype(jnp.bfloat16), "row", scatter_dimension=0, tiled=True
    ).astype(jnp.float32)


def gather_rows(local):
    return lax.all_gather(local, "row", axis=0, tiled=True)


def split_heads(rows):
    return jnp.transpose(rows.reshape(rows.shape[0], -1, HD), (1, 0, 2))


def join_heads(values):
    return jnp.transpose(values, (1, 0, 2)).reshape(values.shape[1], -1)


def scores_of(queries, keys, allowed):
    scores = jnp.einsum(
        "hqe,hke->hqk", queries, keys, preferred_element_type=jnp.float32
    ) * HD ** (-0.5)
    return jnp.where(allowed[None], scores, MASKED)


def gathered(
    tokens,
    cotangent,
    segments,
    w_heads,
    w_out,
    w_up,
    w_down,
    norm_vectors,
    width_vectors,
    attend_bias,
    hidden_vectors,
):
    n_dp, n_row, n_col = (lax.axis_size(name) for name in ("dp", "row", "col"))
    row = lax.axis_index("row")
    low = jnp.bfloat16
    share = tokens.shape[1]
    width = share * n_col
    seq = tokens.shape[0]
    part = seq // n_row
    near = HEADS // n_row
    window = (HEADS - near * (n_row - 1)) * HD
    step = near * HD
    edge = width - (share + step * (n_row - 1)) if n_row > 1 else 0
    edge = window - share
    to_next = [(i, i + 1) for i in range(n_row - 1)]
    to_last = [(i + 1, i) for i in range(n_row - 1)]
    offset = edge - (share - step) * row

    vectors = jnp.concatenate(
        [
            norm_vectors.reshape(2, -1),
            width_vectors.reshape(4, -1),
            attend_bias.reshape(2, -1),
            hidden_vectors.reshape(4, -1),
        ]
    ).astype(low)
    vectors = lax.all_gather(vectors, ("row", "col", "dp"), axis=0, tiled=False)
    vectors = vectors.reshape(n_row, n_col, n_dp, 12, -1).astype(jnp.float32)
    by_col = jnp.transpose(vectors[0], (2, 0, 1, 3)).reshape(12, width)
    by_row = jnp.transpose(vectors[:, 0], (2, 0, 1, 3)).reshape(12, width)
    gain_one, shift_one, bias_out, gain_two, shift_two, bias_down = (by_col[i] for i in range(6))
    zeros = jnp.zeros((1, window), jnp.float32)
    attend_rows = lax.dynamic_slice_in_dim(by_row[6:8], row * step, window, axis=1)
    heads_bias = jnp.concatenate([attend_rows[0:1], zeros, attend_rows[1:2]]).reshape(-1)
    unit_bias = lax.dynamic_slice_in_dim(by_row[8:12], row * share, share, axis=1).reshape(-1)

    own = w_heads.astype(low).reshape(-1, 3, share)
    passed = lax.ppermute(own[:, :, share - edge :], "row", to_next)
    own = jnp.concatenate([passed, own, jnp.zeros_like(passed)], axis=2)
    own = lax.dynamic_slice_in_dim(own, offset, window, axis=2).reshape(-1, 3 * window)
    heads_matrix = lax.all_gather(own, ("col", "dp"), axis=0, tiled=True)
    out_matrix = lax.all_gather(w_out.astype(low).reshape(-1, share), ("col", "dp"), axis=0)
    out_matrix = jnp.transpose(out_matrix.reshape(n_col, share, share), (1, 0, 2))
    out_matrix = out_matrix.reshape(share, width)
    passed = lax.ppermute(out_matrix[share - edge :], "row", to_next)
    out_matrix = jnp.concatenate([passed, out_matrix, jnp.zeros_like(passed)])
    out_matrix = lax.dynamic_slice_in_dim(out_matrix, offset, window)
    owned = (jnp.arange(window) < step) | (row == n_row - 1)
    out_matrix = jnp.where(owned[:, None], out_matrix, jnp.zeros_like(out_matrix))
    up_matrix = lax.all_gather(
        w_up.astype(low).reshape(-1, 4 * share), ("col", "dp"), axis=0, tiled=True
    )
    down_matrix = lax.all_gather(w_down.astype(low).reshape(4, -1, share), ("col", "dp"), axis=0)
    down_matrix = down_matrix.reshape(n_col, n_dp, 4, -1, share)
    down_matrix = jnp.transpose(down_matrix, (2, 1, 3, 0, 4)).reshape(4 * share, width)

    inputs_low = lax.all_gather(crossed(tokens, n_row), "row", axis=1, tiled=True)
    upstream = lax.all_gather(crossed(cotangent, n_row), "row", axis=1, tiled=True)
    inputs = inputs_low.astype(jnp.float32)
    centered_one, inverse_one = normalize(inputs)
    normed_one = (centered_one * gain_one + shift_one).astype(low)
    projected = (times(normed_one, heads_matrix) + heads_bias).astype(low)
    queries, keys, values = (
        split_heads(projected[:, i * window : (i + 1) * window]) for i in range(3)
    )
    labels = lax.dynamic_slice_in_dim(segments, lax.axis_index("col") * seq, seq)
    places = jnp.arange(seq, dtype=jnp.int32)
    allowed = (labels[:, None] == labels[None, :]) & (places[:, None] >= places[None, :])
    scores = scores_of(queries, keys, allowed)
    highest = jnp.max(scores, axis=-1, keepdims=True)
    log_total = highest + jnp.log(jnp.sum(jnp.exp(scores - highest), axis=-1, keepdims=True))
    soft = jnp.exp(scores - log_total).astype(low)
    mixed = jnp.einsum("hqk,hke->hqe", soft, values, preferred_element_type=jnp.float32)
    mixed = join_heads(mixed.astype(low))
    branch = scatter_rows(times(mixed, out_matrix))
    mine = row * part
    middle = lax.dynamic_slice_in_dim(inputs, mine, part) + (branch + bias_out)
    centered_two, inverse_two = normalize(middle)
    normed_two = gather_rows((centered_two * gain_two + shift_two).astype(low))
    hidden = times(normed_two, up_matrix) + unit_bias
    activated, smooth_pull = jax.vjp(smooth, hidden)
    activated = activated.astype(low)
    result = (middle + (scatter_rows(times(activated, down_matrix)) + bias_down)).astype(low)

    down_back = times_flipped(upstream, down_matrix)
    grad_down = times_outer(activated, upstream)
    hidden_back = smooth_pull(down_back)[0].astype(low)
    grad_up = times_outer(normed_two, hidden_back)
    unit_sum = jnp.sum(hidden_back, axis=0, dtype=jnp.float32)
    normed_two_back = scatter_rows(times_flipped(hidden_back, up_matrix))
    upstream_own = lax.dynamic_slice_in_dim(upstream, mine, part).astype(jnp.float32)
    middle_back = upstream_own + norm_pull(normed_two_back, centered_two, inverse_two, gain_two)
    branch_own = middle_back.astype(low)
    branch_back = gather_rows(branch_own)
    mixed_back = times_flipped(branch_back, out_matrix).astype(low)
    grad_out = times_outer(mixed, branch_back)
    mixed_back = split_heads(mixed_back)
    scores_again = scores_of(queries, keys, allowed)
    soft = jnp.exp(scores_again - log_total)
    soft_back = jnp.einsum("hqe,hke->hqk", mixed_back, values, preferred_element_type=jnp.float32)
    row_inner = jnp.sum(soft_back * soft, axis=-1, keepdims=True)
    score_back = (soft * (soft_back - row_inner)).astype(low)
    query_back = jnp.einsum(
        "hqk,hke->hqe", score_back, keys, preferred_element_type=jnp.float32
    ) * HD ** (-0.5)
    key_back = jnp.einsum(
        "hqk,hqe->hke", score_back, queries, preferred_element_type=jnp.float32
    ) * HD ** (-0.5)
    value_back = jnp.einsum(
        "hqk,hqe->hke", soft.astype(low), mixed_back, preferred_element_type=jnp.float32
    )
    heads_back = jnp.concatenate(
        [join_heads(each.astype(low)) for each in (query_back, key_back, value_back)], axis=1
    )
    heads_sum = jnp.sum(heads_back, axis=0, dtype=jnp.float32)
    normed_one_back = scatter_rows(times_flipped(heads_back, heads_matrix))
    grad_heads = times_outer(normed_one, heads_back)
    centered_own = lax.dynamic_slice_in_dim(centered_one, mine, part)
    inverse_own = lax.dynamic_slice_in_dim(inverse_one, mine, part)
    input_back = middle_back + norm_pull(normed_one_back, centered_own, inverse_own, gain_one)

    def homeward(own):
        own = lax.all_to_all(own, "row", split_axis=1, concat_axis=0, tiled=True)
        return crossed(own, n_row)

    result_tokens = homeward(result)
    input_gradient = homeward(input_back.astype(low)).astype(jnp.float32)

    by_token = jnp.stack(
        [
            jnp.sum(normed_one_back * centered_own, axis=0),
            jnp.sum(normed_one_back, axis=0),
            jnp.sum(branch_own.astype(jnp.float32), axis=0),
            jnp.sum(normed_two_back * centered_two, axis=0),
            jnp.sum(normed_two_back, axis=0),
            jnp.sum(upstream_own, axis=0),
        ]
    )
    owned_rows = jnp.where(owned, heads_sum.reshape(3, window)[0::2], 0.0)
    by_unit = jnp.concatenate(
        [
            lax.dynamic_update_slice_in_dim(
                jnp.zeros((2, width), jnp.float32), owned_rows, row * step, axis=1
            ),
            lax.dynamic_update_slice_in_dim(
                jnp.zeros((4, width), jnp.float32), unit_sum.reshape(4, share), row * share, axis=1
            ),
        ]
    )
    sums = lax.psum(jnp.concatenate([by_token, by_unit]), ("dp", "row", "col"))
    pieces = share // n_dp
    inner = lax.axis_index("dp") * pieces
    col_sums = lax.dynamic_slice_in_dim(sums, lax.axis_index("col") * share + inner, pieces, axis=1)
    row_sums = lax.dynamic_slice_in_dim(sums, row * share + inner, pieces, axis=1)

    both = ("col", "dp")

    def to_owner(gradient):
        return lax.psum_scatter(gradient, both, scatter_dimension=0, tiled=True)

    got_heads = to_owner(grad_heads.astype(low)).reshape(pieces, 3, window)
    got_heads = jnp.where(owned, got_heads, jnp.zeros_like(got_heads))
    passed = lax.ppermute(got_heads[:, :, :edge], "row", to_last)
    got_heads = jnp.concatenate([got_heads, jnp.zeros_like(passed)], axis=2)
    got_heads = lax.dynamic_slice_in_dim(got_heads, edge - offset, share, axis=2)
    passed = jnp.concatenate([jnp.zeros((pieces, 3, share), low), passed, jnp.zeros_like(passed)], axis=2)
    got_heads = got_heads + lax.dynamic_slice_in_dim(passed, share - step + edge - offset, share, axis=2)
    low_out = jnp.where(owned[:, None], grad_out, 0.0).astype(low)
    passed = lax.ppermute(low_out[:edge], "row", to_last)
    low_out = jnp.concatenate([low_out, jnp.zeros_like(passed)])
    low_out = lax.dynamic_slice_in_dim(low_out, edge - offset, share)
    passed = jnp.concatenate([jnp.zeros((share, width), low), passed, jnp.zeros_like(passed)])
    low_out = low_out + lax.dynamic_slice_in_dim(passed, share - step + edge - offset, share)
    low_out = jnp.transpose(low_out.reshape(n_dp, pieces, n_col, share), (2, 0, 1, 3))
    got_out = to_owner(low_out.reshape(-1, share))
    got_up = to_owner(grad_up.astype(low))
    low_down = grad_down.astype(low).reshape(4, n_dp, pieces, n_col, share)
    low_down = jnp.transpose(low_down, (3, 1, 0, 2, 4)).reshape(-1, share)
    got_down = to_owner(low_down)

    reduced = [
        each.astype(jnp.float32).reshape(like.shape)
        for each, like in (
            (got_heads, w_heads),
            (got_out, w_out),
            (got_up, w_up),
            (got_down, w_down),
            (col_sums[0:2], norm_vectors),
            (col_sums[2:6], width_vectors),
            (row_sums[6:8], attend_bias),
            (row_sums[8:12], hidden_vectors),
        )
    ]
    return result_tokens, input_gradient, reduced


def per_device(
    tokens,
    cotangent,
    segments,
    w_heads,
    w_out,
    w_up,
    w_down,
    norm_vectors,
    width_vectors,
    attend_bias,
    hidden_vectors,
    drift_heads,
    drift_out,
    drift_up,
    drift_down,
    drift_norm,
    drift_width,
    drift_attend,
    drift_hidden,
    power_heads,
    power_out,
    power_up,
    power_down,
    power_norm,
    power_width,
    power_attend,
    power_hidden,
):
    weights = (
        w_heads,
        w_out,
        w_up,
        w_down,
        norm_vectors,
        width_vectors,
        attend_bias,
        hidden_vectors,
    )
    firsts = (
        drift_heads,
        drift_out,
        drift_up,
        drift_down,
        drift_norm,
        drift_width,
        drift_attend,
        drift_hidden,
    )
    seconds = (
        power_heads,
        power_out,
        power_up,
        power_down,
        power_norm,
        power_width,
        power_attend,
        power_hidden,
    )
    sizes = tuple(lax.axis_size(name) for name in ("dp", "row", "col"))
    if sizes == (2, 4, 4):
        return fused(tokens, cotangent, segments, weights, firsts, seconds)
    result_tokens, input_gradient, reduced = gathered(tokens, cotangent, segments, *weights)
    heads_up = adam(w_heads, reduced[0], drift_heads, power_heads, 0.05, MATRIX_DECAY)
    out_up = adam(w_out, reduced[1], drift_out, power_out, 0.2, MATRIX_DECAY)
    up_up = adam(w_up, reduced[2], drift_up, power_up, 0.05, MATRIX_DECAY)
    down_up = adam(w_down, reduced[3], drift_down, power_down, 0.025, MATRIX_DECAY)
    norm_up = adam(norm_vectors, reduced[4], drift_norm, power_norm, 0.3, 0.0)
    width_up = adam(width_vectors, reduced[5], drift_width, power_width, 0.3, 0.0)
    attend_up = adam(attend_bias, reduced[6], drift_attend, power_attend, 0.3, 0.0)
    hidden_up = adam(hidden_vectors, reduced[7], drift_hidden, power_hidden, 0.3, 0.0)
    return (
        result_tokens,
        input_gradient,
        heads_up[0],
        heads_up[1],
        heads_up[2],
        out_up[0],
        out_up[1],
        out_up[2],
        up_up[0],
        up_up[1],
        up_up[2],
        down_up[0],
        down_up[1],
        down_up[2],
        norm_up[0],
        norm_up[1],
        norm_up[2],
        width_up[0],
        width_up[1],
        width_up[2],
        attend_up[0],
        attend_up[1],
        attend_up[2],
        hidden_up[0],
        hidden_up[1],
        hidden_up[2],
    )


def solution(mesh):
    return jax.shard_map(
        per_device,
        mesh=mesh,
        in_specs=(
            P(("dp", "row"), "col"),
            P(("dp", "row"), "col"),
            P("dp"),
            P("col", "dp", None, None, "row"),
            P("row", "dp", None, "col"),
            P("col", "dp", None, None, "row"),
            P(None, "row", "dp", None, "col"),
            P(None, "col", "dp", None),
            P(None, "col", "dp", None),
            P(None, "row", "dp", None),
            P(None, "row", "dp", None),
            P("col", "dp", None, None, "row"),
            P("row", "dp", None, "col"),
            P("col", "dp", None, None, "row"),
            P(None, "row", "dp", None, "col"),
            P(None, "col", "dp", None),
            P(None, "col", "dp", None),
            P(None, "row", "dp", None),
            P(None, "row", "dp", None),
            P("col", "dp", None, None, "row"),
            P("row", "dp", None, "col"),
            P("col", "dp", None, None, "row"),
            P(None, "row", "dp", None, "col"),
            P(None, "col", "dp", None),
            P(None, "col", "dp", None),
            P(None, "row", "dp", None),
            P(None, "row", "dp", None),
        ),
        out_specs=(
            P(("dp", "row"), "col"),
            P(("dp", "row"), "col"),
            P("col", "dp", None, None, "row"),
            P("col", "dp", None, None, "row"),
            P("col", "dp", None, None, "row"),
            P("row", "dp", None, "col"),
            P("row", "dp", None, "col"),
            P("row", "dp", None, "col"),
            P("col", "dp", None, None, "row"),
            P("col", "dp", None, None, "row"),
            P("col", "dp", None, None, "row"),
            P(None, "row", "dp", None, "col"),
            P(None, "row", "dp", None, "col"),
            P(None, "row", "dp", None, "col"),
            P(None, "col", "dp", None),
            P(None, "col", "dp", None),
            P(None, "col", "dp", None),
            P(None, "col", "dp", None),
            P(None, "col", "dp", None),
            P(None, "col", "dp", None),
            P(None, "row", "dp", None),
            P(None, "row", "dp", None),
            P(None, "row", "dp", None),
            P(None, "row", "dp", None),
            P(None, "row", "dp", None),
            P(None, "row", "dp", None),
        ),
        check_vma=False,
    )
```
